32 devices in a mesh: dp: 4 (over z), seq: 8 (over y, x, core).
Axes of the slice: x: 2, y: 2, z: 4, core: 2. Of those that a mesh axis runs over, the one named last changes fastest.
Arguments:
- block_in: bfloat16 [2, 4, 2048, 512], P(None, 'dp', 'seq'), may hold values from -14 to 14
- cotangent: bfloat16 [2, 4, 2048, 512], P(None, 'dp', 'seq'), may hold values from -6 to 6
- doc_lengths: int32 [2, 4, 4], P(None, 'dp'), may hold values from 1 to 1920, 2048 in all within a row
- norm_gain: float32 [2, 512], replicated, may hold values from 0.25 to 1.75
- norm_shift: float32 [2, 512], replicated, may hold values from -4 to 4
- log_step: float32 [2, 384], replicated, may hold values from -0.3 to 0.3
- lam_re: float32 [2, 384], replicated, may hold values from -1 to 0, as said below
- lam_im: float32 [2, 384], replicated, may hold values from -2048 to 2048
- b_proj: bfloat16 [2, 512, 768], replicated, may hold values from -0.25 to 0.25
- c_proj: bfloat16 [2, 768, 512], replicated, may hold values from -0.09375 to 0.09375
- d_skip: float32 [2, 512], replicated, may hold values from -3 to 3
- w_gate: bfloat16 [2, 512, 512], replicated, may hold values from -0.25 to 0.25
Outputs:
- block_out: bfloat16 [2, 4, 2048, 512], P(None, 'dp', 'seq')
- grad_input: float32 [2, 4, 2048, 512], P(None, 'dp', 'seq')
- grad_norm_gain: float32 [2, 512], replicated
- grad_norm_shift: float32 [2, 512], replicated
- grad_log_step: float32 [2, 384], replicated
- grad_lam_re: float32 [2, 384], replicated
- grad_lam_im: float32 [2, 384], replicated
- grad_b_proj: float32 [2, 512, 768], replicated
- grad_c_proj: float32 [2, 768, 512], replicated
- grad_d_skip: float32 [2, 512], replicated
- grad_w_gate: float32 [2, 512, 512], replicated
The draws below stay inside these ranges and needn't reach their ends.
Inputs may be any that keep to these rules, and one draw needn't show every extreme that they name: `doc_lengths`: in every row the 4 lengths sum to 2048 and the largest is exactly 1920. `lam_re`: negative.
All inputs are finite; a program needn't handle non-finite values.
Results may differ from the reference program's by a relative error of at most 0.019.
Values sent between devices are 32-bit elements; how exact they have to be, the bound alone decides.
No kernel may reach another device: no remote copies, remote signals or barrier semaphores. Data moves between devices by JAX's collectives and lax.ppermute only.
A program may use at most 128 MiB of HBM per device.

```python
import math
import jax
import jax.numpy as jnp
import numpy as np
from jax import lax

H = 512
P_SIZE = 384
LAYERS = 2
MB = 2
DOCS = 4
TL = 256
LEN = 2048
SEQS = 4


def slow_states(key, slow_share):
    return jax.random.bernoulli(jax.random.fold_in(key, 11), slow_share, (LAYERS, P_SIZE))


def draw_block_in(key, part):
    key = jax.random.fold_in(key, 7)
    key_noise, key_offset = jax.random.split(key, 2)
    position = (jnp.arange(LEN, dtype=jnp.float32) / LEN)[None, None, :, None]
    offset = 0.5 * jnp.clip(jax.random.normal(key_offset, (1, 1, 1, H), jnp.float32), -3.0, 3.0) * position
    jitter = jnp.clip(jax.random.normal(key_noise, (MB, SEQS, LEN, H), jnp.float32), -5.0, 5.0)
    return (jitter * (0.6 + 1.2 * position) + offset).astype(jnp.bfloat16)


def draw_lam_re(key, part):
    slow_share = 0.5
    slow_mask = slow_states(key, slow_share)
    key = jax.random.fold_in(key, 3)
    uniform_draw = jax.random.uniform(key, (LAYERS, P_SIZE), jnp.float32)
    slow_rate = jnp.exp(math.log(0.5 / LEN) + uniform_draw * math.log(3.0))
    fast_rate = jnp.exp(math.log(0.01) + uniform_draw * math.log(4.0))
    return -jnp.where(slow_mask, slow_rate, fast_rate)


def draw_lam_im(key, part):
    slow_share = 0.5
    slow_mask = slow_states(key, slow_share)
    key = jax.random.fold_in(key, 5)
    key_sign, key_size = jax.random.split(key)
    sign_flip = jnp.where(jax.random.bernoulli(key_sign, 0.5, (LAYERS, P_SIZE)), 1.0, -1.0)
    uniform_draw = jax.random.uniform(key_size, (LAYERS, P_SIZE), jnp.float32)
    slow_turn = math.sqrt(LEN * 1.0) * (0.3 + 0.7 * uniform_draw)
    fast_turn = 1.0 + 2.0 * uniform_draw
    return sign_flip * jnp.where(slow_mask, slow_turn, fast_turn)


def block_scale(own_key, extent, pieces, least, high):
    def one(axis_at, blocks):
        steps = jax.random.uniform(jax.random.fold_in(jax.random.fold_in(own_key, 6), axis_at), (blocks,), jnp.float32, least / len(pieces), high / len(pieces))
        return jnp.repeat(jnp.exp(steps), extent[axis_at] // blocks).reshape((-1,) + (1,) * (len(extent) - axis_at - 1))

    level = one(*pieces[0])
    for cut in pieces[1:]:
        level = level * one(*cut)
    return level


def length_profile(amount, total, limit, skew):
    portions = [(1 << 20) // math.isqrt(standing ** skew) + 1 for standing in range(2, amount + 1)]
    surplus, given = total - limit - (amount - 1), [1] * (amount - 1)
    while surplus > 0:
        movable = [i for i in range(amount - 1) if given[i] < limit]
        pool, left = sum([portions[i] for i in movable]), surplus
        for i in movable:
            addition = min(limit - given[i], max(1, left * portions[i] // pool), surplus)
            given[i] = given[i] + addition
            surplus = surplus - addition
    return np.array([limit] + given)


def uneven_parts(own_key, amount, total, most, skew):
    if amount == 2:
        one = jax.random.randint(own_key, (), max(1, total - most), min(most, total - 1) + 1)
        return jnp.stack([one, total - one])
    lengths = jnp.asarray(length_profile(amount, total, most, skew), jnp.int32)
    pairs = (amount - 1) // 2
    source_of, receiver = lengths[1:1 + 2 * pairs:2], lengths[2:2 + 2 * pairs:2]
    slack = jnp.minimum(source_of - 1, most - receiver)
    passed = jax.random.randint(jax.random.fold_in(own_key, 1), (pairs,), 0, 1 << 20) % (slack + 1)
    lengths = lengths.at[1:1 + 2 * pairs:2].set(source_of - passed).at[2:2 + 2 * pairs:2].set(receiver + passed)
    return lengths[jax.random.permutation(jax.random.fold_in(own_key, 2), amount)]


def gaussian(own_key, shape, deviation, reach, cuts=(), kind=jnp.bfloat16):
    loudness = block_scale(own_key, shape, cuts, -0.22, 0.18) if cuts else 1.0
    values = jax.random.normal(own_key, shape, jnp.float32) * deviation * loudness
    return jnp.minimum(jnp.maximum(values, -reach), reach).astype(kind)


def setup_inputs(seed: int = 0) -> dict:
    key_of = jax.random.split(jax.random.key(seed), 13)
    block_in = draw_block_in(jax.random.fold_in(key_of[12], 71), 0)
    cotangent = gaussian(key_of[1], (MB, SEQS, LEN, H), 1.0, 6.0, ((1, 4), (2, 8)))
    doc_lengths = jax.vmap(lambda own: uneven_parts(own, DOCS, LEN, LEN - TL // 2, 2))(jax.random.split(key_of[2], MB * SEQS)).reshape((MB, SEQS, DOCS)).astype(jnp.int32)
    norm_gain = jnp.clip(1.0 + 0.15 * jax.random.normal(key_of[3], (LAYERS, H), jnp.float32), 0.25, 1.75)
    norm_shift = gaussian(key_of[4], (LAYERS, H), 0.3, 4.0, (), jnp.float32)
    log_step = jnp.clip(jax.random.uniform(key_of[5], (LAYERS, P_SIZE), jnp.float32, -0.3, 0.3), -0.3, 0.3)
    lam_re = draw_lam_re(jax.random.fold_in(key_of[12], 71), 0)
    lam_im = draw_lam_im(jax.random.fold_in(key_of[12], 71), 0)
    b_proj = gaussian(key_of[8], (LAYERS, H, 2 * P_SIZE), H ** -0.5, 0.25)
    c_proj = gaussian(key_of[9], (LAYERS, 2 * P_SIZE, H), (12 * P_SIZE) ** -0.5, 0.09375)
    d_skip = gaussian(key_of[10], (LAYERS, H), 0.5, 3.0, (), jnp.float32)
    w_gate = gaussian(key_of[11], (LAYERS, H, H), H ** -0.5, 0.25)
    return {"block_in": block_in, "cotangent": cotangent, "doc_lengths": doc_lengths, "norm_gain": norm_gain, "norm_shift": norm_shift, "log_step": log_step, "lam_re": lam_re, "lam_im": lam_im, "b_proj": b_proj, "c_proj": c_proj, "d_skip": d_skip, "w_gate": w_gate}


epsilon = 1e-05
tanh_scale = 0.7978845608028654
cubic_term = 0.044715
highest = lax.Precision.HIGHEST

@jax.custom_vjp
def low(v):
    return lax.optimization_barrier(v.astype(jnp.bfloat16)).astype(jnp.float32)

@jax.custom_vjp
def low_back(v):
    return v

def low_keep(v):
    return (low(v), None)

def low_pass(kept, grad):
    return (grad,)

def back_keep(v):
    return (v, None)

def back_low(kept, grad):
    return (low(grad),)
low.defvjp(low_keep, low_pass)
low_back.defvjp(back_keep, back_low)

def gelu_tanh(pre_act):
    return 0.5 * pre_act * (1.0 + jnp.tanh(tanh_scale * (pre_act + cubic_term * pre_act * pre_act * pre_act)))

def discretize(lam_re, lam_im, log_step):
    step_size = jnp.exp(log_step)
    decay_abs = jnp.exp(lam_re * step_size)
    rotation = lam_im * step_size
    dec_re = decay_abs * jnp.cos(rotation)
    dec_im = decay_abs * jnp.sin(rotation)
    denom_sq = lam_re * lam_re + lam_im * lam_im
    inj_re = ((dec_re - 1.0) * lam_re + dec_im * lam_im) / denom_sq
    inj_im = (dec_im * lam_re - (dec_re - 1.0) * lam_im) / denom_sq
    return (dec_re, dec_im, inj_re, inj_im)

def doc_masks(row_lengths):
    position = jnp.arange(LEN, dtype=jnp.int32)
    doc_ends = jnp.cumsum(row_lengths, axis=-1).astype(jnp.int32)
    begins = doc_ends - row_lengths
    starts = jnp.any(position[None, :, None] == begins[:, None, :], axis=-1)
    finals = jnp.any(position[None, :, None] + 1 == doc_ends[:, None, :], axis=-1)
    return (jnp.where(starts, 0.0, 1.0).astype(jnp.float32), jnp.where(finals, 0.0, 1.0).astype(jnp.float32))

def s5_layer(hidden, keep_mask, reverse, layer_weights):
    norm_gain, norm_shift, log_step, lam_re, lam_im, b_proj, c_proj, d_skip, w_gate = layer_weights
    average = lax.optimization_barrier(jnp.mean(hidden, axis=(0, 1)))
    spread = lax.optimization_barrier(jnp.mean(hidden * hidden, axis=(0, 1))) - average * average
    normed = (hidden - average) * lax.rsqrt(spread + epsilon)
    u_low = low(normed * norm_gain + norm_shift)
    projected = low_back(jnp.einsum('slh,hq->slq', u_low, b_proj, precision=highest))
    half_cols = lam_re.shape[0]
    drive_re = projected[..., :half_cols]
    drive_im = projected[..., half_cols:]
    dec_re, dec_im, inj_re, inj_im = discretize(lam_re, lam_im, log_step)
    input_re = inj_re * drive_re - inj_im * drive_im
    input_im = inj_re * drive_im + inj_im * drive_re

    def advance(carried, element):
        keep_now, push_re, push_im = element
        next_re = keep_now[:, None] * (dec_re * carried[0] - dec_im * carried[1]) + push_re
        next_im = keep_now[:, None] * (dec_re * carried[1] + dec_im * carried[0]) + push_im
        return ((next_re, next_im), (next_re, next_im))
    zero_state = jnp.zeros((hidden.shape[0], half_cols), jnp.float32)
    elements = (jnp.swapaxes(keep_mask, 0, 1), jnp.swapaxes(input_re, 0, 1), jnp.swapaxes(input_im, 0, 1))
    _, (state_re, state_im) = lax.scan(advance, (zero_state, zero_state), elements, reverse=reverse)
    states = low(jnp.concatenate([jnp.swapaxes(state_re, 0, 1), jnp.swapaxes(state_im, 0, 1)], axis=-1))
    mixed_out = low_back(jnp.einsum('slq,qh->slh', states, c_proj, precision=highest)) + d_skip * u_low
    activated = low(gelu_tanh(mixed_out))
    gate_pre = low_back(jnp.einsum('slh,hk->slk', activated, w_gate, precision=highest))
    return hidden + activated * jax.nn.sigmoid(gate_pre)

def add_up(total_part, new_part):
    return total_part + new_part

def reference(block_in, cotangent, doc_lengths, norm_gain, norm_shift, log_step, lam_re, lam_im, b_proj, c_proj, d_skip, w_gate):
    weights = (norm_gain, norm_shift, log_step, lam_re, lam_im, b_proj.astype(jnp.float32), c_proj.astype(jnp.float32), d_skip, w_gate.astype(jnp.float32))

    def micro_step(totals, element):
        inputs, cot_now, row_lengths = element
        keep_fwd, keep_bwd = doc_masks(row_lengths)

        def two_layers(hidden, params):
            layer_one = s5_layer(hidden, keep_fwd, False, tuple((weight_now[0] for weight_now in params)))
            return s5_layer(layer_one, keep_bwd, True, tuple((weight_now[1] for weight_now in params)))
        result, pullback = jax.vjp(two_layers, inputs.astype(jnp.float32), weights)
        grad_in, grad_weights = pullback(cot_now.astype(jnp.float32))
        totals = jax.tree.map(add_up, totals, grad_weights)
        return (totals, (result.astype(jnp.bfloat16), grad_in))
    zero_grads = jax.tree.map(jnp.zeros_like, weights)
    totals, (block_out, grad_input) = lax.scan(micro_step, zero_grads, (block_in, cotangent, doc_lengths))
    return (block_out, grad_input, totals[0], totals[1], totals[2], totals[3], totals[4], totals[5], totals[6], totals[7], totals[8])
```

```python
import functools

import jax
import jax.numpy as jnp
from jax import lax
from jax.experimental import pallas as pl
from jax.experimental.pallas import tpu as pltpu
from jax.sharding import PartitionSpec as P

f32, bf16 = jnp.float32, jnp.bfloat16
epsilon = 1e-05
tanh_scale = 0.7978845608028654
cubic_term = 0.044715
LANES = 128
CHUNKS = 8
ROWS = 32
VMEM_LIMIT = 48 * 1024 * 1024


def dot(left, right, contract=(1, 0)):
    return lax.dot_general(
        left, right, (((contract[0],), (contract[1],)), ((), ())), preferred_element_type=f32
    )


def reorder(span, inverse):
    shape = (span, span)
    kept, moved = (1, 0) if inverse else (0, 1)
    row = lax.broadcasted_iota(jnp.int32, shape, kept)
    position = lax.broadcasted_iota(jnp.int32, shape, moved)
    source = (row & (CHUNKS - 1)) * (span // CHUNKS) + (row >> 3)
    return jnp.where(position == source, 1.0, 0.0).astype(bf16)


def row_loop(count, body, init=0, step=ROWS):
    def one(index, carry):
        return body(pl.multiple_of(index * step, step), carry)

    return lax.fori_loop(0, count // step, one, init)


META = 12


def keep_of(meta, batch, base, step, backward):
    off = 4 if backward else 0
    late = 1 if backward else 0
    stop = base == meta[batch, off] - step - late
    for doc in range(1, 4):
        stop = jnp.logical_or(stop, base == meta[batch, off + doc] - step - late)
    return jnp.where(stop, 0.0, 1.0)


def base_positions(meta, steps):
    return meta[0, 10] + lax.broadcasted_iota(jnp.int32, (CHUNKS, LANES), 0) * steps


def lanes_of(index, half=0):
    return slice(half + index * LANES, half + (index + 1) * LANES)


def coef_tiles(disc, row, groups, conj=False):
    out = []
    for q in range(groups):
        re = jnp.broadcast_to(disc[row : row + 1, lanes_of(q)], (CHUNKS, LANES))
        im = jnp.broadcast_to(disc[row + 1 : row + 2, lanes_of(q)], (CHUNKS, LANES))
        out.append((re, -im if conj else im))
    return out


def times(a, b):
    return (a[0] * b[0] - a[1] * b[1], a[0] * b[1] + a[1] * b[0])


def scan(meta, source, inject, dec, batches, span, groups, reverse, masks_reverse, init, extra, visit):
    steps = span // CHUNKS
    half = groups * LANES
    base = base_positions(meta, steps)

    def pair(index, carry):
        states, more = carry
        states = list(states)
        first = steps - 2 - 2 * index if reverse else 2 * index
        start = pl.multiple_of(first * CHUNKS, 2 * CHUNKS)
        order = (1, 0) if reverse else (0, 1)
        for batch in range(batches):
            keeps = [keep_of(meta, batch, base, first + j, masks_reverse) for j in (0, 1)]
            for q in range(groups):
                rows = pl.ds(batch * span + start, 2 * CHUNKS)
                src_re = source[rows, lanes_of(q)]
                src_im = source[rows, lanes_of(q, half)]
                state = states[batch * groups + q]
                found = [None, None]
                for j in order:
                    part = (
                        src_re[j * CHUNKS : (j + 1) * CHUNKS],
                        src_im[j * CHUNKS : (j + 1) * CHUNKS],
                    )
                    push = times(inject[q], part) if inject is not None else part
                    held = times((keeps[j] * dec[q][0], keeps[j] * dec[q][1]), state)
                    state = (held[0] + push[0], held[1] + push[1])
                    found[j] = state
                states[batch * groups + q] = state
                more = visit(more, batch, q, first, start, found, (src_re, src_im))
            more = visit(more, batch, None, first, start, keeps, None)
        return tuple(states), more

    return lax.fori_loop(0, steps // 2, pair, (tuple(init), extra), unroll=2)


def zero_states(batches, groups):
    zero = jnp.zeros((CHUNKS, LANES), f32)
    return [(zero, zero)] * (batches * groups)


def local_ends(meta, source, inject, dec, dec_chunk, batches, span, groups, reverse, prefix, total):
    ones = tuple(jnp.ones((CHUNKS, LANES), f32) for _ in range(batches))

    def visit(more, batch, q, first, start, found, src):
        if q is not None:
            return more
        return tuple(
            value * found[0] * found[1] if at == batch else value for at, value in enumerate(more)
        )

    ends, kept = scan(
        meta, source, inject, dec, batches, span, groups, reverse, reverse,
        zero_states(batches, groups), ones, visit,
    )
    half = groups * LANES
    row = lax.broadcasted_iota(jnp.int32, (CHUNKS, LANES), 0)
    for batch in range(batches):
        for q in range(groups):
            end = ends[batch * groups + q]
            decay = (kept[batch] * dec_chunk[q][0], kept[batch] * dec_chunk[q][1])
            for shift in (1, 2, 4):
                turn = CHUNKS - shift if reverse else shift
                valid = row < CHUNKS - shift if reverse else row >= shift
                before = [pltpu.roll(value, turn, 0) for value in (*end, *decay)]
                from_before = times(decay, (before[0], before[1]))
                end = (
                    end[0] + jnp.where(valid, from_before[0], 0.0),
                    end[1] + jnp.where(valid, from_before[1], 0.0),
                )
                longer = times(decay, (before[2], before[3]))
                decay = (
                    jnp.where(valid, longer[0], decay[0]),
                    jnp.where(valid, longer[1], decay[1]),
                )
            rows = slice(batch * CHUNKS, (batch + 1) * CHUNKS)
            prefix[0, rows, lanes_of(q)] = end[0]
            prefix[0, rows, lanes_of(q, half)] = end[1]
            prefix[1, rows, lanes_of(q)] = decay[0]
            prefix[1, rows, lanes_of(q, half)] = decay[1]
            last = 0 if reverse else CHUNKS - 1
            total[batch : batch + 1, lanes_of(q)] = end[0][last : last + 1]
            total[batch : batch + 1, lanes_of(q, half)] = end[1][last : last + 1]


def chunk_carries(meta, gathered, disc, prefix, batches, span, groups, reverse, conj):
    half = groups * LANES
    dec_re = disc[6:7, :]
    dec_im = -disc[7:8, :] if conj else disc[7:8, :]
    row = lax.broadcasted_iota(jnp.int32, (CHUNKS, LANES), 0)
    mine = meta[0, 11]
    out = []
    for batch in range(batches):
        enter = (jnp.zeros((1, half), f32), jnp.zeros((1, half), f32))
        for away in range(len(gathered) - 1, -1, -1):
            if reverse:
                reaches = meta[batch, 9] > (mine + 1 + away) * span
            else:
                reaches = meta[batch, 8] < (mine - away) * span
            value = jnp.where(reaches, gathered[away][batch : batch + 1, :], 0.0)
            moved = times((dec_re, dec_im), enter)
            enter = (moved[0] + value[:, :half], moved[1] + value[:, half:])
        rows = slice(batch * CHUNKS, (batch + 1) * CHUNKS)
        for q in range(groups):
            own = tuple(jnp.broadcast_to(part[:, lanes_of(q)], (CHUNKS, LANES)) for part in enter)
            end = (prefix[0, rows, lanes_of(q)], prefix[0, rows, lanes_of(q, half)])
            decay = (prefix[1, rows, lanes_of(q)], prefix[1, rows, lanes_of(q, half)])
            moved = times(decay, own)
            turn, first = (CHUNKS - 1, CHUNKS - 1) if reverse else (1, 0)
            out.append(
                tuple(
                    jnp.where(row == first, own[i], pltpu.roll(end[i] + moved[i], turn, 0))
                    for i in (0, 1)
                )
            )
    return out


def add_sums(target, batches, sums):
    for kind, per_batch in enumerate(sums):
        for batch in range(batches):
            target[kind * batches + batch : kind * batches + batch + 1, :] = jnp.sum(
                per_batch[batch], axis=0, keepdims=True
            )


def fold(value):
    return sum(value[i : i + CHUNKS] for i in range(CHUNKS, value.shape[0], CHUNKS)) + value[:CHUNKS]


def first_sums(batches, span, x, ordered, stats):
    turn = reorder(span, False)
    width = x.shape[1]
    sums, squares = [], []
    for batch in range(batches):
        rows = slice(batch * span, (batch + 1) * span)
        ordered[rows, :] = dot(turn, x[rows, :]).astype(bf16)

        def body(start, carry, batch=batch):
            value = x[pl.ds(batch * span + start, ROWS), :].astype(f32)
            return carry[0] + fold(value), carry[1] + fold(value * value)

        zero = jnp.zeros((CHUNKS, width), f32)
        one, two = row_loop(span, body, (zero, zero))
        sums.append(one)
        squares.append(two)
    add_sums(stats, batches, (sums, squares))


def enter_layer(
    cfg, meta, stats, hidden, gain, shift, disc, b_proj, u, drive, prefix, total, norm
):
    layer, reverse, batches, span, groups, tokens = cfg
    sums = stats[...]
    average = sums[:batches] / tokens
    spread = sums[batches:] / tokens - average * average
    scale = lax.rsqrt(spread + epsilon)
    norm[:batches, :] = average
    norm[batches:, :] = scale
    gain_now, shift_now = gain[layer : layer + 1, :], shift[layer : layer + 1, :]
    for batch in range(batches):

        def body(start, carry, batch=batch):
            rows = pl.ds(batch * span + start, ROWS)
            normed = (hidden[rows, :].astype(f32) - average[batch : batch + 1]) * scale[
                batch : batch + 1
            ]
            u[rows, :] = (normed * gain_now + shift_now).astype(bf16)
            return carry

        row_loop(span, body)
    drive[...] = dot(u[...], b_proj[...])
    now = disc.at[layer]
    local_ends(
        meta, drive, coef_tiles(now, 2, groups), coef_tiles(now, 0, groups),
        coef_tiles(now, 4, groups), batches, span, groups, reverse, prefix, total,
    )


def finish_states(cfg, meta, ends, prefix, disc, drive, states, states_low):
    layer, reverse, batches, span, groups, tokens = cfg
    half = groups * LANES
    padded = span + CHUNKS
    now = disc.at[layer]
    init = chunk_carries(meta, ends, now, prefix, batches, span, groups, reverse, False)
    for batch in range(batches):
        edge = batch * padded + (span if reverse else 0)
        for q in range(groups):
            states[edge : edge + CHUNKS, lanes_of(q)] = init[batch * groups + q][0]
            states[edge : edge + CHUNKS, lanes_of(q, half)] = init[batch * groups + q][1]

    def visit(more, batch, q, first, start, found, src):
        if q is not None:
            for part, off in ((0, 0), (1, half)):
                both = jnp.concatenate([found[0][part], found[1][part]], axis=0)
                at = batch * padded + (0 if reverse else CHUNKS)
                states[pl.ds(at + start, 2 * CHUNKS), lanes_of(q, off)] = both
                states_low[pl.ds(batch * span + start, 2 * CHUNKS), lanes_of(q, off)] = both.astype(
                    bf16
                )
        return more

    scan(
        meta, drive, coef_tiles(now, 2, groups), coef_tiles(now, 0, groups), batches, span, groups,
        reverse, reverse, init, 0, visit,
    )


def forward_finish(
    cfg, meta, ends, prefix, disc, drive, u, hidden, c_proj, d_skip, w_gate,
    states, states_low, act, sig, slope, result, wide, emit,
):
    layer, reverse, batches, span, groups, tokens = cfg
    finish_states(cfg, meta, ends, prefix, disc, drive, states, states_low)
    wide[...] = dot(states_low[...], c_proj[...])
    skip = d_skip[layer : layer + 1, :]

    def body(start, carry):
        rows = pl.ds(start, ROWS)
        mixed = wide[rows, :] + skip * u[rows, :].astype(f32)
        square = mixed * mixed
        th = jnp.tanh(tanh_scale * (mixed + cubic_term * square * mixed))
        half_one = 0.5 * (1.0 + th)
        act[rows, :] = (mixed * half_one).astype(bf16)
        slope[rows, :] = half_one + 0.5 * mixed * (1.0 - th * th) * tanh_scale * (
            1.0 + 3.0 * cubic_term * square
        )
        return carry

    row_loop(batches * span, body)
    wide[...] = dot(act[...], w_gate[...])
    sums, squares = [], []
    for batch in range(batches):

        def gate(start, carry, batch=batch):
            rows = pl.ds(batch * span + start, ROWS)
            sig_now = 0.5 + 0.5 * jnp.tanh(0.5 * wide[rows, :])
            sig[rows, :] = sig_now
            value = hidden[rows, :].astype(f32) + act[rows, :].astype(f32) * sig_now
            result[rows, :] = value.astype(result.dtype)
            if emit is None:
                return carry
            return carry[0] + fold(value), carry[1] + fold(value * value)

        zero = jnp.zeros((CHUNKS, wide.shape[1]), f32)
        one, two = row_loop(span, gate, (zero, zero))
        sums.append(one)
        squares.append(two)
    if emit is not None:
        add_sums(emit, batches, (sums, squares))


def backward_start(
    cfg, meta, grad_out, disc, u, c_proj, w_gate, states_low, act, sig, slope,
    grad_gate, grad_mixed, grad_low, source, prefix, total, grad_d, wide,
):
    layer, reverse, batches, span, groups, tokens = cfg

    def body(start, carry):
        rows = pl.ds(start, ROWS)
        sig_now = sig[rows, :]
        grad_gate[rows, :] = (
            grad_out[rows, :].astype(f32) * act[rows, :].astype(f32) * sig_now * (1.0 - sig_now)
        ).astype(bf16)
        return carry

    row_loop(batches * span, body)
    wide[...] = dot(grad_gate[...], w_gate[...], (1, 1))

    def mixed(start, carry):
        rows = pl.ds(start, ROWS)
        value = (grad_out[rows, :].astype(f32) * sig[rows, :] + wide[rows, :]) * slope[rows, :]
        grad_mixed[rows, :] = value
        grad_low[rows, :] = value.astype(bf16)
        return carry + fold(value * u[rows, :].astype(f32))

    gd = row_loop(batches * span, mixed, jnp.zeros((CHUNKS, wide.shape[1]), f32))
    grad_d[...] = jnp.sum(gd, axis=0, keepdims=True)
    source[...] = dot(grad_low[...], c_proj[...], (1, 1))
    now = disc.at[layer]
    local_ends(
        meta, source, None, coef_tiles(now, 0, groups, True), coef_tiles(now, 4, groups, True),
        batches, span, groups, not reverse, prefix, total,
    )


def middle_forward(
    cfg, meta, ends, prefix, disc, drive, u, hidden, c_proj, d_skip, w_gate,
    states, states_low, act, sig, slope, result, stats, wide,
):
    forward_finish(
        cfg, meta, ends, prefix, disc, drive, u, hidden, c_proj, d_skip, w_gate,
        states, states_low, act, sig, slope, result, wide, stats,
    )


def turn_around(
    cfg, meta, ends, prefix, disc, drive, u, hidden, c_proj, d_skip, w_gate, cotangent,
    block_out, ordered_cot, states, states_low, act, grad_gate, grad_mixed, grad_low, source,
    back_prefix, total, grad_d, sig, slope, wide, result,
):
    layer, reverse, batches, span, groups, tokens = cfg
    turn, back = reorder(span, False), reorder(span, True)
    for batch in range(batches):
        rows = slice(batch * span, (batch + 1) * span)
        ordered_cot[rows, :] = dot(turn, cotangent[rows, :]).astype(bf16)
    forward_finish(
        cfg, meta, ends, prefix, disc, drive, u, hidden, c_proj, d_skip, w_gate,
        states, states_low, act, sig, slope, result, wide, None,
    )
    for batch in range(batches):
        rows = slice(batch * span, (batch + 1) * span)
        block_out[rows, :] = dot(back, result[rows, :]).astype(bf16)
    backward_start(
        cfg, meta, ordered_cot, disc, u, c_proj, w_gate, states_low, act, sig, slope,
        grad_gate, grad_mixed, grad_low, source, back_prefix, total, grad_d, wide,
    )


def backward_finish(
    cfg, meta, ends, prefix, disc, source, drive, states, u, grad_mixed, grad_d, hidden, norm,
    d_skip, b_proj, grad_proj, grad_u, stats, small,
):
    layer, reverse, batches, span, groups, tokens = cfg
    half = groups * LANES
    padded = span + CHUNKS
    steps = span // CHUNKS
    now = disc.at[layer]
    init = chunk_carries(meta, ends, now, prefix, batches, span, groups, not reverse, True)
    inj = coef_tiles(now, 2, groups)
    base = base_positions(meta, steps)
    zero = jnp.zeros((CHUNKS, LANES), f32)

    def visit(more, batch, q, first, start, found, src):
        if q is None:
            return more
        more = list(more)
        rows = pl.ds(batch * span + start, 2 * CHUNKS)
        drive_re, drive_im = drive[rows, lanes_of(q)], drive[rows, lanes_of(q, half)]
        before = pl.ds(batch * padded + start + (CHUNKS if reverse else 0), 2 * CHUNKS)
        prior_re, prior_im = states[before, lanes_of(q)], states[before, lanes_of(q, half)]
        dec_re, dec_im, inj_re, inj_im = more[q]
        out_re, out_im = [], []
        for j in (0, 1):
            part = slice(j * CHUNKS, (j + 1) * CHUNKS)
            adj_re, adj_im = found[j]
            keep = keep_of(meta, batch, base, first + j, reverse)
            kept_re, kept_im = keep * adj_re, keep * adj_im
            dec_re = dec_re + kept_re * prior_re[part] + kept_im * prior_im[part]
            dec_im = dec_im + kept_im * prior_re[part] - kept_re * prior_im[part]
            inj_re = inj_re + adj_re * drive_re[part] + adj_im * drive_im[part]
            inj_im = inj_im + adj_im * drive_re[part] - adj_re * drive_im[part]
            out_re.append(inj[q][0] * adj_re + inj[q][1] * adj_im)
            out_im.append(inj[q][0] * adj_im - inj[q][1] * adj_re)
        grad_proj[rows, lanes_of(q)] = jnp.concatenate(out_re, axis=0).astype(bf16)
        grad_proj[rows, lanes_of(q, half)] = jnp.concatenate(out_im, axis=0).astype(bf16)
        more[q] = (dec_re, dec_im, inj_re, inj_im)
        return tuple(more)

    _, sums = scan(
        meta, source, None, coef_tiles(now, 0, groups, True), batches, span, groups,
        not reverse, not reverse, init, ((zero,) * 4,) * groups, visit,
    )
    small[...] = jnp.zeros_like(small)
    for q in range(groups):
        for kind in range(4):
            small[kind : kind + 1, lanes_of(q)] = jnp.sum(sums[q][kind], axis=0, keepdims=True)
    small[4:5, :] = grad_d[...]
    grad_u[...] = dot(grad_proj[...], b_proj[...], (1, 1))
    skip = d_skip[layer : layer + 1, :]
    plain, times_normed = [], []
    for batch in range(batches):
        average = norm[batch : batch + 1, :]
        scale = norm[batches + batch : batches + batch + 1, :]

        def body(start, carry, batch=batch, average=average, scale=scale):
            rows = pl.ds(batch * span + start, ROWS)
            value = grad_u[rows, :] + grad_mixed[rows, :] * skip
            grad_u[rows, :] = value
            normed = (hidden[rows, :].astype(f32) - average) * scale
            return carry[0] + fold(value), carry[1] + fold(value * normed)

        zero_sum = jnp.zeros((CHUNKS, grad_u.shape[1]), f32)
        one, two = row_loop(span, body, (zero_sum, zero_sum))
        plain.append(one)
        times_normed.append(two)
    add_sums(stats, batches, (plain, times_normed))


def norm_backward(cfg, stats, grad_out, grad_u, hidden, norm, gain, store, shared):
    layer, reverse, batches, span, groups, tokens = cfg
    sums = stats[...]
    shared[0:1, :] = jnp.sum(sums[batches:], axis=0, keepdims=True)
    shared[1:2, :] = jnp.sum(sums[:batches], axis=0, keepdims=True)
    gain_now = gain[layer : layer + 1, :]
    for batch in range(batches):
        average = norm[batch : batch + 1, :]
        scale = norm[batches + batch : batches + batch + 1, :]
        plain = gain_now * sums[batch : batch + 1] / tokens
        slanted = gain_now * sums[batches + batch : batches + batch + 1] / tokens

        def body(start, carry, batch=batch, average=average, scale=scale, plain=plain, slanted=slanted):
            rows = pl.ds(batch * span + start, ROWS)
            normed = (hidden[rows, :].astype(f32) - average) * scale
            value = grad_out[rows, :].astype(f32) + scale * (
                grad_u[rows, :] * gain_now - plain - normed * slanted
            )
            store(rows, value)
            return carry

        row_loop(span, body)


def between_layers(
    cfg, lower, meta, stats, upper_out, upper_u, upper_hidden, upper_norm, gain,
    disc, u, c_proj, w_gate, states_low, act, sig, slope,
    grad_out, shared, grad_gate, grad_mixed, grad_low, source, prefix, total, grad_d, wide,
):
    def store(rows, value):
        grad_out[rows, :] = value

    norm_backward(cfg, stats, upper_out, upper_u, upper_hidden, upper_norm, gain, store, shared)
    backward_start(
        lower, meta, grad_out, disc, u, c_proj, w_gate, states_low, act, sig, slope,
        grad_gate, grad_mixed, grad_low, source, prefix, total, grad_d, wide,
    )


def last_step(cfg, stats, grad_out, grad_u, hidden, norm, gain, target, shared, ordered):
    layer, reverse, batches, span, groups, tokens = cfg
    planes = target.shape[1] // LANES

    def store(rows, value):
        for plane in range(planes):
            ordered[plane, rows, :] = value[:, lanes_of(plane)]

    norm_backward(cfg, stats, grad_out, grad_u, hidden, norm, gain, store, shared)
    steps = span // CHUNKS
    for batch in range(batches):
        for chunk in range(CHUNKS):
            at = batch * span
            for plane in range(planes):
                target[at + chunk * steps : at + (chunk + 1) * steps, lanes_of(plane)] = ordered[
                    plane, pl.ds(at + chunk, steps, stride=CHUNKS), :
                ]


def gate_weights(act, grad_gate, states_low, grad_low, grad_w, grad_c):
    grad_w[...] = dot(act[...], grad_gate[...], (0, 0))
    grad_c[...] = dot(states_low[...], grad_low[...], (0, 0))


def input_weights(u, grad_proj, grad_b):
    grad_b[...] = dot(u[...], grad_proj[...], (0, 0))


def run(body, name, args, outs, scratch=(), scalars=1, flops=0, touched=0):
    specs = [pl.BlockSpec(memory_space=pltpu.SMEM)] * scalars
    specs += [pl.BlockSpec(memory_space=pltpu.VMEM)] * (len(args) - scalars)
    return pl.pallas_call(
        body,
        name=name,
        out_shape=tuple(jax.ShapeDtypeStruct(*out) for out in outs),
        in_specs=specs,
        out_specs=tuple(pl.BlockSpec(memory_space=pltpu.VMEM) for _ in outs),
        scratch_shapes=[pltpu.VMEM(*entry) for entry in scratch],
        compiler_params=pltpu.CompilerParams(vmem_limit_bytes=VMEM_LIMIT),
    )(*args)


def with_ends(body, cfg, count):
    def kernel(meta, *refs):
        body(cfg, meta, refs[:count], *refs[count:])

    return kernel


def add_everywhere(value):
    for axis in ("seq", "dp"):
        size = lax.axis_size(axis)
        found = [
            lax.ppermute(value, axis, [(i, (i + away) % size) for i in range(size)])
            for away in range(1, size)
        ]
        value = sum(found, value)
    return value


def from_before(value, backward):
    size = lax.axis_size("seq")
    out = []
    for away in range(1, size):
        pairs = [(i, i + away) for i in range(size - away)]
        out.append(lax.ppermute(value, "seq", [(b, a) for a, b in pairs] if backward else pairs))
    return out


def discretize(lam_re, lam_im, log_step):
    step_size = jnp.exp(log_step)
    decay_abs = jnp.exp(lam_re * step_size)
    rotation = lam_im * step_size
    dec_re = decay_abs * jnp.cos(rotation)
    dec_im = decay_abs * jnp.sin(rotation)
    denom_sq = lam_re * lam_re + lam_im * lam_im
    inj_re = ((dec_re - 1.0) * lam_re + dec_im * lam_im) / denom_sq
    inj_im = (dec_im * lam_re - (dec_re - 1.0) * lam_im) / denom_sq
    return (dec_re, dec_im, inj_re, inj_im)


def power(value, doublings):
    for _ in range(doublings):
        value = times(value, value)
    return value


def per_device(
    block_in, cotangent, doc_lengths, norm_gain, norm_shift, log_step, lam_re, lam_im,
    b_proj, c_proj, d_skip, w_gate,
):
    batches, seqs, span, width = block_in.shape
    assert seqs == 1 and span % (4 * CHUNKS) == 0
    half = lam_re.shape[1]
    groups = half // LANES
    rows = batches * span
    everyone = ("dp", "seq")
    chunk_doublings = (span // CHUNKS).bit_length() - 1
    span_doublings = span.bit_length() - 1
    assert 1 << span_doublings == span
    tokens = float(seqs * lax.axis_size("dp") * span * lax.axis_size("seq"))
    mine = lax.axis_index("seq")
    lengths = doc_lengths[:, 0, :]
    ends = jnp.cumsum(lengths, axis=-1).astype(jnp.int32)
    begins = ends - lengths
    first = mine * span
    before = jnp.max(jnp.where(begins < first, begins, 0), axis=-1)
    whole = span * lax.axis_size("seq")
    after = jnp.min(jnp.where(ends > first + span, ends, 2 * whole), axis=-1)
    after = jnp.where(first + span < whole, after, 0)
    spot = jnp.broadcast_to(jnp.stack([first, mine])[None], (batches, 2))
    meta = jnp.concatenate([begins, ends, before[:, None], after[:, None], spot], axis=-1).astype(
        jnp.int32
    )
    dec_re, dec_im, inj_re, inj_im = discretize(lam_re, lam_im, log_step)
    dec_chunk = power((dec_re, dec_im), chunk_doublings)
    dec_span = power(dec_chunk, span_doublings - chunk_doublings)
    disc = jnp.stack([dec_re, dec_im, inj_re, inj_im, *dec_chunk, *dec_span], axis=1)

    x = block_in.reshape(rows, width)
    cot = cotangent.reshape(rows, width)
    lower = (0, False, batches, span, groups, tokens)
    upper = (1, True, batches, span, groups, tokens)
    part = functools.partial

    flat, low = ((rows, width), f32), ((rows, width), bf16)
    wide, wide_low = ((rows, 2 * half), f32), ((rows, 2 * half), bf16)
    padded = ((batches * (span + CHUNKS), 2 * half), f32)
    sums = ((2 * batches, width), f32)
    prefix = ((2, batches * CHUNKS, 2 * half), f32)
    total = ((batches, 2 * half), f32)
    line, shared = ((1, width), f32), ((2, width), f32)
    small = ((8, width), f32)

    others = lax.axis_size("seq") - 1

    ordered, stats = run(
        part(first_sums, batches, span), "first_sums", (x,), (low, sums), scalars=0
    )

    def forward(cfg, hidden, stats):
        layer = cfg[0]
        return run(
            part(enter_layer, cfg),
            "enter_layer",
            (meta, add_everywhere(stats), hidden, norm_gain, norm_shift, disc, b_proj[layer]),
            (low, wide, prefix, total, sums),
        )

    u0, drive0, prefix0, total0, norm0 = forward(lower, ordered, stats)
    states0, states_low0, act0, sig0, slope0, hidden1, stats = run(
        with_ends(middle_forward, lower, others),
        "middle_forward",
        (
            meta, *from_before(total0, False), prefix0, disc, drive0, u0, ordered, c_proj[0], d_skip,
            w_gate[0],
        ),
        (padded, wide_low, low, flat, flat, flat, sums),
        (flat,),
    )
    u1, drive1, prefix1, total1, norm1 = forward(upper, hidden1, stats)
    (
        block_out, ordered_cot, states1, states_low1, act1, grad_gate1, grad_mixed1, grad_low1,
        source1, prefix1, total1, grad_d1,
    ) = run(
        with_ends(turn_around, upper, others),
        "turn_around",
        (
            meta, *from_before(total1, True), prefix1, disc, drive1, u1, hidden1, c_proj[1], d_skip,
            w_gate[1], cot,
        ),
        (low, low, padded, wide_low, low, low, flat, low, wide, prefix, total, line),
        (flat, flat, flat, low),
    )
    grad_w1, grad_c1 = run(
        gate_weights, "gate_weights", (act1, grad_gate1, states_low1, grad_low1),
        (((width, width), f32), ((2 * half, width), f32)), scalars=0,
    )

    def finish(cfg, total, prefix, source, drive, states, u, grad_mixed, grad_d, hidden, norm):
        return run(
            with_ends(backward_finish, cfg, others),
            "backward_finish",
            (
                meta, *from_before(total, not cfg[1]), prefix, disc, source, drive, states, u, grad_mixed,
                grad_d, hidden, norm, d_skip, b_proj[cfg[0]],
            ),
            (wide_low, flat, sums, small),
        )

    grad_proj1, grad_u1, stats, small1 = finish(
        upper, total1, prefix1, source1, drive1, states1, u1, grad_mixed1, grad_d1, hidden1, norm1
    )
    (grad_b1,) = run(
        input_weights, "input_weights", (u1, grad_proj1), (((width, 2 * half), f32),), scalars=0
    )
    (
        grad_out0, shared1, grad_gate0, grad_mixed0, grad_low0, source0, prefix0, total0, grad_d0,
    ) = run(
        part(between_layers, upper, lower),
        "between_layers",
        (
            meta, add_everywhere(stats), ordered_cot, grad_u1, hidden1, norm1, norm_gain,
            disc, u0, c_proj[0], w_gate[0], states_low0, act0, sig0, slope0,
        ),
        (flat, shared, low, flat, low, wide, prefix, total, line),
        (flat,),
    )
    grad_w0, grad_c0 = run(
        gate_weights, "gate_weights", (act0, grad_gate0, states_low0, grad_low0),
        (((width, width), f32), ((2 * half, width), f32)), scalars=0,
    )
    grad_proj0, grad_u0, stats, small0 = finish(
        lower, total0, prefix0, source0, drive0, states0, u0, grad_mixed0, grad_d0, ordered, norm0
    )
    (grad_b0,) = run(
        input_weights, "input_weights", (u0, grad_proj0), (((width, 2 * half), f32),), scalars=0
    )
    grad_input, shared0 = run(
        part(last_step, lower),
        "last_step",
        (add_everywhere(stats), grad_out0, grad_u0, ordered, norm0, norm_gain),
        (flat, shared),
        (((width // LANES, rows, LANES), f32),),
        scalars=0,
    )
    small_sum = add_everywhere(jnp.stack([small0, small1]))
    sums1 = lax.psum((grad_b1, grad_c1, grad_w1), everyone)
    sums0 = lax.psum((grad_b0, grad_c0, grad_w0), everyone)
    grad_b, grad_c, grad_w = (jnp.stack(pair) for pair in zip(sums0, sums1))
    _, pullback = jax.vjp(discretize, lam_re, lam_im, log_step)
    grad_lr, grad_li, grad_ls = pullback(tuple(small_sum[:, kind, :half] for kind in range(4)))
    both = jnp.stack([shared0, shared1])
    shape = block_in.shape
    return (
        block_out.reshape(shape), grad_input.reshape(shape), both[:, 0], both[:, 1],
        grad_ls, grad_lr, grad_li, grad_b, grad_c, small_sum[:, 4], grad_w,
    )


def solution(mesh):
    split = P(None, "dp", "seq", None)
    return jax.shard_map(
        per_device,
        mesh=mesh,
        in_specs=(split, split, P(None, "dp", None)) + (P(),) * 9,
        out_specs=(split, split) + (P(),) * 9,
        check_vma=False,
    )
```

```python
import functools

import jax
import jax.numpy as jnp
from jax import lax
from jax.experimental import pallas as pl
from jax.experimental.pallas import tpu as pltpu
from jax.sharding import PartitionSpec as P

f32, bf16 = jnp.float32, jnp.bfloat16
epsilon = 1e-05
tanh_scale = 0.7978845608028654
cubic_term = 0.044715
LANES = 128
CHUNKS = 8
ROWS = 32
VMEM_LIMIT = 48 * 1024 * 1024


def dot(left, right, contract=(1, 0)):
    return lax.dot_general(
        left, right, (((contract[0],), (contract[1],)), ((), ())), preferred_element_type=f32
    )


def reorder(span, inverse):
    shape = (span, span)
    kept, moved = (1, 0) if inverse else (0, 1)
    row = lax.broadcasted_iota(jnp.int32, shape, kept)
    position = lax.broadcasted_iota(jnp.int32, shape, moved)
    source = (row & (CHUNKS - 1)) * (span // CHUNKS) + (row >> 3)
    return jnp.where(position == source, 1.0, 0.0).astype(bf16)


def row_loop(count, body, init=0, step=ROWS):
    def one(index, carry):
        return body(pl.multiple_of(index * step, step), carry)

    return lax.fori_loop(0, count // step, one, init)


META = 12


def keep_of(meta, batch, base, step, backward):
    off = 4 if backward else 0
    late = 1 if backward else 0
    stop = base == meta[batch, off] - step - late
    for doc in range(1, 4):
        stop = jnp.logical_or(stop, base == meta[batch, off + doc] - step - late)
    return jnp.where(stop, 0.0, 1.0)


def base_positions(meta, steps):
    return meta[0, 10] + lax.broadcasted_iota(jnp.int32, (CHUNKS, LANES), 0) * steps


def lanes_of(index, half=0):
    return slice(half + index * LANES, half + (index + 1) * LANES)


def coef_tiles(disc, row, groups, conj=False):
    out = []
    for q in range(groups):
        re = jnp.broadcast_to(disc[row : row + 1, lanes_of(q)], (CHUNKS, LANES))
        im = jnp.broadcast_to(disc[row + 1 : row + 2, lanes_of(q)], (CHUNKS, LANES))
        out.append((re, -im if conj else im))
    return out


def times(a, b):
    return (a[0] * b[0] - a[1] * b[1], a[0] * b[1] + a[1] * b[0])


def scan(meta, source, inject, dec, batches, span, groups, reverse, masks_reverse, init, extra, visit):
    steps = span // CHUNKS
    half = groups * LANES
    base = base_positions(meta, steps)

    def pair(index, carry):
        states, more = carry
        states = list(states)
        first = steps - 2 - 2 * index if reverse else 2 * index
        start = pl.multiple_of(first * CHUNKS, 2 * CHUNKS)
        order = (1, 0) if reverse else (0, 1)
        for batch in range(batches):
            keeps = [keep_of(meta, batch, base, first + j, masks_reverse) for j in (0, 1)]
            for q in range(groups):
                rows = pl.ds(batch * span + start, 2 * CHUNKS)
                src_re = source[rows, lanes_of(q)]
                src_im = source[rows, lanes_of(q, half)]
                state = states[batch * groups + q]
                found = [None, None]
                for j in order:
                    part = (
                        src_re[j * CHUNKS : (j + 1) * CHUNKS],
                        src_im[j * CHUNKS : (j + 1) * CHUNKS],
                    )
                    push = times(inject[q], part) if inject is not None else part
                    held = times((keeps[j] * dec[q][0], keeps[j] * dec[q][1]), state)
                    state = (held[0] + push[0], held[1] + push[1])
                    found[j] = state
                states[batch * groups + q] = state
                more = visit(more, batch, q, first, start, found, (src_re, src_im))
            more = visit(more, batch, None, first, start, keeps, None)
        return tuple(states), more

    return lax.fori_loop(0, steps // 2, pair, (tuple(init), extra), unroll=2)


def zero_states(batches, groups):
    zero = jnp.zeros((CHUNKS, LANES), f32)
    return [(zero, zero)] * (batches * groups)


def local_ends(meta, source, inject, dec, dec_chunk, batches, span, groups, reverse, prefix, total):
    ones = tuple(jnp.ones((CHUNKS, LANES), f32) for _ in range(batches))

    def visit(more, batch, q, first, start, found, src):
        if q is not None:
            return more
        return tuple(
            value * found[0] * found[1] if at == batch else value for at, value in enumerate(more)
        )

    ends, kept = scan(
        meta, source, inject, dec, batches, span, groups, reverse, reverse,
        zero_states(batches, groups), ones, visit,
    )
    half = groups * LANES
    row = lax.broadcasted_iota(jnp.int32, (CHUNKS, LANES), 0)
    for batch in range(batches):
        for q in range(groups):
            end = ends[batch * groups + q]
            decay = (kept[batch] * dec_chunk[q][0], kept[batch] * dec_chunk[q][1])
            for shift in (1, 2, 4):
                turn = CHUNKS - shift if reverse else shift
                valid = row < CHUNKS - shift if reverse else row >= shift
                before = [pltpu.roll(value, turn, 0) for value in (*end, *decay)]
                from_before = times(decay, (before[0], before[1]))
                end = (
                    end[0] + jnp.where(valid, from_before[0], 0.0),
                    end[1] + jnp.where(valid, from_before[1], 0.0),
                )
                longer = times(decay, (before[2], before[3]))
                decay = (
                    jnp.where(valid, longer[0], decay[0]),
                    jnp.where(valid, longer[1], decay[1]),
                )
            rows = slice(batch * CHUNKS, (batch + 1) * CHUNKS)
            prefix[0, rows, lanes_of(q)] = end[0]
            prefix[0, rows, lanes_of(q, half)] = end[1]
            prefix[1, rows, lanes_of(q)] = decay[0]
            prefix[1, rows, lanes_of(q, half)] = decay[1]
            last = 0 if reverse else CHUNKS - 1
            total[batch : batch + 1, lanes_of(q)] = end[0][last : last + 1]
            total[batch : batch + 1, lanes_of(q, half)] = end[1][last : last + 1]


def chunk_carries(meta, gathered, disc, prefix, batches, span, groups, reverse, conj):
    count = gathered.shape[0]
    half = groups * LANES
    dec_re = disc[6:7, :]
    dec_im = -disc[7:8, :] if conj else disc[7:8, :]
    row = lax.broadcasted_iota(jnp.int32, (CHUNKS, LANES), 0)
    mine = meta[0, 11]
    out = []
    for batch in range(batches):

        def add(at, so_far, batch=batch):
            away = count - 2 - at
            if reverse:
                other = mine + 1 + away
                reaches = meta[batch, 9] > other * span
            else:
                other = mine - 1 - away
                reaches = meta[batch, 8] < (mine - away) * span
            other = jnp.clip(other, 0, count - 1)
            value = jnp.where(reaches, gathered[other, pl.ds(batch, 1), :], 0.0)
            moved = times((dec_re, dec_im), so_far)
            return (moved[0] + value[:, :half], moved[1] + value[:, half:])

        zero = jnp.zeros((1, half), f32)
        enter = lax.fori_loop(0, count - 1, add, (zero, zero), unroll=count <= 8)
        rows = slice(batch * CHUNKS, (batch + 1) * CHUNKS)
        for q in range(groups):
            own = tuple(jnp.broadcast_to(part[:, lanes_of(q)], (CHUNKS, LANES)) for part in enter)
            end = (prefix[0, rows, lanes_of(q)], prefix[0, rows, lanes_of(q, half)])
            decay = (prefix[1, rows, lanes_of(q)], prefix[1, rows, lanes_of(q, half)])
            moved = times(decay, own)
            turn, first = (CHUNKS - 1, CHUNKS - 1) if reverse else (1, 0)
            out.append(
                tuple(
                    jnp.where(row == first, own[i], pltpu.roll(end[i] + moved[i], turn, 0))
                    for i in (0, 1)
                )
            )
    return out


def add_sums(target, batches, sums):
    for kind, per_batch in enumerate(sums):
        for batch in range(batches):
            target[kind * batches + batch : kind * batches + batch + 1, :] = jnp.sum(
                per_batch[batch], axis=0, keepdims=True
            )


def fold(value):
    return sum(value[i : i + CHUNKS] for i in range(CHUNKS, value.shape[0], CHUNKS)) + value[:CHUNKS]


def first_sums(batches, span, x, ordered, stats):
    turn = reorder(span, False)
    width = x.shape[1]
    sums, squares = [], []
    for batch in range(batches):
        rows = slice(batch * span, (batch + 1) * span)
        ordered[rows, :] = dot(turn, x[rows, :]).astype(bf16)

        def body(start, carry, batch=batch):
            value = x[pl.ds(batch * span + start, ROWS), :].astype(f32)
            return carry[0] + fold(value), carry[1] + fold(value * value)

        zero = jnp.zeros((CHUNKS, width), f32)
        one, two = row_loop(span, body, (zero, zero))
        sums.append(one)
        squares.append(two)
    add_sums(stats, batches, (sums, squares))


def enter_layer(
    cfg, meta, stats, hidden, gain, shift, disc, b_proj, u, drive, prefix, total, norm
):
    layer, reverse, batches, span, groups, tokens = cfg
    sums = stats[...]
    average = sums[:batches] / tokens
    spread = sums[batches:] / tokens - average * average
    scale = lax.rsqrt(spread + epsilon)
    norm[:batches, :] = average
    norm[batches:, :] = scale
    gain_now, shift_now = gain[layer : layer + 1, :], shift[layer : layer + 1, :]
    for batch in range(batches):

        def body(start, carry, batch=batch):
            rows = pl.ds(batch * span + start, ROWS)
            normed = (hidden[rows, :].astype(f32) - average[batch : batch + 1]) * scale[
                batch : batch + 1
            ]
            u[rows, :] = (normed * gain_now + shift_now).astype(bf16)
            return carry

        row_loop(span, body)
    drive[...] = dot(u[...], b_proj[...])
    now = disc.at[layer]
    local_ends(
        meta, drive, coef_tiles(now, 2, groups), coef_tiles(now, 0, groups),
        coef_tiles(now, 4, groups), batches, span, groups, reverse, prefix, total,
    )


def finish_states(cfg, meta, ends, prefix, disc, drive, states, states_low):
    layer, reverse, batches, span, groups, tokens = cfg
    half = groups * LANES
    padded = span + CHUNKS
    now = disc.at[layer]
    init = chunk_carries(meta, ends, now, prefix, batches, span, groups, reverse, False)
    for batch in range(batches):
        edge = batch * padded + (span if reverse else 0)
        for q in range(groups):
            states[edge : edge + CHUNKS, lanes_of(q)] = init[batch * groups + q][0]
            states[edge : edge + CHUNKS, lanes_of(q, half)] = init[batch * groups + q][1]

    def visit(more, batch, q, first, start, found, src):
        if q is not None:
            for part, off in ((0, 0), (1, half)):
                both = jnp.concatenate([found[0][part], found[1][part]], axis=0)
                at = batch * padded + (0 if reverse else CHUNKS)
                states[pl.ds(at + start, 2 * CHUNKS), lanes_of(q, off)] = both
                states_low[pl.ds(batch * span + start, 2 * CHUNKS), lanes_of(q, off)] = both.astype(
                    bf16
                )
        return more

    scan(
        meta, drive, coef_tiles(now, 2, groups), coef_tiles(now, 0, groups), batches, span, groups,
        reverse, reverse, init, 0, visit,
    )


def forward_finish(
    cfg, meta, ends, prefix, disc, drive, u, hidden, c_proj, d_skip, w_gate,
    states, states_low, act, sig, slope, result, wide, emit,
):
    layer, reverse, batches, span, groups, tokens = cfg
    finish_states(cfg, meta, ends, prefix, disc, drive, states, states_low)
    wide[...] = dot(states_low[...], c_proj[...])
    skip = d_skip[layer : layer + 1, :]

    def body(start, carry):
        rows = pl.ds(start, ROWS)
        mixed = wide[rows, :] + skip * u[rows, :].astype(f32)
        square = mixed * mixed
        th = jnp.tanh(tanh_scale * (mixed + cubic_term * square * mixed))
        half_one = 0.5 * (1.0 + th)
        act[rows, :] = (mixed * half_one).astype(bf16)
        slope[rows, :] = half_one + 0.5 * mixed * (1.0 - th * th) * tanh_scale * (
            1.0 + 3.0 * cubic_term * square
        )
        return carry

    row_loop(batches * span, body)
    wide[...] = dot(act[...], w_gate[...])
    sums, squares = [], []
    for batch in range(batches):

        def gate(start, carry, batch=batch):
            rows = pl.ds(batch * span + start, ROWS)
            sig_now = 0.5 + 0.5 * jnp.tanh(0.5 * wide[rows, :])
            sig[rows, :] = sig_now
            value = hidden[rows, :].astype(f32) + act[rows, :].astype(f32) * sig_now
            result[rows, :] = value.astype(result.dtype)
            if emit is None:
                return carry
            return carry[0] + fold(value), carry[1] + fold(value * value)

        zero = jnp.zeros((CHUNKS, wide.shape[1]), f32)
        one, two = row_loop(span, gate, (zero, zero))
        sums.append(one)
        squares.append(two)
    if emit is not None:
        add_sums(emit, batches, (sums, squares))


def backward_start(
    cfg, meta, grad_out, disc, u, c_proj, w_gate, states_low, act, sig, slope,
    grad_gate, grad_mixed, grad_low, source, prefix, total, grad_d, wide,
):
    layer, reverse, batches, span, groups, tokens = cfg

    def body(start, carry):
        rows = pl.ds(start, ROWS)
        sig_now = sig[rows, :]
        grad_gate[rows, :] = (
            grad_out[rows, :].astype(f32) * act[rows, :].astype(f32) * sig_now * (1.0 - sig_now)
        ).astype(bf16)
        return carry

    row_loop(batches * span, body)
    wide[...] = dot(grad_gate[...], w_gate[...], (1, 1))

    def mixed(start, carry):
        rows = pl.ds(start, ROWS)
        value = (grad_out[rows, :].astype(f32) * sig[rows, :] + wide[rows, :]) * slope[rows, :]
        grad_mixed[rows, :] = value
        grad_low[rows, :] = value.astype(bf16)
        return carry + fold(value * u[rows, :].astype(f32))

    gd = row_loop(batches * span, mixed, jnp.zeros((CHUNKS, wide.shape[1]), f32))
    grad_d[...] = jnp.sum(gd, axis=0, keepdims=True)
    source[...] = dot(grad_low[...], c_proj[...], (1, 1))
    now = disc.at[layer]
    local_ends(
        meta, source, None, coef_tiles(now, 0, groups, True), coef_tiles(now, 4, groups, True),
        batches, span, groups, not reverse, prefix, total,
    )


def middle_forward(
    cfg, meta, ends, prefix, disc, drive, u, hidden, c_proj, d_skip, w_gate,
    states, states_low, act, sig, slope, result, stats, wide,
):
    forward_finish(
        cfg, meta, ends, prefix, disc, drive, u, hidden, c_proj, d_skip, w_gate,
        states, states_low, act, sig, slope, result, wide, stats,
    )


def turn_around(
    cfg, meta, ends, prefix, disc, drive, u, hidden, c_proj, d_skip, w_gate, cotangent,
    block_out, ordered_cot, states, states_low, act, grad_gate, grad_mixed, grad_low, source,
    back_prefix, total, grad_d, sig, slope, wide, result,
):
    layer, reverse, batches, span, groups, tokens = cfg
    turn, back = reorder(span, False), reorder(span, True)
    for batch in range(batches):
        rows = slice(batch * span, (batch + 1) * span)
        ordered_cot[rows, :] = dot(turn, cotangent[rows, :]).astype(bf16)
    forward_finish(
        cfg, meta, ends, prefix, disc, drive, u, hidden, c_proj, d_skip, w_gate,
        states, states_low, act, sig, slope, result, wide, None,
    )
    for batch in range(batches):
        rows = slice(batch * span, (batch + 1) * span)
        block_out[rows, :] = dot(back, result[rows, :]).astype(bf16)
    backward_start(
        cfg, meta, ordered_cot, disc, u, c_proj, w_gate, states_low, act, sig, slope,
        grad_gate, grad_mixed, grad_low, source, back_prefix, total, grad_d, wide,
    )


def backward_finish(
    cfg, meta, ends, prefix, disc, source, drive, states, u, grad_mixed, grad_d, hidden, norm,
    d_skip, b_proj, grad_proj, grad_u, stats, small,
):
    layer, reverse, batches, span, groups, tokens = cfg
    half = groups * LANES
    padded = span + CHUNKS
    steps = span // CHUNKS
    now = disc.at[layer]
    init = chunk_carries(meta, ends, now, prefix, batches, span, groups, not reverse, True)
    inj = coef_tiles(now, 2, groups)
    base = base_positions(meta, steps)
    zero = jnp.zeros((CHUNKS, LANES), f32)

    def visit(more, batch, q, first, start, found, src):
        if q is None:
            return more
        more = list(more)
        rows = pl.ds(batch * span + start, 2 * CHUNKS)
        drive_re, drive_im = drive[rows, lanes_of(q)], drive[rows, lanes_of(q, half)]
        before = pl.ds(batch * padded + start + (CHUNKS if reverse else 0), 2 * CHUNKS)
        prior_re, prior_im = states[before, lanes_of(q)], states[before, lanes_of(q, half)]
        dec_re, dec_im, inj_re, inj_im = more[q]
        out_re, out_im = [], []
        for j in (0, 1):
            part = slice(j * CHUNKS, (j + 1) * CHUNKS)
            adj_re, adj_im = found[j]
            keep = keep_of(meta, batch, base, first + j, reverse)
            kept_re, kept_im = keep * adj_re, keep * adj_im
            dec_re = dec_re + kept_re * prior_re[part] + kept_im * prior_im[part]
            dec_im = dec_im + kept_im * prior_re[part] - kept_re * prior_im[part]
            inj_re = inj_re + adj_re * drive_re[part] + adj_im * drive_im[part]
            inj_im = inj_im + adj_im * drive_re[part] - adj_re * drive_im[part]
            out_re.append(inj[q][0] * adj_re + inj[q][1] * adj_im)
            out_im.append(inj[q][0] * adj_im - inj[q][1] * adj_re)
        grad_proj[rows, lanes_of(q)] = jnp.concatenate(out_re, axis=0).astype(bf16)
        grad_proj[rows, lanes_of(q, half)] = jnp.concatenate(out_im, axis=0).astype(bf16)
        more[q] = (dec_re, dec_im, inj_re, inj_im)
        return tuple(more)

    _, sums = scan(
        meta, source, None, coef_tiles(now, 0, groups, True), batches, span, groups,
        not reverse, not reverse, init, ((zero,) * 4,) * groups, visit,
    )
    small[...] = jnp.zeros_like(small)
    for q in range(groups):
        for kind in range(4):
            small[kind : kind + 1, lanes_of(q)] = jnp.sum(sums[q][kind], axis=0, keepdims=True)
    small[4:5, :] = grad_d[...]
    grad_u[...] = dot(grad_proj[...], b_proj[...], (1, 1))
    skip = d_skip[layer : layer + 1, :]
    plain, times_normed = [], []
    for batch in range(batches):
        average = norm[batch : batch + 1, :]
        scale = norm[batches + batch : batches + batch + 1, :]

        def body(start, carry, batch=batch, average=average, scale=scale):
            rows = pl.ds(batch * span + start, ROWS)
            value = grad_u[rows, :] + grad_mixed[rows, :] * skip
            grad_u[rows, :] = value
            normed = (hidden[rows, :].astype(f32) - average) * scale
            return carry[0] + fold(value), carry[1] + fold(value * normed)

        zero_sum = jnp.zeros((CHUNKS, grad_u.shape[1]), f32)
        one, two = row_loop(span, body, (zero_sum, zero_sum))
        plain.append(one)
        times_normed.append(two)
    add_sums(stats, batches, (plain, times_normed))


def norm_backward(cfg, stats, grad_out, grad_u, hidden, norm, gain, store, shared):
    layer, reverse, batches, span, groups, tokens = cfg
    sums = stats[...]
    shared[0:1, :] = jnp.sum(sums[batches:], axis=0, keepdims=True)
    shared[1:2, :] = jnp.sum(sums[:batches], axis=0, keepdims=True)
    gain_now = gain[layer : layer + 1, :]
    for batch in range(batches):
        average = norm[batch : batch + 1, :]
        scale = norm[batches + batch : batches + batch + 1, :]
        plain = gain_now * sums[batch : batch + 1] / tokens
        slanted = gain_now * sums[batches + batch : batches + batch + 1] / tokens

        def body(start, carry, batch=batch, average=average, scale=scale, plain=plain, slanted=slanted):
            rows = pl.ds(batch * span + start, ROWS)
            normed = (hidden[rows, :].astype(f32) - average) * scale
            value = grad_out[rows, :].astype(f32) + scale * (
                grad_u[rows, :] * gain_now - plain - normed * slanted
            )
            store(rows, value)
            return carry

        row_loop(span, body)


def between_layers(
    cfg, lower, meta, stats, upper_out, upper_u, upper_hidden, upper_norm, gain,
    disc, u, c_proj, w_gate, states_low, act, sig, slope,
    grad_out, shared, grad_gate, grad_mixed, grad_low, source, prefix, total, grad_d, wide,
):
    def store(rows, value):
        grad_out[rows, :] = value

    norm_backward(cfg, stats, upper_out, upper_u, upper_hidden, upper_norm, gain, store, shared)
    backward_start(
        lower, meta, grad_out, disc, u, c_proj, w_gate, states_low, act, sig, slope,
        grad_gate, grad_mixed, grad_low, source, prefix, total, grad_d, wide,
    )


def last_step(cfg, stats, grad_out, grad_u, hidden, norm, gain, target, shared, ordered):
    layer, reverse, batches, span, groups, tokens = cfg
    planes = target.shape[1] // LANES

    def store(rows, value):
        for plane in range(planes):
            ordered[plane, rows, :] = value[:, lanes_of(plane)]

    norm_backward(cfg, stats, grad_out, grad_u, hidden, norm, gain, store, shared)
    steps = span // CHUNKS
    for batch in range(batches):
        for chunk in range(CHUNKS):
            at = batch * span
            for plane in range(planes):
                target[at + chunk * steps : at + (chunk + 1) * steps, lanes_of(plane)] = ordered[
                    plane, pl.ds(at + chunk, steps, stride=CHUNKS), :
                ]


def gate_weights(act, grad_gate, states_low, grad_low, grad_wc):
    width = act.shape[1]
    grad_wc[:width, :] = dot(act[...], grad_gate[...], (0, 0))
    grad_wc[width:, :] = dot(states_low[...], grad_low[...], (0, 0))


def input_weights(u, grad_proj, grad_b):
    grad_b[...] = dot(u[...], grad_proj[...], (0, 0))


def run(body, name, args, outs, scratch=(), scalars=1, flops=0, touched=0):
    specs = [pl.BlockSpec(memory_space=pltpu.SMEM)] * scalars
    specs += [pl.BlockSpec(memory_space=pltpu.VMEM)] * (len(args) - scalars)
    return pl.pallas_call(
        body,
        name=name,
        out_shape=tuple(jax.ShapeDtypeStruct(*out) for out in outs),
        in_specs=specs,
        out_specs=tuple(pl.BlockSpec(memory_space=pltpu.VMEM) for _ in outs),
        scratch_shapes=[pltpu.VMEM(*entry) for entry in scratch],
        compiler_params=pltpu.CompilerParams(vmem_limit_bytes=VMEM_LIMIT),
    )(*args)


def add_everywhere(value):
    for axis in ("seq", "dp"):
        size = lax.axis_size(axis)
        found = [
            lax.ppermute(value, axis, [(i, (i + away) % size) for i in range(size)])
            for away in range(1, size)
        ]
        value = sum(found, value)
    return value


def axis_parts():
    count = lax.axis_size("seq")
    mine = lax.axis_index("seq")
    outer = 1
    while outer * outer * 2 < count:
        outer *= 2
    inner = count // (2 * outer)
    parts = []
    for size, stride in ((2, 1), (inner, 2), (outer, 2 * inner)):
        parts.append(("seq", size, stride, count, (mine // stride) % size))
    size = lax.axis_size("dp")
    parts.append(("dp", size, 1, size, lax.axis_index("dp")))
    return parts


def shifted(value, part, away):
    name, size, stride, count, mine = part
    pairs = []
    for i in range(count):
        place = (i // stride) % size
        pairs.append((i, i + ((place + away) % size - place) * stride))
    return lax.ppermute(value, name, pairs)


def scatter_sum(value, part):
    name, size, stride, count, mine = part
    rows = value.shape[-2] // size

    def piece(place):
        return lax.dynamic_slice_in_dim(value, place * rows, rows, axis=value.ndim - 2)

    found = [shifted(piece((mine + away) % size), part, away) for away in range(1, size)]
    return sum(found, piece(mine))


def gather_rows(value, part):
    name, size, stride, count, mine = part
    axis = value.ndim - 2
    rows = value.shape[axis]
    found = [value] + [shifted(value, part, away) for away in range(1, size)]
    if size == 2:
        low = jnp.where(mine == 0, found[0], found[1])
        high = jnp.where(mine == 0, found[1], found[0])
        return jnp.concatenate([low, high], axis=axis)
    shape = value.shape[:axis] + (rows * size,) + value.shape[axis + 1 :]
    out = jnp.zeros(shape, value.dtype)
    for away in range(size):
        out = lax.dynamic_update_slice_in_dim(
            out, found[away], ((mine - away) % size) * rows, axis=axis
        )
    return out


def sum_over_links(value):
    core, inner, outer, depth = axis_parts()
    own = scatter_sum(value, core)
    cols = own.shape[1] // 2
    left, right = own[:, :cols], own[:, cols:]
    left, right = scatter_sum(left, inner), scatter_sum(right, outer)
    left, right = scatter_sum(left, outer), scatter_sum(right, inner)
    both = gather_rows(scatter_sum(jnp.stack([left, right]), depth), depth)
    left, right = both[0], both[1]
    left, right = gather_rows(left, outer), gather_rows(right, inner)
    left, right = gather_rows(left, inner), gather_rows(right, outer)
    return gather_rows(jnp.concatenate([left, right], axis=1), core)


def discretize(lam_re, lam_im, log_step):
    step_size = jnp.exp(log_step)
    decay_abs = jnp.exp(lam_re * step_size)
    rotation = lam_im * step_size
    dec_re = decay_abs * jnp.cos(rotation)
    dec_im = decay_abs * jnp.sin(rotation)
    denom_sq = lam_re * lam_re + lam_im * lam_im
    inj_re = ((dec_re - 1.0) * lam_re + dec_im * lam_im) / denom_sq
    inj_im = (dec_im * lam_re - (dec_re - 1.0) * lam_im) / denom_sq
    return (dec_re, dec_im, inj_re, inj_im)


def power(value, doublings):
    for _ in range(doublings):
        value = times(value, value)
    return value


def per_device(
    block_in, cotangent, doc_lengths, norm_gain, norm_shift, log_step, lam_re, lam_im,
    b_proj, c_proj, d_skip, w_gate,
):
    batches, seqs, span, width = block_in.shape
    assert seqs == 1 and span % (4 * CHUNKS) == 0
    half = lam_re.shape[1]
    groups = half // LANES
    rows = batches * span
    everyone = ("dp", "seq")
    chunk_doublings = (span // CHUNKS).bit_length() - 1
    span_doublings = span.bit_length() - 1
    assert 1 << span_doublings == span
    tokens = float(seqs * lax.axis_size("dp") * span * lax.axis_size("seq"))
    mine = lax.axis_index("seq")
    lengths = doc_lengths[:, 0, :]
    ends = jnp.cumsum(lengths, axis=-1).astype(jnp.int32)
    begins = ends - lengths
    first = mine * span
    before = jnp.max(jnp.where(begins < first, begins, 0), axis=-1)
    whole = span * lax.axis_size("seq")
    after = jnp.min(jnp.where(ends > first + span, ends, 2 * whole), axis=-1)
    after = jnp.where(first + span < whole, after, 0)
    spot = jnp.broadcast_to(jnp.stack([first, mine])[None], (batches, 2))
    meta = jnp.concatenate([begins, ends, before[:, None], after[:, None], spot], axis=-1).astype(
        jnp.int32
    )
    dec_re, dec_im, inj_re, inj_im = discretize(lam_re, lam_im, log_step)
    dec_chunk = power((dec_re, dec_im), chunk_doublings)
    dec_span = power(dec_chunk, span_doublings - chunk_doublings)
    disc = jnp.stack([dec_re, dec_im, inj_re, inj_im, *dec_chunk, *dec_span], axis=1)

    x = block_in.reshape(rows, width)
    cot = cotangent.reshape(rows, width)
    lower = (0, False, batches, span, groups, tokens)
    upper = (1, True, batches, span, groups, tokens)
    part = functools.partial

    flat, low = ((rows, width), f32), ((rows, width), bf16)
    wide, wide_low = ((rows, 2 * half), f32), ((rows, 2 * half), bf16)
    padded = ((batches * (span + CHUNKS), 2 * half), f32)
    sums = ((2 * batches, width), f32)
    prefix = ((2, batches * CHUNKS, 2 * half), f32)
    total = ((batches, 2 * half), f32)
    line, shared = ((1, width), f32), ((2, width), f32)
    small = ((8, width), f32)

    def gather_row(value):
        return lax.all_gather(value, "seq")

    ordered, stats = run(
        part(first_sums, batches, span), "first_sums", (x,), (low, sums), scalars=0
    )

    def forward(cfg, hidden, stats):
        layer = cfg[0]
        return run(
            part(enter_layer, cfg),
            "enter_layer",
            (meta, add_everywhere(stats), hidden, norm_gain, norm_shift, disc, b_proj[layer]),
            (low, wide, prefix, total, sums),
        )

    u0, drive0, prefix0, total0, norm0 = forward(lower, ordered, stats)
    states0, states_low0, act0, sig0, slope0, hidden1, stats = run(
        part(middle_forward, lower),
        "middle_forward",
        (
            meta, gather_row(total0), prefix0, disc, drive0, u0, ordered, c_proj[0], d_skip,
            w_gate[0],
        ),
        (padded, wide_low, low, flat, flat, flat, sums),
        (flat,),
    )
    u1, drive1, prefix1, total1, norm1 = forward(upper, hidden1, stats)
    (
        block_out, ordered_cot, states1, states_low1, act1, grad_gate1, grad_mixed1, grad_low1,
        source1, prefix1, total1, grad_d1,
    ) = run(
        part(turn_around, upper),
        "turn_around",
        (
            meta, gather_row(total1), prefix1, disc, drive1, u1, hidden1, c_proj[1], d_skip,
            w_gate[1], cot,
        ),
        (low, low, padded, wide_low, low, low, flat, low, wide, prefix, total, line),
        (flat, flat, flat, low),
    )
    (grad_wc1,) = run(
        gate_weights, "gate_weights", (act1, grad_gate1, states_low1, grad_low1),
        (((width + 2 * half, width), f32),), scalars=0,
    )

    def finish(cfg, total, prefix, source, drive, states, u, grad_mixed, grad_d, hidden, norm):
        return run(
            part(backward_finish, cfg),
            "backward_finish",
            (
                meta, gather_row(total), prefix, disc, source, drive, states, u, grad_mixed,
                grad_d, hidden, norm, d_skip, b_proj[cfg[0]],
            ),
            (wide_low, flat, sums, small),
        )

    grad_proj1, grad_u1, stats, small1 = finish(
        upper, total1, prefix1, source1, drive1, states1, u1, grad_mixed1, grad_d1, hidden1, norm1
    )
    (grad_b1,) = run(
        input_weights, "input_weights", (u1, grad_proj1), (((width, 2 * half), f32),), scalars=0
    )
    sum_wc1, sum_b1 = lax.psum((grad_wc1, grad_b1), everyone)
    (
        grad_out0, shared1, grad_gate0, grad_mixed0, grad_low0, source0, prefix0, total0, grad_d0,
    ) = run(
        part(between_layers, upper, lower),
        "between_layers",
        (
            meta, add_everywhere(stats), ordered_cot, grad_u1, hidden1, norm1, norm_gain,
            disc, u0, c_proj[0], w_gate[0], states_low0, act0, sig0, slope0,
        ),
        (flat, shared, low, flat, low, wide, prefix, total, line),
        (flat,),
    )
    (grad_wc0,) = run(
        gate_weights, "gate_weights", (act0, grad_gate0, states_low0, grad_low0),
        (((width + 2 * half, width), f32),), scalars=0,
    )
    grad_proj0, grad_u0, stats, small0 = finish(
        lower, total0, prefix0, source0, drive0, states0, u0, grad_mixed0, grad_d0, ordered, norm0
    )
    (grad_b0,) = run(
        input_weights, "input_weights", (u0, grad_proj0), (((width, 2 * half), f32),), scalars=0
    )
    grad_input, shared0 = run(
        part(last_step, lower),
        "last_step",
        (add_everywhere(stats), grad_out0, grad_u0, ordered, norm0, norm_gain),
        (flat, shared),
        (((width // LANES, rows, LANES), f32),),
        scalars=0,
    )
    small_sum = add_everywhere(jnp.stack([small0, small1]))
    sum_wc0, sum_b0 = sum_over_links(grad_wc0), sum_over_links(grad_b0)
    grad_b = jnp.stack([sum_b0, sum_b1])
    grad_w = jnp.stack([sum_wc0[:width], sum_wc1[:width]])
    grad_c = jnp.stack([sum_wc0[width:], sum_wc1[width:]])
    _, pullback = jax.vjp(discretize, lam_re, lam_im, log_step)
    grad_lr, grad_li, grad_ls = pullback(tuple(small_sum[:, kind, :half] for kind in range(4)))
    both = jnp.stack([shared0, shared1])
    shape = block_in.shape
    return (
        block_out.reshape(shape), grad_input.reshape(shape), both[:, 0], both[:, 1],
        grad_ls, grad_lr, grad_li, grad_b, grad_c, small_sum[:, 4], grad_w,
    )


def solution(mesh):
    split = P(None, "dp", "seq", None)
    return jax.shard_map(
        per_device,
        mesh=mesh,
        in_specs=(split, split, P(None, "dp", None)) + (P(),) * 9,
        out_specs=(split, split) + (P(),) * 9,
        check_vma=False,
    )
```

```python
import functools

import jax
import jax.numpy as jnp
from jax import lax
from jax.experimental import pallas as pl
from jax.experimental.pallas import tpu as pltpu
from jax.sharding import PartitionSpec as P

f32, bf16 = jnp.float32, jnp.bfloat16
epsilon = 1e-05
tanh_scale = 0.7978845608028654
cubic_term = 0.044715
LANES = 128
CHUNKS = 8
ROWS = 32
VMEM_LIMIT = 48 * 1024 * 1024


def dot(left, right, contract=(1, 0)):
    return lax.dot_general(
        left, right, (((contract[0],), (contract[1],)), ((), ())), preferred_element_type=f32
    )


def reorder(span, inverse):
    shape = (span, span)
    kept, moved = (1, 0) if inverse else (0, 1)
    row = lax.broadcasted_iota(jnp.int32, shape, kept)
    position = lax.broadcasted_iota(jnp.int32, shape, moved)
    source = (row & (CHUNKS - 1)) * (span // CHUNKS) + (row >> 3)
    return jnp.where(position == source, 1.0, 0.0).astype(bf16)


def row_loop(count, body, init=0, step=ROWS):
    def one(index, carry):
        return body(pl.multiple_of(index * step, step), carry)

    return lax.fori_loop(0, count // step, one, init)


META = 12


def keep_of(meta, batch, base, step, backward):
    off = 4 if backward else 0
    late = 1 if backward else 0
    stop = base == meta[batch, off] - step - late
    for doc in range(1, 4):
        stop = jnp.logical_or(stop, base == meta[batch, off + doc] - step - late)
    return jnp.where(stop, 0.0, 1.0)


def base_positions(meta, steps):
    return meta[0, 10] + lax.broadcasted_iota(jnp.int32, (CHUNKS, LANES), 0) * steps


def lanes_of(index, half=0):
    return slice(half + index * LANES, half + (index + 1) * LANES)


def coef_tiles(disc, row, groups, conj=False):
    out = []
    for q in range(groups):
        re = jnp.broadcast_to(disc[row : row + 1, lanes_of(q)], (CHUNKS, LANES))
        im = jnp.broadcast_to(disc[row + 1 : row + 2, lanes_of(q)], (CHUNKS, LANES))
        out.append((re, -im if conj else im))
    return out


def times(a, b):
    return (a[0] * b[0] - a[1] * b[1], a[0] * b[1] + a[1] * b[0])


def scan(meta, source, inject, dec, batches, span, groups, reverse, masks_reverse, init, extra, visit):
    steps = span // CHUNKS
    half = groups * LANES
    base = base_positions(meta, steps)

    def pair(index, carry):
        states, more = carry
        states = list(states)
        first = steps - 2 - 2 * index if reverse else 2 * index
        start = pl.multiple_of(first * CHUNKS, 2 * CHUNKS)
        order = (1, 0) if reverse else (0, 1)
        for batch in range(batches):
            keeps = [keep_of(meta, batch, base, first + j, masks_reverse) for j in (0, 1)]
            for q in range(groups):
                rows = pl.ds(batch * span + start, 2 * CHUNKS)
                src_re = source[rows, lanes_of(q)]
                src_im = source[rows, lanes_of(q, half)]
                state = states[batch * groups + q]
                found = [None, None]
                for j in order:
                    part = (
                        src_re[j * CHUNKS : (j + 1) * CHUNKS],
                        src_im[j * CHUNKS : (j + 1) * CHUNKS],
                    )
                    push = times(inject[q], part) if inject is not None else part
                    held = times((keeps[j] * dec[q][0], keeps[j] * dec[q][1]), state)
                    state = (held[0] + push[0], held[1] + push[1])
                    found[j] = state
                states[batch * groups + q] = state
                more = visit(more, batch, q, first, start, found, (src_re, src_im))
            more = visit(more, batch, None, first, start, keeps, None)
        return tuple(states), more

    return lax.fori_loop(0, steps // 2, pair, (tuple(init), extra), unroll=2)


def zero_states(batches, groups):
    zero = jnp.zeros((CHUNKS, LANES), f32)
    return [(zero, zero)] * (batches * groups)


def local_ends(meta, source, inject, dec, dec_chunk, batches, span, groups, reverse, prefix, total):
    ones = tuple(jnp.ones((CHUNKS, LANES), f32) for _ in range(batches))

    def visit(more, batch, q, first, start, found, src):
        if q is not None:
            return more
        return tuple(
            value * found[0] * found[1] if at == batch else value for at, value in enumerate(more)
        )

    ends, kept = scan(
        meta, source, inject, dec, batches, span, groups, reverse, reverse,
        zero_states(batches, groups), ones, visit,
    )
    half = groups * LANES
    row = lax.broadcasted_iota(jnp.int32, (CHUNKS, LANES), 0)
    for batch in range(batches):
        for q in range(groups):
            end = ends[batch * groups + q]
            decay = (kept[batch] * dec_chunk[q][0], kept[batch] * dec_chunk[q][1])
            for shift in (1, 2, 4):
                turn = CHUNKS - shift if reverse else shift
                valid = row < CHUNKS - shift if reverse else row >= shift
                before = [pltpu.roll(value, turn, 0) for value in (*end, *decay)]
                from_before = times(decay, (before[0], before[1]))
                end = (
                    end[0] + jnp.where(valid, from_before[0], 0.0),
                    end[1] + jnp.where(valid, from_before[1], 0.0),
                )
                longer = times(decay, (before[2], before[3]))
                decay = (
                    jnp.where(valid, longer[0], decay[0]),
                    jnp.where(valid, longer[1], decay[1]),
                )
            rows = slice(batch * CHUNKS, (batch + 1) * CHUNKS)
            prefix[0, rows, lanes_of(q)] = end[0]
            prefix[0, rows, lanes_of(q, half)] = end[1]
            prefix[1, rows, lanes_of(q)] = decay[0]
            prefix[1, rows, lanes_of(q, half)] = decay[1]
            last = 0 if reverse else CHUNKS - 1
            total[batch : batch + 1, lanes_of(q)] = end[0][last : last + 1]
            total[batch : batch + 1, lanes_of(q, half)] = end[1][last : last + 1]


def chunk_carries(meta, gathered, disc, prefix, batches, span, groups, reverse, conj):
    count = gathered.shape[0]
    half = groups * LANES
    dec_re = disc[6:7, :]
    dec_im = -disc[7:8, :] if conj else disc[7:8, :]
    row = lax.broadcasted_iota(jnp.int32, (CHUNKS, LANES), 0)
    mine = meta[0, 11]
    out = []
    for batch in range(batches):

        def add(at, so_far, batch=batch):
            away = count - 2 - at
            if reverse:
                other = mine + 1 + away
                reaches = meta[batch, 9] > other * span
            else:
                other = mine - 1 - away
                reaches = meta[batch, 8] < (mine - away) * span
            other = jnp.clip(other, 0, count - 1)
            value = jnp.where(reaches, gathered[other, pl.ds(batch, 1), :], 0.0)
            moved = times((dec_re, dec_im), so_far)
            return (moved[0] + value[:, :half], moved[1] + value[:, half:])

        zero = jnp.zeros((1, half), f32)
        enter = lax.fori_loop(0, count - 1, add, (zero, zero), unroll=count <= 8)
        rows = slice(batch * CHUNKS, (batch + 1) * CHUNKS)
        for q in range(groups):
            own = tuple(jnp.broadcast_to(part[:, lanes_of(q)], (CHUNKS, LANES)) for part in enter)
            end = (prefix[0, rows, lanes_of(q)], prefix[0, rows, lanes_of(q, half)])
            decay = (prefix[1, rows, lanes_of(q)], prefix[1, rows, lanes_of(q, half)])
            moved = times(decay, own)
            turn, first = (CHUNKS - 1, CHUNKS - 1) if reverse else (1, 0)
            out.append(
                tuple(
                    jnp.where(row == first, own[i], pltpu.roll(end[i] + moved[i], turn, 0))
                    for i in (0, 1)
                )
            )
    return out


def add_sums(target, batches, sums):
    for kind, per_batch in enumerate(sums):
        for batch in range(batches):
            target[kind * batches + batch : kind * batches + batch + 1, :] = jnp.sum(
                per_batch[batch], axis=0, keepdims=True
            )


def fold(value):
    return sum(value[i : i + CHUNKS] for i in range(CHUNKS, value.shape[0], CHUNKS)) + value[:CHUNKS]


def first_sums(batches, span, x, ordered, stats):
    turn = reorder(span, False)
    width = x.shape[1]
    sums, squares = [], []
    for batch in range(batches):
        rows = slice(batch * span, (batch + 1) * span)
        ordered[rows, :] = dot(turn, x[rows, :]).astype(bf16)

        def body(start, carry, batch=batch):
            value = x[pl.ds(batch * span + start, ROWS), :].astype(f32)
            return carry[0] + fold(value), carry[1] + fold(value * value)

        zero = jnp.zeros((CHUNKS, width), f32)
        one, two = row_loop(span, body, (zero, zero))
        sums.append(one)
        squares.append(two)
    add_sums(stats, batches, (sums, squares))


def enter_layer(
    cfg, meta, stats, hidden, gain, shift, disc, b_proj, u, drive, prefix, total, norm
):
    layer, reverse, batches, span, groups, tokens = cfg
    sums = stats[...]
    average = sums[:batches] / tokens
    spread = sums[batches:] / tokens - average * average
    scale = lax.rsqrt(spread + epsilon)
    norm[:batches, :] = average
    norm[batches:, :] = scale
    gain_now, shift_now = gain[layer : layer + 1, :], shift[layer : layer + 1, :]
    for batch in range(batches):

        def body(start, carry, batch=batch):
            rows = pl.ds(batch * span + start, ROWS)
            normed = (hidden[rows, :].astype(f32) - average[batch : batch + 1]) * scale[
                batch : batch + 1
            ]
            u[rows, :] = (normed * gain_now + shift_now).astype(bf16)
            return carry

        row_loop(span, body)
    drive[...] = dot(u[...], b_proj[...])
    now = disc.at[layer]
    local_ends(
        meta, drive, coef_tiles(now, 2, groups), coef_tiles(now, 0, groups),
        coef_tiles(now, 4, groups), batches, span, groups, reverse, prefix, total,
    )


def finish_states(cfg, meta, ends, prefix, disc, drive, states, states_low):
    layer, reverse, batches, span, groups, tokens = cfg
    half = groups * LANES
    padded = span + CHUNKS
    now = disc.at[layer]
    init = chunk_carries(meta, ends, now, prefix, batches, span, groups, reverse, False)
    for batch in range(batches):
        edge = batch * padded + (span if reverse else 0)
        for q in range(groups):
            states[edge : edge + CHUNKS, lanes_of(q)] = init[batch * groups + q][0]
            states[edge : edge + CHUNKS, lanes_of(q, half)] = init[batch * groups + q][1]

    def visit(more, batch, q, first, start, found, src):
        if q is not None:
            for part, off in ((0, 0), (1, half)):
                both = jnp.concatenate([found[0][part], found[1][part]], axis=0)
                at = batch * padded + (0 if reverse else CHUNKS)
                states[pl.ds(at + start, 2 * CHUNKS), lanes_of(q, off)] = both
                states_low[pl.ds(batch * span + start, 2 * CHUNKS), lanes_of(q, off)] = both.astype(
                    bf16
                )
        return more

    scan(
        meta, drive, coef_tiles(now, 2, groups), coef_tiles(now, 0, groups), batches, span, groups,
        reverse, reverse, init, 0, visit,
    )


def forward_finish(
    cfg, meta, ends, prefix, disc, drive, u, hidden, c_proj, d_skip, w_gate,
    states, states_low, act, sig, slope, result, wide, emit,
):
    layer, reverse, batches, span, groups, tokens = cfg
    finish_states(cfg, meta, ends, prefix, disc, drive, states, states_low)
    wide[...] = dot(states_low[...], c_proj[...])
    skip = d_skip[layer : layer + 1, :]

    def body(start, carry):
        rows = pl.ds(start, ROWS)
        mixed = wide[rows, :] + skip * u[rows, :].astype(f32)
        square = mixed * mixed
        th = jnp.tanh(tanh_scale * (mixed + cubic_term * square * mixed))
        half_one = 0.5 * (1.0 + th)
        act[rows, :] = (mixed * half_one).astype(bf16)
        slope[rows, :] = half_one + 0.5 * mixed * (1.0 - th * th) * tanh_scale * (
            1.0 + 3.0 * cubic_term * square
        )
        return carry

    row_loop(batches * span, body)
    wide[...] = dot(act[...], w_gate[...])
    sums, squares = [], []
    for batch in range(batches):

        def gate(start, carry, batch=batch):
            rows = pl.ds(batch * span + start, ROWS)
            sig_now = 0.5 + 0.5 * jnp.tanh(0.5 * wide[rows, :])
            sig[rows, :] = sig_now
            value = hidden[rows, :].astype(f32) + act[rows, :].astype(f32) * sig_now
            result[rows, :] = value.astype(result.dtype)
            if emit is None:
                return carry
            return carry[0] + fold(value), carry[1] + fold(value * value)

        zero = jnp.zeros((CHUNKS, wide.shape[1]), f32)
        one, two = row_loop(span, gate, (zero, zero))
        sums.append(one)
        squares.append(two)
    if emit is not None:
        add_sums(emit, batches, (sums, squares))


def backward_start(
    cfg, meta, grad_out, disc, u, c_proj, w_gate, states_low, act, sig, slope,
    grad_gate, grad_mixed, grad_low, source, prefix, total, grad_d, wide,
):
    layer, reverse, batches, span, groups, tokens = cfg

    def body(start, carry):
        rows = pl.ds(start, ROWS)
        sig_now = sig[rows, :]
        grad_gate[rows, :] = (
            grad_out[rows, :].astype(f32) * act[rows, :].astype(f32) * sig_now * (1.0 - sig_now)
        ).astype(bf16)
        return carry

    row_loop(batches * span, body)
    wide[...] = dot(grad_gate[...], w_gate[...], (1, 1))

    def mixed(start, carry):
        rows = pl.ds(start, ROWS)
        value = (grad_out[rows, :].astype(f32) * sig[rows, :] + wide[rows, :]) * slope[rows, :]
        grad_mixed[rows, :] = value
        grad_low[rows, :] = value.astype(bf16)
        return carry + fold(value * u[rows, :].astype(f32))

    gd = row_loop(batches * span, mixed, jnp.zeros((CHUNKS, wide.shape[1]), f32))
    grad_d[...] = jnp.sum(gd, axis=0, keepdims=True)
    source[...] = dot(grad_low[...], c_proj[...], (1, 1))
    now = disc.at[layer]
    local_ends(
        meta, source, None, coef_tiles(now, 0, groups, True), coef_tiles(now, 4, groups, True),
        batches, span, groups, not reverse, prefix, total,
    )


def middle_forward(
    cfg, meta, ends, prefix, disc, drive, u, hidden, c_proj, d_skip, w_gate,
    states, states_low, act, sig, slope, result, stats, wide,
):
    forward_finish(
        cfg, meta, ends, prefix, disc, drive, u, hidden, c_proj, d_skip, w_gate,
        states, states_low, act, sig, slope, result, wide, stats,
    )


def turn_around(
    cfg, meta, ends, prefix, disc, drive, u, hidden, c_proj, d_skip, w_gate, cotangent,
    block_out, ordered_cot, states, states_low, act, grad_gate, grad_mixed, grad_low, source,
    back_prefix, total, grad_d, sig, slope, wide, result,
):
    layer, reverse, batches, span, groups, tokens = cfg
    turn, back = reorder(span, False), reorder(span, True)
    for batch in range(batches):
        rows = slice(batch * span, (batch + 1) * span)
        ordered_cot[rows, :] = dot(turn, cotangent[rows, :]).astype(bf16)
    forward_finish(
        cfg, meta, ends, prefix, disc, drive, u, hidden, c_proj, d_skip, w_gate,
        states, states_low, act, sig, slope, result, wide, None,
    )
    for batch in range(batches):
        rows = slice(batch * span, (batch + 1) * span)
        block_out[rows, :] = dot(back, result[rows, :]).astype(bf16)
    backward_start(
        cfg, meta, ordered_cot, disc, u, c_proj, w_gate, states_low, act, sig, slope,
        grad_gate, grad_mixed, grad_low, source, back_prefix, total, grad_d, wide,
    )


def backward_finish(
    cfg, meta, ends, prefix, disc, source, drive, states, u, grad_mixed, grad_d, hidden, norm,
    d_skip, b_proj, grad_proj, grad_u, stats, small,
):
    layer, reverse, batches, span, groups, tokens = cfg
    half = groups * LANES
    padded = span + CHUNKS
    steps = span // CHUNKS
    now = disc.at[layer]
    init = chunk_carries(meta, ends, now, prefix, batches, span, groups, not reverse, True)
    inj = coef_tiles(now, 2, groups)
    base = base_positions(meta, steps)
    zero = jnp.zeros((CHUNKS, LANES), f32)

    def visit(more, batch, q, first, start, found, src):
        if q is None:
            return more
        more = list(more)
        rows = pl.ds(batch * span + start, 2 * CHUNKS)
        drive_re, drive_im = drive[rows, lanes_of(q)], drive[rows, lanes_of(q, half)]
        before = pl.ds(batch * padded + start + (CHUNKS if reverse else 0), 2 * CHUNKS)
        prior_re, prior_im = states[before, lanes_of(q)], states[before, lanes_of(q, half)]
        dec_re, dec_im, inj_re, inj_im = more[q]
        out_re, out_im = [], []
        for j in (0, 1):
            part = slice(j * CHUNKS, (j + 1) * CHUNKS)
            adj_re, adj_im = found[j]
            keep = keep_of(meta, batch, base, first + j, reverse)
            kept_re, kept_im = keep * adj_re, keep * adj_im
            dec_re = dec_re + kept_re * prior_re[part] + kept_im * prior_im[part]
            dec_im = dec_im + kept_im * prior_re[part] - kept_re * prior_im[part]
            inj_re = inj_re + adj_re * drive_re[part] + adj_im * drive_im[part]
            inj_im = inj_im + adj_im * drive_re[part] - adj_re * drive_im[part]
            out_re.append(inj[q][0] * adj_re + inj[q][1] * adj_im)
            out_im.append(inj[q][0] * adj_im - inj[q][1] * adj_re)
        grad_proj[rows, lanes_of(q)] = jnp.concatenate(out_re, axis=0).astype(bf16)
        grad_proj[rows, lanes_of(q, half)] = jnp.concatenate(out_im, axis=0).astype(bf16)
        more[q] = (dec_re, dec_im, inj_re, inj_im)
        return tuple(more)

    _, sums = scan(
        meta, source, None, coef_tiles(now, 0, groups, True), batches, span, groups,
        not reverse, not reverse, init, ((zero,) * 4,) * groups, visit,
    )
    small[...] = jnp.zeros_like(small)
    for q in range(groups):
        for kind in range(4):
            small[kind : kind + 1, lanes_of(q)] = jnp.sum(sums[q][kind], axis=0, keepdims=True)
    small[4:5, :] = grad_d[...]
    grad_u[...] = dot(grad_proj[...], b_proj[...], (1, 1))
    skip = d_skip[layer : layer + 1, :]
    plain, times_normed = [], []
    for batch in range(batches):
        average = norm[batch : batch + 1, :]
        scale = norm[batches + batch : batches + batch + 1, :]

        def body(start, carry, batch=batch, average=average, scale=scale):
            rows = pl.ds(batch * span + start, ROWS)
            value = grad_u[rows, :] + grad_mixed[rows, :] * skip
            grad_u[rows, :] = value
            normed = (hidden[rows, :].astype(f32) - average) * scale
            return carry[0] + fold(value), carry[1] + fold(value * normed)

        zero_sum = jnp.zeros((CHUNKS, grad_u.shape[1]), f32)
        one, two = row_loop(span, body, (zero_sum, zero_sum))
        plain.append(one)
        times_normed.append(two)
    add_sums(stats, batches, (plain, times_normed))


def norm_backward(cfg, stats, grad_out, grad_u, hidden, norm, gain, store, shared):
    layer, reverse, batches, span, groups, tokens = cfg
    sums = stats[...]
    shared[0:1, :] = jnp.sum(sums[batches:], axis=0, keepdims=True)
    shared[1:2, :] = jnp.sum(sums[:batches], axis=0, keepdims=True)
    gain_now = gain[layer : layer + 1, :]
    for batch in range(batches):
        average = norm[batch : batch + 1, :]
        scale = norm[batches + batch : batches + batch + 1, :]
        plain = gain_now * sums[batch : batch + 1] / tokens
        slanted = gain_now * sums[batches + batch : batches + batch + 1] / tokens

        def body(start, carry, batch=batch, average=average, scale=scale, plain=plain, slanted=slanted):
            rows = pl.ds(batch * span + start, ROWS)
            normed = (hidden[rows, :].astype(f32) - average) * scale
            value = grad_out[rows, :].astype(f32) + scale * (
                grad_u[rows, :] * gain_now - plain - normed * slanted
            )
            store(rows, value)
            return carry

        row_loop(span, body)


def between_layers(
    cfg, lower, meta, stats, upper_out, upper_u, upper_hidden, upper_norm, gain,
    disc, u, c_proj, w_gate, states_low, act, sig, slope,
    grad_out, shared, grad_gate, grad_mixed, grad_low, source, prefix, total, grad_d, wide,
):
    def store(rows, value):
        grad_out[rows, :] = value

    norm_backward(cfg, stats, upper_out, upper_u, upper_hidden, upper_norm, gain, store, shared)
    backward_start(
        lower, meta, grad_out, disc, u, c_proj, w_gate, states_low, act, sig, slope,
        grad_gate, grad_mixed, grad_low, source, prefix, total, grad_d, wide,
    )


def last_step(cfg, stats, grad_out, grad_u, hidden, norm, gain, target, shared, ordered):
    layer, reverse, batches, span, groups, tokens = cfg
    planes = target.shape[1] // LANES

    def store(rows, value):
        for plane in range(planes):
            ordered[plane, rows, :] = value[:, lanes_of(plane)]

    norm_backward(cfg, stats, grad_out, grad_u, hidden, norm, gain, store, shared)
    steps = span // CHUNKS
    for batch in range(batches):
        for chunk in range(CHUNKS):
            at = batch * span
            for plane in range(planes):
                target[at + chunk * steps : at + (chunk + 1) * steps, lanes_of(plane)] = ordered[
                    plane, pl.ds(at + chunk, steps, stride=CHUNKS), :
                ]


def gate_weights(act, grad_gate, states_low, grad_low, grad_wc):
    width, states = act.shape[1], states_low.shape[1]
    part_w, part_c = width // 2, states // 2
    for half in (0, 1):
        at = half * (part_w + part_c)
        grad_wc[at : at + part_w, :] = dot(
            act[:, half * part_w : (half + 1) * part_w], grad_gate[...], (0, 0)
        )
        grad_wc[at + part_w : at + part_w + part_c, :] = dot(
            states_low[:, half * part_c : (half + 1) * part_c], grad_low[...], (0, 0)
        )


def input_weights(u, grad_proj, grad_b):
    grad_b[...] = dot(u[...], grad_proj[...], (0, 0))


def place_upper(wc, b, grad_w, grad_c, grad_b, sems):
    part_w, part_c = grad_w.shape[1] // 2, grad_c.shape[1] // 2
    copies = [pltpu.make_async_copy(b, grad_b.at[1], sems.at[0])]
    for half in (0, 1):
        at = half * (part_w + part_c)
        copies.append(
            pltpu.make_async_copy(
                wc.at[pl.ds(at, part_w)], grad_w.at[1, pl.ds(half * part_w, part_w)],
                sems.at[1 + 2 * half],
            )
        )
        copies.append(
            pltpu.make_async_copy(
                wc.at[pl.ds(at + part_w, part_c)], grad_c.at[1, pl.ds(half * part_c, part_c)],
                sems.at[2 + 2 * half],
            )
        )
    for copy in copies:
        copy.start()
    for copy in copies:
        copy.wait()


def place_lower(
    place, own_wc, other_wc, own_b, other_b, before_w, before_c, before_b, grad_w, grad_c, grad_b, sems
):
    part_w, part_c, part_b = grad_w.shape[1] // 2, grad_c.shape[1] // 2, grad_b.shape[1] // 2
    copies = []
    for at, (wc, b) in enumerate(((own_wc, own_b), (other_wc, other_b))):
        half = place[0] if at == 0 else 1 - place[0]
        for number, (source, target, rows) in enumerate((
            (wc.at[pl.ds(0, part_w)], grad_w, part_w),
            (wc.at[pl.ds(part_w, part_c)], grad_c, part_c),
            (b, grad_b, part_b),
        )):
            spot = pl.multiple_of(half * rows, rows)
            copies.append(
                pltpu.make_async_copy(
                    source, target.at[0, pl.ds(spot, rows)], sems.at[3 * at + number]
                )
            )
    for copy in copies:
        copy.start()
    for copy in copies:
        copy.wait()


def place(body, name, args, outs, in_specs, aliases, copies):
    anywhere = pl.BlockSpec(memory_space=pl.ANY)
    return pl.pallas_call(
        body,
        name=name,
        out_shape=tuple(jax.ShapeDtypeStruct(*out) for out in outs),
        in_specs=in_specs,
        out_specs=(anywhere,) * len(outs),
        scratch_shapes=[pltpu.SemaphoreType.DMA((copies,))],
        input_output_aliases=aliases,
        compiler_params=pltpu.CompilerParams(vmem_limit_bytes=16 * 1024 * 1024),
    )(*args)


def run(body, name, args, outs, scratch=(), scalars=1, flops=0, touched=0):
    specs = [pl.BlockSpec(memory_space=pltpu.SMEM)] * scalars
    specs += [pl.BlockSpec(memory_space=pltpu.VMEM)] * (len(args) - scalars)
    return pl.pallas_call(
        body,
        name=name,
        out_shape=tuple(jax.ShapeDtypeStruct(*out) for out in outs),
        in_specs=specs,
        out_specs=tuple(pl.BlockSpec(memory_space=pltpu.VMEM) for _ in outs),
        scratch_shapes=[pltpu.VMEM(*entry) for entry in scratch],
        compiler_params=pltpu.CompilerParams(vmem_limit_bytes=VMEM_LIMIT),
    )(*args)


def add_everywhere(value):
    for axis in ("seq", "dp"):
        size = lax.axis_size(axis)
        found = [
            lax.ppermute(value, axis, [(i, (i + away) % size) for i in range(size)])
            for away in range(1, size)
        ]
        value = sum(found, value)
    return value


def seq_groups(chips):
    count = lax.axis_size("seq")
    if chips:
        return [list(range(core, count, 2)) for core in (0, 1)]
    return [[at, at + 1] for at in range(0, count, 2)]


def add_by_gather(value):
    for axis in ("seq", "dp"):
        value = jnp.sum(lax.all_gather(value, axis), axis=0)
    return value


def add_by_two(value):
    return lax.psum(lax.psum(value, "seq"), "dp")


def add_by_three(value):
    value = lax.psum(value, "seq", axis_index_groups=seq_groups(False))
    value = lax.psum(value, "seq", axis_index_groups=seq_groups(True))
    return lax.psum(value, "dp")


def gather_by_two(value):
    value = lax.all_gather(value, "seq", axis_index_groups=seq_groups(False))
    value = lax.all_gather(value, "seq", axis_index_groups=seq_groups(True))
    return value.reshape((-1,) + value.shape[2:])


def axis_parts():
    count = lax.axis_size("seq")
    mine = lax.axis_index("seq")
    outer = 1
    while outer * outer * 2 < count:
        outer *= 2
    inner = count // (2 * outer)
    parts = []
    for size, stride in ((2, 1), (inner, 2), (outer, 2 * inner)):
        parts.append(("seq", size, stride, count, (mine // stride) % size))
    size = lax.axis_size("dp")
    parts.append(("dp", size, 1, size, lax.axis_index("dp")))
    return parts


def shifted(value, part, away):
    name, size, stride, count, mine = part
    pairs = []
    for i in range(count):
        place = (i // stride) % size
        pairs.append((i, i + ((place + away) % size - place) * stride))
    return lax.ppermute(value, name, pairs)


def scatter_sum(value, part):
    name, size, stride, count, mine = part
    rows = value.shape[-2] // size

    def piece(place):
        return lax.dynamic_slice_in_dim(value, place * rows, rows, axis=value.ndim - 2)

    found = [shifted(piece((mine + away) % size), part, away) for away in range(1, size)]
    return sum(found, piece(mine))


def gather_rows(value, part):
    name, size, stride, count, mine = part
    axis = value.ndim - 2
    rows = value.shape[axis]
    found = [value] + [shifted(value, part, away) for away in range(1, size)]
    if size == 2:
        low = jnp.where(mine == 0, found[0], found[1])
        high = jnp.where(mine == 0, found[1], found[0])
        return jnp.concatenate([low, high], axis=axis)
    shape = value.shape[:axis] + (rows * size,) + value.shape[axis + 1 :]
    out = jnp.zeros(shape, value.dtype)
    for away in range(size):
        out = lax.dynamic_update_slice_in_dim(
            out, found[away], ((mine - away) % size) * rows, axis=axis
        )
    return out


def sum_over_links(value):
    core, inner, outer, depth = axis_parts()
    own = scatter_sum(value, core)
    cols = own.shape[1] // 2
    left, right = own[:, :cols], own[:, cols:]
    left, right = scatter_sum(left, inner), scatter_sum(right, outer)
    left, right = scatter_sum(left, outer), scatter_sum(right, inner)
    both = gather_rows(scatter_sum(jnp.stack([left, right]), depth), depth)
    left, right = both[0], both[1]
    left, right = gather_rows(left, outer), gather_rows(right, inner)
    left, right = gather_rows(left, inner), gather_rows(right, outer)
    own = jnp.concatenate([left, right], axis=1)
    return own, shifted(own, core, 1)


def discretize(lam_re, lam_im, log_step):
    step_size = jnp.exp(log_step)
    decay_abs = jnp.exp(lam_re * step_size)
    rotation = lam_im * step_size
    dec_re = decay_abs * jnp.cos(rotation)
    dec_im = decay_abs * jnp.sin(rotation)
    denom_sq = lam_re * lam_re + lam_im * lam_im
    inj_re = ((dec_re - 1.0) * lam_re + dec_im * lam_im) / denom_sq
    inj_im = (dec_im * lam_re - (dec_re - 1.0) * lam_im) / denom_sq
    return (dec_re, dec_im, inj_re, inj_im)


def power(value, doublings):
    for _ in range(doublings):
        value = times(value, value)
    return value


def per_device(
    block_in, cotangent, doc_lengths, norm_gain, norm_shift, log_step, lam_re, lam_im,
    b_proj, c_proj, d_skip, w_gate,
):
    batches, seqs, span, width = block_in.shape
    assert seqs == 1 and span % (4 * CHUNKS) == 0
    half = lam_re.shape[1]
    groups = half // LANES
    rows = batches * span
    everyone = ("dp", "seq")
    chunk_doublings = (span // CHUNKS).bit_length() - 1
    span_doublings = span.bit_length() - 1
    assert 1 << span_doublings == span
    tokens = float(seqs * lax.axis_size("dp") * span * lax.axis_size("seq"))
    mine = lax.axis_index("seq")
    lengths = doc_lengths[:, 0, :]
    ends = jnp.cumsum(lengths, axis=-1).astype(jnp.int32)
    begins = ends - lengths
    first = mine * span
    before = jnp.max(jnp.where(begins < first, begins, 0), axis=-1)
    whole = span * lax.axis_size("seq")
    after = jnp.min(jnp.where(ends > first + span, ends, 2 * whole), axis=-1)
    after = jnp.where(first + span < whole, after, 0)
    spot = jnp.broadcast_to(jnp.stack([first, mine])[None], (batches, 2))
    meta = jnp.concatenate([begins, ends, before[:, None], after[:, None], spot], axis=-1).astype(
        jnp.int32
    )
    dec_re, dec_im, inj_re, inj_im = discretize(lam_re, lam_im, log_step)
    dec_chunk = power((dec_re, dec_im), chunk_doublings)
    dec_span = power(dec_chunk, span_doublings - chunk_doublings)
    disc = jnp.stack([dec_re, dec_im, inj_re, inj_im, *dec_chunk, *dec_span], axis=1)

    x = block_in.reshape(rows, width)
    cot = cotangent.reshape(rows, width)
    lower = (0, False, batches, span, groups, tokens)
    upper = (1, True, batches, span, groups, tokens)
    part = functools.partial

    flat, low = ((rows, width), f32), ((rows, width), bf16)
    wide, wide_low = ((rows, 2 * half), f32), ((rows, 2 * half), bf16)
    padded = ((batches * (span + CHUNKS), 2 * half), f32)
    sums = ((2 * batches, width), f32)
    prefix = ((2, batches * CHUNKS, 2 * half), f32)
    total = ((batches, 2 * half), f32)
    line, shared = ((1, width), f32), ((2, width), f32)
    small = ((8, width), f32)

    def gather_row(value):
        return lax.all_gather(value, "seq")

    ordered, stats = run(
        part(first_sums, batches, span), "first_sums", (x,), (low, sums), scalars=0
    )

    def forward(cfg, hidden, total_stats):
        layer = cfg[0]
        return run(
            part(enter_layer, cfg),
            "enter_layer",
            (meta, total_stats, hidden, norm_gain, norm_shift, disc, b_proj[layer]),
            (low, wide, prefix, total, sums),
        )

    u0, drive0, prefix0, total0, norm0 = forward(lower, ordered, add_by_gather(stats))
    states0, states_low0, act0, sig0, slope0, hidden1, stats = run(
        part(middle_forward, lower),
        "middle_forward",
        (
            meta, gather_by_two(total0), prefix0, disc, drive0, u0, ordered, c_proj[0], d_skip,
            w_gate[0],
        ),
        (padded, wide_low, low, flat, flat, flat, sums),
        (flat,),
    )
    u1, drive1, prefix1, total1, norm1 = forward(upper, hidden1, add_by_two(stats))
    (
        block_out, ordered_cot, states1, states_low1, act1, grad_gate1, grad_mixed1, grad_low1,
        source1, prefix1, total1, grad_d1,
    ) = run(
        part(turn_around, upper),
        "turn_around",
        (
            meta, gather_row(total1), prefix1, disc, drive1, u1, hidden1, c_proj[1], d_skip,
            w_gate[1], cot,
        ),
        (low, low, padded, wide_low, low, low, flat, low, wide, prefix, total, line),
        (flat, flat, flat, low),
    )
    (grad_wc1,) = run(
        gate_weights, "gate_weights", (act1, grad_gate1, states_low1, grad_low1),
        (((width + 2 * half, width), f32),), scalars=0,
    )

    grad_wc1, total1 = lax.optimization_barrier((grad_wc1, total1))
    sum_wc1 = lax.psum(grad_wc1, everyone)

    def finish(cfg, total, prefix, source, drive, states, u, grad_mixed, grad_d, hidden, norm):
        return run(
            part(backward_finish, cfg),
            "backward_finish",
            (
                meta, gather_row(total), prefix, disc, source, drive, states, u, grad_mixed,
                grad_d, hidden, norm, d_skip, b_proj[cfg[0]],
            ),
            (wide_low, flat, sums, small),
        )

    grad_proj1, grad_u1, stats, small1 = finish(
        upper, total1, prefix1, source1, drive1, states1, u1, grad_mixed1, grad_d1, hidden1, norm1
    )
    (grad_b1,) = run(
        input_weights, "input_weights", (u1, grad_proj1), (((width, 2 * half), f32),), scalars=0
    )
    grad_b1, sum_wc1 = lax.optimization_barrier((grad_b1, sum_wc1))
    sum_b1 = lax.psum(grad_b1, everyone)
    (
        grad_out0, shared1, grad_gate0, grad_mixed0, grad_low0, source0, prefix0, total0, grad_d0,
    ) = run(
        part(between_layers, upper, lower),
        "between_layers",
        (
            meta, add_by_three(stats), ordered_cot, grad_u1, hidden1, norm1, norm_gain,
            disc, u0, c_proj[0], w_gate[0], states_low0, act0, sig0, slope0,
        ),
        (flat, shared, low, flat, low, wide, prefix, total, line),
        (flat,),
    )
    (grad_wc0,) = run(
        gate_weights, "gate_weights", (act0, grad_gate0, states_low0, grad_low0),
        (((width + 2 * half, width), f32),), scalars=0,
    )
    grad_wc0, total0 = lax.optimization_barrier((grad_wc0, total0))
    grad_proj0, grad_u0, stats, small0 = finish(
        lower, total0, prefix0, source0, drive0, states0, u0, grad_mixed0, grad_d0, ordered, norm0
    )
    (grad_b0,) = run(
        input_weights, "input_weights", (u0, grad_proj0), (((width, 2 * half), f32),), scalars=0
    )
    grad_input, shared0 = run(
        part(last_step, lower),
        "last_step",
        (add_everywhere(stats), grad_out0, grad_u0, ordered, norm0, norm_gain),
        (flat, shared),
        (((width // LANES, rows, LANES), f32),),
        scalars=0,
    )
    small_sum = add_everywhere(jnp.stack([small0, small1]))
    final = (((2, width, width), f32), ((2, 2 * half, width), f32), ((2, width, 2 * half), f32))
    anywhere = pl.BlockSpec(memory_space=pl.ANY)
    placed = place(
        place_upper, "place_upper", (sum_wc1, sum_b1), final, (anywhere,) * 2, {}, 5
    )
    grad_w, grad_c, grad_b = place(
        place_lower,
        "place_lower",
        (
            jnp.reshape(mine % 2, (1,)).astype(jnp.int32), *sum_over_links(grad_wc0),
            *sum_over_links(grad_b0), *placed,
        ),
        final,
        (pl.BlockSpec(memory_space=pltpu.SMEM),) + (anywhere,) * 7,
        {5: 0, 6: 1, 7: 2},
        6,
    )
    _, pullback = jax.vjp(discretize, lam_re, lam_im, log_step)
    grad_lr, grad_li, grad_ls = pullback(tuple(small_sum[:, kind, :half] for kind in range(4)))
    both = jnp.stack([shared0, shared1])
    shape = block_in.shape
    return (
        block_out.reshape(shape), grad_input.reshape(shape), both[:, 0], both[:, 1],
        grad_ls, grad_lr, grad_li, grad_b, grad_c, small_sum[:, 4], grad_w,
    )


def solution(mesh):
    split = P(None, "dp", "seq", None)
    return jax.shard_map(
        per_device,
        mesh=mesh,
        in_specs=(split, split, P(None, "dp", None)) + (P(),) * 9,
        out_specs=(split, split) + (P(),) * 9,
        check_vma=False,
    )
```

```python
import functools

import jax
import jax.numpy as jnp
from jax import lax
from jax.experimental import pallas as pl
from jax.experimental.pallas import tpu as pltpu
from jax.sharding import PartitionSpec as P

f32, bf16 = jnp.float32, jnp.bfloat16
epsilon = 1e-05
tanh_scale = 0.7978845608028654
cubic_term = 0.044715
LANES = 128
CHUNKS = 8
ROWS = 32
VMEM_LIMIT = 26 * 1024 * 1024


def dot(left, right, contract=(1, 0)):
    return lax.dot_general(
        left, right, (((contract[0],), (contract[1],)), ((), ())), preferred_element_type=f32
    )


def reorder(span, inverse):
    shape = (span, span)
    kept, moved = (1, 0) if inverse else (0, 1)
    row = lax.broadcasted_iota(jnp.int32, shape, kept)
    position = lax.broadcasted_iota(jnp.int32, shape, moved)
    source = (row & (CHUNKS - 1)) * (span // CHUNKS) + (row >> 3)
    return jnp.where(position == source, 1.0, 0.0).astype(bf16)


def row_loop(count, body, init=0, step=ROWS):
    def one(index, carry):
        return body(pl.multiple_of(index * step, step), carry)

    return lax.fori_loop(0, count // step, one, init)


def documents(lengths, mine, batches, span, count):
    first = mine[0] * span
    out = []
    for batch in range(batches):
        begins, ends, so_far = [], [], 0
        for doc in range(lengths.shape[2]):
            begins.append(so_far)
            so_far = so_far + lengths[batch, 0, doc]
            ends.append(so_far)
        before, after = 0, 2 * count * span
        for begin, end in zip(begins, ends):
            before = jnp.maximum(before, jnp.where(begin < first, begin, 0))
            after = jnp.minimum(after, jnp.where(end > first + span, end, 2 * count * span))
        after = jnp.where(mine[0] == count - 1, 0, after)
        out.append(begins + ends + [before, after, first, mine[0]])
    return out


def place_documents(cfg, place):
    layer, reverse, batches, span, groups, tokens, count = cfg
    return documents(*place, batches, span, count)


def keep_of(meta, batch, base, step, backward):
    docs = (len(meta[batch]) - 4) // 2
    off = docs if backward else 0
    late = 1 if backward else 0
    stop = base == meta[batch][off] - step - late
    for doc in range(1, docs):
        stop = jnp.logical_or(stop, base == meta[batch][off + doc] - step - late)
    return jnp.where(stop, 0.0, 1.0)


def base_positions(meta, steps):
    return meta[0][-2] + lax.broadcasted_iota(jnp.int32, (CHUNKS, LANES), 0) * steps


def lanes_of(index, half=0):
    return slice(half + index * LANES, half + (index + 1) * LANES)


def coef_tiles(value, groups):
    return [
        tuple(jnp.broadcast_to(part[:, lanes_of(q)], (CHUNKS, LANES)) for part in value)
        for q in range(groups)
    ]


def constants(disc, layer):
    dec_re, dec_im, inj_re, inj_im = (part[layer : layer + 1, :] for part in disc)
    return (dec_re, dec_im), (inj_re, inj_im)


def times(a, b):
    return (a[0] * b[0] - a[1] * b[1], a[0] * b[1] + a[1] * b[0])


def power(value, exponent):
    for _ in range(exponent.bit_length() - 1):
        value = times(value, value)
    return value


def conj(value):
    return (value[0], -value[1])


def scan(meta, source, inject, dec, batches, span, groups, reverse, masks_reverse, init, extra, visit):
    steps = span // CHUNKS
    half = groups * LANES
    base = base_positions(meta, steps)

    def pair(index, carry):
        states, more = carry
        states = list(states)
        first = steps - 2 - 2 * index if reverse else 2 * index
        start = pl.multiple_of(first * CHUNKS, 2 * CHUNKS)
        order = (1, 0) if reverse else (0, 1)
        for batch in range(batches):
            keeps = [keep_of(meta, batch, base, first + j, masks_reverse) for j in (0, 1)]
            for q in range(groups):
                rows = pl.ds(batch * span + start, 2 * CHUNKS)
                src_re = source[rows, lanes_of(q)]
                src_im = source[rows, lanes_of(q, half)]
                state = states[batch * groups + q]
                found = [None, None]
                for j in order:
                    part = (
                        src_re[j * CHUNKS : (j + 1) * CHUNKS],
                        src_im[j * CHUNKS : (j + 1) * CHUNKS],
                    )
                    push = times(inject[q], part) if inject is not None else part
                    held = times((keeps[j] * dec[q][0], keeps[j] * dec[q][1]), state)
                    state = (held[0] + push[0], held[1] + push[1])
                    found[j] = state
                states[batch * groups + q] = state
                more = visit(more, batch, q, first, start, found, (src_re, src_im))
            more = visit(more, batch, None, first, start, keeps, None)
        return tuple(states), more

    return lax.fori_loop(0, steps // 2, pair, (tuple(init), extra), unroll=2)


def zero_states(batches, groups):
    zero = jnp.zeros((CHUNKS, LANES), f32)
    return [(zero, zero)] * (batches * groups)


def local_ends(meta, source, inject, dec, batches, span, groups, reverse, prefix, total):
    ones = tuple(jnp.ones((CHUNKS, LANES), f32) for _ in range(batches))

    def visit(more, batch, q, first, start, found, src):
        if q is not None:
            return more
        return tuple(
            value * found[0] * found[1] if at == batch else value for at, value in enumerate(more)
        )

    dec_chunk = coef_tiles(power(dec, span // CHUNKS), groups)
    ends, kept = scan(
        meta, source, inject, coef_tiles(dec, groups), batches, span, groups, reverse, reverse,
        zero_states(batches, groups), ones, visit,
    )
    half = groups * LANES
    row = lax.broadcasted_iota(jnp.int32, (CHUNKS, LANES), 0)
    for batch in range(batches):
        for q in range(groups):
            end = ends[batch * groups + q]
            decay = (kept[batch] * dec_chunk[q][0], kept[batch] * dec_chunk[q][1])
            for shift in (1, 2, 4):
                turn = CHUNKS - shift if reverse else shift
                valid = row < CHUNKS - shift if reverse else row >= shift
                before = [pltpu.roll(value, turn, 0) for value in (*end, *decay)]
                from_before = times(decay, (before[0], before[1]))
                end = (
                    end[0] + jnp.where(valid, from_before[0], 0.0),
                    end[1] + jnp.where(valid, from_before[1], 0.0),
                )
                longer = times(decay, (before[2], before[3]))
                decay = (
                    jnp.where(valid, longer[0], decay[0]),
                    jnp.where(valid, longer[1], decay[1]),
                )
            rows = slice(batch * CHUNKS, (batch + 1) * CHUNKS)
            prefix[0, rows, lanes_of(q)] = end[0]
            prefix[0, rows, lanes_of(q, half)] = end[1]
            prefix[1, rows, lanes_of(q)] = decay[0]
            prefix[1, rows, lanes_of(q, half)] = decay[1]
            last = 0 if reverse else CHUNKS - 1
            total[batch : batch + 1, lanes_of(q)] = end[0][last : last + 1]
            total[batch : batch + 1, lanes_of(q, half)] = end[1][last : last + 1]


def chunk_carries(meta, gathered, dec, prefix, batches, span, groups, reverse):
    count = gathered.shape[0]
    half = groups * LANES
    dec_span = power(dec, span)
    row = lax.broadcasted_iota(jnp.int32, (CHUNKS, LANES), 0)
    mine = meta[0][-1]
    out = []
    for batch in range(batches):

        def add(at, so_far, batch=batch):
            away = count - 2 - at
            if reverse:
                other = mine + 1 + away
                reaches = meta[batch][-3] > other * span
            else:
                other = mine - 1 - away
                reaches = meta[batch][-4] < (mine - away) * span
            other = jnp.clip(other, 0, count - 1)
            value = jnp.where(reaches, gathered[other, pl.ds(batch, 1), :], 0.0)
            moved = times(dec_span, so_far)
            return (moved[0] + value[:, :half], moved[1] + value[:, half:])

        zero = jnp.zeros((1, half), f32)
        enter = lax.fori_loop(0, count - 1, add, (zero, zero), unroll=count <= 8)
        rows = slice(batch * CHUNKS, (batch + 1) * CHUNKS)
        for q in range(groups):
            own = tuple(jnp.broadcast_to(part[:, lanes_of(q)], (CHUNKS, LANES)) for part in enter)
            end = (prefix[0, rows, lanes_of(q)], prefix[0, rows, lanes_of(q, half)])
            decay = (prefix[1, rows, lanes_of(q)], prefix[1, rows, lanes_of(q, half)])
            moved = times(decay, own)
            turn, first = (CHUNKS - 1, CHUNKS - 1) if reverse else (1, 0)
            out.append(
                tuple(
                    jnp.where(row == first, own[i], pltpu.roll(end[i] + moved[i], turn, 0))
                    for i in (0, 1)
                )
            )
    return out


def add_sums(target, batches, sums):
    for kind, per_batch in enumerate(sums):
        for batch in range(batches):
            target[kind * batches + batch : kind * batches + batch + 1, :] = jnp.sum(
                per_batch[batch], axis=0, keepdims=True
            )


def fold(value):
    return sum(value[i : i + CHUNKS] for i in range(CHUNKS, value.shape[0], CHUNKS)) + value[:CHUNKS]


def first_sums(batches, span, x, ordered, stats):
    turn = reorder(span, False)
    width = x.shape[1]
    sums, squares = [], []
    for batch in range(batches):
        rows = slice(batch * span, (batch + 1) * span)
        ordered[rows, :] = dot(turn, x[rows, :]).astype(bf16)

        def body(start, carry, batch=batch):
            value = x[pl.ds(batch * span + start, ROWS), :].astype(f32)
            return carry[0] + fold(value), carry[1] + fold(value * value)

        zero = jnp.zeros((CHUNKS, width), f32)
        one, two = row_loop(span, body, (zero, zero))
        sums.append(one)
        squares.append(two)
    add_sums(stats, batches, (sums, squares))


def enter_layer(
    cfg, place, stats, hidden, gain, shift, disc, b_proj, u, drive, prefix, total, norm
):
    layer, reverse, batches, span, groups, tokens, count = cfg
    sums = sum(part[...] for part in stats)
    average = sums[:batches] / tokens
    spread = sums[batches:] / tokens - average * average
    scale = lax.rsqrt(spread + epsilon)
    norm[:batches, :] = average
    norm[batches:, :] = scale
    gain_now, shift_now = gain[layer : layer + 1, :], shift[layer : layer + 1, :]
    for batch in range(batches):

        def body(start, carry, batch=batch):
            rows = pl.ds(batch * span + start, ROWS)
            normed = (hidden[rows, :].astype(f32) - average[batch : batch + 1]) * scale[
                batch : batch + 1
            ]
            u[rows, :] = (normed * gain_now + shift_now).astype(bf16)
            return carry

        row_loop(span, body)
    drive[...] = dot(u[...], b_proj[layer])
    meta = place_documents(cfg, place)
    dec, inj = constants(disc, layer)
    local_ends(
        meta, drive, coef_tiles(inj, groups), dec, batches, span, groups, reverse, prefix, total
    )


def finish_states(cfg, meta, ends, prefix, disc, drive, states, states_low):
    layer, reverse, batches, span, groups, tokens, count = cfg
    half = groups * LANES
    padded = span + CHUNKS
    dec, inj = constants(disc, layer)
    init = chunk_carries(meta, ends, dec, prefix, batches, span, groups, reverse)
    for batch in range(batches):
        edge = batch * padded + (span if reverse else 0)
        for q in range(groups):
            states[edge : edge + CHUNKS, lanes_of(q)] = init[batch * groups + q][0]
            states[edge : edge + CHUNKS, lanes_of(q, half)] = init[batch * groups + q][1]

    def visit(more, batch, q, first, start, found, src):
        if q is not None:
            for part, off in ((0, 0), (1, half)):
                both = jnp.concatenate([found[0][part], found[1][part]], axis=0)
                at = batch * padded + (0 if reverse else CHUNKS)
                states[pl.ds(at + start, 2 * CHUNKS), lanes_of(q, off)] = both
                states_low[pl.ds(batch * span + start, 2 * CHUNKS), lanes_of(q, off)] = both.astype(
                    bf16
                )
        return more

    scan(
        meta, drive, coef_tiles(inj, groups), coef_tiles(dec, groups), batches, span, groups,
        reverse, reverse, init, 0, visit,
    )


def forward_finish(
    cfg, meta, ends, prefix, disc, drive, u, hidden, c_proj, d_skip, w_gate,
    states, states_low, act, sig, slope, result, wide, emit,
):
    layer, reverse, batches, span, groups, tokens, count = cfg
    finish_states(cfg, meta, ends, prefix, disc, drive, states, states_low)
    wide[...] = dot(states_low[...], c_proj[layer])
    skip = d_skip[layer : layer + 1, :]

    def body(start, carry):
        rows = pl.ds(start, ROWS)
        mixed = wide[rows, :] + skip * u[rows, :].astype(f32)
        square = mixed * mixed
        th = jnp.tanh(tanh_scale * (mixed + cubic_term * square * mixed))
        half_one = 0.5 * (1.0 + th)
        act[rows, :] = (mixed * half_one).astype(bf16)
        slope[rows, :] = half_one + 0.5 * mixed * (1.0 - th * th) * tanh_scale * (
            1.0 + 3.0 * cubic_term * square
        )
        return carry

    row_loop(batches * span, body)
    wide[...] = dot(act[...], w_gate[layer])
    sums, squares = [], []
    for batch in range(batches):

        def gate(start, carry, batch=batch):
            rows = pl.ds(batch * span + start, ROWS)
            sig_now = 0.5 + 0.5 * jnp.tanh(0.5 * wide[rows, :])
            sig[rows, :] = sig_now
            value = hidden[rows, :].astype(f32) + act[rows, :].astype(f32) * sig_now
            result[rows, :] = value.astype(result.dtype)
            if emit is None:
                return carry
            return carry[0] + fold(value), carry[1] + fold(value * value)

        zero = jnp.zeros((CHUNKS, wide.shape[1]), f32)
        one, two = row_loop(span, gate, (zero, zero))
        sums.append(one)
        squares.append(two)
    if emit is not None:
        add_sums(emit, batches, (sums, squares))


def backward_start(
    cfg, meta, grad_out, disc, u, c_proj, w_gate, states_low, act, sig, slope,
    grad_gate, grad_mixed, grad_low, source, prefix, total, grad_d, wide,
):
    layer, reverse, batches, span, groups, tokens, count = cfg

    def body(start, carry):
        rows = pl.ds(start, ROWS)
        sig_now = sig[rows, :]
        grad_gate[rows, :] = (
            grad_out[rows, :].astype(f32) * act[rows, :].astype(f32) * sig_now * (1.0 - sig_now)
        ).astype(bf16)
        return carry

    row_loop(batches * span, body)
    wide[...] = dot(grad_gate[...], w_gate[layer], (1, 1))

    def mixed(start, carry):
        rows = pl.ds(start, ROWS)
        value = (grad_out[rows, :].astype(f32) * sig[rows, :] + wide[rows, :]) * slope[rows, :]
        grad_mixed[rows, :] = value
        grad_low[rows, :] = value.astype(bf16)
        return carry + fold(value * u[rows, :].astype(f32))

    gd = row_loop(batches * span, mixed, jnp.zeros((CHUNKS, wide.shape[1]), f32))
    grad_d[...] = jnp.sum(gd, axis=0, keepdims=True)
    source[...] = dot(grad_low[...], c_proj[layer], (1, 1))
    local_ends(
        meta, source, None, conj(constants(disc, layer)[0]), batches, span, groups, not reverse,
        prefix, total,
    )


def middle_forward(
    cfg, place, ends, prefix, disc, drive, u, hidden, c_proj, d_skip, w_gate,
    states, states_low, act, sig, slope, result, stats, wide,
):
    meta = place_documents(cfg, place)
    forward_finish(
        cfg, meta, ends, prefix, disc, drive, u, hidden, c_proj, d_skip, w_gate,
        states, states_low, act, sig, slope, result, wide, stats,
    )


def turn_around(
    cfg, place, ends, prefix, disc, drive, u, hidden, c_proj, d_skip, w_gate, cotangent,
    block_out, ordered_cot, states, states_low, act, grad_gate, grad_mixed, grad_low, source,
    back_prefix, total, grad_d, sig, slope, wide, result,
):
    layer, reverse, batches, span, groups, tokens, count = cfg
    meta = place_documents(cfg, place)
    turn, back = reorder(span, False), reorder(span, True)
    for batch in range(batches):
        rows = slice(batch * span, (batch + 1) * span)
        ordered_cot[rows, :] = dot(turn, cotangent[rows, :]).astype(bf16)
    forward_finish(
        cfg, meta, ends, prefix, disc, drive, u, hidden, c_proj, d_skip, w_gate,
        states, states_low, act, sig, slope, result, wide, None,
    )
    for batch in range(batches):
        rows = slice(batch * span, (batch + 1) * span)
        block_out[rows, :] = dot(back, result[rows, :]).astype(bf16)
    backward_start(
        cfg, meta, ordered_cot, disc, u, c_proj, w_gate, states_low, act, sig, slope,
        grad_gate, grad_mixed, grad_low, source, back_prefix, total, grad_d, wide,
    )


def backward_finish(
    cfg, place, ends, prefix, disc, source, drive, states, u, grad_mixed, grad_d, hidden, norm,
    d_skip, b_proj, grad_proj, grad_u, stats, small,
):
    layer, reverse, batches, span, groups, tokens, count = cfg
    half = groups * LANES
    padded = span + CHUNKS
    steps = span // CHUNKS
    meta = place_documents(cfg, place)
    dec, inj = constants(disc, layer)
    dec = conj(dec)
    init = chunk_carries(meta, ends, dec, prefix, batches, span, groups, not reverse)
    inj = coef_tiles(inj, groups)
    base = base_positions(meta, steps)
    zero = jnp.zeros((CHUNKS, LANES), f32)

    def visit(more, batch, q, first, start, found, src):
        if q is None:
            return more
        more = list(more)
        rows = pl.ds(batch * span + start, 2 * CHUNKS)
        drive_re, drive_im = drive[rows, lanes_of(q)], drive[rows, lanes_of(q, half)]
        before = pl.ds(batch * padded + start + (CHUNKS if reverse else 0), 2 * CHUNKS)
        prior_re, prior_im = states[before, lanes_of(q)], states[before, lanes_of(q, half)]
        dec_re, dec_im, inj_re, inj_im = more[q]
        out_re, out_im = [], []
        for j in (0, 1):
            part = slice(j * CHUNKS, (j + 1) * CHUNKS)
            adj_re, adj_im = found[j]
            keep = keep_of(meta, batch, base, first + j, reverse)
            kept_re, kept_im = keep * adj_re, keep * adj_im
            dec_re = dec_re + kept_re * prior_re[part] + kept_im * prior_im[part]
            dec_im = dec_im + kept_im * prior_re[part] - kept_re * prior_im[part]
            inj_re = inj_re + adj_re * drive_re[part] + adj_im * drive_im[part]
            inj_im = inj_im + adj_im * drive_re[part] - adj_re * drive_im[part]
            out_re.append(inj[q][0] * adj_re + inj[q][1] * adj_im)
            out_im.append(inj[q][0] * adj_im - inj[q][1] * adj_re)
        grad_proj[rows, lanes_of(q)] = jnp.concatenate(out_re, axis=0).astype(bf16)
        grad_proj[rows, lanes_of(q, half)] = jnp.concatenate(out_im, axis=0).astype(bf16)
        more[q] = (dec_re, dec_im, inj_re, inj_im)
        return tuple(more)

    _, sums = scan(
        meta, source, None, coef_tiles(dec, groups), batches, span, groups,
        not reverse, not reverse, init, ((zero,) * 4,) * groups, visit,
    )
    small[...] = jnp.zeros_like(small)
    for q in range(groups):
        for kind in range(4):
            small[kind : kind + 1, lanes_of(q)] = jnp.sum(sums[q][kind], axis=0, keepdims=True)
    small[4:5, :] = grad_d[...]
    grad_u[...] = dot(grad_proj[...], b_proj[layer], (1, 1))
    skip = d_skip[layer : layer + 1, :]
    plain, times_normed = [], []
    for batch in range(batches):
        average = norm[batch : batch + 1, :]
        scale = norm[batches + batch : batches + batch + 1, :]

        def body(start, carry, batch=batch, average=average, scale=scale):
            rows = pl.ds(batch * span + start, ROWS)
            value = grad_u[rows, :] + grad_mixed[rows, :] * skip
            grad_u[rows, :] = value
            normed = (hidden[rows, :].astype(f32) - average) * scale
            return carry[0] + fold(value), carry[1] + fold(value * normed)

        zero_sum = jnp.zeros((CHUNKS, grad_u.shape[1]), f32)
        one, two = row_loop(span, body, (zero_sum, zero_sum))
        plain.append(one)
        times_normed.append(two)
    add_sums(stats, batches, (plain, times_normed))


def norm_backward(cfg, stats, grad_out, grad_u, hidden, norm, gain, store, shared):
    layer, reverse, batches, span, groups, tokens, count = cfg
    sums = sum(part[...] for part in stats)
    shared[0:1, :] = jnp.sum(sums[batches:], axis=0, keepdims=True)
    shared[1:2, :] = jnp.sum(sums[:batches], axis=0, keepdims=True)
    gain_now = gain[layer : layer + 1, :]
    for batch in range(batches):
        average = norm[batch : batch + 1, :]
        scale = norm[batches + batch : batches + batch + 1, :]
        plain = gain_now * sums[batch : batch + 1] / tokens
        slanted = gain_now * sums[batches + batch : batches + batch + 1] / tokens

        def body(start, carry, batch=batch, average=average, scale=scale, plain=plain, slanted=slanted):
            rows = pl.ds(batch * span + start, ROWS)
            normed = (hidden[rows, :].astype(f32) - average) * scale
            value = grad_out[rows, :].astype(f32) + scale * (
                grad_u[rows, :] * gain_now - plain - normed * slanted
            )
            store(rows, value)
            return carry

        row_loop(span, body)


def between_layers(
    cfg, lower, place, stats, upper_out, upper_u, upper_hidden, upper_norm, gain,
    disc, u, c_proj, w_gate, states_low, act, sig, slope,
    grad_out, shared, grad_gate, grad_mixed, grad_low, source, prefix, total, grad_d, wide,
):
    def store(rows, value):
        grad_out[rows, :] = value

    norm_backward(cfg, stats, upper_out, upper_u, upper_hidden, upper_norm, gain, store, shared)
    meta = place_documents(lower, place)
    backward_start(
        lower, meta, grad_out, disc, u, c_proj, w_gate, states_low, act, sig, slope,
        grad_gate, grad_mixed, grad_low, source, prefix, total, grad_d, wide,
    )


def last_step(cfg, stats, grad_out, grad_u, hidden, norm, gain, target, shared, ordered):
    layer, reverse, batches, span, groups, tokens, count = cfg
    planes = target.shape[1] // LANES

    def store(rows, value):
        for plane in range(planes):
            ordered[plane, rows, :] = value[:, lanes_of(plane)]

    norm_backward(cfg, stats, grad_out, grad_u, hidden, norm, gain, store, shared)
    steps = span // CHUNKS
    for batch in range(batches):
        for chunk in range(CHUNKS):
            at = batch * span
            for plane in range(planes):
                target[at + chunk * steps : at + (chunk + 1) * steps, lanes_of(plane)] = ordered[
                    plane, pl.ds(at + chunk, steps, stride=CHUNKS), :
                ]


def half_weights(core, refs, own, sent):
    for target, half in ((own, core), (sent, 1 - core)):
        at = 0
        for left, right in refs:
            rows = left.shape[1] // 2
            cols = pl.ds(pl.multiple_of(half * rows, LANES), rows)
            target[at : at + rows, :] = dot(left[:, cols], right[...], (0, 0))
            at += rows


def all_weights(core, act, grad_gate, states_low, grad_low, grad_proj, u, own, sent):
    refs = ((act, grad_gate), (states_low, grad_low), (grad_proj, u))
    half_weights(core[0], refs, own, sent)


def gate_weights(core, act, grad_gate, states_low, grad_low, own, sent):
    half_weights(core[0], ((act, grad_gate), (states_low, grad_low)), own, sent)


def input_weights(core, grad_proj, u, own, sent):
    half_weights(core[0], ((grad_proj, u),), own, sent)


def run(body, name, args, outs, scratch=(), scalars=1):
    vmem, smem = pl.BlockSpec(memory_space=pltpu.VMEM), pl.BlockSpec(memory_space=pltpu.SMEM)
    specs = tuple(
        jax.tree.map(lambda _, at=at: smem if at < scalars else vmem, arg)
        for at, arg in enumerate(args)
    )
    return pl.pallas_call(
        body,
        name=name,
        out_shape=tuple(jax.ShapeDtypeStruct(*out) for out in outs),
        in_specs=specs,
        out_specs=(vmem,) * len(outs),
        scratch_shapes=[pltpu.VMEM(*entry) for entry in scratch],
        compiler_params=pltpu.CompilerParams(vmem_limit_bytes=VMEM_LIMIT),
    )(*args)


def put_halves(core, pieces, *refs):
    grad_w, grad_c, grad_b = refs[-3:]
    step = pl.program_id(0)
    for now in (0, 1):

        @pl.when(step == now)
        def _(now=now):
            rows_w, rows_c = grad_w.shape[1], grad_c.shape[1]
            sources = refs[now * pieces : (now + 1) * pieces]
            gates = sources[0]
            grad_w[0] = gates[:rows_w, :]
            grad_c[0] = gates[rows_w : rows_w + rows_c, :]
            last = sources[-1]
            at = rows_w + rows_c if pieces == 1 else 0
            grad_b[0] = last[at : at + rows_c, :].T


def put_in_place(layer, core, own, other, outs, before):
    width, states = outs[0][0][1], outs[1][0][1]
    pieces = len(own)
    vmem = pl.BlockSpec(memory_space=pltpu.VMEM)

    def half(step, core):
        return jnp.where(step == 0, core[0], 1 - core[0])

    blocks = (
        pl.BlockSpec((1, width // 2, width), lambda i, core: (layer, half(i, core), 0)),
        pl.BlockSpec((1, states // 2, width), lambda i, core: (layer, half(i, core), 0)),
        pl.BlockSpec((1, width, states // 2), lambda i, core: (layer, 0, half(i, core))),
    )

    def body(core_ref, *refs):
        put_halves(core_ref, pieces, *refs[: 2 * pieces], *refs[-3:])

    return pl.pallas_call(
        body,
        name="put_in_place",
        out_shape=tuple(jax.ShapeDtypeStruct(*out) for out in outs),
        grid_spec=pltpu.PrefetchScalarGridSpec(
            num_scalar_prefetch=1,
            grid=(2,),
            in_specs=[vmem] * (2 * pieces) + [pl.BlockSpec(memory_space=pl.ANY)] * len(before),
            out_specs=blocks,
        ),
        input_output_aliases={1 + 2 * pieces + i: i for i in range(len(before))},
        compiler_params=pltpu.CompilerParams(vmem_limit_bytes=VMEM_LIMIT),
    )(core, *own, *other, *before)


def gather_at_once(value, axes):
    size = 1
    for axis in axes:
        size *= lax.axis_size(axis)
    copies = jnp.broadcast_to(value[None], (size,) + value.shape)
    return lax.all_to_all(copies, axes, 0, 0, tiled=True)


def add_by_pairs(value):
    found = None
    for name, size, stride, count, mine in axis_parts():
        bit = 1
        while bit < size:
            if found is not None:
                value = value + found
            pairs = []
            for i in range(count):
                place = (i // stride) % size
                pairs.append((i, i + ((place ^ bit) - place) * stride))
            found = lax.ppermute(value, name, pairs)
            bit *= 2
    return value, found


def axis_parts():
    count = lax.axis_size("seq")
    mine = lax.axis_index("seq")
    outer = 1
    while outer * outer * 2 < count:
        outer *= 2
    inner = count // (2 * outer)
    parts = []
    for size, stride in ((2, 1), (inner, 2), (outer, 2 * inner)):
        parts.append(("seq", size, stride, count, (mine // stride) % size))
    size = lax.axis_size("dp")
    parts.append(("dp", size, 1, size, lax.axis_index("dp")))
    return parts


def shifted(value, part, away):
    name, size, stride, count, mine = part
    pairs = []
    for i in range(count):
        place = (i // stride) % size
        pairs.append((i, i + ((place + away) % size - place) * stride))
    return lax.ppermute(value, name, pairs)


def scatter_sum(value, part):
    name, size, stride, count, mine = part
    rows = value.shape[-2] // size

    def piece(place):
        return lax.dynamic_slice_in_dim(value, place * rows, rows, axis=value.ndim - 2)

    found = [shifted(piece((mine + away) % size), part, away) for away in range(1, size)]
    return sum(found, piece(mine))


def gather_rows(value, part):
    name, size, stride, count, mine = part
    axis = value.ndim - 2
    rows = value.shape[axis]
    found = [value] + [shifted(value, part, away) for away in range(1, size)]
    if size == 2:
        low = jnp.where(mine == 0, found[0], found[1])
        high = jnp.where(mine == 0, found[1], found[0])
        return jnp.concatenate([low, high], axis=axis)
    shape = value.shape[:axis] + (rows * size,) + value.shape[axis + 1 :]
    out = jnp.zeros(shape, value.dtype)
    for away in range(size):
        out = lax.dynamic_update_slice_in_dim(
            out, found[away], ((mine - away) % size) * rows, axis=axis
        )
    return out


def sum_over_links(own, sent):
    core, inner, outer, depth = axis_parts()
    own = own + shifted(sent, core, 1)
    cols = own.shape[1] // 2
    left, right = own[:, :cols], own[:, cols:]
    left, right = scatter_sum(left, inner), scatter_sum(right, outer)
    left, right = scatter_sum(left, outer), scatter_sum(right, inner)
    both = gather_rows(scatter_sum(jnp.stack([left, right]), depth), depth)
    left, right = both[0], both[1]
    left, right = gather_rows(left, outer), gather_rows(right, inner)
    left, right = gather_rows(left, inner), gather_rows(right, outer)
    own = jnp.concatenate([left, right], axis=1)
    return own, shifted(own, core, 1)


def discretize(lam_re, lam_im, log_step):
    step_size = jnp.exp(log_step)
    decay_abs = jnp.exp(lam_re * step_size)
    rotation = lam_im * step_size
    dec_re = decay_abs * jnp.cos(rotation)
    dec_im = decay_abs * jnp.sin(rotation)
    denom_sq = lam_re * lam_re + lam_im * lam_im
    inj_re = ((dec_re - 1.0) * lam_re + dec_im * lam_im) / denom_sq
    inj_im = (dec_im * lam_re - (dec_re - 1.0) * lam_im) / denom_sq
    return (dec_re, dec_im, inj_re, inj_im)


def per_device(
    block_in, cotangent, doc_lengths, norm_gain, norm_shift, log_step, lam_re, lam_im,
    b_proj, c_proj, d_skip, w_gate,
):
    batches, seqs, span, width = block_in.shape
    assert seqs == 1 and span % (4 * CHUNKS) == 0 and span & (span - 1) == 0
    half = lam_re.shape[1]
    groups = half // LANES
    rows = batches * span
    count = lax.axis_size("seq")
    tokens = float(seqs * lax.axis_size("dp") * span * count)
    mine = jnp.reshape(lax.axis_index("seq"), (1,)).astype(jnp.int32)
    core = mine % 2
    place = (doc_lengths, mine)
    disc = discretize(lam_re, lam_im, log_step)

    x = block_in.reshape(rows, width)
    cot = cotangent.reshape(rows, width)
    lower = (0, False, batches, span, groups, tokens, count)
    upper = (1, True, batches, span, groups, tokens, count)
    part = functools.partial

    flat, low = ((rows, width), f32), ((rows, width), bf16)
    wide, wide_low = ((rows, 2 * half), f32), ((rows, 2 * half), bf16)
    padded = ((batches * (span + CHUNKS), 2 * half), f32)
    sums = ((2 * batches, width), f32)
    prefix = ((2, batches * CHUNKS, 2 * half), f32)
    total = ((batches, 2 * half), f32)
    line, shared = ((1, width), f32), ((2, width), f32)
    small = ((8, width), f32)

    def gather_row(value):
        return lax.all_gather(value, "seq")

    ordered, stats = run(
        part(first_sums, batches, span), "first_sums", (x,), (low, sums), scalars=0
    )

    def forward(cfg, hidden, stats):
        return run(
            part(enter_layer, cfg),
            "enter_layer",
            (place, stats, hidden, norm_gain, norm_shift, disc, b_proj),
            (low, wide, prefix, total, sums),
        )

    everywhere = gather_at_once(stats, ("dp", "seq"))
    u0, drive0, prefix0, total0, norm0 = forward(lower, ordered, (jnp.sum(everywhere, axis=0),))
    states0, states_low0, act0, sig0, slope0, hidden1, stats = run(
        part(middle_forward, lower),
        "middle_forward",
        (
            place, gather_at_once(total0, ("seq",)), prefix0, disc, drive0, u0, ordered, c_proj,
            d_skip, w_gate,
        ),
        (padded, wide_low, low, flat, flat, flat, sums),
        (flat,),
    )
    u1, drive1, prefix1, total1, norm1 = forward(upper, hidden1, add_by_pairs(stats))
    (
        block_out, ordered_cot, states1, states_low1, act1, grad_gate1, grad_mixed1, grad_low1,
        source1, prefix1, total1, grad_d1,
    ) = run(
        part(turn_around, upper),
        "turn_around",
        (
            place, gather_row(total1), prefix1, disc, drive1, u1, hidden1, c_proj, d_skip, w_gate,
            cot,
        ),
        (low, low, padded, wide_low, low, low, flat, low, wide, prefix, total, line),
        (flat, flat, flat, low),
    )

    def finish(cfg, ends, prefix, source, drive, states, u, grad_mixed, grad_d, hidden, norm):
        return run(
            part(backward_finish, cfg),
            "backward_finish",
            (
                place, ends, prefix, disc, source, drive, states, u, grad_mixed, grad_d, hidden,
                norm, d_skip, b_proj,
            ),
            (wide_low, flat, sums, small),
        )

    def halves(length):
        return (((length // 2, width), f32),) * 2

    grad_proj1, grad_u1, stats, small1 = finish(
        upper, gather_row(total1), prefix1, source1, drive1, states1, u1, grad_mixed1, grad_d1,
        hidden1, norm1,
    )
    weights1 = run(
        all_weights,
        "all_weights",
        (core, act1, grad_gate1, states_low1, grad_low1, grad_proj1, u1),
        halves(width + 4 * half),
    )
    stats = add_by_pairs(stats)
    weights1, stats = lax.optimization_barrier((weights1, stats))
    (
        grad_out0, shared1, grad_gate0, grad_mixed0, grad_low0, source0, prefix0, total0, grad_d0,
    ) = run(
        part(between_layers, upper, lower),
        "between_layers",
        (
            place, stats, ordered_cot, grad_u1, hidden1, norm1, norm_gain,
            disc, u0, c_proj, w_gate, states_low0, act0, sig0, slope0,
        ),
        (flat, shared, low, flat, low, wide, prefix, total, line),
        (flat,),
    )
    gates0 = run(
        gate_weights, "gate_weights", (core, act0, grad_gate0, states_low0, grad_low0),
        halves(width + 2 * half),
    )
    gates0, ends = lax.optimization_barrier((gates0, gather_row(total0)))
    grad_proj0, grad_u0, stats, small0 = finish(
        lower, ends, prefix0, source0, drive0, states0, u0, grad_mixed0, grad_d0, ordered, norm0
    )
    inputs0 = run(input_weights, "input_weights", (core, grad_proj0, u0), halves(2 * half))
    grad_input, shared0 = run(
        part(last_step, lower),
        "last_step",
        (add_by_pairs(stats), grad_out0, grad_u0, ordered, norm0, norm_gain),
        (flat, shared),
        (((width // LANES, rows, LANES), f32),),
        scalars=0,
    )
    small_pair = add_by_pairs(jnp.stack([small0, small1]))
    small_sum = small_pair[0] + small_pair[1]
    final = (((2, width, width), f32), ((2, 2 * half, width), f32), ((2, width, 2 * half), f32))
    own1, other1 = sum_over_links(*weights1)
    placed = put_in_place(1, core, (own1,), (other1,), final, ())
    own_gates, other_gates = sum_over_links(*gates0)
    own_inputs, other_inputs = sum_over_links(*inputs0)
    grad_w, grad_c, grad_b = put_in_place(
        0, core, (own_gates, own_inputs), (other_gates, other_inputs), final, placed
    )
    _, pullback = jax.vjp(discretize, lam_re, lam_im, log_step)
    grad_lr, grad_li, grad_ls = pullback(tuple(small_sum[:, kind, :half] for kind in range(4)))
    both = jnp.stack([shared0, shared1])
    shape = block_in.shape
    return (
        block_out.reshape(shape), grad_input.reshape(shape), both[:, 0], both[:, 1],
        grad_ls, grad_lr, grad_li, grad_b, grad_c, small_sum[:, 4], grad_w,
    )


def solution(mesh):
    split = P(None, "dp", "seq", None)
    return jax.shard_map(
        per_device,
        mesh=mesh,
        in_specs=(split, split, P(None, "dp", None)) + (P(),) * 9,
        out_specs=(split, split) + (P(),) * 9,
        check_vma=False,
    )
```

```python
import functools

import jax
import jax.numpy as jnp
from jax import lax
from jax.experimental import pallas as pl
from jax.experimental.pallas import tpu as pltpu
from jax.sharding import PartitionSpec as P

f32, bf16 = jnp.float32, jnp.bfloat16
epsilon = 1e-05
tanh_scale = 0.7978845608028654
cubic_term = 0.044715
LANES = 128
CHUNKS = 8
ROWS = 32
VMEM_LIMIT = 26 * 1024 * 1024


def dot(left, right, contract=(1, 0)):
    return lax.dot_general(
        left, right, (((contract[0],), (contract[1],)), ((), ())), preferred_element_type=f32
    )


def reorder(span, inverse):
    shape = (span, span)
    kept, moved = (1, 0) if inverse else (0, 1)
    row = lax.broadcasted_iota(jnp.int32, shape, kept)
    position = lax.broadcasted_iota(jnp.int32, shape, moved)
    source = (row & (CHUNKS - 1)) * (span // CHUNKS) + (row >> 3)
    return jnp.where(position == source, 1.0, 0.0).astype(bf16)


def row_loop(count, body, init=0, step=ROWS):
    def one(index, carry):
        return body(pl.multiple_of(index * step, step), carry)

    return lax.fori_loop(0, count // step, one, init)


def documents(lengths, mine, batches, span, count):
    first = mine[0] * span
    out = []
    for batch in range(batches):
        begins, ends, so_far = [], [], 0
        for doc in range(lengths.shape[2]):
            begins.append(so_far)
            so_far = so_far + lengths[batch, 0, doc]
            ends.append(so_far)
        before, after = 0, 2 * count * span
        for begin, end in zip(begins, ends):
            before = jnp.maximum(before, jnp.where(begin < first, begin, 0))
            after = jnp.minimum(after, jnp.where(end > first + span, end, 2 * count * span))
        after = jnp.where(mine[0] == count - 1, 0, after)
        out.append(begins + ends + [before, after, first, mine[0]])
    return out


def place_documents(cfg, place):
    layer, reverse, batches, span, groups, tokens, count = cfg
    return documents(*place, batches, span, count)


def keep_of(meta, batch, base, step, backward):
    docs = (len(meta[batch]) - 4) // 2
    off = docs if backward else 0
    late = 1 if backward else 0
    stop = base == meta[batch][off] - step - late
    for doc in range(1, docs):
        stop = jnp.logical_or(stop, base == meta[batch][off + doc] - step - late)
    return jnp.where(stop, 0.0, 1.0)


def base_positions(meta, steps):
    return meta[0][-2] + lax.broadcasted_iota(jnp.int32, (CHUNKS, LANES), 0) * steps


def lanes_of(index, half=0):
    return slice(half + index * LANES, half + (index + 1) * LANES)


def coef_tiles(value, groups):
    return [
        tuple(jnp.broadcast_to(part[:, lanes_of(q)], (CHUNKS, LANES)) for part in value)
        for q in range(groups)
    ]


def constants(disc, layer):
    dec_re, dec_im, inj_re, inj_im = (part[layer : layer + 1, :] for part in disc)
    return (dec_re, dec_im), (inj_re, inj_im)


def times(a, b):
    return (a[0] * b[0] - a[1] * b[1], a[0] * b[1] + a[1] * b[0])


def power(value, exponent):
    for _ in range(exponent.bit_length() - 1):
        value = times(value, value)
    return value


def conj(value):
    return (value[0], -value[1])


def scan(meta, source, inject, dec, batches, span, groups, reverse, masks_reverse, init, extra, visit):
    steps = span // CHUNKS
    half = groups * LANES
    base = base_positions(meta, steps)

    def pair(index, carry):
        states, more = carry
        states = list(states)
        first = steps - 2 - 2 * index if reverse else 2 * index
        start = pl.multiple_of(first * CHUNKS, 2 * CHUNKS)
        order = (1, 0) if reverse else (0, 1)
        for batch in range(batches):
            keeps = [keep_of(meta, batch, base, first + j, masks_reverse) for j in (0, 1)]
            for q in range(groups):
                rows = pl.ds(batch * span + start, 2 * CHUNKS)
                src_re = source[rows, lanes_of(q)]
                src_im = source[rows, lanes_of(q, half)]
                state = states[batch * groups + q]
                found = [None, None]
                for j in order:
                    part = (
                        src_re[j * CHUNKS : (j + 1) * CHUNKS],
                        src_im[j * CHUNKS : (j + 1) * CHUNKS],
                    )
                    push = times(inject[q], part) if inject is not None else part
                    held = times((keeps[j] * dec[q][0], keeps[j] * dec[q][1]), state)
                    state = (held[0] + push[0], held[1] + push[1])
                    found[j] = state
                states[batch * groups + q] = state
                more = visit(more, batch, q, first, start, found, (src_re, src_im))
            more = visit(more, batch, None, first, start, keeps, None)
        return tuple(states), more

    return lax.fori_loop(0, steps // 2, pair, (tuple(init), extra), unroll=2)


def zero_states(batches, groups):
    zero = jnp.zeros((CHUNKS, LANES), f32)
    return [(zero, zero)] * (batches * groups)


def local_ends(meta, source, inject, dec, batches, span, groups, reverse, prefix, total):
    ones = tuple(jnp.ones((CHUNKS, LANES), f32) for _ in range(batches))

    def visit(more, batch, q, first, start, found, src):
        if q is not None:
            return more
        return tuple(
            value * found[0] * found[1] if at == batch else value for at, value in enumerate(more)
        )

    dec_chunk = coef_tiles(power(dec, span // CHUNKS), groups)
    ends, kept = scan(
        meta, source, inject, coef_tiles(dec, groups), batches, span, groups, reverse, reverse,
        zero_states(batches, groups), ones, visit,
    )
    half = groups * LANES
    row = lax.broadcasted_iota(jnp.int32, (CHUNKS, LANES), 0)
    for batch in range(batches):
        for q in range(groups):
            end = ends[batch * groups + q]
            decay = (kept[batch] * dec_chunk[q][0], kept[batch] * dec_chunk[q][1])
            for shift in (1, 2, 4):
                turn = CHUNKS - shift if reverse else shift
                valid = row < CHUNKS - shift if reverse else row >= shift
                before = [pltpu.roll(value, turn, 0) for value in (*end, *decay)]
                from_before = times(decay, (before[0], before[1]))
                end = (
                    end[0] + jnp.where(valid, from_before[0], 0.0),
                    end[1] + jnp.where(valid, from_before[1], 0.0),
                )
                longer = times(decay, (before[2], before[3]))
                decay = (
                    jnp.where(valid, longer[0], decay[0]),
                    jnp.where(valid, longer[1], decay[1]),
                )
            rows = slice(batch * CHUNKS, (batch + 1) * CHUNKS)
            prefix[0, rows, lanes_of(q)] = end[0]
            prefix[0, rows, lanes_of(q, half)] = end[1]
            prefix[1, rows, lanes_of(q)] = decay[0]
            prefix[1, rows, lanes_of(q, half)] = decay[1]
            last = 0 if reverse else CHUNKS - 1
            total[batch : batch + 1, lanes_of(q)] = end[0][last : last + 1]
            total[batch : batch + 1, lanes_of(q, half)] = end[1][last : last + 1]


def chunk_carries(meta, gathered, dec, prefix, batches, span, groups, reverse):
    count = gathered.shape[0]
    half = groups * LANES
    dec_span = power(dec, span)
    row = lax.broadcasted_iota(jnp.int32, (CHUNKS, LANES), 0)
    mine = meta[0][-1]
    out = []
    for batch in range(batches):

        def add(at, so_far, batch=batch):
            away = count - 2 - at
            if reverse:
                other = mine + 1 + away
                reaches = meta[batch][-3] > other * span
            else:
                other = mine - 1 - away
                reaches = meta[batch][-4] < (mine - away) * span
            other = jnp.clip(other, 0, count - 1)
            value = jnp.where(reaches, gathered[other, pl.ds(batch, 1), :], 0.0)
            moved = times(dec_span, so_far)
            return (moved[0] + value[:, :half], moved[1] + value[:, half:])

        zero = jnp.zeros((1, half), f32)
        enter = lax.fori_loop(0, count - 1, add, (zero, zero), unroll=count <= 8)
        rows = slice(batch * CHUNKS, (batch + 1) * CHUNKS)
        for q in range(groups):
            own = tuple(jnp.broadcast_to(part[:, lanes_of(q)], (CHUNKS, LANES)) for part in enter)
            end = (prefix[0, rows, lanes_of(q)], prefix[0, rows, lanes_of(q, half)])
            decay = (prefix[1, rows, lanes_of(q)], prefix[1, rows, lanes_of(q, half)])
            moved = times(decay, own)
            turn, first = (CHUNKS - 1, CHUNKS - 1) if reverse else (1, 0)
            out.append(
                tuple(
                    jnp.where(row == first, own[i], pltpu.roll(end[i] + moved[i], turn, 0))
                    for i in (0, 1)
                )
            )
    return out


def add_sums(target, batches, sums):
    for kind, per_batch in enumerate(sums):
        for batch in range(batches):
            target[kind * batches + batch : kind * batches + batch + 1, :] = jnp.sum(
                per_batch[batch], axis=0, keepdims=True
            )


def fold(value):
    return sum(value[i : i + CHUNKS] for i in range(CHUNKS, value.shape[0], CHUNKS)) + value[:CHUNKS]


def first_sums(batches, span, x, ordered, stats):
    turn = reorder(span, False)
    width = x.shape[1]
    sums, squares = [], []
    for batch in range(batches):
        rows = slice(batch * span, (batch + 1) * span)
        ordered[rows, :] = dot(turn, x[rows, :]).astype(bf16)

        def body(start, carry, batch=batch):
            value = x[pl.ds(batch * span + start, ROWS), :].astype(f32)
            return carry[0] + fold(value), carry[1] + fold(value * value)

        zero = jnp.zeros((CHUNKS, width), f32)
        one, two = row_loop(span, body, (zero, zero))
        sums.append(one)
        squares.append(two)
    add_sums(stats, batches, (sums, squares))


def enter_layer(
    cfg, place, stats, hidden, gain, shift, disc, b_proj, u, drive, prefix, total, norm
):
    layer, reverse, batches, span, groups, tokens, count = cfg
    sums = sum(part[...] for part in stats)
    average = sums[:batches] / tokens
    spread = sums[batches:] / tokens - average * average
    scale = lax.rsqrt(spread + epsilon)
    norm[:batches, :] = average
    norm[batches:, :] = scale
    gain_now, shift_now = gain[layer : layer + 1, :], shift[layer : layer + 1, :]
    for batch in range(batches):

        def body(start, carry, batch=batch):
            rows = pl.ds(batch * span + start, ROWS)
            normed = (hidden[rows, :].astype(f32) - average[batch : batch + 1]) * scale[
                batch : batch + 1
            ]
            u[rows, :] = (normed * gain_now + shift_now).astype(bf16)
            return carry

        row_loop(span, body)
    drive[...] = dot(u[...], b_proj[layer])
    meta = place_documents(cfg, place)
    dec, inj = constants(disc, layer)
    local_ends(
        meta, drive, coef_tiles(inj, groups), dec, batches, span, groups, reverse, prefix, total
    )


def finish_states(cfg, meta, ends, prefix, disc, drive, states, states_low):
    layer, reverse, batches, span, groups, tokens, count = cfg
    half = groups * LANES
    padded = span + CHUNKS
    dec, inj = constants(disc, layer)
    init = chunk_carries(meta, ends, dec, prefix, batches, span, groups, reverse)
    for batch in range(batches):
        edge = batch * padded + (span if reverse else 0)
        for q in range(groups):
            states[edge : edge + CHUNKS, lanes_of(q)] = init[batch * groups + q][0]
            states[edge : edge + CHUNKS, lanes_of(q, half)] = init[batch * groups + q][1]

    def visit(more, batch, q, first, start, found, src):
        if q is not None:
            for part, off in ((0, 0), (1, half)):
                both = jnp.concatenate([found[0][part], found[1][part]], axis=0)
                at = batch * padded + (0 if reverse else CHUNKS)
                states[pl.ds(at + start, 2 * CHUNKS), lanes_of(q, off)] = both
                states_low[pl.ds(batch * span + start, 2 * CHUNKS), lanes_of(q, off)] = both.astype(
                    bf16
                )
        return more

    scan(
        meta, drive, coef_tiles(inj, groups), coef_tiles(dec, groups), batches, span, groups,
        reverse, reverse, init, 0, visit,
    )


def forward_finish(
    cfg, meta, ends, prefix, disc, drive, u, hidden, c_proj, d_skip, w_gate,
    states, states_low, act, sig, slope, result, wide, emit,
):
    layer, reverse, batches, span, groups, tokens, count = cfg
    finish_states(cfg, meta, ends, prefix, disc, drive, states, states_low)
    wide[...] = dot(states_low[...], c_proj[layer])
    skip = d_skip[layer : layer + 1, :]

    def body(start, carry):
        rows = pl.ds(start, ROWS)
        mixed = wide[rows, :] + skip * u[rows, :].astype(f32)
        square = mixed * mixed
        th = jnp.tanh(tanh_scale * (mixed + cubic_term * square * mixed))
        half_one = 0.5 * (1.0 + th)
        act[rows, :] = (mixed * half_one).astype(bf16)
        slope[rows, :] = half_one + 0.5 * mixed * (1.0 - th * th) * tanh_scale * (
            1.0 + 3.0 * cubic_term * square
        )
        return carry

    row_loop(batches * span, body)
    wide[...] = dot(act[...], w_gate[layer])
    sums, squares = [], []
    for batch in range(batches):

        def gate(start, carry, batch=batch):
            rows = pl.ds(batch * span + start, ROWS)
            sig_now = 0.5 + 0.5 * jnp.tanh(0.5 * wide[rows, :])
            sig[rows, :] = sig_now
            value = hidden[rows, :].astype(f32) + act[rows, :].astype(f32) * sig_now
            result[rows, :] = value.astype(result.dtype)
            if emit is None:
                return carry
            return carry[0] + fold(value), carry[1] + fold(value * value)

        zero = jnp.zeros((CHUNKS, wide.shape[1]), f32)
        one, two = row_loop(span, gate, (zero, zero))
        sums.append(one)
        squares.append(two)
    if emit is not None:
        add_sums(emit, batches, (sums, squares))


def backward_start(
    cfg, meta, grad_out, disc, u, c_proj, w_gate, states_low, act, sig, slope,
    grad_gate, grad_mixed, grad_low, source, prefix, total, grad_d, wide,
):
    layer, reverse, batches, span, groups, tokens, count = cfg

    def body(start, carry):
        rows = pl.ds(start, ROWS)
        sig_now = sig[rows, :]
        grad_gate[rows, :] = (
            grad_out[rows, :].astype(f32) * act[rows, :].astype(f32) * sig_now * (1.0 - sig_now)
        ).astype(bf16)
        return carry

    row_loop(batches * span, body)
    wide[...] = dot(grad_gate[...], w_gate[layer], (1, 1))

    def mixed(start, carry):
        rows = pl.ds(start, ROWS)
        value = (grad_out[rows, :].astype(f32) * sig[rows, :] + wide[rows, :]) * slope[rows, :]
        grad_mixed[rows, :] = value
        grad_low[rows, :] = value.astype(bf16)
        return carry + fold(value * u[rows, :].astype(f32))

    gd = row_loop(batches * span, mixed, jnp.zeros((CHUNKS, wide.shape[1]), f32))
    grad_d[...] = jnp.sum(gd, axis=0, keepdims=True)
    source[...] = dot(grad_low[...], c_proj[layer], (1, 1))
    local_ends(
        meta, source, None, conj(constants(disc, layer)[0]), batches, span, groups, not reverse,
        prefix, total,
    )


def middle_forward(
    cfg, place, ends, prefix, disc, drive, u, hidden, c_proj, d_skip, w_gate,
    states, states_low, act, sig, slope, result, stats, wide,
):
    meta = place_documents(cfg, place)
    forward_finish(
        cfg, meta, ends, prefix, disc, drive, u, hidden, c_proj, d_skip, w_gate,
        states, states_low, act, sig, slope, result, wide, stats,
    )


def turn_around(
    cfg, place, ends, prefix, disc, drive, u, hidden, c_proj, d_skip, w_gate, cotangent,
    block_out, ordered_cot, states, states_low, act, grad_gate, grad_mixed, grad_low, source,
    back_prefix, total, grad_d, sig, slope, wide, result,
):
    layer, reverse, batches, span, groups, tokens, count = cfg
    meta = place_documents(cfg, place)
    turn, back = reorder(span, False), reorder(span, True)
    for batch in range(batches):
        rows = slice(batch * span, (batch + 1) * span)
        ordered_cot[rows, :] = dot(turn, cotangent[rows, :]).astype(bf16)
    forward_finish(
        cfg, meta, ends, prefix, disc, drive, u, hidden, c_proj, d_skip, w_gate,
        states, states_low, act, sig, slope, result, wide, None,
    )
    for batch in range(batches):
        rows = slice(batch * span, (batch + 1) * span)
        block_out[rows, :] = dot(back, result[rows, :]).astype(bf16)
    backward_start(
        cfg, meta, ordered_cot, disc, u, c_proj, w_gate, states_low, act, sig, slope,
        grad_gate, grad_mixed, grad_low, source, back_prefix, total, grad_d, wide,
    )


def backward_finish(
    cfg, place, ends, prefix, disc, source, drive, states, u, grad_mixed, grad_d, hidden, norm,
    d_skip, b_proj, grad_proj, grad_u, stats, small,
):
    layer, reverse, batches, span, groups, tokens, count = cfg
    half = groups * LANES
    padded = span + CHUNKS
    steps = span // CHUNKS
    meta = place_documents(cfg, place)
    dec, inj = constants(disc, layer)
    dec = conj(dec)
    init = chunk_carries(meta, ends, dec, prefix, batches, span, groups, not reverse)
    inj = coef_tiles(inj, groups)
    base = base_positions(meta, steps)
    zero = jnp.zeros((CHUNKS, LANES), f32)

    def visit(more, batch, q, first, start, found, src):
        if q is None:
            return more
        more = list(more)
        rows = pl.ds(batch * span + start, 2 * CHUNKS)
        drive_re, drive_im = drive[rows, lanes_of(q)], drive[rows, lanes_of(q, half)]
        before = pl.ds(batch * padded + start + (CHUNKS if reverse else 0), 2 * CHUNKS)
        prior_re, prior_im = states[before, lanes_of(q)], states[before, lanes_of(q, half)]
        dec_re, dec_im, inj_re, inj_im = more[q]
        out_re, out_im = [], []
        for j in (0, 1):
            part = slice(j * CHUNKS, (j + 1) * CHUNKS)
            adj_re, adj_im = found[j]
            keep = keep_of(meta, batch, base, first + j, reverse)
            kept_re, kept_im = keep * adj_re, keep * adj_im
            dec_re = dec_re + kept_re * prior_re[part] + kept_im * prior_im[part]
            dec_im = dec_im + kept_im * prior_re[part] - kept_re * prior_im[part]
            inj_re = inj_re + adj_re * drive_re[part] + adj_im * drive_im[part]
            inj_im = inj_im + adj_im * drive_re[part] - adj_re * drive_im[part]
            out_re.append(inj[q][0] * adj_re + inj[q][1] * adj_im)
            out_im.append(inj[q][0] * adj_im - inj[q][1] * adj_re)
        grad_proj[rows, lanes_of(q)] = jnp.concatenate(out_re, axis=0).astype(bf16)
        grad_proj[rows, lanes_of(q, half)] = jnp.concatenate(out_im, axis=0).astype(bf16)
        more[q] = (dec_re, dec_im, inj_re, inj_im)
        return tuple(more)

    _, sums = scan(
        meta, source, None, coef_tiles(dec, groups), batches, span, groups,
        not reverse, not reverse, init, ((zero,) * 4,) * groups, visit,
    )
    small[...] = jnp.zeros_like(small)
    for q in range(groups):
        for kind in range(4):
            small[kind : kind + 1, lanes_of(q)] = jnp.sum(sums[q][kind], axis=0, keepdims=True)
    small[4:5, :] = grad_d[...]
    grad_u[...] = dot(grad_proj[...], b_proj[layer], (1, 1))
    skip = d_skip[layer : layer + 1, :]
    plain, times_normed = [], []
    for batch in range(batches):
        average = norm[batch : batch + 1, :]
        scale = norm[batches + batch : batches + batch + 1, :]

        def body(start, carry, batch=batch, average=average, scale=scale):
            rows = pl.ds(batch * span + start, ROWS)
            value = grad_u[rows, :] + grad_mixed[rows, :] * skip
            grad_u[rows, :] = value
            normed = (hidden[rows, :].astype(f32) - average) * scale
            return carry[0] + fold(value), carry[1] + fold(value * normed)

        zero_sum = jnp.zeros((CHUNKS, grad_u.shape[1]), f32)
        one, two = row_loop(span, body, (zero_sum, zero_sum))
        plain.append(one)
        times_normed.append(two)
    add_sums(stats, batches, (plain, times_normed))


def norm_backward(cfg, stats, grad_out, grad_u, hidden, norm, gain, store, shared):
    layer, reverse, batches, span, groups, tokens, count = cfg
    sums = sum(part[...] for part in stats)
    shared[0:1, :] = jnp.sum(sums[batches:], axis=0, keepdims=True)
    shared[1:2, :] = jnp.sum(sums[:batches], axis=0, keepdims=True)
    gain_now = gain[layer : layer + 1, :]
    for batch in range(batches):
        average = norm[batch : batch + 1, :]
        scale = norm[batches + batch : batches + batch + 1, :]
        plain = gain_now * sums[batch : batch + 1] / tokens
        slanted = gain_now * sums[batches + batch : batches + batch + 1] / tokens

        def body(start, carry, batch=batch, average=average, scale=scale, plain=plain, slanted=slanted):
            rows = pl.ds(batch * span + start, ROWS)
            normed = (hidden[rows, :].astype(f32) - average) * scale
            value = grad_out[rows, :].astype(f32) + scale * (
                grad_u[rows, :] * gain_now - plain - normed * slanted
            )
            store(rows, value)
            return carry

        row_loop(span, body)


def between_layers(
    cfg, lower, place, stats, upper_out, upper_u, upper_hidden, upper_norm, gain,
    disc, u, c_proj, w_gate, states_low, act, sig, slope,
    grad_out, shared, grad_gate, grad_mixed, grad_low, source, prefix, total, grad_d, wide,
):
    def store(rows, value):
        grad_out[rows, :] = value

    norm_backward(cfg, stats, upper_out, upper_u, upper_hidden, upper_norm, gain, store, shared)
    meta = place_documents(lower, place)
    backward_start(
        lower, meta, grad_out, disc, u, c_proj, w_gate, states_low, act, sig, slope,
        grad_gate, grad_mixed, grad_low, source, prefix, total, grad_d, wide,
    )


def last_step(cfg, stats, grad_out, grad_u, hidden, norm, gain, target, shared, ordered):
    layer, reverse, batches, span, groups, tokens, count = cfg
    planes = target.shape[1] // LANES

    def store(rows, value):
        for plane in range(planes):
            ordered[plane, rows, :] = value[:, lanes_of(plane)]

    norm_backward(cfg, stats, grad_out, grad_u, hidden, norm, gain, store, shared)
    steps = span // CHUNKS
    for batch in range(batches):
        for chunk in range(CHUNKS):
            at = batch * span
            for plane in range(planes):
                target[at + chunk * steps : at + (chunk + 1) * steps, lanes_of(plane)] = ordered[
                    plane, pl.ds(at + chunk, steps, stride=CHUNKS), :
                ]


def half_weights(core, refs, own, sent):
    for target, half in ((own, core), (sent, 1 - core)):
        at = 0
        for left, right in refs:
            rows = left.shape[1] // 2
            cols = pl.ds(pl.multiple_of(half * rows, LANES), rows)
            target[at : at + rows, :] = dot(left[:, cols], right[...], (0, 0))
            at += rows


def all_weights(core, act, grad_gate, states_low, grad_low, grad_proj, u, own, sent):
    refs = ((act, grad_gate), (states_low, grad_low), (grad_proj, u))
    half_weights(core[0], refs, own, sent)


def gate_weights(core, act, grad_gate, states_low, grad_low, own, sent):
    half_weights(core[0], ((act, grad_gate), (states_low, grad_low)), own, sent)


def input_weights(core, grad_proj, u, own, sent):
    half_weights(core[0], ((grad_proj, u),), own, sent)


def run(body, name, args, outs, scratch=(), scalars=1):
    vmem, smem = pl.BlockSpec(memory_space=pltpu.VMEM), pl.BlockSpec(memory_space=pltpu.SMEM)
    specs = tuple(
        jax.tree.map(lambda _, at=at: smem if at < scalars else vmem, arg)
        for at, arg in enumerate(args)
    )
    return pl.pallas_call(
        body,
        name=name,
        out_shape=tuple(jax.ShapeDtypeStruct(*out) for out in outs),
        in_specs=specs,
        out_specs=(vmem,) * len(outs),
        scratch_shapes=[pltpu.VMEM(*entry) for entry in scratch],
        compiler_params=pltpu.CompilerParams(vmem_limit_bytes=VMEM_LIMIT),
    )(*args)


def put_halves(core, pieces, *refs):
    grad_w, grad_c, grad_b = refs[-3:]
    step = pl.program_id(0)
    for now in (0, 1):

        @pl.when(step == now)
        def _(now=now):
            rows_w, rows_c = grad_w.shape[1], grad_c.shape[1]
            sources = refs[now * pieces : (now + 1) * pieces]
            gates = sources[0]
            grad_w[0] = gates[:rows_w, :]
            grad_c[0] = gates[rows_w : rows_w + rows_c, :]
            last = sources[-1]
            at = rows_w + rows_c if pieces == 1 else 0
            grad_b[0] = last[at : at + rows_c, :].T


def put_in_place(layer, core, own, other, outs, before):
    width, states = outs[0][0][1], outs[1][0][1]
    pieces = len(own)
    vmem = pl.BlockSpec(memory_space=pltpu.VMEM)

    def half(step, core):
        return jnp.where(step == 0, core[0], 1 - core[0])

    blocks = (
        pl.BlockSpec((1, width // 2, width), lambda i, core: (layer, half(i, core), 0)),
        pl.BlockSpec((1, states // 2, width), lambda i, core: (layer, half(i, core), 0)),
        pl.BlockSpec((1, width, states // 2), lambda i, core: (layer, 0, half(i, core))),
    )

    def body(core_ref, *refs):
        put_halves(core_ref, pieces, *refs[: 2 * pieces], *refs[-3:])

    return pl.pallas_call(
        body,
        name="put_in_place",
        out_shape=tuple(jax.ShapeDtypeStruct(*out) for out in outs),
        grid_spec=pltpu.PrefetchScalarGridSpec(
            num_scalar_prefetch=1,
            grid=(2,),
            in_specs=[vmem] * (2 * pieces) + [pl.BlockSpec(memory_space=pl.ANY)] * len(before),
            out_specs=blocks,
        ),
        input_output_aliases={1 + 2 * pieces + i: i for i in range(len(before))},
        compiler_params=pltpu.CompilerParams(vmem_limit_bytes=VMEM_LIMIT),
    )(core, *own, *other, *before)


def gather_at_once(value, axes):
    size = 1
    for axis in axes:
        size *= lax.axis_size(axis)
    copies = jnp.broadcast_to(value[None], (size,) + value.shape)
    return lax.all_to_all(copies, axes, 0, 0, tiled=True)


def axis_parts():
    count = lax.axis_size("seq")
    mine = lax.axis_index("seq")
    depth = lax.axis_size("dp")
    return (
        ("seq", 2, 1, count, mine % 2),
        ("seq", count // 2, 2, count, mine // 2),
        ("dp", depth, 1, depth, lax.axis_index("dp")),
    )


def add_by_pairs(value):
    found = None
    for name, size, stride, count, mine in axis_parts():
        bit = 1
        while bit < size:
            if found is not None:
                value = value + found
            pairs = []
            for i in range(count):
                place = (i // stride) % size
                pairs.append((i, i + ((place ^ bit) - place) * stride))
            found = lax.ppermute(value, name, pairs)
            bit *= 2
    return value, found


def shifted(value, part, away):
    name, size, stride, count, mine = part
    pairs = []
    for i in range(count):
        place = (i // stride) % size
        pairs.append((i, i + ((place + away) % size - place) * stride))
    return lax.ppermute(value, name, pairs)


def add_and_cut(mine, *refs):
    size = len(refs) - add_and_cut_terms(refs)
    terms, pieces = refs[: len(refs) - size], refs[len(refs) - size :]
    rows = pieces[0].shape[0]
    for away, piece in enumerate(pieces):
        at = lax.rem(mine[0] + away, size) * rows
        where = pl.ds(pl.multiple_of(at, CHUNKS), rows)
        piece[...] = sum(term[where, :] for term in terms)


def add_and_cut_terms(refs):
    return sum(ref.shape[0] == refs[0].shape[0] for ref in refs)


def add_terms(*refs):
    refs[-1][...] = sum(ref[...] for ref in refs[:-1])


def arrange(mine, *refs):
    out, pieces = refs[-1], refs[:-1]
    rows = pieces[0].shape[0]
    for away, piece in enumerate(pieces):
        at = lax.rem(mine[0] + len(pieces) - away, len(pieces)) * rows
        out[pl.ds(pl.multiple_of(at, CHUNKS), rows), :] = piece[...]


def place_of(part):
    return jnp.reshape(part[4], (1,)).astype(jnp.int32)


def cut(terms, part):
    rows, cols = terms[0].shape
    shape = ((rows // part[1], cols), f32)
    return run(add_and_cut, "add_and_cut", (place_of(part), *terms), (shape,) * part[1])


def spread(pieces, part):
    return [pieces[0]] + [shifted(pieces[away], part, away) for away in range(1, part[1])]


def collect(piece, part):
    pieces = [piece] + [shifted(piece, part, away) for away in range(1, part[1])]
    shape = ((piece.shape[0] * part[1], piece.shape[1]), f32)
    return run(arrange, "arrange", (place_of(part), *pieces), (shape,))[0]


def sum_over_links(own, sent):
    core, plane, depth = axis_parts()
    terms = spread(cut([own, shifted(sent, core, 1)], plane), plane)
    if terms[0].shape[0] % (CHUNKS * depth[1]) == 0:
        terms = spread(cut(terms, depth), depth)
        (value,) = run(add_terms, "add_terms", terms, ((terms[0].shape, f32),), scalars=0)
        value = collect(value, depth)
    else:
        value = lax.psum(sum(terms), "dp")
    own = collect(value, plane)
    return own, shifted(own, core, 1)


def discretize(lam_re, lam_im, log_step):
    step_size = jnp.exp(log_step)
    decay_abs = jnp.exp(lam_re * step_size)
    rotation = lam_im * step_size
    dec_re = decay_abs * jnp.cos(rotation)
    dec_im = decay_abs * jnp.sin(rotation)
    denom_sq = lam_re * lam_re + lam_im * lam_im
    inj_re = ((dec_re - 1.0) * lam_re + dec_im * lam_im) / denom_sq
    inj_im = (dec_im * lam_re - (dec_re - 1.0) * lam_im) / denom_sq
    return (dec_re, dec_im, inj_re, inj_im)


def per_device(
    block_in, cotangent, doc_lengths, norm_gain, norm_shift, log_step, lam_re, lam_im,
    b_proj, c_proj, d_skip, w_gate,
):
    batches, seqs, span, width = block_in.shape
    assert seqs == 1 and span % (4 * CHUNKS) == 0 and span & (span - 1) == 0
    half = lam_re.shape[1]
    groups = half // LANES
    rows = batches * span
    count = lax.axis_size("seq")
    tokens = float(seqs * lax.axis_size("dp") * span * count)
    mine = jnp.reshape(lax.axis_index("seq"), (1,)).astype(jnp.int32)
    core = mine % 2
    place = (doc_lengths, mine)
    disc = discretize(lam_re, lam_im, log_step)

    x = block_in.reshape(rows, width)
    cot = cotangent.reshape(rows, width)
    lower = (0, False, batches, span, groups, tokens, count)
    upper = (1, True, batches, span, groups, tokens, count)
    part = functools.partial

    flat, low = ((rows, width), f32), ((rows, width), bf16)
    wide, wide_low = ((rows, 2 * half), f32), ((rows, 2 * half), bf16)
    padded = ((batches * (span + CHUNKS), 2 * half), f32)
    sums = ((2 * batches, width), f32)
    prefix = ((2, batches * CHUNKS, 2 * half), f32)
    total = ((batches, 2 * half), f32)
    line, shared = ((1, width), f32), ((2, width), f32)
    small = ((8, width), f32)

    def gather_row(value):
        return gather_at_once(value, ("seq",))

    ordered, stats = run(
        part(first_sums, batches, span), "first_sums", (x,), (low, sums), scalars=0
    )

    def forward(cfg, hidden, stats):
        return run(
            part(enter_layer, cfg),
            "enter_layer",
            (place, stats, hidden, norm_gain, norm_shift, disc, b_proj),
            (low, wide, prefix, total, sums),
        )

    u0, drive0, prefix0, total0, norm0 = forward(lower, ordered, add_by_pairs(stats))
    states0, states_low0, act0, sig0, slope0, hidden1, stats = run(
        part(middle_forward, lower),
        "middle_forward",
        (
            place, gather_row(total0), prefix0, disc, drive0, u0, ordered, c_proj,
            d_skip, w_gate,
        ),
        (padded, wide_low, low, flat, flat, flat, sums),
        (flat,),
    )
    u1, drive1, prefix1, total1, norm1 = forward(upper, hidden1, add_by_pairs(stats))
    (
        block_out, ordered_cot, states1, states_low1, act1, grad_gate1, grad_mixed1, grad_low1,
        source1, prefix1, total1, grad_d1,
    ) = run(
        part(turn_around, upper),
        "turn_around",
        (
            place, gather_row(total1), prefix1, disc, drive1, u1, hidden1, c_proj, d_skip, w_gate,
            cot,
        ),
        (low, low, padded, wide_low, low, low, flat, low, wide, prefix, total, line),
        (flat, flat, flat, low),
    )

    def finish(cfg, ends, prefix, source, drive, states, u, grad_mixed, grad_d, hidden, norm):
        return run(
            part(backward_finish, cfg),
            "backward_finish",
            (
                place, ends, prefix, disc, source, drive, states, u, grad_mixed, grad_d, hidden,
                norm, d_skip, b_proj,
            ),
            (wide_low, flat, sums, small),
        )

    def halves(length):
        return (((length // 2, width), f32),) * 2

    grad_proj1, grad_u1, stats, small1 = finish(
        upper, gather_row(total1), prefix1, source1, drive1, states1, u1, grad_mixed1, grad_d1,
        hidden1, norm1,
    )
    weights1 = run(
        all_weights,
        "all_weights",
        (core, act1, grad_gate1, states_low1, grad_low1, grad_proj1, u1),
        halves(width + 4 * half),
    )
    stats = add_by_pairs(stats)
    weights1, stats = lax.optimization_barrier((weights1, stats))
    links = axis_parts()[0]
    own1 = weights1[0] + shifted(weights1[1], links, 1)
    chips = [list(range(at, count, 2)) for at in (0, 1)]
    own1 = lax.psum(own1, "seq", axis_index_groups=chips)
    (
        grad_out0, shared1, grad_gate0, grad_mixed0, grad_low0, source0, prefix0, total0, grad_d0,
    ) = run(
        part(between_layers, upper, lower),
        "between_layers",
        (
            place, stats, ordered_cot, grad_u1, hidden1, norm1, norm_gain,
            disc, u0, c_proj, w_gate, states_low0, act0, sig0, slope0,
        ),
        (flat, shared, low, flat, low, wide, prefix, total, line),
        (flat,),
    )
    gates0 = run(
        gate_weights, "gate_weights", (core, act0, grad_gate0, states_low0, grad_low0),
        halves(width + 2 * half),
    )
    gates0, ends = lax.optimization_barrier((gates0, gather_row(total0)))
    grad_proj0, grad_u0, stats, small0 = finish(
        lower, ends, prefix0, source0, drive0, states0, u0, grad_mixed0, grad_d0, ordered, norm0
    )
    grad_proj0, own1 = lax.optimization_barrier((grad_proj0, own1))
    own1 = lax.psum(own1, "dp")
    inputs0 = run(input_weights, "input_weights", (core, grad_proj0, u0), halves(2 * half))
    blank = jnp.zeros((CHUNKS - 2 * batches, width), f32)
    pair = add_by_pairs(jnp.concatenate([stats, blank, small0, small1], axis=0))
    summed = pair[0] + pair[1]
    grad_input, shared0 = run(
        part(last_step, lower),
        "last_step",
        ((summed[:2 * batches],), grad_out0, grad_u0, ordered, norm0, norm_gain),
        (flat, shared),
        (((width // LANES, rows, LANES), f32),),
        scalars=0,
    )
    small_sum = summed[CHUNKS:].reshape(2, CHUNKS, width)
    final = (((2, width, width), f32), ((2, 2 * half, width), f32), ((2, width, 2 * half), f32))
    other1 = shifted(own1, links, 1)
    placed = put_in_place(1, core, (own1,), (other1,), final, ())
    own_gates, other_gates = sum_over_links(*gates0)
    own_inputs, other_inputs = sum_over_links(*inputs0)
    grad_w, grad_c, grad_b = put_in_place(
        0, core, (own_gates, own_inputs), (other_gates, other_inputs), final, placed
    )
    _, pullback = jax.vjp(discretize, lam_re, lam_im, log_step)
    grad_lr, grad_li, grad_ls = pullback(tuple(small_sum[:, kind, :half] for kind in range(4)))
    both = jnp.stack([shared0, shared1])
    shape = block_in.shape
    return (
        block_out.reshape(shape), grad_input.reshape(shape), both[:, 0], both[:, 1],
        grad_ls, grad_lr, grad_li, grad_b, grad_c, small_sum[:, 4], grad_w,
    )


def solution(mesh):
    split = P(None, "dp", "seq", None)
    return jax.shard_map(
        per_device,
        mesh=mesh,
        in_specs=(split, split, P(None, "dp", None)) + (P(),) * 9,
        out_specs=(split, split) + (P(),) * 9,
        check_vma=False,
    )
```

```python
import functools

import jax
import jax.numpy as jnp
from jax import lax
from jax.experimental import pallas as pl
from jax.experimental.pallas import tpu as pltpu
from jax.sharding import PartitionSpec as P

f32, bf16 = jnp.float32, jnp.bfloat16
epsilon = 1e-05
tanh_scale = 0.7978845608028654
cubic_term = 0.044715
LANES = 128
CHUNKS = 8
ROWS = 32
VMEM_LIMIT = 26 * 1024 * 1024


def dot(left, right, contract=(1, 0)):
    return lax.dot_general(
        left, right, (((contract[0],), (contract[1],)), ((), ())), preferred_element_type=f32
    )


def reorder(span, inverse):
    shape = (span, span)
    kept, moved = (1, 0) if inverse else (0, 1)
    row = lax.broadcasted_iota(jnp.int32, shape, kept)
    position = lax.broadcasted_iota(jnp.int32, shape, moved)
    source = (row & (CHUNKS - 1)) * (span // CHUNKS) + (row >> 3)
    return jnp.where(position == source, 1.0, 0.0).astype(bf16)


def row_loop(count, body, init=0, step=ROWS):
    def one(index, carry):
        return body(pl.multiple_of(index * step, step), carry)

    return lax.fori_loop(0, count // step, one, init)


def documents(lengths, mine, batches, span, count):
    first = mine[0] * span
    out = []
    for batch in range(batches):
        begins, ends, so_far = [], [], 0
        for doc in range(lengths.shape[2]):
            begins.append(so_far)
            so_far = so_far + lengths[batch, 0, doc]
            ends.append(so_far)
        before, after = 0, 2 * count * span
        for begin, end in zip(begins, ends):
            before = jnp.maximum(before, jnp.where(begin < first, begin, 0))
            after = jnp.minimum(after, jnp.where(end > first + span, end, 2 * count * span))
        after = jnp.where(mine[0] == count - 1, 0, after)
        out.append(begins + ends + [before, after, first, mine[0]])
    return out


def place_documents(cfg, place):
    layer, reverse, batches, span, groups, tokens, count = cfg
    return documents(*place, batches, span, count)


def keep_of(meta, batch, base, step, backward):
    docs = (len(meta[batch]) - 4) // 2
    off = docs if backward else 0
    late = 1 if backward else 0
    stop = base == meta[batch][off] - step - late
    for doc in range(1, docs):
        stop = jnp.logical_or(stop, base == meta[batch][off + doc] - step - late)
    return jnp.where(stop, 0.0, 1.0)


def base_positions(meta, steps):
    return meta[0][-2] + lax.broadcasted_iota(jnp.int32, (CHUNKS, LANES), 0) * steps


def lanes_of(index, half=0):
    return slice(half + index * LANES, half + (index + 1) * LANES)


def coef_tiles(value, groups):
    return [
        tuple(jnp.broadcast_to(part[:, lanes_of(q)], (CHUNKS, LANES)) for part in value)
        for q in range(groups)
    ]


def constants(disc, layer):
    dec_re, dec_im, inj_re, inj_im = (part[layer : layer + 1, :] for part in disc)
    return (dec_re, dec_im), (inj_re, inj_im)


def times(a, b):
    return (a[0] * b[0] - a[1] * b[1], a[0] * b[1] + a[1] * b[0])


def power(value, exponent):
    for _ in range(exponent.bit_length() - 1):
        value = times(value, value)
    return value


def conj(value):
    return (value[0], -value[1])


def scan(meta, source, inject, dec, batches, span, groups, reverse, masks_reverse, init, extra, visit):
    steps = span // CHUNKS
    half = groups * LANES
    base = base_positions(meta, steps)

    def pair(index, carry):
        states, more = carry
        states = list(states)
        first = steps - 2 - 2 * index if reverse else 2 * index
        start = pl.multiple_of(first * CHUNKS, 2 * CHUNKS)
        order = (1, 0) if reverse else (0, 1)
        for batch in range(batches):
            keeps = [keep_of(meta, batch, base, first + j, masks_reverse) for j in (0, 1)]
            for q in range(groups):
                rows = pl.ds(batch * span + start, 2 * CHUNKS)
                src_re = source[rows, lanes_of(q)]
                src_im = source[rows, lanes_of(q, half)]
                state = states[batch * groups + q]
                found = [None, None]
                for j in order:
                    part = (
                        src_re[j * CHUNKS : (j + 1) * CHUNKS],
                        src_im[j * CHUNKS : (j + 1) * CHUNKS],
                    )
                    push = times(inject[q], part) if inject is not None else part
                    held = times((keeps[j] * dec[q][0], keeps[j] * dec[q][1]), state)
                    state = (held[0] + push[0], held[1] + push[1])
                    found[j] = state
                states[batch * groups + q] = state
                more = visit(more, batch, q, first, start, found, (src_re, src_im))
            more = visit(more, batch, None, first, start, keeps, None)
        return tuple(states), more

    return lax.fori_loop(0, steps // 2, pair, (tuple(init), extra), unroll=2)


def zero_states(batches, groups):
    zero = jnp.zeros((CHUNKS, LANES), f32)
    return [(zero, zero)] * (batches * groups)


def local_ends(meta, source, inject, dec, batches, span, groups, reverse, prefix, total):
    ones = tuple(jnp.ones((CHUNKS, LANES), f32) for _ in range(batches))

    def visit(more, batch, q, first, start, found, src):
        if q is not None:
            return more
        return tuple(
            value * found[0] * found[1] if at == batch else value for at, value in enumerate(more)
        )

    dec_chunk = coef_tiles(power(dec, span // CHUNKS), groups)
    ends, kept = scan(
        meta, source, inject, coef_tiles(dec, groups), batches, span, groups, reverse, reverse,
        zero_states(batches, groups), ones, visit,
    )
    half = groups * LANES
    row = lax.broadcasted_iota(jnp.int32, (CHUNKS, LANES), 0)
    for batch in range(batches):
        for q in range(groups):
            end = ends[batch * groups + q]
            decay = (kept[batch] * dec_chunk[q][0], kept[batch] * dec_chunk[q][1])
            for shift in (1, 2, 4):
                turn = CHUNKS - shift if reverse else shift
                valid = row < CHUNKS - shift if reverse else row >= shift
                before = [pltpu.roll(value, turn, 0) for value in (*end, *decay)]
                from_before = times(decay, (before[0], before[1]))
                end = (
                    end[0] + jnp.where(valid, from_before[0], 0.0),
                    end[1] + jnp.where(valid, from_before[1], 0.0),
                )
                longer = times(decay, (before[2], before[3]))
                decay = (
                    jnp.where(valid, longer[0], decay[0]),
                    jnp.where(valid, longer[1], decay[1]),
                )
            rows = slice(batch * CHUNKS, (batch + 1) * CHUNKS)
            prefix[0, rows, lanes_of(q)] = end[0]
            prefix[0, rows, lanes_of(q, half)] = end[1]
            prefix[1, rows, lanes_of(q)] = decay[0]
            prefix[1, rows, lanes_of(q, half)] = decay[1]
            last = 0 if reverse else CHUNKS - 1
            total[batch : batch + 1, lanes_of(q)] = end[0][last : last + 1]
            total[batch : batch + 1, lanes_of(q, half)] = end[1][last : last + 1]


def chunk_carries(meta, gathered, dec, prefix, batches, span, groups, reverse):
    count = gathered.shape[0]
    half = groups * LANES
    dec_span = power(dec, span)
    row = lax.broadcasted_iota(jnp.int32, (CHUNKS, LANES), 0)
    mine = meta[0][-1]
    out = []
    for batch in range(batches):

        def add(at, so_far, batch=batch):
            away = count - 2 - at
            if reverse:
                other = mine + 1 + away
                reaches = meta[batch][-3] > other * span
            else:
                other = mine - 1 - away
                reaches = meta[batch][-4] < (mine - away) * span
            other = jnp.clip(other, 0, count - 1)
            value = jnp.where(reaches, gathered[other, pl.ds(batch, 1), :], 0.0)
            moved = times(dec_span, so_far)
            return (moved[0] + value[:, :half], moved[1] + value[:, half:])

        zero = jnp.zeros((1, half), f32)
        enter = lax.fori_loop(0, count - 1, add, (zero, zero), unroll=count <= 8)
        rows = slice(batch * CHUNKS, (batch + 1) * CHUNKS)
        for q in range(groups):
            own = tuple(jnp.broadcast_to(part[:, lanes_of(q)], (CHUNKS, LANES)) for part in enter)
            end = (prefix[0, rows, lanes_of(q)], prefix[0, rows, lanes_of(q, half)])
            decay = (prefix[1, rows, lanes_of(q)], prefix[1, rows, lanes_of(q, half)])
            moved = times(decay, own)
            turn, first = (CHUNKS - 1, CHUNKS - 1) if reverse else (1, 0)
            out.append(
                tuple(
                    jnp.where(row == first, own[i], pltpu.roll(end[i] + moved[i], turn, 0))
                    for i in (0, 1)
                )
            )
    return out


def add_sums(target, batches, sums):
    for kind, per_batch in enumerate(sums):
        for batch in range(batches):
            target[kind * batches + batch : kind * batches + batch + 1, :] = jnp.sum(
                per_batch[batch], axis=0, keepdims=True
            )


def fold(value):
    return sum(value[i : i + CHUNKS] for i in range(CHUNKS, value.shape[0], CHUNKS)) + value[:CHUNKS]


def first_sums(batches, span, x, ordered, stats):
    turn = reorder(span, False)
    width = x.shape[1]
    sums, squares = [], []
    for batch in range(batches):
        rows = slice(batch * span, (batch + 1) * span)
        ordered[rows, :] = dot(turn, x[rows, :]).astype(bf16)

        def body(start, carry, batch=batch):
            value = x[pl.ds(batch * span + start, ROWS), :].astype(f32)
            return carry[0] + fold(value), carry[1] + fold(value * value)

        zero = jnp.zeros((CHUNKS, width), f32)
        one, two = row_loop(span, body, (zero, zero))
        sums.append(one)
        squares.append(two)
    add_sums(stats, batches, (sums, squares))


def enter_layer(
    cfg, place, stats, hidden, gain, shift, disc, b_proj, u, drive, prefix, total, norm
):
    layer, reverse, batches, span, groups, tokens, count = cfg
    sums = jnp.sum(stats[...], axis=0)
    average = sums[:batches] / tokens
    spread = sums[batches:] / tokens - average * average
    scale = lax.rsqrt(spread + epsilon)
    norm[:batches, :] = average
    norm[batches:, :] = scale
    gain_now, shift_now = gain[layer : layer + 1, :], shift[layer : layer + 1, :]
    for batch in range(batches):

        def body(start, carry, batch=batch):
            rows = pl.ds(batch * span + start, ROWS)
            normed = (hidden[rows, :].astype(f32) - average[batch : batch + 1]) * scale[
                batch : batch + 1
            ]
            u[rows, :] = (normed * gain_now + shift_now).astype(bf16)
            return carry

        row_loop(span, body)
    drive[...] = dot(u[...], b_proj[layer])
    meta = place_documents(cfg, place)
    dec, inj = constants(disc, layer)
    local_ends(
        meta, drive, coef_tiles(inj, groups), dec, batches, span, groups, reverse, prefix, total
    )


def finish_states(cfg, meta, ends, prefix, disc, drive, states, states_low):
    layer, reverse, batches, span, groups, tokens, count = cfg
    half = groups * LANES
    padded = span + CHUNKS
    dec, inj = constants(disc, layer)
    init = chunk_carries(meta, ends, dec, prefix, batches, span, groups, reverse)
    for batch in range(batches):
        edge = batch * padded + (span if reverse else 0)
        for q in range(groups):
            states[edge : edge + CHUNKS, lanes_of(q)] = init[batch * groups + q][0]
            states[edge : edge + CHUNKS, lanes_of(q, half)] = init[batch * groups + q][1]

    def visit(more, batch, q, first, start, found, src):
        if q is not None:
            for part, off in ((0, 0), (1, half)):
                both = jnp.concatenate([found[0][part], found[1][part]], axis=0)
                at = batch * padded + (0 if reverse else CHUNKS)
                states[pl.ds(at + start, 2 * CHUNKS), lanes_of(q, off)] = both
                states_low[pl.ds(batch * span + start, 2 * CHUNKS), lanes_of(q, off)] = both.astype(
                    bf16
                )
        return more

    scan(
        meta, drive, coef_tiles(inj, groups), coef_tiles(dec, groups), batches, span, groups,
        reverse, reverse, init, 0, visit,
    )


def forward_finish(
    cfg, meta, ends, prefix, disc, drive, u, hidden, c_proj, d_skip, w_gate,
    states, states_low, act, sig, slope, result, wide, emit,
):
    layer, reverse, batches, span, groups, tokens, count = cfg
    finish_states(cfg, meta, ends, prefix, disc, drive, states, states_low)
    wide[...] = dot(states_low[...], c_proj[layer])
    skip = d_skip[layer : layer + 1, :]

    def body(start, carry):
        rows = pl.ds(start, ROWS)
        mixed = wide[rows, :] + skip * u[rows, :].astype(f32)
        square = mixed * mixed
        th = jnp.tanh(tanh_scale * (mixed + cubic_term * square * mixed))
        half_one = 0.5 * (1.0 + th)
        act[rows, :] = (mixed * half_one).astype(bf16)
        slope[rows, :] = half_one + 0.5 * mixed * (1.0 - th * th) * tanh_scale * (
            1.0 + 3.0 * cubic_term * square
        )
        return carry

    row_loop(batches * span, body)
    wide[...] = dot(act[...], w_gate[layer])
    sums, squares = [], []
    for batch in range(batches):

        def gate(start, carry, batch=batch):
            rows = pl.ds(batch * span + start, ROWS)
            sig_now = 0.5 + 0.5 * jnp.tanh(0.5 * wide[rows, :])
            sig[rows, :] = sig_now
            value = hidden[rows, :].astype(f32) + act[rows, :].astype(f32) * sig_now
            result[rows, :] = value.astype(result.dtype)
            if emit is None:
                return carry
            return carry[0] + fold(value), carry[1] + fold(value * value)

        zero = jnp.zeros((CHUNKS, wide.shape[1]), f32)
        one, two = row_loop(span, gate, (zero, zero))
        sums.append(one)
        squares.append(two)
    if emit is not None:
        add_sums(emit, batches, (sums, squares))


def backward_start(
    cfg, meta, grad_out, disc, u, c_proj, w_gate, states_low, act, sig, slope,
    grad_gate, grad_mixed, grad_low, source, prefix, total, grad_d, wide,
):
    layer, reverse, batches, span, groups, tokens, count = cfg

    def body(start, carry):
        rows = pl.ds(start, ROWS)
        sig_now = sig[rows, :]
        grad_gate[rows, :] = (
            grad_out[rows, :].astype(f32) * act[rows, :].astype(f32) * sig_now * (1.0 - sig_now)
        ).astype(bf16)
        return carry

    row_loop(batches * span, body)
    wide[...] = dot(grad_gate[...], w_gate[layer], (1, 1))

    def mixed(start, carry):
        rows = pl.ds(start, ROWS)
        value = (grad_out[rows, :].astype(f32) * sig[rows, :] + wide[rows, :]) * slope[rows, :]
        grad_mixed[rows, :] = value
        grad_low[rows, :] = value.astype(bf16)
        return carry + fold(value * u[rows, :].astype(f32))

    gd = row_loop(batches * span, mixed, jnp.zeros((CHUNKS, wide.shape[1]), f32))
    grad_d[...] = jnp.sum(gd, axis=0, keepdims=True)
    source[...] = dot(grad_low[...], c_proj[layer], (1, 1))
    local_ends(
        meta, source, None, conj(constants(disc, layer)[0]), batches, span, groups, not reverse,
        prefix, total,
    )


def middle_forward(
    cfg, place, ends, prefix, disc, drive, u, hidden, c_proj, d_skip, w_gate,
    states, states_low, act, sig, slope, result, stats, wide,
):
    meta = place_documents(cfg, place)
    forward_finish(
        cfg, meta, ends, prefix, disc, drive, u, hidden, c_proj, d_skip, w_gate,
        states, states_low, act, sig, slope, result, wide, stats,
    )


def turn_around(
    cfg, place, ends, prefix, disc, drive, u, hidden, c_proj, d_skip, w_gate, cotangent,
    block_out, ordered_cot, states, states_low, act, grad_gate, grad_mixed, grad_low, source,
    back_prefix, total, grad_d, sig, slope, wide, result,
):
    layer, reverse, batches, span, groups, tokens, count = cfg
    meta = place_documents(cfg, place)
    turn, back = reorder(span, False), reorder(span, True)
    for batch in range(batches):
        rows = slice(batch * span, (batch + 1) * span)
        ordered_cot[rows, :] = dot(turn, cotangent[rows, :]).astype(bf16)
    forward_finish(
        cfg, meta, ends, prefix, disc, drive, u, hidden, c_proj, d_skip, w_gate,
        states, states_low, act, sig, slope, result, wide, None,
    )
    for batch in range(batches):
        rows = slice(batch * span, (batch + 1) * span)
        block_out[rows, :] = dot(back, result[rows, :]).astype(bf16)
    backward_start(
        cfg, meta, ordered_cot, disc, u, c_proj, w_gate, states_low, act, sig, slope,
        grad_gate, grad_mixed, grad_low, source, back_prefix, total, grad_d, wide,
    )


def backward_finish(
    cfg, place, ends, prefix, disc, source, drive, states, u, grad_mixed, grad_d, hidden, norm,
    d_skip, b_proj, grad_proj, grad_u, stats, small,
):
    layer, reverse, batches, span, groups, tokens, count = cfg
    half = groups * LANES
    padded = span + CHUNKS
    steps = span // CHUNKS
    meta = place_documents(cfg, place)
    dec, inj = constants(disc, layer)
    dec = conj(dec)
    init = chunk_carries(meta, ends, dec, prefix, batches, span, groups, not reverse)
    inj = coef_tiles(inj, groups)
    base = base_positions(meta, steps)
    zero = jnp.zeros((CHUNKS, LANES), f32)

    def visit(more, batch, q, first, start, found, src):
        if q is None:
            return more
        more = list(more)
        rows = pl.ds(batch * span + start, 2 * CHUNKS)
        drive_re, drive_im = drive[rows, lanes_of(q)], drive[rows, lanes_of(q, half)]
        before = pl.ds(batch * padded + start + (CHUNKS if reverse else 0), 2 * CHUNKS)
        prior_re, prior_im = states[before, lanes_of(q)], states[before, lanes_of(q, half)]
        dec_re, dec_im, inj_re, inj_im = more[q]
        out_re, out_im = [], []
        for j in (0, 1):
            part = slice(j * CHUNKS, (j + 1) * CHUNKS)
            adj_re, adj_im = found[j]
            keep = keep_of(meta, batch, base, first + j, reverse)
            kept_re, kept_im = keep * adj_re, keep * adj_im
            dec_re = dec_re + kept_re * prior_re[part] + kept_im * prior_im[part]
            dec_im = dec_im + kept_im * prior_re[part] - kept_re * prior_im[part]
            inj_re = inj_re + adj_re * drive_re[part] + adj_im * drive_im[part]
            inj_im = inj_im + adj_im * drive_re[part] - adj_re * drive_im[part]
            out_re.append(inj[q][0] * adj_re + inj[q][1] * adj_im)
            out_im.append(inj[q][0] * adj_im - inj[q][1] * adj_re)
        grad_proj[rows, lanes_of(q)] = jnp.concatenate(out_re, axis=0).astype(bf16)
        grad_proj[rows, lanes_of(q, half)] = jnp.concatenate(out_im, axis=0).astype(bf16)
        more[q] = (dec_re, dec_im, inj_re, inj_im)
        return tuple(more)

    _, sums = scan(
        meta, source, None, coef_tiles(dec, groups), batches, span, groups,
        not reverse, not reverse, init, ((zero,) * 4,) * groups, visit,
    )
    small[...] = jnp.zeros_like(small)
    for q in range(groups):
        for kind in range(4):
            small[kind : kind + 1, lanes_of(q)] = jnp.sum(sums[q][kind], axis=0, keepdims=True)
    small[4:5, :] = grad_d[...]
    grad_u[...] = dot(grad_proj[...], b_proj[layer], (1, 1))
    skip = d_skip[layer : layer + 1, :]
    plain, times_normed = [], []
    for batch in range(batches):
        average = norm[batch : batch + 1, :]
        scale = norm[batches + batch : batches + batch + 1, :]

        def body(start, carry, batch=batch, average=average, scale=scale):
            rows = pl.ds(batch * span + start, ROWS)
            value = grad_u[rows, :] + grad_mixed[rows, :] * skip
            grad_u[rows, :] = value
            normed = (hidden[rows, :].astype(f32) - average) * scale
            return carry[0] + fold(value), carry[1] + fold(value * normed)

        zero_sum = jnp.zeros((CHUNKS, grad_u.shape[1]), f32)
        one, two = row_loop(span, body, (zero_sum, zero_sum))
        plain.append(one)
        times_normed.append(two)
    add_sums(stats, batches, (plain, times_normed))


def norm_backward(cfg, stats, grad_out, grad_u, hidden, norm, gain, store, shared):
    layer, reverse, batches, span, groups, tokens, count = cfg
    sums = jnp.sum(stats[...], axis=0)
    shared[0:1, :] = jnp.sum(sums[batches:], axis=0, keepdims=True)
    shared[1:2, :] = jnp.sum(sums[:batches], axis=0, keepdims=True)
    gain_now = gain[layer : layer + 1, :]
    for batch in range(batches):
        average = norm[batch : batch + 1, :]
        scale = norm[batches + batch : batches + batch + 1, :]
        plain = gain_now * sums[batch : batch + 1] / tokens
        slanted = gain_now * sums[batches + batch : batches + batch + 1] / tokens

        def body(start, carry, batch=batch, average=average, scale=scale, plain=plain, slanted=slanted):
            rows = pl.ds(batch * span + start, ROWS)
            normed = (hidden[rows, :].astype(f32) - average) * scale
            value = grad_out[rows, :].astype(f32) + scale * (
                grad_u[rows, :] * gain_now - plain - normed * slanted
            )
            store(rows, value)
            return carry

        row_loop(span, body)


def between_layers(
    cfg, lower, place, stats, upper_out, upper_u, upper_hidden, upper_norm, gain,
    disc, u, c_proj, w_gate, states_low, act, sig, slope,
    grad_out, shared, grad_gate, grad_mixed, grad_low, source, prefix, total, grad_d, wide,
):
    def store(rows, value):
        grad_out[rows, :] = value

    norm_backward(cfg, stats, upper_out, upper_u, upper_hidden, upper_norm, gain, store, shared)
    meta = place_documents(lower, place)
    backward_start(
        lower, meta, grad_out, disc, u, c_proj, w_gate, states_low, act, sig, slope,
        grad_gate, grad_mixed, grad_low, source, prefix, total, grad_d, wide,
    )


def last_step(cfg, stats, grad_out, grad_u, hidden, norm, gain, target, shared, ordered):
    layer, reverse, batches, span, groups, tokens, count = cfg
    planes = target.shape[1] // LANES

    def store(rows, value):
        for plane in range(planes):
            ordered[plane, rows, :] = value[:, lanes_of(plane)]

    norm_backward(cfg, stats, grad_out, grad_u, hidden, norm, gain, store, shared)
    steps = span // CHUNKS
    for batch in range(batches):
        for chunk in range(CHUNKS):
            at = batch * span
            for plane in range(planes):
                target[at + chunk * steps : at + (chunk + 1) * steps, lanes_of(plane)] = ordered[
                    plane, pl.ds(at + chunk, steps, stride=CHUNKS), :
                ]


def half_weights(core, refs, own, sent):
    for target, half in ((own, core), (sent, 1 - core)):
        at = 0
        for left, right in refs:
            rows = left.shape[1] // 2
            cols = pl.ds(pl.multiple_of(half * rows, LANES), rows)
            target[at : at + rows, :] = dot(left[:, cols], right[...], (0, 0))
            at += rows


def all_weights(core, act, grad_gate, states_low, grad_low, grad_proj, u, own, sent):
    refs = ((act, grad_gate), (states_low, grad_low), (grad_proj, u))
    half_weights(core[0], refs, own, sent)


def gate_weights(core, act, grad_gate, states_low, grad_low, own, sent):
    half_weights(core[0], ((act, grad_gate), (states_low, grad_low)), own, sent)


def input_weights(core, grad_proj, u, own, sent):
    half_weights(core[0], ((grad_proj, u),), own, sent)


def run(body, name, args, outs, scratch=(), scalars=1):
    vmem, smem = pl.BlockSpec(memory_space=pltpu.VMEM), pl.BlockSpec(memory_space=pltpu.SMEM)
    specs = tuple(
        jax.tree.map(lambda _, at=at: smem if at < scalars else vmem, arg)
        for at, arg in enumerate(args)
    )
    return pl.pallas_call(
        body,
        name=name,
        out_shape=tuple(jax.ShapeDtypeStruct(*out) for out in outs),
        in_specs=specs,
        out_specs=(vmem,) * len(outs),
        scratch_shapes=[pltpu.VMEM(*entry) for entry in scratch],
        compiler_params=pltpu.CompilerParams(vmem_limit_bytes=VMEM_LIMIT),
    )(*args)


def put_halves(core, pieces, *refs):
    grad_w, grad_c, grad_b = refs[-3:]
    step = pl.program_id(0)
    for now in (0, 1):

        @pl.when(step == now)
        def _(now=now):
            rows_w, rows_c = grad_w.shape[1], grad_c.shape[1]
            sources = refs[now * pieces : (now + 1) * pieces]
            gates = sources[0]
            grad_w[0] = gates[:rows_w, :]
            grad_c[0] = gates[rows_w : rows_w + rows_c, :]
            last = sources[-1]
            at = rows_w + rows_c if pieces == 1 else 0
            grad_b[0] = last[at : at + rows_c, :].T


def put_in_place(layer, core, own, other, outs, before):
    width, states = outs[0][0][1], outs[1][0][1]
    pieces = len(own)
    vmem = pl.BlockSpec(memory_space=pltpu.VMEM)

    def half(step, core):
        return jnp.where(step == 0, core[0], 1 - core[0])

    blocks = (
        pl.BlockSpec((1, width // 2, width), lambda i, core: (layer, half(i, core), 0)),
        pl.BlockSpec((1, states // 2, width), lambda i, core: (layer, half(i, core), 0)),
        pl.BlockSpec((1, width, states // 2), lambda i, core: (layer, 0, half(i, core))),
    )

    def body(core_ref, *refs):
        put_halves(core_ref, pieces, *refs[: 2 * pieces], *refs[-3:])

    return pl.pallas_call(
        body,
        name="put_in_place",
        out_shape=tuple(jax.ShapeDtypeStruct(*out) for out in outs),
        grid_spec=pltpu.PrefetchScalarGridSpec(
            num_scalar_prefetch=1,
            grid=(2,),
            in_specs=[vmem] * (2 * pieces) + [pl.BlockSpec(memory_space=pl.ANY)] * len(before),
            out_specs=blocks,
        ),
        input_output_aliases={1 + 2 * pieces + i: i for i in range(len(before))},
        compiler_params=pltpu.CompilerParams(vmem_limit_bytes=VMEM_LIMIT),
    )(core, *own, *other, *before)


def gather_at_once(value, axis):
    copies = jnp.broadcast_to(value[None], (lax.axis_size(axis),) + value.shape)
    return lax.all_to_all(copies, axis, 0, 0, tiled=True)


def add_at_once(value):
    return gather_at_once(jnp.sum(gather_at_once(value, "seq"), axis=0), "dp")


def axis_parts():
    count = lax.axis_size("seq")
    mine = lax.axis_index("seq")
    depth = lax.axis_size("dp")
    return (
        ("seq", 2, 1, count, mine % 2),
        ("seq", count // 2, 2, count, mine // 2),
        ("dp", depth, 1, depth, lax.axis_index("dp")),
    )


def add_by_pairs(value):
    found = None
    for name, size, stride, count, mine in axis_parts():
        bit = 1
        while bit < size:
            if found is not None:
                value = value + found
            pairs = []
            for i in range(count):
                place = (i // stride) % size
                pairs.append((i, i + ((place ^ bit) - place) * stride))
            found = lax.ppermute(value, name, pairs)
            bit *= 2
    return value, found


def shifted(value, part, away):
    name, size, stride, count, mine = part
    pairs = []
    for i in range(count):
        place = (i // stride) % size
        pairs.append((i, i + ((place + away) % size - place) * stride))
    return lax.ppermute(value, name, pairs)


def add_half(*refs):
    out, at = refs[-1], 0
    for own, found in zip(refs[0:-1:2], refs[1:-1:2]):
        rows = own.shape[0]
        out[at : at + rows, :] = own[...] + found[...]
        at += rows


def add_cores(pairs):
    terms, rows = [], 0
    for own, sent in pairs:
        terms += [own, shifted(sent, axis_parts()[0], 1)]
        rows += own.shape[0]
    shape = ((rows, terms[0].shape[1]), f32)
    return run(add_half, "add_cores", terms, (shape,), scalars=0)[0]


def chips():
    count = lax.axis_size("seq")
    return [list(range(at, count, 2)) for at in (0, 1)]


def scatter_sum(value, axis, groups=None):
    size = len(groups[0]) if groups else lax.axis_size(axis)
    found = lax.all_to_all(value, axis, 0, 0, axis_index_groups=groups, tiled=True)
    return jnp.sum(found.reshape((size, -1) + value.shape[1:]), axis=0)


def gather_rows(value, axis, groups=None):
    size = len(groups[0]) if groups else lax.axis_size(axis)
    copies = jnp.broadcast_to(value[None], (size,) + value.shape)
    copies = copies.reshape((-1,) + value.shape[1:])
    return lax.all_to_all(copies, axis, 0, 0, axis_index_groups=groups, tiled=True)


def finish_sum(value):
    value = gather_rows(scatter_sum(value, "dp"), "dp")
    own = gather_rows(value, "seq", chips())
    return own, shifted(own, axis_parts()[0], 1)


def discretize(lam_re, lam_im, log_step):
    step_size = jnp.exp(log_step)
    decay_abs = jnp.exp(lam_re * step_size)
    rotation = lam_im * step_size
    dec_re = decay_abs * jnp.cos(rotation)
    dec_im = decay_abs * jnp.sin(rotation)
    denom_sq = lam_re * lam_re + lam_im * lam_im
    inj_re = ((dec_re - 1.0) * lam_re + dec_im * lam_im) / denom_sq
    inj_im = (dec_im * lam_re - (dec_re - 1.0) * lam_im) / denom_sq
    return (dec_re, dec_im, inj_re, inj_im)


def per_device(
    block_in, cotangent, doc_lengths, norm_gain, norm_shift, log_step, lam_re, lam_im,
    b_proj, c_proj, d_skip, w_gate,
):
    batches, seqs, span, width = block_in.shape
    assert seqs == 1 and span % (4 * CHUNKS) == 0 and span & (span - 1) == 0
    half = lam_re.shape[1]
    groups = half // LANES
    rows = batches * span
    count = lax.axis_size("seq")
    tokens = float(seqs * lax.axis_size("dp") * span * count)
    mine = jnp.reshape(lax.axis_index("seq"), (1,)).astype(jnp.int32)
    core = mine % 2
    place = (doc_lengths, mine)
    disc = discretize(lam_re, lam_im, log_step)

    x = block_in.reshape(rows, width)
    cot = cotangent.reshape(rows, width)
    lower = (0, False, batches, span, groups, tokens, count)
    upper = (1, True, batches, span, groups, tokens, count)
    part = functools.partial

    flat, low = ((rows, width), f32), ((rows, width), bf16)
    wide, wide_low = ((rows, 2 * half), f32), ((rows, 2 * half), bf16)
    padded = ((batches * (span + CHUNKS), 2 * half), f32)
    sums = ((2 * batches, width), f32)
    prefix = ((2, batches * CHUNKS, 2 * half), f32)
    total = ((batches, 2 * half), f32)
    line, shared = ((1, width), f32), ((2, width), f32)
    small = ((8, width), f32)

    def gather_row(value):
        return gather_at_once(value, "seq")

    ordered, stats = run(
        part(first_sums, batches, span), "first_sums", (x,), (low, sums), scalars=0
    )

    def forward(cfg, hidden, stats):
        return run(
            part(enter_layer, cfg),
            "enter_layer",
            (place, stats, hidden, norm_gain, norm_shift, disc, b_proj),
            (low, wide, prefix, total, sums),
        )

    u0, drive0, prefix0, total0, norm0 = forward(lower, ordered, add_at_once(stats))
    states0, states_low0, act0, sig0, slope0, hidden1, stats = run(
        part(middle_forward, lower),
        "middle_forward",
        (
            place, gather_row(total0), prefix0, disc, drive0, u0, ordered, c_proj,
            d_skip, w_gate,
        ),
        (padded, wide_low, low, flat, flat, flat, sums),
        (flat,),
    )
    u1, drive1, prefix1, total1, norm1 = forward(upper, hidden1, add_at_once(stats))
    (
        block_out, ordered_cot, states1, states_low1, act1, grad_gate1, grad_mixed1, grad_low1,
        source1, prefix1, total1, grad_d1,
    ) = run(
        part(turn_around, upper),
        "turn_around",
        (
            place, gather_row(total1), prefix1, disc, drive1, u1, hidden1, c_proj, d_skip, w_gate,
            cot,
        ),
        (low, low, padded, wide_low, low, low, flat, low, wide, prefix, total, line),
        (flat, flat, flat, low),
    )

    def finish(cfg, ends, prefix, source, drive, states, u, grad_mixed, grad_d, hidden, norm):
        return run(
            part(backward_finish, cfg),
            "backward_finish",
            (
                place, ends, prefix, disc, source, drive, states, u, grad_mixed, grad_d, hidden,
                norm, d_skip, b_proj,
            ),
            (wide_low, flat, sums, small),
        )

    def halves(length):
        return (((length // 2, width), f32),) * 2

    grad_proj1, grad_u1, stats, small1 = finish(
        upper, gather_row(total1), prefix1, source1, drive1, states1, u1, grad_mixed1, grad_d1,
        hidden1, norm1,
    )
    weights1 = run(
        all_weights,
        "all_weights",
        (core, act1, grad_gate1, states_low1, grad_low1, grad_proj1, u1),
        halves(width + 4 * half),
    )
    plane1 = add_cores([weights1])
    stats, plane1 = lax.optimization_barrier((add_at_once(stats), plane1))
    plane1 = scatter_sum(plane1, "seq", chips())
    (
        grad_out0, shared1, grad_gate0, grad_mixed0, grad_low0, source0, prefix0, total0, grad_d0,
    ) = run(
        part(between_layers, upper, lower),
        "between_layers",
        (
            place, stats, ordered_cot, grad_u1, hidden1, norm1, norm_gain,
            disc, u0, c_proj, w_gate, states_low0, act0, sig0, slope0,
        ),
        (flat, shared, low, flat, low, wide, prefix, total, line),
        (flat,),
    )
    gates0 = run(
        gate_weights, "gate_weights", (core, act0, grad_gate0, states_low0, grad_low0),
        halves(width + 2 * half),
    )
    gates0, ends, plane1 = lax.optimization_barrier((gates0, gather_row(total0), plane1))
    grad_proj0, grad_u0, stats, small0 = finish(
        lower, ends, prefix0, source0, drive0, states0, u0, grad_mixed0, grad_d0, ordered, norm0
    )
    inputs0 = run(input_weights, "input_weights", (core, grad_proj0, u0), halves(2 * half))
    blank = jnp.zeros((CHUNKS - 2 * batches, width), f32)
    pair = add_by_pairs(jnp.concatenate([stats, blank, small0, small1], axis=0))
    summed = pair[0] + pair[1]
    grad_input, shared0 = run(
        part(last_step, lower),
        "last_step",
        (summed[None, : 2 * batches], grad_out0, grad_u0, ordered, norm0, norm_gain),
        (flat, shared),
        (((width // LANES, rows, LANES), f32),),
        scalars=0,
    )
    small_sum = summed[CHUNKS:].reshape(2, CHUNKS, width)
    final = (((2, width, width), f32), ((2, 2 * half, width), f32), ((2, width, 2 * half), f32))
    own1, other1 = finish_sum(plane1)
    placed = put_in_place(1, core, (own1,), (other1,), final, ())
    own0, other0 = finish_sum(scatter_sum(add_cores([gates0, inputs0]), "seq", chips()))
    grad_w, grad_c, grad_b = put_in_place(0, core, (own0,), (other0,), final, placed)
    _, pullback = jax.vjp(discretize, lam_re, lam_im, log_step)
    grad_lr, grad_li, grad_ls = pullback(tuple(small_sum[:, kind, :half] for kind in range(4)))
    both = jnp.stack([shared0, shared1])
    shape = block_in.shape
    return (
        block_out.reshape(shape), grad_input.reshape(shape), both[:, 0], both[:, 1],
        grad_ls, grad_lr, grad_li, grad_b, grad_c, small_sum[:, 4], grad_w,
    )


def solution(mesh):
    split = P(None, "dp", "seq", None)
    return jax.shard_map(
        per_device,
        mesh=mesh,
        in_specs=(split, split, P(None, "dp", None)) + (P(),) * 9,
        out_specs=(split, split) + (P(),) * 9,
        check_vma=False,
    )
```

```python
import functools

import jax
import jax.numpy as jnp
from jax import lax
from jax.experimental import pallas as pl
from jax.experimental.pallas import tpu as pltpu
from jax.sharding import PartitionSpec as P

f32, bf16 = jnp.float32, jnp.bfloat16
epsilon = 1e-05
tanh_scale = 0.7978845608028654
cubic_term = 0.044715
LANES = 128
CHUNKS = 8
ROWS = 32
VMEM_LIMIT = 16 * 1024 * 1024


def dot(left, right, contract=(1, 0)):
    return lax.dot_general(
        left, right, (((contract[0],), (contract[1],)), ((), ())), preferred_element_type=f32
    )


def reorder(span, inverse):
    shape = (span, span)
    kept, moved = (1, 0) if inverse else (0, 1)
    row = lax.broadcasted_iota(jnp.int32, shape, kept)
    position = lax.broadcasted_iota(jnp.int32, shape, moved)
    source = (row & (CHUNKS - 1)) * (span // CHUNKS) + (row >> 3)
    return jnp.where(position == source, 1.0, 0.0).astype(bf16)


def row_loop(count, body, init=0, step=ROWS):
    def one(index, carry):
        return body(pl.multiple_of(index * step, step), carry)

    return lax.fori_loop(0, count // step, one, init)


def documents(lengths, here, batches, span, count):
    mine = here[0]
    first = mine * span
    out = []
    for batch in range(batches):
        begins, ends, so_far = [], [], 0
        for doc in range(lengths.shape[2]):
            begins.append(so_far)
            so_far = so_far + lengths[batch, 0, doc]
            ends.append(so_far)
        before, after = 0, 2 * count * span
        for begin, end in zip(begins, ends):
            before = jnp.maximum(before, jnp.where(begin < first, begin, 0))
            after = jnp.minimum(after, jnp.where(end > first + span, end, 2 * count * span))
        after = jnp.where(mine == count - 1, 0, after)
        out.append(begins + ends + [before, after, first, mine])
    return out


def place_documents(cfg, place):
    layer, reverse, batches, span, groups, tokens, count = cfg
    return documents(*place, batches, span, count)


def keep_of(meta, batch, base, step, backward):
    docs = (len(meta[batch]) - 4) // 2
    off = docs if backward else 0
    late = 1 if backward else 0
    stop = base == meta[batch][off] - step - late
    for doc in range(1, docs):
        stop = jnp.logical_or(stop, base == meta[batch][off + doc] - step - late)
    return jnp.where(stop, 0.0, 1.0)


def base_positions(meta, steps):
    return meta[0][-2] + lax.broadcasted_iota(jnp.int32, (CHUNKS, LANES), 0) * steps


def lanes_of(index, half=0):
    return slice(half + index * LANES, half + (index + 1) * LANES)


def coef_tiles(value, groups):
    return [
        tuple(jnp.broadcast_to(part[:, lanes_of(q)], (CHUNKS, LANES)) for part in value)
        for q in range(groups)
    ]


def constants(disc, layer):
    dec_re, dec_im, inj_re, inj_im = (part[layer : layer + 1, :] for part in disc)
    return (dec_re, dec_im), (inj_re, inj_im)


def times(a, b):
    return (a[0] * b[0] - a[1] * b[1], a[0] * b[1] + a[1] * b[0])


def power(value, exponent):
    for _ in range(exponent.bit_length() - 1):
        value = times(value, value)
    return value


def conj(value):
    return (value[0], -value[1])


def scan(meta, source, inject, dec, batches, span, groups, reverse, masks_reverse, init, extra, visit):
    steps = span // CHUNKS
    half = groups * LANES
    base = base_positions(meta, steps)

    def pair(index, carry):
        states, more = carry
        states = list(states)
        first = steps - 2 - 2 * index if reverse else 2 * index
        start = pl.multiple_of(first * CHUNKS, 2 * CHUNKS)
        order = (1, 0) if reverse else (0, 1)
        for batch in range(batches):
            keeps = [keep_of(meta, batch, base, first + j, masks_reverse) for j in (0, 1)]
            for q in range(groups):
                rows = pl.ds(batch * span + start, 2 * CHUNKS)
                src_re = source[rows, lanes_of(q)]
                src_im = source[rows, lanes_of(q, half)]
                state = states[batch * groups + q]
                found = [None, None]
                for j in order:
                    part = (
                        src_re[j * CHUNKS : (j + 1) * CHUNKS],
                        src_im[j * CHUNKS : (j + 1) * CHUNKS],
                    )
                    push = times(inject[q], part) if inject is not None else part
                    held = times((keeps[j] * dec[q][0], keeps[j] * dec[q][1]), state)
                    state = (held[0] + push[0], held[1] + push[1])
                    found[j] = state
                states[batch * groups + q] = state
                more = visit(more, batch, q, first, start, found, (src_re, src_im))
            more = visit(more, batch, None, first, start, keeps, None)
        return tuple(states), more

    return lax.fori_loop(0, steps // 2, pair, (tuple(init), extra), unroll=2)


def zero_states(batches, groups):
    zero = jnp.zeros((CHUNKS, LANES), f32)
    return [(zero, zero)] * (batches * groups)


def local_ends(meta, source, inject, dec, batches, span, groups, reverse, prefix, total):
    ones = tuple(jnp.ones((CHUNKS, LANES), f32) for _ in range(batches))

    def visit(more, batch, q, first, start, found, src):
        if q is not None:
            return more
        return tuple(
            value * found[0] * found[1] if at == batch else value for at, value in enumerate(more)
        )

    dec_chunk = coef_tiles(power(dec, span // CHUNKS), groups)
    ends, kept = scan(
        meta, source, inject, coef_tiles(dec, groups), batches, span, groups, reverse, reverse,
        zero_states(batches, groups), ones, visit,
    )
    half = groups * LANES
    row = lax.broadcasted_iota(jnp.int32, (CHUNKS, LANES), 0)
    for batch in range(batches):
        for q in range(groups):
            end = ends[batch * groups + q]
            decay = (kept[batch] * dec_chunk[q][0], kept[batch] * dec_chunk[q][1])
            for shift in (1, 2, 4):
                turn = CHUNKS - shift if reverse else shift
                valid = row < CHUNKS - shift if reverse else row >= shift
                before = [pltpu.roll(value, turn, 0) for value in (*end, *decay)]
                from_before = times(decay, (before[0], before[1]))
                end = (
                    end[0] + jnp.where(valid, from_before[0], 0.0),
                    end[1] + jnp.where(valid, from_before[1], 0.0),
                )
                longer = times(decay, (before[2], before[3]))
                decay = (
                    jnp.where(valid, longer[0], decay[0]),
                    jnp.where(valid, longer[1], decay[1]),
                )
            rows = slice(batch * CHUNKS, (batch + 1) * CHUNKS)
            prefix[0, rows, lanes_of(q)] = end[0]
            prefix[0, rows, lanes_of(q, half)] = end[1]
            prefix[1, rows, lanes_of(q)] = decay[0]
            prefix[1, rows, lanes_of(q, half)] = decay[1]
            last = 0 if reverse else CHUNKS - 1
            total[batch : batch + 1, lanes_of(q)] = end[0][last : last + 1]
            total[batch : batch + 1, lanes_of(q, half)] = end[1][last : last + 1]


def chunk_carries(meta, gathered, dec, prefix, batches, span, groups, reverse):
    count = gathered.shape[0]
    half = groups * LANES
    dec_span = power(dec, span)
    row = lax.broadcasted_iota(jnp.int32, (CHUNKS, LANES), 0)
    mine = meta[0][-1]
    out = []
    for batch in range(batches):

        def add(at, so_far, batch=batch):
            away = count - 2 - at
            if reverse:
                other = mine + 1 + away
                reaches = meta[batch][-3] > other * span
            else:
                other = mine - 1 - away
                reaches = meta[batch][-4] < (mine - away) * span
            other = jnp.clip(other, 0, count - 1)
            value = jnp.where(reaches, gathered[other, pl.ds(batch, 1), :], 0.0)
            moved = times(dec_span, so_far)
            return (moved[0] + value[:, :half], moved[1] + value[:, half:])

        zero = jnp.zeros((1, half), f32)
        enter = lax.fori_loop(0, count - 1, add, (zero, zero), unroll=count <= 8)
        rows = slice(batch * CHUNKS, (batch + 1) * CHUNKS)
        for q in range(groups):
            own = tuple(jnp.broadcast_to(part[:, lanes_of(q)], (CHUNKS, LANES)) for part in enter)
            end = (prefix[0, rows, lanes_of(q)], prefix[0, rows, lanes_of(q, half)])
            decay = (prefix[1, rows, lanes_of(q)], prefix[1, rows, lanes_of(q, half)])
            moved = times(decay, own)
            turn, first = (CHUNKS - 1, CHUNKS - 1) if reverse else (1, 0)
            out.append(
                tuple(
                    jnp.where(row == first, own[i], pltpu.roll(end[i] + moved[i], turn, 0))
                    for i in (0, 1)
                )
            )
    return out


def add_sums(target, batches, sums):
    for kind, per_batch in enumerate(sums):
        for batch in range(batches):
            target[kind * batches + batch : kind * batches + batch + 1, :] = jnp.sum(
                per_batch[batch], axis=0, keepdims=True
            )


def fold(value):
    return sum(value[i : i + CHUNKS] for i in range(CHUNKS, value.shape[0], CHUNKS)) + value[:CHUNKS]


def first_sums(batches, span, x, ordered, stats):
    turn = reorder(span, False)
    width = x.shape[1]
    sums, squares = [], []
    for batch in range(batches):
        rows = slice(batch * span, (batch + 1) * span)
        ordered[rows, :] = dot(turn, x[rows, :]).astype(bf16)

        def body(start, carry, batch=batch):
            value = x[pl.ds(batch * span + start, ROWS), :].astype(f32)
            return carry[0] + fold(value), carry[1] + fold(value * value)

        zero = jnp.zeros((CHUNKS, width), f32)
        one, two = row_loop(span, body, (zero, zero))
        sums.append(one)
        squares.append(two)
    add_sums(stats, batches, (sums, squares))


def enter_layer(
    cfg, place, stats, hidden, gain, shift, disc, b_proj, u, drive, prefix, total, norm
):
    layer, reverse, batches, span, groups, tokens, count = cfg
    sums = sum(part[...] for part in stats)
    average = sums[:batches] / tokens
    spread = sums[batches:] / tokens - average * average
    scale = lax.rsqrt(spread + epsilon)
    norm[:batches, :] = average
    norm[batches:, :] = scale
    gain_now, shift_now = gain[layer : layer + 1, :], shift[layer : layer + 1, :]
    for batch in range(batches):

        def body(start, carry, batch=batch):
            rows = pl.ds(batch * span + start, ROWS)
            normed = (hidden[rows, :].astype(f32) - average[batch : batch + 1]) * scale[
                batch : batch + 1
            ]
            u[rows, :] = (normed * gain_now + shift_now).astype(bf16)
            return carry

        row_loop(span, body)
    drive[...] = dot(u[...], b_proj[layer])
    meta = place_documents(cfg, place)
    dec, inj = constants(disc, layer)
    local_ends(
        meta, drive, coef_tiles(inj, groups), dec, batches, span, groups, reverse, prefix, total
    )


def finish_states(cfg, meta, ends, prefix, disc, drive, states, states_low):
    layer, reverse, batches, span, groups, tokens, count = cfg
    half = groups * LANES
    padded = span + CHUNKS
    dec, inj = constants(disc, layer)
    init = chunk_carries(meta, ends, dec, prefix, batches, span, groups, reverse)
    for batch in range(batches):
        edge = batch * padded + (span if reverse else 0)
        for q in range(groups):
            states[edge : edge + CHUNKS, lanes_of(q)] = init[batch * groups + q][0]
            states[edge : edge + CHUNKS, lanes_of(q, half)] = init[batch * groups + q][1]

    def visit(more, batch, q, first, start, found, src):
        if q is not None:
            for part, off in ((0, 0), (1, half)):
                both = jnp.concatenate([found[0][part], found[1][part]], axis=0)
                at = batch * padded + (0 if reverse else CHUNKS)
                states[pl.ds(at + start, 2 * CHUNKS), lanes_of(q, off)] = both
                states_low[pl.ds(batch * span + start, 2 * CHUNKS), lanes_of(q, off)] = both.astype(
                    bf16
                )
        return more

    scan(
        meta, drive, coef_tiles(inj, groups), coef_tiles(dec, groups), batches, span, groups,
        reverse, reverse, init, 0, visit,
    )


def forward_finish(
    cfg, meta, ends, prefix, disc, drive, u, hidden, c_proj, d_skip, w_gate,
    states, states_low, act, sig, slope, result, wide, emit,
):
    layer, reverse, batches, span, groups, tokens, count = cfg
    finish_states(cfg, meta, ends, prefix, disc, drive, states, states_low)
    wide[...] = dot(states_low[...], c_proj[layer])
    skip = d_skip[layer : layer + 1, :]

    def body(start, carry):
        rows = pl.ds(start, ROWS)
        mixed = wide[rows, :] + skip * u[rows, :].astype(f32)
        square = mixed * mixed
        th = jnp.tanh(tanh_scale * (mixed + cubic_term * square * mixed))
        half_one = 0.5 * (1.0 + th)
        act[rows, :] = (mixed * half_one).astype(bf16)
        slope[rows, :] = half_one + 0.5 * mixed * (1.0 - th * th) * tanh_scale * (
            1.0 + 3.0 * cubic_term * square
        )
        return carry

    row_loop(batches * span, body)
    wide[...] = dot(act[...], w_gate[layer])
    sums, squares = [], []
    for batch in range(batches):

        def gate(start, carry, batch=batch):
            rows = pl.ds(batch * span + start, ROWS)
            sig_now = 0.5 + 0.5 * jnp.tanh(0.5 * wide[rows, :])
            sig[rows, :] = sig_now
            value = hidden[rows, :].astype(f32) + act[rows, :].astype(f32) * sig_now
            result[rows, :] = value.astype(result.dtype)
            if emit is None:
                return carry
            return carry[0] + fold(value), carry[1] + fold(value * value)

        zero = jnp.zeros((CHUNKS, wide.shape[1]), f32)
        one, two = row_loop(span, gate, (zero, zero))
        sums.append(one)
        squares.append(two)
    if emit is not None:
        add_sums(emit, batches, (sums, squares))


def backward_start(
    cfg, meta, grad_out, disc, u, c_proj, w_gate, states_low, act, sig, slope,
    grad_gate, grad_mixed, grad_low, source, prefix, total, grad_d, wide,
):
    layer, reverse, batches, span, groups, tokens, count = cfg

    def body(start, carry):
        rows = pl.ds(start, ROWS)
        sig_now = sig[rows, :]
        grad_gate[rows, :] = (
            grad_out[rows, :].astype(f32) * act[rows, :].astype(f32) * sig_now * (1.0 - sig_now)
        ).astype(bf16)
        return carry

    row_loop(batches * span, body)
    wide[...] = dot(grad_gate[...], w_gate[layer], (1, 1))

    def mixed(start, carry):
        rows = pl.ds(start, ROWS)
        value = (grad_out[rows, :].astype(f32) * sig[rows, :] + wide[rows, :]) * slope[rows, :]
        grad_mixed[rows, :] = value
        grad_low[rows, :] = value.astype(bf16)
        return carry + fold(value * u[rows, :].astype(f32))

    gd = row_loop(batches * span, mixed, jnp.zeros((CHUNKS, wide.shape[1]), f32))
    grad_d[...] = jnp.sum(gd, axis=0, keepdims=True)
    source[...] = dot(grad_low[...], c_proj[layer], (1, 1))
    local_ends(
        meta, source, None, conj(constants(disc, layer)[0]), batches, span, groups, not reverse,
        prefix, total,
    )


def middle_forward(
    cfg, place, ends, prefix, disc, drive, u, hidden, c_proj, d_skip, w_gate,
    states, states_low, act, sig, slope, result, stats, wide,
):
    meta = place_documents(cfg, place)
    forward_finish(
        cfg, meta, ends, prefix, disc, drive, u, hidden, c_proj, d_skip, w_gate,
        states, states_low, act, sig, slope, result, wide, stats,
    )


def turn_around(
    cfg, place, ends, prefix, disc, drive, u, hidden, c_proj, d_skip, w_gate, cotangent,
    block_out, ordered_cot, states, states_low, act, grad_gate, grad_mixed, grad_low, source,
    back_prefix, total, grad_d, sig, slope, wide, result,
):
    layer, reverse, batches, span, groups, tokens, count = cfg
    meta = place_documents(cfg, place)
    turn, back = reorder(span, False), reorder(span, True)
    for batch in range(batches):
        rows = slice(batch * span, (batch + 1) * span)
        ordered_cot[rows, :] = dot(turn, cotangent[rows, :]).astype(bf16)
    forward_finish(
        cfg, meta, ends, prefix, disc, drive, u, hidden, c_proj, d_skip, w_gate,
        states, states_low, act, sig, slope, result, wide, None,
    )
    for batch in range(batches):
        rows = slice(batch * span, (batch + 1) * span)
        block_out[rows, :] = dot(back, result[rows, :]).astype(bf16)
    backward_start(
        cfg, meta, ordered_cot, disc, u, c_proj, w_gate, states_low, act, sig, slope,
        grad_gate, grad_mixed, grad_low, source, back_prefix, total, grad_d, wide,
    )


def backward_finish(
    cfg, place, ends, prefix, disc, source, drive, states, u, grad_mixed, grad_d, hidden, norm,
    d_skip, b_proj, grad_proj, grad_u, stats, small,
):
    layer, reverse, batches, span, groups, tokens, count = cfg
    half = groups * LANES
    padded = span + CHUNKS
    steps = span // CHUNKS
    meta = place_documents(cfg, place)
    dec, inj = constants(disc, layer)
    dec = conj(dec)
    init = chunk_carries(meta, ends, dec, prefix, batches, span, groups, not reverse)
    inj = coef_tiles(inj, groups)
    base = base_positions(meta, steps)
    zero = jnp.zeros((CHUNKS, LANES), f32)

    def visit(more, batch, q, first, start, found, src):
        if q is None:
            return more
        more = list(more)
        rows = pl.ds(batch * span + start, 2 * CHUNKS)
        drive_re, drive_im = drive[rows, lanes_of(q)], drive[rows, lanes_of(q, half)]
        before = pl.ds(batch * padded + start + (CHUNKS if reverse else 0), 2 * CHUNKS)
        prior_re, prior_im = states[before, lanes_of(q)], states[before, lanes_of(q, half)]
        dec_re, dec_im, inj_re, inj_im = more[q]
        out_re, out_im = [], []
        for j in (0, 1):
            part = slice(j * CHUNKS, (j + 1) * CHUNKS)
            adj_re, adj_im = found[j]
            keep = keep_of(meta, batch, base, first + j, reverse)
            kept_re, kept_im = keep * adj_re, keep * adj_im
            dec_re = dec_re + kept_re * prior_re[part] + kept_im * prior_im[part]
            dec_im = dec_im + kept_im * prior_re[part] - kept_re * prior_im[part]
            inj_re = inj_re + adj_re * drive_re[part] + adj_im * drive_im[part]
            inj_im = inj_im + adj_im * drive_re[part] - adj_re * drive_im[part]
            out_re.append(inj[q][0] * adj_re + inj[q][1] * adj_im)
            out_im.append(inj[q][0] * adj_im - inj[q][1] * adj_re)
        grad_proj[rows, lanes_of(q)] = jnp.concatenate(out_re, axis=0).astype(bf16)
        grad_proj[rows, lanes_of(q, half)] = jnp.concatenate(out_im, axis=0).astype(bf16)
        more[q] = (dec_re, dec_im, inj_re, inj_im)
        return tuple(more)

    _, sums = scan(
        meta, source, None, coef_tiles(dec, groups), batches, span, groups,
        not reverse, not reverse, init, ((zero,) * 4,) * groups, visit,
    )
    small[...] = jnp.zeros_like(small)
    for q in range(groups):
        for kind in range(4):
            small[kind : kind + 1, lanes_of(q)] = jnp.sum(sums[q][kind], axis=0, keepdims=True)
    small[4:5, :] = grad_d[...]
    grad_u[...] = dot(grad_proj[...], b_proj[layer], (1, 1))
    skip = d_skip[layer : layer + 1, :]
    plain, times_normed = [], []
    for batch in range(batches):
        average = norm[batch : batch + 1, :]
        scale = norm[batches + batch : batches + batch + 1, :]

        def body(start, carry, batch=batch, average=average, scale=scale):
            rows = pl.ds(batch * span + start, ROWS)
            value = grad_u[rows, :] + grad_mixed[rows, :] * skip
            grad_u[rows, :] = value
            normed = (hidden[rows, :].astype(f32) - average) * scale
            return carry[0] + fold(value), carry[1] + fold(value * normed)

        zero_sum = jnp.zeros((CHUNKS, grad_u.shape[1]), f32)
        one, two = row_loop(span, body, (zero_sum, zero_sum))
        plain.append(one)
        times_normed.append(two)
    add_sums(stats, batches, (plain, times_normed))


def norm_backward(cfg, stats, grad_out, grad_u, hidden, norm, gain, store, shared):
    layer, reverse, batches, span, groups, tokens, count = cfg
    sums = sum(part[...] for part in stats)
    shared[0:1, :] = jnp.sum(sums[batches:], axis=0, keepdims=True)
    shared[1:2, :] = jnp.sum(sums[:batches], axis=0, keepdims=True)
    gain_now = gain[layer : layer + 1, :]
    for batch in range(batches):
        average = norm[batch : batch + 1, :]
        scale = norm[batches + batch : batches + batch + 1, :]
        plain = gain_now * sums[batch : batch + 1] / tokens
        slanted = gain_now * sums[batches + batch : batches + batch + 1] / tokens

        def body(start, carry, batch=batch, average=average, scale=scale, plain=plain, slanted=slanted):
            rows = pl.ds(batch * span + start, ROWS)
            normed = (hidden[rows, :].astype(f32) - average) * scale
            value = grad_out[rows, :].astype(f32) + scale * (
                grad_u[rows, :] * gain_now - plain - normed * slanted
            )
            store(rows, value)
            return carry

        row_loop(span, body)


def between_layers(
    cfg, lower, place, stats, upper_out, upper_u, upper_hidden, upper_norm, gain,
    disc, u, c_proj, w_gate, states_low, act, sig, slope,
    grad_out, shared, grad_gate, grad_mixed, grad_low, source, prefix, total, grad_d, wide,
):
    def store(rows, value):
        grad_out[rows, :] = value

    norm_backward(cfg, stats, upper_out, upper_u, upper_hidden, upper_norm, gain, store, shared)
    meta = place_documents(lower, place)
    backward_start(
        lower, meta, grad_out, disc, u, c_proj, w_gate, states_low, act, sig, slope,
        grad_gate, grad_mixed, grad_low, source, prefix, total, grad_d, wide,
    )


def last_step(cfg, stats, grad_out, grad_u, hidden, norm, gain, target, shared, ordered):
    layer, reverse, batches, span, groups, tokens, count = cfg
    planes = target.shape[1] // LANES

    def store(rows, value):
        for plane in range(planes):
            ordered[plane, rows, :] = value[:, lanes_of(plane)]

    norm_backward(cfg, stats, grad_out, grad_u, hidden, norm, gain, store, shared)
    steps = span // CHUNKS
    for batch in range(batches):
        for chunk in range(CHUNKS):
            at = batch * span
            for plane in range(planes):
                target[at + chunk * steps : at + (chunk + 1) * steps, lanes_of(plane)] = ordered[
                    plane, pl.ds(at + chunk, steps, stride=CHUNKS), :
                ]


def half_weights(core, refs, own, sent):
    for target, half in ((own, core), (sent, 1 - core)):
        at = 0
        for left, right in refs:
            rows = left.shape[1] // 2
            cols = pl.ds(pl.multiple_of(half * rows, LANES), rows)
            target[at : at + rows, :] = dot(left[:, cols], right[...], (0, 0))
            at += rows


def all_weights(here, act, grad_gate, states_low, grad_low, grad_proj, u, own, sent):
    refs = ((act, grad_gate), (states_low, grad_low), (grad_proj, u))
    half_weights(lax.rem(here[0], 2), refs, own, sent)


def gate_weights(here, act, grad_gate, states_low, grad_low, own, sent):
    half_weights(lax.rem(here[0], 2), ((act, grad_gate), (states_low, grad_low)), own, sent)


def input_weights(here, grad_proj, u, own, sent):
    half_weights(lax.rem(here[0], 2), ((grad_proj, u),), own, sent)


def run(body, name, args, outs, scratch=(), scalars=1):
    vmem, smem = pl.BlockSpec(memory_space=pltpu.VMEM), pl.BlockSpec(memory_space=pltpu.SMEM)
    specs = tuple(
        jax.tree.map(lambda _, at=at: smem if at < scalars else vmem, arg)
        for at, arg in enumerate(args)
    )
    return pl.pallas_call(
        body,
        name=name,
        out_shape=tuple(jax.ShapeDtypeStruct(*out) for out in outs),
        in_specs=specs,
        out_specs=(vmem,) * len(outs),
        scratch_shapes=[pltpu.VMEM(*entry) for entry in scratch],
        compiler_params=pltpu.CompilerParams(vmem_limit_bytes=VMEM_LIMIT),
    )(*args)


def put_halves(pieces, *refs):
    grad_w, grad_c, grad_b = refs[-3:]
    step = pl.program_id(0)
    for now in (0, 1):

        @pl.when(step == now)
        def _(now=now):
            rows_w, rows_c = grad_w.shape[1], grad_c.shape[1]
            sources = refs[now * pieces : (now + 1) * pieces]
            gates = sources[0]
            grad_w[0] = gates[:rows_w, :]
            grad_c[0] = gates[rows_w : rows_w + rows_c, :]
            last = sources[-1]
            at = rows_w + rows_c if pieces == 1 else 0
            grad_b[0] = last[at : at + rows_c, :].T


def put_in_place(layer, here, own, other, outs, before):
    width, states = outs[0][0][1], outs[1][0][1]
    pieces = len(own)
    vmem = pl.BlockSpec(memory_space=pltpu.VMEM)

    def half(step, here):
        core = lax.rem(here[0], 2)
        return jnp.where(step == 0, core, 1 - core)

    blocks = (
        pl.BlockSpec((1, width // 2, width), lambda i, here: (layer, half(i, here), 0)),
        pl.BlockSpec((1, states // 2, width), lambda i, here: (layer, half(i, here), 0)),
        pl.BlockSpec((1, width, states // 2), lambda i, here: (layer, 0, half(i, here))),
    )

    def body(here_ref, *refs):
        put_halves(pieces, *refs[: 2 * pieces], *refs[-3:])

    return pl.pallas_call(
        body,
        name="put_in_place",
        out_shape=tuple(jax.ShapeDtypeStruct(*out) for out in outs),
        grid_spec=pltpu.PrefetchScalarGridSpec(
            num_scalar_prefetch=1,
            grid=(2,),
            in_specs=[vmem] * (2 * pieces) + [pl.BlockSpec(memory_space=pl.ANY)] * len(before),
            out_specs=blocks,
        ),
        input_output_aliases={1 + 2 * pieces + i: i for i in range(len(before))},
        compiler_params=pltpu.CompilerParams(vmem_limit_bytes=VMEM_LIMIT),
    )(here, *own, *other, *before)


def axis_parts():
    count, depth = lax.axis_size("seq"), lax.axis_size("dp")
    return (("seq", 2, 1, count), ("seq", count // 2, 2, count), ("dp", depth, 1, depth))


def add_by_pairs(value):
    found = None
    for name, size, stride, count in axis_parts():
        bit = 1
        while bit < size:
            if found is not None:
                value = value + found
            pairs = []
            for i in range(count):
                place = (i // stride) % size
                pairs.append((i, i + ((place ^ bit) - place) * stride))
            found = lax.ppermute(value, name, pairs)
            bit *= 2
    return value, found


def shifted(value, part, away):
    name, size, stride, count = part
    pairs = []
    for i in range(count):
        place = (i // stride) % size
        pairs.append((i, i + ((place + away) % size - place) * stride))
    return lax.ppermute(value, name, pairs)


def add_half(*refs):
    out, at = refs[-1], 0
    for own, found in zip(refs[0:-1:2], refs[1:-1:2]):
        rows = own.shape[0]
        out[at : at + rows, :] = own[...] + found[...]
        at += rows


def add_cores(pairs):
    terms, rows = [], 0
    for own, sent in pairs:
        terms += [own, shifted(sent, axis_parts()[0], 1)]
        rows += own.shape[0]
    shape = ((rows, terms[0].shape[1]), f32)
    return run(add_half, "add_cores", terms, (shape,), scalars=0)[0]


def own_place(here, part):
    name, size, stride, count = part
    return here[1] if name == "dp" else lax.rem(lax.div(here[0], stride), size)


def add_and_cut(part, here, *refs):
    size = part[1]
    terms, pieces = refs[: len(refs) - size], refs[len(refs) - size :]
    rows = pieces[0].shape[0]
    mine = own_place(here, part)
    for away, piece in enumerate(pieces):
        at = lax.rem(mine + away, size) * rows
        where = pl.ds(pl.multiple_of(at, CHUNKS), rows)
        piece[...] = sum(term[where, :] for term in terms)


def add_terms(*refs):
    refs[-1][...] = sum(ref[...] for ref in refs[:-1])


def arrange(part, here, *refs):
    out, pieces = refs[-1], refs[:-1]
    rows, size = pieces[0].shape[0], len(pieces)
    mine = own_place(here, part)
    for away, piece in enumerate(pieces):
        at = lax.rem(mine + size - away, size) * rows
        out[pl.ds(pl.multiple_of(at, CHUNKS), rows), :] = piece[...]


def cut(here, terms, part):
    rows, cols = terms[0].shape
    shape = ((rows // part[1], cols), f32)
    body = functools.partial(add_and_cut, part)
    return run(body, "add_and_cut", (here, *terms), (shape,) * part[1])


def spread(pieces, part):
    return [pieces[0]] + [shifted(pieces[away], part, away) for away in range(1, part[1])]


def collect(here, piece, part):
    pieces = [piece] + [shifted(piece, part, away) for away in range(1, part[1])]
    shape = ((piece.shape[0] * part[1], piece.shape[1]), f32)
    return run(functools.partial(arrange, part), "arrange", (here, *pieces), (shape,))[0]


def plane_sum(here, value):
    plane = axis_parts()[1]
    return spread(cut(here, [value], plane), plane)


def finish_sum(here, terms, *earlier):
    core, plane, depth = axis_parts()
    terms = spread(cut(here, terms, depth), depth)
    (value,) = run(add_terms, "add_terms", terms, ((terms[0].shape, f32),), scalars=0)
    value, *earlier = lax.optimization_barrier((collect(here, value, depth), *earlier))
    own = collect(here, value, plane)
    return own, shifted(own, core, 1), *earlier


def discretize(lam_re, lam_im, log_step):
    step_size = jnp.exp(log_step)
    decay_abs = jnp.exp(lam_re * step_size)
    rotation = lam_im * step_size
    dec_re = decay_abs * jnp.cos(rotation)
    dec_im = decay_abs * jnp.sin(rotation)
    denom_sq = lam_re * lam_re + lam_im * lam_im
    inj_re = ((dec_re - 1.0) * lam_re + dec_im * lam_im) / denom_sq
    inj_im = (dec_im * lam_re - (dec_re - 1.0) * lam_im) / denom_sq
    return (dec_re, dec_im, inj_re, inj_im)


def per_device(
    block_in, cotangent, doc_lengths, norm_gain, norm_shift, log_step, lam_re, lam_im,
    b_proj, c_proj, d_skip, w_gate,
):
    batches, seqs, span, width = block_in.shape
    assert seqs == 1 and span % (4 * CHUNKS) == 0 and span & (span - 1) == 0
    half = lam_re.shape[1]
    groups = half // LANES
    rows = batches * span
    count = lax.axis_size("seq")
    tokens = float(seqs * lax.axis_size("dp") * span * count)
    here = jnp.stack([lax.axis_index("seq"), lax.axis_index("dp")]).astype(jnp.int32)
    here, block_in = lax.optimization_barrier((here, block_in))
    place = (doc_lengths, here)
    disc = discretize(lam_re, lam_im, log_step)

    x = block_in.reshape(rows, width)
    cot = cotangent.reshape(rows, width)
    lower = (0, False, batches, span, groups, tokens, count)
    upper = (1, True, batches, span, groups, tokens, count)
    part = functools.partial

    flat, low = ((rows, width), f32), ((rows, width), bf16)
    wide, wide_low = ((rows, 2 * half), f32), ((rows, 2 * half), bf16)
    padded = ((batches * (span + CHUNKS), 2 * half), f32)
    sums = ((2 * batches, width), f32)
    prefix = ((2, batches * CHUNKS, 2 * half), f32)
    total = ((batches, 2 * half), f32)
    line, shared = ((1, width), f32), ((2, width), f32)
    small = ((8, width), f32)

    def gather_row(value):
        return lax.all_gather(value, "seq")

    ordered, stats = run(
        part(first_sums, batches, span), "first_sums", (x,), (low, sums), scalars=0
    )

    def forward(cfg, hidden, stats):
        return run(
            part(enter_layer, cfg),
            "enter_layer",
            (place, stats, hidden, norm_gain, norm_shift, disc, b_proj),
            (low, wide, prefix, total, sums),
        )

    u0, drive0, prefix0, total0, norm0 = forward(lower, ordered, add_by_pairs(stats))
    states0, states_low0, act0, sig0, slope0, hidden1, stats = run(
        part(middle_forward, lower),
        "middle_forward",
        (
            place, gather_row(total0), prefix0, disc, drive0, u0, ordered, c_proj,
            d_skip, w_gate,
        ),
        (padded, wide_low, low, flat, flat, flat, sums),
        (flat,),
    )
    u1, drive1, prefix1, total1, norm1 = forward(upper, hidden1, add_by_pairs(stats))
    (
        block_out, ordered_cot, states1, states_low1, act1, grad_gate1, grad_mixed1, grad_low1,
        source1, prefix1, total1, grad_d1,
    ) = run(
        part(turn_around, upper),
        "turn_around",
        (
            place, gather_row(total1), prefix1, disc, drive1, u1, hidden1, c_proj, d_skip, w_gate,
            cot,
        ),
        (low, low, padded, wide_low, low, low, flat, low, wide, prefix, total, line),
        (flat, flat, flat, low),
    )

    def finish(cfg, ends, prefix, source, drive, states, u, grad_mixed, grad_d, hidden, norm):
        return run(
            part(backward_finish, cfg),
            "backward_finish",
            (
                place, ends, prefix, disc, source, drive, states, u, grad_mixed, grad_d, hidden,
                norm, d_skip, b_proj,
            ),
            (wide_low, flat, sums, small),
        )

    def halves(length):
        return (((length // 2, width), f32),) * 2

    grad_proj1, grad_u1, stats, small1 = finish(
        upper, gather_row(total1), prefix1, source1, drive1, states1, u1, grad_mixed1, grad_d1,
        hidden1, norm1,
    )
    weights1 = run(
        all_weights,
        "all_weights",
        (here, act1, grad_gate1, states_low1, grad_low1, grad_proj1, u1),
        halves(width + 4 * half),
    )
    plane1 = add_cores([weights1])
    stats, plane1 = lax.optimization_barrier((add_by_pairs(stats), plane1))
    plane1 = plane_sum(here, plane1)
    (
        grad_out0, shared1, grad_gate0, grad_mixed0, grad_low0, source0, prefix0, total0, grad_d0,
    ) = run(
        part(between_layers, upper, lower),
        "between_layers",
        (
            place, stats, ordered_cot, grad_u1, hidden1, norm1, norm_gain,
            disc, u0, c_proj, w_gate, states_low0, act0, sig0, slope0,
        ),
        (flat, shared, low, flat, low, wide, prefix, total, line),
        (flat,),
    )
    gates0 = run(
        gate_weights, "gate_weights", (here, act0, grad_gate0, states_low0, grad_low0),
        halves(width + 2 * half),
    )
    gates0, ends, plane1 = lax.optimization_barrier((gates0, gather_row(total0), plane1))
    grad_proj0, grad_u0, stats, small0 = finish(
        lower, ends, prefix0, source0, drive0, states0, u0, grad_mixed0, grad_d0, ordered, norm0
    )
    inputs0 = run(input_weights, "input_weights", (here, grad_proj0, u0), halves(2 * half))
    blank = jnp.zeros((CHUNKS - 2 * batches, width), f32)
    pair = add_by_pairs(jnp.concatenate([stats, blank, small0, small1], axis=0))
    summed = pair[0] + pair[1]
    grad_input, shared0 = run(
        part(last_step, lower),
        "last_step",
        ((summed[: 2 * batches],), grad_out0, grad_u0, ordered, norm0, norm_gain),
        (flat, shared),
        (((width // LANES, rows, LANES), f32),),
        scalars=0,
    )
    small_sum = summed[CHUNKS:].reshape(2, CHUNKS, width)
    _, pullback = jax.vjp(discretize, lam_re, lam_im, log_step)
    grad_lr, grad_li, grad_ls = pullback(tuple(small_sum[:, kind, :half] for kind in range(4)))
    final = (((2, width, width), f32), ((2, 2 * half, width), f32), ((2, width, 2 * half), f32))
    own1, other1 = finish_sum(here, plane1)
    placed = put_in_place(1, here, (own1,), (other1,), final, ())
    terms0 = plane_sum(here, add_cores([gates0, inputs0]))
    own0, other0, grad_input, grad_lr, grad_li, grad_ls = finish_sum(
        here, terms0, grad_input, grad_lr, grad_li, grad_ls
    )
    grad_w, grad_c, grad_b = put_in_place(0, here, (own0,), (other0,), final, placed)
    both = jnp.stack([shared0, shared1])
    shape = block_in.shape
    return (
        block_out.reshape(shape), grad_input.reshape(shape), both[:, 0], both[:, 1],
        grad_ls, grad_lr, grad_li, grad_b, grad_c, small_sum[:, 4], grad_w,
    )


def solution(mesh):
    split = P(None, "dp", "seq", None)
    return jax.shard_map(
        per_device,
        mesh=mesh,
        in_specs=(split, split, P(None, "dp", None)) + (P(),) * 9,
        out_specs=(split, split) + (P(),) * 9,
        check_vma=False,
    )
```

```python
import functools

import jax
import jax.numpy as jnp
from jax import lax
from jax.experimental import pallas as pl
from jax.experimental.pallas import tpu as pltpu
from jax.sharding import PartitionSpec as P

f32, bf16 = jnp.float32, jnp.bfloat16
epsilon = 1e-05
tanh_scale = 0.7978845608028654
cubic_term = 0.044715
LANES = 128
CHUNKS = 8
ROWS = 32
VMEM_LIMIT = 16 * 1024 * 1024


def dot(left, right, contract=(1, 0)):
    return lax.dot_general(
        left, right, (((contract[0],), (contract[1],)), ((), ())), preferred_element_type=f32
    )


def reorder(span, inverse):
    shape = (span, span)
    kept, moved = (1, 0) if inverse else (0, 1)
    row = lax.broadcasted_iota(jnp.int32, shape, kept)
    position = lax.broadcasted_iota(jnp.int32, shape, moved)
    source = (row & (CHUNKS - 1)) * (span // CHUNKS) + (row >> 3)
    return jnp.where(position == source, 1.0, 0.0).astype(bf16)


def row_loop(count, body, init=0, step=ROWS):
    def one(index, carry):
        return body(pl.multiple_of(index * step, step), carry)

    return lax.fori_loop(0, count // step, one, init)


def documents(lengths, here, batches, span, count):
    mine = here[0]
    first = mine * span
    out = []
    for batch in range(batches):
        begins, ends, so_far = [], [], 0
        for doc in range(lengths.shape[2]):
            begins.append(so_far)
            so_far = so_far + lengths[batch, 0, doc]
            ends.append(so_far)
        before, after = 0, 2 * count * span
        for begin, end in zip(begins, ends):
            before = jnp.maximum(before, jnp.where(begin < first, begin, 0))
            after = jnp.minimum(after, jnp.where(end > first + span, end, 2 * count * span))
        after = jnp.where(mine == count - 1, 0, after)
        out.append(begins + ends + [before, after, first, mine])
    return out


def place_documents(cfg, place):
    layer, reverse, batches, span, groups, tokens, count = cfg
    return documents(*place, batches, span, count)


def keep_of(meta, batch, base, step, backward):
    docs = (len(meta[batch]) - 4) // 2
    off = docs if backward else 0
    late = 1 if backward else 0
    stop = base == meta[batch][off] - step - late
    for doc in range(1, docs):
        stop = jnp.logical_or(stop, base == meta[batch][off + doc] - step - late)
    return jnp.where(stop, 0.0, 1.0)


def base_positions(meta, steps):
    return meta[0][-2] + lax.broadcasted_iota(jnp.int32, (CHUNKS, LANES), 0) * steps


def lanes_of(index, half=0):
    return slice(half + index * LANES, half + (index + 1) * LANES)


def coef_tiles(value, groups):
    return [
        tuple(jnp.broadcast_to(part[:, lanes_of(q)], (CHUNKS, LANES)) for part in value)
        for q in range(groups)
    ]


def constants(disc, layer):
    dec_re, dec_im, inj_re, inj_im = (part[layer : layer + 1, :] for part in disc)
    return (dec_re, dec_im), (inj_re, inj_im)


def times(a, b):
    return (a[0] * b[0] - a[1] * b[1], a[0] * b[1] + a[1] * b[0])


def power(value, exponent):
    for _ in range(exponent.bit_length() - 1):
        value = times(value, value)
    return value


def conj(value):
    return (value[0], -value[1])


def scan(meta, source, inject, dec, batches, span, groups, reverse, masks_reverse, init, extra, visit):
    steps = span // CHUNKS
    half = groups * LANES
    base = base_positions(meta, steps)

    def pair(index, carry):
        states, more = carry
        states = list(states)
        first = steps - 2 - 2 * index if reverse else 2 * index
        start = pl.multiple_of(first * CHUNKS, 2 * CHUNKS)
        order = (1, 0) if reverse else (0, 1)
        for batch in range(batches):
            keeps = [keep_of(meta, batch, base, first + j, masks_reverse) for j in (0, 1)]
            for q in range(groups):
                rows = pl.ds(batch * span + start, 2 * CHUNKS)
                src_re = source[rows, lanes_of(q)]
                src_im = source[rows, lanes_of(q, half)]
                state = states[batch * groups + q]
                found = [None, None]
                for j in order:
                    part = (
                        src_re[j * CHUNKS : (j + 1) * CHUNKS],
                        src_im[j * CHUNKS : (j + 1) * CHUNKS],
                    )
                    push = times(inject[q], part) if inject is not None else part
                    held = times((keeps[j] * dec[q][0], keeps[j] * dec[q][1]), state)
                    state = (held[0] + push[0], held[1] + push[1])
                    found[j] = state
                states[batch * groups + q] = state
                more = visit(more, batch, q, first, start, found, (src_re, src_im))
            more = visit(more, batch, None, first, start, keeps, None)
        return tuple(states), more

    return lax.fori_loop(0, steps // 2, pair, (tuple(init), extra), unroll=2)


def zero_states(batches, groups):
    zero = jnp.zeros((CHUNKS, LANES), f32)
    return [(zero, zero)] * (batches * groups)


def local_ends(meta, source, inject, dec, batches, span, groups, reverse, prefix, total):
    ones = tuple(jnp.ones((CHUNKS, LANES), f32) for _ in range(batches))

    def visit(more, batch, q, first, start, found, src):
        if q is not None:
            return more
        return tuple(
            value * found[0] * found[1] if at == batch else value for at, value in enumerate(more)
        )

    dec_chunk = coef_tiles(power(dec, span // CHUNKS), groups)
    ends, kept = scan(
        meta, source, inject, coef_tiles(dec, groups), batches, span, groups, reverse, reverse,
        zero_states(batches, groups), ones, visit,
    )
    half = groups * LANES
    row = lax.broadcasted_iota(jnp.int32, (CHUNKS, LANES), 0)
    for batch in range(batches):
        for q in range(groups):
            end = ends[batch * groups + q]
            decay = (kept[batch] * dec_chunk[q][0], kept[batch] * dec_chunk[q][1])
            for shift in (1, 2, 4):
                turn = CHUNKS - shift if reverse else shift
                valid = row < CHUNKS - shift if reverse else row >= shift
                before = [pltpu.roll(value, turn, 0) for value in (*end, *decay)]
                from_before = times(decay, (before[0], before[1]))
                end = (
                    end[0] + jnp.where(valid, from_before[0], 0.0),
                    end[1] + jnp.where(valid, from_before[1], 0.0),
                )
                longer = times(decay, (before[2], before[3]))
                decay = (
                    jnp.where(valid, longer[0], decay[0]),
                    jnp.where(valid, longer[1], decay[1]),
                )
            rows = slice(batch * CHUNKS, (batch + 1) * CHUNKS)
            prefix[0, rows, lanes_of(q)] = end[0]
            prefix[0, rows, lanes_of(q, half)] = end[1]
            prefix[1, rows, lanes_of(q)] = decay[0]
            prefix[1, rows, lanes_of(q, half)] = decay[1]
            last = 0 if reverse else CHUNKS - 1
            total[batch : batch + 1, lanes_of(q)] = end[0][last : last + 1]
            total[batch : batch + 1, lanes_of(q, half)] = end[1][last : last + 1]


def chunk_carries(meta, gathered, dec, prefix, batches, span, groups, reverse):
    count = gathered.shape[0]
    half = groups * LANES
    dec_span = power(dec, span)
    row = lax.broadcasted_iota(jnp.int32, (CHUNKS, LANES), 0)
    mine = meta[0][-1]
    out = []
    for batch in range(batches):

        def add(at, so_far, batch=batch):
            away = count - 2 - at
            if reverse:
                other = mine + 1 + away
                reaches = meta[batch][-3] > other * span
            else:
                other = mine - 1 - away
                reaches = meta[batch][-4] < (mine - away) * span
            other = jnp.clip(other, 0, count - 1)
            value = jnp.where(reaches, gathered[other, pl.ds(batch, 1), :], 0.0)
            moved = times(dec_span, so_far)
            return (moved[0] + value[:, :half], moved[1] + value[:, half:])

        zero = jnp.zeros((1, half), f32)
        enter = lax.fori_loop(0, count - 1, add, (zero, zero), unroll=count <= 8)
        rows = slice(batch * CHUNKS, (batch + 1) * CHUNKS)
        for q in range(groups):
            own = tuple(jnp.broadcast_to(part[:, lanes_of(q)], (CHUNKS, LANES)) for part in enter)
            end = (prefix[0, rows, lanes_of(q)], prefix[0, rows, lanes_of(q, half)])
            decay = (prefix[1, rows, lanes_of(q)], prefix[1, rows, lanes_of(q, half)])
            moved = times(decay, own)
            turn, first = (CHUNKS - 1, CHUNKS - 1) if reverse else (1, 0)
            out.append(
                tuple(
                    jnp.where(row == first, own[i], pltpu.roll(end[i] + moved[i], turn, 0))
                    for i in (0, 1)
                )
            )
    return out


def add_sums(target, batches, sums):
    for kind, per_batch in enumerate(sums):
        for batch in range(batches):
            target[kind * batches + batch : kind * batches + batch + 1, :] = jnp.sum(
                per_batch[batch], axis=0, keepdims=True
            )


def fold(value):
    return sum(value[i : i + CHUNKS] for i in range(CHUNKS, value.shape[0], CHUNKS)) + value[:CHUNKS]


def first_sums(batches, span, x, gain, shift, skip, ordered, stats, norms):
    for number, part in enumerate((gain, shift, skip)):
        norms[2 * number : 2 * number + 2, :] = part[...]
    turn = reorder(span, False)
    width = x.shape[1]
    sums, squares = [], []
    for batch in range(batches):
        rows = slice(batch * span, (batch + 1) * span)
        ordered[rows, :] = dot(turn, x[rows, :]).astype(bf16)

        def body(start, carry, batch=batch):
            value = x[pl.ds(batch * span + start, ROWS), :].astype(f32)
            return carry[0] + fold(value), carry[1] + fold(value * value)

        zero = jnp.zeros((CHUNKS, width), f32)
        one, two = row_loop(span, body, (zero, zero))
        sums.append(one)
        squares.append(two)
    add_sums(stats, batches, (sums, squares))


def enter_layer(
    cfg, place, stats, hidden, norms, disc, b_proj, u, drive, prefix, total, norm
):
    layer, reverse, batches, span, groups, tokens, count = cfg
    sums = sum(part[...] for part in stats)
    average = sums[:batches] / tokens
    spread = sums[batches:] / tokens - average * average
    scale = lax.rsqrt(spread + epsilon)
    norm[:batches, :] = average
    norm[batches:, :] = scale
    gain_now, shift_now = norms[layer : layer + 1, :], norms[layer + 2 : layer + 3, :]
    for batch in range(batches):

        def body(start, carry, batch=batch):
            rows = pl.ds(batch * span + start, ROWS)
            normed = (hidden[rows, :].astype(f32) - average[batch : batch + 1]) * scale[
                batch : batch + 1
            ]
            u[rows, :] = (normed * gain_now + shift_now).astype(bf16)
            return carry

        row_loop(span, body)
    drive[...] = dot(u[...], b_proj[layer])
    meta = place_documents(cfg, place)
    dec, inj = constants(disc, layer)
    local_ends(
        meta, drive, coef_tiles(inj, groups), dec, batches, span, groups, reverse, prefix, total
    )


def finish_states(cfg, meta, ends, prefix, disc, drive, states, states_low):
    layer, reverse, batches, span, groups, tokens, count = cfg
    half = groups * LANES
    padded = span + CHUNKS
    dec, inj = constants(disc, layer)
    init = chunk_carries(meta, ends, dec, prefix, batches, span, groups, reverse)
    for batch in range(batches):
        edge = batch * padded + (span if reverse else 0)
        for q in range(groups):
            states[edge : edge + CHUNKS, lanes_of(q)] = init[batch * groups + q][0]
            states[edge : edge + CHUNKS, lanes_of(q, half)] = init[batch * groups + q][1]

    def visit(more, batch, q, first, start, found, src):
        if q is not None:
            for part, off in ((0, 0), (1, half)):
                both = jnp.concatenate([found[0][part], found[1][part]], axis=0)
                at = batch * padded + (0 if reverse else CHUNKS)
                states[pl.ds(at + start, 2 * CHUNKS), lanes_of(q, off)] = both
                states_low[pl.ds(batch * span + start, 2 * CHUNKS), lanes_of(q, off)] = both.astype(
                    bf16
                )
        return more

    scan(
        meta, drive, coef_tiles(inj, groups), coef_tiles(dec, groups), batches, span, groups,
        reverse, reverse, init, 0, visit,
    )


def forward_finish(
    cfg, meta, ends, prefix, disc, drive, u, hidden, c_proj, norms, w_gate,
    states, states_low, act, sig, slope, result, wide, emit,
):
    layer, reverse, batches, span, groups, tokens, count = cfg
    finish_states(cfg, meta, ends, prefix, disc, drive, states, states_low)
    wide[...] = dot(states_low[...], c_proj[layer])
    skip = norms[layer + 4 : layer + 5, :]

    def body(start, carry):
        rows = pl.ds(start, ROWS)
        mixed = wide[rows, :] + skip * u[rows, :].astype(f32)
        square = mixed * mixed
        th = jnp.tanh(tanh_scale * (mixed + cubic_term * square * mixed))
        half_one = 0.5 * (1.0 + th)
        act[rows, :] = (mixed * half_one).astype(bf16)
        slope[rows, :] = half_one + 0.5 * mixed * (1.0 - th * th) * tanh_scale * (
            1.0 + 3.0 * cubic_term * square
        )
        return carry

    row_loop(batches * span, body)
    wide[...] = dot(act[...], w_gate[layer])
    sums, squares = [], []
    for batch in range(batches):

        def gate(start, carry, batch=batch):
            rows = pl.ds(batch * span + start, ROWS)
            sig_now = 0.5 + 0.5 * jnp.tanh(0.5 * wide[rows, :])
            sig[rows, :] = sig_now
            value = hidden[rows, :].astype(f32) + act[rows, :].astype(f32) * sig_now
            result[rows, :] = value.astype(result.dtype)
            if emit is None:
                return carry
            return carry[0] + fold(value), carry[1] + fold(value * value)

        zero = jnp.zeros((CHUNKS, wide.shape[1]), f32)
        one, two = row_loop(span, gate, (zero, zero))
        sums.append(one)
        squares.append(two)
    if emit is not None:
        add_sums(emit, batches, (sums, squares))


def backward_start(
    cfg, meta, grad_out, disc, u, c_proj, w_gate, states_low, act, sig, slope,
    grad_gate, grad_mixed, grad_low, source, prefix, total, grad_d, wide,
):
    layer, reverse, batches, span, groups, tokens, count = cfg

    def body(start, carry):
        rows = pl.ds(start, ROWS)
        sig_now = sig[rows, :]
        grad_gate[rows, :] = (
            grad_out[rows, :].astype(f32) * act[rows, :].astype(f32) * sig_now * (1.0 - sig_now)
        ).astype(bf16)
        return carry

    row_loop(batches * span, body)
    wide[...] = dot(grad_gate[...], w_gate[layer], (1, 1))

    def mixed(start, carry):
        rows = pl.ds(start, ROWS)
        value = (grad_out[rows, :].astype(f32) * sig[rows, :] + wide[rows, :]) * slope[rows, :]
        grad_mixed[rows, :] = value
        grad_low[rows, :] = value.astype(bf16)
        return carry + fold(value * u[rows, :].astype(f32))

    gd = row_loop(batches * span, mixed, jnp.zeros((CHUNKS, wide.shape[1]), f32))
    grad_d[...] = jnp.sum(gd, axis=0, keepdims=True)
    source[...] = dot(grad_low[...], c_proj[layer], (1, 1))
    local_ends(
        meta, source, None, conj(constants(disc, layer)[0]), batches, span, groups, not reverse,
        prefix, total,
    )


def middle_forward(
    cfg, place, ends, prefix, disc, drive, u, hidden, c_proj, norms, w_gate,
    states, states_low, act, sig, slope, result, stats, wide,
):
    meta = place_documents(cfg, place)
    forward_finish(
        cfg, meta, ends, prefix, disc, drive, u, hidden, c_proj, norms, w_gate,
        states, states_low, act, sig, slope, result, wide, stats,
    )


def turn_around(
    cfg, place, ends, prefix, disc, drive, u, hidden, c_proj, norms, w_gate, cotangent,
    block_out, ordered_cot, states, states_low, act, grad_gate, grad_mixed, grad_low, source,
    back_prefix, total, grad_d, sig, slope, wide, result,
):
    layer, reverse, batches, span, groups, tokens, count = cfg
    meta = place_documents(cfg, place)
    turn, back = reorder(span, False), reorder(span, True)
    for batch in range(batches):
        rows = slice(batch * span, (batch + 1) * span)
        ordered_cot[rows, :] = dot(turn, cotangent[rows, :]).astype(bf16)
    forward_finish(
        cfg, meta, ends, prefix, disc, drive, u, hidden, c_proj, norms, w_gate,
        states, states_low, act, sig, slope, result, wide, None,
    )
    for batch in range(batches):
        rows = slice(batch * span, (batch + 1) * span)
        block_out[rows, :] = dot(back, result[rows, :]).astype(bf16)
    backward_start(
        cfg, meta, ordered_cot, disc, u, c_proj, w_gate, states_low, act, sig, slope,
        grad_gate, grad_mixed, grad_low, source, back_prefix, total, grad_d, wide,
    )


def backward_finish(
    cfg, place, ends, prefix, disc, source, drive, states, u, grad_mixed, grad_d, hidden, norm,
    norms, b_proj, grad_proj, grad_u, stats, small,
):
    layer, reverse, batches, span, groups, tokens, count = cfg
    half = groups * LANES
    padded = span + CHUNKS
    steps = span // CHUNKS
    meta = place_documents(cfg, place)
    dec, inj = constants(disc, layer)
    dec = conj(dec)
    init = chunk_carries(meta, ends, dec, prefix, batches, span, groups, not reverse)
    inj = coef_tiles(inj, groups)
    base = base_positions(meta, steps)
    zero = jnp.zeros((CHUNKS, LANES), f32)

    def visit(more, batch, q, first, start, found, src):
        if q is None:
            return more
        more = list(more)
        rows = pl.ds(batch * span + start, 2 * CHUNKS)
        drive_re, drive_im = drive[rows, lanes_of(q)], drive[rows, lanes_of(q, half)]
        before = pl.ds(batch * padded + start + (CHUNKS if reverse else 0), 2 * CHUNKS)
        prior_re, prior_im = states[before, lanes_of(q)], states[before, lanes_of(q, half)]
        dec_re, dec_im, inj_re, inj_im = more[q]
        out_re, out_im = [], []
        for j in (0, 1):
            part = slice(j * CHUNKS, (j + 1) * CHUNKS)
            adj_re, adj_im = found[j]
            keep = keep_of(meta, batch, base, first + j, reverse)
            kept_re, kept_im = keep * adj_re, keep * adj_im
            dec_re = dec_re + kept_re * prior_re[part] + kept_im * prior_im[part]
            dec_im = dec_im + kept_im * prior_re[part] - kept_re * prior_im[part]
            inj_re = inj_re + adj_re * drive_re[part] + adj_im * drive_im[part]
            inj_im = inj_im + adj_im * drive_re[part] - adj_re * drive_im[part]
            out_re.append(inj[q][0] * adj_re + inj[q][1] * adj_im)
            out_im.append(inj[q][0] * adj_im - inj[q][1] * adj_re)
        grad_proj[rows, lanes_of(q)] = jnp.concatenate(out_re, axis=0).astype(bf16)
        grad_proj[rows, lanes_of(q, half)] = jnp.concatenate(out_im, axis=0).astype(bf16)
        more[q] = (dec_re, dec_im, inj_re, inj_im)
        return tuple(more)

    _, sums = scan(
        meta, source, None, coef_tiles(dec, groups), batches, span, groups,
        not reverse, not reverse, init, ((zero,) * 4,) * groups, visit,
    )
    small[...] = jnp.zeros_like(small)
    for q in range(groups):
        for kind in range(4):
            small[kind : kind + 1, lanes_of(q)] = jnp.sum(sums[q][kind], axis=0, keepdims=True)
    small[4:5, :] = grad_d[...]
    grad_u[...] = dot(grad_proj[...], b_proj[layer], (1, 1))
    skip = norms[layer + 4 : layer + 5, :]
    plain, times_normed = [], []
    for batch in range(batches):
        average = norm[batch : batch + 1, :]
        scale = norm[batches + batch : batches + batch + 1, :]

        def body(start, carry, batch=batch, average=average, scale=scale):
            rows = pl.ds(batch * span + start, ROWS)
            value = grad_u[rows, :] + grad_mixed[rows, :] * skip
            grad_u[rows, :] = value
            normed = (hidden[rows, :].astype(f32) - average) * scale
            return carry[0] + fold(value), carry[1] + fold(value * normed)

        zero_sum = jnp.zeros((CHUNKS, grad_u.shape[1]), f32)
        one, two = row_loop(span, body, (zero_sum, zero_sum))
        plain.append(one)
        times_normed.append(two)
    add_sums(stats, batches, (plain, times_normed))


def backward_finish_last(cfg, *refs):
    ins, before, (grad_proj, grad_u, sums) = refs[:-4], refs[-4], refs[-3:]
    sums[...] = jnp.zeros_like(sums)
    sums[2 * CHUNKS :, :] = before[...]
    backward_finish(
        cfg, *ins, grad_proj, grad_u, sums.at[pl.ds(0, CHUNKS)], sums.at[pl.ds(CHUNKS, CHUNKS)]
    )


def norm_backward(cfg, stats, grad_out, grad_u, hidden, norm, norms, store, shared):
    layer, reverse, batches, span, groups, tokens, count = cfg
    sums = sum(part[...] for part in stats)
    shared[0:1, :] = jnp.sum(sums[batches:], axis=0, keepdims=True)
    shared[1:2, :] = jnp.sum(sums[:batches], axis=0, keepdims=True)
    gain_now = norms[layer : layer + 1, :]
    for batch in range(batches):
        average = norm[batch : batch + 1, :]
        scale = norm[batches + batch : batches + batch + 1, :]
        plain = gain_now * sums[batch : batch + 1] / tokens
        slanted = gain_now * sums[batches + batch : batches + batch + 1] / tokens

        def body(start, carry, batch=batch, average=average, scale=scale, plain=plain, slanted=slanted):
            rows = pl.ds(batch * span + start, ROWS)
            normed = (hidden[rows, :].astype(f32) - average) * scale
            value = grad_out[rows, :].astype(f32) + scale * (
                grad_u[rows, :] * gain_now - plain - normed * slanted
            )
            store(rows, value)
            return carry

        row_loop(span, body)


def between_layers(
    cfg, lower, place, stats, upper_out, upper_u, upper_hidden, upper_norm, norms,
    disc, u, c_proj, w_gate, states_low, act, sig, slope,
    grad_out, shared, grad_gate, grad_mixed, grad_low, source, prefix, total, grad_d, wide,
):
    def store(rows, value):
        grad_out[rows, :] = value

    norm_backward(cfg, stats, upper_out, upper_u, upper_hidden, upper_norm, norms, store, shared)
    meta = place_documents(lower, place)
    backward_start(
        lower, meta, grad_out, disc, u, c_proj, w_gate, states_low, act, sig, slope,
        grad_gate, grad_mixed, grad_low, source, prefix, total, grad_d, wide,
    )


def last_step(cfg, stats, grad_out, grad_u, hidden, norm, norms, target, shared, ordered):
    layer, reverse, batches, span, groups, tokens, count = cfg
    planes = target.shape[1] // LANES

    def store(rows, value):
        for plane in range(planes):
            ordered[plane, rows, :] = value[:, lanes_of(plane)]

    norm_backward(cfg, stats, grad_out, grad_u, hidden, norm, norms, store, shared)
    steps = span // CHUNKS
    for batch in range(batches):
        for chunk in range(CHUNKS):
            at = batch * span
            for plane in range(planes):
                target[at + chunk * steps : at + (chunk + 1) * steps, lanes_of(plane)] = ordered[
                    plane, pl.ds(at + chunk, steps, stride=CHUNKS), :
                ]


def half_weights(core, refs, own, sent):
    for target, half in ((own, core), (sent, 1 - core)):
        at = 0
        for left, right in refs:
            rows = left.shape[1] // 2
            cols = pl.ds(pl.multiple_of(half * rows, LANES), rows)
            target[at : at + rows, :] = dot(left[:, cols], right[...], (0, 0))
            at += rows


def all_weights(here, act, grad_gate, states_low, grad_low, grad_proj, u, own, sent):
    refs = ((act, grad_gate), (states_low, grad_low), (grad_proj, u))
    half_weights(lax.rem(here[0], 2), refs, own, sent)


def gate_weights(here, act, grad_gate, states_low, grad_low, own, sent):
    half_weights(lax.rem(here[0], 2), ((act, grad_gate), (states_low, grad_low)), own, sent)


def input_weights(here, grad_proj, u, own, sent):
    half_weights(lax.rem(here[0], 2), ((grad_proj, u),), own, sent)


def run(body, name, args, outs, scratch=(), scalars=1):
    vmem, smem = pl.BlockSpec(memory_space=pltpu.VMEM), pl.BlockSpec(memory_space=pltpu.SMEM)
    specs = tuple(
        jax.tree.map(lambda _, at=at: smem if at < scalars else vmem, arg)
        for at, arg in enumerate(args)
    )
    return pl.pallas_call(
        body,
        name=name,
        out_shape=tuple(jax.ShapeDtypeStruct(*out) for out in outs),
        in_specs=specs,
        out_specs=(vmem,) * len(outs),
        scratch_shapes=[pltpu.VMEM(*entry) for entry in scratch],
        compiler_params=pltpu.CompilerParams(vmem_limit_bytes=VMEM_LIMIT),
    )(*args)


def put_halves(chips, own, other, grad_w, grad_c, grad_b):
    rows_w, rows_c = grad_w.shape[1], grad_c.shape[1]
    gates, inputs = (rows_w + rows_c) // chips, grad_b.shape[2] // chips
    for now, source in ((0, own), (1, other)):

        @pl.when(pl.program_id(0) == now)
        def _(source=source):
            columns = []
            for chip in range(chips):
                at, row = chip * (gates + inputs), chip * gates
                cut_at = min(max(rows_w - row, 0), gates)
                if cut_at:
                    grad_w[0, row : row + cut_at, :] = source[at : at + cut_at, :]
                if cut_at < gates:
                    to = row + cut_at - rows_w
                    grad_c[0, to : to + gates - cut_at, :] = source[at + cut_at : at + gates, :]
                columns.append(source[at + gates : at + gates + inputs, :])
            grad_b[0] = jnp.concatenate(columns, axis=0).T


def put_in_place(layer, here, own, other, outs, before):
    width, states = outs[0][0][1], outs[1][0][1]
    vmem = pl.BlockSpec(memory_space=pltpu.VMEM)
    chips = axis_parts()[1][1]

    def half(step, here):
        core = lax.rem(here[0], 2)
        return jnp.where(step == 0, core, 1 - core)

    blocks = (
        pl.BlockSpec((1, width // 2, width), lambda i, here: (layer, half(i, here), 0)),
        pl.BlockSpec((1, states // 2, width), lambda i, here: (layer, half(i, here), 0)),
        pl.BlockSpec((1, width, states // 2), lambda i, here: (layer, 0, half(i, here))),
    )

    def body(here_ref, *refs):
        put_halves(chips, *refs[:2], *refs[-3:])

    return pl.pallas_call(
        body,
        name="put_in_place",
        out_shape=tuple(jax.ShapeDtypeStruct(*out) for out in outs),
        grid_spec=pltpu.PrefetchScalarGridSpec(
            num_scalar_prefetch=1,
            grid=(2,),
            in_specs=[vmem] * 2 + [pl.BlockSpec(memory_space=pl.ANY)] * len(before),
            out_specs=blocks,
        ),
        input_output_aliases={3 + i: i for i in range(len(before))},
        compiler_params=pltpu.CompilerParams(vmem_limit_bytes=VMEM_LIMIT),
    )(here, own, other, *before)


def axis_parts():
    count, depth = lax.axis_size("seq"), lax.axis_size("dp")
    return (("seq", 2, 1, count), ("seq", count // 2, 2, count), ("dp", depth, 1, depth))


def shifted(value, part, away):
    name, size, stride, count = part
    pairs = []
    for i in range(count):
        place = (i // stride) % size
        pairs.append((i, i + ((place + away) % size - place) * stride))
    return lax.ppermute(value, name, pairs)


def add_by_shifts(value, parts, *earlier):
    for number, part in enumerate(parts):
        if number:
            value = sum(terms[1:], terms[0])
        if number == len(parts) - 1:
            value, *earlier = lax.optimization_barrier((value, *earlier))
        terms = [value] + [shifted(value, part, away) for away in range(1, part[1])]
    return terms, *earlier


def own_place(here, part):
    name, size, stride, count = part
    return here[1] if name == "dp" else lax.rem(lax.div(here[0], stride), size)


def add_and_cut(part, here, *refs):
    size = part[1]
    terms, pieces = refs[: len(refs) - size], refs[len(refs) - size :]
    rows = pieces[0].shape[0]
    mine = own_place(here, part)
    for away, piece in enumerate(pieces):
        at = lax.rem(mine + away, size) * rows
        where = pl.ds(pl.multiple_of(at, CHUNKS), rows)
        piece[...] = sum(term[where, :] for term in terms)


def add_and_cut_cores(part, sizes, here, *refs):
    size = part[1]
    terms, pieces = refs[: len(refs) - size], refs[len(refs) - size :]
    mine = own_place(here, part)
    for away, piece in enumerate(pieces):
        place, at = lax.rem(mine + away, size), 0
        for own, found, share in core_blocks(terms, sizes, size):
            where = pl.ds(pl.multiple_of(share[0] + place * share[1], CHUNKS), share[1])
            piece[at : at + share[1], :] = own[where, :] + found[where, :]
            at += share[1]


def core_blocks(terms, sizes, size):
    gates, inputs = sizes[0] // 2, sizes[1] // 2
    if len(terms) == 2:
        return (
            (terms[0], terms[1], (0, gates // size)),
            (terms[0], terms[1], (gates, inputs // size)),
        )
    return (
        (terms[0], terms[1], (0, gates // size)),
        (terms[2], terms[3], (0, inputs // size)),
    )


def add_terms(*refs):
    refs[-1][...] = sum(ref[...] for ref in refs[:-1])


def arrange(part, here, *refs):
    out, pieces = refs[-1], refs[:-1]
    rows, size = pieces[0].shape[0], len(pieces)
    mine = own_place(here, part)
    for away, piece in enumerate(pieces):
        at = lax.rem(mine + size - away, size) * rows
        out[pl.ds(pl.multiple_of(at, CHUNKS), rows), :] = piece[...]


def cut(here, terms, part):
    rows, cols = terms[0].shape
    shape = ((rows // part[1], cols), f32)
    body = functools.partial(add_and_cut, part)
    return run(body, "add_and_cut", (here, *terms), (shape,) * part[1])


def spread(pieces, part):
    return [pieces[0]] + [shifted(pieces[away], part, away) for away in range(1, part[1])]


def collect(here, piece, part):
    pieces = [piece] + [shifted(piece, part, away) for away in range(1, part[1])]
    shape = ((piece.shape[0] * part[1], piece.shape[1]), f32)
    return run(functools.partial(arrange, part), "arrange", (here, *pieces), (shape,))[0]


def plane_pieces(here, terms, sizes):
    plane = axis_parts()[1]
    shape = ((sum(sizes) // 2 // plane[1], terms[0].shape[1]), f32)
    body = functools.partial(add_and_cut_cores, plane, sizes)
    return run(body, "add_and_cut_cores", (here, *terms), (shape,) * plane[1])


def finish_sum(here, terms, *earlier):
    core, plane, depth = axis_parts()
    terms = spread(cut(here, terms, depth), depth)
    (value,) = run(add_terms, "add_terms", terms, ((terms[0].shape, f32),), scalars=0)
    value, *earlier = lax.optimization_barrier((collect(here, value, depth), *earlier))
    own = collect(here, value, plane)
    return own, shifted(own, core, 1), *earlier


def discretize(lam_re, lam_im, log_step):
    step_size = jnp.exp(log_step)
    decay_abs = jnp.exp(lam_re * step_size)
    rotation = lam_im * step_size
    dec_re = decay_abs * jnp.cos(rotation)
    dec_im = decay_abs * jnp.sin(rotation)
    denom_sq = lam_re * lam_re + lam_im * lam_im
    inj_re = ((dec_re - 1.0) * lam_re + dec_im * lam_im) / denom_sq
    inj_im = (dec_im * lam_re - (dec_re - 1.0) * lam_im) / denom_sq
    return (dec_re, dec_im, inj_re, inj_im)


def per_device(
    block_in, cotangent, doc_lengths, norm_gain, norm_shift, log_step, lam_re, lam_im,
    b_proj, c_proj, d_skip, w_gate,
):
    batches, seqs, span, width = block_in.shape
    assert seqs == 1 and span % (4 * CHUNKS) == 0 and span & (span - 1) == 0
    half = lam_re.shape[1]
    groups = half // LANES
    rows = batches * span
    count = lax.axis_size("seq")
    tokens = float(seqs * lax.axis_size("dp") * span * count)
    here = jnp.stack([lax.axis_index("seq"), lax.axis_index("dp")]).astype(jnp.int32)
    here, block_in = lax.optimization_barrier((here, block_in))
    place = (doc_lengths, here)
    disc = discretize(lam_re, lam_im, log_step)

    x = block_in.reshape(rows, width)
    cot = cotangent.reshape(rows, width)
    lower = (0, False, batches, span, groups, tokens, count)
    upper = (1, True, batches, span, groups, tokens, count)
    part = functools.partial

    flat, low = ((rows, width), f32), ((rows, width), bf16)
    wide, wide_low = ((rows, 2 * half), f32), ((rows, 2 * half), bf16)
    padded = ((batches * (span + CHUNKS), 2 * half), f32)
    sums = ((2 * batches, width), f32)
    prefix = ((2, batches * CHUNKS, 2 * half), f32)
    total = ((batches, 2 * half), f32)
    line, shared = ((1, width), f32), ((2, width), f32)
    small = ((8, width), f32)

    def gather_row(value):
        return lax.all_gather(value, "seq")

    ordered, stats, norms = run(
        part(first_sums, batches, span), "first_sums", (x, norm_gain, norm_shift, d_skip),
        (low, sums, ((CHUNKS, width), f32)), scalars=0,
    )

    def forward(cfg, hidden, stats):
        return run(
            part(enter_layer, cfg),
            "enter_layer",
            (place, stats, hidden, norms, disc, b_proj),
            (low, wide, prefix, total, sums),
        )

    links, plane, depth = axis_parts()
    u0, drive0, prefix0, total0, norm0 = forward(
        lower, ordered, add_by_shifts(stats, (links, plane, depth))[0]
    )
    states0, states_low0, act0, sig0, slope0, hidden1, stats = run(
        part(middle_forward, lower),
        "middle_forward",
        (place, gather_row(total0), prefix0, disc, drive0, u0, ordered, c_proj, norms, w_gate),
        (padded, wide_low, low, flat, flat, flat, sums),
        (flat,),
    )
    u1, drive1, prefix1, total1, norm1 = forward(
        upper, hidden1, add_by_shifts(stats, (links, plane, depth))[0]
    )
    (
        block_out, ordered_cot, states1, states_low1, act1, grad_gate1, grad_mixed1, grad_low1,
        source1, prefix1, total1, grad_d1,
    ) = run(
        part(turn_around, upper),
        "turn_around",
        (
            place, gather_row(total1), prefix1, disc, drive1, u1, hidden1, c_proj, norms, w_gate,
            cot,
        ),
        (low, low, padded, wide_low, low, low, flat, low, wide, prefix, total, line),
        (flat, flat, flat, low),
    )

    def halves(length):
        return (((length // 2, width), f32),) * 2

    grad_proj1, grad_u1, stats, small1 = run(
        part(backward_finish, upper),
        "backward_finish",
        (
            place, gather_row(total1), prefix1, disc, source1, drive1, states1, u1, grad_mixed1,
            grad_d1, hidden1, norm1, norms, b_proj,
        ),
        (wide_low, flat, sums, small),
    )
    sizes = (width + 2 * half, 2 * half)
    own1, sent1 = run(
        all_weights,
        "all_weights",
        (here, act1, grad_gate1, states_low1, grad_low1, grad_proj1, u1),
        halves(sum(sizes)),
    )
    pieces1 = plane_pieces(here, (own1, shifted(sent1, links, 1)), sizes)
    stats, pieces1 = add_by_shifts(stats, (links, plane, depth), pieces1)
    terms1 = spread(pieces1, plane)
    (
        grad_out0, shared1, grad_gate0, grad_mixed0, grad_low0, source0, prefix0, total0, grad_d0,
    ) = run(
        part(between_layers, upper, lower),
        "between_layers",
        (
            place, stats, ordered_cot, grad_u1, hidden1, norm1, norms,
            disc, u0, c_proj, w_gate, states_low0, act0, sig0, slope0,
        ),
        (flat, shared, low, flat, low, wide, prefix, total, line),
        (flat,),
    )
    grad_gate0, terms1 = lax.optimization_barrier((grad_gate0, terms1))
    own_gates, sent_gates = run(
        gate_weights, "gate_weights", (here, act0, grad_gate0, states_low0, grad_low0),
        halves(sizes[0]),
    )
    found_gates = shifted(sent_gates, links, 1)
    own_gates, total0 = lax.optimization_barrier((own_gates, total0))
    found_gates, ends = lax.optimization_barrier((found_gates, gather_row(total0)))
    grad_proj0, grad_u0, last_sums = run(
        part(backward_finish_last, lower),
        "backward_finish",
        (
            place, ends, prefix0, disc, source0, drive0, states0, u0, grad_mixed0, grad_d0,
            ordered, norm0, norms, b_proj, small1,
        ),
        (wide_low, flat, ((3 * CHUNKS, width), f32)),
    )
    own_inputs, sent_inputs = run(
        input_weights, "input_weights", (here, grad_proj0, u0), halves(sizes[1])
    )
    pieces0 = plane_pieces(
        here, (own_gates, found_gates, own_inputs, shifted(sent_inputs, links, 1)), sizes
    )
    last_sums, pieces0 = lax.optimization_barrier((last_sums, pieces0))
    terms0 = spread(pieces0, plane)
    summed, *terms0 = add_by_shifts(last_sums, (depth, links, plane), *terms0)
    summed = sum(summed)
    final = (((2, width, width), f32), ((2, 2 * half, width), f32), ((2, width, 2 * half), f32))
    own1, other1, summed = finish_sum(here, terms1, summed)
    grad_input, shared0 = run(
        part(last_step, lower),
        "last_step",
        ((summed[: 2 * batches],), grad_out0, grad_u0, ordered, norm0, norms),
        (flat, shared),
        (((width // LANES, rows, LANES), f32),),
        scalars=0,
    )
    small_sum = summed[CHUNKS:].reshape(2, CHUNKS, width)
    _, pullback = jax.vjp(discretize, lam_re, lam_im, log_step)
    grad_lr, grad_li, grad_ls = pullback(tuple(small_sum[:, kind, :half] for kind in range(4)))
    own0, other0, own1, grad_input, grad_lr, grad_li, grad_ls = finish_sum(
        here, terms0, own1, grad_input, grad_lr, grad_li, grad_ls
    )
    placed = put_in_place(1, here, own1, other1, final, ())
    grad_w, grad_c, grad_b = put_in_place(0, here, own0, other0, final, placed)
    both = jnp.stack([shared0, shared1])
    shape = block_in.shape
    return (
        block_out.reshape(shape), grad_input.reshape(shape), both[:, 0], both[:, 1],
        grad_ls, grad_lr, grad_li, grad_b, grad_c, small_sum[:, 4], grad_w,
    )


def solution(mesh):
    split = P(None, "dp", "seq", None)
    return jax.shard_map(
        per_device,
        mesh=mesh,
        in_specs=(split, split, P(None, "dp", None)) + (P(),) * 9,
        out_specs=(split, split) + (P(),) * 9,
        check_vma=False,
    )
```

```python
import functools

import jax
import jax.numpy as jnp
from jax import lax
from jax.experimental import pallas as pl
from jax.experimental.pallas import tpu as pltpu
from jax.sharding import PartitionSpec as P

f32, bf16 = jnp.float32, jnp.bfloat16
epsilon = 1e-05
tanh_scale = 0.7978845608028654
cubic_term = 0.044715
LANES = 128
CHUNKS = 8
ROWS = 32
VMEM_LIMIT = 16 * 1024 * 1024


def dot(left, right, contract=(1, 0)):
    return lax.dot_general(
        left, right, (((contract[0],), (contract[1],)), ((), ())), preferred_element_type=f32
    )


def reorder(span, inverse):
    shape = (span, span)
    kept, moved = (1, 0) if inverse else (0, 1)
    row = lax.broadcasted_iota(jnp.int32, shape, kept)
    position = lax.broadcasted_iota(jnp.int32, shape, moved)
    source = (row & (CHUNKS - 1)) * (span // CHUNKS) + (row >> 3)
    return jnp.where(position == source, 1.0, 0.0).astype(bf16)


def row_loop(count, body, init=0, step=ROWS):
    def one(index, carry):
        return body(pl.multiple_of(index * step, step), carry)

    return lax.fori_loop(0, count // step, one, init)


def documents(here, batches, span, count):
    mine = here[0]
    first = mine * span
    out = []
    for batch in range(batches):
        begins, ends, so_far = [], [], 0
        docs = (here.shape[0] - 2) // batches
        for doc in range(docs):
            begins.append(so_far)
            so_far = so_far + here[2 + batch * docs + doc]
            ends.append(so_far)
        before, after = 0, 2 * count * span
        for begin, end in zip(begins, ends):
            before = jnp.maximum(before, jnp.where(begin < first, begin, 0))
            after = jnp.minimum(after, jnp.where(end > first + span, end, 2 * count * span))
        after = jnp.where(mine == count - 1, 0, after)
        out.append(begins + ends + [before, after, first, mine])
    return out


def place_documents(cfg, place):
    layer, reverse, batches, span, groups, tokens, count = cfg
    return documents(place, batches, span, count)


def keep_of(meta, batch, base, step, backward):
    docs = (len(meta[batch]) - 4) // 2
    off = docs if backward else 0
    late = 1 if backward else 0
    stop = base == meta[batch][off] - step - late
    for doc in range(1, docs):
        stop = jnp.logical_or(stop, base == meta[batch][off + doc] - step - late)
    return jnp.where(stop, 0.0, 1.0)


def base_positions(meta, steps):
    return meta[0][-2] + lax.broadcasted_iota(jnp.int32, (CHUNKS, LANES), 0) * steps


def lanes_of(index, half=0):
    return slice(half + index * LANES, half + (index + 1) * LANES)


def coef_tiles(value, groups):
    return [
        tuple(jnp.broadcast_to(part[:, lanes_of(q)], (CHUNKS, LANES)) for part in value)
        for q in range(groups)
    ]


def constants(disc, layer):
    dec_re, dec_im, inj_re, inj_im = (part[layer : layer + 1, :] for part in disc)
    return (dec_re, dec_im), (inj_re, inj_im)


def times(a, b):
    return (a[0] * b[0] - a[1] * b[1], a[0] * b[1] + a[1] * b[0])


def power(value, exponent):
    for _ in range(exponent.bit_length() - 1):
        value = times(value, value)
    return value


def conj(value):
    return (value[0], -value[1])


def scan(meta, source, inject, dec, batches, span, groups, reverse, masks_reverse, init, extra, visit):
    steps = span // CHUNKS
    half = groups * LANES
    base = base_positions(meta, steps)

    def pair(index, carry):
        states, more = carry
        states = list(states)
        first = steps - 2 - 2 * index if reverse else 2 * index
        start = pl.multiple_of(first * CHUNKS, 2 * CHUNKS)
        order = (1, 0) if reverse else (0, 1)
        for batch in range(batches):
            keeps = [keep_of(meta, batch, base, first + j, masks_reverse) for j in (0, 1)]
            for q in range(groups):
                rows = pl.ds(batch * span + start, 2 * CHUNKS)
                src_re = source[rows, lanes_of(q)]
                src_im = source[rows, lanes_of(q, half)]
                state = states[batch * groups + q]
                found = [None, None]
                for j in order:
                    part = (
                        src_re[j * CHUNKS : (j + 1) * CHUNKS],
                        src_im[j * CHUNKS : (j + 1) * CHUNKS],
                    )
                    push = times(inject[q], part) if inject is not None else part
                    held = times((keeps[j] * dec[q][0], keeps[j] * dec[q][1]), state)
                    state = (held[0] + push[0], held[1] + push[1])
                    found[j] = state
                states[batch * groups + q] = state
                more = visit(more, batch, q, first, start, found, (src_re, src_im))
            more = visit(more, batch, None, first, start, keeps, None)
        return tuple(states), more

    return lax.fori_loop(0, steps // 2, pair, (tuple(init), extra), unroll=2)


def zero_states(batches, groups):
    zero = jnp.zeros((CHUNKS, LANES), f32)
    return [(zero, zero)] * (batches * groups)


def local_ends(meta, source, inject, dec, batches, span, groups, reverse, prefix, total):
    ones = tuple(jnp.ones((CHUNKS, LANES), f32) for _ in range(batches))

    def visit(more, batch, q, first, start, found, src):
        if q is not None:
            return more
        return tuple(
            value * found[0] * found[1] if at == batch else value for at, value in enumerate(more)
        )

    dec_chunk = coef_tiles(power(dec, span // CHUNKS), groups)
    ends, kept = scan(
        meta, source, inject, coef_tiles(dec, groups), batches, span, groups, reverse, reverse,
        zero_states(batches, groups), ones, visit,
    )
    half = groups * LANES
    row = lax.broadcasted_iota(jnp.int32, (CHUNKS, LANES), 0)
    for batch in range(batches):
        for q in range(groups):
            end = ends[batch * groups + q]
            decay = (kept[batch] * dec_chunk[q][0], kept[batch] * dec_chunk[q][1])
            for shift in (1, 2, 4):
                turn = CHUNKS - shift if reverse else shift
                valid = row < CHUNKS - shift if reverse else row >= shift
                before = [pltpu.roll(value, turn, 0) for value in (*end, *decay)]
                from_before = times(decay, (before[0], before[1]))
                end = (
                    end[0] + jnp.where(valid, from_before[0], 0.0),
                    end[1] + jnp.where(valid, from_before[1], 0.0),
                )
                longer = times(decay, (before[2], before[3]))
                decay = (
                    jnp.where(valid, longer[0], decay[0]),
                    jnp.where(valid, longer[1], decay[1]),
                )
            rows = slice(batch * CHUNKS, (batch + 1) * CHUNKS)
            prefix[0, rows, lanes_of(q)] = end[0]
            prefix[0, rows, lanes_of(q, half)] = end[1]
            prefix[1, rows, lanes_of(q)] = decay[0]
            prefix[1, rows, lanes_of(q, half)] = decay[1]
            last = 0 if reverse else CHUNKS - 1
            total[batch : batch + 1, lanes_of(q)] = end[0][last : last + 1]
            total[batch : batch + 1, lanes_of(q, half)] = end[1][last : last + 1]


def chunk_carries(meta, gathered, dec, prefix, batches, span, groups, reverse):
    count = gathered.shape[0]
    half = groups * LANES
    dec_span = power(dec, span)
    row = lax.broadcasted_iota(jnp.int32, (CHUNKS, LANES), 0)
    mine = meta[0][-1]
    out = []
    for batch in range(batches):

        def add(at, so_far, batch=batch):
            away = count - 2 - at
            if reverse:
                other = mine + 1 + away
                reaches = meta[batch][-3] > other * span
            else:
                other = mine - 1 - away
                reaches = meta[batch][-4] < (mine - away) * span
            other = jnp.clip(other, 0, count - 1)
            value = jnp.where(reaches, gathered[other, pl.ds(batch, 1), :], 0.0)
            moved = times(dec_span, so_far)
            return (moved[0] + value[:, :half], moved[1] + value[:, half:])

        zero = jnp.zeros((1, half), f32)
        enter = lax.fori_loop(0, count - 1, add, (zero, zero), unroll=count <= 8)
        rows = slice(batch * CHUNKS, (batch + 1) * CHUNKS)
        for q in range(groups):
            own = tuple(jnp.broadcast_to(part[:, lanes_of(q)], (CHUNKS, LANES)) for part in enter)
            end = (prefix[0, rows, lanes_of(q)], prefix[0, rows, lanes_of(q, half)])
            decay = (prefix[1, rows, lanes_of(q)], prefix[1, rows, lanes_of(q, half)])
            moved = times(decay, own)
            turn, first = (CHUNKS - 1, CHUNKS - 1) if reverse else (1, 0)
            out.append(
                tuple(
                    jnp.where(row == first, own[i], pltpu.roll(end[i] + moved[i], turn, 0))
                    for i in (0, 1)
                )
            )
    return out


def add_sums(target, batches, sums):
    for kind, per_batch in enumerate(sums):
        for batch in range(batches):
            target[kind * batches + batch : kind * batches + batch + 1, :] = jnp.sum(
                per_batch[batch], axis=0, keepdims=True
            )


def fold(value):
    return sum(value[i : i + CHUNKS] for i in range(CHUNKS, value.shape[0], CHUNKS)) + value[:CHUNKS]


def first_sums(batches, span, x, ordered, stats):
    turn = reorder(span, False)
    width = x.shape[1]
    sums, squares = [], []
    for batch in range(batches):
        rows = slice(batch * span, (batch + 1) * span)
        ordered[rows, :] = dot(turn, x[rows, :]).astype(bf16)

        def body(start, carry, batch=batch):
            value = x[pl.ds(batch * span + start, ROWS), :].astype(f32)
            return carry[0] + fold(value), carry[1] + fold(value * value)

        zero = jnp.zeros((CHUNKS, width), f32)
        one, two = row_loop(span, body, (zero, zero))
        sums.append(one)
        squares.append(two)
    add_sums(stats, batches, (sums, squares))


def enter_layer(
    cfg, place, stats, hidden, norms, disc, b_proj, u, drive, prefix, total, norm
):
    layer, reverse, batches, span, groups, tokens, count = cfg
    sums = sum(part[...] for part in stats)
    average = sums[:batches] / tokens
    spread = sums[batches:] / tokens - average * average
    scale = lax.rsqrt(spread + epsilon)
    norm[:batches, :] = average
    norm[batches:, :] = scale
    gain_now, shift_now = norms[layer : layer + 1, :], norms[layer + 2 : layer + 3, :]
    for batch in range(batches):

        def body(start, carry, batch=batch):
            rows = pl.ds(batch * span + start, ROWS)
            normed = (hidden[rows, :].astype(f32) - average[batch : batch + 1]) * scale[
                batch : batch + 1
            ]
            u[rows, :] = (normed * gain_now + shift_now).astype(bf16)
            return carry

        row_loop(span, body)
    drive[...] = dot(u[...], b_proj[layer])
    meta = place_documents(cfg, place)
    dec, inj = constants(disc, layer)
    local_ends(
        meta, drive, coef_tiles(inj, groups), dec, batches, span, groups, reverse, prefix, total
    )


def finish_states(cfg, meta, ends, prefix, disc, drive, states, states_low):
    layer, reverse, batches, span, groups, tokens, count = cfg
    half = groups * LANES
    padded = span + CHUNKS
    dec, inj = constants(disc, layer)
    init = chunk_carries(meta, ends, dec, prefix, batches, span, groups, reverse)
    for batch in range(batches):
        edge = batch * padded + (span if reverse else 0)
        for q in range(groups):
            states[edge : edge + CHUNKS, lanes_of(q)] = init[batch * groups + q][0]
            states[edge : edge + CHUNKS, lanes_of(q, half)] = init[batch * groups + q][1]

    def visit(more, batch, q, first, start, found, src):
        if q is not None:
            for part, off in ((0, 0), (1, half)):
                both = jnp.concatenate([found[0][part], found[1][part]], axis=0)
                at = batch * padded + (0 if reverse else CHUNKS)
                states[pl.ds(at + start, 2 * CHUNKS), lanes_of(q, off)] = both
                states_low[pl.ds(batch * span + start, 2 * CHUNKS), lanes_of(q, off)] = both.astype(
                    bf16
                )
        return more

    scan(
        meta, drive, coef_tiles(inj, groups), coef_tiles(dec, groups), batches, span, groups,
        reverse, reverse, init, 0, visit,
    )


def forward_finish(
    cfg, meta, ends, prefix, disc, drive, u, hidden, c_proj, norms, w_gate,
    states, states_low, act, sig, slope, result, wide, emit,
):
    layer, reverse, batches, span, groups, tokens, count = cfg
    finish_states(cfg, meta, ends, prefix, disc, drive, states, states_low)
    wide[...] = dot(states_low[...], c_proj[layer])
    skip = norms[layer + 4 : layer + 5, :]

    def body(start, carry):
        rows = pl.ds(start, ROWS)
        mixed = wide[rows, :] + skip * u[rows, :].astype(f32)
        square = mixed * mixed
        th = jnp.tanh(tanh_scale * (mixed + cubic_term * square * mixed))
        half_one = 0.5 * (1.0 + th)
        act[rows, :] = (mixed * half_one).astype(bf16)
        slope[rows, :] = half_one + 0.5 * mixed * (1.0 - th * th) * tanh_scale * (
            1.0 + 3.0 * cubic_term * square
        )
        return carry

    row_loop(batches * span, body)
    wide[...] = dot(act[...], w_gate[layer])
    sums, squares = [], []
    for batch in range(batches):

        def gate(start, carry, batch=batch):
            rows = pl.ds(batch * span + start, ROWS)
            sig_now = 0.5 + 0.5 * jnp.tanh(0.5 * wide[rows, :])
            sig[rows, :] = sig_now
            value = hidden[rows, :].astype(f32) + act[rows, :].astype(f32) * sig_now
            result[rows, :] = value.astype(result.dtype)
            if emit is None:
                return carry
            return carry[0] + fold(value), carry[1] + fold(value * value)

        zero = jnp.zeros((CHUNKS, wide.shape[1]), f32)
        one, two = row_loop(span, gate, (zero, zero))
        sums.append(one)
        squares.append(two)
    if emit is not None:
        add_sums(emit, batches, (sums, squares))


def backward_start(
    cfg, meta, grad_out, disc, u, c_proj, w_gate, states_low, act, sig, slope,
    grad_gate, grad_mixed, grad_low, source, prefix, total, grad_d, wide,
):
    layer, reverse, batches, span, groups, tokens, count = cfg

    def body(start, carry):
        rows = pl.ds(start, ROWS)
        sig_now = sig[rows, :]
        grad_gate[rows, :] = (
            grad_out[rows, :].astype(f32) * act[rows, :].astype(f32) * sig_now * (1.0 - sig_now)
        ).astype(bf16)
        return carry

    row_loop(batches * span, body)
    wide[...] = dot(grad_gate[...], w_gate[layer], (1, 1))

    def mixed(start, carry):
        rows = pl.ds(start, ROWS)
        value = (grad_out[rows, :].astype(f32) * sig[rows, :] + wide[rows, :]) * slope[rows, :]
        grad_mixed[rows, :] = value
        grad_low[rows, :] = value.astype(bf16)
        return carry + fold(value * u[rows, :].astype(f32))

    gd = row_loop(batches * span, mixed, jnp.zeros((CHUNKS, wide.shape[1]), f32))
    grad_d[...] = jnp.sum(gd, axis=0, keepdims=True)
    source[...] = dot(grad_low[...], c_proj[layer], (1, 1))
    local_ends(
        meta, source, None, conj(constants(disc, layer)[0]), batches, span, groups, not reverse,
        prefix, total,
    )


def middle_forward(
    cfg, place, ends, prefix, disc, drive, u, hidden, c_proj, norms, w_gate,
    states, states_low, act, sig, slope, result, stats, wide,
):
    meta = place_documents(cfg, place)
    forward_finish(
        cfg, meta, ends, prefix, disc, drive, u, hidden, c_proj, norms, w_gate,
        states, states_low, act, sig, slope, result, wide, stats,
    )


def turn_around(
    cfg, place, ends, prefix, disc, drive, u, hidden, c_proj, norms, w_gate, cotangent,
    block_out, ordered_cot, states, states_low, act, grad_gate, grad_mixed, grad_low, source,
    back_prefix, total, grad_d, sig, slope, wide, result,
):
    layer, reverse, batches, span, groups, tokens, count = cfg
    meta = place_documents(cfg, place)
    turn, back = reorder(span, False), reorder(span, True)
    for batch in range(batches):
        rows = slice(batch * span, (batch + 1) * span)
        ordered_cot[rows, :] = dot(turn, cotangent[rows, :]).astype(bf16)
    forward_finish(
        cfg, meta, ends, prefix, disc, drive, u, hidden, c_proj, norms, w_gate,
        states, states_low, act, sig, slope, result, wide, None,
    )
    for batch in range(batches):
        rows = slice(batch * span, (batch + 1) * span)
        block_out[rows, :] = dot(back, result[rows, :]).astype(bf16)
    backward_start(
        cfg, meta, ordered_cot, disc, u, c_proj, w_gate, states_low, act, sig, slope,
        grad_gate, grad_mixed, grad_low, source, back_prefix, total, grad_d, wide,
    )


def backward_finish(
    cfg, place, ends, prefix, disc, source, drive, states, u, grad_mixed, grad_d, hidden, norm,
    norms, b_proj, grad_proj, grad_u, stats, small,
):
    layer, reverse, batches, span, groups, tokens, count = cfg
    half = groups * LANES
    padded = span + CHUNKS
    steps = span // CHUNKS
    meta = place_documents(cfg, place)
    dec, inj = constants(disc, layer)
    dec = conj(dec)
    init = chunk_carries(meta, ends, dec, prefix, batches, span, groups, not reverse)
    inj = coef_tiles(inj, groups)
    base = base_positions(meta, steps)
    zero = jnp.zeros((CHUNKS, LANES), f32)

    def visit(more, batch, q, first, start, found, src):
        if q is None:
            return more
        more = list(more)
        rows = pl.ds(batch * span + start, 2 * CHUNKS)
        drive_re, drive_im = drive[rows, lanes_of(q)], drive[rows, lanes_of(q, half)]
        before = pl.ds(batch * padded + start + (CHUNKS if reverse else 0), 2 * CHUNKS)
        prior_re, prior_im = states[before, lanes_of(q)], states[before, lanes_of(q, half)]
        dec_re, dec_im, inj_re, inj_im = more[q]
        out_re, out_im = [], []
        for j in (0, 1):
            part = slice(j * CHUNKS, (j + 1) * CHUNKS)
            adj_re, adj_im = found[j]
            keep = keep_of(meta, batch, base, first + j, reverse)
            kept_re, kept_im = keep * adj_re, keep * adj_im
            dec_re = dec_re + kept_re * prior_re[part] + kept_im * prior_im[part]
            dec_im = dec_im + kept_im * prior_re[part] - kept_re * prior_im[part]
            inj_re = inj_re + adj_re * drive_re[part] + adj_im * drive_im[part]
            inj_im = inj_im + adj_im * drive_re[part] - adj_re * drive_im[part]
            out_re.append(inj[q][0] * adj_re + inj[q][1] * adj_im)
            out_im.append(inj[q][0] * adj_im - inj[q][1] * adj_re)
        grad_proj[rows, lanes_of(q)] = jnp.concatenate(out_re, axis=0).astype(bf16)
        grad_proj[rows, lanes_of(q, half)] = jnp.concatenate(out_im, axis=0).astype(bf16)
        more[q] = (dec_re, dec_im, inj_re, inj_im)
        return tuple(more)

    _, sums = scan(
        meta, source, None, coef_tiles(dec, groups), batches, span, groups,
        not reverse, not reverse, init, ((zero,) * 4,) * groups, visit,
    )
    small[...] = jnp.zeros_like(small)
    for q in range(groups):
        for kind in range(4):
            small[kind : kind + 1, lanes_of(q)] = jnp.sum(sums[q][kind], axis=0, keepdims=True)
    small[4:5, :] = grad_d[...]
    grad_u[...] = dot(grad_proj[...], b_proj[layer], (1, 1))
    skip = norms[layer + 4 : layer + 5, :]
    plain, times_normed = [], []
    for batch in range(batches):
        average = norm[batch : batch + 1, :]
        scale = norm[batches + batch : batches + batch + 1, :]

        def body(start, carry, batch=batch, average=average, scale=scale):
            rows = pl.ds(batch * span + start, ROWS)
            value = grad_u[rows, :] + grad_mixed[rows, :] * skip
            grad_u[rows, :] = value
            normed = (hidden[rows, :].astype(f32) - average) * scale
            return carry[0] + fold(value), carry[1] + fold(value * normed)

        zero_sum = jnp.zeros((CHUNKS, grad_u.shape[1]), f32)
        one, two = row_loop(span, body, (zero_sum, zero_sum))
        plain.append(one)
        times_normed.append(two)
    add_sums(stats, batches, (plain, times_normed))


def backward_finish_last(cfg, *refs):
    ins, before, (grad_proj, grad_u, sums) = refs[:-4], refs[-4], refs[-3:]
    sums[...] = jnp.zeros_like(sums)
    sums[2 * CHUNKS :, :] = before[...]
    backward_finish(
        cfg, *ins, grad_proj, grad_u, sums.at[pl.ds(0, CHUNKS)], sums.at[pl.ds(CHUNKS, CHUNKS)]
    )


def norm_backward(cfg, stats, grad_out, grad_u, hidden, norm, norms, store, shared):
    layer, reverse, batches, span, groups, tokens, count = cfg
    sums = sum(part[...] for part in stats)
    shared[0:1, :] = jnp.sum(sums[batches:], axis=0, keepdims=True)
    shared[1:2, :] = jnp.sum(sums[:batches], axis=0, keepdims=True)
    gain_now = norms[layer : layer + 1, :]
    for batch in range(batches):
        average = norm[batch : batch + 1, :]
        scale = norm[batches + batch : batches + batch + 1, :]
        plain = gain_now * sums[batch : batch + 1] / tokens
        slanted = gain_now * sums[batches + batch : batches + batch + 1] / tokens

        def body(start, carry, batch=batch, average=average, scale=scale, plain=plain, slanted=slanted):
            rows = pl.ds(batch * span + start, ROWS)
            normed = (hidden[rows, :].astype(f32) - average) * scale
            value = grad_out[rows, :].astype(f32) + scale * (
                grad_u[rows, :] * gain_now - plain - normed * slanted
            )
            store(rows, value)
            return carry

        row_loop(span, body)


def between_layers(
    cfg, lower, place, stats, upper_out, upper_u, upper_hidden, upper_norm, norms,
    disc, u, c_proj, w_gate, states_low, act, sig, slope,
    grad_out, shared, grad_gate, grad_mixed, grad_low, source, prefix, total, grad_d, wide,
):
    def store(rows, value):
        grad_out[rows, :] = value

    norm_backward(cfg, stats, upper_out, upper_u, upper_hidden, upper_norm, norms, store, shared)
    meta = place_documents(lower, place)
    backward_start(
        lower, meta, grad_out, disc, u, c_proj, w_gate, states_low, act, sig, slope,
        grad_gate, grad_mixed, grad_low, source, prefix, total, grad_d, wide,
    )


def last_step(cfg, stats, grad_out, grad_u, hidden, norm, norms, target, shared, ordered):
    layer, reverse, batches, span, groups, tokens, count = cfg
    planes = target.shape[1] // LANES

    def store(rows, value):
        for plane in range(planes):
            ordered[plane, rows, :] = value[:, lanes_of(plane)]

    norm_backward(cfg, stats, grad_out, grad_u, hidden, norm, norms, store, shared)
    steps = span // CHUNKS
    for batch in range(batches):
        for chunk in range(CHUNKS):
            at = batch * span
            for plane in range(planes):
                target[at + chunk * steps : at + (chunk + 1) * steps, lanes_of(plane)] = ordered[
                    plane, pl.ds(at + chunk, steps, stride=CHUNKS), :
                ]


def half_weights(core, refs, own, sent):
    for target, half in ((own, core), (sent, 1 - core)):
        at = 0
        for left, right in refs:
            rows = left.shape[1] // 2
            cols = pl.ds(pl.multiple_of(half * rows, LANES), rows)
            target[at : at + rows, :] = dot(left[:, cols], right[...], (0, 0))
            at += rows


def all_weights(here, act, grad_gate, states_low, grad_low, grad_proj, u, own, sent):
    refs = ((act, grad_gate), (states_low, grad_low), (grad_proj, u))
    half_weights(lax.rem(here[0], 2), refs, own, sent)


def gate_weights(here, act, grad_gate, states_low, grad_low, own, sent):
    half_weights(lax.rem(here[0], 2), ((act, grad_gate), (states_low, grad_low)), own, sent)


def input_weights(here, grad_proj, u, own, sent):
    half_weights(lax.rem(here[0], 2), ((grad_proj, u),), own, sent)


def run(body, name, args, outs, scratch=(), scalars=1):
    vmem, smem = pl.BlockSpec(memory_space=pltpu.VMEM), pl.BlockSpec(memory_space=pltpu.SMEM)
    specs = tuple(
        jax.tree.map(lambda _, at=at: smem if at < scalars else vmem, arg)
        for at, arg in enumerate(args)
    )
    return pl.pallas_call(
        body,
        name=name,
        out_shape=tuple(jax.ShapeDtypeStruct(*out) for out in outs),
        in_specs=specs,
        out_specs=(vmem,) * len(outs),
        scratch_shapes=[pltpu.VMEM(*entry) for entry in scratch],
        compiler_params=pltpu.CompilerParams(vmem_limit_bytes=VMEM_LIMIT),
    )(*args)


def put_halves(own, other, grad_w, grad_c, grad_b):
    rows_w, rows_c = grad_w.shape[1], grad_c.shape[1]
    for now, source in ((0, own), (1, other)):

        @pl.when(pl.program_id(0) == now)
        def _(source=source):
            grad_w[0] = source[:rows_w, :]
            grad_c[0] = source[rows_w : rows_w + rows_c, :]
            grad_b[0] = source[rows_w + rows_c :, :].T


def put_in_place(layer, here, own, other, outs, before):
    width, states = outs[0][0][1], outs[1][0][1]
    vmem = pl.BlockSpec(memory_space=pltpu.VMEM)

    def half(step, here):
        core = lax.rem(here[0], 2)
        return jnp.where(step == 0, core, 1 - core)

    blocks = (
        pl.BlockSpec((1, width // 2, width), lambda i, here: (layer, half(i, here), 0)),
        pl.BlockSpec((1, states // 2, width), lambda i, here: (layer, half(i, here), 0)),
        pl.BlockSpec((1, width, states // 2), lambda i, here: (layer, 0, half(i, here))),
    )

    def body(here_ref, *refs):
        put_halves(*refs[:2], *refs[-3:])

    return pl.pallas_call(
        body,
        name="put_in_place",
        out_shape=tuple(jax.ShapeDtypeStruct(*out) for out in outs),
        grid_spec=pltpu.PrefetchScalarGridSpec(
            num_scalar_prefetch=1,
            grid=(2,),
            in_specs=[vmem] * 2 + [pl.BlockSpec(memory_space=pl.ANY)] * len(before),
            out_specs=blocks,
        ),
        input_output_aliases={3 + i: i for i in range(len(before))},
        compiler_params=pltpu.CompilerParams(vmem_limit_bytes=VMEM_LIMIT),
    )(here, own, other, *before)


def axis_parts():
    count, depth = lax.axis_size("seq"), lax.axis_size("dp")
    return (("seq", 2, 1, count), ("seq", count // 2, 2, count), ("dp", depth, 1, depth))


def shifted(value, part, away):
    name, size, stride, count = part
    pairs = []
    for i in range(count):
        place = (i // stride) % size
        pairs.append((i, i + ((place + away) % size - place) * stride))
    return lax.ppermute(value, name, pairs)


def add_by_shifts(value, parts, *earlier):
    for number, part in enumerate(parts):
        if number:
            value = sum(terms[1:], terms[0])
        if number == len(parts) - 1:
            value, *earlier = lax.optimization_barrier((value, *earlier))
        terms = [value] + [shifted(value, part, away) for away in range(1, part[1])]
    return terms, *earlier


def bits_of(size, stride=1):
    bits = []
    while size > 1:
        bits.append(stride)
        size, stride = size // 2, stride * 2
    return bits


def plane_bits():
    chip_bits = bits_of(lax.axis_size("seq") // 2, 2)
    middle = (len(chip_bits) + 1) // 2
    inner, outer = chip_bits[:middle], chip_bits[middle:]
    return list(zip(inner + outer, outer + inner))


def swap(value, axis, bit):
    return lax.ppermute(value, axis, [(i, i ^ bit) for i in range(lax.axis_size(axis))])


def bit_at(here, axis, bit):
    return lax.rem(lax.div(here[0 if axis == "seq" else 1], bit), 2)


def rows_at(half, rows):
    return pl.ds(pl.multiple_of(half * rows, CHUNKS), rows)


def fold_cores(bits, here, *refs):
    terms, targets = refs[:-4], refs[-4:]
    rows, cols = targets[0].shape
    for side in (0, 1):
        kept, sent = targets[2 * side : 2 * side + 2]
        where = slice(side * cols, (side + 1) * cols)
        bit = bit_at(here, "seq", bits[side])
        for half in (0, 1):

            @pl.when(bit == half)
            def _(half=half, kept=kept, sent=sent, where=where):
                start = 0
                for own, found in zip(terms[0::2], terms[1::2]):
                    for part, target in ((half, kept), (1 - half, sent)):
                        low = max(start, part * rows)
                        high = min(start + own.shape[0], (part + 1) * rows)
                        if low < high:
                            source = slice(low - start, high - start)
                            target[low - part * rows : high - part * rows, :] = (
                                own[source, where] + found[source, where]
                            )
                    start += own.shape[0]


def fold_sides(bits, here, *refs):
    for side in (0, 1):
        own, found = refs[2 * side : 2 * side + 2]
        kept, sent = refs[4 + 2 * side : 6 + 2 * side]
        half, rows = bit_at(here, "seq", bits[side]), kept.shape[0]
        kept[...] = own[rows_at(half, rows), :] + found[rows_at(half, rows), :]
        sent[...] = own[rows_at(1 - half, rows), :] + found[rows_at(1 - half, rows), :]


def fold_join(bit, here, left, found_left, right, found_right, kept, sent):
    rows, cols = kept.shape[0], left.shape[1]
    half = bit_at(here, "dp", bit)
    for side, (own, found) in enumerate(((left, found_left), (right, found_right))):
        where = slice(side * cols, (side + 1) * cols)
        kept[:, where] = own[rows_at(half, rows), :] + found[rows_at(half, rows), :]
        sent[:, where] = own[rows_at(1 - half, rows), :] + found[rows_at(1 - half, rows), :]


def fold_depth(bit, here, own, found, kept, sent):
    half, rows = bit_at(here, "dp", bit), kept.shape[0]
    kept[...] = own[rows_at(half, rows), :] + found[rows_at(half, rows), :]
    sent[...] = own[rows_at(1 - half, rows), :] + found[rows_at(1 - half, rows), :]


def add_two(own, found, out):
    out[...] = own[...] + found[...]


def unfold(bit, here, own, found, out):
    half, rows = bit_at(here, "dp", bit), own.shape[0]
    out[rows_at(half, rows), :] = own[...]
    out[rows_at(1 - half, rows), :] = found[...]


def unfold_split(bit, here, own, found, left, right):
    half, rows, cols = bit_at(here, "dp", bit), own.shape[0], left.shape[1]
    for side, out in enumerate((left, right)):
        where = slice(side * cols, (side + 1) * cols)
        out[rows_at(half, rows), :] = own[:, where]
        out[rows_at(1 - half, rows), :] = found[:, where]


def unfold_sides(bits, joined, here, *refs):
    for side in (0, 1):
        own, found = refs[2 * side : 2 * side + 2]
        half, (rows, cols) = bit_at(here, "seq", bits[side]), own.shape
        out = refs[4] if joined else refs[4 + side]
        where = slice(side * cols, (side + 1) * cols) if joined else slice(0, cols)
        out[rows_at(half, rows), where] = own[...]
        out[rows_at(1 - half, rows), where] = found[...]


def link_call(body, here, args, shapes):
    name = body.func.__name__
    return run(body, name, (here, *args), tuple((shape, f32) for shape in shapes))


class LinkSum:
    def __init__(self, here, terms):
        self.here, self.plane = here, plane_bits()
        self.depth = bits_of(lax.axis_size("dp"))
        rows = sum(term.shape[0] for term in terms[::2])
        self.shape = (rows // 2, terms[0].shape[1] // 2)
        self.parts = link_call(
            functools.partial(fold_cores, self.plane[0]), here, terms, (self.shape,) * 4
        )

    def swap_plane(self, stage):
        (left, right), pieces = self.plane[stage], self.parts
        self.parts = (
            pieces[0], swap(pieces[1], "seq", left), pieces[2], swap(pieces[3], "seq", right)
        )

    def down_plane(self, stage):
        rows, cols = self.shape
        self.shape = (rows // 2, cols)
        body = functools.partial(fold_sides, self.plane[stage])
        self.parts = link_call(body, self.here, self.parts, (self.shape,) * 4)

    def down_join(self):
        rows, cols = self.shape
        self.shape = (rows // 2, 2 * cols)
        body = functools.partial(fold_join, self.depth[0])
        self.parts = link_call(body, self.here, self.parts, (self.shape,) * 2)

    def swap_depth(self, stage):
        self.parts = (self.parts[0], swap(self.parts[1], "dp", self.depth[stage]))

    def down_depth(self, stage):
        rows, cols = self.shape
        self.shape = (rows // 2, cols)
        body = functools.partial(fold_depth, self.depth[stage])
        self.parts = link_call(body, self.here, self.parts, (self.shape,) * 2)

    def middle(self):
        (value,) = run(add_two, "add_two", self.parts, ((self.shape, f32),), scalars=0)
        self.parts = (value, value)

    def up_depth(self, stage):
        rows, cols = self.shape
        self.shape = (rows * 2, cols)
        body = functools.partial(unfold, self.depth[stage])
        (value,) = link_call(body, self.here, self.parts, (self.shape,))
        self.parts = (value, value)

    def up_split(self):
        rows, cols = self.shape
        self.shape = (rows * 2, cols // 2)
        body = functools.partial(unfold_split, self.depth[0])
        left, right = link_call(body, self.here, self.parts, (self.shape,) * 2)
        self.parts = (left, left, right, right)

    def up_plane(self, stage):
        rows, cols = self.shape
        if stage:
            self.shape = (rows * 2, cols)
            body = functools.partial(unfold_sides, self.plane[stage], False)
            left, right = link_call(body, self.here, self.parts, (self.shape,) * 2)
            self.parts = (left, left, right, right)
        else:
            self.shape = (rows * 2, cols * 2)
            body = functools.partial(unfold_sides, self.plane[stage], True)
            self.parts = link_call(body, self.here, self.parts, (self.shape,))

    def after(self, *values):
        self.parts, values = lax.optimization_barrier((self.parts, values))
        return values

    def to_depth(self):
        for stage in range(1, len(self.plane)):
            self.down_plane(stage)
            self.swap_plane(stage)
        self.down_join()

    def over_depth(self):
        last = len(self.depth) - 1
        for stage in range(last):
            self.swap_depth(stage)
            self.down_depth(stage + 1)
        self.swap_depth(last)
        self.middle()
        for stage in range(last, 0, -1):
            self.swap_depth(stage)
            self.up_depth(stage)
        self.swap_depth(0)
        self.up_split()

    def back(self):
        for stage in range(len(self.plane) - 1, -1, -1):
            self.swap_plane(stage)
            self.up_plane(stage)
        return self.parts[0]


def discretize(lam_re, lam_im, log_step):
    step_size = jnp.exp(log_step)
    decay_abs = jnp.exp(lam_re * step_size)
    rotation = lam_im * step_size
    dec_re = decay_abs * jnp.cos(rotation)
    dec_im = decay_abs * jnp.sin(rotation)
    denom_sq = lam_re * lam_re + lam_im * lam_im
    inj_re = ((dec_re - 1.0) * lam_re + dec_im * lam_im) / denom_sq
    inj_im = (dec_im * lam_re - (dec_re - 1.0) * lam_im) / denom_sq
    return (dec_re, dec_im, inj_re, inj_im)


def per_device(
    block_in, cotangent, doc_lengths, norm_gain, norm_shift, log_step, lam_re, lam_im,
    b_proj, c_proj, d_skip, w_gate,
):
    batches, seqs, span, width = block_in.shape
    assert seqs == 1 and span % (4 * CHUNKS) == 0 and span & (span - 1) == 0
    half = lam_re.shape[1]
    groups = half // LANES
    rows = batches * span
    count = lax.axis_size("seq")
    tokens = float(seqs * lax.axis_size("dp") * span * count)
    here = jnp.stack([lax.axis_index("seq"), lax.axis_index("dp")]).astype(jnp.int32)
    place = jnp.concatenate([here, doc_lengths.reshape(-1)])
    place, block_in = lax.optimization_barrier((place, block_in))
    here = place
    disc = discretize(lam_re, lam_im, log_step)

    x = block_in.reshape(rows, width)
    cot = cotangent.reshape(rows, width)
    lower = (0, False, batches, span, groups, tokens, count)
    upper = (1, True, batches, span, groups, tokens, count)
    part = functools.partial

    flat, low = ((rows, width), f32), ((rows, width), bf16)
    wide, wide_low = ((rows, 2 * half), f32), ((rows, 2 * half), bf16)
    padded = ((batches * (span + CHUNKS), 2 * half), f32)
    sums = ((2 * batches, width), f32)
    prefix = ((2, batches * CHUNKS, 2 * half), f32)
    total = ((batches, 2 * half), f32)
    line, shared = ((1, width), f32), ((2, width), f32)
    small = ((8, width), f32)

    def gather_row(value):
        return lax.all_gather(value, "seq")

    ordered, stats = run(
        part(first_sums, batches, span), "first_sums", (x,), (low, sums), scalars=0
    )
    norms = jnp.concatenate([norm_gain, norm_shift, d_skip], axis=0)

    def forward(cfg, hidden, stats):
        return run(
            part(enter_layer, cfg),
            "enter_layer",
            (place, stats, hidden, norms, disc, b_proj),
            (low, wide, prefix, total, sums),
        )

    links, plane, depth = axis_parts()
    u0, drive0, prefix0, total0, norm0 = forward(
        lower, ordered, add_by_shifts(stats, (links, plane, depth))[0]
    )
    states0, states_low0, act0, sig0, slope0, hidden1, stats = run(
        part(middle_forward, lower),
        "middle_forward",
        (place, gather_row(total0), prefix0, disc, drive0, u0, ordered, c_proj, norms, w_gate),
        (padded, wide_low, low, flat, flat, flat, sums),
        (flat,),
    )
    u1, drive1, prefix1, total1, norm1 = forward(
        upper, hidden1, add_by_shifts(stats, (links, plane, depth))[0]
    )
    (
        block_out, ordered_cot, states1, states_low1, act1, grad_gate1, grad_mixed1, grad_low1,
        source1, prefix1, total1, grad_d1,
    ) = run(
        part(turn_around, upper),
        "turn_around",
        (
            place, gather_row(total1), prefix1, disc, drive1, u1, hidden1, c_proj, norms, w_gate,
            cot,
        ),
        (low, low, padded, wide_low, low, low, flat, low, wide, prefix, total, line),
        (flat, flat, flat, low),
    )

    def halves(length):
        return (((length // 2, width), f32),) * 2

    grad_proj1, grad_u1, stats, small1 = run(
        part(backward_finish, upper),
        "backward_finish",
        (
            place, gather_row(total1), prefix1, disc, source1, drive1, states1, u1, grad_mixed1,
            grad_d1, hidden1, norm1, norms, b_proj,
        ),
        (wide_low, flat, sums, small),
    )
    sizes = (width + 2 * half, 2 * half)
    own1, sent1 = run(
        all_weights,
        "all_weights",
        (here, act1, grad_gate1, states_low1, grad_low1, grad_proj1, u1),
        halves(sum(sizes)),
    )
    upper_sum = LinkSum(here, (own1, swap(sent1, "seq", 1)))
    stats, upper_sum.parts = add_by_shifts(stats, (links, plane, depth), upper_sum.parts)
    upper_sum.swap_plane(0)
    stats, *_ = upper_sum.after(stats)
    upper_sum.to_depth()
    (
        grad_out0, shared1, grad_gate0, grad_mixed0, grad_low0, source0, prefix0, total0, grad_d0,
    ) = run(
        part(between_layers, upper, lower),
        "between_layers",
        (
            place, stats, ordered_cot, grad_u1, hidden1, norm1, norms,
            disc, u0, c_proj, w_gate, states_low0, act0, sig0, slope0,
        ),
        (flat, shared, low, flat, low, wide, prefix, total, line),
        (flat,),
    )
    own_gates, sent_gates = run(
        gate_weights, "gate_weights", (here, act0, grad_gate0, states_low0, grad_low0),
        halves(sizes[0]),
    )
    found_gates = swap(sent_gates, "seq", 1)
    own_gates, total0 = lax.optimization_barrier((own_gates, total0))
    found_gates, ends = lax.optimization_barrier((found_gates, gather_row(total0)))
    (ends,) = upper_sum.after(ends)
    grad_proj0, grad_u0, last_sums = run(
        part(backward_finish_last, lower),
        "backward_finish",
        (
            place, ends, prefix0, disc, source0, drive0, states0, u0, grad_mixed0, grad_d0,
            ordered, norm0, norms, b_proj, small1,
        ),
        (wide_low, flat, ((3 * CHUNKS, width), f32)),
    )
    own_inputs, sent_inputs = run(
        input_weights, "input_weights", (here, grad_proj0, u0), halves(sizes[1])
    )
    lower_sum = LinkSum(here, (own_gates, found_gates, own_inputs, swap(sent_inputs, "seq", 1)))
    (last_sums,) = lower_sum.after(last_sums)
    upper_sum.over_depth()
    lower_sum.swap_plane(0)
    lower_sum.to_depth()
    summed, lower_sum.parts = add_by_shifts(last_sums, (depth, links, plane), lower_sum.parts)
    summed = sum(summed)
    final = (((2, width, width), f32), ((2, 2 * half, width), f32), ((2, width, 2 * half), f32))
    (summed,) = upper_sum.after(summed)
    own1 = upper_sum.back()
    other1 = swap(own1, "seq", 1)
    grad_input, shared0 = run(
        part(last_step, lower),
        "last_step",
        ((summed[: 2 * batches],), grad_out0, grad_u0, ordered, norm0, norms),
        (flat, shared),
        (((width // LANES, rows, LANES), f32),),
        scalars=0,
    )
    small_sum = summed[CHUNKS:].reshape(2, CHUNKS, width)
    _, pullback = jax.vjp(discretize, lam_re, lam_im, log_step)
    grad_lr, grad_li, grad_ls = pullback(tuple(small_sum[:, kind, :half] for kind in range(4)))
    lower_sum.over_depth()
    own1, grad_input, grad_lr, grad_li, grad_ls = lower_sum.after(
        own1, grad_input, grad_lr, grad_li, grad_ls
    )
    own0 = lower_sum.back()
    other0 = swap(own0, "seq", 1)
    placed = put_in_place(1, here, own1, other1, final, ())
    grad_w, grad_c, grad_b = put_in_place(0, here, own0, other0, final, placed)
    both = jnp.stack([shared0, shared1])
    shape = block_in.shape
    return (
        block_out.reshape(shape), grad_input.reshape(shape), both[:, 0], both[:, 1],
        grad_ls, grad_lr, grad_li, grad_b, grad_c, small_sum[:, 4], grad_w,
    )


def solution(mesh):
    split = P(None, "dp", "seq", None)
    return jax.shard_map(
        per_device,
        mesh=mesh,
        in_specs=(split, split, P(None, "dp", None)) + (P(),) * 9,
        out_specs=(split, split) + (P(),) * 9,
        check_vma=False,
    )
```

```python
import functools

import jax
import jax.numpy as jnp
from jax import lax
from jax.experimental import pallas as pl
from jax.experimental.pallas import tpu as pltpu
from jax.sharding import PartitionSpec as P

f32, bf16 = jnp.float32, jnp.bfloat16
epsilon = 1e-05
tanh_scale = 0.7978845608028654
cubic_term = 0.044715
LANES = 128
CHUNKS = 8
ROWS = 32
VMEM_LIMIT = 16 * 1024 * 1024


def dot(left, right, contract=(1, 0)):
    return lax.dot_general(
        left, right, (((contract[0],), (contract[1],)), ((), ())), preferred_element_type=f32
    )


def reorder(span, inverse):
    shape = (span, span)
    kept, moved = (1, 0) if inverse else (0, 1)
    row = lax.broadcasted_iota(jnp.int32, shape, kept)
    position = lax.broadcasted_iota(jnp.int32, shape, moved)
    source = (row & (CHUNKS - 1)) * (span // CHUNKS) + (row >> 3)
    return jnp.where(position == source, 1.0, 0.0).astype(bf16)


def row_loop(count, body, init=0, step=ROWS):
    def one(index, carry):
        return body(pl.multiple_of(index * step, step), carry)

    return lax.fori_loop(0, count // step, one, init)


def documents(here, batches, span, count):
    mine = here[0]
    first = mine * span
    out = []
    for batch in range(batches):
        begins, ends, so_far = [], [], 0
        docs = (here.shape[0] - 2) // batches
        for doc in range(docs):
            begins.append(so_far)
            so_far = so_far + here[2 + batch * docs + doc]
            ends.append(so_far)
        before, after = 0, 2 * count * span
        for begin, end in zip(begins, ends):
            before = jnp.maximum(before, jnp.where(begin < first, begin, 0))
            after = jnp.minimum(after, jnp.where(end > first + span, end, 2 * count * span))
        after = jnp.where(mine == count - 1, 0, after)
        out.append(begins + ends + [before, after, first, mine])
    return out


def place_documents(cfg, place):
    layer, reverse, batches, span, groups, tokens, count = cfg
    return documents(place, batches, span, count)


def keep_of(meta, batch, base, step, backward):
    docs = (len(meta[batch]) - 4) // 2
    off = docs if backward else 0
    late = 1 if backward else 0
    stop = base == meta[batch][off] - step - late
    for doc in range(1, docs):
        stop = jnp.logical_or(stop, base == meta[batch][off + doc] - step - late)
    return jnp.where(stop, 0.0, 1.0)


def base_positions(meta, steps):
    return meta[0][-2] + lax.broadcasted_iota(jnp.int32, (CHUNKS, LANES), 0) * steps


def lanes_of(index, half=0):
    return slice(half + index * LANES, half + (index + 1) * LANES)


def coef_tiles(value, groups):
    return [
        tuple(jnp.broadcast_to(part[:, lanes_of(q)], (CHUNKS, LANES)) for part in value)
        for q in range(groups)
    ]


def constants(disc, layer):
    dec_re, dec_im, inj_re, inj_im = (part[layer : layer + 1, :] for part in disc)
    return (dec_re, dec_im), (inj_re, inj_im)


def times(a, b):
    return (a[0] * b[0] - a[1] * b[1], a[0] * b[1] + a[1] * b[0])


def power(value, exponent):
    for _ in range(exponent.bit_length() - 1):
        value = times(value, value)
    return value


def conj(value):
    return (value[0], -value[1])


def scan(meta, source, inject, dec, batches, span, groups, reverse, masks_reverse, init, extra, visit):
    steps = span // CHUNKS
    half = groups * LANES
    base = base_positions(meta, steps)

    def pair(index, carry):
        states, more = carry
        states = list(states)
        first = steps - 2 - 2 * index if reverse else 2 * index
        start = pl.multiple_of(first * CHUNKS, 2 * CHUNKS)
        order = (1, 0) if reverse else (0, 1)
        for batch in range(batches):
            keeps = [keep_of(meta, batch, base, first + j, masks_reverse) for j in (0, 1)]
            for q in range(groups):
                rows = pl.ds(batch * span + start, 2 * CHUNKS)
                src_re = source[rows, lanes_of(q)]
                src_im = source[rows, lanes_of(q, half)]
                state = states[batch * groups + q]
                found = [None, None]
                for j in order:
                    part = (
                        src_re[j * CHUNKS : (j + 1) * CHUNKS],
                        src_im[j * CHUNKS : (j + 1) * CHUNKS],
                    )
                    push = times(inject[q], part) if inject is not None else part
                    held = times((keeps[j] * dec[q][0], keeps[j] * dec[q][1]), state)
                    state = (held[0] + push[0], held[1] + push[1])
                    found[j] = state
                states[batch * groups + q] = state
                more = visit(more, batch, q, first, start, found, (src_re, src_im))
            more = visit(more, batch, None, first, start, keeps, None)
        return tuple(states), more

    return lax.fori_loop(0, steps // 2, pair, (tuple(init), extra), unroll=2)


def zero_states(batches, groups):
    zero = jnp.zeros((CHUNKS, LANES), f32)
    return [(zero, zero)] * (batches * groups)


def local_ends(meta, source, inject, dec, batches, span, groups, reverse, prefix, total):
    ones = tuple(jnp.ones((CHUNKS, LANES), f32) for _ in range(batches))

    def visit(more, batch, q, first, start, found, src):
        if q is not None:
            return more
        return tuple(
            value * found[0] * found[1] if at == batch else value for at, value in enumerate(more)
        )

    dec_chunk = coef_tiles(power(dec, span // CHUNKS), groups)
    ends, kept = scan(
        meta, source, inject, coef_tiles(dec, groups), batches, span, groups, reverse, reverse,
        zero_states(batches, groups), ones, visit,
    )
    half = groups * LANES
    row = lax.broadcasted_iota(jnp.int32, (CHUNKS, LANES), 0)
    for batch in range(batches):
        for q in range(groups):
            end = ends[batch * groups + q]
            decay = (kept[batch] * dec_chunk[q][0], kept[batch] * dec_chunk[q][1])
            for shift in (1, 2, 4):
                turn = CHUNKS - shift if reverse else shift
                valid = row < CHUNKS - shift if reverse else row >= shift
                before = [pltpu.roll(value, turn, 0) for value in (*end, *decay)]
                from_before = times(decay, (before[0], before[1]))
                end = (
                    end[0] + jnp.where(valid, from_before[0], 0.0),
                    end[1] + jnp.where(valid, from_before[1], 0.0),
                )
                longer = times(decay, (before[2], before[3]))
                decay = (
                    jnp.where(valid, longer[0], decay[0]),
                    jnp.where(valid, longer[1], decay[1]),
                )
            rows = slice(batch * CHUNKS, (batch + 1) * CHUNKS)
            prefix[0, rows, lanes_of(q)] = end[0]
            prefix[0, rows, lanes_of(q, half)] = end[1]
            prefix[1, rows, lanes_of(q)] = decay[0]
            prefix[1, rows, lanes_of(q, half)] = decay[1]
            last = 0 if reverse else CHUNKS - 1
            total[batch : batch + 1, lanes_of(q)] = end[0][last : last + 1]
            total[batch : batch + 1, lanes_of(q, half)] = end[1][last : last + 1]


def chunk_carries(meta, gathered, dec, prefix, batches, span, groups, reverse):
    count = gathered.shape[0]
    half = groups * LANES
    dec_span = power(dec, span)
    row = lax.broadcasted_iota(jnp.int32, (CHUNKS, LANES), 0)
    mine = meta[0][-1]
    out = []
    for batch in range(batches):

        def add(at, so_far, batch=batch):
            away = count - 2 - at
            if reverse:
                other = mine + 1 + away
                reaches = meta[batch][-3] > other * span
            else:
                other = mine - 1 - away
                reaches = meta[batch][-4] < (mine - away) * span
            other = jnp.clip(other, 0, count - 1)
            value = jnp.where(reaches, gathered[other, pl.ds(batch, 1), :], 0.0)
            moved = times(dec_span, so_far)
            return (moved[0] + value[:, :half], moved[1] + value[:, half:])

        zero = jnp.zeros((1, half), f32)
        enter = lax.fori_loop(0, count - 1, add, (zero, zero), unroll=count <= 8)
        rows = slice(batch * CHUNKS, (batch + 1) * CHUNKS)
        for q in range(groups):
            own = tuple(jnp.broadcast_to(part[:, lanes_of(q)], (CHUNKS, LANES)) for part in enter)
            end = (prefix[0, rows, lanes_of(q)], prefix[0, rows, lanes_of(q, half)])
            decay = (prefix[1, rows, lanes_of(q)], prefix[1, rows, lanes_of(q, half)])
            moved = times(decay, own)
            turn, first = (CHUNKS - 1, CHUNKS - 1) if reverse else (1, 0)
            out.append(
                tuple(
                    jnp.where(row == first, own[i], pltpu.roll(end[i] + moved[i], turn, 0))
                    for i in (0, 1)
                )
            )
    return out


def add_sums(target, batches, sums):
    for kind, per_batch in enumerate(sums):
        for batch in range(batches):
            target[kind * batches + batch : kind * batches + batch + 1, :] = jnp.sum(
                per_batch[batch], axis=0, keepdims=True
            )


def fold(value):
    return sum(value[i : i + CHUNKS] for i in range(CHUNKS, value.shape[0], CHUNKS)) + value[:CHUNKS]


def first_sums(batches, span, x, ordered, stats):
    turn = reorder(span, False)
    width = x.shape[1]
    sums, squares = [], []
    for batch in range(batches):
        rows = slice(batch * span, (batch + 1) * span)
        ordered[rows, :] = dot(turn, x[rows, :]).astype(bf16)

        def body(start, carry, batch=batch):
            value = x[pl.ds(batch * span + start, ROWS), :].astype(f32)
            return carry[0] + fold(value), carry[1] + fold(value * value)

        zero = jnp.zeros((CHUNKS, width), f32)
        one, two = row_loop(span, body, (zero, zero))
        sums.append(one)
        squares.append(two)
    add_sums(stats, batches, (sums, squares))


def enter_layer(
    cfg, place, stats, hidden, norms, disc, b_proj, u, drive, prefix, total, norm
):
    layer, reverse, batches, span, groups, tokens, count = cfg
    sums = sum(part[...] for part in stats)
    average = sums[:batches] / tokens
    spread = sums[batches:] / tokens - average * average
    scale = lax.rsqrt(spread + epsilon)
    norm[:batches, :] = average
    norm[batches:, :] = scale
    gain_now, shift_now = norms[layer : layer + 1, :], norms[layer + 2 : layer + 3, :]
    for batch in range(batches):

        def body(start, carry, batch=batch):
            rows = pl.ds(batch * span + start, ROWS)
            normed = (hidden[rows, :].astype(f32) - average[batch : batch + 1]) * scale[
                batch : batch + 1
            ]
            u[rows, :] = (normed * gain_now + shift_now).astype(bf16)
            return carry

        row_loop(span, body)
    drive[...] = dot(u[...], b_proj[layer])
    meta = place_documents(cfg, place)
    dec, inj = constants(disc, layer)
    local_ends(
        meta, drive, coef_tiles(inj, groups), dec, batches, span, groups, reverse, prefix, total
    )


def finish_states(cfg, meta, ends, prefix, disc, drive, states, states_low):
    layer, reverse, batches, span, groups, tokens, count = cfg
    half = groups * LANES
    padded = span + CHUNKS
    dec, inj = constants(disc, layer)
    init = chunk_carries(meta, ends, dec, prefix, batches, span, groups, reverse)
    for batch in range(batches):
        edge = batch * padded + (span if reverse else 0)
        for q in range(groups):
            states[edge : edge + CHUNKS, lanes_of(q)] = init[batch * groups + q][0]
            states[edge : edge + CHUNKS, lanes_of(q, half)] = init[batch * groups + q][1]

    def visit(more, batch, q, first, start, found, src):
        if q is not None:
            for part, off in ((0, 0), (1, half)):
                both = jnp.concatenate([found[0][part], found[1][part]], axis=0)
                at = batch * padded + (0 if reverse else CHUNKS)
                states[pl.ds(at + start, 2 * CHUNKS), lanes_of(q, off)] = both
                states_low[pl.ds(batch * span + start, 2 * CHUNKS), lanes_of(q, off)] = both.astype(
                    bf16
                )
        return more

    scan(
        meta, drive, coef_tiles(inj, groups), coef_tiles(dec, groups), batches, span, groups,
        reverse, reverse, init, 0, visit,
    )


def forward_finish(
    cfg, meta, ends, prefix, disc, drive, u, hidden, c_proj, norms, w_gate,
    states, states_low, act, sig, slope, result, wide, emit,
):
    layer, reverse, batches, span, groups, tokens, count = cfg
    finish_states(cfg, meta, ends, prefix, disc, drive, states, states_low)
    wide[...] = dot(states_low[...], c_proj[layer])
    skip = norms[layer + 4 : layer + 5, :]

    def body(start, carry):
        rows = pl.ds(start, ROWS)
        mixed = wide[rows, :] + skip * u[rows, :].astype(f32)
        square = mixed * mixed
        th = jnp.tanh(tanh_scale * (mixed + cubic_term * square * mixed))
        half_one = 0.5 * (1.0 + th)
        act[rows, :] = (mixed * half_one).astype(bf16)
        slope[rows, :] = half_one + 0.5 * mixed * (1.0 - th * th) * tanh_scale * (
            1.0 + 3.0 * cubic_term * square
        )
        return carry

    row_loop(batches * span, body)
    wide[...] = dot(act[...], w_gate[layer])
    sums, squares = [], []
    for batch in range(batches):

        def gate(start, carry, batch=batch):
            rows = pl.ds(batch * span + start, ROWS)
            sig_now = 0.5 + 0.5 * jnp.tanh(0.5 * wide[rows, :])
            sig[rows, :] = sig_now
            value = hidden[rows, :].astype(f32) + act[rows, :].astype(f32) * sig_now
            result[rows, :] = value.astype(result.dtype)
            if emit is None:
                return carry
            return carry[0] + fold(value), carry[1] + fold(value * value)

        zero = jnp.zeros((CHUNKS, wide.shape[1]), f32)
        one, two = row_loop(span, gate, (zero, zero))
        sums.append(one)
        squares.append(two)
    if emit is not None:
        add_sums(emit, batches, (sums, squares))


def backward_start(
    cfg, meta, grad_out, disc, u, c_proj, w_gate, states_low, act, sig, slope,
    grad_gate, grad_mixed, grad_low, source, prefix, total, grad_d, wide,
):
    layer, reverse, batches, span, groups, tokens, count = cfg

    def body(start, carry):
        rows = pl.ds(start, ROWS)
        sig_now = sig[rows, :]
        grad_gate[rows, :] = (
            grad_out[rows, :].astype(f32) * act[rows, :].astype(f32) * sig_now * (1.0 - sig_now)
        ).astype(bf16)
        return carry

    row_loop(batches * span, body)
    wide[...] = dot(grad_gate[...], w_gate[layer], (1, 1))

    def mixed(start, carry):
        rows = pl.ds(start, ROWS)
        value = (grad_out[rows, :].astype(f32) * sig[rows, :] + wide[rows, :]) * slope[rows, :]
        grad_mixed[rows, :] = value
        grad_low[rows, :] = value.astype(bf16)
        return carry + fold(value * u[rows, :].astype(f32))

    gd = row_loop(batches * span, mixed, jnp.zeros((CHUNKS, wide.shape[1]), f32))
    grad_d[...] = jnp.sum(gd, axis=0, keepdims=True)
    source[...] = dot(grad_low[...], c_proj[layer], (1, 1))
    local_ends(
        meta, source, None, conj(constants(disc, layer)[0]), batches, span, groups, not reverse,
        prefix, total,
    )


def middle_forward(
    cfg, place, ends, prefix, disc, drive, u, hidden, c_proj, norms, w_gate,
    states, states_low, act, sig, slope, result, stats, wide,
):
    meta = place_documents(cfg, place)
    forward_finish(
        cfg, meta, ends, prefix, disc, drive, u, hidden, c_proj, norms, w_gate,
        states, states_low, act, sig, slope, result, wide, stats,
    )


def turn_around(
    cfg, place, ends, prefix, disc, drive, u, hidden, c_proj, norms, w_gate, cotangent,
    block_out, ordered_cot, states, states_low, act, grad_gate, grad_mixed, grad_low, source,
    back_prefix, total, grad_d, sig, slope, wide, result,
):
    layer, reverse, batches, span, groups, tokens, count = cfg
    meta = place_documents(cfg, place)
    turn, back = reorder(span, False), reorder(span, True)
    for batch in range(batches):
        rows = slice(batch * span, (batch + 1) * span)
        ordered_cot[rows, :] = dot(turn, cotangent[rows, :]).astype(bf16)
    forward_finish(
        cfg, meta, ends, prefix, disc, drive, u, hidden, c_proj, norms, w_gate,
        states, states_low, act, sig, slope, result, wide, None,
    )
    for batch in range(batches):
        rows = slice(batch * span, (batch + 1) * span)
        block_out[rows, :] = dot(back, result[rows, :]).astype(bf16)
    backward_start(
        cfg, meta, ordered_cot, disc, u, c_proj, w_gate, states_low, act, sig, slope,
        grad_gate, grad_mixed, grad_low, source, back_prefix, total, grad_d, wide,
    )


def backward_finish(
    cfg, place, ends, prefix, disc, source, drive, states, u, grad_mixed, grad_d, hidden, norm,
    norms, b_proj, grad_proj, grad_u, stats, small,
):
    layer, reverse, batches, span, groups, tokens, count = cfg
    half = groups * LANES
    padded = span + CHUNKS
    steps = span // CHUNKS
    meta = place_documents(cfg, place)
    dec, inj = constants(disc, layer)
    dec = conj(dec)
    init = chunk_carries(meta, ends, dec, prefix, batches, span, groups, not reverse)
    inj = coef_tiles(inj, groups)
    base = base_positions(meta, steps)
    zero = jnp.zeros((CHUNKS, LANES), f32)

    def visit(more, batch, q, first, start, found, src):
        if q is None:
            return more
        more = list(more)
        rows = pl.ds(batch * span + start, 2 * CHUNKS)
        drive_re, drive_im = drive[rows, lanes_of(q)], drive[rows, lanes_of(q, half)]
        before = pl.ds(batch * padded + start + (CHUNKS if reverse else 0), 2 * CHUNKS)
        prior_re, prior_im = states[before, lanes_of(q)], states[before, lanes_of(q, half)]
        dec_re, dec_im, inj_re, inj_im = more[q]
        out_re, out_im = [], []
        for j in (0, 1):
            part = slice(j * CHUNKS, (j + 1) * CHUNKS)
            adj_re, adj_im = found[j]
            keep = keep_of(meta, batch, base, first + j, reverse)
            kept_re, kept_im = keep * adj_re, keep * adj_im
            dec_re = dec_re + kept_re * prior_re[part] + kept_im * prior_im[part]
            dec_im = dec_im + kept_im * prior_re[part] - kept_re * prior_im[part]
            inj_re = inj_re + adj_re * drive_re[part] + adj_im * drive_im[part]
            inj_im = inj_im + adj_im * drive_re[part] - adj_re * drive_im[part]
            out_re.append(inj[q][0] * adj_re + inj[q][1] * adj_im)
            out_im.append(inj[q][0] * adj_im - inj[q][1] * adj_re)
        grad_proj[rows, lanes_of(q)] = jnp.concatenate(out_re, axis=0).astype(bf16)
        grad_proj[rows, lanes_of(q, half)] = jnp.concatenate(out_im, axis=0).astype(bf16)
        more[q] = (dec_re, dec_im, inj_re, inj_im)
        return tuple(more)

    _, sums = scan(
        meta, source, None, coef_tiles(dec, groups), batches, span, groups,
        not reverse, not reverse, init, ((zero,) * 4,) * groups, visit,
    )
    small[...] = jnp.zeros_like(small)
    for q in range(groups):
        for kind in range(4):
            small[kind : kind + 1, lanes_of(q)] = jnp.sum(sums[q][kind], axis=0, keepdims=True)
    small[4:5, :] = grad_d[...]
    grad_u[...] = dot(grad_proj[...], b_proj[layer], (1, 1))
    skip = norms[layer + 4 : layer + 5, :]
    plain, times_normed = [], []
    for batch in range(batches):
        average = norm[batch : batch + 1, :]
        scale = norm[batches + batch : batches + batch + 1, :]

        def body(start, carry, batch=batch, average=average, scale=scale):
            rows = pl.ds(batch * span + start, ROWS)
            value = grad_u[rows, :] + grad_mixed[rows, :] * skip
            grad_u[rows, :] = value
            normed = (hidden[rows, :].astype(f32) - average) * scale
            return carry[0] + fold(value), carry[1] + fold(value * normed)

        zero_sum = jnp.zeros((CHUNKS, grad_u.shape[1]), f32)
        one, two = row_loop(span, body, (zero_sum, zero_sum))
        plain.append(one)
        times_normed.append(two)
    add_sums(stats, batches, (plain, times_normed))


def backward_finish_last(cfg, *refs):
    ins, before, (grad_proj, grad_u, sums) = refs[:-4], refs[-4], refs[-3:]
    sums[...] = jnp.zeros_like(sums)
    sums[2 * CHUNKS :, :] = before[...]
    backward_finish(
        cfg, *ins, grad_proj, grad_u, sums.at[pl.ds(0, CHUNKS)], sums.at[pl.ds(CHUNKS, CHUNKS)]
    )


def norm_backward(cfg, stats, grad_out, grad_u, hidden, norm, norms, store, shared):
    layer, reverse, batches, span, groups, tokens, count = cfg
    sums = sum(part[...] for part in stats)
    shared[0:1, :] = jnp.sum(sums[batches:], axis=0, keepdims=True)
    shared[1:2, :] = jnp.sum(sums[:batches], axis=0, keepdims=True)
    gain_now = norms[layer : layer + 1, :]
    for batch in range(batches):
        average = norm[batch : batch + 1, :]
        scale = norm[batches + batch : batches + batch + 1, :]
        plain = gain_now * sums[batch : batch + 1] / tokens
        slanted = gain_now * sums[batches + batch : batches + batch + 1] / tokens

        def body(start, carry, batch=batch, average=average, scale=scale, plain=plain, slanted=slanted):
            rows = pl.ds(batch * span + start, ROWS)
            normed = (hidden[rows, :].astype(f32) - average) * scale
            value = grad_out[rows, :].astype(f32) + scale * (
                grad_u[rows, :] * gain_now - plain - normed * slanted
            )
            store(rows, value)
            return carry

        row_loop(span, body)


def between_layers(
    cfg, lower, place, stats, upper_out, upper_u, upper_hidden, upper_norm, norms,
    disc, u, c_proj, w_gate, states_low, act, sig, slope,
    grad_out, shared, grad_gate, grad_mixed, grad_low, source, prefix, total, grad_d, wide,
):
    def store(rows, value):
        grad_out[rows, :] = value

    norm_backward(cfg, stats, upper_out, upper_u, upper_hidden, upper_norm, norms, store, shared)
    meta = place_documents(lower, place)
    backward_start(
        lower, meta, grad_out, disc, u, c_proj, w_gate, states_low, act, sig, slope,
        grad_gate, grad_mixed, grad_low, source, prefix, total, grad_d, wide,
    )


def last_step(cfg, stats, grad_out, grad_u, hidden, norm, norms, target, shared, ordered):
    layer, reverse, batches, span, groups, tokens, count = cfg
    planes = target.shape[1] // LANES

    def store(rows, value):
        for plane in range(planes):
            ordered[plane, rows, :] = value[:, lanes_of(plane)]

    norm_backward(cfg, stats, grad_out, grad_u, hidden, norm, norms, store, shared)
    steps = span // CHUNKS
    for batch in range(batches):
        for chunk in range(CHUNKS):
            at = batch * span
            for plane in range(planes):
                target[at + chunk * steps : at + (chunk + 1) * steps, lanes_of(plane)] = ordered[
                    plane, pl.ds(at + chunk, steps, stride=CHUNKS), :
                ]


def half_weights(core, refs, own, sent):
    for target, half in ((own, core), (sent, 1 - core)):
        at = 0
        for left, right in refs:
            rows = left.shape[1] // 2
            cols = pl.ds(pl.multiple_of(half * rows, LANES), rows)
            target[at : at + rows, :] = dot(left[:, cols], right[...], (0, 0))
            at += rows


def all_weights(here, act, grad_gate, states_low, grad_low, grad_proj, u, own, sent):
    refs = ((act, grad_gate), (states_low, grad_low), (grad_proj, u))
    half_weights(lax.rem(here[0], 2), refs, own, sent)


def gate_weights(here, act, grad_gate, states_low, grad_low, own, sent):
    half_weights(lax.rem(here[0], 2), ((act, grad_gate), (states_low, grad_low)), own, sent)


def input_weights(here, grad_proj, u, own, sent):
    half_weights(lax.rem(here[0], 2), ((grad_proj, u),), own, sent)


def run(body, name, args, outs, scratch=(), scalars=1):
    vmem, smem = pl.BlockSpec(memory_space=pltpu.VMEM), pl.BlockSpec(memory_space=pltpu.SMEM)
    specs = tuple(
        jax.tree.map(lambda _, at=at: smem if at < scalars else vmem, arg)
        for at, arg in enumerate(args)
    )
    return pl.pallas_call(
        body,
        name=name,
        out_shape=tuple(jax.ShapeDtypeStruct(*out) for out in outs),
        in_specs=specs,
        out_specs=(vmem,) * len(outs),
        scratch_shapes=[pltpu.VMEM(*entry) for entry in scratch],
        compiler_params=pltpu.CompilerParams(vmem_limit_bytes=VMEM_LIMIT),
    )(*args)


def put_in_place(layer, here, halves, outs, before):
    width, states = outs[0][0][1], outs[1][0][1]
    rows_w, rows_c = width // 2, states // 2
    vmem, count = pl.BlockSpec(memory_space=pltpu.VMEM), len(halves)

    def half(step, here):
        core = lax.rem(here[0], 2)
        spots = [1 - core if other else core for other, _ in halves]
        return spots[0] if count == 1 else jnp.where(step == 0, *spots)

    blocks = (
        pl.BlockSpec((1, rows_w, width), lambda i, here: (layer, half(i, here), 0)),
        pl.BlockSpec((1, rows_c, width), lambda i, here: (layer, half(i, here), 0)),
        pl.BlockSpec((1, width, rows_c), lambda i, here: (layer, 0, half(i, here))),
    )

    def body(here, *refs):
        grad_w, grad_c, grad_b = refs[-3:]
        for now in range(count):

            @pl.when(pl.program_id(0) == now)
            def _(source=refs[now]):
                grad_w[0] = source[:rows_w, :]
                grad_c[0] = source[rows_w : rows_w + rows_c, :]
                grad_b[0] = source[rows_w + rows_c :, :].T

    return pl.pallas_call(
        body,
        name="put_in_place",
        out_shape=tuple(jax.ShapeDtypeStruct(*out) for out in outs),
        grid_spec=pltpu.PrefetchScalarGridSpec(
            num_scalar_prefetch=1,
            grid=(count,),
            in_specs=[vmem] * count + [pl.BlockSpec(memory_space=pl.ANY)] * len(before),
            out_specs=blocks,
        ),
        input_output_aliases={1 + count + i: i for i in range(len(before))},
        compiler_params=pltpu.CompilerParams(vmem_limit_bytes=VMEM_LIMIT),
    )(here, *(rows for _, rows in halves), *before)


def axis_parts():
    count, depth = lax.axis_size("seq"), lax.axis_size("dp")
    return (("seq", 2, 1, count), ("seq", count // 2, 2, count), ("dp", depth, 1, depth))


def shifted(value, part, away):
    name, size, stride, count = part
    pairs = []
    for i in range(count):
        place = (i // stride) % size
        pairs.append((i, i + ((place + away) % size - place) * stride))
    return lax.ppermute(value, name, pairs)


def add_by_shifts(value, parts, *earlier):
    for number, part in enumerate(parts):
        if number:
            value = sum(terms[1:], terms[0])
        if number == len(parts) - 1:
            value, *earlier = lax.optimization_barrier((value, *earlier))
        terms = [value] + [shifted(value, part, away) for away in range(1, part[1])]
    return terms, *earlier


def bits_of(size, stride=1):
    bits = []
    while size > 1:
        bits.append(stride)
        size, stride = size // 2, stride * 2
    return bits


def plane_bits():
    chip_bits = bits_of(lax.axis_size("seq") // 2, 2)
    middle = (len(chip_bits) + 1) // 2
    inner, outer = chip_bits[:middle], chip_bits[middle:]
    return list(zip(inner + outer, outer + inner))


def swap(value, axis, bit):
    return lax.ppermute(value, axis, [(i, i ^ bit) for i in range(lax.axis_size(axis))])


def bit_at(here, axis, bit):
    return lax.rem(lax.div(here[0 if axis == "seq" else 1], bit), 2)


def rows_at(half, rows):
    return pl.ds(pl.multiple_of(half * rows, CHUNKS), rows)


def fold_cores(bits, here, *refs):
    terms, targets = refs[:-4], refs[-4:]
    rows, cols = targets[0].shape
    for side in (0, 1):
        kept, sent = targets[2 * side : 2 * side + 2]
        where = slice(side * cols, (side + 1) * cols)
        bit = bit_at(here, "seq", bits[side])
        for half in (0, 1):

            @pl.when(bit == half)
            def _(half=half, kept=kept, sent=sent, where=where):
                start = 0
                for own, found in zip(terms[0::2], terms[1::2]):
                    for part, target in ((half, kept), (1 - half, sent)):
                        low = max(start, part * rows)
                        high = min(start + own.shape[0], (part + 1) * rows)
                        if low < high:
                            source = slice(low - start, high - start)
                            target[low - part * rows : high - part * rows, :] = (
                                own[source, where] + found[source, where]
                            )
                    start += own.shape[0]


def fold_sides(bits, here, *refs):
    for side in (0, 1):
        own, found = refs[2 * side : 2 * side + 2]
        kept, sent = refs[4 + 2 * side : 6 + 2 * side]
        half, rows = bit_at(here, "seq", bits[side]), kept.shape[0]
        kept[...] = own[rows_at(half, rows), :] + found[rows_at(half, rows), :]
        sent[...] = own[rows_at(1 - half, rows), :] + found[rows_at(1 - half, rows), :]


def fold_join(bit, here, left, found_left, right, found_right, kept, sent):
    rows, cols = kept.shape[0], left.shape[1]
    half = bit_at(here, "dp", bit)
    for side, (own, found) in enumerate(((left, found_left), (right, found_right))):
        where = slice(side * cols, (side + 1) * cols)
        kept[:, where] = own[rows_at(half, rows), :] + found[rows_at(half, rows), :]
        sent[:, where] = own[rows_at(1 - half, rows), :] + found[rows_at(1 - half, rows), :]


def fold_depth(bit, here, own, found, kept, sent):
    half, rows = bit_at(here, "dp", bit), kept.shape[0]
    kept[...] = own[rows_at(half, rows), :] + found[rows_at(half, rows), :]
    sent[...] = own[rows_at(1 - half, rows), :] + found[rows_at(1 - half, rows), :]


def add_two(own, found, out):
    out[...] = own[...] + found[...]


def unfold(bit, here, own, found, out):
    half, rows = bit_at(here, "dp", bit), own.shape[0]
    out[rows_at(half, rows), :] = own[...]
    out[rows_at(1 - half, rows), :] = found[...]


def unfold_split(bit, here, own, found, left, right):
    half, rows, cols = bit_at(here, "dp", bit), own.shape[0], left.shape[1]
    for side, out in enumerate((left, right)):
        where = slice(side * cols, (side + 1) * cols)
        out[rows_at(half, rows), :] = own[:, where]
        out[rows_at(1 - half, rows), :] = found[:, where]


def unfold_sides(bits, joined, here, *refs):
    for side in (0, 1):
        own, found = refs[2 * side : 2 * side + 2]
        half, (rows, cols) = bit_at(here, "seq", bits[side]), own.shape
        out = refs[4] if joined else refs[4 + side]
        where = slice(side * cols, (side + 1) * cols) if joined else slice(0, cols)
        out[rows_at(half, rows), where] = own[...]
        out[rows_at(1 - half, rows), where] = found[...]


def link_call(body, here, args, shapes):
    name = body.func.__name__
    return run(body, name, (here, *args), tuple((shape, f32) for shape in shapes))


class LinkSum:
    def __init__(self, here, terms):
        self.here, self.plane = here, plane_bits()
        self.depth = bits_of(lax.axis_size("dp"))
        rows = sum(term.shape[0] for term in terms[::2])
        self.shape = (rows // 2, terms[0].shape[1] // 2)
        self.parts = link_call(
            functools.partial(fold_cores, self.plane[0]), here, terms, (self.shape,) * 4
        )

    def swap_plane(self, stage):
        (left, right), pieces = self.plane[stage], self.parts
        self.parts = (
            pieces[0], swap(pieces[1], "seq", left), pieces[2], swap(pieces[3], "seq", right)
        )

    def down_plane(self, stage):
        rows, cols = self.shape
        self.shape = (rows // 2, cols)
        body = functools.partial(fold_sides, self.plane[stage])
        self.parts = link_call(body, self.here, self.parts, (self.shape,) * 4)

    def down_join(self):
        rows, cols = self.shape
        self.shape = (rows // 2, 2 * cols)
        body = functools.partial(fold_join, self.depth[0])
        self.parts = link_call(body, self.here, self.parts, (self.shape,) * 2)

    def swap_depth(self, stage):
        self.parts = (self.parts[0], swap(self.parts[1], "dp", self.depth[stage]))

    def down_depth(self, stage):
        rows, cols = self.shape
        self.shape = (rows // 2, cols)
        body = functools.partial(fold_depth, self.depth[stage])
        self.parts = link_call(body, self.here, self.parts, (self.shape,) * 2)

    def middle(self):
        (value,) = run(add_two, "add_two", self.parts, ((self.shape, f32),), scalars=0)
        self.parts = (value, value)

    def up_depth(self, stage):
        rows, cols = self.shape
        self.shape = (rows * 2, cols)
        body = functools.partial(unfold, self.depth[stage])
        (value,) = link_call(body, self.here, self.parts, (self.shape,))
        self.parts = (value, value)

    def up_split(self):
        rows, cols = self.shape
        self.shape = (rows * 2, cols // 2)
        body = functools.partial(unfold_split, self.depth[0])
        left, right = link_call(body, self.here, self.parts, (self.shape,) * 2)
        self.parts = (left, left, right, right)

    def up_plane(self, stage):
        rows, cols = self.shape
        if stage:
            self.shape = (rows * 2, cols)
            body = functools.partial(unfold_sides, self.plane[stage], False)
            left, right = link_call(body, self.here, self.parts, (self.shape,) * 2)
            self.parts = (left, left, right, right)
        else:
            self.shape = (rows * 2, cols * 2)
            body = functools.partial(unfold_sides, self.plane[stage], True)
            self.parts = link_call(body, self.here, self.parts, (self.shape,))

    def back(self):
        for stage in range(len(self.plane) - 1, -1, -1):
            self.up_plane(stage)
            if stage:
                self.swap_plane(stage - 1)
        return self.parts[0]

    def follow(self, other):
        self.parts, other.parts = lax.optimization_barrier((self.parts, other.parts))

    def after(self, *values):
        self.parts, values = lax.optimization_barrier((self.parts, values))
        return values

    def to_depth(self):
        for stage in range(2, len(self.plane)):
            self.swap_plane(stage - 1)
            self.down_plane(stage)
        self.swap_plane(len(self.plane) - 1)

    def scatter_depth(self):
        for stage in range(len(self.depth) - 1):
            if stage:
                self.down_depth(stage)
            self.swap_depth(stage)

    def swap_whole(self):
        self.parts = (self.parts[0], swap(self.parts[0], "dp", self.depth[-1]))

    def gather_depth(self):
        for stage in range(len(self.depth) - 2, 0, -1):
            self.swap_depth(stage)
            self.up_depth(stage)
        self.swap_depth(0)


def discretize(lam_re, lam_im, log_step):
    step_size = jnp.exp(log_step)
    decay_abs = jnp.exp(lam_re * step_size)
    rotation = lam_im * step_size
    dec_re = decay_abs * jnp.cos(rotation)
    dec_im = decay_abs * jnp.sin(rotation)
    denom_sq = lam_re * lam_re + lam_im * lam_im
    inj_re = ((dec_re - 1.0) * lam_re + dec_im * lam_im) / denom_sq
    inj_im = (dec_im * lam_re - (dec_re - 1.0) * lam_im) / denom_sq
    return (dec_re, dec_im, inj_re, inj_im)


def per_device(
    block_in, cotangent, doc_lengths, norm_gain, norm_shift, log_step, lam_re, lam_im,
    b_proj, c_proj, d_skip, w_gate,
):
    batches, seqs, span, width = block_in.shape
    assert seqs == 1 and span % (4 * CHUNKS) == 0 and span & (span - 1) == 0
    half = lam_re.shape[1]
    groups = half // LANES
    rows = batches * span
    count = lax.axis_size("seq")
    tokens = float(seqs * lax.axis_size("dp") * span * count)
    here = jnp.stack([lax.axis_index("seq"), lax.axis_index("dp")]).astype(jnp.int32)
    place = jnp.concatenate([here] + [doc_lengths[batch, 0] for batch in range(batches)])
    place, block_in = lax.optimization_barrier((place, block_in))
    here = place
    disc = discretize(lam_re, lam_im, log_step)

    x = block_in.reshape(rows, width)
    cot = cotangent.reshape(rows, width)
    lower = (0, False, batches, span, groups, tokens, count)
    upper = (1, True, batches, span, groups, tokens, count)
    part = functools.partial

    flat, low = ((rows, width), f32), ((rows, width), bf16)
    wide, wide_low = ((rows, 2 * half), f32), ((rows, 2 * half), bf16)
    padded = ((batches * (span + CHUNKS), 2 * half), f32)
    sums = ((2 * batches, width), f32)
    prefix = ((2, batches * CHUNKS, 2 * half), f32)
    total = ((batches, 2 * half), f32)
    line, shared = ((1, width), f32), ((2, width), f32)
    small = ((8, width), f32)

    def gather_row(value):
        return lax.all_gather(value, "seq")

    ordered, stats = run(
        part(first_sums, batches, span), "first_sums", (x,), (low, sums), scalars=0
    )
    norms = jnp.concatenate([norm_gain, norm_shift, d_skip], axis=0)

    def forward(cfg, hidden, stats):
        return run(
            part(enter_layer, cfg),
            "enter_layer",
            (place, stats, hidden, norms, disc, b_proj),
            (low, wide, prefix, total, sums),
        )

    links, plane, depth = axis_parts()
    u0, drive0, prefix0, total0, norm0 = forward(
        lower, ordered, add_by_shifts(stats, (links, plane, depth))[0]
    )
    states0, states_low0, act0, sig0, slope0, hidden1, stats = run(
        part(middle_forward, lower),
        "middle_forward",
        (place, gather_row(total0), prefix0, disc, drive0, u0, ordered, c_proj, norms, w_gate),
        (padded, wide_low, low, flat, flat, flat, sums),
        (flat,),
    )
    u1, drive1, prefix1, total1, norm1 = forward(
        upper, hidden1, add_by_shifts(stats, (links, plane, depth))[0]
    )
    (
        block_out, ordered_cot, states1, states_low1, act1, grad_gate1, grad_mixed1, grad_low1,
        source1, prefix1, total1, grad_d1,
    ) = run(
        part(turn_around, upper),
        "turn_around",
        (
            place, gather_row(total1), prefix1, disc, drive1, u1, hidden1, c_proj, norms, w_gate,
            cot,
        ),
        (low, low, padded, wide_low, low, low, flat, low, wide, prefix, total, line),
        (flat, flat, flat, low),
    )

    def halves(length):
        return (((length // 2, width), f32),) * 2

    grad_proj1, grad_u1, stats, small1 = run(
        part(backward_finish, upper),
        "backward_finish",
        (
            place, gather_row(total1), prefix1, disc, source1, drive1, states1, u1, grad_mixed1,
            grad_d1, hidden1, norm1, norms, b_proj,
        ),
        (wide_low, flat, sums, small),
    )
    sizes = (width + 2 * half, 2 * half)
    own1, sent1 = run(
        all_weights,
        "all_weights",
        (here, act1, grad_gate1, states_low1, grad_low1, grad_proj1, u1),
        halves(sum(sizes)),
    )
    upper_sum = LinkSum(here, (own1, swap(sent1, "seq", 1)))
    stats, upper_sum.parts = add_by_shifts(stats, (links, plane, depth), upper_sum.parts)
    upper_sum.swap_plane(0)
    (
        grad_out0, shared1, grad_gate0, grad_mixed0, grad_low0, source0, prefix0, total0, grad_d0,
    ) = run(
        part(between_layers, upper, lower),
        "between_layers",
        (
            place, stats, ordered_cot, grad_u1, hidden1, norm1, norms,
            disc, u0, c_proj, w_gate, states_low0, act0, sig0, slope0,
        ),
        (flat, shared, low, flat, low, wide, prefix, total, line),
        (flat,),
    )
    (grad_gate0,) = upper_sum.after(grad_gate0)
    upper_sum.down_plane(1)
    upper_sum.to_depth()
    own_gates, sent_gates = run(
        gate_weights, "gate_weights", (here, act0, grad_gate0, states_low0, grad_low0),
        halves(sizes[0]),
    )
    found_gates = swap(sent_gates, "seq", 1)
    own_gates, total0 = lax.optimization_barrier((own_gates, total0))
    found_gates, ends = lax.optimization_barrier((found_gates, gather_row(total0)))
    (ends,) = upper_sum.after(ends)
    upper_sum.down_join()
    upper_sum.parts, ends = lax.optimization_barrier((upper_sum.parts, ends))
    upper_sum.scatter_depth()
    grad_proj0, grad_u0, last_sums = run(
        part(backward_finish_last, lower),
        "backward_finish",
        (
            place, ends, prefix0, disc, source0, drive0, states0, u0, grad_mixed0, grad_d0,
            ordered, norm0, norms, b_proj, small1,
        ),
        (wide_low, flat, ((3 * CHUNKS, width), f32)),
    )
    own_inputs, sent_inputs = run(
        input_weights, "input_weights", (here, grad_proj0, u0), halves(sizes[1])
    )
    found_inputs = swap(sent_inputs, "seq", 1)
    upper_sum.middle()
    upper_sum.parts, found_inputs = lax.optimization_barrier((upper_sum.parts, found_inputs))
    upper_sum.swap_whole()
    lower_sum = LinkSum(here, (own_gates, found_gates, own_inputs, found_inputs))
    (last_sums,) = lower_sum.after(last_sums)
    lower_sum.swap_plane(0)
    lower_sum.down_plane(1)
    lower_sum.to_depth()
    lower_sum.down_join()
    upper_sum.follow(lower_sum)
    upper_sum.middle()
    upper_sum.gather_depth()
    summed, lower_sum.parts = add_by_shifts(last_sums, (depth, links, plane), lower_sum.parts)
    summed = sum(summed)
    final = (((2, width, width), f32), ((2, 2 * half, width), f32), ((2, width, 2 * half), f32))
    lower_sum.scatter_depth()
    lower_sum.middle()
    upper_sum.follow(lower_sum)
    upper_sum.up_split()
    (summed,) = upper_sum.after(summed)
    upper_sum.swap_plane(len(upper_sum.plane) - 1)
    lower_sum.swap_whole()
    lower_sum.middle()
    upper_sum.follow(lower_sum)
    lower_sum.gather_depth()
    lower_sum.up_split()
    own1 = upper_sum.back()
    own1, lower_sum.parts = lax.optimization_barrier((own1, lower_sum.parts))
    other1 = swap(own1, "seq", 1)
    grad_input, shared0 = run(
        part(last_step, lower),
        "last_step",
        ((summed[: 2 * batches],), grad_out0, grad_u0, ordered, norm0, norms),
        (flat, shared),
        (((width // LANES, rows, LANES), f32),),
        scalars=0,
    )
    small_sum = summed[CHUNKS:].reshape(2, CHUNKS, width)
    _, pullback = jax.vjp(discretize, lam_re, lam_im, log_step)
    grad_lr, grad_li, grad_ls = pullback(tuple(small_sum[:, kind, :half] for kind in range(4)))
    lower_sum.swap_plane(len(lower_sum.plane) - 1)
    placed = put_in_place(1, here, ((False, own1), (True, other1)), final, ())
    grad_input, grad_lr, grad_li, grad_ls, *placed = lower_sum.after(
        grad_input, grad_lr, grad_li, grad_ls, *placed
    )
    own0 = lower_sum.back()
    other0 = swap(own0, "seq", 1)
    placed = put_in_place(0, here, ((False, own0),), final, placed)
    grad_w, grad_c, grad_b = put_in_place(0, here, ((True, other0),), final, placed)
    both = jnp.stack([shared0, shared1])
    shape = block_in.shape
    return (
        block_out.reshape(shape), grad_input.reshape(shape), both[:, 0], both[:, 1],
        grad_ls, grad_lr, grad_li, grad_b, grad_c, small_sum[:, 4], grad_w,
    )


def solution(mesh):
    split = P(None, "dp", "seq", None)
    return jax.shard_map(
        per_device,
        mesh=mesh,
        in_specs=(split, split, P(None, "dp", None)) + (P(),) * 9,
        out_specs=(split, split) + (P(),) * 9,
        check_vma=False,
    )
```

```python
import functools

import jax
import jax.numpy as jnp
from jax import lax
from jax.experimental import pallas as pl
from jax.experimental.pallas import tpu as pltpu
from jax.sharding import PartitionSpec as P

f32, bf16 = jnp.float32, jnp.bfloat16
epsilon = 1e-05
tanh_scale = 0.7978845608028654
cubic_term = 0.044715
LANES = 128
CHUNKS = 8
ROWS = 32
VMEM_LIMIT = 16 * 1024 * 1024


def dot(left, right, contract=(1, 0)):
    return lax.dot_general(
        left, right, (((contract[0],), (contract[1],)), ((), ())), preferred_element_type=f32
    )


def reorder(span, inverse):
    shape = (span, span)
    kept, moved = (1, 0) if inverse else (0, 1)
    row = lax.broadcasted_iota(jnp.int32, shape, kept)
    position = lax.broadcasted_iota(jnp.int32, shape, moved)
    source = (row & (CHUNKS - 1)) * (span // CHUNKS) + (row >> 3)
    return jnp.where(position == source, 1.0, 0.0).astype(bf16)


def row_loop(count, body, init=0, step=ROWS):
    def one(index, carry):
        return body(pl.multiple_of(index * step, step), carry)

    return lax.fori_loop(0, count // step, one, init)


def documents(here, batches, span, count):
    mine = here[0]
    first = mine * span
    out = []
    for batch in range(batches):
        begins, ends, so_far = [], [], 0
        docs = (here.shape[0] - 2) // batches
        for doc in range(docs):
            begins.append(so_far)
            so_far = so_far + here[2 + batch * docs + doc]
            ends.append(so_far)
        before, after = 0, 2 * count * span
        for begin, end in zip(begins, ends):
            before = jnp.maximum(before, jnp.where(begin < first, begin, 0))
            after = jnp.minimum(after, jnp.where(end > first + span, end, 2 * count * span))
        after = jnp.where(mine == count - 1, 0, after)
        out.append(begins + ends + [before, after, first, mine])
    return out


def place_documents(cfg, place):
    layer, reverse, batches, span, groups, tokens, count = cfg
    return documents(place, batches, span, count)


def keep_of(meta, batch, base, step, backward):
    docs = (len(meta[batch]) - 4) // 2
    off = docs if backward else 0
    late = 1 if backward else 0
    stop = base == meta[batch][off] - step - late
    for doc in range(1, docs):
        stop = jnp.logical_or(stop, base == meta[batch][off + doc] - step - late)
    return jnp.where(stop, 0.0, 1.0)


def base_positions(meta, steps):
    return meta[0][-2] + lax.broadcasted_iota(jnp.int32, (CHUNKS, LANES), 0) * steps


def lanes_of(index, half=0):
    return slice(half + index * LANES, half + (index + 1) * LANES)


def coef_tiles(value, groups):
    return [
        tuple(jnp.broadcast_to(part[:, lanes_of(q)], (CHUNKS, LANES)) for part in value)
        for q in range(groups)
    ]


def constants(disc, layer):
    dec_re, dec_im, inj_re, inj_im = (part[layer : layer + 1, :] for part in disc)
    return (dec_re, dec_im), (inj_re, inj_im)


def times(a, b):
    return (a[0] * b[0] - a[1] * b[1], a[0] * b[1] + a[1] * b[0])


def power(value, exponent):
    for _ in range(exponent.bit_length() - 1):
        value = times(value, value)
    return value


def conj(value):
    return (value[0], -value[1])


def scan(meta, source, inject, dec, batches, span, groups, reverse, masks_reverse, init, extra, visit):
    steps = span // CHUNKS
    half = groups * LANES
    base = base_positions(meta, steps)

    def pair(index, carry):
        states, more = carry
        states = list(states)
        first = steps - 2 - 2 * index if reverse else 2 * index
        start = pl.multiple_of(first * CHUNKS, 2 * CHUNKS)
        order = (1, 0) if reverse else (0, 1)
        for batch in range(batches):
            keeps = [keep_of(meta, batch, base, first + j, masks_reverse) for j in (0, 1)]
            for q in range(groups):
                rows = pl.ds(batch * span + start, 2 * CHUNKS)
                src_re = source[rows, lanes_of(q)]
                src_im = source[rows, lanes_of(q, half)]
                state = states[batch * groups + q]
                found = [None, None]
                for j in order:
                    part = (
                        src_re[j * CHUNKS : (j + 1) * CHUNKS],
                        src_im[j * CHUNKS : (j + 1) * CHUNKS],
                    )
                    push = times(inject[q], part) if inject is not None else part
                    held = times((keeps[j] * dec[q][0], keeps[j] * dec[q][1]), state)
                    state = (held[0] + push[0], held[1] + push[1])
                    found[j] = state
                states[batch * groups + q] = state
                more = visit(more, batch, q, first, start, found, (src_re, src_im))
            more = visit(more, batch, None, first, start, keeps, None)
        return tuple(states), more

    return lax.fori_loop(0, steps // 2, pair, (tuple(init), extra), unroll=2)


def zero_states(batches, groups):
    zero = jnp.zeros((CHUNKS, LANES), f32)
    return [(zero, zero)] * (batches * groups)


def local_ends(meta, source, inject, dec, batches, span, groups, reverse, prefix, total):
    ones = tuple(jnp.ones((CHUNKS, LANES), f32) for _ in range(batches))

    def visit(more, batch, q, first, start, found, src):
        if q is not None:
            return more
        return tuple(
            value * found[0] * found[1] if at == batch else value for at, value in enumerate(more)
        )

    dec_chunk = coef_tiles(power(dec, span // CHUNKS), groups)
    ends, kept = scan(
        meta, source, inject, coef_tiles(dec, groups), batches, span, groups, reverse, reverse,
        zero_states(batches, groups), ones, visit,
    )
    half = groups * LANES
    row = lax.broadcasted_iota(jnp.int32, (CHUNKS, LANES), 0)
    for batch in range(batches):
        for q in range(groups):
            end = ends[batch * groups + q]
            decay = (kept[batch] * dec_chunk[q][0], kept[batch] * dec_chunk[q][1])
            for shift in (1, 2, 4):
                turn = CHUNKS - shift if reverse else shift
                valid = row < CHUNKS - shift if reverse else row >= shift
                before = [pltpu.roll(value, turn, 0) for value in (*end, *decay)]
                from_before = times(decay, (before[0], before[1]))
                end = (
                    end[0] + jnp.where(valid, from_before[0], 0.0),
                    end[1] + jnp.where(valid, from_before[1], 0.0),
                )
                longer = times(decay, (before[2], before[3]))
                decay = (
                    jnp.where(valid, longer[0], decay[0]),
                    jnp.where(valid, longer[1], decay[1]),
                )
            rows = slice(batch * CHUNKS, (batch + 1) * CHUNKS)
            prefix[0, rows, lanes_of(q)] = end[0]
            prefix[0, rows, lanes_of(q, half)] = end[1]
            prefix[1, rows, lanes_of(q)] = decay[0]
            prefix[1, rows, lanes_of(q, half)] = decay[1]
            last = 0 if reverse else CHUNKS - 1
            total[batch : batch + 1, lanes_of(q)] = end[0][last : last + 1]
            total[batch : batch + 1, lanes_of(q, half)] = end[1][last : last + 1]


def chunk_carries(meta, gathered, dec, prefix, batches, span, groups, reverse):
    count = gathered.shape[0]
    half = groups * LANES
    dec_span = power(dec, span)
    row = lax.broadcasted_iota(jnp.int32, (CHUNKS, LANES), 0)
    mine = meta[0][-1]
    out = []
    for batch in range(batches):

        def add(at, so_far, batch=batch):
            away = count - 2 - at
            if reverse:
                other = mine + 1 + away
                reaches = meta[batch][-3] > other * span
            else:
                other = mine - 1 - away
                reaches = meta[batch][-4] < (mine - away) * span
            other = jnp.clip(other, 0, count - 1)
            value = jnp.where(reaches, gathered[other, pl.ds(batch, 1), :], 0.0)
            moved = times(dec_span, so_far)
            return (moved[0] + value[:, :half], moved[1] + value[:, half:])

        zero = jnp.zeros((1, half), f32)
        enter = lax.fori_loop(0, count - 1, add, (zero, zero), unroll=count <= 8)
        rows = slice(batch * CHUNKS, (batch + 1) * CHUNKS)
        for q in range(groups):
            own = tuple(jnp.broadcast_to(part[:, lanes_of(q)], (CHUNKS, LANES)) for part in enter)
            end = (prefix[0, rows, lanes_of(q)], prefix[0, rows, lanes_of(q, half)])
            decay = (prefix[1, rows, lanes_of(q)], prefix[1, rows, lanes_of(q, half)])
            moved = times(decay, own)
            turn, first = (CHUNKS - 1, CHUNKS - 1) if reverse else (1, 0)
            out.append(
                tuple(
                    jnp.where(row == first, own[i], pltpu.roll(end[i] + moved[i], turn, 0))
                    for i in (0, 1)
                )
            )
    return out


def add_sums(target, batches, sums):
    for kind, per_batch in enumerate(sums):
        for batch in range(batches):
            target[kind * batches + batch : kind * batches + batch + 1, :] = jnp.sum(
                per_batch[batch], axis=0, keepdims=True
            )


def fold(value):
    return sum(value[i : i + CHUNKS] for i in range(CHUNKS, value.shape[0], CHUNKS)) + value[:CHUNKS]


def first_sums(batches, span, x, ordered, stats):
    turn = reorder(span, False)
    width = x.shape[1]
    sums, squares = [], []
    for batch in range(batches):
        rows = slice(batch * span, (batch + 1) * span)
        ordered[rows, :] = dot(turn, x[rows, :]).astype(bf16)

        def body(start, carry, batch=batch):
            value = x[pl.ds(batch * span + start, ROWS), :].astype(f32)
            return carry[0] + fold(value), carry[1] + fold(value * value)

        zero = jnp.zeros((CHUNKS, width), f32)
        one, two = row_loop(span, body, (zero, zero))
        sums.append(one)
        squares.append(two)
    add_sums(stats, batches, (sums, squares))


def enter_layer(
    cfg, place, stats, hidden, norms, disc, b_proj, u, drive, prefix, total, norm
):
    layer, reverse, batches, span, groups, tokens, count = cfg
    sums = sum(part[...] for part in stats)
    average = sums[:batches] / tokens
    spread = sums[batches:] / tokens - average * average
    scale = lax.rsqrt(spread + epsilon)
    norm[:batches, :] = average
    norm[batches:, :] = scale
    gain_now, shift_now = norms[layer : layer + 1, :], norms[layer + 2 : layer + 3, :]
    for batch in range(batches):

        def body(start, carry, batch=batch):
            rows = pl.ds(batch * span + start, ROWS)
            normed = (hidden[rows, :].astype(f32) - average[batch : batch + 1]) * scale[
                batch : batch + 1
            ]
            u[rows, :] = (normed * gain_now + shift_now).astype(bf16)
            return carry

        row_loop(span, body)
    drive[...] = dot(u[...], b_proj[layer])
    meta = place_documents(cfg, place)
    dec, inj = constants(disc, layer)
    local_ends(
        meta, drive, coef_tiles(inj, groups), dec, batches, span, groups, reverse, prefix, total
    )


def finish_states(cfg, meta, ends, prefix, disc, drive, states, states_low):
    layer, reverse, batches, span, groups, tokens, count = cfg
    half = groups * LANES
    padded = span + CHUNKS
    dec, inj = constants(disc, layer)
    init = chunk_carries(meta, ends, dec, prefix, batches, span, groups, reverse)
    for batch in range(batches):
        edge = batch * padded + (span if reverse else 0)
        for q in range(groups):
            states[edge : edge + CHUNKS, lanes_of(q)] = init[batch * groups + q][0]
            states[edge : edge + CHUNKS, lanes_of(q, half)] = init[batch * groups + q][1]

    def visit(more, batch, q, first, start, found, src):
        if q is not None:
            for part, off in ((0, 0), (1, half)):
                both = jnp.concatenate([found[0][part], found[1][part]], axis=0)
                at = batch * padded + (0 if reverse else CHUNKS)
                states[pl.ds(at + start, 2 * CHUNKS), lanes_of(q, off)] = both
                states_low[pl.ds(batch * span + start, 2 * CHUNKS), lanes_of(q, off)] = both.astype(
                    bf16
                )
        return more

    scan(
        meta, drive, coef_tiles(inj, groups), coef_tiles(dec, groups), batches, span, groups,
        reverse, reverse, init, 0, visit,
    )


def forward_finish(
    cfg, meta, ends, prefix, disc, drive, u, hidden, c_proj, norms, w_gate,
    states, states_low, act, sig, slope, result, wide, emit,
):
    layer, reverse, batches, span, groups, tokens, count = cfg
    finish_states(cfg, meta, ends, prefix, disc, drive, states, states_low)
    wide[...] = dot(states_low[...], c_proj[layer])
    skip = norms[layer + 4 : layer + 5, :]

    def body(start, carry):
        rows = pl.ds(start, ROWS)
        mixed = wide[rows, :] + skip * u[rows, :].astype(f32)
        square = mixed * mixed
        th = jnp.tanh(tanh_scale * (mixed + cubic_term * square * mixed))
        half_one = 0.5 * (1.0 + th)
        act[rows, :] = (mixed * half_one).astype(bf16)
        slope[rows, :] = half_one + 0.5 * mixed * (1.0 - th * th) * tanh_scale * (
            1.0 + 3.0 * cubic_term * square
        )
        return carry

    row_loop(batches * span, body)
    wide[...] = dot(act[...], w_gate[layer])
    sums, squares = [], []
    for batch in range(batches):

        def gate(start, carry, batch=batch):
            rows = pl.ds(batch * span + start, ROWS)
            sig_now = 0.5 + 0.5 * jnp.tanh(0.5 * wide[rows, :])
            sig[rows, :] = sig_now
            value = hidden[rows, :].astype(f32) + act[rows, :].astype(f32) * sig_now
            result[rows, :] = value.astype(result.dtype)
            if emit is None:
                return carry
            return carry[0] + fold(value), carry[1] + fold(value * value)

        zero = jnp.zeros((CHUNKS, wide.shape[1]), f32)
        one, two = row_loop(span, gate, (zero, zero))
        sums.append(one)
        squares.append(two)
    if emit is not None:
        add_sums(emit, batches, (sums, squares))


def backward_start(
    cfg, meta, grad_out, disc, u, c_proj, w_gate, states_low, act, sig, slope,
    grad_gate, grad_mixed, grad_low, source, prefix, total, grad_d, wide,
):
    layer, reverse, batches, span, groups, tokens, count = cfg

    def body(start, carry):
        rows = pl.ds(start, ROWS)
        sig_now = sig[rows, :]
        grad_gate[rows, :] = (
            grad_out[rows, :].astype(f32) * act[rows, :].astype(f32) * sig_now * (1.0 - sig_now)
        ).astype(bf16)
        return carry

    row_loop(batches * span, body)
    wide[...] = dot(grad_gate[...], w_gate[layer], (1, 1))

    def mixed(start, carry):
        rows = pl.ds(start, ROWS)
        value = (grad_out[rows, :].astype(f32) * sig[rows, :] + wide[rows, :]) * slope[rows, :]
        grad_mixed[rows, :] = value
        grad_low[rows, :] = value.astype(bf16)
        return carry + fold(value * u[rows, :].astype(f32))

    gd = row_loop(batches * span, mixed, jnp.zeros((CHUNKS, wide.shape[1]), f32))
    grad_d[...] = jnp.sum(gd, axis=0, keepdims=True)
    source[...] = dot(grad_low[...], c_proj[layer], (1, 1))
    local_ends(
        meta, source, None, conj(constants(disc, layer)[0]), batches, span, groups, not reverse,
        prefix, total,
    )


def middle_forward(
    cfg, place, ends, prefix, disc, drive, u, hidden, c_proj, norms, w_gate,
    states, states_low, act, sig, slope, result, stats, wide,
):
    meta = place_documents(cfg, place)
    forward_finish(
        cfg, meta, ends, prefix, disc, drive, u, hidden, c_proj, norms, w_gate,
        states, states_low, act, sig, slope, result, wide, stats,
    )


def turn_around(
    cfg, place, ends, prefix, disc, drive, u, hidden, c_proj, norms, w_gate, cotangent,
    block_out, ordered_cot, states, states_low, act, grad_gate, grad_mixed, grad_low, source,
    back_prefix, total, grad_d, sig, slope, wide, result,
):
    layer, reverse, batches, span, groups, tokens, count = cfg
    meta = place_documents(cfg, place)
    turn, back = reorder(span, False), reorder(span, True)
    for batch in range(batches):
        rows = slice(batch * span, (batch + 1) * span)
        ordered_cot[rows, :] = dot(turn, cotangent[rows, :]).astype(bf16)
    forward_finish(
        cfg, meta, ends, prefix, disc, drive, u, hidden, c_proj, norms, w_gate,
        states, states_low, act, sig, slope, result, wide, None,
    )
    for batch in range(batches):
        rows = slice(batch * span, (batch + 1) * span)
        block_out[rows, :] = dot(back, result[rows, :]).astype(bf16)
    backward_start(
        cfg, meta, ordered_cot, disc, u, c_proj, w_gate, states_low, act, sig, slope,
        grad_gate, grad_mixed, grad_low, source, back_prefix, total, grad_d, wide,
    )


def backward_finish(
    cfg, place, ends, prefix, disc, source, drive, states, u, grad_mixed, grad_d, hidden, norm,
    norms, b_proj, grad_proj, grad_u, stats, small,
):
    layer, reverse, batches, span, groups, tokens, count = cfg
    half = groups * LANES
    padded = span + CHUNKS
    steps = span // CHUNKS
    meta = place_documents(cfg, place)
    dec, inj = constants(disc, layer)
    dec = conj(dec)
    init = chunk_carries(meta, ends, dec, prefix, batches, span, groups, not reverse)
    inj = coef_tiles(inj, groups)
    base = base_positions(meta, steps)
    zero = jnp.zeros((CHUNKS, LANES), f32)

    def visit(more, batch, q, first, start, found, src):
        if q is None:
            return more
        more = list(more)
        rows = pl.ds(batch * span + start, 2 * CHUNKS)
        drive_re, drive_im = drive[rows, lanes_of(q)], drive[rows, lanes_of(q, half)]
        before = pl.ds(batch * padded + start + (CHUNKS if reverse else 0), 2 * CHUNKS)
        prior_re, prior_im = states[before, lanes_of(q)], states[before, lanes_of(q, half)]
        dec_re, dec_im, inj_re, inj_im = more[q]
        out_re, out_im = [], []
        for j in (0, 1):
            part = slice(j * CHUNKS, (j + 1) * CHUNKS)
            adj_re, adj_im = found[j]
            keep = keep_of(meta, batch, base, first + j, reverse)
            kept_re, kept_im = keep * adj_re, keep * adj_im
            dec_re = dec_re + kept_re * prior_re[part] + kept_im * prior_im[part]
            dec_im = dec_im + kept_im * prior_re[part] - kept_re * prior_im[part]
            inj_re = inj_re + adj_re * drive_re[part] + adj_im * drive_im[part]
            inj_im = inj_im + adj_im * drive_re[part] - adj_re * drive_im[part]
            out_re.append(inj[q][0] * adj_re + inj[q][1] * adj_im)
            out_im.append(inj[q][0] * adj_im - inj[q][1] * adj_re)
        grad_proj[rows, lanes_of(q)] = jnp.concatenate(out_re, axis=0).astype(bf16)
        grad_proj[rows, lanes_of(q, half)] = jnp.concatenate(out_im, axis=0).astype(bf16)
        more[q] = (dec_re, dec_im, inj_re, inj_im)
        return tuple(more)

    _, sums = scan(
        meta, source, None, coef_tiles(dec, groups), batches, span, groups,
        not reverse, not reverse, init, ((zero,) * 4,) * groups, visit,
    )
    small[...] = jnp.zeros_like(small)
    for q in range(groups):
        for kind in range(4):
            small[kind : kind + 1, lanes_of(q)] = jnp.sum(sums[q][kind], axis=0, keepdims=True)
    small[4:5, :] = grad_d[...]
    grad_u[...] = dot(grad_proj[...], b_proj[layer], (1, 1))
    skip = norms[layer + 4 : layer + 5, :]
    plain, times_normed = [], []
    for batch in range(batches):
        average = norm[batch : batch + 1, :]
        scale = norm[batches + batch : batches + batch + 1, :]

        def body(start, carry, batch=batch, average=average, scale=scale):
            rows = pl.ds(batch * span + start, ROWS)
            value = grad_u[rows, :] + grad_mixed[rows, :] * skip
            grad_u[rows, :] = value
            normed = (hidden[rows, :].astype(f32) - average) * scale
            return carry[0] + fold(value), carry[1] + fold(value * normed)

        zero_sum = jnp.zeros((CHUNKS, grad_u.shape[1]), f32)
        one, two = row_loop(span, body, (zero_sum, zero_sum))
        plain.append(one)
        times_normed.append(two)
    add_sums(stats, batches, (plain, times_normed))


def backward_finish_last(cfg, *refs):
    ins, before, (grad_proj, grad_u, sums) = refs[:-4], refs[-4], refs[-3:]
    sums[...] = jnp.zeros_like(sums)
    sums[2 * CHUNKS :, :] = before[...]
    backward_finish(
        cfg, *ins, grad_proj, grad_u, sums.at[pl.ds(0, CHUNKS)], sums.at[pl.ds(CHUNKS, CHUNKS)]
    )


def norm_backward(cfg, stats, grad_out, grad_u, hidden, norm, norms, store, shared):
    layer, reverse, batches, span, groups, tokens, count = cfg
    sums = sum(part[...] for part in stats)
    shared[0:1, :] = jnp.sum(sums[batches:], axis=0, keepdims=True)
    shared[1:2, :] = jnp.sum(sums[:batches], axis=0, keepdims=True)
    gain_now = norms[layer : layer + 1, :]
    for batch in range(batches):
        average = norm[batch : batch + 1, :]
        scale = norm[batches + batch : batches + batch + 1, :]
        plain = gain_now * sums[batch : batch + 1] / tokens
        slanted = gain_now * sums[batches + batch : batches + batch + 1] / tokens

        def body(start, carry, batch=batch, average=average, scale=scale, plain=plain, slanted=slanted):
            rows = pl.ds(batch * span + start, ROWS)
            normed = (hidden[rows, :].astype(f32) - average) * scale
            value = grad_out[rows, :].astype(f32) + scale * (
                grad_u[rows, :] * gain_now - plain - normed * slanted
            )
            store(rows, value)
            return carry

        row_loop(span, body)


def between_layers(
    cfg, lower, place, stats, upper_out, upper_u, upper_hidden, upper_norm, norms,
    disc, u, c_proj, w_gate, states_low, act, sig, slope,
    grad_out, shared, grad_gate, grad_mixed, grad_low, source, prefix, total, grad_d, wide,
):
    def store(rows, value):
        grad_out[rows, :] = value

    norm_backward(cfg, stats, upper_out, upper_u, upper_hidden, upper_norm, norms, store, shared)
    meta = place_documents(lower, place)
    backward_start(
        lower, meta, grad_out, disc, u, c_proj, w_gate, states_low, act, sig, slope,
        grad_gate, grad_mixed, grad_low, source, prefix, total, grad_d, wide,
    )


def last_step(cfg, stats, grad_out, grad_u, hidden, norm, norms, target, shared, ordered):
    layer, reverse, batches, span, groups, tokens, count = cfg
    planes = target.shape[1] // LANES

    def store(rows, value):
        for plane in range(planes):
            ordered[plane, rows, :] = value[:, lanes_of(plane)]

    norm_backward(cfg, stats, grad_out, grad_u, hidden, norm, norms, store, shared)
    steps = span // CHUNKS
    for batch in range(batches):
        for chunk in range(CHUNKS):
            at = batch * span
            for plane in range(planes):
                target[at + chunk * steps : at + (chunk + 1) * steps, lanes_of(plane)] = ordered[
                    plane, pl.ds(at + chunk, steps, stride=CHUNKS), :
                ]


def half_weights(core, refs, own, sent):
    for target, half in ((own, core), (sent, 1 - core)):
        at = 0
        for left, right in refs:
            rows = left.shape[1] // 2
            cols = pl.ds(pl.multiple_of(half * rows, LANES), rows)
            target[at : at + rows, :] = dot(left[:, cols], right[...], (0, 0))
            at += rows


def all_weights(here, act, grad_gate, states_low, grad_low, grad_proj, u, own, sent):
    refs = ((act, grad_gate), (states_low, grad_low), (grad_proj, u))
    half_weights(lax.rem(here[0], 2), refs, own, sent)


def gate_weights(here, act, grad_gate, states_low, grad_low, own, sent):
    half_weights(lax.rem(here[0], 2), ((act, grad_gate), (states_low, grad_low)), own, sent)


def input_weights(here, grad_proj, u, own, sent):
    half_weights(lax.rem(here[0], 2), ((grad_proj, u),), own, sent)


def run(body, name, args, outs, scratch=(), scalars=1):
    vmem, smem = pl.BlockSpec(memory_space=pltpu.VMEM), pl.BlockSpec(memory_space=pltpu.SMEM)
    specs = tuple(
        jax.tree.map(lambda _, at=at: smem if at < scalars else vmem, arg)
        for at, arg in enumerate(args)
    )
    return pl.pallas_call(
        body,
        name=name,
        out_shape=tuple(jax.ShapeDtypeStruct(*out) for out in outs),
        in_specs=specs,
        out_specs=(vmem,) * len(outs),
        scratch_shapes=[pltpu.VMEM(*entry) for entry in scratch],
        compiler_params=pltpu.CompilerParams(vmem_limit_bytes=VMEM_LIMIT),
    )(*args)


def put_in_place(layer, here, halves, outs, before, pieces=1):
    width, states = outs[0][0][1], outs[1][0][1]
    rows_w, rows_c = width // 2, states // 2
    vmem, count = pl.BlockSpec(memory_space=pltpu.VMEM), len(halves)

    def half(step, here):
        core = lax.rem(here[0], 2)
        spots = [1 - core if other else core for other, _ in halves]
        return spots[0] if count == 1 else jnp.where(step == 0, *spots)

    blocks = (
        pl.BlockSpec((1, rows_w, width), lambda i, here: (layer, half(i, here), 0)),
        pl.BlockSpec((1, rows_c, width), lambda i, here: (layer, half(i, here), 0)),
        pl.BlockSpec((1, width, rows_c), lambda i, here: (layer, 0, half(i, here))),
    )

    def body(here, *refs):
        grad_w, grad_c, grad_b = refs[-3:]
        for now in range(count):

            @pl.when(pl.program_id(0) == now)
            def _(source=refs[now]):
                gates, inputs = (rows_w + rows_c) // pieces, rows_c // pieces
                columns = []
                for piece in range(pieces):
                    at, row = piece * (gates + inputs), piece * gates
                    turn = min(max(rows_w - row, 0), gates)
                    if turn:
                        grad_w[0, row : row + turn, :] = source[at : at + turn, :]
                    if turn < gates:
                        to = row + turn - rows_w
                        grad_c[0, to : to + gates - turn, :] = source[at + turn : at + gates, :]
                    columns.append(source[at + gates : at + gates + inputs, :])
                grad_b[0] = jnp.concatenate(columns, axis=0).T

    return pl.pallas_call(
        body,
        name="put_in_place",
        out_shape=tuple(jax.ShapeDtypeStruct(*out) for out in outs),
        grid_spec=pltpu.PrefetchScalarGridSpec(
            num_scalar_prefetch=1,
            grid=(count,),
            in_specs=[vmem] * count + [pl.BlockSpec(memory_space=pl.ANY)] * len(before),
            out_specs=blocks,
        ),
        input_output_aliases={1 + count + i: i for i in range(len(before))},
        compiler_params=pltpu.CompilerParams(vmem_limit_bytes=VMEM_LIMIT),
    )(here, *(rows for _, rows in halves), *before)


def axis_parts():
    count, depth = lax.axis_size("seq"), lax.axis_size("dp")
    return (("seq", 2, 1, count), ("seq", count // 2, 2, count), ("dp", depth, 1, depth))


def shifted(value, part, away):
    name, size, stride, count = part
    pairs = []
    for i in range(count):
        place = (i // stride) % size
        pairs.append((i, i + ((place + away) % size - place) * stride))
    return lax.ppermute(value, name, pairs)


def add_by_shifts(value, parts, *earlier):
    for number, part in enumerate(parts):
        if number:
            value = sum(terms[1:], terms[0])
        if number == len(parts) - 1:
            value, *earlier = lax.optimization_barrier((value, *earlier))
        terms = [value] + [shifted(value, part, away) for away in range(1, part[1])]
    return terms, *earlier


def bits_of(size, stride=1):
    bits = []
    while size > 1:
        bits.append(stride)
        size, stride = size // 2, stride * 2
    return bits


def plane_bits():
    chip_bits = bits_of(lax.axis_size("seq") // 2, 2)
    middle = (len(chip_bits) + 1) // 2
    inner, outer = chip_bits[:middle], chip_bits[middle:]
    return list(zip(inner + outer, outer + inner))


def swap(value, axis, bit):
    return lax.ppermute(value, axis, [(i, i ^ bit) for i in range(lax.axis_size(axis))])


def bit_at(here, axis, bit):
    return lax.rem(lax.div(here[0 if axis == "seq" else 1], bit), 2)


def rows_at(half, rows):
    return pl.ds(pl.multiple_of(half * rows, CHUNKS), rows)


def fold_cores(bits, here, *refs):
    terms, targets = refs[:-4], refs[-4:]
    rows, cols = targets[0].shape
    for side in (0, 1):
        kept, sent = targets[2 * side : 2 * side + 2]
        where = slice(side * cols, (side + 1) * cols)
        bit = bit_at(here, "seq", bits[side])
        for half in (0, 1):

            @pl.when(bit == half)
            def _(half=half, kept=kept, sent=sent, where=where):
                start = 0
                for own, found in zip(terms[0::2], terms[1::2]):
                    for part, target in ((half, kept), (1 - half, sent)):
                        low = max(start, part * rows)
                        high = min(start + own.shape[0], (part + 1) * rows)
                        if low < high:
                            source = slice(low - start, high - start)
                            target[low - part * rows : high - part * rows, :] = (
                                own[source, where] + found[source, where]
                            )
                    start += own.shape[0]


def fold_sides(bits, here, *refs):
    targets, blocks = refs[-4:], refs[:-4]
    for side in (0, 1):
        kept, sent = targets[2 * side : 2 * side + 2]
        half, start = bit_at(here, "seq", bits[side]), 0
        for at in range(0, len(blocks), 4):
            own, found = blocks[at + 2 * side : at + 2 * side + 2]
            rows = own.shape[0] // 2
            to = slice(start, start + rows)
            kept[to, :] = own[rows_at(half, rows), :] + found[rows_at(half, rows), :]
            sent[to, :] = own[rows_at(1 - half, rows), :] + found[rows_at(1 - half, rows), :]
            start += rows


def fold_join(bit, here, left, found_left, right, found_right, kept, sent):
    rows, cols = kept.shape[0], left.shape[1]
    half = bit_at(here, "dp", bit)
    for side, (own, found) in enumerate(((left, found_left), (right, found_right))):
        where = slice(side * cols, (side + 1) * cols)
        kept[:, where] = own[rows_at(half, rows), :] + found[rows_at(half, rows), :]
        sent[:, where] = own[rows_at(1 - half, rows), :] + found[rows_at(1 - half, rows), :]


def fold_depth(bit, here, own, found, kept, sent):
    half, rows = bit_at(here, "dp", bit), kept.shape[0]
    kept[...] = own[rows_at(half, rows), :] + found[rows_at(half, rows), :]
    sent[...] = own[rows_at(1 - half, rows), :] + found[rows_at(1 - half, rows), :]


def add_two(own, found, out):
    out[...] = own[...] + found[...]


def unfold(bit, here, own, found, out):
    half, rows = bit_at(here, "dp", bit), own.shape[0]
    out[rows_at(half, rows), :] = own[...]
    out[rows_at(1 - half, rows), :] = found[...]


def unfold_split(bit, here, own, found, left, right):
    half, rows, cols = bit_at(here, "dp", bit), own.shape[0], left.shape[1]
    for side, out in enumerate((left, right)):
        where = slice(side * cols, (side + 1) * cols)
        out[rows_at(half, rows), :] = own[:, where]
        out[rows_at(1 - half, rows), :] = found[:, where]


def unfold_sides(bits, joined, here, *refs):
    for side in (0, 1):
        own, found = refs[2 * side : 2 * side + 2]
        half, (rows, cols) = bit_at(here, "seq", bits[side]), own.shape
        out = refs[4] if joined else refs[4 + side]
        where = slice(side * cols, (side + 1) * cols) if joined else slice(0, cols)
        out[rows_at(half, rows), where] = own[...]
        out[rows_at(1 - half, rows), where] = found[...]


def link_call(body, here, args, shapes):
    name = body.func.__name__
    return run(body, name, (here, *args), tuple((shape, f32) for shape in shapes))


class LinkSum:
    def __init__(self, here, terms):
        self.here, self.plane = here, plane_bits()
        self.depth = bits_of(lax.axis_size("dp"))
        rows = sum(term.shape[0] for term in terms[::2])
        self.shape = (rows // 2, terms[0].shape[1] // 2)
        self.parts = link_call(
            functools.partial(fold_cores, self.plane[0]), here, terms, (self.shape,) * 4
        )

    def swap_plane(self, stage):
        (left, right), pieces = self.plane[stage], self.parts
        self.parts = (
            pieces[0], swap(pieces[1], "seq", left), pieces[2], swap(pieces[3], "seq", right)
        )

    def down_plane(self, stage, *others):
        parts, rows, cols = list(self.parts), *self.shape
        for other in others:
            parts += other.parts
            rows += other.shape[0]
        self.shape = (rows // 2, cols)
        body = functools.partial(fold_sides, self.plane[stage])
        self.parts = link_call(body, self.here, parts, (self.shape,) * 4)

    def down_join(self):
        rows, cols = self.shape
        self.shape = (rows // 2, 2 * cols)
        body = functools.partial(fold_join, self.depth[0])
        self.parts = link_call(body, self.here, self.parts, (self.shape,) * 2)

    def swap_depth(self, stage):
        self.parts = (self.parts[0], swap(self.parts[1], "dp", self.depth[stage]))

    def down_depth(self, stage):
        rows, cols = self.shape
        self.shape = (rows // 2, cols)
        body = functools.partial(fold_depth, self.depth[stage])
        self.parts = link_call(body, self.here, self.parts, (self.shape,) * 2)

    def middle(self):
        (value,) = run(add_two, "add_two", self.parts, ((self.shape, f32),), scalars=0)
        self.parts = (value, value)

    def up_depth(self, stage):
        rows, cols = self.shape
        self.shape = (rows * 2, cols)
        body = functools.partial(unfold, self.depth[stage])
        (value,) = link_call(body, self.here, self.parts, (self.shape,))
        self.parts = (value, value)

    def up_split(self):
        rows, cols = self.shape
        self.shape = (rows * 2, cols // 2)
        body = functools.partial(unfold_split, self.depth[0])
        left, right = link_call(body, self.here, self.parts, (self.shape,) * 2)
        self.parts = (left, left, right, right)

    def up_plane(self, stage):
        rows, cols = self.shape
        if stage:
            self.shape = (rows * 2, cols)
            body = functools.partial(unfold_sides, self.plane[stage], False)
            left, right = link_call(body, self.here, self.parts, (self.shape,) * 2)
            self.parts = (left, left, right, right)
        else:
            self.shape = (rows * 2, cols * 2)
            body = functools.partial(unfold_sides, self.plane[stage], True)
            self.parts = link_call(body, self.here, self.parts, (self.shape,))

    def back(self):
        for stage in range(len(self.plane) - 1, -1, -1):
            self.up_plane(stage)
            if stage:
                self.swap_plane(stage - 1)
        return self.parts[0]

    def follow(self, other):
        self.parts, other.parts = lax.optimization_barrier((self.parts, other.parts))

    def after(self, *values):
        self.parts, values = lax.optimization_barrier((self.parts, values))
        return values

    def to_depth(self):
        for stage in range(2, len(self.plane)):
            self.swap_plane(stage - 1)
            self.down_plane(stage)
        self.swap_plane(len(self.plane) - 1)

    def scatter_depth(self):
        for stage in range(len(self.depth) - 1):
            if stage:
                self.down_depth(stage)
            self.swap_depth(stage)

    def swap_whole(self):
        self.parts = (self.parts[0], swap(self.parts[0], "dp", self.depth[-1]))

    def gather_depth(self):
        for stage in range(len(self.depth) - 2, 0, -1):
            self.swap_depth(stage)
            self.up_depth(stage)
        self.swap_depth(0)


def discretize(lam_re, lam_im, log_step):
    step_size = jnp.exp(log_step)
    decay_abs = jnp.exp(lam_re * step_size)
    rotation = lam_im * step_size
    dec_re = decay_abs * jnp.cos(rotation)
    dec_im = decay_abs * jnp.sin(rotation)
    denom_sq = lam_re * lam_re + lam_im * lam_im
    inj_re = ((dec_re - 1.0) * lam_re + dec_im * lam_im) / denom_sq
    inj_im = (dec_im * lam_re - (dec_re - 1.0) * lam_im) / denom_sq
    return (dec_re, dec_im, inj_re, inj_im)


def per_device(
    block_in, cotangent, doc_lengths, norm_gain, norm_shift, log_step, lam_re, lam_im,
    b_proj, c_proj, d_skip, w_gate,
):
    batches, seqs, span, width = block_in.shape
    assert seqs == 1 and span % (4 * CHUNKS) == 0 and span & (span - 1) == 0
    half = lam_re.shape[1]
    groups = half // LANES
    rows = batches * span
    count = lax.axis_size("seq")
    tokens = float(seqs * lax.axis_size("dp") * span * count)
    here = jnp.stack([lax.axis_index("seq"), lax.axis_index("dp")]).astype(jnp.int32)
    place = jnp.concatenate([here] + [doc_lengths[batch, 0] for batch in range(batches)])
    place, block_in = lax.optimization_barrier((place, block_in))
    here = place
    disc = discretize(lam_re, lam_im, log_step)

    x = block_in.reshape(rows, width)
    cot = cotangent.reshape(rows, width)
    lower = (0, False, batches, span, groups, tokens, count)
    upper = (1, True, batches, span, groups, tokens, count)
    part = functools.partial

    flat, low = ((rows, width), f32), ((rows, width), bf16)
    wide, wide_low = ((rows, 2 * half), f32), ((rows, 2 * half), bf16)
    padded = ((batches * (span + CHUNKS), 2 * half), f32)
    sums = ((2 * batches, width), f32)
    prefix = ((2, batches * CHUNKS, 2 * half), f32)
    total = ((batches, 2 * half), f32)
    line, shared = ((1, width), f32), ((2, width), f32)
    small = ((8, width), f32)

    def gather_row(value):
        return lax.all_gather(value, "seq")

    ordered, stats = run(
        part(first_sums, batches, span), "first_sums", (x,), (low, sums), scalars=0
    )
    norms = jnp.concatenate([norm_gain, norm_shift, d_skip], axis=0)

    def forward(cfg, hidden, stats):
        return run(
            part(enter_layer, cfg),
            "enter_layer",
            (place, stats, hidden, norms, disc, b_proj),
            (low, wide, prefix, total, sums),
        )

    links, plane, depth = axis_parts()
    u0, drive0, prefix0, total0, norm0 = forward(
        lower, ordered, add_by_shifts(stats, (links, plane, depth))[0]
    )
    states0, states_low0, act0, sig0, slope0, hidden1, stats = run(
        part(middle_forward, lower),
        "middle_forward",
        (place, gather_row(total0), prefix0, disc, drive0, u0, ordered, c_proj, norms, w_gate),
        (padded, wide_low, low, flat, flat, flat, sums),
        (flat,),
    )
    u1, drive1, prefix1, total1, norm1 = forward(
        upper, hidden1, add_by_shifts(stats, (links, plane, depth))[0]
    )
    (
        block_out, ordered_cot, states1, states_low1, act1, grad_gate1, grad_mixed1, grad_low1,
        source1, prefix1, total1, grad_d1,
    ) = run(
        part(turn_around, upper),
        "turn_around",
        (
            place, gather_row(total1), prefix1, disc, drive1, u1, hidden1, c_proj, norms, w_gate,
            cot,
        ),
        (low, low, padded, wide_low, low, low, flat, low, wide, prefix, total, line),
        (flat, flat, flat, low),
    )

    def halves(length):
        return (((length // 2, width), f32),) * 2

    grad_proj1, grad_u1, stats, small1 = run(
        part(backward_finish, upper),
        "backward_finish",
        (
            place, gather_row(total1), prefix1, disc, source1, drive1, states1, u1, grad_mixed1,
            grad_d1, hidden1, norm1, norms, b_proj,
        ),
        (wide_low, flat, sums, small),
    )
    sizes = (width + 2 * half, 2 * half)
    own1, sent1 = run(
        all_weights,
        "all_weights",
        (here, act1, grad_gate1, states_low1, grad_low1, grad_proj1, u1),
        halves(sum(sizes)),
    )
    upper_sum = LinkSum(here, (own1, swap(sent1, "seq", 1)))
    stats, upper_sum.parts = add_by_shifts(stats, (links, plane, depth), upper_sum.parts)
    upper_sum.swap_plane(0)
    (
        grad_out0, shared1, grad_gate0, grad_mixed0, grad_low0, source0, prefix0, total0, grad_d0,
    ) = run(
        part(between_layers, upper, lower),
        "between_layers",
        (
            place, stats, ordered_cot, grad_u1, hidden1, norm1, norms,
            disc, u0, c_proj, w_gate, states_low0, act0, sig0, slope0,
        ),
        (flat, shared, low, flat, low, wide, prefix, total, line),
        (flat,),
    )
    (grad_gate0,) = upper_sum.after(grad_gate0)
    upper_sum.down_plane(1)
    upper_sum.to_depth()
    own_gates, sent_gates = run(
        gate_weights, "gate_weights", (here, act0, grad_gate0, states_low0, grad_low0),
        halves(sizes[0]),
    )
    found_gates = swap(sent_gates, "seq", 1)
    own_gates, total0 = lax.optimization_barrier((own_gates, total0))
    found_gates, ends = lax.optimization_barrier((found_gates, gather_row(total0)))
    (ends,) = upper_sum.after(ends)
    upper_sum.down_join()
    (ends,) = upper_sum.after(ends)
    upper_sum.scatter_depth()
    grad_proj0, grad_u0, last_sums = run(
        part(backward_finish_last, lower),
        "backward_finish",
        (
            place, ends, prefix0, disc, source0, drive0, states0, u0, grad_mixed0, grad_d0,
            ordered, norm0, norms, b_proj, small1,
        ),
        (wide_low, flat, ((3 * CHUNKS, width), f32)),
    )
    own_inputs, sent_inputs = run(
        input_weights, "input_weights", (here, grad_proj0, u0), halves(sizes[1])
    )
    found_inputs = swap(sent_inputs, "seq", 1)
    lower_sum = LinkSum(here, (own_gates, found_gates))
    lower_sum.swap_plane(0)
    inputs_sum = LinkSum(here, (own_inputs, found_inputs))
    (last_sums,) = inputs_sum.after(last_sums)
    upper_sum.follow(inputs_sum)
    inputs_sum.swap_plane(0)
    upper_sum.middle()
    upper_sum.swap_whole()
    lower_sum.down_plane(1, inputs_sum)
    lower_sum.to_depth()
    lower_sum.down_join()
    upper_sum.follow(lower_sum)
    upper_sum.middle()
    upper_sum.gather_depth()
    summed, lower_sum.parts = add_by_shifts(last_sums, (depth, links, plane), lower_sum.parts)
    summed = sum(summed)
    final = (((2, width, width), f32), ((2, 2 * half, width), f32), ((2, width, 2 * half), f32))
    lower_sum.scatter_depth()
    lower_sum.middle()
    upper_sum.follow(lower_sum)
    upper_sum.up_split()
    (summed,) = upper_sum.after(summed)
    upper_sum.swap_plane(len(upper_sum.plane) - 1)
    lower_sum.swap_whole()
    lower_sum.middle()
    upper_sum.follow(lower_sum)
    lower_sum.gather_depth()
    lower_sum.up_split()
    own1 = upper_sum.back()
    own1, lower_sum.parts = lax.optimization_barrier((own1, lower_sum.parts))
    other1 = swap(own1, "seq", 1)
    grad_input, shared0 = run(
        part(last_step, lower),
        "last_step",
        ((summed[: 2 * batches],), grad_out0, grad_u0, ordered, norm0, norms),
        (flat, shared),
        (((width // LANES, rows, LANES), f32),),
        scalars=0,
    )
    small_sum = summed[CHUNKS:].reshape(2, CHUNKS, width)
    _, pullback = jax.vjp(discretize, lam_re, lam_im, log_step)
    grad_lr, grad_li, grad_ls = pullback(tuple(small_sum[:, kind, :half] for kind in range(4)))
    lower_sum.swap_plane(len(lower_sum.plane) - 1)
    placed = put_in_place(1, here, ((False, own1), (True, other1)), final, ())
    grad_input, grad_lr, grad_li, grad_ls, *placed = lower_sum.after(
        grad_input, grad_lr, grad_li, grad_ls, *placed
    )
    own0 = lower_sum.back()
    other0 = swap(own0, "seq", 1)
    placed = put_in_place(0, here, ((False, own0),), final, placed, 4)
    grad_w, grad_c, grad_b = put_in_place(0, here, ((True, other0),), final, placed, 4)
    both = jnp.stack([shared0, shared1])
    shape = block_in.shape
    return (
        block_out.reshape(shape), grad_input.reshape(shape), both[:, 0], both[:, 1],
        grad_ls, grad_lr, grad_li, grad_b, grad_c, small_sum[:, 4], grad_w,
    )


def solution(mesh):
    split = P(None, "dp", "seq", None)
    return jax.shard_map(
        per_device,
        mesh=mesh,
        in_specs=(split, split, P(None, "dp", None)) + (P(),) * 9,
        out_specs=(split, split) + (P(),) * 9,
        check_vma=False,
    )
```

```python
import functools

import jax
import jax.numpy as jnp
from jax import lax
from jax.experimental import pallas as pl
from jax.experimental.pallas import tpu as pltpu
from jax.sharding import PartitionSpec as P

f32, bf16 = jnp.float32, jnp.bfloat16
epsilon = 1e-05
tanh_scale = 0.7978845608028654
cubic_term = 0.044715
LANES = 128
CHUNKS = 8
ROWS = 32
VMEM_LIMIT = 16 * 1024 * 1024


def dot(left, right, contract=(1, 0)):
    return lax.dot_general(
        left, right, (((contract[0],), (contract[1],)), ((), ())), preferred_element_type=f32
    )


def reorder(span, inverse):
    shape = (span, span)
    kept, moved = (1, 0) if inverse else (0, 1)
    row = lax.broadcasted_iota(jnp.int32, shape, kept)
    position = lax.broadcasted_iota(jnp.int32, shape, moved)
    source = (row & (CHUNKS - 1)) * (span // CHUNKS) + (row >> 3)
    return jnp.where(position == source, 1.0, 0.0).astype(bf16)


def row_loop(count, body, init=0, step=ROWS):
    def one(index, carry):
        return body(pl.multiple_of(index * step, step), carry)

    return lax.fori_loop(0, count // step, one, init)


def documents(here, batches, span, count):
    mine = here[0]
    first = mine * span
    out = []
    for batch in range(batches):
        begins, ends, so_far = [], [], 0
        docs = (here.shape[0] - 2) // batches
        for doc in range(docs):
            begins.append(so_far)
            so_far = so_far + here[2 + batch * docs + doc]
            ends.append(so_far)
        before, after = 0, 2 * count * span
        for begin, end in zip(begins, ends):
            before = jnp.maximum(before, jnp.where(begin < first, begin, 0))
            after = jnp.minimum(after, jnp.where(end > first + span, end, 2 * count * span))
        after = jnp.where(mine == count - 1, 0, after)
        out.append(begins + ends + [before, after, first, mine])
    return out


def place_documents(cfg, place):
    layer, reverse, batches, span, groups, tokens, count = cfg
    return documents(place, batches, span, count)


def keep_of(meta, batch, base, step, backward):
    docs = (len(meta[batch]) - 4) // 2
    off = docs if backward else 0
    late = 1 if backward else 0
    stop = base == meta[batch][off] - step - late
    for doc in range(1, docs):
        stop = jnp.logical_or(stop, base == meta[batch][off + doc] - step - late)
    return jnp.where(stop, 0.0, 1.0)


def base_positions(meta, steps):
    return meta[0][-2] + lax.broadcasted_iota(jnp.int32, (CHUNKS, LANES), 0) * steps


def lanes_of(index, half=0):
    return slice(half + index * LANES, half + (index + 1) * LANES)


def coef_tiles(value, groups):
    return [
        tuple(jnp.broadcast_to(part[:, lanes_of(q)], (CHUNKS, LANES)) for part in value)
        for q in range(groups)
    ]


def constants(disc, layer):
    dec_re, dec_im, inj_re, inj_im = (part[layer : layer + 1, :] for part in disc)
    return (dec_re, dec_im), (inj_re, inj_im)


def times(a, b):
    return (a[0] * b[0] - a[1] * b[1], a[0] * b[1] + a[1] * b[0])


def power(value, exponent):
    for _ in range(exponent.bit_length() - 1):
        value = times(value, value)
    return value


def conj(value):
    return (value[0], -value[1])


def scan(meta, source, inject, dec, batches, span, groups, reverse, masks_reverse, init, extra, visit):
    steps = span // CHUNKS
    half = groups * LANES
    base = base_positions(meta, steps)

    def pair(index, carry):
        states, more = carry
        states = list(states)
        first = steps - 2 - 2 * index if reverse else 2 * index
        start = pl.multiple_of(first * CHUNKS, 2 * CHUNKS)
        order = (1, 0) if reverse else (0, 1)
        for batch in range(batches):
            keeps = [keep_of(meta, batch, base, first + j, masks_reverse) for j in (0, 1)]
            for q in range(groups):
                rows = pl.ds(batch * span + start, 2 * CHUNKS)
                src_re = source[rows, lanes_of(q)]
                src_im = source[rows, lanes_of(q, half)]
                state = states[batch * groups + q]
                found = [None, None]
                for j in order:
                    part = (
                        src_re[j * CHUNKS : (j + 1) * CHUNKS],
                        src_im[j * CHUNKS : (j + 1) * CHUNKS],
                    )
                    push = times(inject[q], part) if inject is not None else part
                    held = times((keeps[j] * dec[q][0], keeps[j] * dec[q][1]), state)
                    state = (held[0] + push[0], held[1] + push[1])
                    found[j] = state
                states[batch * groups + q] = state
                more = visit(more, batch, q, first, start, found, (src_re, src_im))
            more = visit(more, batch, None, first, start, keeps, None)
        return tuple(states), more

    return lax.fori_loop(0, steps // 2, pair, (tuple(init), extra), unroll=2)


def zero_states(batches, groups):
    zero = jnp.zeros((CHUNKS, LANES), f32)
    return [(zero, zero)] * (batches * groups)


def local_ends(meta, source, inject, dec, batches, span, groups, reverse, prefix, total):
    ones = tuple(jnp.ones((CHUNKS, LANES), f32) for _ in range(batches))

    def visit(more, batch, q, first, start, found, src):
        if q is not None:
            return more
        return tuple(
            value * found[0] * found[1] if at == batch else value for at, value in enumerate(more)
        )

    dec_chunk = coef_tiles(power(dec, span // CHUNKS), groups)
    ends, kept = scan(
        meta, source, inject, coef_tiles(dec, groups), batches, span, groups, reverse, reverse,
        zero_states(batches, groups), ones, visit,
    )
    half = groups * LANES
    row = lax.broadcasted_iota(jnp.int32, (CHUNKS, LANES), 0)
    for batch in range(batches):
        for q in range(groups):
            end = ends[batch * groups + q]
            decay = (kept[batch] * dec_chunk[q][0], kept[batch] * dec_chunk[q][1])
            for shift in (1, 2, 4):
                turn = CHUNKS - shift if reverse else shift
                valid = row < CHUNKS - shift if reverse else row >= shift
                before = [pltpu.roll(value, turn, 0) for value in (*end, *decay)]
                from_before = times(decay, (before[0], before[1]))
                end = (
                    end[0] + jnp.where(valid, from_before[0], 0.0),
                    end[1] + jnp.where(valid, from_before[1], 0.0),
                )
                longer = times(decay, (before[2], before[3]))
                decay = (
                    jnp.where(valid, longer[0], decay[0]),
                    jnp.where(valid, longer[1], decay[1]),
                )
            rows = slice(batch * CHUNKS, (batch + 1) * CHUNKS)
            prefix[0, rows, lanes_of(q)] = end[0]
            prefix[0, rows, lanes_of(q, half)] = end[1]
            prefix[1, rows, lanes_of(q)] = decay[0]
            prefix[1, rows, lanes_of(q, half)] = decay[1]
            last = 0 if reverse else CHUNKS - 1
            total[batch : batch + 1, lanes_of(q)] = end[0][last : last + 1]
            total[batch : batch + 1, lanes_of(q, half)] = end[1][last : last + 1]


def chunk_carries(meta, gathered, dec, prefix, batches, span, groups, reverse):
    count = gathered.shape[0]
    half = groups * LANES
    dec_span = power(dec, span)
    row = lax.broadcasted_iota(jnp.int32, (CHUNKS, LANES), 0)
    mine = meta[0][-1]
    out = []
    for batch in range(batches):

        def add(at, so_far, batch=batch):
            away = count - 2 - at
            if reverse:
                other = mine + 1 + away
                reaches = meta[batch][-3] > other * span
            else:
                other = mine - 1 - away
                reaches = meta[batch][-4] < (mine - away) * span
            other = jnp.clip(other, 0, count - 1)
            value = jnp.where(reaches, gathered[other, pl.ds(batch, 1), :], 0.0)
            moved = times(dec_span, so_far)
            return (moved[0] + value[:, :half], moved[1] + value[:, half:])

        zero = jnp.zeros((1, half), f32)
        enter = lax.fori_loop(0, count - 1, add, (zero, zero), unroll=count <= 8)
        rows = slice(batch * CHUNKS, (batch + 1) * CHUNKS)
        for q in range(groups):
            own = tuple(jnp.broadcast_to(part[:, lanes_of(q)], (CHUNKS, LANES)) for part in enter)
            end = (prefix[0, rows, lanes_of(q)], prefix[0, rows, lanes_of(q, half)])
            decay = (prefix[1, rows, lanes_of(q)], prefix[1, rows, lanes_of(q, half)])
            moved = times(decay, own)
            turn, first = (CHUNKS - 1, CHUNKS - 1) if reverse else (1, 0)
            out.append(
                tuple(
                    jnp.where(row == first, own[i], pltpu.roll(end[i] + moved[i], turn, 0))
                    for i in (0, 1)
                )
            )
    return out


def add_sums(target, batches, sums):
    for kind, per_batch in enumerate(sums):
        for batch in range(batches):
            target[kind * batches + batch : kind * batches + batch + 1, :] = jnp.sum(
                per_batch[batch], axis=0, keepdims=True
            )


def fold(value):
    return sum(value[i : i + CHUNKS] for i in range(CHUNKS, value.shape[0], CHUNKS)) + value[:CHUNKS]


def first_sums(batches, span, x, ordered, stats):
    turn = reorder(span, False)
    width = x.shape[1]
    sums, squares = [], []
    for batch in range(batches):
        rows = slice(batch * span, (batch + 1) * span)
        ordered[rows, :] = dot(turn, x[rows, :]).astype(bf16)

        def body(start, carry, batch=batch):
            value = x[pl.ds(batch * span + start, ROWS), :].astype(f32)
            return carry[0] + fold(value), carry[1] + fold(value * value)

        zero = jnp.zeros((CHUNKS, width), f32)
        one, two = row_loop(span, body, (zero, zero))
        sums.append(one)
        squares.append(two)
    add_sums(stats, batches, (sums, squares))


def enter_layer(
    cfg, place, stats, hidden, norms, disc, b_proj, u, drive, prefix, total, norm
):
    layer, reverse, batches, span, groups, tokens, count = cfg
    sums = sum(part[...] for part in stats)
    average = sums[:batches] / tokens
    spread = sums[batches:] / tokens - average * average
    scale = lax.rsqrt(spread + epsilon)
    norm[:batches, :] = average
    norm[batches:, :] = scale
    gain_now, shift_now = norms[layer : layer + 1, :], norms[layer + 2 : layer + 3, :]
    for batch in range(batches):

        def body(start, carry, batch=batch):
            rows = pl.ds(batch * span + start, ROWS)
            normed = (hidden[rows, :].astype(f32) - average[batch : batch + 1]) * scale[
                batch : batch + 1
            ]
            u[rows, :] = (normed * gain_now + shift_now).astype(bf16)
            return carry

        row_loop(span, body)
    drive[...] = dot(u[...], b_proj[layer])
    meta = place_documents(cfg, place)
    dec, inj = constants(disc, layer)
    local_ends(
        meta, drive, coef_tiles(inj, groups), dec, batches, span, groups, reverse, prefix, total
    )


def finish_states(cfg, meta, ends, prefix, disc, drive, states, states_low):
    layer, reverse, batches, span, groups, tokens, count = cfg
    half = groups * LANES
    padded = span + CHUNKS
    dec, inj = constants(disc, layer)
    init = chunk_carries(meta, ends, dec, prefix, batches, span, groups, reverse)
    for batch in range(batches):
        edge = batch * padded + (span if reverse else 0)
        for q in range(groups):
            states[edge : edge + CHUNKS, lanes_of(q)] = init[batch * groups + q][0]
            states[edge : edge + CHUNKS, lanes_of(q, half)] = init[batch * groups + q][1]

    def visit(more, batch, q, first, start, found, src):
        if q is not None:
            for part, off in ((0, 0), (1, half)):
                both = jnp.concatenate([found[0][part], found[1][part]], axis=0)
                at = batch * padded + (0 if reverse else CHUNKS)
                states[pl.ds(at + start, 2 * CHUNKS), lanes_of(q, off)] = both
                states_low[pl.ds(batch * span + start, 2 * CHUNKS), lanes_of(q, off)] = both.astype(
                    bf16
                )
        return more

    scan(
        meta, drive, coef_tiles(inj, groups), coef_tiles(dec, groups), batches, span, groups,
        reverse, reverse, init, 0, visit,
    )


def forward_finish(
    cfg, meta, ends, prefix, disc, drive, u, hidden, c_proj, norms, w_gate,
    states, states_low, act, sig, slope, result, wide, emit,
):
    layer, reverse, batches, span, groups, tokens, count = cfg
    finish_states(cfg, meta, ends, prefix, disc, drive, states, states_low)
    wide[...] = dot(states_low[...], c_proj[layer])
    skip = norms[layer + 4 : layer + 5, :]

    def body(start, carry):
        rows = pl.ds(start, ROWS)
        mixed = wide[rows, :] + skip * u[rows, :].astype(f32)
        square = mixed * mixed
        th = jnp.tanh(tanh_scale * (mixed + cubic_term * square * mixed))
        half_one = 0.5 * (1.0 + th)
        act[rows, :] = (mixed * half_one).astype(bf16)
        slope[rows, :] = half_one + 0.5 * mixed * (1.0 - th * th) * tanh_scale * (
            1.0 + 3.0 * cubic_term * square
        )
        return carry

    row_loop(batches * span, body)
    wide[...] = dot(act[...], w_gate[layer])
    sums, squares = [], []
    for batch in range(batches):

        def gate(start, carry, batch=batch):
            rows = pl.ds(batch * span + start, ROWS)
            sig_now = 0.5 + 0.5 * jnp.tanh(0.5 * wide[rows, :])
            sig[rows, :] = sig_now
            value = hidden[rows, :].astype(f32) + act[rows, :].astype(f32) * sig_now
            result[rows, :] = value.astype(result.dtype)
            if emit is None:
                return carry
            return carry[0] + fold(value), carry[1] + fold(value * value)

        zero = jnp.zeros((CHUNKS, wide.shape[1]), f32)
        one, two = row_loop(span, gate, (zero, zero))
        sums.append(one)
        squares.append(two)
    if emit is not None:
        add_sums(emit, batches, (sums, squares))


def backward_start(
    cfg, meta, grad_out, disc, u, c_proj, w_gate, states_low, act, sig, slope,
    grad_gate, grad_mixed, grad_low, source, prefix, total, grad_d, wide,
):
    layer, reverse, batches, span, groups, tokens, count = cfg

    def body(start, carry):
        rows = pl.ds(start, ROWS)
        sig_now = sig[rows, :]
        grad_gate[rows, :] = (
            grad_out[rows, :].astype(f32) * act[rows, :].astype(f32) * sig_now * (1.0 - sig_now)
        ).astype(bf16)
        return carry

    row_loop(batches * span, body)
    wide[...] = dot(grad_gate[...], w_gate[layer], (1, 1))

    def mixed(start, carry):
        rows = pl.ds(start, ROWS)
        value = (grad_out[rows, :].astype(f32) * sig[rows, :] + wide[rows, :]) * slope[rows, :]
        grad_mixed[rows, :] = value
        grad_low[rows, :] = value.astype(bf16)
        return carry + fold(value * u[rows, :].astype(f32))

    gd = row_loop(batches * span, mixed, jnp.zeros((CHUNKS, wide.shape[1]), f32))
    grad_d[...] = jnp.sum(gd, axis=0, keepdims=True)
    source[...] = dot(grad_low[...], c_proj[layer], (1, 1))
    local_ends(
        meta, source, None, conj(constants(disc, layer)[0]), batches, span, groups, not reverse,
        prefix, total,
    )


def middle_forward(
    cfg, place, ends, prefix, disc, drive, u, hidden, c_proj, norms, w_gate,
    states, states_low, act, sig, slope, result, stats, wide,
):
    meta = place_documents(cfg, place)
    forward_finish(
        cfg, meta, ends, prefix, disc, drive, u, hidden, c_proj, norms, w_gate,
        states, states_low, act, sig, slope, result, wide, stats,
    )


def turn_around(
    cfg, place, ends, prefix, disc, drive, u, hidden, c_proj, norms, w_gate, cotangent,
    block_out, ordered_cot, states, states_low, act, grad_gate, grad_mixed, grad_low, source,
    back_prefix, total, grad_d, sig, slope, wide, result,
):
    layer, reverse, batches, span, groups, tokens, count = cfg
    meta = place_documents(cfg, place)
    turn, back = reorder(span, False), reorder(span, True)
    for batch in range(batches):
        rows = slice(batch * span, (batch + 1) * span)
        ordered_cot[rows, :] = dot(turn, cotangent[rows, :]).astype(bf16)
    forward_finish(
        cfg, meta, ends, prefix, disc, drive, u, hidden, c_proj, norms, w_gate,
        states, states_low, act, sig, slope, result, wide, None,
    )
    for batch in range(batches):
        rows = slice(batch * span, (batch + 1) * span)
        block_out[rows, :] = dot(back, result[rows, :]).astype(bf16)
    backward_start(
        cfg, meta, ordered_cot, disc, u, c_proj, w_gate, states_low, act, sig, slope,
        grad_gate, grad_mixed, grad_low, source, back_prefix, total, grad_d, wide,
    )


def backward_finish(
    cfg, place, ends, prefix, disc, source, drive, states, u, grad_mixed, grad_d, hidden, norm,
    norms, b_proj, grad_proj, grad_u, stats, small,
):
    layer, reverse, batches, span, groups, tokens, count = cfg
    half = groups * LANES
    padded = span + CHUNKS
    steps = span // CHUNKS
    meta = place_documents(cfg, place)
    dec, inj = constants(disc, layer)
    dec = conj(dec)
    init = chunk_carries(meta, ends, dec, prefix, batches, span, groups, not reverse)
    inj = coef_tiles(inj, groups)
    base = base_positions(meta, steps)
    zero = jnp.zeros((CHUNKS, LANES), f32)

    def visit(more, batch, q, first, start, found, src):
        if q is None:
            return more
        more = list(more)
        rows = pl.ds(batch * span + start, 2 * CHUNKS)
        drive_re, drive_im = drive[rows, lanes_of(q)], drive[rows, lanes_of(q, half)]
        before = pl.ds(batch * padded + start + (CHUNKS if reverse else 0), 2 * CHUNKS)
        prior_re, prior_im = states[before, lanes_of(q)], states[before, lanes_of(q, half)]
        dec_re, dec_im, inj_re, inj_im = more[q]
        out_re, out_im = [], []
        for j in (0, 1):
            part = slice(j * CHUNKS, (j + 1) * CHUNKS)
            adj_re, adj_im = found[j]
            keep = keep_of(meta, batch, base, first + j, reverse)
            kept_re, kept_im = keep * adj_re, keep * adj_im
            dec_re = dec_re + kept_re * prior_re[part] + kept_im * prior_im[part]
            dec_im = dec_im + kept_im * prior_re[part] - kept_re * prior_im[part]
            inj_re = inj_re + adj_re * drive_re[part] + adj_im * drive_im[part]
            inj_im = inj_im + adj_im * drive_re[part] - adj_re * drive_im[part]
            out_re.append(inj[q][0] * adj_re + inj[q][1] * adj_im)
            out_im.append(inj[q][0] * adj_im - inj[q][1] * adj_re)
        grad_proj[rows, lanes_of(q)] = jnp.concatenate(out_re, axis=0).astype(bf16)
        grad_proj[rows, lanes_of(q, half)] = jnp.concatenate(out_im, axis=0).astype(bf16)
        more[q] = (dec_re, dec_im, inj_re, inj_im)
        return tuple(more)

    _, sums = scan(
        meta, source, None, coef_tiles(dec, groups), batches, span, groups,
        not reverse, not reverse, init, ((zero,) * 4,) * groups, visit,
    )
    small[...] = jnp.zeros_like(small)
    for q in range(groups):
        for kind in range(4):
            small[kind : kind + 1, lanes_of(q)] = jnp.sum(sums[q][kind], axis=0, keepdims=True)
    small[4:5, :] = grad_d[...]
    grad_u[...] = dot(grad_proj[...], b_proj[layer], (1, 1))
    skip = norms[layer + 4 : layer + 5, :]
    plain, times_normed = [], []
    for batch in range(batches):
        average = norm[batch : batch + 1, :]
        scale = norm[batches + batch : batches + batch + 1, :]

        def body(start, carry, batch=batch, average=average, scale=scale):
            rows = pl.ds(batch * span + start, ROWS)
            value = grad_u[rows, :] + grad_mixed[rows, :] * skip
            grad_u[rows, :] = value
            normed = (hidden[rows, :].astype(f32) - average) * scale
            return carry[0] + fold(value), carry[1] + fold(value * normed)

        zero_sum = jnp.zeros((CHUNKS, grad_u.shape[1]), f32)
        one, two = row_loop(span, body, (zero_sum, zero_sum))
        plain.append(one)
        times_normed.append(two)
    add_sums(stats, batches, (plain, times_normed))


def backward_finish_last(cfg, *refs):
    ins, before, (grad_proj, grad_u, sums) = refs[:-4], refs[-4], refs[-3:]
    sums[...] = jnp.zeros_like(sums)
    sums[2 * CHUNKS :, :] = before[...]
    backward_finish(
        cfg, *ins, grad_proj, grad_u, sums.at[pl.ds(0, CHUNKS)], sums.at[pl.ds(CHUNKS, CHUNKS)]
    )


def norm_backward(cfg, stats, grad_out, grad_u, hidden, norm, norms, store, shared):
    layer, reverse, batches, span, groups, tokens, count = cfg
    sums = sum(part[...] for part in stats)
    shared[0:1, :] = jnp.sum(sums[batches:], axis=0, keepdims=True)
    shared[1:2, :] = jnp.sum(sums[:batches], axis=0, keepdims=True)
    gain_now = norms[layer : layer + 1, :]
    for batch in range(batches):
        average = norm[batch : batch + 1, :]
        scale = norm[batches + batch : batches + batch + 1, :]
        plain = gain_now * sums[batch : batch + 1] / tokens
        slanted = gain_now * sums[batches + batch : batches + batch + 1] / tokens

        def body(start, carry, batch=batch, average=average, scale=scale, plain=plain, slanted=slanted):
            rows = pl.ds(batch * span + start, ROWS)
            normed = (hidden[rows, :].astype(f32) - average) * scale
            value = grad_out[rows, :].astype(f32) + scale * (
                grad_u[rows, :] * gain_now - plain - normed * slanted
            )
            store(rows, value)
            return carry

        row_loop(span, body)


def between_layers(
    cfg, lower, place, stats, upper_out, upper_u, upper_hidden, upper_norm, norms,
    disc, u, c_proj, w_gate, states_low, act, sig, slope,
    grad_out, shared, grad_gate, grad_mixed, grad_low, source, prefix, total, grad_d, wide,
):
    def store(rows, value):
        grad_out[rows, :] = value

    norm_backward(cfg, stats, upper_out, upper_u, upper_hidden, upper_norm, norms, store, shared)
    meta = place_documents(lower, place)
    backward_start(
        lower, meta, grad_out, disc, u, c_proj, w_gate, states_low, act, sig, slope,
        grad_gate, grad_mixed, grad_low, source, prefix, total, grad_d, wide,
    )


def last_step(cfg, stats, grad_out, grad_u, hidden, norm, norms, target, shared, ordered):
    layer, reverse, batches, span, groups, tokens, count = cfg
    planes = target.shape[1] // LANES

    def store(rows, value):
        for plane in range(planes):
            ordered[plane, rows, :] = value[:, lanes_of(plane)]

    norm_backward(cfg, stats, grad_out, grad_u, hidden, norm, norms, store, shared)
    steps = span // CHUNKS
    for batch in range(batches):
        for chunk in range(CHUNKS):
            at = batch * span
            for plane in range(planes):
                target[at + chunk * steps : at + (chunk + 1) * steps, lanes_of(plane)] = ordered[
                    plane, pl.ds(at + chunk, steps, stride=CHUNKS), :
                ]


def half_weights(core, refs, own, sent):
    for target, half in ((own, core), (sent, 1 - core)):
        at = 0
        for left, right in refs:
            rows = left.shape[1] // 2
            cols = pl.ds(pl.multiple_of(half * rows, LANES), rows)
            target[at : at + rows, :] = dot(left[:, cols], right[...], (0, 0))
            at += rows


def all_weights(here, act, grad_gate, states_low, grad_low, grad_proj, u, own, sent):
    refs = ((act, grad_gate), (states_low, grad_low), (grad_proj, u))
    half_weights(lax.rem(here[0], 2), refs, own, sent)


def gate_weights(here, act, grad_gate, states_low, grad_low, own, sent):
    half_weights(lax.rem(here[0], 2), ((act, grad_gate), (states_low, grad_low)), own, sent)


def input_weights(here, grad_proj, u, own, sent):
    half_weights(lax.rem(here[0], 2), ((grad_proj, u),), own, sent)


def run(body, name, args, outs, scratch=(), scalars=1):
    vmem, smem = pl.BlockSpec(memory_space=pltpu.VMEM), pl.BlockSpec(memory_space=pltpu.SMEM)
    specs = tuple(
        jax.tree.map(lambda _, at=at: smem if at < scalars else vmem, arg)
        for at, arg in enumerate(args)
    )
    return pl.pallas_call(
        body,
        name=name,
        out_shape=tuple(jax.ShapeDtypeStruct(*out) for out in outs),
        in_specs=specs,
        out_specs=(vmem,) * len(outs),
        scratch_shapes=[pltpu.VMEM(*entry) for entry in scratch],
        compiler_params=pltpu.CompilerParams(vmem_limit_bytes=VMEM_LIMIT),
    )(*args)


def put_in_place(layer, here, halves, outs, before, pieces=1):
    width, states = outs[0][0][1], outs[1][0][1]
    rows_w, rows_c = width // 2, states // 2
    vmem, count = pl.BlockSpec(memory_space=pltpu.VMEM), len(halves)

    def half(step, here):
        core = lax.rem(here[0], 2)
        spots = [1 - core if other else core for other, _ in halves]
        return spots[0] if count == 1 else jnp.where(step == 0, *spots)

    blocks = (
        pl.BlockSpec((1, rows_w, width), lambda i, here: (layer, half(i, here), 0)),
        pl.BlockSpec((1, rows_c, width), lambda i, here: (layer, half(i, here), 0)),
        pl.BlockSpec((1, width, rows_c), lambda i, here: (layer, 0, half(i, here))),
    )

    def body(here, *refs):
        grad_w, grad_c, grad_b = refs[-3:]
        for now in range(count):

            @pl.when(pl.program_id(0) == now)
            def _(source=refs[now]):
                gates, inputs = (rows_w + rows_c) // pieces, rows_c // pieces
                columns = []
                for piece in range(pieces):
                    at, row = piece * (gates + inputs), piece * gates
                    turn = min(max(rows_w - row, 0), gates)
                    if turn:
                        grad_w[0, row : row + turn, :] = source[at : at + turn, :]
                    if turn < gates:
                        to = row + turn - rows_w
                        grad_c[0, to : to + gates - turn, :] = source[at + turn : at + gates, :]
                    columns.append(source[at + gates : at + gates + inputs, :])
                grad_b[0] = jnp.concatenate(columns, axis=0).T

    return pl.pallas_call(
        body,
        name="put_in_place",
        out_shape=tuple(jax.ShapeDtypeStruct(*out) for out in outs),
        grid_spec=pltpu.PrefetchScalarGridSpec(
            num_scalar_prefetch=1,
            grid=(count,),
            in_specs=[vmem] * count + [pl.BlockSpec(memory_space=pl.ANY)] * len(before),
            out_specs=blocks,
        ),
        input_output_aliases={1 + count + i: i for i in range(len(before))},
        compiler_params=pltpu.CompilerParams(vmem_limit_bytes=VMEM_LIMIT),
    )(here, *(rows for _, rows in halves), *before)


def axis_parts():
    count, depth = lax.axis_size("seq"), lax.axis_size("dp")
    return (("seq", 2, 1, count), ("seq", count // 2, 2, count), ("dp", depth, 1, depth))


def shifted(value, part, away):
    name, size, stride, count = part
    pairs = []
    for i in range(count):
        place = (i // stride) % size
        pairs.append((i, i + ((place + away) % size - place) * stride))
    return lax.ppermute(value, name, pairs)


def add_by_shifts(value, parts, *earlier):
    for number, part in enumerate(parts):
        if number:
            value = sum(terms[1:], terms[0])
        if number == len(parts) - 1:
            value, *earlier = lax.optimization_barrier((value, *earlier))
        terms = [value] + [shifted(value, part, away) for away in range(1, part[1])]
    return terms, *earlier


def bits_of(size, stride=1):
    bits = []
    while size > 1:
        bits.append(stride)
        size, stride = size // 2, stride * 2
    return bits


def plane_bits():
    chip_bits = bits_of(lax.axis_size("seq") // 2, 2)
    middle = (len(chip_bits) + 1) // 2
    inner, outer = chip_bits[:middle], chip_bits[middle:]
    return list(zip(inner + outer, outer + inner))


def swap(value, axis, bit):
    return lax.ppermute(value, axis, [(i, i ^ bit) for i in range(lax.axis_size(axis))])


def bit_at(here, axis, bit):
    return lax.rem(lax.div(here[0 if axis == "seq" else 1], bit), 2)


def rows_at(half, rows):
    return pl.ds(pl.multiple_of(half * rows, CHUNKS), rows)


def fold_cores(bits, here, *refs):
    terms, targets = refs[:-4], refs[-4:]
    rows, cols = targets[0].shape
    for side in (0, 1):
        kept, sent = targets[2 * side : 2 * side + 2]
        where = slice(side * cols, (side + 1) * cols)
        bit = bit_at(here, "seq", bits[side])
        for half in (0, 1):

            @pl.when(bit == half)
            def _(half=half, kept=kept, sent=sent, where=where):
                start = 0
                for own, found in zip(terms[0::2], terms[1::2]):
                    for part, target in ((half, kept), (1 - half, sent)):
                        low = max(start, part * rows)
                        high = min(start + own.shape[0], (part + 1) * rows)
                        if low < high:
                            source = slice(low - start, high - start)
                            target[low - part * rows : high - part * rows, :] = (
                                own[source, where] + found[source, where]
                            )
                    start += own.shape[0]


def fold_sides(bits, here, *refs):
    targets, blocks = refs[-4:], refs[:-4]
    for side in (0, 1):
        kept, sent = targets[2 * side : 2 * side + 2]
        half, start = bit_at(here, "seq", bits[side]), 0
        for at in range(0, len(blocks), 4):
            own, found = blocks[at + 2 * side : at + 2 * side + 2]
            rows = own.shape[0] // 2
            to = slice(start, start + rows)
            kept[to, :] = own[rows_at(half, rows), :] + found[rows_at(half, rows), :]
            sent[to, :] = own[rows_at(1 - half, rows), :] + found[rows_at(1 - half, rows), :]
            start += rows


def fold_join(bit, here, left, found_left, right, found_right, kept, sent):
    rows, cols = kept.shape[0], left.shape[1]
    half = bit_at(here, "dp", bit)
    for side, (own, found) in enumerate(((left, found_left), (right, found_right))):
        where = slice(side * cols, (side + 1) * cols)
        kept[:, where] = own[rows_at(half, rows), :] + found[rows_at(half, rows), :]
        sent[:, where] = own[rows_at(1 - half, rows), :] + found[rows_at(1 - half, rows), :]


def fold_depth(bit, here, own, found, kept, sent):
    half, rows = bit_at(here, "dp", bit), kept.shape[0]
    kept[...] = own[rows_at(half, rows), :] + found[rows_at(half, rows), :]
    sent[...] = own[rows_at(1 - half, rows), :] + found[rows_at(1 - half, rows), :]


def add_two(own, found, out):
    out[...] = own[...] + found[...]


def unfold(bit, here, own, found, out):
    half, rows = bit_at(here, "dp", bit), own.shape[0]
    out[rows_at(half, rows), :] = own[...]
    out[rows_at(1 - half, rows), :] = found[...]


def unfold_split(bit, here, own, found, left, right):
    half, rows, cols = bit_at(here, "dp", bit), own.shape[0], left.shape[1]
    for side, out in enumerate((left, right)):
        where = slice(side * cols, (side + 1) * cols)
        out[rows_at(half, rows), :] = own[:, where]
        out[rows_at(1 - half, rows), :] = found[:, where]


def unfold_sides(bits, joined, here, *refs):
    for side in (0, 1):
        own, found = refs[2 * side : 2 * side + 2]
        half, (rows, cols) = bit_at(here, "seq", bits[side]), own.shape
        out = refs[4] if joined else refs[4 + side]
        where = slice(side * cols, (side + 1) * cols) if joined else slice(0, cols)
        out[rows_at(half, rows), where] = own[...]
        out[rows_at(1 - half, rows), where] = found[...]


def link_call(body, here, args, shapes):
    name = body.func.__name__
    return run(body, name, (here, *args), tuple((shape, f32) for shape in shapes))


class LinkSum:
    def __init__(self, here, terms):
        self.here, self.plane = here, plane_bits()
        self.depth = bits_of(lax.axis_size("dp"))
        rows = sum(term.shape[0] for term in terms[::2])
        self.shape = (rows // 2, terms[0].shape[1] // 2)
        self.parts = link_call(
            functools.partial(fold_cores, self.plane[0]), here, terms, (self.shape,) * 4
        )

    def swap_plane(self, stage):
        (left, right), pieces = self.plane[stage], self.parts
        self.parts = (
            pieces[0], swap(pieces[1], "seq", left), pieces[2], swap(pieces[3], "seq", right)
        )

    def down_plane(self, stage, *others):
        parts, rows, cols = list(self.parts), *self.shape
        for other in others:
            parts += other.parts
            rows += other.shape[0]
        self.shape = (rows // 2, cols)
        body = functools.partial(fold_sides, self.plane[stage])
        self.parts = link_call(body, self.here, parts, (self.shape,) * 4)

    def down_join(self):
        rows, cols = self.shape
        self.shape = (rows // 2, 2 * cols)
        body = functools.partial(fold_join, self.depth[0])
        self.parts = link_call(body, self.here, self.parts, (self.shape,) * 2)

    def swap_depth(self, stage):
        self.parts = (self.parts[0], swap(self.parts[1], "dp", self.depth[stage]))

    def down_depth(self, stage):
        rows, cols = self.shape
        self.shape = (rows // 2, cols)
        body = functools.partial(fold_depth, self.depth[stage])
        self.parts = link_call(body, self.here, self.parts, (self.shape,) * 2)

    def middle(self):
        (value,) = run(add_two, "add_two", self.parts, ((self.shape, f32),), scalars=0)
        self.parts = (value, value)

    def up_depth(self, stage):
        rows, cols = self.shape
        self.shape = (rows * 2, cols)
        body = functools.partial(unfold, self.depth[stage])
        (value,) = link_call(body, self.here, self.parts, (self.shape,))
        self.parts = (value, value)

    def up_split(self):
        rows, cols = self.shape
        self.shape = (rows * 2, cols // 2)
        body = functools.partial(unfold_split, self.depth[0])
        left, right = link_call(body, self.here, self.parts, (self.shape,) * 2)
        self.parts = (left, left, right, right)

    def up_plane(self, stage):
        rows, cols = self.shape
        if stage:
            self.shape = (rows * 2, cols)
            body = functools.partial(unfold_sides, self.plane[stage], False)
            left, right = link_call(body, self.here, self.parts, (self.shape,) * 2)
            self.parts = (left, left, right, right)
        else:
            self.shape = (rows * 2, cols * 2)
            body = functools.partial(unfold_sides, self.plane[stage], True)
            self.parts = link_call(body, self.here, self.parts, (self.shape,))

    def back(self):
        for stage in range(len(self.plane) - 1, -1, -1):
            self.up_plane(stage)
            if stage:
                self.swap_plane(stage - 1)
        return self.parts[0]

    def after(self, *values):
        self.parts, values = lax.optimization_barrier((self.parts, values))
        return values

    def to_depth(self):
        for stage in range(2, len(self.plane)):
            self.swap_plane(stage - 1)
            self.down_plane(stage)
        self.swap_plane(len(self.plane) - 1)

    def scatter_depth(self):
        for stage in range(len(self.depth) - 1):
            if stage:
                self.down_depth(stage)
            self.swap_depth(stage)

    def swap_whole(self):
        self.parts = (self.parts[0], swap(self.parts[0], "dp", self.depth[-1]))

    def gather_depth(self):
        for stage in range(len(self.depth) - 2, 0, -1):
            self.swap_depth(stage)
            self.up_depth(stage)
        self.swap_depth(0)


def wait_for(*things):
    sums = [thing for thing in things if isinstance(thing, LinkSum)]
    values = [thing for thing in things if not isinstance(thing, LinkSum)]
    parts, values = lax.optimization_barrier(([entry.parts for entry in sums], values))
    for entry, part in zip(sums, parts):
        entry.parts = part
    return values


def discretize(lam_re, lam_im, log_step):
    step_size = jnp.exp(log_step)
    decay_abs = jnp.exp(lam_re * step_size)
    rotation = lam_im * step_size
    dec_re = decay_abs * jnp.cos(rotation)
    dec_im = decay_abs * jnp.sin(rotation)
    denom_sq = lam_re * lam_re + lam_im * lam_im
    inj_re = ((dec_re - 1.0) * lam_re + dec_im * lam_im) / denom_sq
    inj_im = (dec_im * lam_re - (dec_re - 1.0) * lam_im) / denom_sq
    return (dec_re, dec_im, inj_re, inj_im)


def per_device(
    block_in, cotangent, doc_lengths, norm_gain, norm_shift, log_step, lam_re, lam_im,
    b_proj, c_proj, d_skip, w_gate,
):
    batches, seqs, span, width = block_in.shape
    assert seqs == 1 and span % (4 * CHUNKS) == 0 and span & (span - 1) == 0
    half = lam_re.shape[1]
    groups = half // LANES
    rows = batches * span
    count = lax.axis_size("seq")
    tokens = float(seqs * lax.axis_size("dp") * span * count)
    here = jnp.stack([lax.axis_index("seq"), lax.axis_index("dp")]).astype(jnp.int32)
    place = jnp.concatenate([here] + [doc_lengths[batch, 0] for batch in range(batches)])
    place, block_in = lax.optimization_barrier((place, block_in))
    here = place
    disc = discretize(lam_re, lam_im, log_step)

    x = block_in.reshape(rows, width)
    cot = cotangent.reshape(rows, width)
    lower = (0, False, batches, span, groups, tokens, count)
    upper = (1, True, batches, span, groups, tokens, count)
    part = functools.partial

    flat, low = ((rows, width), f32), ((rows, width), bf16)
    wide, wide_low = ((rows, 2 * half), f32), ((rows, 2 * half), bf16)
    padded = ((batches * (span + CHUNKS), 2 * half), f32)
    sums = ((2 * batches, width), f32)
    prefix = ((2, batches * CHUNKS, 2 * half), f32)
    total = ((batches, 2 * half), f32)
    line, shared = ((1, width), f32), ((2, width), f32)
    small = ((8, width), f32)

    def gather_row(value):
        return lax.all_gather(value, "seq")

    ordered, stats = run(
        part(first_sums, batches, span), "first_sums", (x,), (low, sums), scalars=0
    )
    norms = jnp.concatenate([norm_gain, norm_shift, d_skip], axis=0)

    def forward(cfg, hidden, stats):
        return run(
            part(enter_layer, cfg),
            "enter_layer",
            (place, stats, hidden, norms, disc, b_proj),
            (low, wide, prefix, total, sums),
        )

    links, plane, depth = axis_parts()
    u0, drive0, prefix0, total0, norm0 = forward(
        lower, ordered, add_by_shifts(stats, (links, plane, depth))[0]
    )
    states0, states_low0, act0, sig0, slope0, hidden1, stats = run(
        part(middle_forward, lower),
        "middle_forward",
        (place, gather_row(total0), prefix0, disc, drive0, u0, ordered, c_proj, norms, w_gate),
        (padded, wide_low, low, flat, flat, flat, sums),
        (flat,),
    )
    u1, drive1, prefix1, total1, norm1 = forward(
        upper, hidden1, add_by_shifts(stats, (links, plane, depth))[0]
    )
    (
        block_out, ordered_cot, states1, states_low1, act1, grad_gate1, grad_mixed1, grad_low1,
        source1, prefix1, total1, grad_d1,
    ) = run(
        part(turn_around, upper),
        "turn_around",
        (
            place, gather_row(total1), prefix1, disc, drive1, u1, hidden1, c_proj, norms, w_gate,
            cot,
        ),
        (low, low, padded, wide_low, low, low, flat, low, wide, prefix, total, line),
        (flat, flat, flat, low),
    )

    def halves(length):
        return (((length // 2, width), f32),) * 2

    grad_proj1, grad_u1, stats, small1 = run(
        part(backward_finish, upper),
        "backward_finish",
        (
            place, gather_row(total1), prefix1, disc, source1, drive1, states1, u1, grad_mixed1,
            grad_d1, hidden1, norm1, norms, b_proj,
        ),
        (wide_low, flat, sums, small),
    )
    sizes = (width + 2 * half, 2 * half)
    own1, sent1 = run(
        all_weights,
        "all_weights",
        (here, act1, grad_gate1, states_low1, grad_low1, grad_proj1, u1),
        halves(sum(sizes)),
    )
    upper_sum = LinkSum(here, (own1, swap(sent1, "seq", 1)))
    stats, upper_sum.parts = add_by_shifts(stats, (links, plane, depth), upper_sum.parts)
    upper_sum.swap_plane(0)
    (
        grad_out0, shared1, grad_gate0, grad_mixed0, grad_low0, source0, prefix0, total0, grad_d0,
    ) = run(
        part(between_layers, upper, lower),
        "between_layers",
        (
            place, stats, ordered_cot, grad_u1, hidden1, norm1, norms,
            disc, u0, c_proj, w_gate, states_low0, act0, sig0, slope0,
        ),
        (flat, shared, low, flat, low, wide, prefix, total, line),
        (flat,),
    )
    (grad_gate0,) = upper_sum.after(grad_gate0)
    upper_sum.down_plane(1)
    upper_sum.to_depth()
    own_gates, sent_gates = run(
        gate_weights, "gate_weights", (here, act0, grad_gate0, states_low0, grad_low0),
        halves(sizes[0]),
    )
    found_gates = swap(sent_gates, "seq", 1)
    own_gates, total0 = lax.optimization_barrier((own_gates, total0))
    found_gates, ends = lax.optimization_barrier((found_gates, gather_row(total0)))
    (ends,) = upper_sum.after(ends)
    upper_sum.down_join()
    (ends,) = upper_sum.after(ends)
    upper_sum.scatter_depth()
    grad_proj0, grad_u0, last_sums = run(
        part(backward_finish_last, lower),
        "backward_finish",
        (
            place, ends, prefix0, disc, source0, drive0, states0, u0, grad_mixed0, grad_d0,
            ordered, norm0, norms, b_proj, small1,
        ),
        (wide_low, flat, ((3 * CHUNKS, width), f32)),
    )
    lower_sum = LinkSum(here, (own_gates, found_gates))
    (grad_proj0,) = wait_for(upper_sum, lower_sum, grad_proj0)
    own_inputs, sent_inputs = run(
        input_weights, "input_weights", (here, grad_proj0, u0), halves(sizes[1])
    )
    inputs_sum = LinkSum(here, (own_inputs, swap(sent_inputs, "seq", 1)))
    upper_sum.middle()
    upper_sum.swap_whole()
    lower_sum.swap_plane(0)
    inputs_sum.swap_plane(0)
    (last_sums,) = wait_for(upper_sum, lower_sum, inputs_sum, last_sums)

    lower_sum.down_plane(1, inputs_sum)
    upper_sum.middle()
    upper_sum.gather_depth()
    lower_sum.to_depth()
    last_terms = [last_sums] + [shifted(last_sums, depth, away) for away in range(1, depth[1])]
    last_terms = wait_for(upper_sum, lower_sum, *last_terms)

    lower_sum.down_join()
    upper_sum.up_split()
    lower_sum.scatter_depth()
    upper_sum.swap_plane(len(upper_sum.plane) - 1)
    last_sums = sum(last_terms)
    last_sums = last_sums + swap(last_sums, "seq", 1)
    last_terms = [last_sums] + [shifted(last_sums, plane, away) for away in range(1, plane[1])]
    last_terms = wait_for(upper_sum, lower_sum, *last_terms)
    summed = sum(last_terms)

    lower_sum.middle()
    lower_sum.swap_whole()
    for stage in range(len(upper_sum.plane) - 1, 0, -1):
        upper_sum.up_plane(stage)
        upper_sum.swap_plane(stage - 1)
    grad_input, shared0 = run(
        part(last_step, lower),
        "last_step",
        ((summed[: 2 * batches],), grad_out0, grad_u0, ordered, norm0, norms),
        (flat, shared),
        (((width // LANES, rows, LANES), f32),),
        scalars=0,
    )
    small_sum = summed[CHUNKS:].reshape(2, CHUNKS, width)
    _, pullback = jax.vjp(discretize, lam_re, lam_im, log_step)
    grad_lr, grad_li, grad_ls = pullback(tuple(small_sum[:, kind, :half] for kind in range(4)))
    grad_input, grad_lr, grad_li, grad_ls = wait_for(
        upper_sum, lower_sum, grad_input, grad_lr, grad_li, grad_ls
    )

    lower_sum.middle()
    lower_sum.gather_depth()
    upper_sum.up_plane(0)
    own1 = upper_sum.parts[0]
    own1, lower_sum.parts = lax.optimization_barrier((own1, lower_sum.parts))
    other1 = swap(own1, "seq", 1)
    final = (((2, width, width), f32), ((2, 2 * half, width), f32), ((2, width, 2 * half), f32))
    lower_sum.up_split()
    lower_sum.swap_plane(len(lower_sum.plane) - 1)
    placed = put_in_place(1, here, ((False, own1), (True, other1)), final, ())
    placed = wait_for(lower_sum, *placed)
    own0 = lower_sum.back()
    other0 = swap(own0, "seq", 1)
    placed = put_in_place(0, here, ((False, own0),), final, placed, 4)
    grad_w, grad_c, grad_b = put_in_place(0, here, ((True, other0),), final, placed, 4)
    both = jnp.stack([shared0, shared1])
    shape = block_in.shape
    return (
        block_out.reshape(shape), grad_input.reshape(shape), both[:, 0], both[:, 1],
        grad_ls, grad_lr, grad_li, grad_b, grad_c, small_sum[:, 4], grad_w,
    )


def solution(mesh):
    split = P(None, "dp", "seq", None)
    return jax.shard_map(
        per_device,
        mesh=mesh,
        in_specs=(split, split, P(None, "dp", None)) + (P(),) * 9,
        out_specs=(split, split) + (P(),) * 9,
        check_vma=False,
    )
```

```python
import functools

import jax
import jax.numpy as jnp
from jax import lax
from jax.experimental import pallas as pl
from jax.experimental.pallas import tpu as pltpu
from jax.sharding import PartitionSpec as P

f32, bf16 = jnp.float32, jnp.bfloat16
epsilon = 1e-05
tanh_scale = 0.7978845608028654
cubic_term = 0.044715
LANES = 128
CHUNKS = 8
ROWS = 32
VMEM_LIMIT = 16 * 1024 * 1024


def dot(left, right, contract=(1, 0)):
    return lax.dot_general(
        left, right, (((contract[0],), (contract[1],)), ((), ())), preferred_element_type=f32
    )


def reorder(span, inverse):
    shape = (span, span)
    kept, moved = (1, 0) if inverse else (0, 1)
    row = lax.broadcasted_iota(jnp.int32, shape, kept)
    position = lax.broadcasted_iota(jnp.int32, shape, moved)
    source = (row & (CHUNKS - 1)) * (span // CHUNKS) + (row >> 3)
    return jnp.where(position == source, 1.0, 0.0).astype(bf16)


def row_loop(count, body, init=0, step=ROWS):
    def one(index, carry):
        return body(pl.multiple_of(index * step, step), carry)

    return lax.fori_loop(0, count // step, one, init)


def documents(here, batches, span, count):
    mine = here[0]
    first = mine * span
    out = []
    for batch in range(batches):
        begins, ends, so_far = [], [], 0
        docs = (here.shape[0] - 2) // batches
        for doc in range(docs):
            begins.append(so_far)
            so_far = so_far + here[2 + batch * docs + doc]
            ends.append(so_far)
        before, after = 0, 2 * count * span
        for begin, end in zip(begins, ends):
            before = jnp.maximum(before, jnp.where(begin < first, begin, 0))
            after = jnp.minimum(after, jnp.where(end > first + span, end, 2 * count * span))
        after = jnp.where(mine == count - 1, 0, after)
        out.append(begins + ends + [before, after, first, mine])
    return out


def place_documents(cfg, place):
    layer, reverse, batches, span, groups, tokens, count = cfg
    return documents(place, batches, span, count)


def keep_of(meta, batch, base, step, backward):
    docs = (len(meta[batch]) - 4) // 2
    off = docs if backward else 0
    late = 1 if backward else 0
    stop = base == meta[batch][off] - step - late
    for doc in range(1, docs):
        stop = jnp.logical_or(stop, base == meta[batch][off + doc] - step - late)
    return jnp.where(stop, 0.0, 1.0)


def base_positions(meta, steps):
    return meta[0][-2] + lax.broadcasted_iota(jnp.int32, (CHUNKS, LANES), 0) * steps


def lanes_of(index, half=0):
    return slice(half + index * LANES, half + (index + 1) * LANES)


def coef_tiles(value, groups):
    return [
        tuple(jnp.broadcast_to(part[:, lanes_of(q)], (CHUNKS, LANES)) for part in value)
        for q in range(groups)
    ]


def constants(disc, layer):
    dec_re, dec_im, inj_re, inj_im = (part[layer : layer + 1, :] for part in disc)
    return (dec_re, dec_im), (inj_re, inj_im)


def times(a, b):
    return (a[0] * b[0] - a[1] * b[1], a[0] * b[1] + a[1] * b[0])


def power(value, exponent):
    for _ in range(exponent.bit_length() - 1):
        value = times(value, value)
    return value


def conj(value):
    return (value[0], -value[1])


def scan(meta, source, inject, dec, batches, span, groups, reverse, masks_reverse, init, extra, visit):
    steps = span // CHUNKS
    half = groups * LANES
    base = base_positions(meta, steps)

    def pair(index, carry):
        states, more = carry
        states = list(states)
        first = steps - 2 - 2 * index if reverse else 2 * index
        start = pl.multiple_of(first * CHUNKS, 2 * CHUNKS)
        order = (1, 0) if reverse else (0, 1)
        for batch in range(batches):
            keeps = [keep_of(meta, batch, base, first + j, masks_reverse) for j in (0, 1)]
            for q in range(groups):
                rows = pl.ds(batch * span + start, 2 * CHUNKS)
                src_re = source[rows, lanes_of(q)]
                src_im = source[rows, lanes_of(q, half)]
                state = states[batch * groups + q]
                found = [None, None]
                for j in order:
                    part = (
                        src_re[j * CHUNKS : (j + 1) * CHUNKS],
                        src_im[j * CHUNKS : (j + 1) * CHUNKS],
                    )
                    push = times(inject[q], part) if inject is not None else part
                    held = times((keeps[j] * dec[q][0], keeps[j] * dec[q][1]), state)
                    state = (held[0] + push[0], held[1] + push[1])
                    found[j] = state
                states[batch * groups + q] = state
                more = visit(more, batch, q, first, start, found, (src_re, src_im))
            more = visit(more, batch, None, first, start, keeps, None)
        return tuple(states), more

    return lax.fori_loop(0, steps // 2, pair, (tuple(init), extra), unroll=2)


def zero_states(batches, groups):
    zero = jnp.zeros((CHUNKS, LANES), f32)
    return [(zero, zero)] * (batches * groups)


def local_ends(meta, source, inject, dec, batches, span, groups, reverse, prefix, total):
    ones = tuple(jnp.ones((CHUNKS, LANES), f32) for _ in range(batches))

    def visit(more, batch, q, first, start, found, src):
        if q is not None:
            return more
        return tuple(
            value * found[0] * found[1] if at == batch else value for at, value in enumerate(more)
        )

    dec_chunk = coef_tiles(power(dec, span // CHUNKS), groups)
    ends, kept = scan(
        meta, source, inject, coef_tiles(dec, groups), batches, span, groups, reverse, reverse,
        zero_states(batches, groups), ones, visit,
    )
    half = groups * LANES
    row = lax.broadcasted_iota(jnp.int32, (CHUNKS, LANES), 0)
    for batch in range(batches):
        for q in range(groups):
            end = ends[batch * groups + q]
            decay = (kept[batch] * dec_chunk[q][0], kept[batch] * dec_chunk[q][1])
            for shift in (1, 2, 4):
                turn = CHUNKS - shift if reverse else shift
                valid = row < CHUNKS - shift if reverse else row >= shift
                before = [pltpu.roll(value, turn, 0) for value in (*end, *decay)]
                from_before = times(decay, (before[0], before[1]))
                end = (
                    end[0] + jnp.where(valid, from_before[0], 0.0),
                    end[1] + jnp.where(valid, from_before[1], 0.0),
                )
                longer = times(decay, (before[2], before[3]))
                decay = (
                    jnp.where(valid, longer[0], decay[0]),
                    jnp.where(valid, longer[1], decay[1]),
                )
            rows = slice(batch * CHUNKS, (batch + 1) * CHUNKS)
            prefix[0, rows, lanes_of(q)] = end[0]
            prefix[0, rows, lanes_of(q, half)] = end[1]
            prefix[1, rows, lanes_of(q)] = decay[0]
            prefix[1, rows, lanes_of(q, half)] = decay[1]
            last = 0 if reverse else CHUNKS - 1
            total[batch : batch + 1, lanes_of(q)] = end[0][last : last + 1]
            total[batch : batch + 1, lanes_of(q, half)] = end[1][last : last + 1]


def chunk_carries(meta, gathered, dec, prefix, batches, span, groups, reverse):
    count = gathered.shape[0]
    half = groups * LANES
    dec_span = power(dec, span)
    row = lax.broadcasted_iota(jnp.int32, (CHUNKS, LANES), 0)
    mine = meta[0][-1]
    out = []
    for batch in range(batches):

        def add(at, so_far, batch=batch):
            away = count - 2 - at
            if reverse:
                other = mine + 1 + away
                reaches = meta[batch][-3] > other * span
            else:
                other = mine - 1 - away
                reaches = meta[batch][-4] < (mine - away) * span
            other = jnp.clip(other, 0, count - 1)
            value = jnp.where(reaches, gathered[other, pl.ds(batch, 1), :], 0.0)
            moved = times(dec_span, so_far)
            return (moved[0] + value[:, :half], moved[1] + value[:, half:])

        zero = jnp.zeros((1, half), f32)
        enter = lax.fori_loop(0, count - 1, add, (zero, zero), unroll=count <= 8)
        rows = slice(batch * CHUNKS, (batch + 1) * CHUNKS)
        for q in range(groups):
            own = tuple(jnp.broadcast_to(part[:, lanes_of(q)], (CHUNKS, LANES)) for part in enter)
            end = (prefix[0, rows, lanes_of(q)], prefix[0, rows, lanes_of(q, half)])
            decay = (prefix[1, rows, lanes_of(q)], prefix[1, rows, lanes_of(q, half)])
            moved = times(decay, own)
            turn, first = (CHUNKS - 1, CHUNKS - 1) if reverse else (1, 0)
            out.append(
                tuple(
                    jnp.where(row == first, own[i], pltpu.roll(end[i] + moved[i], turn, 0))
                    for i in (0, 1)
                )
            )
    return out


def add_sums(target, batches, sums):
    for kind, per_batch in enumerate(sums):
        for batch in range(batches):
            target[kind * batches + batch : kind * batches + batch + 1, :] = jnp.sum(
                per_batch[batch], axis=0, keepdims=True
            )


def fold(value):
    return sum(value[i : i + CHUNKS] for i in range(CHUNKS, value.shape[0], CHUNKS)) + value[:CHUNKS]


def first_sums(batches, span, x, ordered, stats):
    turn = reorder(span, False)
    width = x.shape[1]
    sums, squares = [], []
    for batch in range(batches):
        rows = slice(batch * span, (batch + 1) * span)
        ordered[rows, :] = dot(turn, x[rows, :]).astype(bf16)

        def body(start, carry, batch=batch):
            value = x[pl.ds(batch * span + start, ROWS), :].astype(f32)
            return carry[0] + fold(value), carry[1] + fold(value * value)

        zero = jnp.zeros((CHUNKS, width), f32)
        one, two = row_loop(span, body, (zero, zero))
        sums.append(one)
        squares.append(two)
    add_sums(stats, batches, (sums, squares))


def enter_layer(
    cfg, place, stats, hidden, norms, disc, b_proj, u, drive, prefix, total, norm
):
    layer, reverse, batches, span, groups, tokens, count = cfg
    sums = sum(part[...] for part in stats)
    average = sums[:batches] / tokens
    spread = sums[batches:] / tokens - average * average
    scale = lax.rsqrt(spread + epsilon)
    norm[:batches, :] = average
    norm[batches:, :] = scale
    gain_now, shift_now = norms[layer : layer + 1, :], norms[layer + 2 : layer + 3, :]
    for batch in range(batches):

        def body(start, carry, batch=batch):
            rows = pl.ds(batch * span + start, ROWS)
            normed = (hidden[rows, :].astype(f32) - average[batch : batch + 1]) * scale[
                batch : batch + 1
            ]
            u[rows, :] = (normed * gain_now + shift_now).astype(bf16)
            return carry

        row_loop(span, body)
    drive[...] = dot(u[...], b_proj[layer])
    meta = place_documents(cfg, place)
    dec, inj = constants(disc, layer)
    local_ends(
        meta, drive, coef_tiles(inj, groups), dec, batches, span, groups, reverse, prefix, total
    )


def finish_states(cfg, meta, ends, prefix, disc, drive, states, states_low):
    layer, reverse, batches, span, groups, tokens, count = cfg
    half = groups * LANES
    padded = span + CHUNKS
    dec, inj = constants(disc, layer)
    init = chunk_carries(meta, ends, dec, prefix, batches, span, groups, reverse)
    for batch in range(batches):
        edge = batch * padded + (span if reverse else 0)
        for q in range(groups):
            states[edge : edge + CHUNKS, lanes_of(q)] = init[batch * groups + q][0]
            states[edge : edge + CHUNKS, lanes_of(q, half)] = init[batch * groups + q][1]

    def visit(more, batch, q, first, start, found, src):
        if q is not None:
            for part, off in ((0, 0), (1, half)):
                both = jnp.concatenate([found[0][part], found[1][part]], axis=0)
                at = batch * padded + (0 if reverse else CHUNKS)
                states[pl.ds(at + start, 2 * CHUNKS), lanes_of(q, off)] = both
                states_low[pl.ds(batch * span + start, 2 * CHUNKS), lanes_of(q, off)] = both.astype(
                    bf16
                )
        return more

    scan(
        meta, drive, coef_tiles(inj, groups), coef_tiles(dec, groups), batches, span, groups,
        reverse, reverse, init, 0, visit,
    )


def forward_finish(
    cfg, meta, ends, prefix, disc, drive, u, hidden, c_proj, norms, w_gate,
    states, states_low, act, sig, slope, result, wide, emit,
):
    layer, reverse, batches, span, groups, tokens, count = cfg
    finish_states(cfg, meta, ends, prefix, disc, drive, states, states_low)
    wide[...] = dot(states_low[...], c_proj[layer])
    skip = norms[layer + 4 : layer + 5, :]

    def body(start, carry):
        rows = pl.ds(start, ROWS)
        mixed = wide[rows, :] + skip * u[rows, :].astype(f32)
        square = mixed * mixed
        th = jnp.tanh(tanh_scale * (mixed + cubic_term * square * mixed))
        half_one = 0.5 * (1.0 + th)
        act[rows, :] = (mixed * half_one).astype(bf16)
        slope[rows, :] = half_one + 0.5 * mixed * (1.0 - th * th) * tanh_scale * (
            1.0 + 3.0 * cubic_term * square
        )
        return carry

    row_loop(batches * span, body)
    wide[...] = dot(act[...], w_gate[layer])
    sums, squares = [], []
    for batch in range(batches):

        def gate(start, carry, batch=batch):
            rows = pl.ds(batch * span + start, ROWS)
            sig_now = 0.5 + 0.5 * jnp.tanh(0.5 * wide[rows, :])
            sig[rows, :] = sig_now
            value = hidden[rows, :].astype(f32) + act[rows, :].astype(f32) * sig_now
            result[rows, :] = value.astype(result.dtype)
            if emit is None:
                return carry
            return carry[0] + fold(value), carry[1] + fold(value * value)

        zero = jnp.zeros((CHUNKS, wide.shape[1]), f32)
        one, two = row_loop(span, gate, (zero, zero))
        sums.append(one)
        squares.append(two)
    if emit is not None:
        add_sums(emit, batches, (sums, squares))


def backward_start(
    cfg, meta, grad_out, disc, u, c_proj, w_gate, states_low, act, sig, slope,
    grad_gate, grad_mixed, grad_low, source, prefix, total, grad_d, wide,
):
    layer, reverse, batches, span, groups, tokens, count = cfg

    def body(start, carry):
        rows = pl.ds(start, ROWS)
        sig_now = sig[rows, :]
        grad_gate[rows, :] = (
            grad_out[rows, :].astype(f32) * act[rows, :].astype(f32) * sig_now * (1.0 - sig_now)
        ).astype(bf16)
        return carry

    row_loop(batches * span, body)
    wide[...] = dot(grad_gate[...], w_gate[layer], (1, 1))

    def mixed(start, carry):
        rows = pl.ds(start, ROWS)
        value = (grad_out[rows, :].astype(f32) * sig[rows, :] + wide[rows, :]) * slope[rows, :]
        grad_mixed[rows, :] = value
        grad_low[rows, :] = value.astype(bf16)
        return carry + fold(value * u[rows, :].astype(f32))

    gd = row_loop(batches * span, mixed, jnp.zeros((CHUNKS, wide.shape[1]), f32))
    grad_d[...] = jnp.sum(gd, axis=0, keepdims=True)
    source[...] = dot(grad_low[...], c_proj[layer], (1, 1))
    local_ends(
        meta, source, None, conj(constants(disc, layer)[0]), batches, span, groups, not reverse,
        prefix, total,
    )


def middle_forward(
    cfg, place, ends, prefix, disc, drive, u, hidden, c_proj, norms, w_gate,
    states, states_low, act, sig, slope, result, stats, wide,
):
    meta = place_documents(cfg, place)
    forward_finish(
        cfg, meta, ends, prefix, disc, drive, u, hidden, c_proj, norms, w_gate,
        states, states_low, act, sig, slope, result, wide, stats,
    )


def turn_around(
    cfg, place, ends, prefix, disc, drive, u, hidden, c_proj, norms, w_gate, cotangent,
    block_out, ordered_cot, states, states_low, act, grad_gate, grad_mixed, grad_low, source,
    back_prefix, total, grad_d, sig, slope, wide, result,
):
    layer, reverse, batches, span, groups, tokens, count = cfg
    meta = place_documents(cfg, place)
    turn, back = reorder(span, False), reorder(span, True)
    for batch in range(batches):
        rows = slice(batch * span, (batch + 1) * span)
        ordered_cot[rows, :] = dot(turn, cotangent[rows, :]).astype(bf16)
    forward_finish(
        cfg, meta, ends, prefix, disc, drive, u, hidden, c_proj, norms, w_gate,
        states, states_low, act, sig, slope, result, wide, None,
    )
    for batch in range(batches):
        rows = slice(batch * span, (batch + 1) * span)
        block_out[rows, :] = dot(back, result[rows, :]).astype(bf16)
    backward_start(
        cfg, meta, ordered_cot, disc, u, c_proj, w_gate, states_low, act, sig, slope,
        grad_gate, grad_mixed, grad_low, source, back_prefix, total, grad_d, wide,
    )


def backward_finish(
    cfg, place, ends, prefix, disc, source, drive, states, u, grad_mixed, grad_d, hidden, norm,
    norms, b_proj, grad_proj, grad_u, stats, small,
):
    layer, reverse, batches, span, groups, tokens, count = cfg
    half = groups * LANES
    padded = span + CHUNKS
    steps = span // CHUNKS
    meta = place_documents(cfg, place)
    dec, inj = constants(disc, layer)
    dec = conj(dec)
    init = chunk_carries(meta, ends, dec, prefix, batches, span, groups, not reverse)
    inj = coef_tiles(inj, groups)
    base = base_positions(meta, steps)
    zero = jnp.zeros((CHUNKS, LANES), f32)

    def visit(more, batch, q, first, start, found, src):
        if q is None:
            return more
        more = list(more)
        rows = pl.ds(batch * span + start, 2 * CHUNKS)
        drive_re, drive_im = drive[rows, lanes_of(q)], drive[rows, lanes_of(q, half)]
        before = pl.ds(batch * padded + start + (CHUNKS if reverse else 0), 2 * CHUNKS)
        prior_re, prior_im = states[before, lanes_of(q)], states[before, lanes_of(q, half)]
        dec_re, dec_im, inj_re, inj_im = more[q]
        out_re, out_im = [], []
        for j in (0, 1):
            part = slice(j * CHUNKS, (j + 1) * CHUNKS)
            adj_re, adj_im = found[j]
            keep = keep_of(meta, batch, base, first + j, reverse)
            kept_re, kept_im = keep * adj_re, keep * adj_im
            dec_re = dec_re + kept_re * prior_re[part] + kept_im * prior_im[part]
            dec_im = dec_im + kept_im * prior_re[part] - kept_re * prior_im[part]
            inj_re = inj_re + adj_re * drive_re[part] + adj_im * drive_im[part]
            inj_im = inj_im + adj_im * drive_re[part] - adj_re * drive_im[part]
            out_re.append(inj[q][0] * adj_re + inj[q][1] * adj_im)
            out_im.append(inj[q][0] * adj_im - inj[q][1] * adj_re)
        grad_proj[rows, lanes_of(q)] = jnp.concatenate(out_re, axis=0).astype(bf16)
        grad_proj[rows, lanes_of(q, half)] = jnp.concatenate(out_im, axis=0).astype(bf16)
        more[q] = (dec_re, dec_im, inj_re, inj_im)
        return tuple(more)

    _, sums = scan(
        meta, source, None, coef_tiles(dec, groups), batches, span, groups,
        not reverse, not reverse, init, ((zero,) * 4,) * groups, visit,
    )
    small[...] = jnp.zeros_like(small)
    for q in range(groups):
        for kind in range(4):
            small[kind : kind + 1, lanes_of(q)] = jnp.sum(sums[q][kind], axis=0, keepdims=True)
    small[4:5, :] = grad_d[...]
    grad_u[...] = dot(grad_proj[...], b_proj[layer], (1, 1))
    skip = norms[layer + 4 : layer + 5, :]
    plain, times_normed = [], []
    for batch in range(batches):
        average = norm[batch : batch + 1, :]
        scale = norm[batches + batch : batches + batch + 1, :]

        def body(start, carry, batch=batch, average=average, scale=scale):
            rows = pl.ds(batch * span + start, ROWS)
            value = grad_u[rows, :] + grad_mixed[rows, :] * skip
            grad_u[rows, :] = value
            normed = (hidden[rows, :].astype(f32) - average) * scale
            return carry[0] + fold(value), carry[1] + fold(value * normed)

        zero_sum = jnp.zeros((CHUNKS, grad_u.shape[1]), f32)
        one, two = row_loop(span, body, (zero_sum, zero_sum))
        plain.append(one)
        times_normed.append(two)
    add_sums(stats, batches, (plain, times_normed))


def backward_finish_last(cfg, *refs):
    ins, before, (grad_proj, grad_u, sums) = refs[:-4], refs[-4], refs[-3:]
    sums[...] = jnp.zeros_like(sums)
    sums[2 * CHUNKS :, :] = before[...]
    backward_finish(
        cfg, *ins, grad_proj, grad_u, sums.at[pl.ds(0, CHUNKS)], sums.at[pl.ds(CHUNKS, CHUNKS)]
    )


def norm_backward(cfg, stats, grad_out, grad_u, hidden, norm, norms, store, shared):
    layer, reverse, batches, span, groups, tokens, count = cfg
    sums = sum(part[...] for part in stats)
    shared[0:1, :] = jnp.sum(sums[batches:], axis=0, keepdims=True)
    shared[1:2, :] = jnp.sum(sums[:batches], axis=0, keepdims=True)
    gain_now = norms[layer : layer + 1, :]
    for batch in range(batches):
        average = norm[batch : batch + 1, :]
        scale = norm[batches + batch : batches + batch + 1, :]
        plain = gain_now * sums[batch : batch + 1] / tokens
        slanted = gain_now * sums[batches + batch : batches + batch + 1] / tokens

        def body(start, carry, batch=batch, average=average, scale=scale, plain=plain, slanted=slanted):
            rows = pl.ds(batch * span + start, ROWS)
            normed = (hidden[rows, :].astype(f32) - average) * scale
            value = grad_out[rows, :].astype(f32) + scale * (
                grad_u[rows, :] * gain_now - plain - normed * slanted
            )
            store(rows, value)
            return carry

        row_loop(span, body)


def between_layers(
    cfg, lower, place, stats, upper_out, upper_u, upper_hidden, upper_norm, norms,
    disc, u, c_proj, w_gate, states_low, act, sig, slope,
    grad_out, shared, grad_gate, grad_mixed, grad_low, source, prefix, total, grad_d, wide,
):
    def store(rows, value):
        grad_out[rows, :] = value

    norm_backward(cfg, stats, upper_out, upper_u, upper_hidden, upper_norm, norms, store, shared)
    meta = place_documents(lower, place)
    backward_start(
        lower, meta, grad_out, disc, u, c_proj, w_gate, states_low, act, sig, slope,
        grad_gate, grad_mixed, grad_low, source, prefix, total, grad_d, wide,
    )


def last_step(cfg, stats, grad_out, grad_u, hidden, norm, norms, target, shared, ordered):
    layer, reverse, batches, span, groups, tokens, count = cfg
    planes = target.shape[1] // LANES

    def store(rows, value):
        for plane in range(planes):
            ordered[plane, rows, :] = value[:, lanes_of(plane)]

    norm_backward(cfg, stats, grad_out, grad_u, hidden, norm, norms, store, shared)
    steps = span // CHUNKS
    for batch in range(batches):
        for chunk in range(CHUNKS):
            at = batch * span
            for plane in range(planes):
                target[at + chunk * steps : at + (chunk + 1) * steps, lanes_of(plane)] = ordered[
                    plane, pl.ds(at + chunk, steps, stride=CHUNKS), :
                ]


def half_weights(core, refs, own, sent):
    for target, half in ((own, core), (sent, 1 - core)):
        at = 0
        for left, right in refs:
            rows = left.shape[1] // 2
            cols = pl.ds(pl.multiple_of(half * rows, LANES), rows)
            target[at : at + rows, :] = dot(left[:, cols], right[...], (0, 0))
            at += rows


def all_weights(here, act, grad_gate, states_low, grad_low, grad_proj, u, own, sent):
    refs = ((act, grad_gate), (states_low, grad_low), (grad_proj, u))
    half_weights(lax.rem(here[0], 2), refs, own, sent)


def gate_weights(here, act, grad_gate, states_low, grad_low, own, sent):
    half_weights(lax.rem(here[0], 2), ((act, grad_gate), (states_low, grad_low)), own, sent)


def input_weights(here, grad_proj, u, own, sent):
    half_weights(lax.rem(here[0], 2), ((grad_proj, u),), own, sent)


def run(body, name, args, outs, scratch=(), scalars=1):
    vmem, smem = pl.BlockSpec(memory_space=pltpu.VMEM), pl.BlockSpec(memory_space=pltpu.SMEM)
    specs = tuple(
        jax.tree.map(lambda _, at=at: smem if at < scalars else vmem, arg)
        for at, arg in enumerate(args)
    )
    return pl.pallas_call(
        body,
        name=name,
        out_shape=tuple(jax.ShapeDtypeStruct(*out) for out in outs),
        in_specs=specs,
        out_specs=(vmem,) * len(outs),
        scratch_shapes=[pltpu.VMEM(*entry) for entry in scratch],
        compiler_params=pltpu.CompilerParams(vmem_limit_bytes=VMEM_LIMIT),
    )(*args)


def put_in_place(layer, here, halves, outs, before, pieces=1):
    width, states = outs[0][0][1], outs[1][0][1]
    rows_w, rows_c = width // 2, states // 2
    vmem, count = pl.BlockSpec(memory_space=pltpu.VMEM), len(halves)

    def half(step, here):
        core = lax.rem(here[0], 2)
        spots = [1 - core if other else core for other, _ in halves]
        return spots[0] if count == 1 else jnp.where(step == 0, *spots)

    blocks = (
        pl.BlockSpec((1, rows_w, width), lambda i, here: (layer, half(i, here), 0)),
        pl.BlockSpec((1, rows_c, width), lambda i, here: (layer, half(i, here), 0)),
        pl.BlockSpec((1, width, rows_c), lambda i, here: (layer, 0, half(i, here))),
    )

    def body(here, *refs):
        grad_w, grad_c, grad_b = refs[-3:]
        for now in range(count):

            @pl.when(pl.program_id(0) == now)
            def _(source=refs[now]):
                gates, inputs = (rows_w + rows_c) // pieces, rows_c // pieces
                columns = []
                for piece in range(pieces):
                    at, row = piece * (gates + inputs), piece * gates
                    turn = min(max(rows_w - row, 0), gates)
                    if turn:
                        grad_w[0, row : row + turn, :] = source[at : at + turn, :]
                    if turn < gates:
                        to = row + turn - rows_w
                        grad_c[0, to : to + gates - turn, :] = source[at + turn : at + gates, :]
                    columns.append(source[at + gates : at + gates + inputs, :])
                grad_b[0] = jnp.concatenate(columns, axis=0).T

    return pl.pallas_call(
        body,
        name="put_in_place",
        out_shape=tuple(jax.ShapeDtypeStruct(*out) for out in outs),
        grid_spec=pltpu.PrefetchScalarGridSpec(
            num_scalar_prefetch=1,
            grid=(count,),
            in_specs=[vmem] * count + [pl.BlockSpec(memory_space=pl.ANY)] * len(before),
            out_specs=blocks,
        ),
        input_output_aliases={1 + count + i: i for i in range(len(before))},
        compiler_params=pltpu.CompilerParams(vmem_limit_bytes=VMEM_LIMIT),
    )(here, *(rows for _, rows in halves), *before)


def axis_parts():
    count, depth = lax.axis_size("seq"), lax.axis_size("dp")
    return (("seq", 2, 1, count), ("seq", count // 2, 2, count), ("dp", depth, 1, depth))


def shifted(value, part, away):
    name, size, stride, count = part
    pairs = []
    for i in range(count):
        place = (i // stride) % size
        pairs.append((i, i + ((place + away) % size - place) * stride))
    return lax.ppermute(value, name, pairs)


def add_by_shifts(value, parts, *earlier):
    for number, part in enumerate(parts):
        if number:
            value = sum(terms[1:], terms[0])
        if number == len(parts) - 1:
            value, *earlier = lax.optimization_barrier((value, *earlier))
        terms = [value] + [shifted(value, part, away) for away in range(1, part[1])]
    return terms, *earlier


def bits_of(size, stride=1):
    bits = []
    while size > 1:
        bits.append(stride)
        size, stride = size // 2, stride * 2
    return bits


def plane_bits():
    chip_bits = bits_of(lax.axis_size("seq") // 2, 2)
    middle = (len(chip_bits) + 1) // 2
    inner, outer = chip_bits[:middle], chip_bits[middle:]
    return list(zip(inner + outer, outer + inner))


def swap(value, axis, bit):
    return lax.ppermute(value, axis, [(i, i ^ bit) for i in range(lax.axis_size(axis))])


def bit_at(here, axis, bit):
    return lax.rem(lax.div(here[0 if axis == "seq" else 1], bit), 2)


def rows_at(half, rows):
    return pl.ds(pl.multiple_of(half * rows, CHUNKS), rows)


def fold_cores(bits, here, *refs):
    terms, targets = refs[:-4], refs[-4:]
    rows, cols = targets[0].shape
    for side in (0, 1):
        kept, sent = targets[2 * side : 2 * side + 2]
        where = slice(side * cols, (side + 1) * cols)
        bit = bit_at(here, "seq", bits[side])
        for half in (0, 1):

            @pl.when(bit == half)
            def _(half=half, kept=kept, sent=sent, where=where):
                start = 0
                for own, found in zip(terms[0::2], terms[1::2]):
                    for part, target in ((half, kept), (1 - half, sent)):
                        low = max(start, part * rows)
                        high = min(start + own.shape[0], (part + 1) * rows)
                        if low < high:
                            source = slice(low - start, high - start)
                            target[low - part * rows : high - part * rows, :] = (
                                own[source, where] + found[source, where]
                            )
                    start += own.shape[0]


def fold_sides(bits, here, *refs):
    targets, blocks = refs[-4:], refs[:-4]
    for side in (0, 1):
        kept, sent = targets[2 * side : 2 * side + 2]
        half, start = bit_at(here, "seq", bits[side]), 0
        for at in range(0, len(blocks), 4):
            own, found = blocks[at + 2 * side : at + 2 * side + 2]
            rows = own.shape[0] // 2
            to = slice(start, start + rows)
            kept[to, :] = own[rows_at(half, rows), :] + found[rows_at(half, rows), :]
            sent[to, :] = own[rows_at(1 - half, rows), :] + found[rows_at(1 - half, rows), :]
            start += rows


def fold_join(bit, here, left, found_left, right, found_right, kept, sent):
    rows, cols = kept.shape[0], left.shape[1]
    half = bit_at(here, "dp", bit)
    for side, (own, found) in enumerate(((left, found_left), (right, found_right))):
        where = slice(side * cols, (side + 1) * cols)
        kept[:, where] = own[rows_at(half, rows), :] + found[rows_at(half, rows), :]
        sent[:, where] = own[rows_at(1 - half, rows), :] + found[rows_at(1 - half, rows), :]


def fold_depth(bit, here, own, found, kept, sent):
    half, rows = bit_at(here, "dp", bit), kept.shape[0]
    kept[...] = own[rows_at(half, rows), :] + found[rows_at(half, rows), :]
    sent[...] = own[rows_at(1 - half, rows), :] + found[rows_at(1 - half, rows), :]


def add_two(own, found, out):
    out[...] = own[...] + found[...]


def unfold(bit, here, own, found, out):
    half, rows = bit_at(here, "dp", bit), own.shape[0]
    out[rows_at(half, rows), :] = own[...]
    out[rows_at(1 - half, rows), :] = found[...]


def unfold_split(bit, here, own, found, left, right):
    half, rows, cols = bit_at(here, "dp", bit), own.shape[0], left.shape[1]
    for side, out in enumerate((left, right)):
        where = slice(side * cols, (side + 1) * cols)
        out[rows_at(half, rows), :] = own[:, where]
        out[rows_at(1 - half, rows), :] = found[:, where]


def unfold_sides(bits, joined, here, *refs):
    for side in (0, 1):
        own, found = refs[2 * side : 2 * side + 2]
        half, (rows, cols) = bit_at(here, "seq", bits[side]), own.shape
        out = refs[4] if joined else refs[4 + side]
        where = slice(side * cols, (side + 1) * cols) if joined else slice(0, cols)
        out[rows_at(half, rows), where] = own[...]
        out[rows_at(1 - half, rows), where] = found[...]


def link_call(body, here, args, shapes):
    name = body.func.__name__
    return run(body, name, (here, *args), tuple((shape, f32) for shape in shapes))


class LinkSum:
    def __init__(self, here, terms):
        self.here, self.plane = here, plane_bits()
        self.depth = bits_of(lax.axis_size("dp"))
        rows = sum(term.shape[0] for term in terms[::2])
        self.shape = (rows // 2, terms[0].shape[1] // 2)
        self.parts = link_call(
            functools.partial(fold_cores, self.plane[0]), here, terms, (self.shape,) * 4
        )

    def swap_plane(self, stage):
        (left, right), pieces = self.plane[stage], self.parts
        self.parts = (
            pieces[0], swap(pieces[1], "seq", left), pieces[2], swap(pieces[3], "seq", right)
        )

    def down_plane(self, stage, *others):
        parts, rows, cols = list(self.parts), *self.shape
        for other in others:
            parts += other.parts
            rows += other.shape[0]
        self.shape = (rows // 2, cols)
        body = functools.partial(fold_sides, self.plane[stage])
        self.parts = link_call(body, self.here, parts, (self.shape,) * 4)

    def down_join(self):
        rows, cols = self.shape
        self.shape = (rows // 2, 2 * cols)
        body = functools.partial(fold_join, self.depth[0])
        self.parts = link_call(body, self.here, self.parts, (self.shape,) * 2)

    def swap_depth(self, stage):
        self.parts = (self.parts[0], swap(self.parts[1], "dp", self.depth[stage]))

    def down_depth(self, stage):
        rows, cols = self.shape
        self.shape = (rows // 2, cols)
        body = functools.partial(fold_depth, self.depth[stage])
        self.parts = link_call(body, self.here, self.parts, (self.shape,) * 2)

    def middle(self):
        (value,) = run(add_two, "add_two", self.parts, ((self.shape, f32),), scalars=0)
        self.parts = (value, value)

    def up_depth(self, stage):
        rows, cols = self.shape
        self.shape = (rows * 2, cols)
        body = functools.partial(unfold, self.depth[stage])
        (value,) = link_call(body, self.here, self.parts, (self.shape,))
        self.parts = (value, value)

    def up_split(self):
        rows, cols = self.shape
        self.shape = (rows * 2, cols // 2)
        body = functools.partial(unfold_split, self.depth[0])
        left, right = link_call(body, self.here, self.parts, (self.shape,) * 2)
        self.parts = (left, left, right, right)

    def up_plane(self, stage):
        rows, cols = self.shape
        if stage:
            self.shape = (rows * 2, cols)
            body = functools.partial(unfold_sides, self.plane[stage], False)
            left, right = link_call(body, self.here, self.parts, (self.shape,) * 2)
            self.parts = (left, left, right, right)
        else:
            self.shape = (rows * 2, cols * 2)
            body = functools.partial(unfold_sides, self.plane[stage], True)
            self.parts = link_call(body, self.here, self.parts, (self.shape,))

    def after(self, *values):
        self.parts, values = lax.optimization_barrier((self.parts, values))
        return values

    def to_depth(self):
        for stage in range(2, len(self.plane)):
            self.swap_plane(stage - 1)
            self.down_plane(stage)
        self.swap_plane(len(self.plane) - 1)

    def scatter_depth(self):
        for stage in range(len(self.depth) - 1):
            if stage:
                self.down_depth(stage)
            self.swap_depth(stage)

    def swap_whole(self):
        self.parts = (self.parts[0], swap(self.parts[0], "dp", self.depth[-1]))

    def gather_depth(self):
        for stage in range(len(self.depth) - 2, 0, -1):
            self.swap_depth(stage)
            self.up_depth(stage)
        self.swap_depth(0)


def wait_for(*things):
    sums = [thing for thing in things if isinstance(thing, LinkSum)]
    values = [thing for thing in things if not isinstance(thing, LinkSum)]
    parts, values = lax.optimization_barrier(([entry.parts for entry in sums], values))
    for entry, part in zip(sums, parts):
        entry.parts = part
    return values


def discretize(lam_re, lam_im, log_step):
    step_size = jnp.exp(log_step)
    decay_abs = jnp.exp(lam_re * step_size)
    rotation = lam_im * step_size
    dec_re = decay_abs * jnp.cos(rotation)
    dec_im = decay_abs * jnp.sin(rotation)
    denom_sq = lam_re * lam_re + lam_im * lam_im
    inj_re = ((dec_re - 1.0) * lam_re + dec_im * lam_im) / denom_sq
    inj_im = (dec_im * lam_re - (dec_re - 1.0) * lam_im) / denom_sq
    return (dec_re, dec_im, inj_re, inj_im)


def per_device(
    block_in, cotangent, doc_lengths, norm_gain, norm_shift, log_step, lam_re, lam_im,
    b_proj, c_proj, d_skip, w_gate,
):
    batches, seqs, span, width = block_in.shape
    assert seqs == 1 and span % (4 * CHUNKS) == 0 and span & (span - 1) == 0
    half = lam_re.shape[1]
    groups = half // LANES
    rows = batches * span
    count = lax.axis_size("seq")
    tokens = float(seqs * lax.axis_size("dp") * span * count)
    here = jnp.stack([lax.axis_index("seq"), lax.axis_index("dp")]).astype(jnp.int32)
    place = jnp.concatenate([here] + [doc_lengths[batch, 0] for batch in range(batches)])
    place, block_in = lax.optimization_barrier((place, block_in))
    here = place
    disc = discretize(lam_re, lam_im, log_step)

    x = block_in.reshape(rows, width)
    cot = cotangent.reshape(rows, width)
    lower = (0, False, batches, span, groups, tokens, count)
    upper = (1, True, batches, span, groups, tokens, count)
    part = functools.partial

    flat, low = ((rows, width), f32), ((rows, width), bf16)
    wide, wide_low = ((rows, 2 * half), f32), ((rows, 2 * half), bf16)
    padded = ((batches * (span + CHUNKS), 2 * half), f32)
    sums = ((2 * batches, width), f32)
    prefix = ((2, batches * CHUNKS, 2 * half), f32)
    total = ((batches, 2 * half), f32)
    line, shared = ((1, width), f32), ((2, width), f32)
    small = ((8, width), f32)

    def gather_row(value):
        return lax.all_gather(value, "seq")

    ordered, stats = run(
        part(first_sums, batches, span), "first_sums", (x,), (low, sums), scalars=0
    )
    norms = jnp.concatenate([norm_gain, norm_shift, d_skip], axis=0)

    def forward(cfg, hidden, stats):
        return run(
            part(enter_layer, cfg),
            "enter_layer",
            (place, stats, hidden, norms, disc, b_proj),
            (low, wide, prefix, total, sums),
        )

    links, plane, depth = axis_parts()
    u0, drive0, prefix0, total0, norm0 = forward(
        lower, ordered, add_by_shifts(stats, (links, plane, depth))[0]
    )
    states0, states_low0, act0, sig0, slope0, hidden1, stats = run(
        part(middle_forward, lower),
        "middle_forward",
        (place, gather_row(total0), prefix0, disc, drive0, u0, ordered, c_proj, norms, w_gate),
        (padded, wide_low, low, flat, flat, flat, sums),
        (flat,),
    )
    u1, drive1, prefix1, total1, norm1 = forward(
        upper, hidden1, add_by_shifts(stats, (links, plane, depth))[0]
    )
    (
        block_out, ordered_cot, states1, states_low1, act1, grad_gate1, grad_mixed1, grad_low1,
        source1, prefix1, total1, grad_d1,
    ) = run(
        part(turn_around, upper),
        "turn_around",
        (
            place, gather_row(total1), prefix1, disc, drive1, u1, hidden1, c_proj, norms, w_gate,
            cot,
        ),
        (low, low, padded, wide_low, low, low, flat, low, wide, prefix, total, line),
        (flat, flat, flat, low),
    )

    def halves(length):
        return (((length // 2, width), f32),) * 2

    grad_proj1, grad_u1, stats, small1 = run(
        part(backward_finish, upper),
        "backward_finish",
        (
            place, gather_row(total1), prefix1, disc, source1, drive1, states1, u1, grad_mixed1,
            grad_d1, hidden1, norm1, norms, b_proj,
        ),
        (wide_low, flat, sums, small),
    )
    sizes = (width + 2 * half, 2 * half)
    own1, sent1 = run(
        all_weights,
        "all_weights",
        (here, act1, grad_gate1, states_low1, grad_low1, grad_proj1, u1),
        halves(sum(sizes)),
    )
    stats = stats + swap(stats, "seq", 1)
    stats, sent1 = lax.optimization_barrier((stats, sent1))
    upper_sum = LinkSum(here, (own1, swap(sent1, "seq", 1)))
    stats, upper_sum.parts = add_by_shifts(stats, (plane, depth), upper_sum.parts)
    upper_sum.swap_plane(0)
    (
        grad_out0, shared1, grad_gate0, grad_mixed0, grad_low0, source0, prefix0, total0, grad_d0,
    ) = run(
        part(between_layers, upper, lower),
        "between_layers",
        (
            place, stats, ordered_cot, grad_u1, hidden1, norm1, norms,
            disc, u0, c_proj, w_gate, states_low0, act0, sig0, slope0,
        ),
        (flat, shared, low, flat, low, wide, prefix, total, line),
        (flat,),
    )
    (total0,) = upper_sum.after(total0)
    ends, grad_gate0 = lax.optimization_barrier((gather_row(total0), grad_gate0))
    own_gates, sent_gates = run(
        gate_weights, "gate_weights", (here, act0, grad_gate0, states_low0, grad_low0),
        halves(sizes[0]),
    )
    own_gates, ends = lax.optimization_barrier((own_gates, ends))
    grad_proj0, grad_u0, last_sums = run(
        part(backward_finish_last, lower),
        "backward_finish",
        (
            place, ends, prefix0, disc, source0, drive0, states0, u0, grad_mixed0, grad_d0,
            ordered, norm0, norms, b_proj, small1,
        ),
        (wide_low, flat, ((3 * CHUNKS, width), f32)),
    )
    own_inputs, sent_inputs = run(
        input_weights, "input_weights", (here, grad_proj0, u0), halves(sizes[1])
    )
    (own_inputs,) = upper_sum.after(own_inputs)
    upper_sum.down_plane(1)
    (own_gates,) = upper_sum.after(own_gates)
    upper_sum.to_depth()
    lower_sum = LinkSum(here, (own_gates, swap(sent_gates, "seq", 1)))
    lower_sum.swap_plane(0)
    inputs_sum = LinkSum(here, (own_inputs, swap(sent_inputs, "seq", 1)))
    wait_for(upper_sum, inputs_sum)
    inputs_sum.swap_plane(0)
    upper_sum.down_join()
    upper_sum.scatter_depth()
    wait_for(upper_sum, lower_sum, inputs_sum)

    lower_sum.down_plane(1, inputs_sum)
    lower_sum.to_depth()
    upper_sum.middle()
    upper_sum.swap_whole()
    lower_sum.down_join()
    (last_sums,) = lower_sum.after(last_sums)
    lower_sum.scatter_depth()
    last_sums = last_sums + swap(last_sums, "seq", 1)
    last_terms = [last_sums] + [shifted(last_sums, plane, away) for away in range(1, plane[1])]
    last_terms = wait_for(upper_sum, lower_sum, *last_terms)

    lower_sum.middle()
    lower_sum.swap_whole()
    upper_sum.middle()
    upper_sum.gather_depth()
    upper_sum.up_split()
    last_sums = sum(last_terms)
    last_terms = [last_sums] + [shifted(last_sums, depth, away) for away in range(1, depth[1])]
    last_terms = wait_for(upper_sum, lower_sum, *last_terms)

    lower_sum.middle()
    lower_sum.gather_depth()
    for stage in range(len(upper_sum.plane) - 1, 0, -1):
        upper_sum.swap_plane(stage)
        upper_sum.up_plane(stage)
    wait_for(upper_sum, lower_sum)

    lower_sum.up_split()
    wait_for(upper_sum, lower_sum)
    lower_sum.swap_plane(len(lower_sum.plane) - 1)
    upper_sum.swap_plane(0)
    for stage in range(len(lower_sum.plane) - 1, 0, -1):
        lower_sum.up_plane(stage)
        if stage == 1:
            wait_for(upper_sum, lower_sum)
        lower_sum.swap_plane(stage - 1)
    upper_sum.up_plane(0)
    own1 = upper_sum.parts[0]
    other1 = swap(own1, "seq", 1)
    summed = sum(last_terms)
    grad_input, shared0 = run(
        part(last_step, lower),
        "last_step",
        ((summed[: 2 * batches],), grad_out0, grad_u0, ordered, norm0, norms),
        (flat, shared),
        (((width // LANES, rows, LANES), f32),),
        scalars=0,
    )
    small_sum = summed[CHUNKS:].reshape(2, CHUNKS, width)
    _, pullback = jax.vjp(discretize, lam_re, lam_im, log_step)
    grad_lr, grad_li, grad_ls = pullback(tuple(small_sum[:, kind, :half] for kind in range(4)))
    final = (((2, width, width), f32), ((2, 2 * half, width), f32), ((2, width, 2 * half), f32))
    placed = put_in_place(1, here, ((False, own1), (True, other1)), final, ())
    grad_input, grad_lr, grad_li, grad_ls, *placed = wait_for(
        lower_sum, grad_input, grad_lr, grad_li, grad_ls, *placed
    )

    lower_sum.up_plane(0)
    own0 = lower_sum.parts[0]
    other0 = swap(own0, "seq", 1)
    placed = put_in_place(0, here, ((False, own0),), final, placed, 4)
    grad_w, grad_c, grad_b = put_in_place(0, here, ((True, other0),), final, placed, 4)
    both = jnp.stack([shared0, shared1])
    shape = block_in.shape
    return (
        block_out.reshape(shape), grad_input.reshape(shape), both[:, 0], both[:, 1],
        grad_ls, grad_lr, grad_li, grad_b, grad_c, small_sum[:, 4], grad_w,
    )


def solution(mesh):
    split = P(None, "dp", "seq", None)
    return jax.shard_map(
        per_device,
        mesh=mesh,
        in_specs=(split, split, P(None, "dp", None)) + (P(),) * 9,
        out_specs=(split, split) + (P(),) * 9,
        check_vma=False,
    )
```

```python
import functools

import jax
import jax.numpy as jnp
from jax import lax
from jax.experimental import pallas as pl
from jax.experimental.pallas import tpu as pltpu
from jax.sharding import PartitionSpec as P

f32, bf16 = jnp.float32, jnp.bfloat16
epsilon = 1e-05
tanh_scale = 0.7978845608028654
cubic_term = 0.044715
LANES = 128
CHUNKS = 8
ROWS = 32
VMEM_LIMIT = 16 * 1024 * 1024


def dot(left, right, contract=(1, 0)):
    return lax.dot_general(
        left, right, (((contract[0],), (contract[1],)), ((), ())), preferred_element_type=f32
    )


def reorder(span, inverse):
    shape = (span, span)
    kept, moved = (1, 0) if inverse else (0, 1)
    row = lax.broadcasted_iota(jnp.int32, shape, kept)
    position = lax.broadcasted_iota(jnp.int32, shape, moved)
    source = (row & (CHUNKS - 1)) * (span // CHUNKS) + (row >> 3)
    return jnp.where(position == source, 1.0, 0.0).astype(bf16)


def row_loop(count, body, init=0, step=ROWS):
    def one(index, carry):
        return body(pl.multiple_of(index * step, step), carry)

    return lax.fori_loop(0, count // step, one, init)


def documents(here, batches, span, count):
    mine = here[0]
    first = mine * span
    out = []
    for batch in range(batches):
        begins, ends, so_far = [], [], 0
        docs = (here.shape[0] - 2) // batches
        for doc in range(docs):
            begins.append(so_far)
            so_far = so_far + here[2 + batch * docs + doc]
            ends.append(so_far)
        before, after = 0, 2 * count * span
        for begin, end in zip(begins, ends):
            before = jnp.maximum(before, jnp.where(begin < first, begin, 0))
            after = jnp.minimum(after, jnp.where(end > first + span, end, 2 * count * span))
        after = jnp.where(mine == count - 1, 0, after)
        out.append(begins + ends + [before, after, first, mine])
    return out


def place_documents(cfg, place):
    layer, reverse, batches, span, groups, tokens, count = cfg
    return documents(place, batches, span, count)


def keep_of(meta, batch, base, step, backward):
    docs = (len(meta[batch]) - 4) // 2
    off = docs if backward else 0
    late = 1 if backward else 0
    stop = base == meta[batch][off] - step - late
    for doc in range(1, docs):
        stop = jnp.logical_or(stop, base == meta[batch][off + doc] - step - late)
    return jnp.where(stop, 0.0, 1.0)


def base_positions(meta, steps):
    return meta[0][-2] + lax.broadcasted_iota(jnp.int32, (CHUNKS, LANES), 0) * steps


def lanes_of(index, half=0):
    return slice(half + index * LANES, half + (index + 1) * LANES)


def coef_tiles(value, groups):
    return [
        tuple(jnp.broadcast_to(part[:, lanes_of(q)], (CHUNKS, LANES)) for part in value)
        for q in range(groups)
    ]


def constants(disc, layer):
    dec_re, dec_im, inj_re, inj_im = (part[layer : layer + 1, :] for part in disc)
    return (dec_re, dec_im), (inj_re, inj_im)


def times(a, b):
    return (a[0] * b[0] - a[1] * b[1], a[0] * b[1] + a[1] * b[0])


def power(value, exponent):
    for _ in range(exponent.bit_length() - 1):
        value = times(value, value)
    return value


def conj(value):
    return (value[0], -value[1])


def scan(meta, source, inject, dec, batches, span, groups, reverse, masks_reverse, init, extra, visit):
    steps = span // CHUNKS
    half = groups * LANES
    base = base_positions(meta, steps)

    def pair(index, carry):
        states, more = carry
        states = list(states)
        first = steps - 2 - 2 * index if reverse else 2 * index
        start = pl.multiple_of(first * CHUNKS, 2 * CHUNKS)
        order = (1, 0) if reverse else (0, 1)
        for batch in range(batches):
            keeps = [keep_of(meta, batch, base, first + j, masks_reverse) for j in (0, 1)]
            for q in range(groups):
                rows = pl.ds(batch * span + start, 2 * CHUNKS)
                src_re = source[rows, lanes_of(q)]
                src_im = source[rows, lanes_of(q, half)]
                state = states[batch * groups + q]
                found = [None, None]
                for j in order:
                    part = (
                        src_re[j * CHUNKS : (j + 1) * CHUNKS],
                        src_im[j * CHUNKS : (j + 1) * CHUNKS],
                    )
                    push = times(inject[q], part) if inject is not None else part
                    held = times((keeps[j] * dec[q][0], keeps[j] * dec[q][1]), state)
                    state = (held[0] + push[0], held[1] + push[1])
                    found[j] = state
                states[batch * groups + q] = state
                more = visit(more, batch, q, first, start, found, (src_re, src_im))
            more = visit(more, batch, None, first, start, keeps, None)
        return tuple(states), more

    return lax.fori_loop(0, steps // 2, pair, (tuple(init), extra), unroll=2)


def zero_states(batches, groups):
    zero = jnp.zeros((CHUNKS, LANES), f32)
    return [(zero, zero)] * (batches * groups)


def local_ends(meta, source, inject, dec, batches, span, groups, reverse, prefix, total):
    ones = tuple(jnp.ones((CHUNKS, LANES), f32) for _ in range(batches))

    def visit(more, batch, q, first, start, found, src):
        if q is not None:
            return more
        return tuple(
            value * found[0] * found[1] if at == batch else value for at, value in enumerate(more)
        )

    dec_chunk = coef_tiles(power(dec, span // CHUNKS), groups)
    ends, kept = scan(
        meta, source, inject, coef_tiles(dec, groups), batches, span, groups, reverse, reverse,
        zero_states(batches, groups), ones, visit,
    )
    half = groups * LANES
    row = lax.broadcasted_iota(jnp.int32, (CHUNKS, LANES), 0)
    for batch in range(batches):
        for q in range(groups):
            end = ends[batch * groups + q]
            decay = (kept[batch] * dec_chunk[q][0], kept[batch] * dec_chunk[q][1])
            for shift in (1, 2, 4):
                turn = CHUNKS - shift if reverse else shift
                valid = row < CHUNKS - shift if reverse else row >= shift
                before = [pltpu.roll(value, turn, 0) for value in (*end, *decay)]
                from_before = times(decay, (before[0], before[1]))
                end = (
                    end[0] + jnp.where(valid, from_before[0], 0.0),
                    end[1] + jnp.where(valid, from_before[1], 0.0),
                )
                longer = times(decay, (before[2], before[3]))
                decay = (
                    jnp.where(valid, longer[0], decay[0]),
                    jnp.where(valid, longer[1], decay[1]),
                )
            rows = slice(batch * CHUNKS, (batch + 1) * CHUNKS)
            prefix[0, rows, lanes_of(q)] = end[0]
            prefix[0, rows, lanes_of(q, half)] = end[1]
            prefix[1, rows, lanes_of(q)] = decay[0]
            prefix[1, rows, lanes_of(q, half)] = decay[1]
            last = 0 if reverse else CHUNKS - 1
            total[batch : batch + 1, lanes_of(q)] = end[0][last : last + 1]
            total[batch : batch + 1, lanes_of(q, half)] = end[1][last : last + 1]


def chunk_carries(meta, gathered, dec, prefix, batches, span, groups, reverse):
    count = gathered.shape[0]
    half = groups * LANES
    dec_span = power(dec, span)
    row = lax.broadcasted_iota(jnp.int32, (CHUNKS, LANES), 0)
    mine = meta[0][-1]
    out = []
    for batch in range(batches):

        def add(at, so_far, batch=batch):
            away = count - 2 - at
            if reverse:
                other = mine + 1 + away
                reaches = meta[batch][-3] > other * span
            else:
                other = mine - 1 - away
                reaches = meta[batch][-4] < (mine - away) * span
            other = jnp.clip(other, 0, count - 1)
            value = jnp.where(reaches, gathered[other, pl.ds(batch, 1), :], 0.0)
            moved = times(dec_span, so_far)
            return (moved[0] + value[:, :half], moved[1] + value[:, half:])

        zero = jnp.zeros((1, half), f32)
        enter = lax.fori_loop(0, count - 1, add, (zero, zero), unroll=count <= 8)
        rows = slice(batch * CHUNKS, (batch + 1) * CHUNKS)
        for q in range(groups):
            own = tuple(jnp.broadcast_to(part[:, lanes_of(q)], (CHUNKS, LANES)) for part in enter)
            end = (prefix[0, rows, lanes_of(q)], prefix[0, rows, lanes_of(q, half)])
            decay = (prefix[1, rows, lanes_of(q)], prefix[1, rows, lanes_of(q, half)])
            moved = times(decay, own)
            turn, first = (CHUNKS - 1, CHUNKS - 1) if reverse else (1, 0)
            out.append(
                tuple(
                    jnp.where(row == first, own[i], pltpu.roll(end[i] + moved[i], turn, 0))
                    for i in (0, 1)
                )
            )
    return out


def add_sums(target, batches, sums):
    for kind, per_batch in enumerate(sums):
        for batch in range(batches):
            target[kind * batches + batch : kind * batches + batch + 1, :] = jnp.sum(
                per_batch[batch], axis=0, keepdims=True
            )


def fold(value):
    return sum(value[i : i + CHUNKS] for i in range(CHUNKS, value.shape[0], CHUNKS)) + value[:CHUNKS]


def first_sums(batches, span, x, ordered, stats):
    turn = reorder(span, False)
    width = x.shape[1]
    sums, squares = [], []
    for batch in range(batches):
        rows = slice(batch * span, (batch + 1) * span)
        ordered[rows, :] = dot(turn, x[rows, :]).astype(bf16)

        def body(start, carry, batch=batch):
            value = x[pl.ds(batch * span + start, ROWS), :].astype(f32)
            return carry[0] + fold(value), carry[1] + fold(value * value)

        zero = jnp.zeros((CHUNKS, width), f32)
        one, two = row_loop(span, body, (zero, zero))
        sums.append(one)
        squares.append(two)
    add_sums(stats, batches, (sums, squares))


def enter_layer(
    cfg, place, stats, hidden, norms, disc, b_proj, u, drive, prefix, total, norm
):
    layer, reverse, batches, span, groups, tokens, count = cfg
    sums = sum(part[...] for part in stats)
    average = sums[:batches] / tokens
    spread = sums[batches:] / tokens - average * average
    scale = lax.rsqrt(spread + epsilon)
    norm[:batches, :] = average
    norm[batches:, :] = scale
    gain_now, shift_now = norms[layer : layer + 1, :], norms[layer + 2 : layer + 3, :]
    for batch in range(batches):

        def body(start, carry, batch=batch):
            rows = pl.ds(batch * span + start, ROWS)
            normed = (hidden[rows, :].astype(f32) - average[batch : batch + 1]) * scale[
                batch : batch + 1
            ]
            u[rows, :] = (normed * gain_now + shift_now).astype(bf16)
            return carry

        row_loop(span, body)
    drive[...] = dot(u[...], b_proj[layer])
    meta = place_documents(cfg, place)
    dec, inj = constants(disc, layer)
    local_ends(
        meta, drive, coef_tiles(inj, groups), dec, batches, span, groups, reverse, prefix, total
    )


def finish_states(cfg, meta, ends, prefix, disc, drive, states, states_low):
    layer, reverse, batches, span, groups, tokens, count = cfg
    half = groups * LANES
    padded = span + CHUNKS
    dec, inj = constants(disc, layer)
    init = chunk_carries(meta, ends, dec, prefix, batches, span, groups, reverse)
    for batch in range(batches):
        edge = batch * padded + (span if reverse else 0)
        for q in range(groups):
            states[edge : edge + CHUNKS, lanes_of(q)] = init[batch * groups + q][0]
            states[edge : edge + CHUNKS, lanes_of(q, half)] = init[batch * groups + q][1]

    def visit(more, batch, q, first, start, found, src):
        if q is not None:
            for part, off in ((0, 0), (1, half)):
                both = jnp.concatenate([found[0][part], found[1][part]], axis=0)
                at = batch * padded + (0 if reverse else CHUNKS)
                states[pl.ds(at + start, 2 * CHUNKS), lanes_of(q, off)] = both
                states_low[pl.ds(batch * span + start, 2 * CHUNKS), lanes_of(q, off)] = both.astype(
                    bf16
                )
        return more

    scan(
        meta, drive, coef_tiles(inj, groups), coef_tiles(dec, groups), batches, span, groups,
        reverse, reverse, init, 0, visit,
    )


def forward_finish(
    cfg, meta, ends, prefix, disc, drive, u, hidden, c_proj, norms, w_gate,
    states, states_low, act, sig, slope, result, wide, emit,
):
    layer, reverse, batches, span, groups, tokens, count = cfg
    finish_states(cfg, meta, ends, prefix, disc, drive, states, states_low)
    wide[...] = dot(states_low[...], c_proj[layer])
    skip = norms[layer + 4 : layer + 5, :]

    def body(start, carry):
        rows = pl.ds(start, ROWS)
        mixed = wide[rows, :] + skip * u[rows, :].astype(f32)
        square = mixed * mixed
        th = jnp.tanh(tanh_scale * (mixed + cubic_term * square * mixed))
        half_one = 0.5 * (1.0 + th)
        act[rows, :] = (mixed * half_one).astype(bf16)
        slope[rows, :] = half_one + 0.5 * mixed * (1.0 - th * th) * tanh_scale * (
            1.0 + 3.0 * cubic_term * square
        )
        return carry

    row_loop(batches * span, body)
    wide[...] = dot(act[...], w_gate[layer])
    sums, squares = [], []
    for batch in range(batches):

        def gate(start, carry, batch=batch):
            rows = pl.ds(batch * span + start, ROWS)
            sig_now = 0.5 + 0.5 * jnp.tanh(0.5 * wide[rows, :])
            sig[rows, :] = sig_now
            value = hidden[rows, :].astype(f32) + act[rows, :].astype(f32) * sig_now
            result[rows, :] = value.astype(result.dtype)
            if emit is None:
                return carry
            return carry[0] + fold(value), carry[1] + fold(value * value)

        zero = jnp.zeros((CHUNKS, wide.shape[1]), f32)
        one, two = row_loop(span, gate, (zero, zero))
        sums.append(one)
        squares.append(two)
    if emit is not None:
        add_sums(emit, batches, (sums, squares))


def backward_start(
    cfg, meta, grad_out, disc, u, c_proj, w_gate, states_low, act, sig, slope,
    grad_gate, grad_mixed, grad_low, source, prefix, total, grad_d, wide,
):
    layer, reverse, batches, span, groups, tokens, count = cfg

    def body(start, carry):
        rows = pl.ds(start, ROWS)
        sig_now = sig[rows, :]
        grad_gate[rows, :] = (
            grad_out[rows, :].astype(f32) * act[rows, :].astype(f32) * sig_now * (1.0 - sig_now)
        ).astype(bf16)
        return carry

    row_loop(batches * span, body)
    wide[...] = dot(grad_gate[...], w_gate[layer], (1, 1))

    def mixed(start, carry):
        rows = pl.ds(start, ROWS)
        value = (grad_out[rows, :].astype(f32) * sig[rows, :] + wide[rows, :]) * slope[rows, :]
        grad_mixed[rows, :] = value
        grad_low[rows, :] = value.astype(bf16)
        return carry + fold(value * u[rows, :].astype(f32))

    gd = row_loop(batches * span, mixed, jnp.zeros((CHUNKS, wide.shape[1]), f32))
    grad_d[...] = jnp.sum(gd, axis=0, keepdims=True)
    source[...] = dot(grad_low[...], c_proj[layer], (1, 1))
    local_ends(
        meta, source, None, conj(constants(disc, layer)[0]), batches, span, groups, not reverse,
        prefix, total,
    )


def middle_forward(
    cfg, place, ends, prefix, disc, drive, u, hidden, c_proj, norms, w_gate,
    states, states_low, act, sig, slope, result, stats, wide,
):
    meta = place_documents(cfg, place)
    forward_finish(
        cfg, meta, ends, prefix, disc, drive, u, hidden, c_proj, norms, w_gate,
        states, states_low, act, sig, slope, result, wide, stats,
    )


def turn_around(
    cfg, place, ends, prefix, disc, drive, u, hidden, c_proj, norms, w_gate, cotangent,
    block_out, ordered_cot, states, states_low, act, grad_gate, grad_mixed, grad_low, source,
    back_prefix, total, grad_d, sig, slope, wide, result,
):
    layer, reverse, batches, span, groups, tokens, count = cfg
    meta = place_documents(cfg, place)
    turn, back = reorder(span, False), reorder(span, True)
    for batch in range(batches):
        rows = slice(batch * span, (batch + 1) * span)
        ordered_cot[rows, :] = dot(turn, cotangent[rows, :]).astype(bf16)
    forward_finish(
        cfg, meta, ends, prefix, disc, drive, u, hidden, c_proj, norms, w_gate,
        states, states_low, act, sig, slope, result, wide, None,
    )
    for batch in range(batches):
        rows = slice(batch * span, (batch + 1) * span)
        block_out[rows, :] = dot(back, result[rows, :]).astype(bf16)
    backward_start(
        cfg, meta, ordered_cot, disc, u, c_proj, w_gate, states_low, act, sig, slope,
        grad_gate, grad_mixed, grad_low, source, back_prefix, total, grad_d, wide,
    )


def backward_finish(
    cfg, place, ends, prefix, disc, source, drive, states, u, grad_mixed, grad_d, hidden, norm,
    norms, b_proj, grad_proj, grad_u, stats, small,
):
    layer, reverse, batches, span, groups, tokens, count = cfg
    half = groups * LANES
    padded = span + CHUNKS
    steps = span // CHUNKS
    meta = place_documents(cfg, place)
    dec, inj = constants(disc, layer)
    dec = conj(dec)
    init = chunk_carries(meta, ends, dec, prefix, batches, span, groups, not reverse)
    inj = coef_tiles(inj, groups)
    base = base_positions(meta, steps)
    zero = jnp.zeros((CHUNKS, LANES), f32)

    def visit(more, batch, q, first, start, found, src):
        if q is None:
            return more
        more = list(more)
        rows = pl.ds(batch * span + start, 2 * CHUNKS)
        drive_re, drive_im = drive[rows, lanes_of(q)], drive[rows, lanes_of(q, half)]
        before = pl.ds(batch * padded + start + (CHUNKS if reverse else 0), 2 * CHUNKS)
        prior_re, prior_im = states[before, lanes_of(q)], states[before, lanes_of(q, half)]
        dec_re, dec_im, inj_re, inj_im = more[q]
        out_re, out_im = [], []
        for j in (0, 1):
            part = slice(j * CHUNKS, (j + 1) * CHUNKS)
            adj_re, adj_im = found[j]
            keep = keep_of(meta, batch, base, first + j, reverse)
            kept_re, kept_im = keep * adj_re, keep * adj_im
            dec_re = dec_re + kept_re * prior_re[part] + kept_im * prior_im[part]
            dec_im = dec_im + kept_im * prior_re[part] - kept_re * prior_im[part]
            inj_re = inj_re + adj_re * drive_re[part] + adj_im * drive_im[part]
            inj_im = inj_im + adj_im * drive_re[part] - adj_re * drive_im[part]
            out_re.append(inj[q][0] * adj_re + inj[q][1] * adj_im)
            out_im.append(inj[q][0] * adj_im - inj[q][1] * adj_re)
        grad_proj[rows, lanes_of(q)] = jnp.concatenate(out_re, axis=0).astype(bf16)
        grad_proj[rows, lanes_of(q, half)] = jnp.concatenate(out_im, axis=0).astype(bf16)
        more[q] = (dec_re, dec_im, inj_re, inj_im)
        return tuple(more)

    _, sums = scan(
        meta, source, None, coef_tiles(dec, groups), batches, span, groups,
        not reverse, not reverse, init, ((zero,) * 4,) * groups, visit,
    )
    small[...] = jnp.zeros_like(small)
    for q in range(groups):
        for kind in range(4):
            small[kind : kind + 1, lanes_of(q)] = jnp.sum(sums[q][kind], axis=0, keepdims=True)
    small[4:5, :] = grad_d[...]
    grad_u[...] = dot(grad_proj[...], b_proj[layer], (1, 1))
    skip = norms[layer + 4 : layer + 5, :]
    plain, times_normed = [], []
    for batch in range(batches):
        average = norm[batch : batch + 1, :]
        scale = norm[batches + batch : batches + batch + 1, :]

        def body(start, carry, batch=batch, average=average, scale=scale):
            rows = pl.ds(batch * span + start, ROWS)
            value = grad_u[rows, :] + grad_mixed[rows, :] * skip
            grad_u[rows, :] = value
            normed = (hidden[rows, :].astype(f32) - average) * scale
            return carry[0] + fold(value), carry[1] + fold(value * normed)

        zero_sum = jnp.zeros((CHUNKS, grad_u.shape[1]), f32)
        one, two = row_loop(span, body, (zero_sum, zero_sum))
        plain.append(one)
        times_normed.append(two)
    add_sums(stats, batches, (plain, times_normed))


def backward_finish_last(cfg, *refs):
    ins, before, (grad_proj, grad_u, sums) = refs[:-4], refs[-4], refs[-3:]
    sums[...] = jnp.zeros_like(sums)
    sums[2 * CHUNKS :, :] = before[...]
    backward_finish(
        cfg, *ins, grad_proj, grad_u, sums.at[pl.ds(0, CHUNKS)], sums.at[pl.ds(CHUNKS, CHUNKS)]
    )


def norm_backward(cfg, stats, grad_out, grad_u, hidden, norm, norms, store, shared):
    layer, reverse, batches, span, groups, tokens, count = cfg
    sums = sum(part[...] for part in stats)
    shared[0:1, :] = jnp.sum(sums[batches:], axis=0, keepdims=True)
    shared[1:2, :] = jnp.sum(sums[:batches], axis=0, keepdims=True)
    gain_now = norms[layer : layer + 1, :]
    for batch in range(batches):
        average = norm[batch : batch + 1, :]
        scale = norm[batches + batch : batches + batch + 1, :]
        plain = gain_now * sums[batch : batch + 1] / tokens
        slanted = gain_now * sums[batches + batch : batches + batch + 1] / tokens

        def body(start, carry, batch=batch, average=average, scale=scale, plain=plain, slanted=slanted):
            rows = pl.ds(batch * span + start, ROWS)
            normed = (hidden[rows, :].astype(f32) - average) * scale
            value = grad_out[rows, :].astype(f32) + scale * (
                grad_u[rows, :] * gain_now - plain - normed * slanted
            )
            store(rows, value)
            return carry

        row_loop(span, body)


def between_layers(
    cfg, lower, place, stats, upper_out, upper_u, upper_hidden, upper_norm, norms,
    disc, u, c_proj, w_gate, states_low, act, sig, slope,
    grad_out, shared, grad_gate, grad_mixed, grad_low, source, prefix, total, grad_d, wide,
):
    def store(rows, value):
        grad_out[rows, :] = value

    norm_backward(cfg, stats, upper_out, upper_u, upper_hidden, upper_norm, norms, store, shared)
    meta = place_documents(lower, place)
    backward_start(
        lower, meta, grad_out, disc, u, c_proj, w_gate, states_low, act, sig, slope,
        grad_gate, grad_mixed, grad_low, source, prefix, total, grad_d, wide,
    )


def last_step(cfg, stats, grad_out, grad_u, hidden, norm, norms, target, shared, ordered):
    layer, reverse, batches, span, groups, tokens, count = cfg
    planes = target.shape[1] // LANES

    def store(rows, value):
        for plane in range(planes):
            ordered[plane, rows, :] = value[:, lanes_of(plane)]

    norm_backward(cfg, stats, grad_out, grad_u, hidden, norm, norms, store, shared)
    steps = span // CHUNKS
    for batch in range(batches):
        for chunk in range(CHUNKS):
            at = batch * span
            for plane in range(planes):
                target[at + chunk * steps : at + (chunk + 1) * steps, lanes_of(plane)] = ordered[
                    plane, pl.ds(at + chunk, steps, stride=CHUNKS), :
                ]


def half_weights(core, refs, own, sent):
    for target, half in ((own, core), (sent, 1 - core)):
        at = 0
        for left, right in refs:
            rows = left.shape[1] // 2
            cols = pl.ds(pl.multiple_of(half * rows, LANES), rows)
            target[at : at + rows, :] = dot(left[:, cols], right[...], (0, 0))
            at += rows


def all_weights(here, act, grad_gate, states_low, grad_low, grad_proj, u, own, sent):
    refs = ((act, grad_gate), (states_low, grad_low), (grad_proj, u))
    half_weights(lax.rem(here[0], 2), refs, own, sent)


def gate_weights(here, act, grad_gate, states_low, grad_low, own, sent):
    half_weights(lax.rem(here[0], 2), ((act, grad_gate), (states_low, grad_low)), own, sent)


def input_weights(here, grad_proj, u, own, sent):
    half_weights(lax.rem(here[0], 2), ((grad_proj, u),), own, sent)


def run(body, name, args, outs, scratch=(), scalars=1):
    vmem, smem = pl.BlockSpec(memory_space=pltpu.VMEM), pl.BlockSpec(memory_space=pltpu.SMEM)
    specs = tuple(
        jax.tree.map(lambda _, at=at: smem if at < scalars else vmem, arg)
        for at, arg in enumerate(args)
    )
    return pl.pallas_call(
        body,
        name=name,
        out_shape=tuple(jax.ShapeDtypeStruct(*out) for out in outs),
        in_specs=specs,
        out_specs=(vmem,) * len(outs),
        scratch_shapes=[pltpu.VMEM(*entry) for entry in scratch],
        compiler_params=pltpu.CompilerParams(vmem_limit_bytes=VMEM_LIMIT),
    )(*args)


def put_in_place(layer, here, halves, outs, before, pieces=1):
    width, states = outs[0][0][1], outs[1][0][1]
    rows_w, rows_c = width // 2, states // 2
    vmem, count = pl.BlockSpec(memory_space=pltpu.VMEM), len(halves)

    def half(step, here):
        core = lax.rem(here[0], 2)
        spots = [1 - core if other else core for other, _ in halves]
        return spots[0] if count == 1 else jnp.where(step == 0, *spots)

    blocks = (
        pl.BlockSpec((1, rows_w, width), lambda i, here: (layer, half(i, here), 0)),
        pl.BlockSpec((1, rows_c, width), lambda i, here: (layer, half(i, here), 0)),
        pl.BlockSpec((1, width, rows_c), lambda i, here: (layer, 0, half(i, here))),
    )

    def body(here, *refs):
        grad_w, grad_c, grad_b = refs[-3:]
        for now in range(count):

            @pl.when(pl.program_id(0) == now)
            def _(source=refs[now]):
                gates, inputs = (rows_w + rows_c) // pieces, rows_c // pieces
                columns = []
                for piece in range(pieces):
                    at, row = piece * (gates + inputs), piece * gates
                    turn = min(max(rows_w - row, 0), gates)
                    if turn:
                        grad_w[0, row : row + turn, :] = source[at : at + turn, :]
                    if turn < gates:
                        to = row + turn - rows_w
                        grad_c[0, to : to + gates - turn, :] = source[at + turn : at + gates, :]
                    columns.append(source[at + gates : at + gates + inputs, :])
                grad_b[0] = jnp.concatenate(columns, axis=0).T

    return pl.pallas_call(
        body,
        name="put_in_place",
        out_shape=tuple(jax.ShapeDtypeStruct(*out) for out in outs),
        grid_spec=pltpu.PrefetchScalarGridSpec(
            num_scalar_prefetch=1,
            grid=(count,),
            in_specs=[vmem] * count + [pl.BlockSpec(memory_space=pl.ANY)] * len(before),
            out_specs=blocks,
        ),
        input_output_aliases={1 + count + i: i for i in range(len(before))},
        compiler_params=pltpu.CompilerParams(vmem_limit_bytes=VMEM_LIMIT),
    )(here, *(rows for _, rows in halves), *before)


def axis_parts():
    count, depth = lax.axis_size("seq"), lax.axis_size("dp")
    return (("seq", 2, 1, count), ("seq", count // 2, 2, count), ("dp", depth, 1, depth))


def shifted(value, part, away):
    name, size, stride, count = part
    pairs = []
    for i in range(count):
        place = (i // stride) % size
        pairs.append((i, i + ((place + away) % size - place) * stride))
    return lax.ppermute(value, name, pairs)


def add_by_shifts(value, parts, *earlier):
    for number, part in enumerate(parts):
        if number:
            value = sum(terms[1:], terms[0])
        if number == len(parts) - 1:
            value, *earlier = lax.optimization_barrier((value, *earlier))
        terms = [value] + [shifted(value, part, away) for away in range(1, part[1])]
    return terms, *earlier


def bits_of(size, stride=1):
    bits = []
    while size > 1:
        bits.append(stride)
        size, stride = size // 2, stride * 2
    return bits


def plane_bits():
    chip_bits = bits_of(lax.axis_size("seq") // 2, 2)
    middle = (len(chip_bits) + 1) // 2
    inner, outer = chip_bits[:middle], chip_bits[middle:]
    return list(zip(inner + outer, outer + inner))


def swap(value, axis, bit):
    return lax.ppermute(value, axis, [(i, i ^ bit) for i in range(lax.axis_size(axis))])


def bit_at(here, axis, bit):
    return lax.rem(lax.div(here[0 if axis == "seq" else 1], bit), 2)


def rows_at(half, rows):
    return pl.ds(pl.multiple_of(half * rows, CHUNKS), rows)


def fold_cores(bits, here, *refs):
    terms, targets = refs[:-4], refs[-4:]
    rows, cols = targets[0].shape
    for side in (0, 1):
        kept, sent = targets[2 * side : 2 * side + 2]
        where = slice(side * cols, (side + 1) * cols)
        bit = bit_at(here, "seq", bits[side])
        for half in (0, 1):

            @pl.when(bit == half)
            def _(half=half, kept=kept, sent=sent, where=where):
                start = 0
                for own, found in zip(terms[0::2], terms[1::2]):
                    for part, target in ((half, kept), (1 - half, sent)):
                        low = max(start, part * rows)
                        high = min(start + own.shape[0], (part + 1) * rows)
                        if low < high:
                            source = slice(low - start, high - start)
                            target[low - part * rows : high - part * rows, :] = (
                                own[source, where] + found[source, where]
                            )
                    start += own.shape[0]


def fold_sides(bits, here, *refs):
    targets, blocks = refs[-4:], refs[:-4]
    for side in (0, 1):
        kept, sent = targets[2 * side : 2 * side + 2]
        half, start = bit_at(here, "seq", bits[side]), 0
        for at in range(0, len(blocks), 4):
            own, found = blocks[at + 2 * side : at + 2 * side + 2]
            rows = own.shape[0] // 2
            to = slice(start, start + rows)
            kept[to, :] = own[rows_at(half, rows), :] + found[rows_at(half, rows), :]
            sent[to, :] = own[rows_at(1 - half, rows), :] + found[rows_at(1 - half, rows), :]
            start += rows


def fold_join(bit, here, left, found_left, right, found_right, kept, sent):
    rows, cols = kept.shape[0], left.shape[1]
    half = bit_at(here, "dp", bit)
    for side, (own, found) in enumerate(((left, found_left), (right, found_right))):
        where = slice(side * cols, (side + 1) * cols)
        kept[:, where] = own[rows_at(half, rows), :] + found[rows_at(half, rows), :]
        sent[:, where] = own[rows_at(1 - half, rows), :] + found[rows_at(1 - half, rows), :]


def fold_depth(bit, here, own, found, kept, sent):
    half, rows = bit_at(here, "dp", bit), kept.shape[0]
    kept[...] = own[rows_at(half, rows), :] + found[rows_at(half, rows), :]
    sent[...] = own[rows_at(1 - half, rows), :] + found[rows_at(1 - half, rows), :]


def add_two(own, found, out):
    out[...] = own[...] + found[...]


def unfold(bit, here, own, found, out):
    half, rows = bit_at(here, "dp", bit), own.shape[0]
    out[rows_at(half, rows), :] = own[...]
    out[rows_at(1 - half, rows), :] = found[...]


def unfold_split(bit, here, own, found, left, right):
    half, rows, cols = bit_at(here, "dp", bit), own.shape[0], left.shape[1]
    for side, out in enumerate((left, right)):
        where = slice(side * cols, (side + 1) * cols)
        out[rows_at(half, rows), :] = own[:, where]
        out[rows_at(1 - half, rows), :] = found[:, where]


def unfold_sides(bits, joined, here, *refs):
    for side in (0, 1):
        own, found = refs[2 * side : 2 * side + 2]
        half, (rows, cols) = bit_at(here, "seq", bits[side]), own.shape
        out = refs[4] if joined else refs[4 + side]
        where = slice(side * cols, (side + 1) * cols) if joined else slice(0, cols)
        out[rows_at(half, rows), where] = own[...]
        out[rows_at(1 - half, rows), where] = found[...]


def link_call(body, here, args, shapes):
    name = body.func.__name__
    return run(body, name, (here, *args), tuple((shape, f32) for shape in shapes))


class LinkSum:
    def __init__(self, here, terms):
        self.here, self.plane = here, plane_bits()
        self.depth = bits_of(lax.axis_size("dp"))
        rows = sum(term.shape[0] for term in terms[::2])
        self.shape = (rows // 2, terms[0].shape[1] // 2)
        self.parts = link_call(
            functools.partial(fold_cores, self.plane[0]), here, terms, (self.shape,) * 4
        )

    def swap_plane(self, stage):
        (left, right), pieces = self.plane[stage], self.parts
        self.parts = (
            pieces[0], swap(pieces[1], "seq", left), pieces[2], swap(pieces[3], "seq", right)
        )

    def down_plane(self, stage, *others):
        parts, rows, cols = list(self.parts), *self.shape
        for other in others:
            parts += other.parts
            rows += other.shape[0]
        self.shape = (rows // 2, cols)
        body = functools.partial(fold_sides, self.plane[stage])
        self.parts = link_call(body, self.here, parts, (self.shape,) * 4)

    def down_join(self):
        rows, cols = self.shape
        self.shape = (rows // 2, 2 * cols)
        body = functools.partial(fold_join, self.depth[0])
        self.parts = link_call(body, self.here, self.parts, (self.shape,) * 2)

    def swap_depth(self, stage):
        self.parts = (self.parts[0], swap(self.parts[1], "dp", self.depth[stage]))

    def down_depth(self, stage):
        rows, cols = self.shape
        self.shape = (rows // 2, cols)
        body = functools.partial(fold_depth, self.depth[stage])
        self.parts = link_call(body, self.here, self.parts, (self.shape,) * 2)

    def middle(self):
        (value,) = run(add_two, "add_two", self.parts, ((self.shape, f32),), scalars=0)
        self.parts = (value, value)

    def up_depth(self, stage):
        rows, cols = self.shape
        self.shape = (rows * 2, cols)
        body = functools.partial(unfold, self.depth[stage])
        (value,) = link_call(body, self.here, self.parts, (self.shape,))
        self.parts = (value, value)

    def up_split(self):
        rows, cols = self.shape
        self.shape = (rows * 2, cols // 2)
        body = functools.partial(unfold_split, self.depth[0])
        left, right = link_call(body, self.here, self.parts, (self.shape,) * 2)
        self.parts = (left, left, right, right)

    def up_plane(self, stage):
        rows, cols = self.shape
        if stage:
            self.shape = (rows * 2, cols)
            body = functools.partial(unfold_sides, self.plane[stage], False)
            left, right = link_call(body, self.here, self.parts, (self.shape,) * 2)
            self.parts = (left, left, right, right)
        else:
            self.shape = (rows * 2, cols * 2)
            body = functools.partial(unfold_sides, self.plane[stage], True)
            self.parts = link_call(body, self.here, self.parts, (self.shape,))

    def after(self, *values):
        self.parts, values = lax.optimization_barrier((self.parts, values))
        return values

    def to_depth(self):
        for stage in range(2, len(self.plane)):
            self.swap_plane(stage - 1)
            self.down_plane(stage)
        self.swap_plane(len(self.plane) - 1)

    def scatter_depth(self):
        for stage in range(len(self.depth) - 1):
            if stage:
                self.down_depth(stage)
            self.swap_depth(stage)

    def swap_whole(self):
        self.parts = (self.parts[0], swap(self.parts[0], "dp", self.depth[-1]))

    def gather_depth(self):
        for stage in range(len(self.depth) - 2, 0, -1):
            self.swap_depth(stage)
            self.up_depth(stage)
        self.swap_depth(0)


def wait_for(*things):
    sums = [thing for thing in things if isinstance(thing, LinkSum)]
    values = [thing for thing in things if not isinstance(thing, LinkSum)]
    parts, values = lax.optimization_barrier(([entry.parts for entry in sums], values))
    for entry, part in zip(sums, parts):
        entry.parts = part
    return values


def discretize(lam_re, lam_im, log_step):
    step_size = jnp.exp(log_step)
    decay_abs = jnp.exp(lam_re * step_size)
    rotation = lam_im * step_size
    dec_re = decay_abs * jnp.cos(rotation)
    dec_im = decay_abs * jnp.sin(rotation)
    denom_sq = lam_re * lam_re + lam_im * lam_im
    inj_re = ((dec_re - 1.0) * lam_re + dec_im * lam_im) / denom_sq
    inj_im = (dec_im * lam_re - (dec_re - 1.0) * lam_im) / denom_sq
    return (dec_re, dec_im, inj_re, inj_im)


def per_device(
    block_in, cotangent, doc_lengths, norm_gain, norm_shift, log_step, lam_re, lam_im,
    b_proj, c_proj, d_skip, w_gate,
):
    batches, seqs, span, width = block_in.shape
    assert seqs == 1 and span % (4 * CHUNKS) == 0 and span & (span - 1) == 0
    half = lam_re.shape[1]
    groups = half // LANES
    rows = batches * span
    count = lax.axis_size("seq")
    tokens = float(seqs * lax.axis_size("dp") * span * count)
    here = jnp.stack([lax.axis_index("seq"), lax.axis_index("dp")]).astype(jnp.int32)
    place = jnp.concatenate([here] + [doc_lengths[batch, 0] for batch in range(batches)])
    place, block_in = lax.optimization_barrier((place, block_in))
    here = place
    disc = discretize(lam_re, lam_im, log_step)

    x = block_in.reshape(rows, width)
    cot = cotangent.reshape(rows, width)
    lower = (0, False, batches, span, groups, tokens, count)
    upper = (1, True, batches, span, groups, tokens, count)
    part = functools.partial

    flat, low = ((rows, width), f32), ((rows, width), bf16)
    wide, wide_low = ((rows, 2 * half), f32), ((rows, 2 * half), bf16)
    padded = ((batches * (span + CHUNKS), 2 * half), f32)
    sums = ((2 * batches, width), f32)
    prefix = ((2, batches * CHUNKS, 2 * half), f32)
    total = ((batches, 2 * half), f32)
    line, shared = ((1, width), f32), ((2, width), f32)
    small = ((8, width), f32)

    def gather_row(value):
        return lax.all_gather(value, "seq")

    ordered, stats = run(
        part(first_sums, batches, span), "first_sums", (x,), (low, sums), scalars=0
    )
    norms = jnp.concatenate([norm_gain, norm_shift, d_skip], axis=0)

    def forward(cfg, hidden, stats):
        return run(
            part(enter_layer, cfg),
            "enter_layer",
            (place, stats, hidden, norms, disc, b_proj),
            (low, wide, prefix, total, sums),
        )

    links, plane, depth = axis_parts()
    u0, drive0, prefix0, total0, norm0 = forward(
        lower, ordered, add_by_shifts(stats, (links, plane, depth))[0]
    )
    states0, states_low0, act0, sig0, slope0, hidden1, stats = run(
        part(middle_forward, lower),
        "middle_forward",
        (place, gather_row(total0), prefix0, disc, drive0, u0, ordered, c_proj, norms, w_gate),
        (padded, wide_low, low, flat, flat, flat, sums),
        (flat,),
    )
    u1, drive1, prefix1, total1, norm1 = forward(
        upper, hidden1, add_by_shifts(stats, (links, plane, depth))[0]
    )
    (
        block_out, ordered_cot, states1, states_low1, act1, grad_gate1, grad_mixed1, grad_low1,
        source1, prefix1, total1, grad_d1,
    ) = run(
        part(turn_around, upper),
        "turn_around",
        (
            place, gather_row(total1), prefix1, disc, drive1, u1, hidden1, c_proj, norms, w_gate,
            cot,
        ),
        (low, low, padded, wide_low, low, low, flat, low, wide, prefix, total, line),
        (flat, flat, flat, low),
    )

    def halves(length):
        return (((length // 2, width), f32),) * 2

    grad_proj1, grad_u1, stats, small1 = run(
        part(backward_finish, upper),
        "backward_finish",
        (
            place, gather_row(total1), prefix1, disc, source1, drive1, states1, u1, grad_mixed1,
            grad_d1, hidden1, norm1, norms, b_proj,
        ),
        (wide_low, flat, sums, small),
    )
    sizes = (width + 2 * half, 2 * half)
    own1, sent1 = run(
        all_weights,
        "all_weights",
        (here, act1, grad_gate1, states_low1, grad_low1, grad_proj1, u1),
        halves(sum(sizes)),
    )
    stats = stats + swap(stats, "seq", 1)
    stats, sent1 = lax.optimization_barrier((stats, sent1))
    upper_sum = LinkSum(here, (own1, swap(sent1, "seq", 1)))
    stats, upper_sum.parts = add_by_shifts(stats, (plane, depth), upper_sum.parts)
    upper_sum.swap_plane(0)
    (
        grad_out0, shared1, grad_gate0, grad_mixed0, grad_low0, source0, prefix0, total0, grad_d0,
    ) = run(
        part(between_layers, upper, lower),
        "between_layers",
        (
            place, stats, ordered_cot, grad_u1, hidden1, norm1, norms,
            disc, u0, c_proj, w_gate, states_low0, act0, sig0, slope0,
        ),
        (flat, shared, low, flat, low, wide, prefix, total, line),
        (flat,),
    )
    (total0,) = upper_sum.after(total0)
    upper_sum.down_plane(1)
    (total0,) = upper_sum.after(total0)
    upper_sum.to_depth()
    ends, grad_gate0 = wait_for(upper_sum, gather_row(total0), grad_gate0)
    upper_sum.down_join()
    ends, grad_gate0 = wait_for(upper_sum, ends, grad_gate0)
    upper_sum.scatter_depth()
    own_gates, sent_gates = run(
        gate_weights, "gate_weights", (here, act0, grad_gate0, states_low0, grad_low0),
        halves(sizes[0]),
    )
    own_gates, ends = lax.optimization_barrier((own_gates, ends))
    grad_proj0, grad_u0, last_sums = run(
        part(backward_finish_last, lower),
        "backward_finish",
        (
            place, ends, prefix0, disc, source0, drive0, states0, u0, grad_mixed0, grad_d0,
            ordered, norm0, norms, b_proj, small1,
        ),
        (wide_low, flat, ((3 * CHUNKS, width), f32)),
    )
    lower_sum = LinkSum(here, (own_gates, swap(sent_gates, "seq", 1)))
    (grad_proj0,) = wait_for(upper_sum, lower_sum, grad_proj0)
    own_inputs, sent_inputs = run(
        input_weights, "input_weights", (here, grad_proj0, u0), halves(sizes[1])
    )
    inputs_sum = LinkSum(here, (own_inputs, swap(sent_inputs, "seq", 1)))
    upper_sum.middle()
    upper_sum.swap_whole()
    lower_sum.swap_plane(0)
    inputs_sum.swap_plane(0)
    wait_for(upper_sum, lower_sum, inputs_sum)

    lower_sum.down_plane(1, inputs_sum)
    upper_sum.middle()
    upper_sum.gather_depth()
    lower_sum.to_depth()
    wait_for(upper_sum, lower_sum)

    lower_sum.down_join()
    upper_sum.up_split()
    lower_sum.scatter_depth()
    upper_sum.swap_plane(len(upper_sum.plane) - 1)
    wait_for(upper_sum, lower_sum)

    lower_sum.middle()
    lower_sum.swap_whole()
    for stage in range(len(upper_sum.plane) - 1, 0, -1):
        upper_sum.up_plane(stage)
        upper_sum.swap_plane(stage - 1)
    (last_sums,) = wait_for(upper_sum, lower_sum, last_sums)

    lower_sum.middle()
    (last_sums,) = lower_sum.after(last_sums)
    lower_sum.gather_depth()
    last_sums = last_sums + swap(last_sums, "seq", 1)
    last_terms = [last_sums] + [shifted(last_sums, plane, away) for away in range(1, plane[1])]
    last_terms = wait_for(lower_sum, *last_terms)

    lower_sum.up_split()
    wait_for(upper_sum, lower_sum)
    upper_sum.up_plane(0)
    own1 = upper_sum.parts[0]
    other1 = swap(own1, "seq", 1)
    last_terms = lower_sum.after(*last_terms)
    last_sums = sum(last_terms)
    last_terms = [last_sums] + [shifted(last_sums, depth, away) for away in range(1, depth[1])]
    lower_sum.swap_plane(len(lower_sum.plane) - 1)
    last_terms = wait_for(lower_sum, *last_terms)
    for stage in range(len(lower_sum.plane) - 1, 0, -1):
        lower_sum.up_plane(stage)
        lower_sum.swap_plane(stage - 1)
    summed = sum(last_terms)
    grad_input, shared0 = run(
        part(last_step, lower),
        "last_step",
        ((summed[: 2 * batches],), grad_out0, grad_u0, ordered, norm0, norms),
        (flat, shared),
        (((width // LANES, rows, LANES), f32),),
        scalars=0,
    )
    small_sum = summed[CHUNKS:].reshape(2, CHUNKS, width)
    _, pullback = jax.vjp(discretize, lam_re, lam_im, log_step)
    grad_lr, grad_li, grad_ls = pullback(tuple(small_sum[:, kind, :half] for kind in range(4)))
    final = (((2, width, width), f32), ((2, 2 * half, width), f32), ((2, width, 2 * half), f32))
    placed = put_in_place(1, here, ((False, own1), (True, other1)), final, ())
    grad_input, grad_lr, grad_li, grad_ls, *placed = wait_for(
        lower_sum, grad_input, grad_lr, grad_li, grad_ls, *placed
    )

    lower_sum.up_plane(0)
    own0 = lower_sum.parts[0]
    other0 = swap(own0, "seq", 1)
    placed = put_in_place(0, here, ((False, own0),), final, placed, 4)
    grad_w, grad_c, grad_b = put_in_place(0, here, ((True, other0),), final, placed, 4)
    both = jnp.stack([shared0, shared1])
    shape = block_in.shape
    return (
        block_out.reshape(shape), grad_input.reshape(shape), both[:, 0], both[:, 1],
        grad_ls, grad_lr, grad_li, grad_b, grad_c, small_sum[:, 4], grad_w,
    )


def solution(mesh):
    split = P(None, "dp", "seq", None)
    return jax.shard_map(
        per_device,
        mesh=mesh,
        in_specs=(split, split, P(None, "dp", None)) + (P(),) * 9,
        out_specs=(split, split) + (P(),) * 9,
        check_vma=False,
    )
```

```python
import functools

import jax
import jax.numpy as jnp
from jax import lax
from jax.experimental import pallas as pl
from jax.experimental.pallas import tpu as pltpu
from jax.sharding import PartitionSpec as P

f32, bf16 = jnp.float32, jnp.bfloat16
epsilon = 1e-05
tanh_scale = 0.7978845608028654
cubic_term = 0.044715
LANES = 128
CHUNKS = 8
ROWS = 32
VMEM_LIMIT = 16 * 1024 * 1024


def dot(left, right, contract=(1, 0)):
    return lax.dot_general(
        left, right, (((contract[0],), (contract[1],)), ((), ())), preferred_element_type=f32
    )


def reorder(span, inverse):
    shape = (span, span)
    kept, moved = (1, 0) if inverse else (0, 1)
    row = lax.broadcasted_iota(jnp.int32, shape, kept)
    position = lax.broadcasted_iota(jnp.int32, shape, moved)
    source = (row & (CHUNKS - 1)) * (span // CHUNKS) + (row >> 3)
    return jnp.where(position == source, 1.0, 0.0).astype(bf16)


def row_loop(count, body, init=0, step=ROWS):
    def one(index, carry):
        return body(pl.multiple_of(index * step, step), carry)

    return lax.fori_loop(0, count // step, one, init)


def documents(here, batches, span, count):
    mine = here[0]
    first = mine * span
    out = []
    for batch in range(batches):
        begins, ends, so_far = [], [], 0
        docs = (here.shape[0] - 2) // batches
        for doc in range(docs):
            begins.append(so_far)
            so_far = so_far + here[2 + batch * docs + doc]
            ends.append(so_far)
        before, after = 0, 2 * count * span
        for begin, end in zip(begins, ends):
            before = jnp.maximum(before, jnp.where(begin < first, begin, 0))
            after = jnp.minimum(after, jnp.where(end > first + span, end, 2 * count * span))
        after = jnp.where(mine == count - 1, 0, after)
        out.append(begins + ends + [before, after, first, mine])
    return out


def place_documents(cfg, place):
    layer, reverse, batches, span, groups, tokens, count = cfg
    return documents(place, batches, span, count)


def keep_of(meta, batch, base, step, backward):
    docs = (len(meta[batch]) - 4) // 2
    off = docs if backward else 0
    late = 1 if backward else 0
    stop = base == meta[batch][off] - step - late
    for doc in range(1, docs):
        stop = jnp.logical_or(stop, base == meta[batch][off + doc] - step - late)
    return jnp.where(stop, 0.0, 1.0)


def base_positions(meta, steps):
    return meta[0][-2] + lax.broadcasted_iota(jnp.int32, (CHUNKS, LANES), 0) * steps


def lanes_of(index, half=0):
    return slice(half + index * LANES, half + (index + 1) * LANES)


def coef_tiles(value, groups):
    return [
        tuple(jnp.broadcast_to(part[:, lanes_of(q)], (CHUNKS, LANES)) for part in value)
        for q in range(groups)
    ]


def constants(disc, layer):
    dec_re, dec_im, inj_re, inj_im = (part[layer : layer + 1, :] for part in disc)
    return (dec_re, dec_im), (inj_re, inj_im)


def times(a, b):
    return (a[0] * b[0] - a[1] * b[1], a[0] * b[1] + a[1] * b[0])


def power(value, exponent):
    for _ in range(exponent.bit_length() - 1):
        value = times(value, value)
    return value


def conj(value):
    return (value[0], -value[1])


def scan(meta, source, inject, dec, batches, span, groups, reverse, masks_reverse, init, extra, visit):
    steps = span // CHUNKS
    half = groups * LANES
    base = base_positions(meta, steps)

    def pair(index, carry):
        states, more = carry
        states = list(states)
        first = steps - 2 - 2 * index if reverse else 2 * index
        start = pl.multiple_of(first * CHUNKS, 2 * CHUNKS)
        order = (1, 0) if reverse else (0, 1)
        for batch in range(batches):
            keeps = [keep_of(meta, batch, base, first + j, masks_reverse) for j in (0, 1)]
            for q in range(groups):
                rows = pl.ds(batch * span + start, 2 * CHUNKS)
                src_re = source[rows, lanes_of(q)]
                src_im = source[rows, lanes_of(q, half)]
                state = states[batch * groups + q]
                found = [None, None]
                for j in order:
                    part = (
                        src_re[j * CHUNKS : (j + 1) * CHUNKS],
                        src_im[j * CHUNKS : (j + 1) * CHUNKS],
                    )
                    push = times(inject[q], part) if inject is not None else part
                    held = times((keeps[j] * dec[q][0], keeps[j] * dec[q][1]), state)
                    state = (held[0] + push[0], held[1] + push[1])
                    found[j] = state
                states[batch * groups + q] = state
                more = visit(more, batch, q, first, start, found, (src_re, src_im))
            more = visit(more, batch, None, first, start, keeps, None)
        return tuple(states), more

    return lax.fori_loop(0, steps // 2, pair, (tuple(init), extra), unroll=2)


def zero_states(batches, groups):
    zero = jnp.zeros((CHUNKS, LANES), f32)
    return [(zero, zero)] * (batches * groups)


def local_ends(meta, source, inject, dec, batches, span, groups, reverse, prefix, total):
    ones = tuple(jnp.ones((CHUNKS, LANES), f32) for _ in range(batches))

    def visit(more, batch, q, first, start, found, src):
        if q is not None:
            return more
        return tuple(
            value * found[0] * found[1] if at == batch else value for at, value in enumerate(more)
        )

    dec_chunk = coef_tiles(power(dec, span // CHUNKS), groups)
    ends, kept = scan(
        meta, source, inject, coef_tiles(dec, groups), batches, span, groups, reverse, reverse,
        zero_states(batches, groups), ones, visit,
    )
    half = groups * LANES
    row = lax.broadcasted_iota(jnp.int32, (CHUNKS, LANES), 0)
    for batch in range(batches):
        for q in range(groups):
            end = ends[batch * groups + q]
            decay = (kept[batch] * dec_chunk[q][0], kept[batch] * dec_chunk[q][1])
            for shift in (1, 2, 4):
                turn = CHUNKS - shift if reverse else shift
                valid = row < CHUNKS - shift if reverse else row >= shift
                before = [pltpu.roll(value, turn, 0) for value in (*end, *decay)]
                from_before = times(decay, (before[0], before[1]))
                end = (
                    end[0] + jnp.where(valid, from_before[0], 0.0),
                    end[1] + jnp.where(valid, from_before[1], 0.0),
                )
                longer = times(decay, (before[2], before[3]))
                decay = (
                    jnp.where(valid, longer[0], decay[0]),
                    jnp.where(valid, longer[1], decay[1]),
                )
            rows = slice(batch * CHUNKS, (batch + 1) * CHUNKS)
            prefix[0, rows, lanes_of(q)] = end[0]
            prefix[0, rows, lanes_of(q, half)] = end[1]
            prefix[1, rows, lanes_of(q)] = decay[0]
            prefix[1, rows, lanes_of(q, half)] = decay[1]
            last = 0 if reverse else CHUNKS - 1
            total[batch : batch + 1, lanes_of(q)] = end[0][last : last + 1]
            total[batch : batch + 1, lanes_of(q, half)] = end[1][last : last + 1]


def chunk_carries(meta, gathered, dec, prefix, batches, span, groups, reverse):
    count = gathered.shape[0]
    half = groups * LANES
    dec_span = power(dec, span)
    row = lax.broadcasted_iota(jnp.int32, (CHUNKS, LANES), 0)
    mine = meta[0][-1]
    out = []
    for batch in range(batches):

        def add(at, so_far, batch=batch):
            away = count - 2 - at
            if reverse:
                other = mine + 1 + away
                reaches = meta[batch][-3] > other * span
            else:
                other = mine - 1 - away
                reaches = meta[batch][-4] < (mine - away) * span
            other = jnp.clip(other, 0, count - 1)
            value = jnp.where(reaches, gathered[other, pl.ds(batch, 1), :], 0.0)
            moved = times(dec_span, so_far)
            return (moved[0] + value[:, :half], moved[1] + value[:, half:])

        zero = jnp.zeros((1, half), f32)
        enter = lax.fori_loop(0, count - 1, add, (zero, zero), unroll=count <= 8)
        rows = slice(batch * CHUNKS, (batch + 1) * CHUNKS)
        for q in range(groups):
            own = tuple(jnp.broadcast_to(part[:, lanes_of(q)], (CHUNKS, LANES)) for part in enter)
            end = (prefix[0, rows, lanes_of(q)], prefix[0, rows, lanes_of(q, half)])
            decay = (prefix[1, rows, lanes_of(q)], prefix[1, rows, lanes_of(q, half)])
            moved = times(decay, own)
            turn, first = (CHUNKS - 1, CHUNKS - 1) if reverse else (1, 0)
            out.append(
                tuple(
                    jnp.where(row == first, own[i], pltpu.roll(end[i] + moved[i], turn, 0))
                    for i in (0, 1)
                )
            )
    return out


def add_sums(target, batches, sums):
    for kind, per_batch in enumerate(sums):
        for batch in range(batches):
            target[kind * batches + batch : kind * batches + batch + 1, :] = jnp.sum(
                per_batch[batch], axis=0, keepdims=True
            )


def fold(value):
    return sum(value[i : i + CHUNKS] for i in range(CHUNKS, value.shape[0], CHUNKS)) + value[:CHUNKS]


def order_rows(batches, span, inverse, x, out):
    turn = reorder(span, inverse)
    for batch in range(batches):
        rows = slice(batch * span, (batch + 1) * span)
        out[rows, :] = dot(turn, x[rows, :]).astype(bf16)


def first_sums(batches, span, x, stats):
    width = x.shape[1]
    sums, squares = [], []
    for batch in range(batches):

        def body(start, carry, batch=batch):
            value = x[pl.ds(batch * span + start, ROWS), :].astype(f32)
            return carry[0] + fold(value), carry[1] + fold(value * value)

        zero = jnp.zeros((CHUNKS, width), f32)
        one, two = row_loop(span, body, (zero, zero))
        sums.append(one)
        squares.append(two)
    add_sums(stats, batches, (sums, squares))


def enter_layer(
    cfg, place, stats, hidden, norms, disc, b_proj, u, drive, prefix, total, norm
):
    layer, reverse, batches, span, groups, tokens, count = cfg
    sums = sum(part[...] for part in stats)
    average = sums[:batches] / tokens
    spread = sums[batches:] / tokens - average * average
    scale = lax.rsqrt(spread + epsilon)
    norm[:batches, :] = average
    norm[batches:, :] = scale
    gain_now, shift_now = norms[layer : layer + 1, :], norms[layer + 2 : layer + 3, :]
    for batch in range(batches):

        def body(start, carry, batch=batch):
            rows = pl.ds(batch * span + start, ROWS)
            normed = (hidden[rows, :].astype(f32) - average[batch : batch + 1]) * scale[
                batch : batch + 1
            ]
            u[rows, :] = (normed * gain_now + shift_now).astype(bf16)
            return carry

        row_loop(span, body)
    drive[...] = dot(u[...], b_proj[layer])
    meta = place_documents(cfg, place)
    dec, inj = constants(disc, layer)
    local_ends(
        meta, drive, coef_tiles(inj, groups), dec, batches, span, groups, reverse, prefix, total
    )


def finish_states(cfg, meta, ends, prefix, disc, drive, states, states_low):
    layer, reverse, batches, span, groups, tokens, count = cfg
    half = groups * LANES
    padded = span + CHUNKS
    dec, inj = constants(disc, layer)
    init = chunk_carries(meta, ends, dec, prefix, batches, span, groups, reverse)
    for batch in range(batches):
        edge = batch * padded + (span if reverse else 0)
        for q in range(groups):
            states[edge : edge + CHUNKS, lanes_of(q)] = init[batch * groups + q][0]
            states[edge : edge + CHUNKS, lanes_of(q, half)] = init[batch * groups + q][1]

    def visit(more, batch, q, first, start, found, src):
        if q is not None:
            for part, off in ((0, 0), (1, half)):
                both = jnp.concatenate([found[0][part], found[1][part]], axis=0)
                at = batch * padded + (0 if reverse else CHUNKS)
                states[pl.ds(at + start, 2 * CHUNKS), lanes_of(q, off)] = both
                states_low[pl.ds(batch * span + start, 2 * CHUNKS), lanes_of(q, off)] = both.astype(
                    bf16
                )
        return more

    scan(
        meta, drive, coef_tiles(inj, groups), coef_tiles(dec, groups), batches, span, groups,
        reverse, reverse, init, 0, visit,
    )


def forward_finish(
    cfg, meta, ends, prefix, disc, drive, u, hidden, c_proj, norms, w_gate,
    states, states_low, act, sig, slope, result, wide, emit,
):
    layer, reverse, batches, span, groups, tokens, count = cfg
    finish_states(cfg, meta, ends, prefix, disc, drive, states, states_low)
    wide[...] = dot(states_low[...], c_proj[layer])
    skip = norms[layer + 4 : layer + 5, :]

    def body(start, carry):
        rows = pl.ds(start, ROWS)
        mixed = wide[rows, :] + skip * u[rows, :].astype(f32)
        square = mixed * mixed
        th = jnp.tanh(tanh_scale * (mixed + cubic_term * square * mixed))
        half_one = 0.5 * (1.0 + th)
        act[rows, :] = (mixed * half_one).astype(bf16)
        slope[rows, :] = half_one + 0.5 * mixed * (1.0 - th * th) * tanh_scale * (
            1.0 + 3.0 * cubic_term * square
        )
        return carry

    row_loop(batches * span, body)
    wide[...] = dot(act[...], w_gate[layer])
    sums, squares = [], []
    for batch in range(batches):

        def gate(start, carry, batch=batch):
            rows = pl.ds(batch * span + start, ROWS)
            sig_now = 0.5 + 0.5 * jnp.tanh(0.5 * wide[rows, :])
            sig[rows, :] = sig_now
            value = hidden[rows, :].astype(f32) + act[rows, :].astype(f32) * sig_now
            result[rows, :] = value.astype(result.dtype)
            if emit is None:
                return carry
            return carry[0] + fold(value), carry[1] + fold(value * value)

        zero = jnp.zeros((CHUNKS, wide.shape[1]), f32)
        one, two = row_loop(span, gate, (zero, zero))
        sums.append(one)
        squares.append(two)
    if emit is not None:
        add_sums(emit, batches, (sums, squares))


def backward_start(
    cfg, meta, grad_out, disc, u, c_proj, w_gate, states_low, act, sig, slope,
    grad_gate, grad_mixed, grad_low, source, prefix, total, grad_d, wide,
):
    layer, reverse, batches, span, groups, tokens, count = cfg

    def body(start, carry):
        rows = pl.ds(start, ROWS)
        sig_now = sig[rows, :]
        grad_gate[rows, :] = (
            grad_out[rows, :].astype(f32) * act[rows, :].astype(f32) * sig_now * (1.0 - sig_now)
        ).astype(bf16)
        return carry

    row_loop(batches * span, body)
    wide[...] = dot(grad_gate[...], w_gate[layer], (1, 1))

    def mixed(start, carry):
        rows = pl.ds(start, ROWS)
        value = (grad_out[rows, :].astype(f32) * sig[rows, :] + wide[rows, :]) * slope[rows, :]
        grad_mixed[rows, :] = value
        grad_low[rows, :] = value.astype(bf16)
        return carry + fold(value * u[rows, :].astype(f32))

    gd = row_loop(batches * span, mixed, jnp.zeros((CHUNKS, wide.shape[1]), f32))
    grad_d[...] = jnp.sum(gd, axis=0, keepdims=True)
    source[...] = dot(grad_low[...], c_proj[layer], (1, 1))
    local_ends(
        meta, source, None, conj(constants(disc, layer)[0]), batches, span, groups, not reverse,
        prefix, total,
    )


def middle_forward(
    cfg, place, ends, prefix, disc, drive, u, hidden, c_proj, norms, w_gate,
    states, states_low, act, sig, slope, result, stats, wide,
):
    meta = place_documents(cfg, place)
    forward_finish(
        cfg, meta, ends, prefix, disc, drive, u, hidden, c_proj, norms, w_gate,
        states, states_low, act, sig, slope, result, wide, stats,
    )


def turn_around(
    cfg, place, ends, prefix, disc, drive, u, hidden, c_proj, norms, w_gate, ordered_cot,
    result, states, states_low, act, grad_gate, grad_mixed, grad_low, source,
    back_prefix, total, grad_d, sig, slope, wide,
):
    layer, reverse, batches, span, groups, tokens, count = cfg
    meta = place_documents(cfg, place)
    forward_finish(
        cfg, meta, ends, prefix, disc, drive, u, hidden, c_proj, norms, w_gate,
        states, states_low, act, sig, slope, result, wide, None,
    )
    backward_start(
        cfg, meta, ordered_cot, disc, u, c_proj, w_gate, states_low, act, sig, slope,
        grad_gate, grad_mixed, grad_low, source, back_prefix, total, grad_d, wide,
    )


def backward_finish(
    cfg, place, ends, prefix, disc, source, drive, states, u, grad_mixed, grad_d, hidden, norm,
    norms, b_proj, grad_proj, grad_u, stats, small,
):
    layer, reverse, batches, span, groups, tokens, count = cfg
    half = groups * LANES
    padded = span + CHUNKS
    steps = span // CHUNKS
    meta = place_documents(cfg, place)
    dec, inj = constants(disc, layer)
    dec = conj(dec)
    init = chunk_carries(meta, ends, dec, prefix, batches, span, groups, not reverse)
    inj = coef_tiles(inj, groups)
    base = base_positions(meta, steps)
    zero = jnp.zeros((CHUNKS, LANES), f32)

    def visit(more, batch, q, first, start, found, src):
        if q is None:
            return more
        more = list(more)
        rows = pl.ds(batch * span + start, 2 * CHUNKS)
        drive_re, drive_im = drive[rows, lanes_of(q)], drive[rows, lanes_of(q, half)]
        before = pl.ds(batch * padded + start + (CHUNKS if reverse else 0), 2 * CHUNKS)
        prior_re, prior_im = states[before, lanes_of(q)], states[before, lanes_of(q, half)]
        dec_re, dec_im, inj_re, inj_im = more[q]
        out_re, out_im = [], []
        for j in (0, 1):
            part = slice(j * CHUNKS, (j + 1) * CHUNKS)
            adj_re, adj_im = found[j]
            keep = keep_of(meta, batch, base, first + j, reverse)
            kept_re, kept_im = keep * adj_re, keep * adj_im
            dec_re = dec_re + kept_re * prior_re[part] + kept_im * prior_im[part]
            dec_im = dec_im + kept_im * prior_re[part] - kept_re * prior_im[part]
            inj_re = inj_re + adj_re * drive_re[part] + adj_im * drive_im[part]
            inj_im = inj_im + adj_im * drive_re[part] - adj_re * drive_im[part]
            out_re.append(inj[q][0] * adj_re + inj[q][1] * adj_im)
            out_im.append(inj[q][0] * adj_im - inj[q][1] * adj_re)
        grad_proj[rows, lanes_of(q)] = jnp.concatenate(out_re, axis=0).astype(bf16)
        grad_proj[rows, lanes_of(q, half)] = jnp.concatenate(out_im, axis=0).astype(bf16)
        more[q] = (dec_re, dec_im, inj_re, inj_im)
        return tuple(more)

    _, sums = scan(
        meta, source, None, coef_tiles(dec, groups), batches, span, groups,
        not reverse, not reverse, init, ((zero,) * 4,) * groups, visit,
    )
    small[...] = jnp.zeros_like(small)
    for q in range(groups):
        for kind in range(4):
            small[kind : kind + 1, lanes_of(q)] = jnp.sum(sums[q][kind], axis=0, keepdims=True)
    small[4:5, :] = grad_d[...]
    grad_u[...] = dot(grad_proj[...], b_proj[layer], (1, 1))
    skip = norms[layer + 4 : layer + 5, :]
    plain, times_normed = [], []
    for batch in range(batches):
        average = norm[batch : batch + 1, :]
        scale = norm[batches + batch : batches + batch + 1, :]

        def body(start, carry, batch=batch, average=average, scale=scale):
            rows = pl.ds(batch * span + start, ROWS)
            value = grad_u[rows, :] + grad_mixed[rows, :] * skip
            grad_u[rows, :] = value
            normed = (hidden[rows, :].astype(f32) - average) * scale
            return carry[0] + fold(value), carry[1] + fold(value * normed)

        zero_sum = jnp.zeros((CHUNKS, grad_u.shape[1]), f32)
        one, two = row_loop(span, body, (zero_sum, zero_sum))
        plain.append(one)
        times_normed.append(two)
    add_sums(stats, batches, (plain, times_normed))


def backward_finish_last(cfg, *refs):
    ins, before, (grad_proj, grad_u, sums) = refs[:-4], refs[-4], refs[-3:]
    sums[...] = jnp.zeros_like(sums)
    sums[2 * CHUNKS :, :] = before[...]
    backward_finish(
        cfg, *ins, grad_proj, grad_u, sums.at[pl.ds(0, CHUNKS)], sums.at[pl.ds(CHUNKS, CHUNKS)]
    )


def norm_backward(cfg, stats, grad_out, grad_u, hidden, norm, norms, store, shared):
    layer, reverse, batches, span, groups, tokens, count = cfg
    sums = sum(part[...] for part in stats)
    shared[0:1, :] = jnp.sum(sums[batches:], axis=0, keepdims=True)
    shared[1:2, :] = jnp.sum(sums[:batches], axis=0, keepdims=True)
    gain_now = norms[layer : layer + 1, :]
    for batch in range(batches):
        average = norm[batch : batch + 1, :]
        scale = norm[batches + batch : batches + batch + 1, :]
        plain = gain_now * sums[batch : batch + 1] / tokens
        slanted = gain_now * sums[batches + batch : batches + batch + 1] / tokens

        def body(start, carry, batch=batch, average=average, scale=scale, plain=plain, slanted=slanted):
            rows = pl.ds(batch * span + start, ROWS)
            normed = (hidden[rows, :].astype(f32) - average) * scale
            value = grad_out[rows, :].astype(f32) + scale * (
                grad_u[rows, :] * gain_now - plain - normed * slanted
            )
            store(rows, value)
            return carry

        row_loop(span, body)


def between_layers(
    cfg, lower, place, stats, upper_out, upper_u, upper_hidden, upper_norm, norms,
    disc, u, c_proj, w_gate, states_low, act, sig, slope,
    grad_out, shared, grad_gate, grad_mixed, grad_low, source, prefix, total, grad_d, wide,
):
    def store(rows, value):
        grad_out[rows, :] = value

    norm_backward(cfg, stats, upper_out, upper_u, upper_hidden, upper_norm, norms, store, shared)
    meta = place_documents(lower, place)
    backward_start(
        lower, meta, grad_out, disc, u, c_proj, w_gate, states_low, act, sig, slope,
        grad_gate, grad_mixed, grad_low, source, prefix, total, grad_d, wide,
    )


def last_step(cfg, stats, grad_out, grad_u, hidden, norm, norms, target, shared, ordered):
    layer, reverse, batches, span, groups, tokens, count = cfg
    planes = target.shape[1] // LANES

    def store(rows, value):
        for plane in range(planes):
            ordered[plane, rows, :] = value[:, lanes_of(plane)]

    norm_backward(cfg, stats, grad_out, grad_u, hidden, norm, norms, store, shared)
    steps = span // CHUNKS
    for batch in range(batches):
        for chunk in range(CHUNKS):
            at = batch * span
            for plane in range(planes):
                target[at + chunk * steps : at + (chunk + 1) * steps, lanes_of(plane)] = ordered[
                    plane, pl.ds(at + chunk, steps, stride=CHUNKS), :
                ]


def half_weights(core, refs, own, sent):
    for target, half in ((own, core), (sent, 1 - core)):
        at = 0
        for left, right in refs:
            rows = left.shape[1] // 2
            cols = pl.ds(pl.multiple_of(half * rows, LANES), rows)
            target[at : at + rows, :] = dot(left[:, cols], right[...], (0, 0))
            at += rows


def all_weights(here, act, grad_gate, states_low, grad_low, grad_proj, u, own, sent):
    refs = ((act, grad_gate), (states_low, grad_low), (grad_proj, u))
    half_weights(lax.rem(here[0], 2), refs, own, sent)


def gate_weights(here, act, grad_gate, states_low, grad_low, own, sent):
    half_weights(lax.rem(here[0], 2), ((act, grad_gate), (states_low, grad_low)), own, sent)


def input_weights(here, grad_proj, u, own, sent):
    half_weights(lax.rem(here[0], 2), ((grad_proj, u),), own, sent)


def run(body, name, args, outs, scratch=(), scalars=1):
    vmem, smem = pl.BlockSpec(memory_space=pltpu.VMEM), pl.BlockSpec(memory_space=pltpu.SMEM)
    specs = tuple(
        jax.tree.map(lambda _, at=at: smem if at < scalars else vmem, arg)
        for at, arg in enumerate(args)
    )
    return pl.pallas_call(
        body,
        name=name,
        out_shape=tuple(jax.ShapeDtypeStruct(*out) for out in outs),
        in_specs=specs,
        out_specs=(vmem,) * len(outs),
        scratch_shapes=[pltpu.VMEM(*entry) for entry in scratch],
        compiler_params=pltpu.CompilerParams(vmem_limit_bytes=VMEM_LIMIT),
    )(*args)


def put_in_place(layer, here, halves, outs, before, pieces=1):
    width, states = outs[0][0][1], outs[1][0][1]
    rows_w, rows_c = width // 2, states // 2
    vmem, count = pl.BlockSpec(memory_space=pltpu.VMEM), len(halves)

    def half(step, here):
        core = lax.rem(here[0], 2)
        spots = [1 - core if other else core for other, _ in halves]
        return spots[0] if count == 1 else jnp.where(step == 0, *spots)

    blocks = (
        pl.BlockSpec((1, rows_w, width), lambda i, here: (layer, half(i, here), 0)),
        pl.BlockSpec((1, rows_c, width), lambda i, here: (layer, half(i, here), 0)),
        pl.BlockSpec((1, width, rows_c), lambda i, here: (layer, 0, half(i, here))),
    )

    def body(here, *refs):
        grad_w, grad_c, grad_b = refs[-3:]
        for now in range(count):

            @pl.when(pl.program_id(0) == now)
            def _(source=refs[now]):
                gates, inputs = (rows_w + rows_c) // pieces, rows_c // pieces
                columns = []
                for piece in range(pieces):
                    at, row = piece * (gates + inputs), piece * gates
                    turn = min(max(rows_w - row, 0), gates)
                    if turn:
                        grad_w[0, row : row + turn, :] = source[at : at + turn, :]
                    if turn < gates:
                        to = row + turn - rows_w
                        grad_c[0, to : to + gates - turn, :] = source[at + turn : at + gates, :]
                    columns.append(source[at + gates : at + gates + inputs, :])
                grad_b[0] = jnp.concatenate(columns, axis=0).T

    return pl.pallas_call(
        body,
        name="put_in_place",
        out_shape=tuple(jax.ShapeDtypeStruct(*out) for out in outs),
        grid_spec=pltpu.PrefetchScalarGridSpec(
            num_scalar_prefetch=1,
            grid=(count,),
            in_specs=[vmem] * count + [pl.BlockSpec(memory_space=pl.ANY)] * len(before),
            out_specs=blocks,
        ),
        input_output_aliases={1 + count + i: i for i in range(len(before))},
        compiler_params=pltpu.CompilerParams(vmem_limit_bytes=VMEM_LIMIT),
    )(here, *(rows for _, rows in halves), *before)


def axis_parts():
    count, depth = lax.axis_size("seq"), lax.axis_size("dp")
    return (("seq", 2, 1, count), ("seq", count // 2, 2, count), ("dp", depth, 1, depth))


def shifted(value, part, away):
    name, size, stride, count = part
    pairs = []
    for i in range(count):
        place = (i // stride) % size
        pairs.append((i, i + ((place + away) % size - place) * stride))
    return lax.ppermute(value, name, pairs)


def add_by_shifts(value, parts, *earlier):
    for number, part in enumerate(parts):
        if number:
            value = sum(terms[1:], terms[0])
        if number == len(parts) - 1:
            value, *earlier = lax.optimization_barrier((value, *earlier))
        terms = [value] + [shifted(value, part, away) for away in range(1, part[1])]
    return terms, *earlier


def bits_of(size, stride=1):
    bits = []
    while size > 1:
        bits.append(stride)
        size, stride = size // 2, stride * 2
    return bits


def plane_bits():
    chip_bits = bits_of(lax.axis_size("seq") // 2, 2)
    middle = (len(chip_bits) + 1) // 2
    inner, outer = chip_bits[:middle], chip_bits[middle:]
    return list(zip(inner + outer, outer + inner))


def swap(value, axis, bit):
    return lax.ppermute(value, axis, [(i, i ^ bit) for i in range(lax.axis_size(axis))])


def bit_at(here, axis, bit):
    return lax.rem(lax.div(here[0 if axis == "seq" else 1], bit), 2)


def rows_at(half, rows):
    return pl.ds(pl.multiple_of(half * rows, CHUNKS), rows)


def fold_cores(bits, here, *refs):
    terms, targets = refs[:-4], refs[-4:]
    rows, cols = targets[0].shape
    for side in (0, 1):
        kept, sent = targets[2 * side : 2 * side + 2]
        where = slice(side * cols, (side + 1) * cols)
        bit = bit_at(here, "seq", bits[side])
        for half in (0, 1):

            @pl.when(bit == half)
            def _(half=half, kept=kept, sent=sent, where=where):
                start = 0
                for own, found in zip(terms[0::2], terms[1::2]):
                    for part, target in ((half, kept), (1 - half, sent)):
                        low = max(start, part * rows)
                        high = min(start + own.shape[0], (part + 1) * rows)
                        if low < high:
                            source = slice(low - start, high - start)
                            target[low - part * rows : high - part * rows, :] = (
                                own[source, where] + found[source, where]
                            )
                    start += own.shape[0]


def fold_sides(bits, here, *refs):
    targets, blocks = refs[-4:], refs[:-4]
    for side in (0, 1):
        kept, sent = targets[2 * side : 2 * side + 2]
        half, start = bit_at(here, "seq", bits[side]), 0
        for at in range(0, len(blocks), 4):
            own, found = blocks[at + 2 * side : at + 2 * side + 2]
            rows = own.shape[0] // 2
            to = slice(start, start + rows)
            kept[to, :] = own[rows_at(half, rows), :] + found[rows_at(half, rows), :]
            sent[to, :] = own[rows_at(1 - half, rows), :] + found[rows_at(1 - half, rows), :]
            start += rows


def fold_join(bit, here, left, found_left, right, found_right, kept, sent):
    rows, cols = kept.shape[0], left.shape[1]
    half = bit_at(here, "dp", bit)
    for side, (own, found) in enumerate(((left, found_left), (right, found_right))):
        where = slice(side * cols, (side + 1) * cols)
        kept[:, where] = own[rows_at(half, rows), :] + found[rows_at(half, rows), :]
        sent[:, where] = own[rows_at(1 - half, rows), :] + found[rows_at(1 - half, rows), :]


def fold_depth(bit, here, own, found, kept, sent):
    half, rows = bit_at(here, "dp", bit), kept.shape[0]
    kept[...] = own[rows_at(half, rows), :] + found[rows_at(half, rows), :]
    sent[...] = own[rows_at(1 - half, rows), :] + found[rows_at(1 - half, rows), :]


def add_two(own, found, out):
    out[...] = own[...] + found[...]


def unfold(bit, here, own, found, out):
    half, rows = bit_at(here, "dp", bit), own.shape[0]
    out[rows_at(half, rows), :] = own[...]
    out[rows_at(1 - half, rows), :] = found[...]


def unfold_split(bit, here, own, found, left, right):
    half, rows, cols = bit_at(here, "dp", bit), own.shape[0], left.shape[1]
    for side, out in enumerate((left, right)):
        where = slice(side * cols, (side + 1) * cols)
        out[rows_at(half, rows), :] = own[:, where]
        out[rows_at(1 - half, rows), :] = found[:, where]


def unfold_sides(bits, joined, here, *refs):
    for side in (0, 1):
        own, found = refs[2 * side : 2 * side + 2]
        half, (rows, cols) = bit_at(here, "seq", bits[side]), own.shape
        out = refs[4] if joined else refs[4 + side]
        where = slice(side * cols, (side + 1) * cols) if joined else slice(0, cols)
        out[rows_at(half, rows), where] = own[...]
        out[rows_at(1 - half, rows), where] = found[...]


def link_call(body, here, args, shapes):
    name = body.func.__name__
    return run(body, name, (here, *args), tuple((shape, f32) for shape in shapes))


class LinkSum:
    def __init__(self, here, terms):
        self.here, self.plane = here, plane_bits()
        self.depth = bits_of(lax.axis_size("dp"))
        rows = sum(term.shape[0] for term in terms[::2])
        self.shape = (rows // 2, terms[0].shape[1] // 2)
        self.parts = link_call(
            functools.partial(fold_cores, self.plane[0]), here, terms, (self.shape,) * 4
        )

    def swap_plane(self, stage):
        (left, right), pieces = self.plane[stage], self.parts
        self.parts = (
            pieces[0], swap(pieces[1], "seq", left), pieces[2], swap(pieces[3], "seq", right)
        )

    def down_plane(self, stage, *others):
        parts, rows, cols = list(self.parts), *self.shape
        for other in others:
            parts += other.parts
            rows += other.shape[0]
        self.shape = (rows // 2, cols)
        body = functools.partial(fold_sides, self.plane[stage])
        self.parts = link_call(body, self.here, parts, (self.shape,) * 4)

    def down_join(self):
        rows, cols = self.shape
        self.shape = (rows // 2, 2 * cols)
        body = functools.partial(fold_join, self.depth[0])
        self.parts = link_call(body, self.here, self.parts, (self.shape,) * 2)

    def swap_depth(self, stage):
        self.parts = (self.parts[0], swap(self.parts[1], "dp", self.depth[stage]))

    def down_depth(self, stage):
        rows, cols = self.shape
        self.shape = (rows // 2, cols)
        body = functools.partial(fold_depth, self.depth[stage])
        self.parts = link_call(body, self.here, self.parts, (self.shape,) * 2)

    def middle(self):
        (value,) = run(add_two, "add_two", self.parts, ((self.shape, f32),), scalars=0)
        self.parts = (value, value)

    def up_depth(self, stage):
        rows, cols = self.shape
        self.shape = (rows * 2, cols)
        body = functools.partial(unfold, self.depth[stage])
        (value,) = link_call(body, self.here, self.parts, (self.shape,))
        self.parts = (value, value)

    def up_split(self):
        rows, cols = self.shape
        self.shape = (rows * 2, cols // 2)
        body = functools.partial(unfold_split, self.depth[0])
        left, right = link_call(body, self.here, self.parts, (self.shape,) * 2)
        self.parts = (left, left, right, right)

    def up_plane(self, stage):
        rows, cols = self.shape
        if stage:
            self.shape = (rows * 2, cols)
            body = functools.partial(unfold_sides, self.plane[stage], False)
            left, right = link_call(body, self.here, self.parts, (self.shape,) * 2)
            self.parts = (left, left, right, right)
        else:
            self.shape = (rows * 2, cols * 2)
            body = functools.partial(unfold_sides, self.plane[stage], True)
            self.parts = link_call(body, self.here, self.parts, (self.shape,))

    def after(self, *values):
        self.parts, values = lax.optimization_barrier((self.parts, values))
        return values

    def to_depth(self):
        for stage in range(2, len(self.plane)):
            self.swap_plane(stage - 1)
            self.down_plane(stage)
        self.swap_plane(len(self.plane) - 1)

    def scatter_depth(self):
        for stage in range(len(self.depth) - 1):
            if stage:
                self.down_depth(stage)
            self.swap_depth(stage)

    def swap_whole(self):
        self.parts = (self.parts[0], swap(self.parts[0], "dp", self.depth[-1]))

    def gather_depth(self):
        for stage in range(len(self.depth) - 2, 0, -1):
            self.swap_depth(stage)
            self.up_depth(stage)
        self.swap_depth(0)


def wait_for(*things):
    sums = [thing for thing in things if isinstance(thing, LinkSum)]
    values = [thing for thing in things if not isinstance(thing, LinkSum)]
    parts, values = lax.optimization_barrier(([entry.parts for entry in sums], values))
    for entry, part in zip(sums, parts):
        entry.parts = part
    return values


def discretize(lam_re, lam_im, log_step):
    step_size = jnp.exp(log_step)
    decay_abs = jnp.exp(lam_re * step_size)
    rotation = lam_im * step_size
    dec_re = decay_abs * jnp.cos(rotation)
    dec_im = decay_abs * jnp.sin(rotation)
    denom_sq = lam_re * lam_re + lam_im * lam_im
    inj_re = ((dec_re - 1.0) * lam_re + dec_im * lam_im) / denom_sq
    inj_im = (dec_im * lam_re - (dec_re - 1.0) * lam_im) / denom_sq
    return (dec_re, dec_im, inj_re, inj_im)


def per_device(
    block_in, cotangent, doc_lengths, norm_gain, norm_shift, log_step, lam_re, lam_im,
    b_proj, c_proj, d_skip, w_gate,
):
    batches, seqs, span, width = block_in.shape
    assert seqs == 1 and span % (4 * CHUNKS) == 0 and span & (span - 1) == 0
    half = lam_re.shape[1]
    groups = half // LANES
    rows = batches * span
    count = lax.axis_size("seq")
    tokens = float(seqs * lax.axis_size("dp") * span * count)
    here = jnp.stack([lax.axis_index("seq"), lax.axis_index("dp")]).astype(jnp.int32)
    place = jnp.concatenate([here] + [doc_lengths[batch, 0] for batch in range(batches)])
    place, block_in = lax.optimization_barrier((place, block_in))
    here = place
    disc = discretize(lam_re, lam_im, log_step)

    x = block_in.reshape(rows, width)
    cot = cotangent.reshape(rows, width)
    lower = (0, False, batches, span, groups, tokens, count)
    upper = (1, True, batches, span, groups, tokens, count)
    part = functools.partial

    flat, low = ((rows, width), f32), ((rows, width), bf16)
    wide, wide_low = ((rows, 2 * half), f32), ((rows, 2 * half), bf16)
    padded = ((batches * (span + CHUNKS), 2 * half), f32)
    sums = ((2 * batches, width), f32)
    prefix = ((2, batches * CHUNKS, 2 * half), f32)
    total = ((batches, 2 * half), f32)
    line, shared = ((1, width), f32), ((2, width), f32)
    small = ((8, width), f32)

    def gather_row(value):
        return lax.all_gather(value, "seq")

    (stats,) = run(part(first_sums, batches, span), "first_sums", (x,), (sums,), scalars=0)

    def order(value, inverse):
        body = part(order_rows, batches, span, inverse)
        return run(body, "order_rows", (value,), (low,), scalars=0)[0]

    norms = jnp.concatenate([norm_gain, norm_shift, d_skip], axis=0)

    def forward(cfg, hidden, stats):
        return run(
            part(enter_layer, cfg),
            "enter_layer",
            (place, stats, hidden, norms, disc, b_proj),
            (low, wide, prefix, total, sums),
        )

    links, plane, depth = axis_parts()
    stats, ordered = lax.optimization_barrier(
        (add_by_shifts(stats, (links, plane, depth))[0], order(x, False))
    )
    u0, drive0, prefix0, total0, norm0 = forward(lower, ordered, stats)
    states0, states_low0, act0, sig0, slope0, hidden1, stats = run(
        part(middle_forward, lower),
        "middle_forward",
        (place, gather_row(total0), prefix0, disc, drive0, u0, ordered, c_proj, norms, w_gate),
        (padded, wide_low, low, flat, flat, flat, sums),
        (flat,),
    )
    cot, stats = lax.optimization_barrier((cot, stats))
    stats, ordered_cot = lax.optimization_barrier(
        (add_by_shifts(stats, (links, plane, depth))[0], order(cot, False))
    )
    u1, drive1, prefix1, total1, norm1 = forward(upper, hidden1, stats)
    (
        result1, states1, states_low1, act1, grad_gate1, grad_mixed1, grad_low1,
        source1, prefix1, total1, grad_d1,
    ) = run(
        part(turn_around, upper),
        "turn_around",
        (
            place, gather_row(total1), prefix1, disc, drive1, u1, hidden1, c_proj, norms, w_gate,
            ordered_cot,
        ),
        (low, padded, wide_low, low, low, flat, low, wide, prefix, total, line),
        (flat, flat, flat),
    )

    def halves(length):
        return (((length // 2, width), f32),) * 2

    grad_proj1, grad_u1, stats, small1 = run(
        part(backward_finish, upper),
        "backward_finish",
        (
            place, gather_row(total1), prefix1, disc, source1, drive1, states1, u1, grad_mixed1,
            grad_d1, hidden1, norm1, norms, b_proj,
        ),
        (wide_low, flat, sums, small),
    )
    sizes = (width + 2 * half, 2 * half)
    own1, sent1 = run(
        all_weights,
        "all_weights",
        (here, act1, grad_gate1, states_low1, grad_low1, grad_proj1, u1),
        halves(sum(sizes)),
    )
    stats = stats + swap(stats, "seq", 1)
    stats, sent1 = lax.optimization_barrier((stats, sent1))
    upper_sum = LinkSum(here, (own1, swap(sent1, "seq", 1)))
    stats, upper_sum.parts = add_by_shifts(stats, (plane, depth), upper_sum.parts)
    upper_sum.swap_plane(0)
    (
        grad_out0, shared1, grad_gate0, grad_mixed0, grad_low0, source0, prefix0, total0, grad_d0,
    ) = run(
        part(between_layers, upper, lower),
        "between_layers",
        (
            place, stats, ordered_cot, grad_u1, hidden1, norm1, norms,
            disc, u0, c_proj, w_gate, states_low0, act0, sig0, slope0,
        ),
        (flat, shared, low, flat, low, wide, prefix, total, line),
        (flat,),
    )
    (total0,) = upper_sum.after(total0)
    upper_sum.down_plane(1)
    (total0,) = upper_sum.after(total0)
    upper_sum.to_depth()
    ends, grad_gate0 = wait_for(upper_sum, gather_row(total0), grad_gate0)
    upper_sum.down_join()
    ends, grad_gate0 = wait_for(upper_sum, ends, grad_gate0)
    upper_sum.scatter_depth()
    own_gates, sent_gates = run(
        gate_weights, "gate_weights", (here, act0, grad_gate0, states_low0, grad_low0),
        halves(sizes[0]),
    )
    own_gates, ends = lax.optimization_barrier((own_gates, ends))
    grad_proj0, grad_u0, last_sums = run(
        part(backward_finish_last, lower),
        "backward_finish",
        (
            place, ends, prefix0, disc, source0, drive0, states0, u0, grad_mixed0, grad_d0,
            ordered, norm0, norms, b_proj, small1,
        ),
        (wide_low, flat, ((3 * CHUNKS, width), f32)),
    )
    lower_sum = LinkSum(here, (own_gates, swap(sent_gates, "seq", 1)))
    (grad_proj0,) = wait_for(upper_sum, lower_sum, grad_proj0)
    own_inputs, sent_inputs = run(
        input_weights, "input_weights", (here, grad_proj0, u0), halves(sizes[1])
    )
    inputs_sum = LinkSum(here, (own_inputs, swap(sent_inputs, "seq", 1)))
    upper_sum.middle()
    upper_sum.swap_whole()
    lower_sum.swap_plane(0)
    inputs_sum.swap_plane(0)
    wait_for(upper_sum, lower_sum, inputs_sum)

    lower_sum.down_plane(1, inputs_sum)
    upper_sum.middle()
    upper_sum.gather_depth()
    lower_sum.to_depth()
    wait_for(upper_sum, lower_sum)

    lower_sum.down_join()
    upper_sum.up_split()
    lower_sum.scatter_depth()
    upper_sum.swap_plane(len(upper_sum.plane) - 1)
    wait_for(upper_sum, lower_sum)

    lower_sum.middle()
    (last_sums,) = lower_sum.after(last_sums)
    lower_sum.swap_whole()
    for stage in range(len(upper_sum.plane) - 1, 0, -1):
        upper_sum.up_plane(stage)
        upper_sum.swap_plane(stage - 1)
    last_terms = [last_sums] + [shifted(last_sums, depth, away) for away in range(1, depth[1])]
    last_terms = wait_for(upper_sum, lower_sum, *last_terms)

    lower_sum.middle()
    last_terms = lower_sum.after(*last_terms)
    lower_sum.gather_depth()
    last_sums = sum(last_terms)
    last_sums = last_sums + swap(last_sums, "seq", 1)
    last_terms = [last_sums] + [shifted(last_sums, plane, away) for away in range(1, plane[1])]
    last_terms = wait_for(lower_sum, *last_terms)

    lower_sum.up_split()
    wait_for(upper_sum, lower_sum)
    lower_sum.swap_plane(len(lower_sum.plane) - 1)
    upper_sum.up_plane(0)
    own1, result1 = lax.optimization_barrier((upper_sum.parts[0], result1))
    other1 = swap(own1, "seq", 1)
    for stage in range(len(lower_sum.plane) - 1, 0, -1):
        lower_sum.up_plane(stage)
        lower_sum.swap_plane(stage - 1)
    summed = sum(last_terms)
    grad_input, shared0 = run(
        part(last_step, lower),
        "last_step",
        ((summed[: 2 * batches],), grad_out0, grad_u0, ordered, norm0, norms),
        (flat, shared),
        (((width // LANES, rows, LANES), f32),),
        scalars=0,
    )
    small_sum = summed[CHUNKS:].reshape(2, CHUNKS, width)
    _, pullback = jax.vjp(discretize, lam_re, lam_im, log_step)
    grad_lr, grad_li, grad_ls = pullback(tuple(small_sum[:, kind, :half] for kind in range(4)))
    final = (((2, width, width), f32), ((2, 2 * half, width), f32), ((2, width, 2 * half), f32))
    placed = put_in_place(1, here, ((False, own1), (True, other1)), final, ())
    block_out = order(result1, True)
    block_out, grad_input, grad_lr, grad_li, grad_ls, *placed = wait_for(
        lower_sum, block_out, grad_input, grad_lr, grad_li, grad_ls, *placed
    )

    lower_sum.up_plane(0)
    own0 = lower_sum.parts[0]
    other0 = swap(own0, "seq", 1)
    placed = put_in_place(0, here, ((False, own0),), final, placed, 4)
    grad_w, grad_c, grad_b = put_in_place(0, here, ((True, other0),), final, placed, 4)
    both = jnp.stack([shared0, shared1])
    shape = block_in.shape
    return (
        block_out.reshape(shape), grad_input.reshape(shape), both[:, 0], both[:, 1],
        grad_ls, grad_lr, grad_li, grad_b, grad_c, small_sum[:, 4], grad_w,
    )


def solution(mesh):
    split = P(None, "dp", "seq", None)
    return jax.shard_map(
        per_device,
        mesh=mesh,
        in_specs=(split, split, P(None, "dp", None)) + (P(),) * 9,
        out_specs=(split, split) + (P(),) * 9,
        check_vma=False,
    )
```

```python
import functools

import jax
import jax.numpy as jnp
from jax import lax
from jax.experimental import pallas as pl
from jax.experimental.pallas import tpu as pltpu
from jax.sharding import PartitionSpec as P

f32, bf16 = jnp.float32, jnp.bfloat16
epsilon = 1e-05
tanh_scale = 0.7978845608028654
cubic_term = 0.044715
LANES = 128
CHUNKS = 8
ROWS = 32
VMEM_LIMIT = 16 * 1024 * 1024


def dot(left, right, contract=(1, 0)):
    return lax.dot_general(
        left, right, (((contract[0],), (contract[1],)), ((), ())), preferred_element_type=f32
    )


def reorder(span, inverse):
    shape = (span, span)
    kept, moved = (1, 0) if inverse else (0, 1)
    row = lax.broadcasted_iota(jnp.int32, shape, kept)
    position = lax.broadcasted_iota(jnp.int32, shape, moved)
    source = (row & (CHUNKS - 1)) * (span // CHUNKS) + (row >> 3)
    return jnp.where(position == source, 1.0, 0.0).astype(bf16)


def row_loop(count, body, init=0, step=ROWS):
    def one(index, carry):
        return body(pl.multiple_of(index * step, step), carry)

    return lax.fori_loop(0, count // step, one, init)


def documents(here, batches, span, count):
    mine = here[0]
    first = mine * span
    out = []
    for batch in range(batches):
        begins, ends, so_far = [], [], 0
        docs = (here.shape[0] - 2) // batches
        for doc in range(docs):
            begins.append(so_far)
            so_far = so_far + here[2 + batch * docs + doc]
            ends.append(so_far)
        before, after = 0, 2 * count * span
        for begin, end in zip(begins, ends):
            before = jnp.maximum(before, jnp.where(begin < first, begin, 0))
            after = jnp.minimum(after, jnp.where(end > first + span, end, 2 * count * span))
        after = jnp.where(mine == count - 1, 0, after)
        out.append(begins + ends + [before, after, first, mine])
    return out


def place_documents(cfg, place):
    layer, reverse, batches, span, groups, tokens, count = cfg
    return documents(place, batches, span, count)


def keep_of(meta, batch, base, step, backward):
    docs = (len(meta[batch]) - 4) // 2
    off = docs if backward else 0
    late = 1 if backward else 0
    stop = base == meta[batch][off] - step - late
    for doc in range(1, docs):
        stop = jnp.logical_or(stop, base == meta[batch][off + doc] - step - late)
    return jnp.where(stop, 0.0, 1.0)


def base_positions(meta, steps):
    return meta[0][-2] + lax.broadcasted_iota(jnp.int32, (CHUNKS, LANES), 0) * steps


def lanes_of(index, half=0):
    return slice(half + index * LANES, half + (index + 1) * LANES)


def coef_tiles(value, groups):
    return [
        tuple(jnp.broadcast_to(part[:, lanes_of(q)], (CHUNKS, LANES)) for part in value)
        for q in range(groups)
    ]


def constants(disc, layer):
    dec_re, dec_im, inj_re, inj_im = (part[layer : layer + 1, :] for part in disc)
    return (dec_re, dec_im), (inj_re, inj_im)


def times(a, b):
    return (a[0] * b[0] - a[1] * b[1], a[0] * b[1] + a[1] * b[0])


def power(value, exponent):
    for _ in range(exponent.bit_length() - 1):
        value = times(value, value)
    return value


def conj(value):
    return (value[0], -value[1])


def scan(meta, source, inject, dec, batches, span, groups, reverse, masks_reverse, init, extra, visit):
    steps = span // CHUNKS
    half = groups * LANES
    base = base_positions(meta, steps)

    def pair(index, carry):
        states, more = carry
        states = list(states)
        first = steps - 2 - 2 * index if reverse else 2 * index
        start = pl.multiple_of(first * CHUNKS, 2 * CHUNKS)
        order = (1, 0) if reverse else (0, 1)
        for batch in range(batches):
            keeps = [keep_of(meta, batch, base, first + j, masks_reverse) for j in (0, 1)]
            for q in range(groups):
                rows = pl.ds(batch * span + start, 2 * CHUNKS)
                src_re = source[rows, lanes_of(q)]
                src_im = source[rows, lanes_of(q, half)]
                state = states[batch * groups + q]
                found = [None, None]
                for j in order:
                    part = (
                        src_re[j * CHUNKS : (j + 1) * CHUNKS],
                        src_im[j * CHUNKS : (j + 1) * CHUNKS],
                    )
                    push = times(inject[q], part) if inject is not None else part
                    held = times((keeps[j] * dec[q][0], keeps[j] * dec[q][1]), state)
                    state = (held[0] + push[0], held[1] + push[1])
                    found[j] = state
                states[batch * groups + q] = state
                more = visit(more, batch, q, first, start, found, (src_re, src_im))
            more = visit(more, batch, None, first, start, keeps, None)
        return tuple(states), more

    return lax.fori_loop(0, steps // 2, pair, (tuple(init), extra), unroll=2)


def zero_states(batches, groups):
    zero = jnp.zeros((CHUNKS, LANES), f32)
    return [(zero, zero)] * (batches * groups)


def local_ends(meta, source, inject, dec, batches, span, groups, reverse, prefix, total):
    ones = tuple(jnp.ones((CHUNKS, LANES), f32) for _ in range(batches))

    def visit(more, batch, q, first, start, found, src):
        if q is not None:
            return more
        return tuple(
            value * found[0] * found[1] if at == batch else value for at, value in enumerate(more)
        )

    dec_chunk = coef_tiles(power(dec, span // CHUNKS), groups)
    ends, kept = scan(
        meta, source, inject, coef_tiles(dec, groups), batches, span, groups, reverse, reverse,
        zero_states(batches, groups), ones, visit,
    )
    half = groups * LANES
    row = lax.broadcasted_iota(jnp.int32, (CHUNKS, LANES), 0)
    for batch in range(batches):
        for q in range(groups):
            end = ends[batch * groups + q]
            decay = (kept[batch] * dec_chunk[q][0], kept[batch] * dec_chunk[q][1])
            for shift in (1, 2, 4):
                turn = CHUNKS - shift if reverse else shift
                valid = row < CHUNKS - shift if reverse else row >= shift
                before = [pltpu.roll(value, turn, 0) for value in (*end, *decay)]
                from_before = times(decay, (before[0], before[1]))
                end = (
                    end[0] + jnp.where(valid, from_before[0], 0.0),
                    end[1] + jnp.where(valid, from_before[1], 0.0),
                )
                longer = times(decay, (before[2], before[3]))
                decay = (
                    jnp.where(valid, longer[0], decay[0]),
                    jnp.where(valid, longer[1], decay[1]),
                )
            rows = slice(batch * CHUNKS, (batch + 1) * CHUNKS)
            prefix[0, rows, lanes_of(q)] = end[0]
            prefix[0, rows, lanes_of(q, half)] = end[1]
            prefix[1, rows, lanes_of(q)] = decay[0]
            prefix[1, rows, lanes_of(q, half)] = decay[1]
            last = 0 if reverse else CHUNKS - 1
            total[batch : batch + 1, lanes_of(q)] = end[0][last : last + 1]
            total[batch : batch + 1, lanes_of(q, half)] = end[1][last : last + 1]


def chunk_carries(meta, gathered, dec, prefix, batches, span, groups, reverse):
    count = gathered.shape[0]
    half = groups * LANES
    dec_span = power(dec, span)
    row = lax.broadcasted_iota(jnp.int32, (CHUNKS, LANES), 0)
    mine = meta[0][-1]
    out = []
    for batch in range(batches):

        def add(at, so_far, batch=batch):
            away = count - 2 - at
            if reverse:
                other = mine + 1 + away
                reaches = meta[batch][-3] > other * span
            else:
                other = mine - 1 - away
                reaches = meta[batch][-4] < (mine - away) * span
            other = jnp.clip(other, 0, count - 1)
            value = jnp.where(reaches, gathered[other, pl.ds(batch, 1), :], 0.0)
            moved = times(dec_span, so_far)
            return (moved[0] + value[:, :half], moved[1] + value[:, half:])

        zero = jnp.zeros((1, half), f32)
        enter = lax.fori_loop(0, count - 1, add, (zero, zero), unroll=count <= 8)
        rows = slice(batch * CHUNKS, (batch + 1) * CHUNKS)
        for q in range(groups):
            own = tuple(jnp.broadcast_to(part[:, lanes_of(q)], (CHUNKS, LANES)) for part in enter)
            end = (prefix[0, rows, lanes_of(q)], prefix[0, rows, lanes_of(q, half)])
            decay = (prefix[1, rows, lanes_of(q)], prefix[1, rows, lanes_of(q, half)])
            moved = times(decay, own)
            turn, first = (CHUNKS - 1, CHUNKS - 1) if reverse else (1, 0)
            out.append(
                tuple(
                    jnp.where(row == first, own[i], pltpu.roll(end[i] + moved[i], turn, 0))
                    for i in (0, 1)
                )
            )
    return out


def add_sums(target, batches, sums):
    for kind, per_batch in enumerate(sums):
        for batch in range(batches):
            target[kind * batches + batch : kind * batches + batch + 1, :] = jnp.sum(
                per_batch[batch], axis=0, keepdims=True
            )


def fold(value):
    return sum(value[i : i + CHUNKS] for i in range(CHUNKS, value.shape[0], CHUNKS)) + value[:CHUNKS]


def order_rows(batches, span, inverse, x, out):
    turn = reorder(span, inverse)
    for batch in range(batches):
        rows = slice(batch * span, (batch + 1) * span)
        out[rows, :] = dot(turn, x[rows, :]).astype(bf16)


def first_sums(batches, span, x, stats):
    width = x.shape[1]
    sums, squares = [], []
    for batch in range(batches):

        def body(start, carry, batch=batch):
            value = x[pl.ds(batch * span + start, ROWS), :].astype(f32)
            return carry[0] + fold(value), carry[1] + fold(value * value)

        zero = jnp.zeros((CHUNKS, width), f32)
        one, two = row_loop(span, body, (zero, zero))
        sums.append(one)
        squares.append(two)
    add_sums(stats, batches, (sums, squares))


def enter_layer(
    cfg, place, stats, hidden, norms, disc, b_proj, u, drive, prefix, total, norm
):
    layer, reverse, batches, span, groups, tokens, count = cfg
    sums = sum(part[...] for part in stats)
    average = sums[:batches] / tokens
    spread = sums[batches:] / tokens - average * average
    scale = lax.rsqrt(spread + epsilon)
    norm[:batches, :] = average
    norm[batches:, :] = scale
    gain_now, shift_now = norms[layer : layer + 1, :], norms[layer + 2 : layer + 3, :]
    for batch in range(batches):

        def body(start, carry, batch=batch):
            rows = pl.ds(batch * span + start, ROWS)
            normed = (hidden[rows, :].astype(f32) - average[batch : batch + 1]) * scale[
                batch : batch + 1
            ]
            u[rows, :] = (normed * gain_now + shift_now).astype(bf16)
            return carry

        row_loop(span, body)
    drive[...] = dot(u[...], b_proj[layer])
    meta = place_documents(cfg, place)
    dec, inj = constants(disc, layer)
    local_ends(
        meta, drive, coef_tiles(inj, groups), dec, batches, span, groups, reverse, prefix, total
    )


def finish_states(cfg, meta, ends, prefix, disc, drive, states, states_low):
    layer, reverse, batches, span, groups, tokens, count = cfg
    half = groups * LANES
    padded = span + CHUNKS
    dec, inj = constants(disc, layer)
    init = chunk_carries(meta, ends, dec, prefix, batches, span, groups, reverse)
    for batch in range(batches):
        edge = batch * padded + (span if reverse else 0)
        for q in range(groups):
            states[edge : edge + CHUNKS, lanes_of(q)] = init[batch * groups + q][0]
            states[edge : edge + CHUNKS, lanes_of(q, half)] = init[batch * groups + q][1]

    def visit(more, batch, q, first, start, found, src):
        if q is not None:
            for part, off in ((0, 0), (1, half)):
                both = jnp.concatenate([found[0][part], found[1][part]], axis=0)
                at = batch * padded + (0 if reverse else CHUNKS)
                states[pl.ds(at + start, 2 * CHUNKS), lanes_of(q, off)] = both
                states_low[pl.ds(batch * span + start, 2 * CHUNKS), lanes_of(q, off)] = both.astype(
                    bf16
                )
        return more

    scan(
        meta, drive, coef_tiles(inj, groups), coef_tiles(dec, groups), batches, span, groups,
        reverse, reverse, init, 0, visit,
    )


def forward_finish(
    cfg, meta, ends, prefix, disc, drive, u, hidden, c_proj, norms, w_gate,
    states, states_low, act, sig, slope, result, wide, emit,
):
    layer, reverse, batches, span, groups, tokens, count = cfg
    finish_states(cfg, meta, ends, prefix, disc, drive, states, states_low)
    wide[...] = dot(states_low[...], c_proj[layer])
    skip = norms[layer + 4 : layer + 5, :]

    def body(start, carry):
        rows = pl.ds(start, ROWS)
        mixed = wide[rows, :] + skip * u[rows, :].astype(f32)
        square = mixed * mixed
        th = jnp.tanh(tanh_scale * (mixed + cubic_term * square * mixed))
        half_one = 0.5 * (1.0 + th)
        act[rows, :] = (mixed * half_one).astype(bf16)
        slope[rows, :] = half_one + 0.5 * mixed * (1.0 - th * th) * tanh_scale * (
            1.0 + 3.0 * cubic_term * square
        )
        return carry

    row_loop(batches * span, body)
    wide[...] = dot(act[...], w_gate[layer])
    sums, squares = [], []
    for batch in range(batches):

        def gate(start, carry, batch=batch):
            rows = pl.ds(batch * span + start, ROWS)
            sig_now = 0.5 + 0.5 * jnp.tanh(0.5 * wide[rows, :])
            sig[rows, :] = sig_now
            value = hidden[rows, :].astype(f32) + act[rows, :].astype(f32) * sig_now
            result[rows, :] = value.astype(result.dtype)
            if emit is None:
                return carry
            return carry[0] + fold(value), carry[1] + fold(value * value)

        zero = jnp.zeros((CHUNKS, wide.shape[1]), f32)
        one, two = row_loop(span, gate, (zero, zero))
        sums.append(one)
        squares.append(two)
    if emit is not None:
        add_sums(emit, batches, (sums, squares))


def backward_start(
    cfg, meta, grad_out, disc, u, c_proj, w_gate, states_low, act, sig, slope,
    grad_gate, grad_mixed, grad_low, source, prefix, total, grad_d, wide,
):
    layer, reverse, batches, span, groups, tokens, count = cfg

    def body(start, carry):
        rows = pl.ds(start, ROWS)
        sig_now = sig[rows, :]
        grad_gate[rows, :] = (
            grad_out[rows, :].astype(f32) * act[rows, :].astype(f32) * sig_now * (1.0 - sig_now)
        ).astype(bf16)
        return carry

    row_loop(batches * span, body)
    wide[...] = dot(grad_gate[...], w_gate[layer], (1, 1))

    def mixed(start, carry):
        rows = pl.ds(start, ROWS)
        value = (grad_out[rows, :].astype(f32) * sig[rows, :] + wide[rows, :]) * slope[rows, :]
        grad_mixed[rows, :] = value
        grad_low[rows, :] = value.astype(bf16)
        return carry + fold(value * u[rows, :].astype(f32))

    gd = row_loop(batches * span, mixed, jnp.zeros((CHUNKS, wide.shape[1]), f32))
    grad_d[...] = jnp.sum(gd, axis=0, keepdims=True)
    source[...] = dot(grad_low[...], c_proj[layer], (1, 1))
    local_ends(
        meta, source, None, conj(constants(disc, layer)[0]), batches, span, groups, not reverse,
        prefix, total,
    )


def middle_forward(
    cfg, place, ends, prefix, disc, drive, u, hidden, c_proj, norms, w_gate,
    states, states_low, act, sig, slope, result, stats, wide,
):
    meta = place_documents(cfg, place)
    forward_finish(
        cfg, meta, ends, prefix, disc, drive, u, hidden, c_proj, norms, w_gate,
        states, states_low, act, sig, slope, result, wide, stats,
    )


def turn_around(
    cfg, place, ends, prefix, disc, drive, u, hidden, c_proj, norms, w_gate, ordered_cot,
    result, states, states_low, act, grad_gate, grad_mixed, grad_low, source,
    back_prefix, total, grad_d, sig, slope, wide,
):
    layer, reverse, batches, span, groups, tokens, count = cfg
    meta = place_documents(cfg, place)
    forward_finish(
        cfg, meta, ends, prefix, disc, drive, u, hidden, c_proj, norms, w_gate,
        states, states_low, act, sig, slope, result, wide, None,
    )
    backward_start(
        cfg, meta, ordered_cot, disc, u, c_proj, w_gate, states_low, act, sig, slope,
        grad_gate, grad_mixed, grad_low, source, back_prefix, total, grad_d, wide,
    )


def backward_finish(
    cfg, place, ends, prefix, disc, source, drive, states, u, grad_mixed, grad_d, hidden, norm,
    norms, b_proj, grad_proj, grad_u, stats, small,
):
    layer, reverse, batches, span, groups, tokens, count = cfg
    half = groups * LANES
    padded = span + CHUNKS
    steps = span // CHUNKS
    meta = place_documents(cfg, place)
    dec, inj = constants(disc, layer)
    dec = conj(dec)
    init = chunk_carries(meta, ends, dec, prefix, batches, span, groups, not reverse)
    inj = coef_tiles(inj, groups)
    base = base_positions(meta, steps)
    zero = jnp.zeros((CHUNKS, LANES), f32)

    def visit(more, batch, q, first, start, found, src):
        if q is None:
            return more
        more = list(more)
        rows = pl.ds(batch * span + start, 2 * CHUNKS)
        drive_re, drive_im = drive[rows, lanes_of(q)], drive[rows, lanes_of(q, half)]
        before = pl.ds(batch * padded + start + (CHUNKS if reverse else 0), 2 * CHUNKS)
        prior_re, prior_im = states[before, lanes_of(q)], states[before, lanes_of(q, half)]
        dec_re, dec_im, inj_re, inj_im = more[q]
        out_re, out_im = [], []
        for j in (0, 1):
            part = slice(j * CHUNKS, (j + 1) * CHUNKS)
            adj_re, adj_im = found[j]
            keep = keep_of(meta, batch, base, first + j, reverse)
            kept_re, kept_im = keep * adj_re, keep * adj_im
            dec_re = dec_re + kept_re * prior_re[part] + kept_im * prior_im[part]
            dec_im = dec_im + kept_im * prior_re[part] - kept_re * prior_im[part]
            inj_re = inj_re + adj_re * drive_re[part] + adj_im * drive_im[part]
            inj_im = inj_im + adj_im * drive_re[part] - adj_re * drive_im[part]
            out_re.append(inj[q][0] * adj_re + inj[q][1] * adj_im)
            out_im.append(inj[q][0] * adj_im - inj[q][1] * adj_re)
        grad_proj[rows, lanes_of(q)] = jnp.concatenate(out_re, axis=0).astype(bf16)
        grad_proj[rows, lanes_of(q, half)] = jnp.concatenate(out_im, axis=0).astype(bf16)
        more[q] = (dec_re, dec_im, inj_re, inj_im)
        return tuple(more)

    _, sums = scan(
        meta, source, None, coef_tiles(dec, groups), batches, span, groups,
        not reverse, not reverse, init, ((zero,) * 4,) * groups, visit,
    )
    small[...] = jnp.zeros_like(small)
    for q in range(groups):
        for kind in range(4):
            small[kind : kind + 1, lanes_of(q)] = jnp.sum(sums[q][kind], axis=0, keepdims=True)
    small[4:5, :] = grad_d[...]
    grad_u[...] = dot(grad_proj[...], b_proj[layer], (1, 1))
    skip = norms[layer + 4 : layer + 5, :]
    plain, times_normed = [], []
    for batch in range(batches):
        average = norm[batch : batch + 1, :]
        scale = norm[batches + batch : batches + batch + 1, :]

        def body(start, carry, batch=batch, average=average, scale=scale):
            rows = pl.ds(batch * span + start, ROWS)
            value = grad_u[rows, :] + grad_mixed[rows, :] * skip
            grad_u[rows, :] = value
            normed = (hidden[rows, :].astype(f32) - average) * scale
            return carry[0] + fold(value), carry[1] + fold(value * normed)

        zero_sum = jnp.zeros((CHUNKS, grad_u.shape[1]), f32)
        one, two = row_loop(span, body, (zero_sum, zero_sum))
        plain.append(one)
        times_normed.append(two)
    add_sums(stats, batches, (plain, times_normed))


def backward_finish_last(cfg, *refs):
    ins, before, (grad_proj, grad_u, sums) = refs[:-4], refs[-4], refs[-3:]
    sums[...] = jnp.zeros_like(sums)
    sums[2 * CHUNKS :, :] = before[...]
    backward_finish(
        cfg, *ins, grad_proj, grad_u, sums.at[pl.ds(0, CHUNKS)], sums.at[pl.ds(CHUNKS, CHUNKS)]
    )


def norm_backward(cfg, stats, grad_out, grad_u, hidden, norm, norms, store, shared):
    layer, reverse, batches, span, groups, tokens, count = cfg
    sums = sum(part[...] for part in stats)
    shared[0:1, :] = jnp.sum(sums[batches:], axis=0, keepdims=True)
    shared[1:2, :] = jnp.sum(sums[:batches], axis=0, keepdims=True)
    gain_now = norms[layer : layer + 1, :]
    for batch in range(batches):
        average = norm[batch : batch + 1, :]
        scale = norm[batches + batch : batches + batch + 1, :]
        plain = gain_now * sums[batch : batch + 1] / tokens
        slanted = gain_now * sums[batches + batch : batches + batch + 1] / tokens

        def body(start, carry, batch=batch, average=average, scale=scale, plain=plain, slanted=slanted):
            rows = pl.ds(batch * span + start, ROWS)
            normed = (hidden[rows, :].astype(f32) - average) * scale
            value = grad_out[rows, :].astype(f32) + scale * (
                grad_u[rows, :] * gain_now - plain - normed * slanted
            )
            store(rows, value)
            return carry

        row_loop(span, body)


def between_layers(
    cfg, lower, place, stats, upper_out, upper_u, upper_hidden, upper_norm, norms,
    disc, u, c_proj, w_gate, states_low, act, sig, slope,
    grad_out, shared, grad_gate, grad_mixed, grad_low, source, prefix, total, grad_d, wide,
):
    def store(rows, value):
        grad_out[rows, :] = value

    norm_backward(cfg, stats, upper_out, upper_u, upper_hidden, upper_norm, norms, store, shared)
    meta = place_documents(lower, place)
    backward_start(
        lower, meta, grad_out, disc, u, c_proj, w_gate, states_low, act, sig, slope,
        grad_gate, grad_mixed, grad_low, source, prefix, total, grad_d, wide,
    )


def last_step(cfg, stats, grad_out, grad_u, hidden, norm, norms, target, shared, ordered):
    layer, reverse, batches, span, groups, tokens, count = cfg
    planes = target.shape[1] // LANES

    def store(rows, value):
        for plane in range(planes):
            ordered[plane, rows, :] = value[:, lanes_of(plane)]

    norm_backward(cfg, stats, grad_out, grad_u, hidden, norm, norms, store, shared)
    steps = span // CHUNKS
    for batch in range(batches):
        for chunk in range(CHUNKS):
            at = batch * span
            for plane in range(planes):
                target[at + chunk * steps : at + (chunk + 1) * steps, lanes_of(plane)] = ordered[
                    plane, pl.ds(at + chunk, steps, stride=CHUNKS), :
                ]


def half_weights(core, refs, own, sent):
    for target, half in ((own, core), (sent, 1 - core)):
        at = 0
        for left, right in refs:
            rows = left.shape[1] // 2
            cols = pl.ds(pl.multiple_of(half * rows, LANES), rows)
            target[at : at + rows, :] = dot(left[:, cols], right[...], (0, 0))
            at += rows


def all_weights(here, act, grad_gate, states_low, grad_low, grad_proj, u, own, sent):
    refs = ((act, grad_gate), (states_low, grad_low), (grad_proj, u))
    half_weights(lax.rem(here[0], 2), refs, own, sent)


def gate_weights(here, act, grad_gate, states_low, grad_low, own, sent):
    half_weights(lax.rem(here[0], 2), ((act, grad_gate), (states_low, grad_low)), own, sent)


def input_weights(here, grad_proj, u, own, sent):
    half_weights(lax.rem(here[0], 2), ((grad_proj, u),), own, sent)


def run(body, name, args, outs, scratch=(), scalars=1):
    vmem, smem = pl.BlockSpec(memory_space=pltpu.VMEM), pl.BlockSpec(memory_space=pltpu.SMEM)
    specs = tuple(
        jax.tree.map(lambda _, at=at: smem if at < scalars else vmem, arg)
        for at, arg in enumerate(args)
    )
    return pl.pallas_call(
        body,
        name=name,
        out_shape=tuple(jax.ShapeDtypeStruct(*out) for out in outs),
        in_specs=specs,
        out_specs=(vmem,) * len(outs),
        scratch_shapes=[pltpu.VMEM(*entry) for entry in scratch],
        compiler_params=pltpu.CompilerParams(vmem_limit_bytes=VMEM_LIMIT),
    )(*args)


def put_in_place(layer, here, halves, outs, before, pieces=1):
    width, states = outs[0][0][1], outs[1][0][1]
    rows_w, rows_c = width // 2, states // 2
    vmem, count = pl.BlockSpec(memory_space=pltpu.VMEM), len(halves)

    def half(step, here):
        core = lax.rem(here[0], 2)
        spots = [1 - core if other else core for other, _ in halves]
        return spots[0] if count == 1 else jnp.where(step == 0, *spots)

    blocks = (
        pl.BlockSpec((1, rows_w, width), lambda i, here: (layer, half(i, here), 0)),
        pl.BlockSpec((1, rows_c, width), lambda i, here: (layer, half(i, here), 0)),
        pl.BlockSpec((1, width, rows_c), lambda i, here: (layer, 0, half(i, here))),
    )

    def body(here, *refs):
        grad_w, grad_c, grad_b = refs[-3:]
        for now in range(count):

            @pl.when(pl.program_id(0) == now)
            def _(source=refs[now]):
                gates, inputs = (rows_w + rows_c) // pieces, rows_c // pieces
                columns = []
                for piece in range(pieces):
                    at, row = piece * (gates + inputs), piece * gates
                    turn = min(max(rows_w - row, 0), gates)
                    if turn:
                        grad_w[0, row : row + turn, :] = source[at : at + turn, :]
                    if turn < gates:
                        to = row + turn - rows_w
                        grad_c[0, to : to + gates - turn, :] = source[at + turn : at + gates, :]
                    columns.append(source[at + gates : at + gates + inputs, :])
                grad_b[0] = jnp.concatenate(columns, axis=0).T

    return pl.pallas_call(
        body,
        name="put_in_place",
        out_shape=tuple(jax.ShapeDtypeStruct(*out) for out in outs),
        grid_spec=pltpu.PrefetchScalarGridSpec(
            num_scalar_prefetch=1,
            grid=(count,),
            in_specs=[vmem] * count + [pl.BlockSpec(memory_space=pl.ANY)] * len(before),
            out_specs=blocks,
        ),
        input_output_aliases={1 + count + i: i for i in range(len(before))},
        compiler_params=pltpu.CompilerParams(vmem_limit_bytes=VMEM_LIMIT),
    )(here, *(rows for _, rows in halves), *before)


def axis_parts():
    count, depth = lax.axis_size("seq"), lax.axis_size("dp")
    return (("seq", 2, 1, count), ("seq", count // 2, 2, count), ("dp", depth, 1, depth))


def shifted(value, part, away):
    name, size, stride, count = part
    pairs = []
    for i in range(count):
        place = (i // stride) % size
        pairs.append((i, i + ((place + away) % size - place) * stride))
    return lax.ppermute(value, name, pairs)


def add_by_shifts(value, parts, *earlier):
    for number, part in enumerate(parts):
        if number:
            value = sum(terms[1:], terms[0])
        if number == len(parts) - 1:
            value, *earlier = lax.optimization_barrier((value, *earlier))
        terms = [value] + [shifted(value, part, away) for away in range(1, part[1])]
    return terms, *earlier


def bits_of(size, stride=1):
    bits = []
    while size > 1:
        bits.append(stride)
        size, stride = size // 2, stride * 2
    return bits


def plane_bits():
    chip_bits = bits_of(lax.axis_size("seq") // 2, 2)
    middle = (len(chip_bits) + 1) // 2
    inner, outer = chip_bits[:middle], chip_bits[middle:]
    return list(zip(inner + outer, outer + inner))


def swap(value, axis, bit):
    return lax.ppermute(value, axis, [(i, i ^ bit) for i in range(lax.axis_size(axis))])


def bit_at(here, axis, bit):
    return lax.rem(lax.div(here[0 if axis == "seq" else 1], bit), 2)


def rows_at(half, rows):
    return pl.ds(pl.multiple_of(half * rows, CHUNKS), rows)


def fold_cores(bits, here, *refs):
    terms, targets = refs[:-4], refs[-4:]
    rows, cols = targets[0].shape
    for side in (0, 1):
        kept, sent = targets[2 * side : 2 * side + 2]
        where = slice(side * cols, (side + 1) * cols)
        bit = bit_at(here, "seq", bits[side])
        for half in (0, 1):

            @pl.when(bit == half)
            def _(half=half, kept=kept, sent=sent, where=where):
                start = 0
                for own, found in zip(terms[0::2], terms[1::2]):
                    for part, target in ((half, kept), (1 - half, sent)):
                        low = max(start, part * rows)
                        high = min(start + own.shape[0], (part + 1) * rows)
                        if low < high:
                            source = slice(low - start, high - start)
                            target[low - part * rows : high - part * rows, :] = (
                                own[source, where] + found[source, where]
                            )
                    start += own.shape[0]


def fold_sides(bits, here, *refs):
    targets, blocks = refs[-4:], refs[:-4]
    for side in (0, 1):
        kept, sent = targets[2 * side : 2 * side + 2]
        half, start = bit_at(here, "seq", bits[side]), 0
        for at in range(0, len(blocks), 4):
            own, found = blocks[at + 2 * side : at + 2 * side + 2]
            rows = own.shape[0] // 2
            to = slice(start, start + rows)
            kept[to, :] = own[rows_at(half, rows), :] + found[rows_at(half, rows), :]
            sent[to, :] = own[rows_at(1 - half, rows), :] + found[rows_at(1 - half, rows), :]
            start += rows


def fold_join(bit, here, left, found_left, right, found_right, kept, sent):
    rows, cols = kept.shape[0], left.shape[1]
    half = bit_at(here, "dp", bit)
    for side, (own, found) in enumerate(((left, found_left), (right, found_right))):
        where = slice(side * cols, (side + 1) * cols)
        kept[:, where] = own[rows_at(half, rows), :] + found[rows_at(half, rows), :]
        sent[:, where] = own[rows_at(1 - half, rows), :] + found[rows_at(1 - half, rows), :]


def fold_depth(bit, here, own, found, kept, sent):
    half, rows = bit_at(here, "dp", bit), kept.shape[0]
    kept[...] = own[rows_at(half, rows), :] + found[rows_at(half, rows), :]
    sent[...] = own[rows_at(1 - half, rows), :] + found[rows_at(1 - half, rows), :]


def add_two(own, found, out):
    out[...] = own[...] + found[...]


def unfold(bit, here, own, found, out):
    half, rows = bit_at(here, "dp", bit), own.shape[0]
    out[rows_at(half, rows), :] = own[...]
    out[rows_at(1 - half, rows), :] = found[...]


def unfold_split(bit, here, own, found, left, right):
    half, rows, cols = bit_at(here, "dp", bit), own.shape[0], left.shape[1]
    for side, out in enumerate((left, right)):
        where = slice(side * cols, (side + 1) * cols)
        out[rows_at(half, rows), :] = own[:, where]
        out[rows_at(1 - half, rows), :] = found[:, where]


def unfold_sides(bits, joined, here, *refs):
    for side in (0, 1):
        own, found = refs[2 * side : 2 * side + 2]
        half, (rows, cols) = bit_at(here, "seq", bits[side]), own.shape
        out = refs[4] if joined else refs[4 + side]
        where = slice(side * cols, (side + 1) * cols) if joined else slice(0, cols)
        out[rows_at(half, rows), where] = own[...]
        out[rows_at(1 - half, rows), where] = found[...]


def link_call(body, here, args, shapes):
    name = body.func.__name__
    return run(body, name, (here, *args), tuple((shape, f32) for shape in shapes))


class LinkSum:
    def __init__(self, here, terms):
        self.here, self.plane = here, plane_bits()
        self.depth = bits_of(lax.axis_size("dp"))
        rows = sum(term.shape[0] for term in terms[::2])
        self.shape = (rows // 2, terms[0].shape[1] // 2)
        self.parts = link_call(
            functools.partial(fold_cores, self.plane[0]), here, terms, (self.shape,) * 4
        )

    def swap_plane(self, stage):
        (left, right), pieces = self.plane[stage], self.parts
        self.parts = (
            pieces[0], swap(pieces[1], "seq", left), pieces[2], swap(pieces[3], "seq", right)
        )

    def down_plane(self, stage, *others):
        parts, rows, cols = list(self.parts), *self.shape
        for other in others:
            parts += other.parts
            rows += other.shape[0]
        self.shape = (rows // 2, cols)
        body = functools.partial(fold_sides, self.plane[stage])
        self.parts = link_call(body, self.here, parts, (self.shape,) * 4)

    def down_join(self):
        rows, cols = self.shape
        self.shape = (rows // 2, 2 * cols)
        body = functools.partial(fold_join, self.depth[0])
        self.parts = link_call(body, self.here, self.parts, (self.shape,) * 2)

    def swap_depth(self, stage):
        self.parts = (self.parts[0], swap(self.parts[1], "dp", self.depth[stage]))

    def down_depth(self, stage):
        rows, cols = self.shape
        self.shape = (rows // 2, cols)
        body = functools.partial(fold_depth, self.depth[stage])
        self.parts = link_call(body, self.here, self.parts, (self.shape,) * 2)

    def middle(self):
        (value,) = run(add_two, "add_two", self.parts, ((self.shape, f32),), scalars=0)
        self.parts = (value, value)

    def up_depth(self, stage):
        rows, cols = self.shape
        self.shape = (rows * 2, cols)
        body = functools.partial(unfold, self.depth[stage])
        (value,) = link_call(body, self.here, self.parts, (self.shape,))
        self.parts = (value, value)

    def up_split(self):
        rows, cols = self.shape
        self.shape = (rows * 2, cols // 2)
        body = functools.partial(unfold_split, self.depth[0])
        left, right = link_call(body, self.here, self.parts, (self.shape,) * 2)
        self.parts = (left, left, right, right)

    def up_plane(self, stage):
        rows, cols = self.shape
        if stage:
            self.shape = (rows * 2, cols)
            body = functools.partial(unfold_sides, self.plane[stage], False)
            left, right = link_call(body, self.here, self.parts, (self.shape,) * 2)
            self.parts = (left, left, right, right)
        else:
            self.shape = (rows * 2, cols * 2)
            body = functools.partial(unfold_sides, self.plane[stage], True)
            self.parts = link_call(body, self.here, self.parts, (self.shape,))

    def after(self, *values):
        self.parts, values = lax.optimization_barrier((self.parts, values))
        return values

    def to_depth(self):
        for stage in range(2, len(self.plane)):
            self.swap_plane(stage - 1)
            self.down_plane(stage)
        self.swap_plane(len(self.plane) - 1)

    def scatter_depth(self):
        for stage in range(len(self.depth) - 1):
            if stage:
                self.down_depth(stage)
            self.swap_depth(stage)

    def swap_whole(self):
        self.parts = (self.parts[0], swap(self.parts[0], "dp", self.depth[-1]))

    def gather_depth(self):
        for stage in range(len(self.depth) - 2, 0, -1):
            self.swap_depth(stage)
            self.up_depth(stage)
        self.swap_depth(0)


def wait_for(*things):
    sums = [thing for thing in things if isinstance(thing, LinkSum)]
    values = [thing for thing in things if not isinstance(thing, LinkSum)]
    parts, values = lax.optimization_barrier(([entry.parts for entry in sums], values))
    for entry, part in zip(sums, parts):
        entry.parts = part
    return values


def discretize(lam_re, lam_im, log_step):
    step_size = jnp.exp(log_step)
    decay_abs = jnp.exp(lam_re * step_size)
    rotation = lam_im * step_size
    dec_re = decay_abs * jnp.cos(rotation)
    dec_im = decay_abs * jnp.sin(rotation)
    denom_sq = lam_re * lam_re + lam_im * lam_im
    inj_re = ((dec_re - 1.0) * lam_re + dec_im * lam_im) / denom_sq
    inj_im = (dec_im * lam_re - (dec_re - 1.0) * lam_im) / denom_sq
    return (dec_re, dec_im, inj_re, inj_im)


def per_device(
    block_in, cotangent, doc_lengths, norm_gain, norm_shift, log_step, lam_re, lam_im,
    b_proj, c_proj, d_skip, w_gate,
):
    batches, seqs, span, width = block_in.shape
    assert seqs == 1 and span % (4 * CHUNKS) == 0 and span & (span - 1) == 0
    half = lam_re.shape[1]
    groups = half // LANES
    rows = batches * span
    count = lax.axis_size("seq")
    tokens = float(seqs * lax.axis_size("dp") * span * count)
    here = jnp.stack([lax.axis_index("seq"), lax.axis_index("dp")]).astype(jnp.int32)
    place = jnp.concatenate([here] + [doc_lengths[batch, 0] for batch in range(batches)])
    place, block_in = lax.optimization_barrier((place, block_in))
    here = place
    disc = discretize(lam_re, lam_im, log_step)

    x = block_in.reshape(rows, width)
    cot = cotangent.reshape(rows, width)
    lower = (0, False, batches, span, groups, tokens, count)
    upper = (1, True, batches, span, groups, tokens, count)
    part = functools.partial

    flat, low = ((rows, width), f32), ((rows, width), bf16)
    wide, wide_low = ((rows, 2 * half), f32), ((rows, 2 * half), bf16)
    padded = ((batches * (span + CHUNKS), 2 * half), f32)
    sums = ((2 * batches, width), f32)
    prefix = ((2, batches * CHUNKS, 2 * half), f32)
    total = ((batches, 2 * half), f32)
    line, shared = ((1, width), f32), ((2, width), f32)
    small = ((8, width), f32)

    def gather_row(value):
        return lax.all_gather(value, "seq")

    (stats,) = run(part(first_sums, batches, span), "first_sums", (x,), (sums,), scalars=0)

    def order(value, inverse):
        body = part(order_rows, batches, span, inverse)
        return run(body, "order_rows", (value,), (low,), scalars=0)[0]

    norms = jnp.concatenate([norm_gain, norm_shift, d_skip], axis=0)

    def forward(cfg, hidden, stats):
        return run(
            part(enter_layer, cfg),
            "enter_layer",
            (place, stats, hidden, norms, disc, b_proj),
            (low, wide, prefix, total, sums),
        )

    links, plane, depth = axis_parts()
    stats, ordered = lax.optimization_barrier(
        (add_by_shifts(stats, (links, plane, depth))[0], order(x, False))
    )
    u0, drive0, prefix0, total0, norm0 = forward(lower, ordered, stats)
    states0, states_low0, act0, sig0, slope0, hidden1, stats = run(
        part(middle_forward, lower),
        "middle_forward",
        (place, gather_row(total0), prefix0, disc, drive0, u0, ordered, c_proj, norms, w_gate),
        (padded, wide_low, low, flat, flat, flat, sums),
        (flat,),
    )
    cot, stats = lax.optimization_barrier((cot, stats))
    stats, ordered_cot = lax.optimization_barrier(
        (add_by_shifts(stats, (links, plane, depth))[0], order(cot, False))
    )
    u1, drive1, prefix1, total1, norm1 = forward(upper, hidden1, stats)
    (
        result1, states1, states_low1, act1, grad_gate1, grad_mixed1, grad_low1,
        source1, prefix1, total1, grad_d1,
    ) = run(
        part(turn_around, upper),
        "turn_around",
        (
            place, gather_row(total1), prefix1, disc, drive1, u1, hidden1, c_proj, norms, w_gate,
            ordered_cot,
        ),
        (low, padded, wide_low, low, low, flat, low, wide, prefix, total, line),
        (flat, flat, flat),
    )

    def halves(length):
        return (((length // 2, width), f32),) * 2

    grad_proj1, grad_u1, stats, small1 = run(
        part(backward_finish, upper),
        "backward_finish",
        (
            place, gather_row(total1), prefix1, disc, source1, drive1, states1, u1, grad_mixed1,
            grad_d1, hidden1, norm1, norms, b_proj,
        ),
        (wide_low, flat, sums, small),
    )
    sizes = (width + 2 * half, 2 * half)
    own1, sent1 = run(
        all_weights,
        "all_weights",
        (here, act1, grad_gate1, states_low1, grad_low1, grad_proj1, u1),
        halves(sum(sizes)),
    )
    stats = stats + swap(stats, "seq", 1)
    stats, sent1 = lax.optimization_barrier((stats, sent1))
    upper_sum = LinkSum(here, (own1, swap(sent1, "seq", 1)))
    stats, upper_sum.parts = add_by_shifts(stats, (plane, depth), upper_sum.parts)
    upper_sum.swap_plane(0)
    (
        grad_out0, shared1, grad_gate0, grad_mixed0, grad_low0, source0, prefix0, total0, grad_d0,
    ) = run(
        part(between_layers, upper, lower),
        "between_layers",
        (
            place, stats, ordered_cot, grad_u1, hidden1, norm1, norms,
            disc, u0, c_proj, w_gate, states_low0, act0, sig0, slope0,
        ),
        (flat, shared, low, flat, low, wide, prefix, total, line),
        (flat,),
    )
    (total0,) = upper_sum.after(total0)
    upper_sum.down_plane(1)
    (total0,) = upper_sum.after(total0)
    upper_sum.to_depth()
    ends, grad_gate0 = wait_for(upper_sum, gather_row(total0), grad_gate0)
    upper_sum.down_join()
    ends, grad_gate0 = wait_for(upper_sum, ends, grad_gate0)
    upper_sum.scatter_depth()
    own_gates, sent_gates = run(
        gate_weights, "gate_weights", (here, act0, grad_gate0, states_low0, grad_low0),
        halves(sizes[0]),
    )
    own_gates, ends = lax.optimization_barrier((own_gates, ends))
    grad_proj0, grad_u0, last_sums = run(
        part(backward_finish_last, lower),
        "backward_finish",
        (
            place, ends, prefix0, disc, source0, drive0, states0, u0, grad_mixed0, grad_d0,
            ordered, norm0, norms, b_proj, small1,
        ),
        (wide_low, flat, ((3 * CHUNKS, width), f32)),
    )
    lower_sum = LinkSum(here, (own_gates, swap(sent_gates, "seq", 1)))
    (grad_proj0,) = wait_for(upper_sum, lower_sum, grad_proj0)
    own_inputs, sent_inputs = run(
        input_weights, "input_weights", (here, grad_proj0, u0), halves(sizes[1])
    )
    inputs_sum = LinkSum(here, (own_inputs, swap(sent_inputs, "seq", 1)))
    upper_sum.middle()
    upper_sum.swap_whole()
    lower_sum.swap_plane(0)
    inputs_sum.swap_plane(0)
    wait_for(upper_sum, lower_sum, inputs_sum)

    lower_sum.down_plane(1, inputs_sum)
    upper_sum.middle()
    upper_sum.gather_depth()
    lower_sum.to_depth()
    wait_for(upper_sum, lower_sum)

    lower_sum.down_join()
    upper_sum.up_split()
    lower_sum.scatter_depth()
    upper_sum.swap_plane(len(upper_sum.plane) - 1)
    wait_for(upper_sum, lower_sum)

    lower_sum.middle()
    lower_sum.swap_whole()
    for stage in range(len(upper_sum.plane) - 1, 0, -1):
        upper_sum.up_plane(stage)
        upper_sum.swap_plane(stage - 1)
    (last_sums,) = wait_for(upper_sum, lower_sum, last_sums)

    lower_sum.middle()
    (last_sums,) = lower_sum.after(last_sums)
    lower_sum.gather_depth()
    last_sums = last_sums + swap(last_sums, "seq", 1)
    last_terms = [last_sums] + [shifted(last_sums, plane, away) for away in range(1, plane[1])]
    last_terms = wait_for(lower_sum, *last_terms)

    lower_sum.up_split()
    wait_for(upper_sum, lower_sum)
    lower_sum.swap_plane(len(lower_sum.plane) - 1)
    upper_sum.up_plane(0)
    own1, result1 = lax.optimization_barrier((upper_sum.parts[0], result1))
    other1 = swap(own1, "seq", 1)
    block_out = order(result1, True)
    final = (((2, width, width), f32), ((2, 2 * half, width), f32), ((2, width, 2 * half), f32))
    placed = put_in_place(1, here, ((False, own1), (True, other1)), final, ())
    last_sums, bits = sum(last_terms), bits_of(lax.axis_size("dp"))
    for bit in bits[:-1]:
        last_sums = last_sums + swap(last_sums, "dp", bit)
    last_sums, block_out, *placed = wait_for(lower_sum, last_sums, block_out, *placed)

    for stage in range(len(lower_sum.plane) - 1, 0, -1):
        lower_sum.up_plane(stage)
        if stage == 1:
            (last_sums,) = lower_sum.after(last_sums)
        lower_sum.swap_plane(stage - 1)
    summed = last_sums + swap(last_sums, "dp", bits[-1])
    grad_input, shared0 = run(
        part(last_step, lower),
        "last_step",
        ((summed[: 2 * batches],), grad_out0, grad_u0, ordered, norm0, norms),
        (flat, shared),
        (((width // LANES, rows, LANES), f32),),
        scalars=0,
    )
    small_sum = summed[CHUNKS:].reshape(2, CHUNKS, width)
    _, pullback = jax.vjp(discretize, lam_re, lam_im, log_step)
    grad_lr, grad_li, grad_ls = pullback(tuple(small_sum[:, kind, :half] for kind in range(4)))
    grad_input, grad_lr, grad_li, grad_ls = wait_for(
        lower_sum, grad_input, grad_lr, grad_li, grad_ls
    )

    lower_sum.up_plane(0)
    own0 = lower_sum.parts[0]
    other0 = swap(own0, "seq", 1)
    placed = put_in_place(0, here, ((False, own0),), final, placed, 4)
    grad_w, grad_c, grad_b = put_in_place(0, here, ((True, other0),), final, placed, 4)
    both = jnp.stack([shared0, shared1])
    shape = block_in.shape
    return (
        block_out.reshape(shape), grad_input.reshape(shape), both[:, 0], both[:, 1],
        grad_ls, grad_lr, grad_li, grad_b, grad_c, small_sum[:, 4], grad_w,
    )


def solution(mesh):
    split = P(None, "dp", "seq", None)
    return jax.shard_map(
        per_device,
        mesh=mesh,
        in_specs=(split, split, P(None, "dp", None)) + (P(),) * 9,
        out_specs=(split, split) + (P(),) * 9,
        check_vma=False,
    )
```

```python
import functools

import jax
import jax.numpy as jnp
from jax import lax
from jax.experimental import pallas as pl
from jax.experimental.pallas import tpu as pltpu
from jax.sharding import PartitionSpec as P

f32, bf16 = jnp.float32, jnp.bfloat16
epsilon = 1e-05
tanh_scale = 0.7978845608028654
cubic_term = 0.044715
LANES = 128
CHUNKS = 8
ROWS = 32
VMEM_LIMIT = 16 * 1024 * 1024


def dot(left, right, contract=(1, 0)):
    return lax.dot_general(
        left, right, (((contract[0],), (contract[1],)), ((), ())), preferred_element_type=f32
    )


def reorder(span, inverse):
    shape = (span, span)
    kept, moved = (1, 0) if inverse else (0, 1)
    row = lax.broadcasted_iota(jnp.int32, shape, kept)
    position = lax.broadcasted_iota(jnp.int32, shape, moved)
    source = (row & (CHUNKS - 1)) * (span // CHUNKS) + (row >> 3)
    return jnp.where(position == source, 1.0, 0.0).astype(bf16)


def row_loop(count, body, init=0, step=ROWS):
    def one(index, carry):
        return body(pl.multiple_of(index * step, step), carry)

    return lax.fori_loop(0, count // step, one, init, unroll=2)


def documents(here, batches, span, count):
    mine = here[0]
    first = mine * span
    out = []
    for batch in range(batches):
        begins, ends, so_far = [], [], 0
        docs = (here.shape[0] - 2) // batches
        for doc in range(docs):
            begins.append(so_far)
            so_far = so_far + here[2 + batch * docs + doc]
            ends.append(so_far)
        before, after = 0, 2 * count * span
        for begin, end in zip(begins, ends):
            before = jnp.maximum(before, jnp.where(begin < first, begin, 0))
            after = jnp.minimum(after, jnp.where(end > first + span, end, 2 * count * span))
        after = jnp.where(mine == count - 1, 0, after)
        out.append(begins + ends + [before, after, first, mine])
    return out


def place_documents(cfg, place):
    layer, reverse, batches, span, groups, tokens, count = cfg
    return documents(place, batches, span, count)


def keep_of(meta, batch, base, step, backward):
    docs = (len(meta[batch]) - 4) // 2
    off = docs if backward else 0
    late = 1 if backward else 0
    stop = base == meta[batch][off] - step - late
    for doc in range(1, docs):
        stop = jnp.logical_or(stop, base == meta[batch][off + doc] - step - late)
    return jnp.where(stop, 0.0, 1.0)


def base_positions(meta, steps):
    return meta[0][-2] + lax.broadcasted_iota(jnp.int32, (CHUNKS, LANES), 0) * steps


def lanes_of(index, half=0):
    return slice(half + index * LANES, half + (index + 1) * LANES)


def coef_tiles(value, groups):
    return [
        tuple(jnp.broadcast_to(part[:, lanes_of(q)], (CHUNKS, LANES)) for part in value)
        for q in range(groups)
    ]


def constants(disc, layer):
    dec_re, dec_im, inj_re, inj_im = (part[layer : layer + 1, :] for part in disc)
    return (dec_re, dec_im), (inj_re, inj_im)


def times(a, b):
    return (a[0] * b[0] - a[1] * b[1], a[0] * b[1] + a[1] * b[0])


def power(value, exponent):
    for _ in range(exponent.bit_length() - 1):
        value = times(value, value)
    return value


def conj(value):
    return (value[0], -value[1])


def scan(meta, source, inject, dec, batches, span, groups, reverse, masks_reverse, init, extra, visit):
    steps = span // CHUNKS
    half = groups * LANES
    base = base_positions(meta, steps)

    def pair(index, carry):
        states, more = carry
        states = list(states)
        first = steps - 2 - 2 * index if reverse else 2 * index
        start = pl.multiple_of(first * CHUNKS, 2 * CHUNKS)
        order = (1, 0) if reverse else (0, 1)
        for batch in range(batches):
            keeps = [keep_of(meta, batch, base, first + j, masks_reverse) for j in (0, 1)]
            for q in range(groups):
                rows = pl.ds(batch * span + start, 2 * CHUNKS)
                src_re = source[rows, lanes_of(q)]
                src_im = source[rows, lanes_of(q, half)]
                state = states[batch * groups + q]
                found = [None, None]
                for j in order:
                    part = (
                        src_re[j * CHUNKS : (j + 1) * CHUNKS],
                        src_im[j * CHUNKS : (j + 1) * CHUNKS],
                    )
                    push = times(inject[q], part) if inject is not None else part
                    held = times((keeps[j] * dec[q][0], keeps[j] * dec[q][1]), state)
                    state = (held[0] + push[0], held[1] + push[1])
                    found[j] = state
                states[batch * groups + q] = state
                more = visit(more, batch, q, first, start, found, (src_re, src_im))
            more = visit(more, batch, None, first, start, keeps, None)
        return tuple(states), more

    return lax.fori_loop(0, steps // 2, pair, (tuple(init), extra), unroll=4)


def zero_states(batches, groups):
    zero = jnp.zeros((CHUNKS, LANES), f32)
    return [(zero, zero)] * (batches * groups)


def local_ends(meta, source, inject, dec, batches, span, groups, reverse, prefix, total):
    ones = tuple(jnp.ones((CHUNKS, LANES), f32) for _ in range(batches))

    def visit(more, batch, q, first, start, found, src):
        if q is not None:
            return more
        return tuple(
            value * found[0] * found[1] if at == batch else value for at, value in enumerate(more)
        )

    dec_chunk = coef_tiles(power(dec, span // CHUNKS), groups)
    ends, kept = scan(
        meta, source, inject, coef_tiles(dec, groups), batches, span, groups, reverse, reverse,
        zero_states(batches, groups), ones, visit,
    )
    half = groups * LANES
    row = lax.broadcasted_iota(jnp.int32, (CHUNKS, LANES), 0)
    for batch in range(batches):
        for q in range(groups):
            end = ends[batch * groups + q]
            decay = (kept[batch] * dec_chunk[q][0], kept[batch] * dec_chunk[q][1])
            for shift in (1, 2, 4):
                turn = CHUNKS - shift if reverse else shift
                valid = row < CHUNKS - shift if reverse else row >= shift
                before = [pltpu.roll(value, turn, 0) for value in (*end, *decay)]
                from_before = times(decay, (before[0], before[1]))
                end = (
                    end[0] + jnp.where(valid, from_before[0], 0.0),
                    end[1] + jnp.where(valid, from_before[1], 0.0),
                )
                longer = times(decay, (before[2], before[3]))
                decay = (
                    jnp.where(valid, longer[0], decay[0]),
                    jnp.where(valid, longer[1], decay[1]),
                )
            rows = slice(batch * CHUNKS, (batch + 1) * CHUNKS)
            prefix[0, rows, lanes_of(q)] = end[0]
            prefix[0, rows, lanes_of(q, half)] = end[1]
            prefix[1, rows, lanes_of(q)] = decay[0]
            prefix[1, rows, lanes_of(q, half)] = decay[1]
            last = 0 if reverse else CHUNKS - 1
            total[batch : batch + 1, lanes_of(q)] = end[0][last : last + 1]
            total[batch : batch + 1, lanes_of(q, half)] = end[1][last : last + 1]


def chunk_carries(meta, gathered, dec, prefix, batches, span, groups, reverse):
    count = gathered.shape[0]
    half = groups * LANES
    dec_span = power(dec, span)
    row = lax.broadcasted_iota(jnp.int32, (CHUNKS, LANES), 0)
    mine = meta[0][-1]
    out = []
    for batch in range(batches):

        def add(at, so_far, batch=batch):
            away = count - 2 - at
            if reverse:
                other = mine + 1 + away
                reaches = meta[batch][-3] > other * span
            else:
                other = mine - 1 - away
                reaches = meta[batch][-4] < (mine - away) * span
            other = jnp.clip(other, 0, count - 1)
            value = jnp.where(reaches, gathered[other, pl.ds(batch, 1), :], 0.0)
            moved = times(dec_span, so_far)
            return (moved[0] + value[:, :half], moved[1] + value[:, half:])

        zero = jnp.zeros((1, half), f32)
        enter = lax.fori_loop(0, count - 1, add, (zero, zero), unroll=count <= 8)
        rows = slice(batch * CHUNKS, (batch + 1) * CHUNKS)
        for q in range(groups):
            own = tuple(jnp.broadcast_to(part[:, lanes_of(q)], (CHUNKS, LANES)) for part in enter)
            end = (prefix[0, rows, lanes_of(q)], prefix[0, rows, lanes_of(q, half)])
            decay = (prefix[1, rows, lanes_of(q)], prefix[1, rows, lanes_of(q, half)])
            moved = times(decay, own)
            turn, first = (CHUNKS - 1, CHUNKS - 1) if reverse else (1, 0)
            out.append(
                tuple(
                    jnp.where(row == first, own[i], pltpu.roll(end[i] + moved[i], turn, 0))
                    for i in (0, 1)
                )
            )
    return out


def add_sums(target, batches, sums):
    for kind, per_batch in enumerate(sums):
        for batch in range(batches):
            target[kind * batches + batch : kind * batches + batch + 1, :] = jnp.sum(
                per_batch[batch], axis=0, keepdims=True
            )


def fold(value):
    return sum(value[i : i + CHUNKS] for i in range(CHUNKS, value.shape[0], CHUNKS)) + value[:CHUNKS]


def order_rows(batches, span, inverse, x, out):
    turn = reorder(span, inverse)
    for batch in range(batches):
        rows = slice(batch * span, (batch + 1) * span)
        out[rows, :] = dot(turn, x[rows, :]).astype(bf16)


def first_sums(batches, span, x, stats):
    width = x.shape[1]
    sums, squares = [], []
    for batch in range(batches):

        def body(start, carry, batch=batch):
            value = x[pl.ds(batch * span + start, ROWS), :].astype(f32)
            return carry[0] + fold(value), carry[1] + fold(value * value)

        zero = jnp.zeros((CHUNKS, width), f32)
        one, two = row_loop(span, body, (zero, zero))
        sums.append(one)
        squares.append(two)
    add_sums(stats, batches, (sums, squares))


def enter_layer(
    cfg, place, stats, hidden, norms, disc, b_proj, u, drive, prefix, total, norm
):
    layer, reverse, batches, span, groups, tokens, count = cfg
    sums = sum(part[...] for part in stats)
    average = sums[:batches] / tokens
    spread = sums[batches:] / tokens - average * average
    scale = lax.rsqrt(spread + epsilon)
    norm[:batches, :] = average
    norm[batches:, :] = scale
    gain_now, shift_now = norms[layer : layer + 1, :], norms[layer + 2 : layer + 3, :]
    for batch in range(batches):

        def body(start, carry, batch=batch):
            rows = pl.ds(batch * span + start, ROWS)
            normed = (hidden[rows, :].astype(f32) - average[batch : batch + 1]) * scale[
                batch : batch + 1
            ]
            u[rows, :] = (normed * gain_now + shift_now).astype(bf16)
            return carry

        row_loop(span, body)
    drive[...] = dot(u[...], b_proj[layer])
    meta = place_documents(cfg, place)
    dec, inj = constants(disc, layer)
    local_ends(
        meta, drive, coef_tiles(inj, groups), dec, batches, span, groups, reverse, prefix, total
    )


def finish_states(cfg, meta, ends, prefix, disc, drive, states, states_low):
    layer, reverse, batches, span, groups, tokens, count = cfg
    half = groups * LANES
    padded = span + CHUNKS
    dec, inj = constants(disc, layer)
    init = chunk_carries(meta, ends, dec, prefix, batches, span, groups, reverse)
    for batch in range(batches):
        edge = batch * padded + (span if reverse else 0)
        for q in range(groups):
            states[edge : edge + CHUNKS, lanes_of(q)] = init[batch * groups + q][0]
            states[edge : edge + CHUNKS, lanes_of(q, half)] = init[batch * groups + q][1]

    def visit(more, batch, q, first, start, found, src):
        if q is not None:
            for part, off in ((0, 0), (1, half)):
                both = jnp.concatenate([found[0][part], found[1][part]], axis=0)
                at = batch * padded + (0 if reverse else CHUNKS)
                states[pl.ds(at + start, 2 * CHUNKS), lanes_of(q, off)] = both
                states_low[pl.ds(batch * span + start, 2 * CHUNKS), lanes_of(q, off)] = both.astype(
                    bf16
                )
        return more

    scan(
        meta, drive, coef_tiles(inj, groups), coef_tiles(dec, groups), batches, span, groups,
        reverse, reverse, init, 0, visit,
    )


def forward_finish(
    cfg, meta, ends, prefix, disc, drive, u, hidden, c_proj, norms, w_gate,
    states, states_low, act, sig, slope, result, wide, emit,
):
    layer, reverse, batches, span, groups, tokens, count = cfg
    finish_states(cfg, meta, ends, prefix, disc, drive, states, states_low)
    wide[...] = dot(states_low[...], c_proj[layer])
    skip = norms[layer + 4 : layer + 5, :]

    def body(start, carry):
        rows = pl.ds(start, ROWS)
        mixed = wide[rows, :] + skip * u[rows, :].astype(f32)
        square = mixed * mixed
        th = jnp.tanh(tanh_scale * (mixed + cubic_term * square * mixed))
        half_one = 0.5 * (1.0 + th)
        act[rows, :] = (mixed * half_one).astype(bf16)
        slope[rows, :] = half_one + 0.5 * mixed * (1.0 - th * th) * tanh_scale * (
            1.0 + 3.0 * cubic_term * square
        )
        return carry

    row_loop(batches * span, body)
    wide[...] = dot(act[...], w_gate[layer])
    sums, squares = [], []
    for batch in range(batches):

        def gate(start, carry, batch=batch):
            rows = pl.ds(batch * span + start, ROWS)
            sig_now = 0.5 + 0.5 * jnp.tanh(0.5 * wide[rows, :])
            sig[rows, :] = sig_now
            value = hidden[rows, :].astype(f32) + act[rows, :].astype(f32) * sig_now
            result[rows, :] = value.astype(result.dtype)
            if emit is None:
                return carry
            return carry[0] + fold(value), carry[1] + fold(value * value)

        zero = jnp.zeros((CHUNKS, wide.shape[1]), f32)
        one, two = row_loop(span, gate, (zero, zero))
        sums.append(one)
        squares.append(two)
    if emit is not None:
        add_sums(emit, batches, (sums, squares))


def backward_start(
    cfg, meta, grad_out, disc, u, c_proj, w_gate, states_low, act, sig, slope,
    grad_gate, grad_mixed, grad_low, source, prefix, total, grad_d, wide,
):
    layer, reverse, batches, span, groups, tokens, count = cfg

    def body(start, carry):
        rows = pl.ds(start, ROWS)
        sig_now = sig[rows, :]
        grad_gate[rows, :] = (
            grad_out[rows, :].astype(f32) * act[rows, :].astype(f32) * sig_now * (1.0 - sig_now)
        ).astype(bf16)
        return carry

    row_loop(batches * span, body)
    wide[...] = dot(grad_gate[...], w_gate[layer], (1, 1))

    def mixed(start, carry):
        rows = pl.ds(start, ROWS)
        value = (grad_out[rows, :].astype(f32) * sig[rows, :] + wide[rows, :]) * slope[rows, :]
        grad_mixed[rows, :] = value
        grad_low[rows, :] = value.astype(bf16)
        return carry + fold(value * u[rows, :].astype(f32))

    gd = row_loop(batches * span, mixed, jnp.zeros((CHUNKS, wide.shape[1]), f32))
    grad_d[...] = jnp.sum(gd, axis=0, keepdims=True)
    source[...] = dot(grad_low[...], c_proj[layer], (1, 1))
    local_ends(
        meta, source, None, conj(constants(disc, layer)[0]), batches, span, groups, not reverse,
        prefix, total,
    )


def middle_forward(
    cfg, place, ends, prefix, disc, drive, u, hidden, c_proj, norms, w_gate,
    states, states_low, act, sig, slope, result, stats, wide,
):
    meta = place_documents(cfg, place)
    forward_finish(
        cfg, meta, ends, prefix, disc, drive, u, hidden, c_proj, norms, w_gate,
        states, states_low, act, sig, slope, result, wide, stats,
    )


def turn_around(
    cfg, place, ends, prefix, disc, drive, u, hidden, c_proj, norms, w_gate, ordered_cot,
    result, states, states_low, act, grad_gate, grad_mixed, grad_low, source,
    back_prefix, total, grad_d, sig, slope, wide,
):
    layer, reverse, batches, span, groups, tokens, count = cfg
    meta = place_documents(cfg, place)
    forward_finish(
        cfg, meta, ends, prefix, disc, drive, u, hidden, c_proj, norms, w_gate,
        states, states_low, act, sig, slope, result, wide, None,
    )
    backward_start(
        cfg, meta, ordered_cot, disc, u, c_proj, w_gate, states_low, act, sig, slope,
        grad_gate, grad_mixed, grad_low, source, back_prefix, total, grad_d, wide,
    )


def backward_finish(
    cfg, place, ends, prefix, disc, source, drive, states, u, grad_mixed, grad_d, hidden, norm,
    norms, b_proj, grad_proj, grad_u, stats, small,
):
    layer, reverse, batches, span, groups, tokens, count = cfg
    half = groups * LANES
    padded = span + CHUNKS
    steps = span // CHUNKS
    meta = place_documents(cfg, place)
    dec, inj = constants(disc, layer)
    dec = conj(dec)
    init = chunk_carries(meta, ends, dec, prefix, batches, span, groups, not reverse)
    inj = coef_tiles(inj, groups)
    base = base_positions(meta, steps)
    zero = jnp.zeros((CHUNKS, LANES), f32)

    def visit(more, batch, q, first, start, found, src):
        if q is None:
            return more
        more = list(more)
        rows = pl.ds(batch * span + start, 2 * CHUNKS)
        drive_re, drive_im = drive[rows, lanes_of(q)], drive[rows, lanes_of(q, half)]
        before = pl.ds(batch * padded + start + (CHUNKS if reverse else 0), 2 * CHUNKS)
        prior_re, prior_im = states[before, lanes_of(q)], states[before, lanes_of(q, half)]
        dec_re, dec_im, inj_re, inj_im = more[q]
        out_re, out_im = [], []
        for j in (0, 1):
            part = slice(j * CHUNKS, (j + 1) * CHUNKS)
            adj_re, adj_im = found[j]
            keep = keep_of(meta, batch, base, first + j, reverse)
            kept_re, kept_im = keep * adj_re, keep * adj_im
            dec_re = dec_re + kept_re * prior_re[part] + kept_im * prior_im[part]
            dec_im = dec_im + kept_im * prior_re[part] - kept_re * prior_im[part]
            inj_re = inj_re + adj_re * drive_re[part] + adj_im * drive_im[part]
            inj_im = inj_im + adj_im * drive_re[part] - adj_re * drive_im[part]
            out_re.append(inj[q][0] * adj_re + inj[q][1] * adj_im)
            out_im.append(inj[q][0] * adj_im - inj[q][1] * adj_re)
        grad_proj[rows, lanes_of(q)] = jnp.concatenate(out_re, axis=0).astype(bf16)
        grad_proj[rows, lanes_of(q, half)] = jnp.concatenate(out_im, axis=0).astype(bf16)
        more[q] = (dec_re, dec_im, inj_re, inj_im)
        return tuple(more)

    _, sums = scan(
        meta, source, None, coef_tiles(dec, groups), batches, span, groups,
        not reverse, not reverse, init, ((zero,) * 4,) * groups, visit,
    )
    small[...] = jnp.zeros_like(small)
    for q in range(groups):
        for kind in range(4):
            small[kind : kind + 1, lanes_of(q)] = jnp.sum(sums[q][kind], axis=0, keepdims=True)
    small[4:5, :] = grad_d[...]
    grad_u[...] = dot(grad_proj[...], b_proj[layer], (1, 1))
    skip = norms[layer + 4 : layer + 5, :]
    plain, times_normed = [], []
    for batch in range(batches):
        average = norm[batch : batch + 1, :]
        scale = norm[batches + batch : batches + batch + 1, :]

        def body(start, carry, batch=batch, average=average, scale=scale):
            rows = pl.ds(batch * span + start, ROWS)
            value = grad_u[rows, :] + grad_mixed[rows, :] * skip
            grad_u[rows, :] = value
            normed = (hidden[rows, :].astype(f32) - average) * scale
            return carry[0] + fold(value), carry[1] + fold(value * normed)

        zero_sum = jnp.zeros((CHUNKS, grad_u.shape[1]), f32)
        one, two = row_loop(span, body, (zero_sum, zero_sum))
        plain.append(one)
        times_normed.append(two)
    add_sums(stats, batches, (plain, times_normed))


def backward_finish_last(cfg, *refs):
    ins, before, (grad_proj, grad_u, sums) = refs[:-4], refs[-4], refs[-3:]
    sums[...] = jnp.zeros_like(sums)
    sums[2 * CHUNKS :, :] = before[...]
    backward_finish(
        cfg, *ins, grad_proj, grad_u, sums.at[pl.ds(0, CHUNKS)], sums.at[pl.ds(CHUNKS, CHUNKS)]
    )


def norm_backward(cfg, stats, grad_out, grad_u, hidden, norm, norms, store, shared):
    layer, reverse, batches, span, groups, tokens, count = cfg
    sums = sum(part[...] for part in stats)
    shared[0:1, :] = jnp.sum(sums[batches:], axis=0, keepdims=True)
    shared[1:2, :] = jnp.sum(sums[:batches], axis=0, keepdims=True)
    gain_now = norms[layer : layer + 1, :]
    for batch in range(batches):
        average = norm[batch : batch + 1, :]
        scale = norm[batches + batch : batches + batch + 1, :]
        plain = gain_now * sums[batch : batch + 1] / tokens
        slanted = gain_now * sums[batches + batch : batches + batch + 1] / tokens

        def body(start, carry, batch=batch, average=average, scale=scale, plain=plain, slanted=slanted):
            rows = pl.ds(batch * span + start, ROWS)
            normed = (hidden[rows, :].astype(f32) - average) * scale
            value = grad_out[rows, :].astype(f32) + scale * (
                grad_u[rows, :] * gain_now - plain - normed * slanted
            )
            store(rows, value)
            return carry

        row_loop(span, body)


def between_layers(
    cfg, lower, place, stats, upper_out, upper_u, upper_hidden, upper_norm, norms,
    disc, u, c_proj, w_gate, states_low, act, sig, slope,
    grad_out, shared, grad_gate, grad_mixed, grad_low, source, prefix, total, grad_d, wide,
):
    def store(rows, value):
        grad_out[rows, :] = value

    norm_backward(cfg, stats, upper_out, upper_u, upper_hidden, upper_norm, norms, store, shared)
    meta = place_documents(lower, place)
    backward_start(
        lower, meta, grad_out, disc, u, c_proj, w_gate, states_low, act, sig, slope,
        grad_gate, grad_mixed, grad_low, source, prefix, total, grad_d, wide,
    )


def last_step(cfg, stats, grad_out, grad_u, hidden, norm, norms, target, shared, ordered):
    layer, reverse, batches, span, groups, tokens, count = cfg
    planes = target.shape[1] // LANES

    def store(rows, value):
        for plane in range(planes):
            ordered[plane, rows, :] = value[:, lanes_of(plane)]

    norm_backward(cfg, stats, grad_out, grad_u, hidden, norm, norms, store, shared)
    steps = span // CHUNKS
    for batch in range(batches):
        for chunk in range(CHUNKS):
            at = batch * span
            for plane in range(planes):
                target[at + chunk * steps : at + (chunk + 1) * steps, lanes_of(plane)] = ordered[
                    plane, pl.ds(at + chunk, steps, stride=CHUNKS), :
                ]


def half_weights(core, refs, own, sent):
    for target, half in ((own, core), (sent, 1 - core)):
        at = 0
        for left, right in refs:
            rows = left.shape[1] // 2
            cols = pl.ds(pl.multiple_of(half * rows, LANES), rows)
            target[at : at + rows, :] = dot(left[:, cols], right[...], (0, 0))
            at += rows


def all_weights(here, act, grad_gate, states_low, grad_low, grad_proj, u, own, sent):
    refs = ((act, grad_gate), (states_low, grad_low), (grad_proj, u))
    half_weights(lax.rem(here[0], 2), refs, own, sent)


def gate_weights(here, act, grad_gate, states_low, grad_low, own, sent):
    half_weights(lax.rem(here[0], 2), ((act, grad_gate), (states_low, grad_low)), own, sent)


def input_weights(here, grad_proj, u, own, sent):
    half_weights(lax.rem(here[0], 2), ((grad_proj, u),), own, sent)


def run(body, name, args, outs, scratch=(), scalars=1):
    vmem, smem = pl.BlockSpec(memory_space=pltpu.VMEM), pl.BlockSpec(memory_space=pltpu.SMEM)
    specs = tuple(
        jax.tree.map(lambda _, at=at: smem if at < scalars else vmem, arg)
        for at, arg in enumerate(args)
    )
    return pl.pallas_call(
        body,
        name=name,
        out_shape=tuple(jax.ShapeDtypeStruct(*out) for out in outs),
        in_specs=specs,
        out_specs=(vmem,) * len(outs),
        scratch_shapes=[pltpu.VMEM(*entry) for entry in scratch],
        compiler_params=pltpu.CompilerParams(vmem_limit_bytes=VMEM_LIMIT),
    )(*args)


def put_in_place(layer, here, halves, outs, before, pieces=1):
    width, states = outs[0][0][1], outs[1][0][1]
    rows_w, rows_c = width // 2, states // 2
    vmem, count = pl.BlockSpec(memory_space=pltpu.VMEM), len(halves)

    def half(step, here):
        core = lax.rem(here[0], 2)
        spots = [1 - core if other else core for other, _ in halves]
        return spots[0] if count == 1 else jnp.where(step == 0, *spots)

    blocks = (
        pl.BlockSpec((1, rows_w, width), lambda i, here: (layer, half(i, here), 0)),
        pl.BlockSpec((1, rows_c, width), lambda i, here: (layer, half(i, here), 0)),
        pl.BlockSpec((1, width, rows_c), lambda i, here: (layer, 0, half(i, here))),
    )

    def body(here, *refs):
        grad_w, grad_c, grad_b = refs[-3:]
        for now in range(count):

            @pl.when(pl.program_id(0) == now)
            def _(source=refs[now]):
                gates, inputs = (rows_w + rows_c) // pieces, rows_c // pieces
                columns = []
                for piece in range(pieces):
                    at, row = piece * (gates + inputs), piece * gates
                    turn = min(max(rows_w - row, 0), gates)
                    if turn:
                        grad_w[0, row : row + turn, :] = source[at : at + turn, :]
                    if turn < gates:
                        to = row + turn - rows_w
                        grad_c[0, to : to + gates - turn, :] = source[at + turn : at + gates, :]
                    columns.append(source[at + gates : at + gates + inputs, :])
                grad_b[0] = jnp.concatenate(columns, axis=0).T

    return pl.pallas_call(
        body,
        name="put_in_place",
        out_shape=tuple(jax.ShapeDtypeStruct(*out) for out in outs),
        grid_spec=pltpu.PrefetchScalarGridSpec(
            num_scalar_prefetch=1,
            grid=(count,),
            in_specs=[vmem] * count + [pl.BlockSpec(memory_space=pl.ANY)] * len(before),
            out_specs=blocks,
        ),
        input_output_aliases={1 + count + i: i for i in range(len(before))},
        compiler_params=pltpu.CompilerParams(vmem_limit_bytes=VMEM_LIMIT),
    )(here, *(rows for _, rows in halves), *before)


def axis_parts():
    count, depth = lax.axis_size("seq"), lax.axis_size("dp")
    return (("seq", 2, 1, count), ("seq", count // 2, 2, count), ("dp", depth, 1, depth))


def shifted(value, part, away):
    name, size, stride, count = part
    pairs = []
    for i in range(count):
        place = (i // stride) % size
        pairs.append((i, i + ((place + away) % size - place) * stride))
    return lax.ppermute(value, name, pairs)


def add_by_shifts(value, parts, *earlier):
    for number, part in enumerate(parts):
        if number:
            value = sum(terms[1:], terms[0])
        if number == len(parts) - 1:
            value, *earlier = lax.optimization_barrier((value, *earlier))
        terms = [value] + [shifted(value, part, away) for away in range(1, part[1])]
    return terms, *earlier


def bits_of(size, stride=1):
    bits = []
    while size > 1:
        bits.append(stride)
        size, stride = size // 2, stride * 2
    return bits


def plane_bits():
    chip_bits = bits_of(lax.axis_size("seq") // 2, 2)
    middle = (len(chip_bits) + 1) // 2
    inner, outer = chip_bits[:middle], chip_bits[middle:]
    return list(zip(inner + outer, outer + inner))


def swap(value, axis, bit):
    return lax.ppermute(value, axis, [(i, i ^ bit) for i in range(lax.axis_size(axis))])


def bit_at(here, axis, bit):
    return lax.rem(lax.div(here[0 if axis == "seq" else 1], bit), 2)


def rows_at(half, rows):
    return pl.ds(pl.multiple_of(half * rows, CHUNKS), rows)


def fold_cores(bits, here, *refs):
    terms, targets = refs[:-4], refs[-4:]
    rows, cols = targets[0].shape
    for side in (0, 1):
        kept, sent = targets[2 * side : 2 * side + 2]
        where = slice(side * cols, (side + 1) * cols)
        bit = bit_at(here, "seq", bits[side])
        for half in (0, 1):

            @pl.when(bit == half)
            def _(half=half, kept=kept, sent=sent, where=where):
                start = 0
                for own, found in zip(terms[0::2], terms[1::2]):
                    for part, target in ((half, kept), (1 - half, sent)):
                        low = max(start, part * rows)
                        high = min(start + own.shape[0], (part + 1) * rows)
                        if low < high:
                            source = slice(low - start, high - start)
                            target[low - part * rows : high - part * rows, :] = (
                                own[source, where] + found[source, where]
                            )
                    start += own.shape[0]


def fold_sides(bits, here, *refs):
    targets, blocks = refs[-4:], refs[:-4]
    for side in (0, 1):
        kept, sent = targets[2 * side : 2 * side + 2]
        half, start = bit_at(here, "seq", bits[side]), 0
        for at in range(0, len(blocks), 4):
            own, found = blocks[at + 2 * side : at + 2 * side + 2]
            rows = own.shape[0] // 2
            to = slice(start, start + rows)
            kept[to, :] = own[rows_at(half, rows), :] + found[rows_at(half, rows), :]
            sent[to, :] = own[rows_at(1 - half, rows), :] + found[rows_at(1 - half, rows), :]
            start += rows


def fold_join(bit, here, left, found_left, right, found_right, kept, sent):
    rows, cols = kept.shape[0], left.shape[1]
    half = bit_at(here, "dp", bit)
    for side, (own, found) in enumerate(((left, found_left), (right, found_right))):
        where = slice(side * cols, (side + 1) * cols)
        kept[:, where] = own[rows_at(half, rows), :] + found[rows_at(half, rows), :]
        sent[:, where] = own[rows_at(1 - half, rows), :] + found[rows_at(1 - half, rows), :]


def fold_depth(bit, here, own, found, kept, sent):
    half, rows = bit_at(here, "dp", bit), kept.shape[0]
    kept[...] = own[rows_at(half, rows), :] + found[rows_at(half, rows), :]
    sent[...] = own[rows_at(1 - half, rows), :] + found[rows_at(1 - half, rows), :]


def add_two(own, found, out):
    out[...] = own[...] + found[...]


def unfold(bit, here, own, found, out):
    half, rows = bit_at(here, "dp", bit), own.shape[0]
    out[rows_at(half, rows), :] = own[...]
    out[rows_at(1 - half, rows), :] = found[...]


def unfold_split(bit, here, own, found, left, right):
    half, rows, cols = bit_at(here, "dp", bit), own.shape[0], left.shape[1]
    for side, out in enumerate((left, right)):
        where = slice(side * cols, (side + 1) * cols)
        out[rows_at(half, rows), :] = own[:, where]
        out[rows_at(1 - half, rows), :] = found[:, where]


def unfold_sides(bits, joined, here, *refs):
    for side in (0, 1):
        own, found = refs[2 * side : 2 * side + 2]
        half, (rows, cols) = bit_at(here, "seq", bits[side]), own.shape
        out = refs[4] if joined else refs[4 + side]
        where = slice(side * cols, (side + 1) * cols) if joined else slice(0, cols)
        out[rows_at(half, rows), where] = own[...]
        out[rows_at(1 - half, rows), where] = found[...]


def link_call(body, here, args, shapes):
    name = body.func.__name__
    return run(body, name, (here, *args), tuple((shape, f32) for shape in shapes))


class LinkSum:
    def __init__(self, here, terms):
        self.here, self.plane = here, plane_bits()
        self.depth = bits_of(lax.axis_size("dp"))
        rows = sum(term.shape[0] for term in terms[::2])
        self.shape = (rows // 2, terms[0].shape[1] // 2)
        self.parts = link_call(
            functools.partial(fold_cores, self.plane[0]), here, terms, (self.shape,) * 4
        )

    def swap_plane(self, stage):
        (left, right), pieces = self.plane[stage], self.parts
        self.parts = (
            pieces[0], swap(pieces[1], "seq", left), pieces[2], swap(pieces[3], "seq", right)
        )

    def down_plane(self, stage, *others):
        parts, rows, cols = list(self.parts), *self.shape
        for other in others:
            parts += other.parts
            rows += other.shape[0]
        self.shape = (rows // 2, cols)
        body = functools.partial(fold_sides, self.plane[stage])
        self.parts = link_call(body, self.here, parts, (self.shape,) * 4)

    def down_join(self):
        rows, cols = self.shape
        self.shape = (rows // 2, 2 * cols)
        body = functools.partial(fold_join, self.depth[0])
        self.parts = link_call(body, self.here, self.parts, (self.shape,) * 2)

    def swap_depth(self, stage):
        self.parts = (self.parts[0], swap(self.parts[1], "dp", self.depth[stage]))

    def down_depth(self, stage):
        rows, cols = self.shape
        self.shape = (rows // 2, cols)
        body = functools.partial(fold_depth, self.depth[stage])
        self.parts = link_call(body, self.here, self.parts, (self.shape,) * 2)

    def middle(self):
        (value,) = run(add_two, "add_two", self.parts, ((self.shape, f32),), scalars=0)
        self.parts = (value, value)

    def up_depth(self, stage):
        rows, cols = self.shape
        self.shape = (rows * 2, cols)
        body = functools.partial(unfold, self.depth[stage])
        (value,) = link_call(body, self.here, self.parts, (self.shape,))
        self.parts = (value, value)

    def up_split(self):
        rows, cols = self.shape
        self.shape = (rows * 2, cols // 2)
        body = functools.partial(unfold_split, self.depth[0])
        left, right = link_call(body, self.here, self.parts, (self.shape,) * 2)
        self.parts = (left, left, right, right)

    def up_plane(self, stage):
        rows, cols = self.shape
        if stage:
            self.shape = (rows * 2, cols)
            body = functools.partial(unfold_sides, self.plane[stage], False)
            left, right = link_call(body, self.here, self.parts, (self.shape,) * 2)
            self.parts = (left, left, right, right)
        else:
            self.shape = (rows * 2, cols * 2)
            body = functools.partial(unfold_sides, self.plane[stage], True)
            self.parts = link_call(body, self.here, self.parts, (self.shape,))

    def after(self, *values):
        self.parts, values = lax.optimization_barrier((self.parts, values))
        return values

    def to_depth(self):
        for stage in range(2, len(self.plane)):
            self.swap_plane(stage - 1)
            self.down_plane(stage)
        self.swap_plane(len(self.plane) - 1)

    def scatter_depth(self):
        for stage in range(len(self.depth) - 1):
            if stage:
                self.down_depth(stage)
            self.swap_depth(stage)

    def swap_whole(self):
        self.parts = (self.parts[0], swap(self.parts[0], "dp", self.depth[-1]))

    def gather_depth(self):
        for stage in range(len(self.depth) - 2, 0, -1):
            self.swap_depth(stage)
            self.up_depth(stage)
        self.swap_depth(0)


def wait_for(*things):
    sums = [thing for thing in things if isinstance(thing, LinkSum)]
    values = [thing for thing in things if not isinstance(thing, LinkSum)]
    parts, values = lax.optimization_barrier(([entry.parts for entry in sums], values))
    for entry, part in zip(sums, parts):
        entry.parts = part
    return values


def discretize(lam_re, lam_im, log_step):
    step_size = jnp.exp(log_step)
    decay_abs = jnp.exp(lam_re * step_size)
    rotation = lam_im * step_size
    dec_re = decay_abs * jnp.cos(rotation)
    dec_im = decay_abs * jnp.sin(rotation)
    denom_sq = lam_re * lam_re + lam_im * lam_im
    inj_re = ((dec_re - 1.0) * lam_re + dec_im * lam_im) / denom_sq
    inj_im = (dec_im * lam_re - (dec_re - 1.0) * lam_im) / denom_sq
    return (dec_re, dec_im, inj_re, inj_im)


def per_device(
    block_in, cotangent, doc_lengths, norm_gain, norm_shift, log_step, lam_re, lam_im,
    b_proj, c_proj, d_skip, w_gate,
):
    batches, seqs, span, width = block_in.shape
    assert seqs == 1 and span % (4 * CHUNKS) == 0 and span & (span - 1) == 0
    half = lam_re.shape[1]
    groups = half // LANES
    rows = batches * span
    count = lax.axis_size("seq")
    tokens = float(seqs * lax.axis_size("dp") * span * count)
    here = jnp.stack([lax.axis_index("seq"), lax.axis_index("dp")]).astype(jnp.int32)
    place = jnp.concatenate([here] + [doc_lengths[batch, 0] for batch in range(batches)])
    place, block_in = lax.optimization_barrier((place, block_in))
    here = place
    disc = discretize(lam_re, lam_im, log_step)

    x = block_in.reshape(rows, width)
    cot = cotangent.reshape(rows, width)
    lower = (0, False, batches, span, groups, tokens, count)
    upper = (1, True, batches, span, groups, tokens, count)
    part = functools.partial

    flat, low = ((rows, width), f32), ((rows, width), bf16)
    wide, wide_low = ((rows, 2 * half), f32), ((rows, 2 * half), bf16)
    padded = ((batches * (span + CHUNKS), 2 * half), f32)
    sums = ((2 * batches, width), f32)
    prefix = ((2, batches * CHUNKS, 2 * half), f32)
    total = ((batches, 2 * half), f32)
    line, shared = ((1, width), f32), ((2, width), f32)
    small = ((8, width), f32)

    def gather_row(value):
        return lax.all_gather(value, "seq")

    (stats,) = run(part(first_sums, batches, span), "first_sums", (x,), (sums,), scalars=0)

    def order(value, inverse):
        body = part(order_rows, batches, span, inverse)
        return run(body, "order_rows", (value,), (low,), scalars=0)[0]

    norms = jnp.concatenate([norm_gain, norm_shift, d_skip], axis=0)

    def forward(cfg, hidden, stats):
        return run(
            part(enter_layer, cfg),
            "enter_layer",
            (place, stats, hidden, norms, disc, b_proj),
            (low, wide, prefix, total, sums),
        )

    links, plane, depth = axis_parts()
    stats, ordered = lax.optimization_barrier(
        (add_by_shifts(stats, (links, plane, depth))[0], order(x, False))
    )
    u0, drive0, prefix0, total0, norm0 = forward(lower, ordered, stats)
    states0, states_low0, act0, sig0, slope0, hidden1, stats = run(
        part(middle_forward, lower),
        "middle_forward",
        (place, gather_row(total0), prefix0, disc, drive0, u0, ordered, c_proj, norms, w_gate),
        (padded, wide_low, low, flat, flat, flat, sums),
        (flat,),
    )
    cot, stats = lax.optimization_barrier((cot, stats))
    stats, ordered_cot = lax.optimization_barrier(
        (add_by_shifts(stats, (links, plane, depth))[0], order(cot, False))
    )
    u1, drive1, prefix1, total1, norm1 = forward(upper, hidden1, stats)
    (
        result1, states1, states_low1, act1, grad_gate1, grad_mixed1, grad_low1,
        source1, prefix1, total1, grad_d1,
    ) = run(
        part(turn_around, upper),
        "turn_around",
        (
            place, gather_row(total1), prefix1, disc, drive1, u1, hidden1, c_proj, norms, w_gate,
            ordered_cot,
        ),
        (low, padded, wide_low, low, low, flat, low, wide, prefix, total, line),
        (flat, flat, flat),
    )

    def halves(length):
        return (((length // 2, width), f32),) * 2

    grad_proj1, grad_u1, stats, small1 = run(
        part(backward_finish, upper),
        "backward_finish",
        (
            place, gather_row(total1), prefix1, disc, source1, drive1, states1, u1, grad_mixed1,
            grad_d1, hidden1, norm1, norms, b_proj,
        ),
        (wide_low, flat, sums, small),
    )
    sizes = (width + 2 * half, 2 * half)
    own1, sent1 = run(
        all_weights,
        "all_weights",
        (here, act1, grad_gate1, states_low1, grad_low1, grad_proj1, u1),
        halves(sum(sizes)),
    )
    stats = stats + swap(stats, "seq", 1)
    stats, sent1 = lax.optimization_barrier((stats, sent1))
    upper_sum = LinkSum(here, (own1, swap(sent1, "seq", 1)))
    stats, upper_sum.parts = add_by_shifts(stats, (plane, depth), upper_sum.parts)
    upper_sum.swap_plane(0)
    (
        grad_out0, shared1, grad_gate0, grad_mixed0, grad_low0, source0, prefix0, total0, grad_d0,
    ) = run(
        part(between_layers, upper, lower),
        "between_layers",
        (
            place, stats, ordered_cot, grad_u1, hidden1, norm1, norms,
            disc, u0, c_proj, w_gate, states_low0, act0, sig0, slope0,
        ),
        (flat, shared, low, flat, low, wide, prefix, total, line),
        (flat,),
    )
    (total0,) = upper_sum.after(total0)
    upper_sum.down_plane(1)
    (total0,) = upper_sum.after(total0)
    upper_sum.to_depth()
    ends, grad_gate0 = wait_for(upper_sum, gather_row(total0), grad_gate0)
    upper_sum.down_join()
    ends, grad_gate0 = wait_for(upper_sum, ends, grad_gate0)
    upper_sum.scatter_depth()
    own_gates, sent_gates = run(
        gate_weights, "gate_weights", (here, act0, grad_gate0, states_low0, grad_low0),
        halves(sizes[0]),
    )
    own_gates, ends = lax.optimization_barrier((own_gates, ends))
    grad_proj0, grad_u0, last_sums = run(
        part(backward_finish_last, lower),
        "backward_finish",
        (
            place, ends, prefix0, disc, source0, drive0, states0, u0, grad_mixed0, grad_d0,
            ordered, norm0, norms, b_proj, small1,
        ),
        (wide_low, flat, ((3 * CHUNKS, width), f32)),
    )
    lower_sum = LinkSum(here, (own_gates, swap(sent_gates, "seq", 1)))
    (grad_proj0,) = wait_for(upper_sum, lower_sum, grad_proj0)
    own_inputs, sent_inputs = run(
        input_weights, "input_weights", (here, grad_proj0, u0), halves(sizes[1])
    )
    inputs_sum = LinkSum(here, (own_inputs, swap(sent_inputs, "seq", 1)))
    upper_sum.middle()
    upper_sum.swap_whole()
    lower_sum.swap_plane(0)
    inputs_sum.swap_plane(0)
    wait_for(upper_sum, lower_sum, inputs_sum)

    lower_sum.down_plane(1, inputs_sum)
    upper_sum.middle()
    upper_sum.gather_depth()
    lower_sum.to_depth()
    wait_for(upper_sum, lower_sum)

    lower_sum.down_join()
    upper_sum.up_split()
    lower_sum.scatter_depth()
    upper_sum.swap_plane(len(upper_sum.plane) - 1)
    wait_for(upper_sum, lower_sum)

    lower_sum.middle()
    lower_sum.swap_whole()
    for stage in range(len(upper_sum.plane) - 1, 0, -1):
        upper_sum.up_plane(stage)
        upper_sum.swap_plane(stage - 1)
    (last_sums,) = wait_for(upper_sum, lower_sum, last_sums)

    lower_sum.middle()
    (last_sums,) = lower_sum.after(last_sums)
    lower_sum.gather_depth()
    last_sums = last_sums + swap(last_sums, "seq", 1)
    last_terms = [last_sums] + [shifted(last_sums, plane, away) for away in range(1, plane[1])]
    last_terms = wait_for(lower_sum, *last_terms)

    lower_sum.up_split()
    wait_for(upper_sum, lower_sum)
    lower_sum.swap_plane(len(lower_sum.plane) - 1)
    upper_sum.up_plane(0)
    own1, result1 = lax.optimization_barrier((upper_sum.parts[0], result1))
    other1 = swap(own1, "seq", 1)
    block_out = order(result1, True)
    final = (((2, width, width), f32), ((2, 2 * half, width), f32), ((2, width, 2 * half), f32))
    placed = put_in_place(1, here, ((False, own1), (True, other1)), final, ())
    summed = sum(last_terms)
    for bit in bits_of(lax.axis_size("dp")):
        summed = summed + swap(summed, "dp", bit)
    summed, block_out = wait_for(lower_sum, summed, block_out)

    for stage in range(len(lower_sum.plane) - 1, 0, -1):
        lower_sum.up_plane(stage)
        if stage == 1:
            (summed,) = lower_sum.after(summed)
        lower_sum.swap_plane(stage - 1)
    grad_input, shared0 = run(
        part(last_step, lower),
        "last_step",
        ((summed[: 2 * batches],), grad_out0, grad_u0, ordered, norm0, norms),
        (flat, shared),
        (((width // LANES, rows, LANES), f32),),
        scalars=0,
    )
    small_sum = summed[CHUNKS:].reshape(2, CHUNKS, width)
    _, pullback = jax.vjp(discretize, lam_re, lam_im, log_step)
    grad_lr, grad_li, grad_ls = pullback(tuple(small_sum[:, kind, :half] for kind in range(4)))
    grad_input, grad_lr, grad_li, grad_ls, *placed = wait_for(
        lower_sum, grad_input, grad_lr, grad_li, grad_ls, *placed
    )

    lower_sum.up_plane(0)
    own0 = lower_sum.parts[0]
    other0 = swap(own0, "seq", 1)
    placed = put_in_place(0, here, ((False, own0),), final, placed, 4)
    grad_w, grad_c, grad_b = put_in_place(0, here, ((True, other0),), final, placed, 4)
    both = jnp.stack([shared0, shared1])
    shape = block_in.shape
    return (
        block_out.reshape(shape), grad_input.reshape(shape), both[:, 0], both[:, 1],
        grad_ls, grad_lr, grad_li, grad_b, grad_c, small_sum[:, 4], grad_w,
    )


def solution(mesh):
    split = P(None, "dp", "seq", None)
    return jax.shard_map(
        per_device,
        mesh=mesh,
        in_specs=(split, split, P(None, "dp", None)) + (P(),) * 9,
        out_specs=(split, split) + (P(),) * 9,
        check_vma=False,
    )
```

```python
import functools

import jax
import jax.numpy as jnp
from jax import lax
from jax.experimental import pallas as pl
from jax.experimental.pallas import tpu as pltpu
from jax.sharding import PartitionSpec as P

f32, bf16 = jnp.float32, jnp.bfloat16
epsilon = 1e-05
tanh_scale = 0.7978845608028654
cubic_term = 0.044715
LANES = 128
CHUNKS = 8
ROWS = 32
VMEM_LIMIT = 16 * 1024 * 1024


def dot(left, right, contract=(1, 0)):
    return lax.dot_general(
        left, right, (((contract[0],), (contract[1],)), ((), ())), preferred_element_type=f32
    )


def reorder(span, inverse):
    shape = (span, span)
    kept, moved = (1, 0) if inverse else (0, 1)
    row = lax.broadcasted_iota(jnp.int32, shape, kept)
    position = lax.broadcasted_iota(jnp.int32, shape, moved)
    source = (row & (CHUNKS - 1)) * (span // CHUNKS) + (row >> 3)
    return jnp.where(position == source, 1.0, 0.0).astype(bf16)


def row_loop(count, body, init=0, step=ROWS):
    def one(index, carry):
        return body(pl.multiple_of(index * step, step), carry)

    return lax.fori_loop(0, count // step, one, init, unroll=2)


def documents(here, batches, span, count):
    mine = here[0]
    first = mine * span
    out = []
    for batch in range(batches):
        begins, ends, so_far = [], [], 0
        docs = (here.shape[0] - 2) // batches
        for doc in range(docs):
            begins.append(so_far)
            so_far = so_far + here[2 + batch * docs + doc]
            ends.append(so_far)
        before, after = 0, 2 * count * span
        for begin, end in zip(begins, ends):
            before = jnp.maximum(before, jnp.where(begin < first, begin, 0))
            after = jnp.minimum(after, jnp.where(end > first + span, end, 2 * count * span))
        after = jnp.where(mine == count - 1, 0, after)
        out.append(begins + ends + [before, after, first, mine])
    return out


def place_documents(cfg, place):
    layer, reverse, batches, span, groups, tokens, count = cfg
    return documents(place, batches, span, count)


def keep_of(meta, batch, base, step, backward):
    docs = (len(meta[batch]) - 4) // 2
    off = docs if backward else 0
    late = 1 if backward else 0
    stop = base == meta[batch][off] - step - late
    for doc in range(1, docs):
        stop = jnp.logical_or(stop, base == meta[batch][off + doc] - step - late)
    return jnp.where(stop, 0.0, 1.0)


def base_positions(meta, steps):
    return meta[0][-2] + lax.broadcasted_iota(jnp.int32, (CHUNKS, LANES), 0) * steps


def lanes_of(index, half=0):
    return slice(half + index * LANES, half + (index + 1) * LANES)


def coef_tiles(value, groups):
    return [
        tuple(jnp.broadcast_to(part[:, lanes_of(q)], (CHUNKS, LANES)) for part in value)
        for q in range(groups)
    ]


def constants(disc, layer):
    dec_re, dec_im, inj_re, inj_im = (part[layer : layer + 1, :] for part in disc)
    return (dec_re, dec_im), (inj_re, inj_im)


def times(a, b):
    return (a[0] * b[0] - a[1] * b[1], a[0] * b[1] + a[1] * b[0])


def power(value, exponent):
    for _ in range(exponent.bit_length() - 1):
        value = times(value, value)
    return value


def conj(value):
    return (value[0], -value[1])


def scan(meta, source, inject, dec, batches, span, groups, reverse, masks_reverse, init, extra, visit):
    steps = span // CHUNKS
    half = groups * LANES
    base = base_positions(meta, steps)

    def pair(index, carry):
        states, more = carry
        states = list(states)
        first = steps - 2 - 2 * index if reverse else 2 * index
        start = pl.multiple_of(first * CHUNKS, 2 * CHUNKS)
        order = (1, 0) if reverse else (0, 1)
        for batch in range(batches):
            keeps = [keep_of(meta, batch, base, first + j, masks_reverse) for j in (0, 1)]
            for q in range(groups):
                rows = pl.ds(batch * span + start, 2 * CHUNKS)
                src_re = source[rows, lanes_of(q)]
                src_im = source[rows, lanes_of(q, half)]
                state = states[batch * groups + q]
                found = [None, None]
                for j in order:
                    part = (
                        src_re[j * CHUNKS : (j + 1) * CHUNKS],
                        src_im[j * CHUNKS : (j + 1) * CHUNKS],
                    )
                    push = times(inject[q], part) if inject is not None else part
                    held = times((keeps[j] * dec[q][0], keeps[j] * dec[q][1]), state)
                    state = (held[0] + push[0], held[1] + push[1])
                    found[j] = state
                states[batch * groups + q] = state
                more = visit(more, batch, q, first, start, found, (src_re, src_im))
            more = visit(more, batch, None, first, start, keeps, None)
        return tuple(states), more

    return lax.fori_loop(0, steps // 2, pair, (tuple(init), extra), unroll=4)


def zero_states(batches, groups):
    zero = jnp.zeros((CHUNKS, LANES), f32)
    return [(zero, zero)] * (batches * groups)


def local_ends(meta, source, inject, dec, batches, span, groups, reverse, prefix, total):
    ones = tuple(jnp.ones((CHUNKS, LANES), f32) for _ in range(batches))

    def visit(more, batch, q, first, start, found, src):
        if q is not None:
            return more
        return tuple(
            value * found[0] * found[1] if at == batch else value for at, value in enumerate(more)
        )

    dec_chunk = coef_tiles(power(dec, span // CHUNKS), groups)
    ends, kept = scan(
        meta, source, inject, coef_tiles(dec, groups), batches, span, groups, reverse, reverse,
        zero_states(batches, groups), ones, visit,
    )
    half = groups * LANES
    row = lax.broadcasted_iota(jnp.int32, (CHUNKS, LANES), 0)
    for batch in range(batches):
        for q in range(groups):
            end = ends[batch * groups + q]
            decay = (kept[batch] * dec_chunk[q][0], kept[batch] * dec_chunk[q][1])
            for shift in (1, 2, 4):
                turn = CHUNKS - shift if reverse else shift
                valid = row < CHUNKS - shift if reverse else row >= shift
                before = [pltpu.roll(value, turn, 0) for value in (*end, *decay)]
                from_before = times(decay, (before[0], before[1]))
                end = (
                    end[0] + jnp.where(valid, from_before[0], 0.0),
                    end[1] + jnp.where(valid, from_before[1], 0.0),
                )
                longer = times(decay, (before[2], before[3]))
                decay = (
                    jnp.where(valid, longer[0], decay[0]),
                    jnp.where(valid, longer[1], decay[1]),
                )
            rows = slice(batch * CHUNKS, (batch + 1) * CHUNKS)
            prefix[0, rows, lanes_of(q)] = end[0]
            prefix[0, rows, lanes_of(q, half)] = end[1]
            prefix[1, rows, lanes_of(q)] = decay[0]
            prefix[1, rows, lanes_of(q, half)] = decay[1]
            last = 0 if reverse else CHUNKS - 1
            total[batch : batch + 1, lanes_of(q)] = end[0][last : last + 1]
            total[batch : batch + 1, lanes_of(q, half)] = end[1][last : last + 1]


def chunk_carries(meta, gathered, dec, prefix, batches, span, groups, reverse):
    half = groups * LANES
    dec_span = power(dec, span)
    row = lax.broadcasted_iota(jnp.int32, (CHUNKS, LANES), 0)
    mine = meta[0][-1]
    core = lax.rem(mine, 2)
    out = []
    for batch in range(batches):
        enter = (jnp.zeros((1, half), f32), jnp.zeros((1, half), f32))
        for away in range(len(gathered) - 1, -1, -1):
            for kind in (1, 0) if reverse else (0, 1):
                if away == 0 and kind == (0 if reverse else 1):
                    continue
                if reverse:
                    other = mine - core + 2 * away + kind
                    reaches = meta[batch][-3] > other * span
                else:
                    other = mine - core - 2 * away + kind
                    reaches = meta[batch][-4] < (other + 1) * span
                same = gathered[away][batch : batch + 1, :]
                unlike = gathered[away][batches + batch : batches + batch + 1, :]
                value = jnp.where(reaches, jnp.where(core == kind, same, unlike), 0.0)
                moved = times(dec_span, enter)
                after = (moved[0] + value[:, :half], moved[1] + value[:, half:])
                if away == 0:
                    after = tuple(jnp.where(core == kind, old, new) for old, new in zip(enter, after))
                enter = after
        rows = slice(batch * CHUNKS, (batch + 1) * CHUNKS)
        for q in range(groups):
            own = tuple(jnp.broadcast_to(part[:, lanes_of(q)], (CHUNKS, LANES)) for part in enter)
            end = (prefix[0, rows, lanes_of(q)], prefix[0, rows, lanes_of(q, half)])
            decay = (prefix[1, rows, lanes_of(q)], prefix[1, rows, lanes_of(q, half)])
            moved = times(decay, own)
            turn, first = (CHUNKS - 1, CHUNKS - 1) if reverse else (1, 0)
            out.append(
                tuple(
                    jnp.where(row == first, own[i], pltpu.roll(end[i] + moved[i], turn, 0))
                    for i in (0, 1)
                )
            )
    return out


def add_sums(target, batches, sums):
    for kind, per_batch in enumerate(sums):
        for batch in range(batches):
            target[kind * batches + batch : kind * batches + batch + 1, :] = jnp.sum(
                per_batch[batch], axis=0, keepdims=True
            )


def fold(value):
    return sum(value[i : i + CHUNKS] for i in range(CHUNKS, value.shape[0], CHUNKS)) + value[:CHUNKS]


def order_rows(batches, span, inverse, x, out):
    turn = reorder(span, inverse)
    for batch in range(batches):
        rows = slice(batch * span, (batch + 1) * span)
        out[rows, :] = dot(turn, x[rows, :]).astype(bf16)


def first_sums(batches, span, x, stats):
    width = x.shape[1]
    sums, squares = [], []
    for batch in range(batches):

        def body(start, carry, batch=batch):
            value = x[pl.ds(batch * span + start, ROWS), :].astype(f32)
            return carry[0] + fold(value), carry[1] + fold(value * value)

        zero = jnp.zeros((CHUNKS, width), f32)
        one, two = row_loop(span, body, (zero, zero))
        sums.append(one)
        squares.append(two)
    add_sums(stats, batches, (sums, squares))


def enter_layer(
    cfg, place, stats, hidden, norms, disc, b_proj, u, drive, prefix, total, norm
):
    layer, reverse, batches, span, groups, tokens, count = cfg
    sums = sum(part[...] for part in stats)
    average = sums[:batches] / tokens
    spread = sums[batches:] / tokens - average * average
    scale = lax.rsqrt(spread + epsilon)
    norm[:batches, :] = average
    norm[batches:, :] = scale
    gain_now, shift_now = norms[layer : layer + 1, :], norms[layer + 2 : layer + 3, :]
    for batch in range(batches):

        def body(start, carry, batch=batch):
            rows = pl.ds(batch * span + start, ROWS)
            normed = (hidden[rows, :].astype(f32) - average[batch : batch + 1]) * scale[
                batch : batch + 1
            ]
            u[rows, :] = (normed * gain_now + shift_now).astype(bf16)
            return carry

        row_loop(span, body)
    drive[...] = dot(u[...], b_proj[layer])
    meta = place_documents(cfg, place)
    dec, inj = constants(disc, layer)
    local_ends(
        meta, drive, coef_tiles(inj, groups), dec, batches, span, groups, reverse, prefix, total
    )


def finish_states(cfg, meta, ends, prefix, disc, drive, states, states_low):
    layer, reverse, batches, span, groups, tokens, count = cfg
    half = groups * LANES
    padded = span + CHUNKS
    dec, inj = constants(disc, layer)
    init = chunk_carries(meta, ends, dec, prefix, batches, span, groups, reverse)
    for batch in range(batches):
        edge = batch * padded + (span if reverse else 0)
        for q in range(groups):
            states[edge : edge + CHUNKS, lanes_of(q)] = init[batch * groups + q][0]
            states[edge : edge + CHUNKS, lanes_of(q, half)] = init[batch * groups + q][1]

    def visit(more, batch, q, first, start, found, src):
        if q is not None:
            for part, off in ((0, 0), (1, half)):
                both = jnp.concatenate([found[0][part], found[1][part]], axis=0)
                at = batch * padded + (0 if reverse else CHUNKS)
                states[pl.ds(at + start, 2 * CHUNKS), lanes_of(q, off)] = both
                states_low[pl.ds(batch * span + start, 2 * CHUNKS), lanes_of(q, off)] = both.astype(
                    bf16
                )
        return more

    scan(
        meta, drive, coef_tiles(inj, groups), coef_tiles(dec, groups), batches, span, groups,
        reverse, reverse, init, 0, visit,
    )


def forward_finish(
    cfg, meta, ends, prefix, disc, drive, u, hidden, c_proj, norms, w_gate,
    states, states_low, act, sig, slope, result, wide, emit,
):
    layer, reverse, batches, span, groups, tokens, count = cfg
    finish_states(cfg, meta, ends, prefix, disc, drive, states, states_low)
    wide[...] = dot(states_low[...], c_proj[layer])
    skip = norms[layer + 4 : layer + 5, :]

    def body(start, carry):
        rows = pl.ds(start, ROWS)
        mixed = wide[rows, :] + skip * u[rows, :].astype(f32)
        square = mixed * mixed
        th = jnp.tanh(tanh_scale * (mixed + cubic_term * square * mixed))
        half_one = 0.5 * (1.0 + th)
        act[rows, :] = (mixed * half_one).astype(bf16)
        slope[rows, :] = half_one + 0.5 * mixed * (1.0 - th * th) * tanh_scale * (
            1.0 + 3.0 * cubic_term * square
        )
        return carry

    row_loop(batches * span, body)
    wide[...] = dot(act[...], w_gate[layer])
    sums, squares = [], []
    for batch in range(batches):

        def gate(start, carry, batch=batch):
            rows = pl.ds(batch * span + start, ROWS)
            sig_now = 0.5 + 0.5 * jnp.tanh(0.5 * wide[rows, :])
            sig[rows, :] = sig_now
            value = hidden[rows, :].astype(f32) + act[rows, :].astype(f32) * sig_now
            result[rows, :] = value.astype(result.dtype)
            if emit is None:
                return carry
            return carry[0] + fold(value), carry[1] + fold(value * value)

        zero = jnp.zeros((CHUNKS, wide.shape[1]), f32)
        one, two = row_loop(span, gate, (zero, zero))
        sums.append(one)
        squares.append(two)
    if emit is not None:
        add_sums(emit, batches, (sums, squares))


def backward_start(
    cfg, meta, grad_out, disc, u, c_proj, w_gate, states_low, act, sig, slope,
    grad_gate, grad_mixed, grad_low, source, prefix, total, grad_d, wide,
):
    layer, reverse, batches, span, groups, tokens, count = cfg

    def body(start, carry):
        rows = pl.ds(start, ROWS)
        sig_now = sig[rows, :]
        grad_gate[rows, :] = (
            grad_out[rows, :].astype(f32) * act[rows, :].astype(f32) * sig_now * (1.0 - sig_now)
        ).astype(bf16)
        return carry

    row_loop(batches * span, body)
    wide[...] = dot(grad_gate[...], w_gate[layer], (1, 1))

    def mixed(start, carry):
        rows = pl.ds(start, ROWS)
        value = (grad_out[rows, :].astype(f32) * sig[rows, :] + wide[rows, :]) * slope[rows, :]
        grad_mixed[rows, :] = value
        grad_low[rows, :] = value.astype(bf16)
        return carry + fold(value * u[rows, :].astype(f32))

    gd = row_loop(batches * span, mixed, jnp.zeros((CHUNKS, wide.shape[1]), f32))
    grad_d[...] = jnp.sum(gd, axis=0, keepdims=True)
    source[...] = dot(grad_low[...], c_proj[layer], (1, 1))
    local_ends(
        meta, source, None, conj(constants(disc, layer)[0]), batches, span, groups, not reverse,
        prefix, total,
    )


def middle_forward(
    cfg, place, ends, prefix, disc, drive, u, hidden, c_proj, norms, w_gate,
    states, states_low, act, sig, slope, result, stats, wide,
):
    meta = place_documents(cfg, place)
    forward_finish(
        cfg, meta, ends, prefix, disc, drive, u, hidden, c_proj, norms, w_gate,
        states, states_low, act, sig, slope, result, wide, stats,
    )


def turn_around(
    cfg, place, ends, prefix, disc, drive, u, hidden, c_proj, norms, w_gate, ordered_cot,
    result, states, states_low, act, grad_gate, grad_mixed, grad_low, source,
    back_prefix, total, grad_d, sig, slope, wide,
):
    layer, reverse, batches, span, groups, tokens, count = cfg
    meta = place_documents(cfg, place)
    forward_finish(
        cfg, meta, ends, prefix, disc, drive, u, hidden, c_proj, norms, w_gate,
        states, states_low, act, sig, slope, result, wide, None,
    )
    backward_start(
        cfg, meta, ordered_cot, disc, u, c_proj, w_gate, states_low, act, sig, slope,
        grad_gate, grad_mixed, grad_low, source, back_prefix, total, grad_d, wide,
    )


def backward_finish(
    cfg, place, ends, prefix, disc, source, drive, states, u, grad_mixed, grad_d, hidden, norm,
    norms, b_proj, grad_proj, grad_u, stats, small,
):
    layer, reverse, batches, span, groups, tokens, count = cfg
    half = groups * LANES
    padded = span + CHUNKS
    steps = span // CHUNKS
    meta = place_documents(cfg, place)
    dec, inj = constants(disc, layer)
    dec = conj(dec)
    init = chunk_carries(meta, ends, dec, prefix, batches, span, groups, not reverse)
    inj = coef_tiles(inj, groups)
    base = base_positions(meta, steps)
    zero = jnp.zeros((CHUNKS, LANES), f32)

    def visit(more, batch, q, first, start, found, src):
        if q is None:
            return more
        more = list(more)
        rows = pl.ds(batch * span + start, 2 * CHUNKS)
        drive_re, drive_im = drive[rows, lanes_of(q)], drive[rows, lanes_of(q, half)]
        before = pl.ds(batch * padded + start + (CHUNKS if reverse else 0), 2 * CHUNKS)
        prior_re, prior_im = states[before, lanes_of(q)], states[before, lanes_of(q, half)]
        dec_re, dec_im, inj_re, inj_im = more[q]
        out_re, out_im = [], []
        for j in (0, 1):
            part = slice(j * CHUNKS, (j + 1) * CHUNKS)
            adj_re, adj_im = found[j]
            keep = keep_of(meta, batch, base, first + j, reverse)
            kept_re, kept_im = keep * adj_re, keep * adj_im
            dec_re = dec_re + kept_re * prior_re[part] + kept_im * prior_im[part]
            dec_im = dec_im + kept_im * prior_re[part] - kept_re * prior_im[part]
            inj_re = inj_re + adj_re * drive_re[part] + adj_im * drive_im[part]
            inj_im = inj_im + adj_im * drive_re[part] - adj_re * drive_im[part]
            out_re.append(inj[q][0] * adj_re + inj[q][1] * adj_im)
            out_im.append(inj[q][0] * adj_im - inj[q][1] * adj_re)
        grad_proj[rows, lanes_of(q)] = jnp.concatenate(out_re, axis=0).astype(bf16)
        grad_proj[rows, lanes_of(q, half)] = jnp.concatenate(out_im, axis=0).astype(bf16)
        more[q] = (dec_re, dec_im, inj_re, inj_im)
        return tuple(more)

    _, sums = scan(
        meta, source, None, coef_tiles(dec, groups), batches, span, groups,
        not reverse, not reverse, init, ((zero,) * 4,) * groups, visit,
    )
    small[...] = jnp.zeros_like(small)
    for q in range(groups):
        for kind in range(4):
            small[kind : kind + 1, lanes_of(q)] = jnp.sum(sums[q][kind], axis=0, keepdims=True)
    small[4:5, :] = grad_d[...]
    grad_u[...] = dot(grad_proj[...], b_proj[layer], (1, 1))
    skip = norms[layer + 4 : layer + 5, :]
    plain, times_normed = [], []
    for batch in range(batches):
        average = norm[batch : batch + 1, :]
        scale = norm[batches + batch : batches + batch + 1, :]

        def body(start, carry, batch=batch, average=average, scale=scale):
            rows = pl.ds(batch * span + start, ROWS)
            value = grad_u[rows, :] + grad_mixed[rows, :] * skip
            grad_u[rows, :] = value
            normed = (hidden[rows, :].astype(f32) - average) * scale
            return carry[0] + fold(value), carry[1] + fold(value * normed)

        zero_sum = jnp.zeros((CHUNKS, grad_u.shape[1]), f32)
        one, two = row_loop(span, body, (zero_sum, zero_sum))
        plain.append(one)
        times_normed.append(two)
    add_sums(stats, batches, (plain, times_normed))


def backward_finish_last(cfg, *refs):
    ins, before, (grad_proj, grad_u, sums) = refs[:-4], refs[-4], refs[-3:]
    sums[...] = jnp.zeros_like(sums)
    sums[2 * CHUNKS :, :] = before[...]
    backward_finish(
        cfg, *ins, grad_proj, grad_u, sums.at[pl.ds(0, CHUNKS)], sums.at[pl.ds(CHUNKS, CHUNKS)]
    )


def norm_backward(cfg, stats, grad_out, grad_u, hidden, norm, norms, store, shared):
    layer, reverse, batches, span, groups, tokens, count = cfg
    sums = sum(part[...] for part in stats)
    shared[0:1, :] = jnp.sum(sums[batches:], axis=0, keepdims=True)
    shared[1:2, :] = jnp.sum(sums[:batches], axis=0, keepdims=True)
    gain_now = norms[layer : layer + 1, :]
    for batch in range(batches):
        average = norm[batch : batch + 1, :]
        scale = norm[batches + batch : batches + batch + 1, :]
        plain = gain_now * sums[batch : batch + 1] / tokens
        slanted = gain_now * sums[batches + batch : batches + batch + 1] / tokens

        def body(start, carry, batch=batch, average=average, scale=scale, plain=plain, slanted=slanted):
            rows = pl.ds(batch * span + start, ROWS)
            normed = (hidden[rows, :].astype(f32) - average) * scale
            value = grad_out[rows, :].astype(f32) + scale * (
                grad_u[rows, :] * gain_now - plain - normed * slanted
            )
            store(rows, value)
            return carry

        row_loop(span, body)


def between_layers(
    cfg, lower, place, stats, upper_out, upper_u, upper_hidden, upper_norm, norms,
    disc, u, c_proj, w_gate, states_low, act, sig, slope,
    grad_out, shared, grad_gate, grad_mixed, grad_low, source, prefix, total, grad_d, wide,
):
    def store(rows, value):
        grad_out[rows, :] = value

    norm_backward(cfg, stats, upper_out, upper_u, upper_hidden, upper_norm, norms, store, shared)
    meta = place_documents(lower, place)
    backward_start(
        lower, meta, grad_out, disc, u, c_proj, w_gate, states_low, act, sig, slope,
        grad_gate, grad_mixed, grad_low, source, prefix, total, grad_d, wide,
    )


def last_step(cfg, stats, grad_out, grad_u, hidden, norm, norms, target, shared, ordered):
    layer, reverse, batches, span, groups, tokens, count = cfg
    planes = target.shape[1] // LANES

    def store(rows, value):
        for plane in range(planes):
            ordered[plane, rows, :] = value[:, lanes_of(plane)]

    norm_backward(cfg, stats, grad_out, grad_u, hidden, norm, norms, store, shared)
    steps = span // CHUNKS
    for batch in range(batches):
        for chunk in range(CHUNKS):
            at = batch * span
            for plane in range(planes):
                target[at + chunk * steps : at + (chunk + 1) * steps, lanes_of(plane)] = ordered[
                    plane, pl.ds(at + chunk, steps, stride=CHUNKS), :
                ]


def half_weights(core, refs, own, sent):
    for target, half in ((own, core), (sent, 1 - core)):
        at = 0
        for left, right in refs:
            rows = left.shape[1] // 2
            cols = pl.ds(pl.multiple_of(half * rows, LANES), rows)
            target[at : at + rows, :] = dot(left[:, cols], right[...], (0, 0))
            at += rows


def all_weights(here, act, grad_gate, states_low, grad_low, grad_proj, u, own, sent):
    refs = ((act, grad_gate), (states_low, grad_low), (grad_proj, u))
    half_weights(lax.rem(here[0], 2), refs, own, sent)


def gate_weights(here, act, grad_gate, states_low, grad_low, own, sent):
    half_weights(lax.rem(here[0], 2), ((act, grad_gate), (states_low, grad_low)), own, sent)


def input_weights(here, grad_proj, u, own, sent):
    half_weights(lax.rem(here[0], 2), ((grad_proj, u),), own, sent)


def run(body, name, args, outs, scratch=(), scalars=1):
    vmem, smem = pl.BlockSpec(memory_space=pltpu.VMEM), pl.BlockSpec(memory_space=pltpu.SMEM)
    specs = tuple(
        jax.tree.map(lambda _, at=at: smem if at < scalars else vmem, arg)
        for at, arg in enumerate(args)
    )
    return pl.pallas_call(
        body,
        name=name,
        out_shape=tuple(jax.ShapeDtypeStruct(*out) for out in outs),
        in_specs=specs,
        out_specs=(vmem,) * len(outs),
        scratch_shapes=[pltpu.VMEM(*entry) for entry in scratch],
        compiler_params=pltpu.CompilerParams(vmem_limit_bytes=VMEM_LIMIT),
    )(*args)


def put_in_place(layer, here, halves, outs, before, pieces=1):
    width, states = outs[0][0][1], outs[1][0][1]
    rows_w, rows_c = width // 2, states // 2
    vmem, count = pl.BlockSpec(memory_space=pltpu.VMEM), len(halves)

    def half(step, here):
        core = lax.rem(here[0], 2)
        spots = [1 - core if other else core for other, _ in halves]
        return spots[0] if count == 1 else jnp.where(step == 0, *spots)

    blocks = (
        pl.BlockSpec((1, rows_w, width), lambda i, here: (layer, half(i, here), 0)),
        pl.BlockSpec((1, rows_c, width), lambda i, here: (layer, half(i, here), 0)),
        pl.BlockSpec((1, width, rows_c), lambda i, here: (layer, 0, half(i, here))),
    )

    def body(here, *refs):
        grad_w, grad_c, grad_b = refs[-3:]
        for now in range(count):

            @pl.when(pl.program_id(0) == now)
            def _(source=refs[now]):
                gates, inputs = (rows_w + rows_c) // pieces, rows_c // pieces
                columns = []
                for piece in range(pieces):
                    at, row = piece * (gates + inputs), piece * gates
                    turn = min(max(rows_w - row, 0), gates)
                    if turn:
                        grad_w[0, row : row + turn, :] = source[at : at + turn, :]
                    if turn < gates:
                        to = row + turn - rows_w
                        grad_c[0, to : to + gates - turn, :] = source[at + turn : at + gates, :]
                    columns.append(source[at + gates : at + gates + inputs, :])
                grad_b[0] = jnp.concatenate(columns, axis=0).T

    return pl.pallas_call(
        body,
        name="put_in_place",
        out_shape=tuple(jax.ShapeDtypeStruct(*out) for out in outs),
        grid_spec=pltpu.PrefetchScalarGridSpec(
            num_scalar_prefetch=1,
            grid=(count,),
            in_specs=[vmem] * count + [pl.BlockSpec(memory_space=pl.ANY)] * len(before),
            out_specs=blocks,
        ),
        input_output_aliases={1 + count + i: i for i in range(len(before))},
        compiler_params=pltpu.CompilerParams(vmem_limit_bytes=VMEM_LIMIT),
    )(here, *(rows for _, rows in halves), *before)


def axis_parts():
    count, depth = lax.axis_size("seq"), lax.axis_size("dp")
    return (("seq", 2, 1, count), ("seq", count // 2, 2, count), ("dp", depth, 1, depth))


def shifted(value, part, away):
    name, size, stride, count = part
    pairs = []
    for i in range(count):
        place = (i // stride) % size
        pairs.append((i, i + ((place + away) % size - place) * stride))
    return lax.ppermute(value, name, pairs)


def add_by_shifts(value, parts, *earlier):
    for number, part in enumerate(parts):
        if number:
            value = sum(terms[1:], terms[0])
        if number == len(parts) - 1:
            value, *earlier = lax.optimization_barrier((value, *earlier))
        terms = [value] + [shifted(value, part, away) for away in range(1, part[1])]
    return terms, *earlier


def bits_of(size, stride=1):
    bits = []
    while size > 1:
        bits.append(stride)
        size, stride = size // 2, stride * 2
    return bits


def plane_bits():
    chip_bits = bits_of(lax.axis_size("seq") // 2, 2)
    middle = (len(chip_bits) + 1) // 2
    inner, outer = chip_bits[:middle], chip_bits[middle:]
    return list(zip(inner + outer, outer + inner))


def swap(value, axis, bit):
    return lax.ppermute(value, axis, [(i, i ^ bit) for i in range(lax.axis_size(axis))])


def bit_at(here, axis, bit):
    return lax.rem(lax.div(here[0 if axis == "seq" else 1], bit), 2)


def rows_at(half, rows):
    return pl.ds(pl.multiple_of(half * rows, CHUNKS), rows)


def fold_cores(bits, here, *refs):
    terms, targets = refs[:-4], refs[-4:]
    rows, cols = targets[0].shape
    for side in (0, 1):
        kept, sent = targets[2 * side : 2 * side + 2]
        where = slice(side * cols, (side + 1) * cols)
        bit = bit_at(here, "seq", bits[side])
        for half in (0, 1):

            @pl.when(bit == half)
            def _(half=half, kept=kept, sent=sent, where=where):
                start = 0
                for own, found in zip(terms[0::2], terms[1::2]):
                    for part, target in ((half, kept), (1 - half, sent)):
                        low = max(start, part * rows)
                        high = min(start + own.shape[0], (part + 1) * rows)
                        if low < high:
                            source = slice(low - start, high - start)
                            target[low - part * rows : high - part * rows, :] = (
                                own[source, where] + found[source, where]
                            )
                    start += own.shape[0]


def fold_sides(bits, here, *refs):
    targets, blocks = refs[-4:], refs[:-4]
    for side in (0, 1):
        kept, sent = targets[2 * side : 2 * side + 2]
        half, start = bit_at(here, "seq", bits[side]), 0
        for at in range(0, len(blocks), 4):
            own, found = blocks[at + 2 * side : at + 2 * side + 2]
            rows = own.shape[0] // 2
            to = slice(start, start + rows)
            kept[to, :] = own[rows_at(half, rows), :] + found[rows_at(half, rows), :]
            sent[to, :] = own[rows_at(1 - half, rows), :] + found[rows_at(1 - half, rows), :]
            start += rows


def fold_join(bit, here, left, found_left, right, found_right, kept, sent):
    rows, cols = kept.shape[0], left.shape[1]
    half = bit_at(here, "dp", bit)
    for side, (own, found) in enumerate(((left, found_left), (right, found_right))):
        where = slice(side * cols, (side + 1) * cols)
        kept[:, where] = own[rows_at(half, rows), :] + found[rows_at(half, rows), :]
        sent[:, where] = own[rows_at(1 - half, rows), :] + found[rows_at(1 - half, rows), :]


def fold_depth(bit, here, own, found, kept, sent):
    half, rows = bit_at(here, "dp", bit), kept.shape[0]
    kept[...] = own[rows_at(half, rows), :] + found[rows_at(half, rows), :]
    sent[...] = own[rows_at(1 - half, rows), :] + found[rows_at(1 - half, rows), :]


def add_two(own, found, out):
    out[...] = own[...] + found[...]


def unfold(bit, here, own, found, out):
    half, rows = bit_at(here, "dp", bit), own.shape[0]
    out[rows_at(half, rows), :] = own[...]
    out[rows_at(1 - half, rows), :] = found[...]


def unfold_split(bit, here, own, found, left, right):
    half, rows, cols = bit_at(here, "dp", bit), own.shape[0], left.shape[1]
    for side, out in enumerate((left, right)):
        where = slice(side * cols, (side + 1) * cols)
        out[rows_at(half, rows), :] = own[:, where]
        out[rows_at(1 - half, rows), :] = found[:, where]


def unfold_sides(bits, joined, here, *refs):
    for side in (0, 1):
        own, found = refs[2 * side : 2 * side + 2]
        half, (rows, cols) = bit_at(here, "seq", bits[side]), own.shape
        out = refs[4] if joined else refs[4 + side]
        where = slice(side * cols, (side + 1) * cols) if joined else slice(0, cols)
        out[rows_at(half, rows), where] = own[...]
        out[rows_at(1 - half, rows), where] = found[...]


def link_call(body, here, args, shapes):
    name = body.func.__name__
    return run(body, name, (here, *args), tuple((shape, f32) for shape in shapes))


class LinkSum:
    def __init__(self, here, terms):
        self.here, self.plane = here, plane_bits()
        self.depth = bits_of(lax.axis_size("dp"))
        rows = sum(term.shape[0] for term in terms[::2])
        self.shape = (rows // 2, terms[0].shape[1] // 2)
        self.parts = link_call(
            functools.partial(fold_cores, self.plane[0]), here, terms, (self.shape,) * 4
        )

    def swap_plane(self, stage):
        (left, right), pieces = self.plane[stage], self.parts
        self.parts = (
            pieces[0], swap(pieces[1], "seq", left), pieces[2], swap(pieces[3], "seq", right)
        )

    def down_plane(self, stage, *others):
        parts, rows, cols = list(self.parts), *self.shape
        for other in others:
            parts += other.parts
            rows += other.shape[0]
        self.shape = (rows // 2, cols)
        body = functools.partial(fold_sides, self.plane[stage])
        self.parts = link_call(body, self.here, parts, (self.shape,) * 4)

    def down_join(self):
        rows, cols = self.shape
        self.shape = (rows // 2, 2 * cols)
        body = functools.partial(fold_join, self.depth[0])
        self.parts = link_call(body, self.here, self.parts, (self.shape,) * 2)

    def swap_depth(self, stage):
        self.parts = (self.parts[0], swap(self.parts[1], "dp", self.depth[stage]))

    def down_depth(self, stage):
        rows, cols = self.shape
        self.shape = (rows // 2, cols)
        body = functools.partial(fold_depth, self.depth[stage])
        self.parts = link_call(body, self.here, self.parts, (self.shape,) * 2)

    def middle(self):
        (value,) = run(add_two, "add_two", self.parts, ((self.shape, f32),), scalars=0)
        self.parts = (value, value)

    def up_depth(self, stage):
        rows, cols = self.shape
        self.shape = (rows * 2, cols)
        body = functools.partial(unfold, self.depth[stage])
        (value,) = link_call(body, self.here, self.parts, (self.shape,))
        self.parts = (value, value)

    def up_split(self):
        rows, cols = self.shape
        self.shape = (rows * 2, cols // 2)
        body = functools.partial(unfold_split, self.depth[0])
        left, right = link_call(body, self.here, self.parts, (self.shape,) * 2)
        self.parts = (left, left, right, right)

    def up_plane(self, stage):
        rows, cols = self.shape
        if stage:
            self.shape = (rows * 2, cols)
            body = functools.partial(unfold_sides, self.plane[stage], False)
            left, right = link_call(body, self.here, self.parts, (self.shape,) * 2)
            self.parts = (left, left, right, right)
        else:
            self.shape = (rows * 2, cols * 2)
            body = functools.partial(unfold_sides, self.plane[stage], True)
            self.parts = link_call(body, self.here, self.parts, (self.shape,))

    def after(self, *values):
        self.parts, values = lax.optimization_barrier((self.parts, values))
        return values

    def to_depth(self):
        for stage in range(2, len(self.plane)):
            self.swap_plane(stage - 1)
            self.down_plane(stage)
        self.swap_plane(len(self.plane) - 1)

    def scatter_depth(self):
        for stage in range(len(self.depth) - 1):
            if stage:
                self.down_depth(stage)
            self.swap_depth(stage)

    def swap_whole(self):
        self.parts = (self.parts[0], swap(self.parts[0], "dp", self.depth[-1]))

    def gather_depth(self):
        for stage in range(len(self.depth) - 2, 0, -1):
            self.swap_depth(stage)
            self.up_depth(stage)
        self.swap_depth(0)


def wait_for(*things):
    sums = [thing for thing in things if isinstance(thing, LinkSum)]
    values = [thing for thing in things if not isinstance(thing, LinkSum)]
    parts, values = lax.optimization_barrier(([entry.parts for entry in sums], values))
    for entry, part in zip(sums, parts):
        entry.parts = part
    return values


def discretize(lam_re, lam_im, log_step):
    step_size = jnp.exp(log_step)
    decay_abs = jnp.exp(lam_re * step_size)
    rotation = lam_im * step_size
    dec_re = decay_abs * jnp.cos(rotation)
    dec_im = decay_abs * jnp.sin(rotation)
    denom_sq = lam_re * lam_re + lam_im * lam_im
    inj_re = ((dec_re - 1.0) * lam_re + dec_im * lam_im) / denom_sq
    inj_im = (dec_im * lam_re - (dec_re - 1.0) * lam_im) / denom_sq
    return (dec_re, dec_im, inj_re, inj_im)


def per_device(
    block_in, cotangent, doc_lengths, norm_gain, norm_shift, log_step, lam_re, lam_im,
    b_proj, c_proj, d_skip, w_gate,
):
    batches, seqs, span, width = block_in.shape
    assert seqs == 1 and span % (4 * CHUNKS) == 0 and span & (span - 1) == 0
    half = lam_re.shape[1]
    groups = half // LANES
    rows = batches * span
    count = lax.axis_size("seq")
    tokens = float(seqs * lax.axis_size("dp") * span * count)
    here = jnp.stack([lax.axis_index("seq"), lax.axis_index("dp")]).astype(jnp.int32)
    place = jnp.concatenate([here] + [doc_lengths[batch, 0] for batch in range(batches)])
    place, block_in = lax.optimization_barrier((place, block_in))
    here = place
    disc = discretize(lam_re, lam_im, log_step)

    x = block_in.reshape(rows, width)
    cot = cotangent.reshape(rows, width)
    lower = (0, False, batches, span, groups, tokens, count)
    upper = (1, True, batches, span, groups, tokens, count)
    part = functools.partial

    flat, low = ((rows, width), f32), ((rows, width), bf16)
    wide, wide_low = ((rows, 2 * half), f32), ((rows, 2 * half), bf16)
    padded = ((batches * (span + CHUNKS), 2 * half), f32)
    sums = ((2 * batches, width), f32)
    prefix = ((2, batches * CHUNKS, 2 * half), f32)
    total = ((batches, 2 * half), f32)
    line, shared = ((1, width), f32), ((2, width), f32)
    small = ((8, width), f32)

    def gather_row(value, reverse):
        both = jnp.concatenate([value, swap(value, "seq", 1)], axis=0)
        chips = count // 2
        return [both] + [
            shifted(both, plane, chips - away if reverse else away) for away in range(1, chips)
        ]

    (stats,) = run(part(first_sums, batches, span), "first_sums", (x,), (sums,), scalars=0)

    def order(value, inverse):
        body = part(order_rows, batches, span, inverse)
        return run(body, "order_rows", (value,), (low,), scalars=0)[0]

    norms = jnp.concatenate([norm_gain, norm_shift, d_skip], axis=0)

    def forward(cfg, hidden, stats):
        return run(
            part(enter_layer, cfg),
            "enter_layer",
            (place, stats, hidden, norms, disc, b_proj),
            (low, wide, prefix, total, sums),
        )

    links, plane, depth = axis_parts()
    stats, ordered = lax.optimization_barrier(
        (add_by_shifts(stats, (links, plane, depth))[0], order(x, False))
    )
    u0, drive0, prefix0, total0, norm0 = forward(lower, ordered, stats)
    states0, states_low0, act0, sig0, slope0, hidden1, stats = run(
        part(middle_forward, lower),
        "middle_forward",
        (place, gather_row(total0, False), prefix0, disc, drive0, u0, ordered, c_proj, norms, w_gate),
        (padded, wide_low, low, flat, flat, flat, sums),
        (flat,),
    )
    cot, stats = lax.optimization_barrier((cot, stats))
    stats, ordered_cot = lax.optimization_barrier(
        (add_by_shifts(stats, (links, plane, depth))[0], order(cot, False))
    )
    u1, drive1, prefix1, total1, norm1 = forward(upper, hidden1, stats)
    (
        result1, states1, states_low1, act1, grad_gate1, grad_mixed1, grad_low1,
        source1, prefix1, total1, grad_d1,
    ) = run(
        part(turn_around, upper),
        "turn_around",
        (
            place, gather_row(total1, True), prefix1, disc, drive1, u1, hidden1, c_proj, norms, w_gate,
            ordered_cot,
        ),
        (low, padded, wide_low, low, low, flat, low, wide, prefix, total, line),
        (flat, flat, flat),
    )

    def halves(length):
        return (((length // 2, width), f32),) * 2

    grad_proj1, grad_u1, stats, small1 = run(
        part(backward_finish, upper),
        "backward_finish",
        (
            place, gather_row(total1, False), prefix1, disc, source1, drive1, states1, u1, grad_mixed1,
            grad_d1, hidden1, norm1, norms, b_proj,
        ),
        (wide_low, flat, sums, small),
    )
    sizes = (width + 2 * half, 2 * half)
    own1, sent1 = run(
        all_weights,
        "all_weights",
        (here, act1, grad_gate1, states_low1, grad_low1, grad_proj1, u1),
        halves(sum(sizes)),
    )
    stats = stats + swap(stats, "seq", 1)
    stats, sent1 = lax.optimization_barrier((stats, sent1))
    upper_sum = LinkSum(here, (own1, swap(sent1, "seq", 1)))
    stats, upper_sum.parts = add_by_shifts(stats, (plane, depth), upper_sum.parts)
    upper_sum.swap_plane(0)
    (
        grad_out0, shared1, grad_gate0, grad_mixed0, grad_low0, source0, prefix0, total0, grad_d0,
    ) = run(
        part(between_layers, upper, lower),
        "between_layers",
        (
            place, stats, ordered_cot, grad_u1, hidden1, norm1, norms,
            disc, u0, c_proj, w_gate, states_low0, act0, sig0, slope0,
        ),
        (flat, shared, low, flat, low, wide, prefix, total, line),
        (flat,),
    )
    (total0,) = upper_sum.after(total0)
    upper_sum.down_plane(1)
    (total0,) = upper_sum.after(total0)
    upper_sum.to_depth()
    ends, grad_gate0 = wait_for(upper_sum, gather_row(total0, True), grad_gate0)
    upper_sum.down_join()
    ends, grad_gate0 = wait_for(upper_sum, ends, grad_gate0)
    upper_sum.scatter_depth()
    own_gates, sent_gates = run(
        gate_weights, "gate_weights", (here, act0, grad_gate0, states_low0, grad_low0),
        halves(sizes[0]),
    )
    own_gates, ends = lax.optimization_barrier((own_gates, ends))
    grad_proj0, grad_u0, last_sums = run(
        part(backward_finish_last, lower),
        "backward_finish",
        (
            place, ends, prefix0, disc, source0, drive0, states0, u0, grad_mixed0, grad_d0,
            ordered, norm0, norms, b_proj, small1,
        ),
        (wide_low, flat, ((3 * CHUNKS, width), f32)),
    )
    lower_sum = LinkSum(here, (own_gates, swap(sent_gates, "seq", 1)))
    (grad_proj0,) = wait_for(upper_sum, lower_sum, grad_proj0)
    own_inputs, sent_inputs = run(
        input_weights, "input_weights", (here, grad_proj0, u0), halves(sizes[1])
    )
    inputs_sum = LinkSum(here, (own_inputs, swap(sent_inputs, "seq", 1)))
    upper_sum.middle()
    upper_sum.swap_whole()
    lower_sum.swap_plane(0)
    inputs_sum.swap_plane(0)
    wait_for(upper_sum, lower_sum, inputs_sum)

    lower_sum.down_plane(1, inputs_sum)
    upper_sum.middle()
    upper_sum.gather_depth()
    lower_sum.to_depth()
    wait_for(upper_sum, lower_sum)

    lower_sum.down_join()
    upper_sum.up_split()
    lower_sum.scatter_depth()
    upper_sum.swap_plane(len(upper_sum.plane) - 1)
    wait_for(upper_sum, lower_sum)

    lower_sum.middle()
    lower_sum.swap_whole()
    for stage in range(len(upper_sum.plane) - 1, 0, -1):
        upper_sum.up_plane(stage)
        upper_sum.swap_plane(stage - 1)
    (last_sums,) = wait_for(upper_sum, lower_sum, last_sums)

    lower_sum.middle()
    (last_sums,) = lower_sum.after(last_sums)
    lower_sum.gather_depth()
    last_sums = last_sums + swap(last_sums, "seq", 1)
    last_terms = [last_sums] + [shifted(last_sums, plane, away) for away in range(1, plane[1])]
    last_terms = wait_for(lower_sum, *last_terms)

    lower_sum.up_split()
    wait_for(upper_sum, lower_sum)
    lower_sum.swap_plane(len(lower_sum.plane) - 1)
    upper_sum.up_plane(0)
    own1, result1 = lax.optimization_barrier((upper_sum.parts[0], result1))
    other1 = swap(own1, "seq", 1)
    block_out = order(result1, True)
    final = (((2, width, width), f32), ((2, 2 * half, width), f32), ((2, width, 2 * half), f32))
    placed = put_in_place(1, here, ((False, own1), (True, other1)), final, ())
    summed = sum(last_terms)
    for bit in bits_of(lax.axis_size("dp")):
        summed = summed + swap(summed, "dp", bit)
    summed, block_out = wait_for(lower_sum, summed, block_out)

    for stage in range(len(lower_sum.plane) - 1, 0, -1):
        lower_sum.up_plane(stage)
        if stage == 1:
            (summed,) = lower_sum.after(summed)
        lower_sum.swap_plane(stage - 1)
    grad_input, shared0 = run(
        part(last_step, lower),
        "last_step",
        ((summed[: 2 * batches],), grad_out0, grad_u0, ordered, norm0, norms),
        (flat, shared),
        (((width // LANES, rows, LANES), f32),),
        scalars=0,
    )
    small_sum = summed[CHUNKS:].reshape(2, CHUNKS, width)
    _, pullback = jax.vjp(discretize, lam_re, lam_im, log_step)
    grad_lr, grad_li, grad_ls = pullback(tuple(small_sum[:, kind, :half] for kind in range(4)))
    grad_input, grad_lr, grad_li, grad_ls, *placed = wait_for(
        lower_sum, grad_input, grad_lr, grad_li, grad_ls, *placed
    )

    lower_sum.up_plane(0)
    own0 = lower_sum.parts[0]
    other0 = swap(own0, "seq", 1)
    placed = put_in_place(0, here, ((False, own0),), final, placed, 4)
    grad_w, grad_c, grad_b = put_in_place(0, here, ((True, other0),), final, placed, 4)
    both = jnp.stack([shared0, shared1])
    shape = block_in.shape
    return (
        block_out.reshape(shape), grad_input.reshape(shape), both[:, 0], both[:, 1],
        grad_ls, grad_lr, grad_li, grad_b, grad_c, small_sum[:, 4], grad_w,
    )


def solution(mesh):
    split = P(None, "dp", "seq", None)
    return jax.shard_map(
        per_device,
        mesh=mesh,
        in_specs=(split, split, P(None, "dp", None)) + (P(),) * 9,
        out_specs=(split, split) + (P(),) * 9,
        check_vma=False,
    )
```

```python
import copy
import functools

import jax
import jax.numpy as jnp
from jax import lax
from jax.experimental import pallas as pl
from jax.experimental.pallas import tpu as pltpu
from jax.sharding import PartitionSpec as P

f32, bf16 = jnp.float32, jnp.bfloat16
epsilon = 1e-05
tanh_scale = 0.7978845608028654
cubic_term = 0.044715
LANES = 128
CHUNKS = 8
ROWS = 32
VMEM_LIMIT = 16 * 1024 * 1024


def dot(left, right, contract=(1, 0)):
    return lax.dot_general(
        left, right, (((contract[0],), (contract[1],)), ((), ())), preferred_element_type=f32
    )


def reorder(span, inverse):
    shape = (span, span)
    kept, moved = (1, 0) if inverse else (0, 1)
    row = lax.broadcasted_iota(jnp.int32, shape, kept)
    position = lax.broadcasted_iota(jnp.int32, shape, moved)
    source = (row & (CHUNKS - 1)) * (span // CHUNKS) + (row >> 3)
    return jnp.where(position == source, 1.0, 0.0).astype(bf16)


def row_loop(count, body, init=0, step=ROWS):
    def one(index, carry):
        return body(pl.multiple_of(index * step, step), carry)

    return lax.fori_loop(0, count // step, one, init, unroll=2)


def documents(here, batches, span, count):
    mine = here[0]
    first = mine * span
    out = []
    for batch in range(batches):
        begins, ends, so_far = [], [], 0
        docs = (here.shape[0] - 2) // batches
        for doc in range(docs):
            begins.append(so_far)
            so_far = so_far + here[2 + batch * docs + doc]
            ends.append(so_far)
        before, after = 0, 2 * count * span
        for begin, end in zip(begins, ends):
            before = jnp.maximum(before, jnp.where(begin < first, begin, 0))
            after = jnp.minimum(after, jnp.where(end > first + span, end, 2 * count * span))
        after = jnp.where(mine == count - 1, 0, after)
        out.append(begins + ends + [before, after, first, mine])
    return out


def place_documents(cfg, place):
    layer, reverse, batches, span, groups, tokens, count = cfg
    return documents(place, batches, span, count)


def keep_of(meta, batch, base, step, backward):
    docs = (len(meta[batch]) - 4) // 2
    off = docs if backward else 0
    late = 1 if backward else 0
    stop = base == meta[batch][off] - step - late
    for doc in range(1, docs):
        stop = jnp.logical_or(stop, base == meta[batch][off + doc] - step - late)
    return jnp.where(stop, 0.0, 1.0)


def base_positions(meta, steps):
    return meta[0][-2] + lax.broadcasted_iota(jnp.int32, (CHUNKS, LANES), 0) * steps


def lanes_of(index, half=0):
    return slice(half + index * LANES, half + (index + 1) * LANES)


def coef_tiles(value, groups):
    return [
        tuple(jnp.broadcast_to(part[:, lanes_of(q)], (CHUNKS, LANES)) for part in value)
        for q in range(groups)
    ]


def constants(disc, layer):
    dec_re, dec_im, inj_re, inj_im = (part[layer : layer + 1, :] for part in disc)
    return (dec_re, dec_im), (inj_re, inj_im)


def times(a, b):
    return (a[0] * b[0] - a[1] * b[1], a[0] * b[1] + a[1] * b[0])


def power(value, exponent):
    for _ in range(exponent.bit_length() - 1):
        value = times(value, value)
    return value


def conj(value):
    return (value[0], -value[1])


def scan(meta, source, inject, dec, batches, span, groups, reverse, masks_reverse, init, extra, visit):
    steps = span // CHUNKS
    half = groups * LANES
    base = base_positions(meta, steps)

    def pair(index, carry):
        states, more = carry
        states = list(states)
        first = steps - 2 - 2 * index if reverse else 2 * index
        start = pl.multiple_of(first * CHUNKS, 2 * CHUNKS)
        order = (1, 0) if reverse else (0, 1)
        for batch in range(batches):
            keeps = [keep_of(meta, batch, base, first + j, masks_reverse) for j in (0, 1)]
            for q in range(groups):
                rows = pl.ds(batch * span + start, 2 * CHUNKS)
                src_re = source[rows, lanes_of(q)]
                src_im = source[rows, lanes_of(q, half)]
                state = states[batch * groups + q]
                found = [None, None]
                for j in order:
                    part = (
                        src_re[j * CHUNKS : (j + 1) * CHUNKS],
                        src_im[j * CHUNKS : (j + 1) * CHUNKS],
                    )
                    push = times(inject[q], part) if inject is not None else part
                    held = times((keeps[j] * dec[q][0], keeps[j] * dec[q][1]), state)
                    state = (held[0] + push[0], held[1] + push[1])
                    found[j] = state
                states[batch * groups + q] = state
                more = visit(more, batch, q, first, start, found, (src_re, src_im))
            more = visit(more, batch, None, first, start, keeps, None)
        return tuple(states), more

    return lax.fori_loop(0, steps // 2, pair, (tuple(init), extra), unroll=4)


def zero_states(batches, groups):
    zero = jnp.zeros((CHUNKS, LANES), f32)
    return [(zero, zero)] * (batches * groups)


def local_ends(meta, source, inject, dec, batches, span, groups, reverse, prefix, total):
    ones = tuple(jnp.ones((CHUNKS, LANES), f32) for _ in range(batches))

    def visit(more, batch, q, first, start, found, src):
        if q is not None:
            return more
        return tuple(
            value * found[0] * found[1] if at == batch else value for at, value in enumerate(more)
        )

    dec_chunk = coef_tiles(power(dec, span // CHUNKS), groups)
    ends, kept = scan(
        meta, source, inject, coef_tiles(dec, groups), batches, span, groups, reverse, reverse,
        zero_states(batches, groups), ones, visit,
    )
    half = groups * LANES
    row = lax.broadcasted_iota(jnp.int32, (CHUNKS, LANES), 0)
    for batch in range(batches):
        for q in range(groups):
            end = ends[batch * groups + q]
            decay = (kept[batch] * dec_chunk[q][0], kept[batch] * dec_chunk[q][1])
            for shift in (1, 2, 4):
                turn = CHUNKS - shift if reverse else shift
                valid = row < CHUNKS - shift if reverse else row >= shift
                before = [pltpu.roll(value, turn, 0) for value in (*end, *decay)]
                from_before = times(decay, (before[0], before[1]))
                end = (
                    end[0] + jnp.where(valid, from_before[0], 0.0),
                    end[1] + jnp.where(valid, from_before[1], 0.0),
                )
                longer = times(decay, (before[2], before[3]))
                decay = (
                    jnp.where(valid, longer[0], decay[0]),
                    jnp.where(valid, longer[1], decay[1]),
                )
            rows = slice(batch * CHUNKS, (batch + 1) * CHUNKS)
            prefix[0, rows, lanes_of(q)] = end[0]
            prefix[0, rows, lanes_of(q, half)] = end[1]
            prefix[1, rows, lanes_of(q)] = decay[0]
            prefix[1, rows, lanes_of(q, half)] = decay[1]
            last = 0 if reverse else CHUNKS - 1
            total[batch : batch + 1, lanes_of(q)] = end[0][last : last + 1]
            total[batch : batch + 1, lanes_of(q, half)] = end[1][last : last + 1]


def chunk_carries(meta, gathered, dec, prefix, batches, span, groups, reverse):
    half = groups * LANES
    dec_span = power(dec, span)
    row = lax.broadcasted_iota(jnp.int32, (CHUNKS, LANES), 0)
    mine = meta[0][-1]
    core = lax.rem(mine, 2)
    out = []
    for batch in range(batches):
        enter = (jnp.zeros((1, half), f32), jnp.zeros((1, half), f32))
        for away in range(len(gathered) - 1, -1, -1):
            for kind in (1, 0) if reverse else (0, 1):
                if away == 0 and kind == (0 if reverse else 1):
                    continue
                if reverse:
                    other = mine - core + 2 * away + kind
                    reaches = meta[batch][-3] > other * span
                else:
                    other = mine - core - 2 * away + kind
                    reaches = meta[batch][-4] < (other + 1) * span
                same = gathered[away][batch : batch + 1, :]
                unlike = gathered[away][batches + batch : batches + batch + 1, :]
                value = jnp.where(reaches, jnp.where(core == kind, same, unlike), 0.0)
                moved = times(dec_span, enter)
                after = (moved[0] + value[:, :half], moved[1] + value[:, half:])
                if away == 0:
                    after = tuple(jnp.where(core == kind, old, new) for old, new in zip(enter, after))
                enter = after
        rows = slice(batch * CHUNKS, (batch + 1) * CHUNKS)
        for q in range(groups):
            own = tuple(jnp.broadcast_to(part[:, lanes_of(q)], (CHUNKS, LANES)) for part in enter)
            end = (prefix[0, rows, lanes_of(q)], prefix[0, rows, lanes_of(q, half)])
            decay = (prefix[1, rows, lanes_of(q)], prefix[1, rows, lanes_of(q, half)])
            moved = times(decay, own)
            turn, first = (CHUNKS - 1, CHUNKS - 1) if reverse else (1, 0)
            out.append(
                tuple(
                    jnp.where(row == first, own[i], pltpu.roll(end[i] + moved[i], turn, 0))
                    for i in (0, 1)
                )
            )
    return out


def add_sums(target, batches, sums):
    for kind, per_batch in enumerate(sums):
        for batch in range(batches):
            target[kind * batches + batch : kind * batches + batch + 1, :] = jnp.sum(
                per_batch[batch], axis=0, keepdims=True
            )


def fold(value):
    return sum(value[i : i + CHUNKS] for i in range(CHUNKS, value.shape[0], CHUNKS)) + value[:CHUNKS]


def order_rows(batches, span, inverse, x, out):
    turn = reorder(span, inverse)
    for batch in range(batches):
        rows = slice(batch * span, (batch + 1) * span)
        out[rows, :] = dot(turn, x[rows, :]).astype(bf16)


def first_sums(batches, span, x, stats):
    width = x.shape[1]
    sums, squares = [], []
    for batch in range(batches):

        def body(start, carry, batch=batch):
            value = x[pl.ds(batch * span + start, ROWS), :].astype(f32)
            return carry[0] + fold(value), carry[1] + fold(value * value)

        zero = jnp.zeros((CHUNKS, width), f32)
        one, two = row_loop(span, body, (zero, zero))
        sums.append(one)
        squares.append(two)
    add_sums(stats, batches, (sums, squares))


def enter_layer(
    cfg, place, stats, hidden, norms, disc, b_proj, u, drive, prefix, total, norm
):
    layer, reverse, batches, span, groups, tokens, count = cfg
    sums = sum(part[...] for part in stats)
    average = sums[:batches] / tokens
    spread = sums[batches:] / tokens - average * average
    scale = lax.rsqrt(spread + epsilon)
    norm[:batches, :] = average
    norm[batches:, :] = scale
    gain_now, shift_now = norms[layer : layer + 1, :], norms[layer + 2 : layer + 3, :]
    for batch in range(batches):

        def body(start, carry, batch=batch):
            rows = pl.ds(batch * span + start, ROWS)
            normed = (hidden[rows, :].astype(f32) - average[batch : batch + 1]) * scale[
                batch : batch + 1
            ]
            u[rows, :] = (normed * gain_now + shift_now).astype(bf16)
            return carry

        row_loop(span, body)
    drive[...] = dot(u[...], b_proj[layer])
    meta = place_documents(cfg, place)
    dec, inj = constants(disc, layer)
    local_ends(
        meta, drive, coef_tiles(inj, groups), dec, batches, span, groups, reverse, prefix, total
    )


def finish_states(cfg, meta, ends, prefix, disc, drive, states, states_low):
    layer, reverse, batches, span, groups, tokens, count = cfg
    half = groups * LANES
    padded = span + CHUNKS
    dec, inj = constants(disc, layer)
    init = chunk_carries(meta, ends, dec, prefix, batches, span, groups, reverse)
    for batch in range(batches):
        edge = batch * padded + (span if reverse else 0)
        for q in range(groups):
            states[edge : edge + CHUNKS, lanes_of(q)] = init[batch * groups + q][0]
            states[edge : edge + CHUNKS, lanes_of(q, half)] = init[batch * groups + q][1]

    def visit(more, batch, q, first, start, found, src):
        if q is not None:
            for part, off in ((0, 0), (1, half)):
                both = jnp.concatenate([found[0][part], found[1][part]], axis=0)
                at = batch * padded + (0 if reverse else CHUNKS)
                states[pl.ds(at + start, 2 * CHUNKS), lanes_of(q, off)] = both
                states_low[pl.ds(batch * span + start, 2 * CHUNKS), lanes_of(q, off)] = both.astype(
                    bf16
                )
        return more

    scan(
        meta, drive, coef_tiles(inj, groups), coef_tiles(dec, groups), batches, span, groups,
        reverse, reverse, init, 0, visit,
    )


def forward_finish(
    cfg, meta, ends, prefix, disc, drive, u, hidden, c_proj, norms, w_gate,
    states, states_low, act, sig, slope, result, wide, emit,
):
    layer, reverse, batches, span, groups, tokens, count = cfg
    finish_states(cfg, meta, ends, prefix, disc, drive, states, states_low)
    wide[...] = dot(states_low[...], c_proj[layer])
    skip = norms[layer + 4 : layer + 5, :]

    def body(start, carry):
        rows = pl.ds(start, ROWS)
        mixed = wide[rows, :] + skip * u[rows, :].astype(f32)
        square = mixed * mixed
        th = jnp.tanh(tanh_scale * (mixed + cubic_term * square * mixed))
        half_one = 0.5 * (1.0 + th)
        act[rows, :] = (mixed * half_one).astype(bf16)
        slope[rows, :] = half_one + 0.5 * mixed * (1.0 - th * th) * tanh_scale * (
            1.0 + 3.0 * cubic_term * square
        )
        return carry

    row_loop(batches * span, body)
    wide[...] = dot(act[...], w_gate[layer])
    sums, squares = [], []
    for batch in range(batches):

        def gate(start, carry, batch=batch):
            rows = pl.ds(batch * span + start, ROWS)
            sig_now = 0.5 + 0.5 * jnp.tanh(0.5 * wide[rows, :])
            sig[rows, :] = sig_now
            value = hidden[rows, :].astype(f32) + act[rows, :].astype(f32) * sig_now
            result[rows, :] = value.astype(result.dtype)
            if emit is None:
                return carry
            return carry[0] + fold(value), carry[1] + fold(value * value)

        zero = jnp.zeros((CHUNKS, wide.shape[1]), f32)
        one, two = row_loop(span, gate, (zero, zero))
        sums.append(one)
        squares.append(two)
    if emit is not None:
        add_sums(emit, batches, (sums, squares))


def backward_start(
    cfg, meta, grad_out, disc, u, c_proj, w_gate, states_low, act, sig, slope,
    grad_gate, grad_mixed, grad_low, source, prefix, total, grad_d, wide,
):
    layer, reverse, batches, span, groups, tokens, count = cfg

    def body(start, carry):
        rows = pl.ds(start, ROWS)
        sig_now = sig[rows, :]
        grad_gate[rows, :] = (
            grad_out[rows, :].astype(f32) * act[rows, :].astype(f32) * sig_now * (1.0 - sig_now)
        ).astype(bf16)
        return carry

    row_loop(batches * span, body)
    wide[...] = dot(grad_gate[...], w_gate[layer], (1, 1))

    def mixed(start, carry):
        rows = pl.ds(start, ROWS)
        value = (grad_out[rows, :].astype(f32) * sig[rows, :] + wide[rows, :]) * slope[rows, :]
        grad_mixed[rows, :] = value
        grad_low[rows, :] = value.astype(bf16)
        return carry + fold(value * u[rows, :].astype(f32))

    gd = row_loop(batches * span, mixed, jnp.zeros((CHUNKS, wide.shape[1]), f32))
    grad_d[...] = jnp.sum(gd, axis=0, keepdims=True)
    source[...] = dot(grad_low[...], c_proj[layer], (1, 1))
    local_ends(
        meta, source, None, conj(constants(disc, layer)[0]), batches, span, groups, not reverse,
        prefix, total,
    )


def middle_forward(
    cfg, place, ends, prefix, disc, drive, u, hidden, c_proj, norms, w_gate,
    states, states_low, act, sig, slope, result, stats, wide,
):
    meta = place_documents(cfg, place)
    forward_finish(
        cfg, meta, ends, prefix, disc, drive, u, hidden, c_proj, norms, w_gate,
        states, states_low, act, sig, slope, result, wide, stats,
    )


def turn_around(
    cfg, place, ends, prefix, disc, drive, u, hidden, c_proj, norms, w_gate, ordered_cot,
    result, states, states_low, act, grad_gate, grad_mixed, grad_low, source,
    back_prefix, total, grad_d, sig, slope, wide,
):
    layer, reverse, batches, span, groups, tokens, count = cfg
    meta = place_documents(cfg, place)
    forward_finish(
        cfg, meta, ends, prefix, disc, drive, u, hidden, c_proj, norms, w_gate,
        states, states_low, act, sig, slope, result, wide, None,
    )
    backward_start(
        cfg, meta, ordered_cot, disc, u, c_proj, w_gate, states_low, act, sig, slope,
        grad_gate, grad_mixed, grad_low, source, back_prefix, total, grad_d, wide,
    )


def backward_finish(
    cfg, place, ends, prefix, disc, source, drive, states, u, grad_mixed, grad_d, hidden, norm,
    norms, b_proj, grad_proj, grad_u, stats, small,
):
    layer, reverse, batches, span, groups, tokens, count = cfg
    half = groups * LANES
    padded = span + CHUNKS
    steps = span // CHUNKS
    meta = place_documents(cfg, place)
    dec, inj = constants(disc, layer)
    dec = conj(dec)
    init = chunk_carries(meta, ends, dec, prefix, batches, span, groups, not reverse)
    inj = coef_tiles(inj, groups)
    base = base_positions(meta, steps)
    zero = jnp.zeros((CHUNKS, LANES), f32)

    def visit(more, batch, q, first, start, found, src):
        if q is None:
            return more
        more = list(more)
        rows = pl.ds(batch * span + start, 2 * CHUNKS)
        drive_re, drive_im = drive[rows, lanes_of(q)], drive[rows, lanes_of(q, half)]
        before = pl.ds(batch * padded + start + (CHUNKS if reverse else 0), 2 * CHUNKS)
        prior_re, prior_im = states[before, lanes_of(q)], states[before, lanes_of(q, half)]
        dec_re, dec_im, inj_re, inj_im = more[q]
        out_re, out_im = [], []
        for j in (0, 1):
            part = slice(j * CHUNKS, (j + 1) * CHUNKS)
            adj_re, adj_im = found[j]
            keep = keep_of(meta, batch, base, first + j, reverse)
            kept_re, kept_im = keep * adj_re, keep * adj_im
            dec_re = dec_re + kept_re * prior_re[part] + kept_im * prior_im[part]
            dec_im = dec_im + kept_im * prior_re[part] - kept_re * prior_im[part]
            inj_re = inj_re + adj_re * drive_re[part] + adj_im * drive_im[part]
            inj_im = inj_im + adj_im * drive_re[part] - adj_re * drive_im[part]
            out_re.append(inj[q][0] * adj_re + inj[q][1] * adj_im)
            out_im.append(inj[q][0] * adj_im - inj[q][1] * adj_re)
        grad_proj[rows, lanes_of(q)] = jnp.concatenate(out_re, axis=0).astype(bf16)
        grad_proj[rows, lanes_of(q, half)] = jnp.concatenate(out_im, axis=0).astype(bf16)
        more[q] = (dec_re, dec_im, inj_re, inj_im)
        return tuple(more)

    _, sums = scan(
        meta, source, None, coef_tiles(dec, groups), batches, span, groups,
        not reverse, not reverse, init, ((zero,) * 4,) * groups, visit,
    )
    small[...] = jnp.zeros_like(small)
    for q in range(groups):
        for kind in range(4):
            small[kind : kind + 1, lanes_of(q)] = jnp.sum(sums[q][kind], axis=0, keepdims=True)
    small[4:5, :] = grad_d[...]
    grad_u[...] = dot(grad_proj[...], b_proj[layer], (1, 1))
    skip = norms[layer + 4 : layer + 5, :]
    plain, times_normed = [], []
    for batch in range(batches):
        average = norm[batch : batch + 1, :]
        scale = norm[batches + batch : batches + batch + 1, :]

        def body(start, carry, batch=batch, average=average, scale=scale):
            rows = pl.ds(batch * span + start, ROWS)
            value = grad_u[rows, :] + grad_mixed[rows, :] * skip
            grad_u[rows, :] = value
            normed = (hidden[rows, :].astype(f32) - average) * scale
            return carry[0] + fold(value), carry[1] + fold(value * normed)

        zero_sum = jnp.zeros((CHUNKS, grad_u.shape[1]), f32)
        one, two = row_loop(span, body, (zero_sum, zero_sum))
        plain.append(one)
        times_normed.append(two)
    add_sums(stats, batches, (plain, times_normed))


def backward_finish_last(cfg, *refs):
    ins, before, (grad_proj, grad_u, sums) = refs[:-4], refs[-4], refs[-3:]
    sums[...] = jnp.zeros_like(sums)
    sums[2 * CHUNKS :, :] = before[...]
    backward_finish(
        cfg, *ins, grad_proj, grad_u, sums.at[pl.ds(0, CHUNKS)], sums.at[pl.ds(CHUNKS, CHUNKS)]
    )


def norm_backward(cfg, stats, grad_out, grad_u, hidden, norm, norms, store, shared):
    layer, reverse, batches, span, groups, tokens, count = cfg
    sums = sum(part[...] for part in stats)
    shared[0:1, :] = jnp.sum(sums[batches:], axis=0, keepdims=True)
    shared[1:2, :] = jnp.sum(sums[:batches], axis=0, keepdims=True)
    gain_now = norms[layer : layer + 1, :]
    for batch in range(batches):
        average = norm[batch : batch + 1, :]
        scale = norm[batches + batch : batches + batch + 1, :]
        plain = gain_now * sums[batch : batch + 1] / tokens
        slanted = gain_now * sums[batches + batch : batches + batch + 1] / tokens

        def body(start, carry, batch=batch, average=average, scale=scale, plain=plain, slanted=slanted):
            rows = pl.ds(batch * span + start, ROWS)
            normed = (hidden[rows, :].astype(f32) - average) * scale
            value = grad_out[rows, :].astype(f32) + scale * (
                grad_u[rows, :] * gain_now - plain - normed * slanted
            )
            store(rows, value)
            return carry

        row_loop(span, body)


def between_layers(
    cfg, lower, place, stats, upper_out, upper_u, upper_hidden, upper_norm, norms,
    disc, u, c_proj, w_gate, states_low, act, sig, slope,
    grad_out, shared, grad_gate, grad_mixed, grad_low, source, prefix, total, grad_d, wide,
):
    def store(rows, value):
        grad_out[rows, :] = value

    norm_backward(cfg, stats, upper_out, upper_u, upper_hidden, upper_norm, norms, store, shared)
    meta = place_documents(lower, place)
    backward_start(
        lower, meta, grad_out, disc, u, c_proj, w_gate, states_low, act, sig, slope,
        grad_gate, grad_mixed, grad_low, source, prefix, total, grad_d, wide,
    )


def last_step(cfg, stats, grad_out, grad_u, hidden, norm, norms, target, shared, ordered):
    layer, reverse, batches, span, groups, tokens, count = cfg
    planes = target.shape[1] // LANES

    def store(rows, value):
        for plane in range(planes):
            ordered[plane, rows, :] = value[:, lanes_of(plane)]

    norm_backward(cfg, stats, grad_out, grad_u, hidden, norm, norms, store, shared)
    steps = span // CHUNKS
    for batch in range(batches):
        for chunk in range(CHUNKS):
            at = batch * span
            for plane in range(planes):
                target[at + chunk * steps : at + (chunk + 1) * steps, lanes_of(plane)] = ordered[
                    plane, pl.ds(at + chunk, steps, stride=CHUNKS), :
                ]


def half_weights(core, refs, own, sent):
    for target, half in ((own, core), (sent, 1 - core)):
        at = 0
        for left, right in refs:
            rows = left.shape[1] // 2
            cols = pl.ds(pl.multiple_of(half * rows, LANES), rows)
            target[at : at + rows, :] = dot(left[:, cols], right[...], (0, 0))
            at += rows


def all_weights(here, act, grad_gate, states_low, grad_low, grad_proj, u, own, sent):
    refs = ((act, grad_gate), (states_low, grad_low), (grad_proj, u))
    half_weights(lax.rem(here[0], 2), refs, own, sent)


def gate_weights(here, act, grad_gate, states_low, grad_low, own, sent):
    half_weights(lax.rem(here[0], 2), ((act, grad_gate), (states_low, grad_low)), own, sent)


def input_weights(here, grad_proj, u, own, sent):
    half_weights(lax.rem(here[0], 2), ((grad_proj, u),), own, sent)


def run(body, name, args, outs, scratch=(), scalars=1):
    vmem, smem = pl.BlockSpec(memory_space=pltpu.VMEM), pl.BlockSpec(memory_space=pltpu.SMEM)
    specs = tuple(
        jax.tree.map(lambda _, at=at: smem if at < scalars else vmem, arg)
        for at, arg in enumerate(args)
    )
    return pl.pallas_call(
        body,
        name=name,
        out_shape=tuple(jax.ShapeDtypeStruct(*out) for out in outs),
        in_specs=specs,
        out_specs=(vmem,) * len(outs),
        scratch_shapes=[pltpu.VMEM(*entry) for entry in scratch],
        compiler_params=pltpu.CompilerParams(vmem_limit_bytes=VMEM_LIMIT),
    )(*args)


def put_in_place(layer, here, halves, outs, before, pieces=1):
    width, states = outs[0][0][1], outs[1][0][1]
    rows_w, rows_c = width // 2, states // 2
    vmem, count = pl.BlockSpec(memory_space=pltpu.VMEM), len(halves)

    def half(step, here):
        core = lax.rem(here[0], 2)
        spots = [1 - core if other else core for other, _ in halves]
        return spots[0] if count == 1 else jnp.where(step == 0, *spots)

    blocks = (
        pl.BlockSpec((1, rows_w, width), lambda i, here: (layer, half(i, here), 0)),
        pl.BlockSpec((1, rows_c, width), lambda i, here: (layer, half(i, here), 0)),
        pl.BlockSpec((1, width, rows_c), lambda i, here: (layer, 0, half(i, here))),
    )

    def body(here, *refs):
        grad_w, grad_c, grad_b = refs[-3:]
        for now in range(count):

            @pl.when(pl.program_id(0) == now)
            def _(source=refs[now]):
                gates, inputs = (rows_w + rows_c) // pieces, rows_c // pieces
                columns = []
                for piece in range(pieces):
                    at, row = piece * (gates + inputs), piece * gates
                    turn = min(max(rows_w - row, 0), gates)
                    if turn:
                        grad_w[0, row : row + turn, :] = source[at : at + turn, :]
                    if turn < gates:
                        to = row + turn - rows_w
                        grad_c[0, to : to + gates - turn, :] = source[at + turn : at + gates, :]
                    columns.append(source[at + gates : at + gates + inputs, :])
                grad_b[0] = jnp.concatenate(columns, axis=0).T

    return pl.pallas_call(
        body,
        name="put_in_place",
        out_shape=tuple(jax.ShapeDtypeStruct(*out) for out in outs),
        grid_spec=pltpu.PrefetchScalarGridSpec(
            num_scalar_prefetch=1,
            grid=(count,),
            in_specs=[vmem] * count + [pl.BlockSpec(memory_space=pl.ANY)] * len(before),
            out_specs=blocks,
        ),
        input_output_aliases={1 + count + i: i for i in range(len(before))},
        compiler_params=pltpu.CompilerParams(vmem_limit_bytes=VMEM_LIMIT),
    )(here, *(rows for _, rows in halves), *before)


def axis_parts():
    count, depth = lax.axis_size("seq"), lax.axis_size("dp")
    return (("seq", 2, 1, count), ("seq", count // 2, 2, count), ("dp", depth, 1, depth))


def shifted(value, part, away):
    name, size, stride, count = part
    pairs = []
    for i in range(count):
        place = (i // stride) % size
        pairs.append((i, i + ((place + away) % size - place) * stride))
    return lax.ppermute(value, name, pairs)


def add_by_shifts(value, parts, *earlier):
    for number, part in enumerate(parts):
        if number:
            value = sum(terms[1:], terms[0])
        if number == len(parts) - 1:
            value, *earlier = lax.optimization_barrier((value, *earlier))
        terms = [value] + [shifted(value, part, away) for away in range(1, part[1])]
    return terms, *earlier


def bits_of(size, stride=1):
    bits = []
    while size > 1:
        bits.append(stride)
        size, stride = size // 2, stride * 2
    return bits


def plane_bits():
    chip_bits = bits_of(lax.axis_size("seq") // 2, 2)
    middle = (len(chip_bits) + 1) // 2
    inner, outer = chip_bits[:middle], chip_bits[middle:]
    return list(zip(inner + outer, outer + inner))


def swap(value, axis, bit):
    return lax.ppermute(value, axis, [(i, i ^ bit) for i in range(lax.axis_size(axis))])


def bit_at(here, axis, bit):
    return lax.rem(lax.div(here[0 if axis == "seq" else 1], bit), 2)


def rows_at(half, rows):
    return pl.ds(pl.multiple_of(half * rows, CHUNKS), rows)


def fold_cores(bits, here, *refs):
    terms, targets = refs[:-4], refs[-4:]
    rows, cols = targets[0].shape
    for side in (0, 1):
        kept, sent = targets[2 * side : 2 * side + 2]
        where = slice(side * cols, (side + 1) * cols)
        bit = bit_at(here, "seq", bits[side])
        for half in (0, 1):

            @pl.when(bit == half)
            def _(half=half, kept=kept, sent=sent, where=where):
                start = 0
                for own, found in zip(terms[0::2], terms[1::2]):
                    for part, target in ((half, kept), (1 - half, sent)):
                        low = max(start, part * rows)
                        high = min(start + own.shape[0], (part + 1) * rows)
                        if low < high:
                            source = slice(low - start, high - start)
                            target[low - part * rows : high - part * rows, :] = (
                                own[source, where] + found[source, where]
                            )
                    start += own.shape[0]


def fold_sides(bits, here, *refs):
    targets, blocks = refs[-4:], refs[:-4]
    for side in (0, 1):
        kept, sent = targets[2 * side : 2 * side + 2]
        half, start = bit_at(here, "seq", bits[side]), 0
        for at in range(0, len(blocks), 4):
            own, found = blocks[at + 2 * side : at + 2 * side + 2]
            rows = own.shape[0] // 2
            to = slice(start, start + rows)
            kept[to, :] = own[rows_at(half, rows), :] + found[rows_at(half, rows), :]
            sent[to, :] = own[rows_at(1 - half, rows), :] + found[rows_at(1 - half, rows), :]
            start += rows


def fold_join(bit, here, left, found_left, right, found_right, kept, sent):
    rows, cols = kept.shape[0], left.shape[1]
    half = bit_at(here, "dp", bit)
    for side, (own, found) in enumerate(((left, found_left), (right, found_right))):
        where = slice(side * cols, (side + 1) * cols)
        kept[:, where] = own[rows_at(half, rows), :] + found[rows_at(half, rows), :]
        sent[:, where] = own[rows_at(1 - half, rows), :] + found[rows_at(1 - half, rows), :]


def fold_depth(bit, here, own, found, kept, sent):
    half, rows = bit_at(here, "dp", bit), kept.shape[0]
    kept[...] = own[rows_at(half, rows), :] + found[rows_at(half, rows), :]
    sent[...] = own[rows_at(1 - half, rows), :] + found[rows_at(1 - half, rows), :]


def add_two(own, found, out):
    out[...] = own[...] + found[...]


def unfold(bit, here, own, found, out):
    half, rows = bit_at(here, "dp", bit), own.shape[0]
    out[rows_at(half, rows), :] = own[...]
    out[rows_at(1 - half, rows), :] = found[...]


def unfold_split(bit, here, own, found, left, right):
    half, rows, cols = bit_at(here, "dp", bit), own.shape[0], left.shape[1]
    for side, out in enumerate((left, right)):
        where = slice(side * cols, (side + 1) * cols)
        out[rows_at(half, rows), :] = own[:, where]
        out[rows_at(1 - half, rows), :] = found[:, where]


def unfold_sides(bits, joined, here, *refs):
    for side in (0, 1):
        own, found = refs[2 * side : 2 * side + 2]
        half, (rows, cols) = bit_at(here, "seq", bits[side]), own.shape
        out = refs[4] if joined else refs[4 + side]
        where = slice(side * cols, (side + 1) * cols) if joined else slice(0, cols)
        out[rows_at(half, rows), where] = own[...]
        out[rows_at(1 - half, rows), where] = found[...]


def link_call(body, here, args, shapes):
    name = body.func.__name__
    return run(body, name, (here, *args), tuple((shape, f32) for shape in shapes))


class LinkSum:
    def __init__(self, here, terms):
        self.here, self.plane = here, plane_bits()
        self.depth = bits_of(lax.axis_size("dp"))
        rows = sum(term.shape[0] for term in terms[::2])
        self.shape = (rows // 2, terms[0].shape[1] // 2)
        self.parts = link_call(
            functools.partial(fold_cores, self.plane[0]), here, terms, (self.shape,) * 4
        )

    def swap_plane(self, stage):
        (left, right), pieces = self.plane[stage], self.parts
        self.parts = (
            pieces[0], swap(pieces[1], "seq", left), pieces[2], swap(pieces[3], "seq", right)
        )

    def down_plane(self, stage, *others):
        parts, rows, cols = list(self.parts), *self.shape
        for other in others:
            parts += other.parts
            rows += other.shape[0]
        self.shape = (rows // 2, cols)
        body = functools.partial(fold_sides, self.plane[stage])
        self.parts = link_call(body, self.here, parts, (self.shape,) * 4)

    def down_join(self):
        rows, cols = self.shape
        self.shape = (rows // 2, 2 * cols)
        body = functools.partial(fold_join, self.depth[0])
        self.parts = link_call(body, self.here, self.parts, (self.shape,) * 2)

    def swap_depth(self, stage):
        self.parts = (self.parts[0], swap(self.parts[1], "dp", self.depth[stage]))

    def down_depth(self, stage):
        rows, cols = self.shape
        self.shape = (rows // 2, cols)
        body = functools.partial(fold_depth, self.depth[stage])
        self.parts = link_call(body, self.here, self.parts, (self.shape,) * 2)

    def middle(self):
        (value,) = run(add_two, "add_two", self.parts, ((self.shape, f32),), scalars=0)
        self.parts = (value, value)

    def up_depth(self, stage):
        rows, cols = self.shape
        self.shape = (rows * 2, cols)
        body = functools.partial(unfold, self.depth[stage])
        (value,) = link_call(body, self.here, self.parts, (self.shape,))
        self.parts = (value, value)

    def up_split(self):
        rows, cols = self.shape
        self.shape = (rows * 2, cols // 2)
        body = functools.partial(unfold_split, self.depth[0])
        left, right = link_call(body, self.here, self.parts, (self.shape,) * 2)
        self.parts = (left, left, right, right)

    def up_plane(self, stage):
        rows, cols = self.shape
        if stage:
            self.shape = (rows * 2, cols)
            body = functools.partial(unfold_sides, self.plane[stage], False)
            left, right = link_call(body, self.here, self.parts, (self.shape,) * 2)
            self.parts = (left, left, right, right)
        else:
            self.shape = (rows * 2, cols * 2)
            body = functools.partial(unfold_sides, self.plane[stage], True)
            self.parts = link_call(body, self.here, self.parts, (self.shape,))

    def after(self, *values):
        self.parts, values = lax.optimization_barrier((self.parts, values))
        return values

    def to_depth(self):
        for stage in range(2, len(self.plane)):
            self.swap_plane(stage - 1)
            self.down_plane(stage)
        self.swap_plane(len(self.plane) - 1)

    def scatter_depth(self):
        for stage in range(len(self.depth) - 1):
            if stage:
                self.down_depth(stage)
            self.swap_depth(stage)

    def swap_whole(self):
        self.parts = (self.parts[0], swap(self.parts[0], "dp", self.depth[-1]))

    def gather_depth(self):
        for stage in range(len(self.depth) - 2, 0, -1):
            self.swap_depth(stage)
            self.up_depth(stage)
        self.swap_depth(0)


def wait_for(*things):
    sums = [thing for thing in things if isinstance(thing, LinkSum)]
    values = [thing for thing in things if not isinstance(thing, LinkSum)]
    parts, values = lax.optimization_barrier(([entry.parts for entry in sums], values))
    for entry, part in zip(sums, parts):
        entry.parts = part
    return values


def discretize(lam_re, lam_im, log_step):
    step_size = jnp.exp(log_step)
    decay_abs = jnp.exp(lam_re * step_size)
    rotation = lam_im * step_size
    dec_re = decay_abs * jnp.cos(rotation)
    dec_im = decay_abs * jnp.sin(rotation)
    denom_sq = lam_re * lam_re + lam_im * lam_im
    inj_re = ((dec_re - 1.0) * lam_re + dec_im * lam_im) / denom_sq
    inj_im = (dec_im * lam_re - (dec_re - 1.0) * lam_im) / denom_sq
    return (dec_re, dec_im, inj_re, inj_im)


def per_device(
    block_in, cotangent, doc_lengths, norm_gain, norm_shift, log_step, lam_re, lam_im,
    b_proj, c_proj, d_skip, w_gate,
):
    batches, seqs, span, width = block_in.shape
    assert seqs == 1 and span % (4 * CHUNKS) == 0 and span & (span - 1) == 0
    half = lam_re.shape[1]
    groups = half // LANES
    rows = batches * span
    count = lax.axis_size("seq")
    tokens = float(seqs * lax.axis_size("dp") * span * count)
    here = jnp.stack([lax.axis_index("seq"), lax.axis_index("dp")]).astype(jnp.int32)
    place = jnp.concatenate([here] + [doc_lengths[batch, 0] for batch in range(batches)])
    place, block_in = lax.optimization_barrier((place, block_in))
    here = place
    disc = discretize(lam_re, lam_im, log_step)

    x = block_in.reshape(rows, width)
    cot = cotangent.reshape(rows, width)
    lower = (0, False, batches, span, groups, tokens, count)
    upper = (1, True, batches, span, groups, tokens, count)
    part = functools.partial

    flat, low = ((rows, width), f32), ((rows, width), bf16)
    wide, wide_low = ((rows, 2 * half), f32), ((rows, 2 * half), bf16)
    padded = ((batches * (span + CHUNKS), 2 * half), f32)
    sums = ((2 * batches, width), f32)
    prefix = ((2, batches * CHUNKS, 2 * half), f32)
    total = ((batches, 2 * half), f32)
    line, shared = ((1, width), f32), ((2, width), f32)
    small = ((8, width), f32)

    def gather_row(value, reverse):
        both = jnp.concatenate([value, swap(value, "seq", 1)], axis=0)
        chips = count // 2
        return [both] + [
            shifted(both, plane, chips - away if reverse else away) for away in range(1, chips)
        ]

    (stats,) = run(part(first_sums, batches, span), "first_sums", (x,), (sums,), scalars=0)

    def order(value, inverse):
        body = part(order_rows, batches, span, inverse)
        return run(body, "order_rows", (value,), (low,), scalars=0)[0]

    norms = jnp.concatenate([norm_gain, norm_shift, d_skip], axis=0)

    def forward(cfg, hidden, stats):
        return run(
            part(enter_layer, cfg),
            "enter_layer",
            (place, stats, hidden, norms, disc, b_proj),
            (low, wide, prefix, total, sums),
        )

    links, plane, depth = axis_parts()
    stats, ordered = lax.optimization_barrier(
        (add_by_shifts(stats, (links, plane, depth))[0], order(x, False))
    )
    u0, drive0, prefix0, total0, norm0 = forward(lower, ordered, stats)
    states0, states_low0, act0, sig0, slope0, hidden1, stats = run(
        part(middle_forward, lower),
        "middle_forward",
        (place, gather_row(total0, False), prefix0, disc, drive0, u0, ordered, c_proj, norms, w_gate),
        (padded, wide_low, low, flat, flat, flat, sums),
        (flat,),
    )
    cot, stats = lax.optimization_barrier((cot, stats))
    stats, ordered_cot = lax.optimization_barrier(
        (add_by_shifts(stats, (links, plane, depth))[0], order(cot, False))
    )
    u1, drive1, prefix1, total1, norm1 = forward(upper, hidden1, stats)
    (
        result1, states1, states_low1, act1, grad_gate1, grad_mixed1, grad_low1,
        source1, prefix1, total1, grad_d1,
    ) = run(
        part(turn_around, upper),
        "turn_around",
        (
            place, gather_row(total1, True), prefix1, disc, drive1, u1, hidden1, c_proj, norms, w_gate,
            ordered_cot,
        ),
        (low, padded, wide_low, low, low, flat, low, wide, prefix, total, line),
        (flat, flat, flat),
    )

    def halves(length):
        return (((length // 2, width), f32),) * 2

    grad_proj1, grad_u1, stats, small1 = run(
        part(backward_finish, upper),
        "backward_finish",
        (
            place, gather_row(total1, False), prefix1, disc, source1, drive1, states1, u1, grad_mixed1,
            grad_d1, hidden1, norm1, norms, b_proj,
        ),
        (wide_low, flat, sums, small),
    )
    sizes = (width + 2 * half, 2 * half)
    own1, sent1 = run(
        all_weights,
        "all_weights",
        (here, act1, grad_gate1, states_low1, grad_low1, grad_proj1, u1),
        halves(sum(sizes)),
    )
    stats = stats + swap(stats, "seq", 1)
    stats, sent1 = lax.optimization_barrier((stats, sent1))
    upper_sum = LinkSum(here, (own1, swap(sent1, "seq", 1)))
    stats, upper_sum.parts = add_by_shifts(stats, (plane, depth), upper_sum.parts)
    upper_sum.swap_plane(0)
    (
        grad_out0, shared1, grad_gate0, grad_mixed0, grad_low0, source0, prefix0, total0, grad_d0,
    ) = run(
        part(between_layers, upper, lower),
        "between_layers",
        (
            place, stats, ordered_cot, grad_u1, hidden1, norm1, norms,
            disc, u0, c_proj, w_gate, states_low0, act0, sig0, slope0,
        ),
        (flat, shared, low, flat, low, wide, prefix, total, line),
        (flat,),
    )
    (total0,) = upper_sum.after(total0)
    upper_sum.down_plane(1)
    (total0,) = upper_sum.after(total0)
    upper_sum.to_depth()
    ends, grad_gate0 = wait_for(upper_sum, gather_row(total0, True), grad_gate0)
    upper_sum.down_join()
    ends, grad_gate0 = wait_for(upper_sum, ends, grad_gate0)
    upper_sum.scatter_depth()
    own_gates, sent_gates = run(
        gate_weights, "gate_weights", (here, act0, grad_gate0, states_low0, grad_low0),
        halves(sizes[0]),
    )
    own_gates, ends = lax.optimization_barrier((own_gates, ends))
    grad_proj0, grad_u0, last_sums = run(
        part(backward_finish_last, lower),
        "backward_finish",
        (
            place, ends, prefix0, disc, source0, drive0, states0, u0, grad_mixed0, grad_d0,
            ordered, norm0, norms, b_proj, small1,
        ),
        (wide_low, flat, ((3 * CHUNKS, width), f32)),
    )
    lower_sum = LinkSum(here, (own_gates, swap(sent_gates, "seq", 1)))
    (grad_proj0,) = wait_for(upper_sum, lower_sum, grad_proj0)
    own_inputs, sent_inputs = run(
        input_weights, "input_weights", (here, grad_proj0, u0), halves(sizes[1])
    )
    inputs_sum = LinkSum(here, (own_inputs, swap(sent_inputs, "seq", 1)))
    upper_sum.middle()
    upper_sum.swap_whole()
    lower_sum.swap_plane(0)
    inputs_sum.swap_plane(0)
    wait_for(upper_sum, lower_sum, inputs_sum)

    lower_sum.down_plane(1, inputs_sum)
    upper_sum.middle()
    upper_sum.gather_depth()
    lower_sum.to_depth()
    wait_for(upper_sum, lower_sum)

    lower_sum.down_join()
    upper_sum.up_split()
    lower_sum.scatter_depth()
    upper_sum.swap_plane(len(upper_sum.plane) - 1)
    wait_for(upper_sum, lower_sum)

    lower_sum.middle()
    lower_sum.swap_whole()
    for stage in range(len(upper_sum.plane) - 1, 0, -1):
        upper_sum.up_plane(stage)
        upper_sum.swap_plane(stage - 1)
    (last_sums,) = wait_for(upper_sum, lower_sum, last_sums)

    lower_sum.middle()
    (last_sums,) = lower_sum.after(last_sums)
    lower_sum.gather_depth()
    last_sums = last_sums + swap(last_sums, "seq", 1)
    last_terms = [last_sums] + [shifted(last_sums, plane, away) for away in range(1, plane[1])]
    last_terms = wait_for(lower_sum, *last_terms)

    lower_sum.up_split()
    wait_for(upper_sum, lower_sum)
    lower_sum.swap_plane(len(lower_sum.plane) - 1)
    upper_sum.up_plane(0)
    own1, result1 = lax.optimization_barrier((upper_sum.parts[0], result1))
    other1 = swap(own1, "seq", 1)
    block_out = order(result1, True)
    final = (((2, width, width), f32), ((2, 2 * half, width), f32), ((2, width, 2 * half), f32))
    placed = put_in_place(1, here, ((False, own1), (True, other1)), final, ())
    summed = sum(last_terms)
    for bit in bits_of(lax.axis_size("dp")):
        summed = summed + swap(summed, "dp", bit)
    summed, block_out = wait_for(lower_sum, summed, block_out)

    for stage in range(len(lower_sum.plane) - 1, 0, -1):
        lower_sum.up_plane(stage)
        if stage == 1:
            (summed,) = lower_sum.after(summed)
        lower_sum.swap_plane(stage - 1)
    grad_input, shared0 = run(
        part(last_step, lower),
        "last_step",
        ((summed[: 2 * batches],), grad_out0, grad_u0, ordered, norm0, norms),
        (flat, shared),
        (((width // LANES, rows, LANES), f32),),
        scalars=0,
    )
    small_sum = summed[CHUNKS:].reshape(2, CHUNKS, width)
    _, pullback = jax.vjp(discretize, lam_re, lam_im, log_step)
    grad_lr, grad_li, grad_ls = pullback(tuple(small_sum[:, kind, :half] for kind in range(4)))
    both = jnp.stack([shared0, shared1])
    grad_gain, grad_shift = both[:, 0], both[:, 1]
    early = [swap(lower_sum.parts[at], "seq", 1) for at in (0, 2)]
    grad_skip = small_sum[:, 4]
    grad_input, grad_lr, grad_li, grad_ls, grad_gain, grad_shift, grad_skip, *rest = wait_for(
        lower_sum, grad_input, grad_lr, grad_li, grad_ls, grad_gain, grad_shift, grad_skip,
        *early, *placed,
    )
    early, placed = rest[:2], rest[2:]

    late = [swap(lower_sum.parts[at], "seq", 1) for at in (1, 3)]
    other_sum = copy.copy(lower_sum)
    other_sum.parts = (early[0], late[0], early[1], late[1])
    lower_sum.up_plane(0)
    placed = put_in_place(0, here, ((False, lower_sum.parts[0]),), final, placed, 4)
    other_sum.up_plane(0)
    grad_w, grad_c, grad_b = put_in_place(
        0, here, ((True, other_sum.parts[0]),), final, placed, 4
    )
    shape = block_in.shape
    return (
        block_out.reshape(shape), grad_input.reshape(shape), grad_gain, grad_shift,
        grad_ls, grad_lr, grad_li, grad_b, grad_c, grad_skip, grad_w,
    )


def solution(mesh):
    split = P(None, "dp", "seq", None)
    return jax.shard_map(
        per_device,
        mesh=mesh,
        in_specs=(split, split, P(None, "dp", None)) + (P(),) * 9,
        out_specs=(split, split) + (P(),) * 9,
        check_vma=False,
    )
```

```python
import copy
import functools

import jax
import jax.numpy as jnp
from jax import lax
from jax.experimental import pallas as pl
from jax.experimental.pallas import tpu as pltpu
from jax.sharding import PartitionSpec as P

f32, bf16 = jnp.float32, jnp.bfloat16
epsilon = 1e-05
tanh_scale = 0.7978845608028654
cubic_term = 0.044715
LANES = 128
CHUNKS = 8
ROWS = 32
VMEM_LIMIT = 16 * 1024 * 1024


def dot(left, right, contract=(1, 0)):
    return lax.dot_general(
        left, right, (((contract[0],), (contract[1],)), ((), ())), preferred_element_type=f32
    )


def reorder(span, inverse):
    shape = (span, span)
    kept, moved = (1, 0) if inverse else (0, 1)
    row = lax.broadcasted_iota(jnp.int32, shape, kept)
    position = lax.broadcasted_iota(jnp.int32, shape, moved)
    source = (row & (CHUNKS - 1)) * (span // CHUNKS) + (row >> 3)
    return jnp.where(position == source, 1.0, 0.0).astype(bf16)


def row_loop(count, body, init=0, step=ROWS):
    def one(index, carry):
        return body(pl.multiple_of(index * step, step), carry)

    return lax.fori_loop(0, count // step, one, init, unroll=2)


def documents(here, batches, span, count):
    mine = here[0]
    first = mine * span
    out = []
    for batch in range(batches):
        begins, ends, so_far = [], [], 0
        docs = (here.shape[0] - 2) // batches
        for doc in range(docs):
            begins.append(so_far)
            so_far = so_far + here[2 + batch * docs + doc]
            ends.append(so_far)
        before, after = 0, 2 * count * span
        for begin, end in zip(begins, ends):
            before = jnp.maximum(before, jnp.where(begin < first, begin, 0))
            after = jnp.minimum(after, jnp.where(end > first + span, end, 2 * count * span))
        after = jnp.where(mine == count - 1, 0, after)
        out.append(begins + ends + [before, after, first, mine])
    return out


def place_documents(cfg, place):
    layer, reverse, batches, span, groups, tokens, count = cfg
    return documents(place, batches, span, count)


def keep_of(meta, batch, base, step, backward):
    docs = (len(meta[batch]) - 4) // 2
    off = docs if backward else 0
    late = 1 if backward else 0
    stop = base == meta[batch][off] - step - late
    for doc in range(1, docs):
        stop = jnp.logical_or(stop, base == meta[batch][off + doc] - step - late)
    return jnp.where(stop, 0.0, 1.0)


def base_positions(meta, steps):
    return meta[0][-2] + lax.broadcasted_iota(jnp.int32, (CHUNKS, LANES), 0) * steps


def lanes_of(index, half=0):
    return slice(half + index * LANES, half + (index + 1) * LANES)


def coef_tiles(value, groups):
    return [
        tuple(jnp.broadcast_to(part[:, lanes_of(q)], (CHUNKS, LANES)) for part in value)
        for q in range(groups)
    ]


def constants(disc, layer):
    dec_re, dec_im, inj_re, inj_im = (part[layer : layer + 1, :] for part in disc)
    return (dec_re, dec_im), (inj_re, inj_im)


def times(a, b):
    return (a[0] * b[0] - a[1] * b[1], a[0] * b[1] + a[1] * b[0])


def power(value, exponent):
    for _ in range(exponent.bit_length() - 1):
        value = times(value, value)
    return value


def conj(value):
    return (value[0], -value[1])


def scan(meta, source, inject, dec, batches, span, groups, reverse, masks_reverse, init, extra, visit):
    steps = span // CHUNKS
    half = groups * LANES
    base = base_positions(meta, steps)

    def pair(index, carry):
        states, more = carry
        states = list(states)
        first = steps - 2 - 2 * index if reverse else 2 * index
        start = pl.multiple_of(first * CHUNKS, 2 * CHUNKS)
        order = (1, 0) if reverse else (0, 1)
        for batch in range(batches):
            keeps = [keep_of(meta, batch, base, first + j, masks_reverse) for j in (0, 1)]
            for q in range(groups):
                rows = pl.ds(batch * span + start, 2 * CHUNKS)
                src_re = source[rows, lanes_of(q)]
                src_im = source[rows, lanes_of(q, half)]
                state = states[batch * groups + q]
                found = [None, None]
                for j in order:
                    part = (
                        src_re[j * CHUNKS : (j + 1) * CHUNKS],
                        src_im[j * CHUNKS : (j + 1) * CHUNKS],
                    )
                    push = times(inject[q], part) if inject is not None else part
                    held = times((keeps[j] * dec[q][0], keeps[j] * dec[q][1]), state)
                    state = (held[0] + push[0], held[1] + push[1])
                    found[j] = state
                states[batch * groups + q] = state
                more = visit(more, batch, q, first, start, found, (src_re, src_im))
            more = visit(more, batch, None, first, start, keeps, None)
        return tuple(states), more

    return lax.fori_loop(0, steps // 2, pair, (tuple(init), extra), unroll=8)


def zero_states(batches, groups):
    zero = jnp.zeros((CHUNKS, LANES), f32)
    return [(zero, zero)] * (batches * groups)


def local_ends(meta, source, inject, dec, batches, span, groups, reverse, prefix, total):
    ones = tuple(jnp.ones((CHUNKS, LANES), f32) for _ in range(batches))

    def visit(more, batch, q, first, start, found, src):
        if q is not None:
            return more
        return tuple(
            value * found[0] * found[1] if at == batch else value for at, value in enumerate(more)
        )

    dec_chunk = coef_tiles(power(dec, span // CHUNKS), groups)
    ends, kept = scan(
        meta, source, inject, coef_tiles(dec, groups), batches, span, groups, reverse, reverse,
        zero_states(batches, groups), ones, visit,
    )
    half = groups * LANES
    row = lax.broadcasted_iota(jnp.int32, (CHUNKS, LANES), 0)
    for batch in range(batches):
        for q in range(groups):
            end = ends[batch * groups + q]
            decay = (kept[batch] * dec_chunk[q][0], kept[batch] * dec_chunk[q][1])
            for shift in (1, 2, 4):
                turn = CHUNKS - shift if reverse else shift
                valid = row < CHUNKS - shift if reverse else row >= shift
                before = [pltpu.roll(value, turn, 0) for value in (*end, *decay)]
                from_before = times(decay, (before[0], before[1]))
                end = (
                    end[0] + jnp.where(valid, from_before[0], 0.0),
                    end[1] + jnp.where(valid, from_before[1], 0.0),
                )
                longer = times(decay, (before[2], before[3]))
                decay = (
                    jnp.where(valid, longer[0], decay[0]),
                    jnp.where(valid, longer[1], decay[1]),
                )
            rows = slice(batch * CHUNKS, (batch + 1) * CHUNKS)
            prefix[0, rows, lanes_of(q)] = end[0]
            prefix[0, rows, lanes_of(q, half)] = end[1]
            prefix[1, rows, lanes_of(q)] = decay[0]
            prefix[1, rows, lanes_of(q, half)] = decay[1]
            last = 0 if reverse else CHUNKS - 1
            total[batch : batch + 1, lanes_of(q)] = end[0][last : last + 1]
            total[batch : batch + 1, lanes_of(q, half)] = end[1][last : last + 1]


def chunk_carries(meta, gathered, dec, prefix, batches, span, groups, reverse):
    half = groups * LANES
    dec_span = power(dec, span)
    row = lax.broadcasted_iota(jnp.int32, (CHUNKS, LANES), 0)
    mine = meta[0][-1]
    core = lax.rem(mine, 2)
    out = []
    for batch in range(batches):
        enter = (jnp.zeros((1, half), f32), jnp.zeros((1, half), f32))
        for away in range(len(gathered) - 1, -1, -1):
            for kind in (1, 0) if reverse else (0, 1):
                if away == 0 and kind == (0 if reverse else 1):
                    continue
                if reverse:
                    other = mine - core + 2 * away + kind
                    reaches = meta[batch][-3] > other * span
                else:
                    other = mine - core - 2 * away + kind
                    reaches = meta[batch][-4] < (other + 1) * span
                same = gathered[away][batch : batch + 1, :]
                unlike = gathered[away][batches + batch : batches + batch + 1, :]
                value = jnp.where(reaches, jnp.where(core == kind, same, unlike), 0.0)
                moved = times(dec_span, enter)
                after = (moved[0] + value[:, :half], moved[1] + value[:, half:])
                if away == 0:
                    after = tuple(jnp.where(core == kind, old, new) for old, new in zip(enter, after))
                enter = after
        rows = slice(batch * CHUNKS, (batch + 1) * CHUNKS)
        for q in range(groups):
            own = tuple(jnp.broadcast_to(part[:, lanes_of(q)], (CHUNKS, LANES)) for part in enter)
            end = (prefix[0, rows, lanes_of(q)], prefix[0, rows, lanes_of(q, half)])
            decay = (prefix[1, rows, lanes_of(q)], prefix[1, rows, lanes_of(q, half)])
            moved = times(decay, own)
            turn, first = (CHUNKS - 1, CHUNKS - 1) if reverse else (1, 0)
            out.append(
                tuple(
                    jnp.where(row == first, own[i], pltpu.roll(end[i] + moved[i], turn, 0))
                    for i in (0, 1)
                )
            )
    return out


def add_sums(target, batches, sums):
    for kind, per_batch in enumerate(sums):
        for batch in range(batches):
            target[kind * batches + batch : kind * batches + batch + 1, :] = jnp.sum(
                per_batch[batch], axis=0, keepdims=True
            )


def fold(value):
    return sum(value[i : i + CHUNKS] for i in range(CHUNKS, value.shape[0], CHUNKS)) + value[:CHUNKS]


def order_rows(batches, span, inverse, x, out):
    turn = reorder(span, inverse)
    for batch in range(batches):
        rows = slice(batch * span, (batch + 1) * span)
        out[rows, :] = dot(turn, x[rows, :]).astype(bf16)


def first_sums(batches, span, x, stats):
    width = x.shape[1]
    sums, squares = [], []
    for batch in range(batches):

        def body(start, carry, batch=batch):
            value = x[pl.ds(batch * span + start, ROWS), :].astype(f32)
            return carry[0] + fold(value), carry[1] + fold(value * value)

        zero = jnp.zeros((CHUNKS, width), f32)
        one, two = row_loop(span, body, (zero, zero))
        sums.append(one)
        squares.append(two)
    add_sums(stats, batches, (sums, squares))


def enter_layer(
    cfg, place, stats, hidden, norms, disc, b_proj, u, drive, prefix, total, norm
):
    layer, reverse, batches, span, groups, tokens, count = cfg
    sums = sum(part[...] for part in stats)
    average = sums[:batches] / tokens
    spread = sums[batches:] / tokens - average * average
    scale = lax.rsqrt(spread + epsilon)
    norm[:batches, :] = average
    norm[batches:, :] = scale
    gain_now, shift_now = norms[layer : layer + 1, :], norms[layer + 2 : layer + 3, :]
    for batch in range(batches):

        def body(start, carry, batch=batch):
            rows = pl.ds(batch * span + start, ROWS)
            normed = (hidden[rows, :].astype(f32) - average[batch : batch + 1]) * scale[
                batch : batch + 1
            ]
            u[rows, :] = (normed * gain_now + shift_now).astype(bf16)
            return carry

        row_loop(span, body)
    drive[...] = dot(u[...], b_proj[layer])
    meta = place_documents(cfg, place)
    dec, inj = constants(disc, layer)
    local_ends(
        meta, drive, coef_tiles(inj, groups), dec, batches, span, groups, reverse, prefix, total
    )


def finish_states(cfg, meta, ends, prefix, disc, drive, states, states_low):
    layer, reverse, batches, span, groups, tokens, count = cfg
    half = groups * LANES
    padded = span + CHUNKS
    dec, inj = constants(disc, layer)
    init = chunk_carries(meta, ends, dec, prefix, batches, span, groups, reverse)
    for batch in range(batches):
        edge = batch * padded + (span if reverse else 0)
        for q in range(groups):
            states[edge : edge + CHUNKS, lanes_of(q)] = init[batch * groups + q][0]
            states[edge : edge + CHUNKS, lanes_of(q, half)] = init[batch * groups + q][1]

    def visit(more, batch, q, first, start, found, src):
        if q is not None:
            for part, off in ((0, 0), (1, half)):
                both = jnp.concatenate([found[0][part], found[1][part]], axis=0)
                at = batch * padded + (0 if reverse else CHUNKS)
                states[pl.ds(at + start, 2 * CHUNKS), lanes_of(q, off)] = both
                states_low[pl.ds(batch * span + start, 2 * CHUNKS), lanes_of(q, off)] = both.astype(
                    bf16
                )
        return more

    scan(
        meta, drive, coef_tiles(inj, groups), coef_tiles(dec, groups), batches, span, groups,
        reverse, reverse, init, 0, visit,
    )


def forward_finish(
    cfg, meta, ends, prefix, disc, drive, u, hidden, c_proj, norms, w_gate,
    states, states_low, act, sig, slope, result, wide, emit,
):
    layer, reverse, batches, span, groups, tokens, count = cfg
    finish_states(cfg, meta, ends, prefix, disc, drive, states, states_low)
    wide[...] = dot(states_low[...], c_proj[layer])
    skip = norms[layer + 4 : layer + 5, :]

    def body(start, carry):
        rows = pl.ds(start, ROWS)
        mixed = wide[rows, :] + skip * u[rows, :].astype(f32)
        square = mixed * mixed
        th = jnp.tanh(tanh_scale * (mixed + cubic_term * square * mixed))
        half_one = 0.5 * (1.0 + th)
        act[rows, :] = (mixed * half_one).astype(bf16)
        slope[rows, :] = half_one + 0.5 * mixed * (1.0 - th * th) * tanh_scale * (
            1.0 + 3.0 * cubic_term * square
        )
        return carry

    row_loop(batches * span, body)
    wide[...] = dot(act[...], w_gate[layer])
    sums, squares = [], []
    for batch in range(batches):

        def gate(start, carry, batch=batch):
            rows = pl.ds(batch * span + start, ROWS)
            sig_now = 0.5 + 0.5 * jnp.tanh(0.5 * wide[rows, :])
            sig[rows, :] = sig_now
            value = hidden[rows, :].astype(f32) + act[rows, :].astype(f32) * sig_now
            result[rows, :] = value.astype(result.dtype)
            if emit is None:
                return carry
            return carry[0] + fold(value), carry[1] + fold(value * value)

        zero = jnp.zeros((CHUNKS, wide.shape[1]), f32)
        one, two = row_loop(span, gate, (zero, zero))
        sums.append(one)
        squares.append(two)
    if emit is not None:
        add_sums(emit, batches, (sums, squares))


def backward_start(
    cfg, meta, grad_out, disc, u, c_proj, w_gate, states_low, act, sig, slope,
    grad_gate, grad_mixed, grad_low, source, prefix, total, grad_d, wide,
):
    layer, reverse, batches, span, groups, tokens, count = cfg

    def body(start, carry):
        rows = pl.ds(start, ROWS)
        sig_now = sig[rows, :]
        grad_gate[rows, :] = (
            grad_out[rows, :].astype(f32) * act[rows, :].astype(f32) * sig_now * (1.0 - sig_now)
        ).astype(bf16)
        return carry

    row_loop(batches * span, body)
    wide[...] = dot(grad_gate[...], w_gate[layer], (1, 1))

    def mixed(start, carry):
        rows = pl.ds(start, ROWS)
        value = (grad_out[rows, :].astype(f32) * sig[rows, :] + wide[rows, :]) * slope[rows, :]
        grad_mixed[rows, :] = value
        grad_low[rows, :] = value.astype(bf16)
        return carry + fold(value * u[rows, :].astype(f32))

    gd = row_loop(batches * span, mixed, jnp.zeros((CHUNKS, wide.shape[1]), f32))
    grad_d[...] = jnp.sum(gd, axis=0, keepdims=True)
    source[...] = dot(grad_low[...], c_proj[layer], (1, 1))
    local_ends(
        meta, source, None, conj(constants(disc, layer)[0]), batches, span, groups, not reverse,
        prefix, total,
    )


def middle_forward(
    cfg, place, ends, prefix, disc, drive, u, hidden, c_proj, norms, w_gate,
    states, states_low, act, sig, slope, result, stats, wide,
):
    meta = place_documents(cfg, place)
    forward_finish(
        cfg, meta, ends, prefix, disc, drive, u, hidden, c_proj, norms, w_gate,
        states, states_low, act, sig, slope, result, wide, stats,
    )


def turn_around(
    cfg, place, ends, prefix, disc, drive, u, hidden, c_proj, norms, w_gate, ordered_cot,
    result, states, states_low, act, grad_gate, grad_mixed, grad_low, source,
    back_prefix, total, grad_d, sig, slope, wide,
):
    layer, reverse, batches, span, groups, tokens, count = cfg
    meta = place_documents(cfg, place)
    forward_finish(
        cfg, meta, ends, prefix, disc, drive, u, hidden, c_proj, norms, w_gate,
        states, states_low, act, sig, slope, result, wide, None,
    )
    backward_start(
        cfg, meta, ordered_cot, disc, u, c_proj, w_gate, states_low, act, sig, slope,
        grad_gate, grad_mixed, grad_low, source, back_prefix, total, grad_d, wide,
    )


def backward_finish(
    cfg, place, ends, prefix, disc, source, drive, states, u, grad_mixed, grad_d, hidden, norm,
    norms, b_proj, grad_proj, grad_u, stats, small,
):
    layer, reverse, batches, span, groups, tokens, count = cfg
    half = groups * LANES
    padded = span + CHUNKS
    steps = span // CHUNKS
    meta = place_documents(cfg, place)
    dec, inj = constants(disc, layer)
    dec = conj(dec)
    init = chunk_carries(meta, ends, dec, prefix, batches, span, groups, not reverse)
    inj = coef_tiles(inj, groups)
    base = base_positions(meta, steps)
    zero = jnp.zeros((CHUNKS, LANES), f32)

    def visit(more, batch, q, first, start, found, src):
        if q is None:
            return more
        more = list(more)
        rows = pl.ds(batch * span + start, 2 * CHUNKS)
        drive_re, drive_im = drive[rows, lanes_of(q)], drive[rows, lanes_of(q, half)]
        before = pl.ds(batch * padded + start + (CHUNKS if reverse else 0), 2 * CHUNKS)
        prior_re, prior_im = states[before, lanes_of(q)], states[before, lanes_of(q, half)]
        dec_re, dec_im, inj_re, inj_im = more[q]
        out_re, out_im = [], []
        for j in (0, 1):
            part = slice(j * CHUNKS, (j + 1) * CHUNKS)
            adj_re, adj_im = found[j]
            keep = keep_of(meta, batch, base, first + j, reverse)
            kept_re, kept_im = keep * adj_re, keep * adj_im
            dec_re = dec_re + kept_re * prior_re[part] + kept_im * prior_im[part]
            dec_im = dec_im + kept_im * prior_re[part] - kept_re * prior_im[part]
            inj_re = inj_re + adj_re * drive_re[part] + adj_im * drive_im[part]
            inj_im = inj_im + adj_im * drive_re[part] - adj_re * drive_im[part]
            out_re.append(inj[q][0] * adj_re + inj[q][1] * adj_im)
            out_im.append(inj[q][0] * adj_im - inj[q][1] * adj_re)
        grad_proj[rows, lanes_of(q)] = jnp.concatenate(out_re, axis=0).astype(bf16)
        grad_proj[rows, lanes_of(q, half)] = jnp.concatenate(out_im, axis=0).astype(bf16)
        more[q] = (dec_re, dec_im, inj_re, inj_im)
        return tuple(more)

    _, sums = scan(
        meta, source, None, coef_tiles(dec, groups), batches, span, groups,
        not reverse, not reverse, init, ((zero,) * 4,) * groups, visit,
    )
    small[...] = jnp.zeros_like(small)
    for q in range(groups):
        for kind in range(4):
            small[kind : kind + 1, lanes_of(q)] = jnp.sum(sums[q][kind], axis=0, keepdims=True)
    small[4:5, :] = grad_d[...]
    grad_u[...] = dot(grad_proj[...], b_proj[layer], (1, 1))
    skip = norms[layer + 4 : layer + 5, :]
    plain, times_normed = [], []
    for batch in range(batches):
        average = norm[batch : batch + 1, :]
        scale = norm[batches + batch : batches + batch + 1, :]

        def body(start, carry, batch=batch, average=average, scale=scale):
            rows = pl.ds(batch * span + start, ROWS)
            value = grad_u[rows, :] + grad_mixed[rows, :] * skip
            grad_u[rows, :] = value
            normed = (hidden[rows, :].astype(f32) - average) * scale
            return carry[0] + fold(value), carry[1] + fold(value * normed)

        zero_sum = jnp.zeros((CHUNKS, grad_u.shape[1]), f32)
        one, two = row_loop(span, body, (zero_sum, zero_sum))
        plain.append(one)
        times_normed.append(two)
    add_sums(stats, batches, (plain, times_normed))


def backward_finish_last(cfg, *refs):
    ins, before, (grad_proj, grad_u, sums) = refs[:-4], refs[-4], refs[-3:]
    sums[...] = jnp.zeros_like(sums)
    sums[2 * CHUNKS :, :] = before[...]
    backward_finish(
        cfg, *ins, grad_proj, grad_u, sums.at[pl.ds(0, CHUNKS)], sums.at[pl.ds(CHUNKS, CHUNKS)]
    )


def norm_backward(cfg, stats, grad_out, grad_u, hidden, norm, norms, store, shared):
    layer, reverse, batches, span, groups, tokens, count = cfg
    sums = sum(part[...] for part in stats)
    shared[0:1, :] = jnp.sum(sums[batches:], axis=0, keepdims=True)
    shared[1:2, :] = jnp.sum(sums[:batches], axis=0, keepdims=True)
    gain_now = norms[layer : layer + 1, :]
    for batch in range(batches):
        average = norm[batch : batch + 1, :]
        scale = norm[batches + batch : batches + batch + 1, :]
        plain = gain_now * sums[batch : batch + 1] / tokens
        slanted = gain_now * sums[batches + batch : batches + batch + 1] / tokens

        def body(start, carry, batch=batch, average=average, scale=scale, plain=plain, slanted=slanted):
            rows = pl.ds(batch * span + start, ROWS)
            normed = (hidden[rows, :].astype(f32) - average) * scale
            value = grad_out[rows, :].astype(f32) + scale * (
                grad_u[rows, :] * gain_now - plain - normed * slanted
            )
            store(rows, value)
            return carry

        row_loop(span, body)


def between_layers(
    cfg, lower, place, stats, upper_out, upper_u, upper_hidden, upper_norm, norms,
    disc, u, c_proj, w_gate, states_low, act, sig, slope,
    grad_out, shared, grad_gate, grad_mixed, grad_low, source, prefix, total, grad_d, wide,
):
    def store(rows, value):
        grad_out[rows, :] = value

    norm_backward(cfg, stats, upper_out, upper_u, upper_hidden, upper_norm, norms, store, shared)
    meta = place_documents(lower, place)
    backward_start(
        lower, meta, grad_out, disc, u, c_proj, w_gate, states_low, act, sig, slope,
        grad_gate, grad_mixed, grad_low, source, prefix, total, grad_d, wide,
    )


def last_step(cfg, stats, grad_out, grad_u, hidden, norm, norms, target, shared, ordered):
    layer, reverse, batches, span, groups, tokens, count = cfg
    planes = target.shape[1] // LANES

    def store(rows, value):
        for plane in range(planes):
            ordered[plane, rows, :] = value[:, lanes_of(plane)]

    norm_backward(cfg, stats, grad_out, grad_u, hidden, norm, norms, store, shared)
    steps = span // CHUNKS
    for batch in range(batches):
        for chunk in range(CHUNKS):
            at = batch * span
            for plane in range(planes):
                target[at + chunk * steps : at + (chunk + 1) * steps, lanes_of(plane)] = ordered[
                    plane, pl.ds(at + chunk, steps, stride=CHUNKS), :
                ]


def half_weights(core, refs, own, sent):
    for target, half in ((own, core), (sent, 1 - core)):
        at = 0
        for left, right in refs:
            rows = left.shape[1] // 2
            cols = pl.ds(pl.multiple_of(half * rows, LANES), rows)
            target[at : at + rows, :] = dot(left[:, cols], right[...], (0, 0))
            at += rows


def all_weights(here, act, grad_gate, states_low, grad_low, grad_proj, u, own, sent):
    refs = ((act, grad_gate), (states_low, grad_low), (grad_proj, u))
    half_weights(lax.rem(here[0], 2), refs, own, sent)


def gate_weights(here, act, grad_gate, states_low, grad_low, own, sent):
    half_weights(lax.rem(here[0], 2), ((act, grad_gate), (states_low, grad_low)), own, sent)


def input_weights(here, grad_proj, u, own, sent):
    half_weights(lax.rem(here[0], 2), ((grad_proj, u),), own, sent)


def run(body, name, args, outs, scratch=(), scalars=1):
    vmem, smem = pl.BlockSpec(memory_space=pltpu.VMEM), pl.BlockSpec(memory_space=pltpu.SMEM)
    specs = tuple(
        jax.tree.map(lambda _, at=at: smem if at < scalars else vmem, arg)
        for at, arg in enumerate(args)
    )
    return pl.pallas_call(
        body,
        name=name,
        out_shape=tuple(jax.ShapeDtypeStruct(*out) for out in outs),
        in_specs=specs,
        out_specs=(vmem,) * len(outs),
        scratch_shapes=[pltpu.VMEM(*entry) for entry in scratch],
        compiler_params=pltpu.CompilerParams(vmem_limit_bytes=VMEM_LIMIT),
    )(*args)


def put_in_place(layer, here, halves, outs, before, pieces=1):
    width, states = outs[0][0][1], outs[1][0][1]
    rows_w, rows_c = width // 2, states // 2
    vmem, count = pl.BlockSpec(memory_space=pltpu.VMEM), len(halves)

    def half(step, here):
        core = lax.rem(here[0], 2)
        spots = [1 - core if other else core for other, _ in halves]
        return spots[0] if count == 1 else jnp.where(step == 0, *spots)

    blocks = (
        pl.BlockSpec((1, rows_w, width), lambda i, here: (layer, half(i, here), 0)),
        pl.BlockSpec((1, rows_c, width), lambda i, here: (layer, half(i, here), 0)),
        pl.BlockSpec((1, width, rows_c), lambda i, here: (layer, 0, half(i, here))),
    )

    def body(here, *refs):
        grad_w, grad_c, grad_b = refs[-3:]
        for now in range(count):

            @pl.when(pl.program_id(0) == now)
            def _(source=refs[now]):
                gates, inputs = (rows_w + rows_c) // pieces, rows_c // pieces
                columns = []
                for piece in range(pieces):
                    at, row = piece * (gates + inputs), piece * gates
                    turn = min(max(rows_w - row, 0), gates)
                    if turn:
                        grad_w[0, row : row + turn, :] = source[at : at + turn, :]
                    if turn < gates:
                        to = row + turn - rows_w
                        grad_c[0, to : to + gates - turn, :] = source[at + turn : at + gates, :]
                    columns.append(source[at + gates : at + gates + inputs, :])
                grad_b[0] = jnp.concatenate(columns, axis=0).T

    return pl.pallas_call(
        body,
        name="put_in_place",
        out_shape=tuple(jax.ShapeDtypeStruct(*out) for out in outs),
        grid_spec=pltpu.PrefetchScalarGridSpec(
            num_scalar_prefetch=1,
            grid=(count,),
            in_specs=[vmem] * count + [pl.BlockSpec(memory_space=pl.ANY)] * len(before),
            out_specs=blocks,
        ),
        input_output_aliases={1 + count + i: i for i in range(len(before))},
        compiler_params=pltpu.CompilerParams(vmem_limit_bytes=VMEM_LIMIT),
    )(here, *(rows for _, rows in halves), *before)


def axis_parts():
    count, depth = lax.axis_size("seq"), lax.axis_size("dp")
    return (("seq", 2, 1, count), ("seq", count // 2, 2, count), ("dp", depth, 1, depth))


def shifted(value, part, away):
    name, size, stride, count = part
    pairs = []
    for i in range(count):
        place = (i // stride) % size
        pairs.append((i, i + ((place + away) % size - place) * stride))
    return lax.ppermute(value, name, pairs)


def add_by_shifts(value, parts, *earlier):
    for number, part in enumerate(parts):
        if number:
            value = sum(terms[1:], terms[0])
        if number == len(parts) - 1:
            value, *earlier = lax.optimization_barrier((value, *earlier))
        terms = [value] + [shifted(value, part, away) for away in range(1, part[1])]
    return terms, *earlier


def bits_of(size, stride=1):
    bits = []
    while size > 1:
        bits.append(stride)
        size, stride = size // 2, stride * 2
    return bits


def plane_bits():
    chip_bits = bits_of(lax.axis_size("seq") // 2, 2)
    middle = (len(chip_bits) + 1) // 2
    inner, outer = chip_bits[:middle], chip_bits[middle:]
    return list(zip(inner + outer, outer + inner))


def swap(value, axis, bit):
    return lax.ppermute(value, axis, [(i, i ^ bit) for i in range(lax.axis_size(axis))])


def bit_at(here, axis, bit):
    return lax.rem(lax.div(here[0 if axis == "seq" else 1], bit), 2)


def rows_at(half, rows):
    return pl.ds(pl.multiple_of(half * rows, CHUNKS), rows)


def fold_cores(bits, here, *refs):
    terms, targets = refs[:-4], refs[-4:]
    rows, cols = targets[0].shape
    for side in (0, 1):
        kept, sent = targets[2 * side : 2 * side + 2]
        where = slice(side * cols, (side + 1) * cols)
        bit = bit_at(here, "seq", bits[side])
        for half in (0, 1):

            @pl.when(bit == half)
            def _(half=half, kept=kept, sent=sent, where=where):
                start = 0
                for own, found in zip(terms[0::2], terms[1::2]):
                    for part, target in ((half, kept), (1 - half, sent)):
                        low = max(start, part * rows)
                        high = min(start + own.shape[0], (part + 1) * rows)
                        if low < high:
                            source = slice(low - start, high - start)
                            target[low - part * rows : high - part * rows, :] = (
                                own[source, where] + found[source, where]
                            )
                    start += own.shape[0]


def fold_sides(bits, here, *refs):
    targets, blocks = refs[-4:], refs[:-4]
    for side in (0, 1):
        kept, sent = targets[2 * side : 2 * side + 2]
        half, start = bit_at(here, "seq", bits[side]), 0
        for at in range(0, len(blocks), 4):
            own, found = blocks[at + 2 * side : at + 2 * side + 2]
            rows = own.shape[0] // 2
            to = slice(start, start + rows)
            kept[to, :] = own[rows_at(half, rows), :] + found[rows_at(half, rows), :]
            sent[to, :] = own[rows_at(1 - half, rows), :] + found[rows_at(1 - half, rows), :]
            start += rows


def fold_join(bit, here, left, found_left, right, found_right, kept, sent):
    rows, cols = kept.shape[0], left.shape[1]
    half = bit_at(here, "dp", bit)
    for side, (own, found) in enumerate(((left, found_left), (right, found_right))):
        where = slice(side * cols, (side + 1) * cols)
        kept[:, where] = own[rows_at(half, rows), :] + found[rows_at(half, rows), :]
        sent[:, where] = own[rows_at(1 - half, rows), :] + found[rows_at(1 - half, rows), :]


def fold_depth(bit, here, own, found, kept, sent):
    half, rows = bit_at(here, "dp", bit), kept.shape[0]
    kept[...] = own[rows_at(half, rows), :] + found[rows_at(half, rows), :]
    sent[...] = own[rows_at(1 - half, rows), :] + found[rows_at(1 - half, rows), :]


def add_two(own, found, out):
    out[...] = own[...] + found[...]


def unfold(bit, here, own, found, out):
    half, rows = bit_at(here, "dp", bit), own.shape[0]
    out[rows_at(half, rows), :] = own[...]
    out[rows_at(1 - half, rows), :] = found[...]


def unfold_split(bit, here, own, found, left, right):
    half, rows, cols = bit_at(here, "dp", bit), own.shape[0], left.shape[1]
    for side, out in enumerate((left, right)):
        where = slice(side * cols, (side + 1) * cols)
        out[rows_at(half, rows), :] = own[:, where]
        out[rows_at(1 - half, rows), :] = found[:, where]


def unfold_sides(bits, joined, here, *refs):
    for side in (0, 1):
        own, found = refs[2 * side : 2 * side + 2]
        half, (rows, cols) = bit_at(here, "seq", bits[side]), own.shape
        out = refs[4] if joined else refs[4 + side]
        where = slice(side * cols, (side + 1) * cols) if joined else slice(0, cols)
        out[rows_at(half, rows), where] = own[...]
        out[rows_at(1 - half, rows), where] = found[...]


def link_call(body, here, args, shapes):
    name = body.func.__name__
    return run(body, name, (here, *args), tuple((shape, f32) for shape in shapes))


class LinkSum:
    def __init__(self, here, terms):
        self.here, self.plane = here, plane_bits()
        self.depth = bits_of(lax.axis_size("dp"))
        rows = sum(term.shape[0] for term in terms[::2])
        self.shape = (rows // 2, terms[0].shape[1] // 2)
        self.parts = link_call(
            functools.partial(fold_cores, self.plane[0]), here, terms, (self.shape,) * 4
        )

    def swap_plane(self, stage):
        (left, right), pieces = self.plane[stage], self.parts
        self.parts = (
            pieces[0], swap(pieces[1], "seq", left), pieces[2], swap(pieces[3], "seq", right)
        )

    def down_plane(self, stage, *others):
        parts, rows, cols = list(self.parts), *self.shape
        for other in others:
            parts += other.parts
            rows += other.shape[0]
        self.shape = (rows // 2, cols)
        body = functools.partial(fold_sides, self.plane[stage])
        self.parts = link_call(body, self.here, parts, (self.shape,) * 4)

    def down_join(self):
        rows, cols = self.shape
        self.shape = (rows // 2, 2 * cols)
        body = functools.partial(fold_join, self.depth[0])
        self.parts = link_call(body, self.here, self.parts, (self.shape,) * 2)

    def swap_depth(self, stage):
        self.parts = (self.parts[0], swap(self.parts[1], "dp", self.depth[stage]))

    def down_depth(self, stage):
        rows, cols = self.shape
        self.shape = (rows // 2, cols)
        body = functools.partial(fold_depth, self.depth[stage])
        self.parts = link_call(body, self.here, self.parts, (self.shape,) * 2)

    def middle(self):
        (value,) = run(add_two, "add_two", self.parts, ((self.shape, f32),), scalars=0)
        self.parts = (value, value)

    def up_depth(self, stage):
        rows, cols = self.shape
        self.shape = (rows * 2, cols)
        body = functools.partial(unfold, self.depth[stage])
        (value,) = link_call(body, self.here, self.parts, (self.shape,))
        self.parts = (value, value)

    def up_split(self):
        rows, cols = self.shape
        self.shape = (rows * 2, cols // 2)
        body = functools.partial(unfold_split, self.depth[0])
        left, right = link_call(body, self.here, self.parts, (self.shape,) * 2)
        self.parts = (left, left, right, right)

    def up_plane(self, stage):
        rows, cols = self.shape
        if stage:
            self.shape = (rows * 2, cols)
            body = functools.partial(unfold_sides, self.plane[stage], False)
            left, right = link_call(body, self.here, self.parts, (self.shape,) * 2)
            self.parts = (left, left, right, right)
        else:
            self.shape = (rows * 2, cols * 2)
            body = functools.partial(unfold_sides, self.plane[stage], True)
            self.parts = link_call(body, self.here, self.parts, (self.shape,))

    def after(self, *values):
        self.parts, values = lax.optimization_barrier((self.parts, values))
        return values

    def to_depth(self):
        for stage in range(2, len(self.plane)):
            self.swap_plane(stage - 1)
            self.down_plane(stage)
        self.swap_plane(len(self.plane) - 1)

    def scatter_depth(self):
        for stage in range(len(self.depth) - 1):
            if stage:
                self.down_depth(stage)
            self.swap_depth(stage)

    def swap_whole(self):
        self.parts = (self.parts[0], swap(self.parts[0], "dp", self.depth[-1]))

    def gather_depth(self):
        for stage in range(len(self.depth) - 2, 0, -1):
            self.swap_depth(stage)
            self.up_depth(stage)
        self.swap_depth(0)


def wait_for(*things):
    sums = [thing for thing in things if isinstance(thing, LinkSum)]
    values = [thing for thing in things if not isinstance(thing, LinkSum)]
    parts, values = lax.optimization_barrier(([entry.parts for entry in sums], values))
    for entry, part in zip(sums, parts):
        entry.parts = part
    return values


def discretize(lam_re, lam_im, log_step):
    step_size = jnp.exp(log_step)
    decay_abs = jnp.exp(lam_re * step_size)
    rotation = lam_im * step_size
    dec_re = decay_abs * jnp.cos(rotation)
    dec_im = decay_abs * jnp.sin(rotation)
    denom_sq = lam_re * lam_re + lam_im * lam_im
    inj_re = ((dec_re - 1.0) * lam_re + dec_im * lam_im) / denom_sq
    inj_im = (dec_im * lam_re - (dec_re - 1.0) * lam_im) / denom_sq
    return (dec_re, dec_im, inj_re, inj_im)


def per_device(
    block_in, cotangent, doc_lengths, norm_gain, norm_shift, log_step, lam_re, lam_im,
    b_proj, c_proj, d_skip, w_gate,
):
    batches, seqs, span, width = block_in.shape
    assert seqs == 1 and span % (4 * CHUNKS) == 0 and span & (span - 1) == 0
    half = lam_re.shape[1]
    groups = half // LANES
    rows = batches * span
    count = lax.axis_size("seq")
    tokens = float(seqs * lax.axis_size("dp") * span * count)
    here = jnp.stack([lax.axis_index("seq"), lax.axis_index("dp")]).astype(jnp.int32)
    place = jnp.concatenate([here] + [doc_lengths[batch, 0] for batch in range(batches)])
    place, block_in = lax.optimization_barrier((place, block_in))
    here = place
    disc = discretize(lam_re, lam_im, log_step)

    x = block_in.reshape(rows, width)
    cot = cotangent.reshape(rows, width)
    lower = (0, False, batches, span, groups, tokens, count)
    upper = (1, True, batches, span, groups, tokens, count)
    part = functools.partial

    flat, low = ((rows, width), f32), ((rows, width), bf16)
    wide, wide_low = ((rows, 2 * half), f32), ((rows, 2 * half), bf16)
    padded = ((batches * (span + CHUNKS), 2 * half), f32)
    sums = ((2 * batches, width), f32)
    prefix = ((2, batches * CHUNKS, 2 * half), f32)
    total = ((batches, 2 * half), f32)
    line, shared = ((1, width), f32), ((2, width), f32)
    small = ((8, width), f32)

    def gather_row(value, reverse):
        both = jnp.concatenate([value, swap(value, "seq", 1)], axis=0)
        chips = count // 2
        return [both] + [
            shifted(both, plane, chips - away if reverse else away) for away in range(1, chips)
        ]

    (stats,) = run(part(first_sums, batches, span), "first_sums", (x,), (sums,), scalars=0)

    def order(value, inverse):
        body = part(order_rows, batches, span, inverse)
        return run(body, "order_rows", (value,), (low,), scalars=0)[0]

    norms = jnp.concatenate([norm_gain, norm_shift, d_skip], axis=0)

    def forward(cfg, hidden, stats):
        return run(
            part(enter_layer, cfg),
            "enter_layer",
            (place, stats, hidden, norms, disc, b_proj),
            (low, wide, prefix, total, sums),
        )

    links, plane, depth = axis_parts()
    stats, ordered = lax.optimization_barrier(
        (add_by_shifts(stats, (links, plane, depth))[0], order(x, False))
    )
    u0, drive0, prefix0, total0, norm0 = forward(lower, ordered, stats)
    states0, states_low0, act0, sig0, slope0, hidden1, stats = run(
        part(middle_forward, lower),
        "middle_forward",
        (place, gather_row(total0, False), prefix0, disc, drive0, u0, ordered, c_proj, norms, w_gate),
        (padded, wide_low, low, flat, flat, flat, sums),
        (flat,),
    )
    cot, stats = lax.optimization_barrier((cot, stats))
    stats, ordered_cot = lax.optimization_barrier(
        (add_by_shifts(stats, (links, plane, depth))[0], order(cot, False))
    )
    u1, drive1, prefix1, total1, norm1 = forward(upper, hidden1, stats)
    (
        result1, states1, states_low1, act1, grad_gate1, grad_mixed1, grad_low1,
        source1, prefix1, total1, grad_d1,
    ) = run(
        part(turn_around, upper),
        "turn_around",
        (
            place, gather_row(total1, True), prefix1, disc, drive1, u1, hidden1, c_proj, norms, w_gate,
            ordered_cot,
        ),
        (low, padded, wide_low, low, low, flat, low, wide, prefix, total, line),
        (flat, flat, flat),
    )

    def halves(length):
        return (((length // 2, width), f32),) * 2

    grad_proj1, grad_u1, stats, small1 = run(
        part(backward_finish, upper),
        "backward_finish",
        (
            place, gather_row(total1, False), prefix1, disc, source1, drive1, states1, u1, grad_mixed1,
            grad_d1, hidden1, norm1, norms, b_proj,
        ),
        (wide_low, flat, sums, small),
    )
    sizes = (width + 2 * half, 2 * half)
    own1, sent1 = run(
        all_weights,
        "all_weights",
        (here, act1, grad_gate1, states_low1, grad_low1, grad_proj1, u1),
        halves(sum(sizes)),
    )
    stats = stats + swap(stats, "seq", 1)
    stats, sent1 = lax.optimization_barrier((stats, sent1))
    upper_sum = LinkSum(here, (own1, swap(sent1, "seq", 1)))
    stats, upper_sum.parts = add_by_shifts(stats, (plane, depth), upper_sum.parts)
    upper_sum.swap_plane(0)
    (
        grad_out0, shared1, grad_gate0, grad_mixed0, grad_low0, source0, prefix0, total0, grad_d0,
    ) = run(
        part(between_layers, upper, lower),
        "between_layers",
        (
            place, stats, ordered_cot, grad_u1, hidden1, norm1, norms,
            disc, u0, c_proj, w_gate, states_low0, act0, sig0, slope0,
        ),
        (flat, shared, low, flat, low, wide, prefix, total, line),
        (flat,),
    )
    (total0,) = upper_sum.after(total0)
    upper_sum.down_plane(1)
    (total0,) = upper_sum.after(total0)
    upper_sum.to_depth()
    ends, grad_gate0 = wait_for(upper_sum, gather_row(total0, True), grad_gate0)
    upper_sum.down_join()
    ends, grad_gate0 = wait_for(upper_sum, ends, grad_gate0)
    upper_sum.scatter_depth()
    own_gates, sent_gates = run(
        gate_weights, "gate_weights", (here, act0, grad_gate0, states_low0, grad_low0),
        halves(sizes[0]),
    )
    own_gates, ends = lax.optimization_barrier((own_gates, ends))
    grad_proj0, grad_u0, last_sums = run(
        part(backward_finish_last, lower),
        "backward_finish",
        (
            place, ends, prefix0, disc, source0, drive0, states0, u0, grad_mixed0, grad_d0,
            ordered, norm0, norms, b_proj, small1,
        ),
        (wide_low, flat, ((3 * CHUNKS, width), f32)),
    )
    lower_sum = LinkSum(here, (own_gates, swap(sent_gates, "seq", 1)))
    (grad_proj0,) = wait_for(upper_sum, lower_sum, grad_proj0)
    own_inputs, sent_inputs = run(
        input_weights, "input_weights", (here, grad_proj0, u0), halves(sizes[1])
    )
    inputs_sum = LinkSum(here, (own_inputs, swap(sent_inputs, "seq", 1)))
    upper_sum.middle()
    upper_sum.swap_whole()
    lower_sum.swap_plane(0)
    inputs_sum.swap_plane(0)
    wait_for(upper_sum, lower_sum, inputs_sum)

    lower_sum.down_plane(1, inputs_sum)
    upper_sum.middle()
    upper_sum.gather_depth()
    lower_sum.to_depth()
    wait_for(upper_sum, lower_sum)

    lower_sum.down_join()
    upper_sum.up_split()
    lower_sum.scatter_depth()
    upper_sum.swap_plane(len(upper_sum.plane) - 1)
    wait_for(upper_sum, lower_sum)

    lower_sum.middle()
    lower_sum.swap_whole()
    for stage in range(len(upper_sum.plane) - 1, 0, -1):
        upper_sum.up_plane(stage)
        upper_sum.swap_plane(stage - 1)
    (last_sums,) = wait_for(upper_sum, lower_sum, last_sums)

    lower_sum.middle()
    (last_sums,) = lower_sum.after(last_sums)
    lower_sum.gather_depth()
    last_sums = last_sums + swap(last_sums, "seq", 1)
    last_terms = [last_sums] + [shifted(last_sums, plane, away) for away in range(1, plane[1])]
    last_terms = wait_for(lower_sum, *last_terms)

    lower_sum.up_split()
    wait_for(upper_sum, lower_sum)
    lower_sum.swap_plane(len(lower_sum.plane) - 1)
    upper_sum.up_plane(0)
    own1, result1 = lax.optimization_barrier((upper_sum.parts[0], result1))
    other1 = swap(own1, "seq", 1)
    block_out = order(result1, True)
    final = (((2, width, width), f32), ((2, 2 * half, width), f32), ((2, width, 2 * half), f32))
    placed = put_in_place(1, here, ((False, own1), (True, other1)), final, ())
    summed = sum(last_terms)
    for bit in bits_of(lax.axis_size("dp")):
        summed = summed + swap(summed, "dp", bit)
    summed, block_out = wait_for(lower_sum, summed, block_out)

    for stage in range(len(lower_sum.plane) - 1, 0, -1):
        lower_sum.up_plane(stage)
        if stage == 1:
            (summed,) = lower_sum.after(summed)
        lower_sum.swap_plane(stage - 1)
    grad_input, shared0 = run(
        part(last_step, lower),
        "last_step",
        ((summed[: 2 * batches],), grad_out0, grad_u0, ordered, norm0, norms),
        (flat, shared),
        (((width // LANES, rows, LANES), f32),),
        scalars=0,
    )
    small_sum = summed[CHUNKS:].reshape(2, CHUNKS, width)
    _, pullback = jax.vjp(discretize, lam_re, lam_im, log_step)
    grad_lr, grad_li, grad_ls = pullback(tuple(small_sum[:, kind, :half] for kind in range(4)))
    both = jnp.stack([shared0, shared1])
    grad_gain, grad_shift = both[:, 0], both[:, 1]
    early = [swap(lower_sum.parts[at], "seq", 1) for at in (0, 2)]
    grad_skip = small_sum[:, 4]
    grad_input, grad_lr, grad_li, grad_ls, grad_gain, grad_shift, grad_skip, *rest = wait_for(
        lower_sum, grad_input, grad_lr, grad_li, grad_ls, grad_gain, grad_shift, grad_skip,
        *early, *placed,
    )
    early, placed = rest[:2], rest[2:]

    late = [swap(lower_sum.parts[at], "seq", 1) for at in (1, 3)]
    other_sum = copy.copy(lower_sum)
    other_sum.parts = (early[0], late[0], early[1], late[1])
    lower_sum.up_plane(0)
    placed = put_in_place(0, here, ((False, lower_sum.parts[0]),), final, placed, 4)
    other_sum.up_plane(0)
    grad_w, grad_c, grad_b = put_in_place(
        0, here, ((True, other_sum.parts[0]),), final, placed, 4
    )
    shape = block_in.shape
    return (
        block_out.reshape(shape), grad_input.reshape(shape), grad_gain, grad_shift,
        grad_ls, grad_lr, grad_li, grad_b, grad_c, grad_skip, grad_w,
    )


def solution(mesh):
    split = P(None, "dp", "seq", None)
    return jax.shard_map(
        per_device,
        mesh=mesh,
        in_specs=(split, split, P(None, "dp", None)) + (P(),) * 9,
        out_specs=(split, split) + (P(),) * 9,
        check_vma=False,
    )
```

```python
import copy
import functools

import jax
import jax.numpy as jnp
from jax import lax
from jax.experimental import pallas as pl
from jax.experimental.pallas import tpu as pltpu
from jax.sharding import PartitionSpec as P

f32, bf16 = jnp.float32, jnp.bfloat16
epsilon = 1e-05
tanh_scale = 0.7978845608028654
cubic_term = 0.044715
LANES = 128
CHUNKS = 8
ROWS = 32
VMEM_LIMIT = 16 * 1024 * 1024


def dot(left, right, contract=(1, 0)):
    return lax.dot_general(
        left, right, (((contract[0],), (contract[1],)), ((), ())), preferred_element_type=f32
    )


def reorder(span, inverse):
    shape = (span, span)
    kept, moved = (1, 0) if inverse else (0, 1)
    row = lax.broadcasted_iota(jnp.int32, shape, kept)
    position = lax.broadcasted_iota(jnp.int32, shape, moved)
    source = (row & (CHUNKS - 1)) * (span // CHUNKS) + (row >> 3)
    return jnp.where(position == source, 1.0, 0.0).astype(bf16)


def row_loop(count, body, init=0, step=ROWS):
    def one(index, carry):
        return body(pl.multiple_of(index * step, step), carry)

    return lax.fori_loop(0, count // step, one, init, unroll=4)


def documents(here, batches, span, count):
    mine = here[0]
    first = mine * span
    out = []
    for batch in range(batches):
        begins, ends, so_far = [], [], 0
        docs = (here.shape[0] - 2) // batches
        for doc in range(docs):
            begins.append(so_far)
            so_far = so_far + here[2 + batch * docs + doc]
            ends.append(so_far)
        before, after = 0, 2 * count * span
        for begin, end in zip(begins, ends):
            before = jnp.maximum(before, jnp.where(begin < first, begin, 0))
            after = jnp.minimum(after, jnp.where(end > first + span, end, 2 * count * span))
        after = jnp.where(mine == count - 1, 0, after)
        out.append(begins + ends + [before, after, first, mine])
    return out


def place_documents(cfg, place):
    layer, reverse, batches, span, groups, tokens, count = cfg
    return documents(place, batches, span, count)


def keep_of(meta, batch, base, step, backward):
    docs = (len(meta[batch]) - 4) // 2
    off = docs if backward else 0
    late = 1 if backward else 0
    stop = base == meta[batch][off] - step - late
    for doc in range(1, docs):
        stop = jnp.logical_or(stop, base == meta[batch][off + doc] - step - late)
    return jnp.where(stop, 0.0, 1.0)


def base_positions(meta, steps):
    return meta[0][-2] + lax.broadcasted_iota(jnp.int32, (CHUNKS, LANES), 0) * steps


def lanes_of(index, half=0):
    return slice(half + index * LANES, half + (index + 1) * LANES)


def coef_tiles(value, groups):
    return [
        tuple(jnp.broadcast_to(part[:, lanes_of(q)], (CHUNKS, LANES)) for part in value)
        for q in range(groups)
    ]


def constants(disc, layer):
    dec_re, dec_im, inj_re, inj_im = (part[layer : layer + 1, :] for part in disc)
    return (dec_re, dec_im), (inj_re, inj_im)


def times(a, b):
    return (a[0] * b[0] - a[1] * b[1], a[0] * b[1] + a[1] * b[0])


def power(value, exponent):
    for _ in range(exponent.bit_length() - 1):
        value = times(value, value)
    return value


def conj(value):
    return (value[0], -value[1])


def scan(meta, source, inject, dec, batches, span, groups, reverse, masks_reverse, init, extra, visit):
    steps = span // CHUNKS
    half = groups * LANES
    base = base_positions(meta, steps)

    def pair(index, carry):
        states, more = carry
        states = list(states)
        first = steps - 2 - 2 * index if reverse else 2 * index
        start = pl.multiple_of(first * CHUNKS, 2 * CHUNKS)
        order = (1, 0) if reverse else (0, 1)
        for batch in range(batches):
            keeps = [keep_of(meta, batch, base, first + j, masks_reverse) for j in (0, 1)]
            for q in range(groups):
                rows = pl.ds(batch * span + start, 2 * CHUNKS)
                src_re = source[rows, lanes_of(q)]
                src_im = source[rows, lanes_of(q, half)]
                state = states[batch * groups + q]
                found = [None, None]
                for j in order:
                    part = (
                        src_re[j * CHUNKS : (j + 1) * CHUNKS],
                        src_im[j * CHUNKS : (j + 1) * CHUNKS],
                    )
                    push = times(inject[q], part) if inject is not None else part
                    held = times((keeps[j] * dec[q][0], keeps[j] * dec[q][1]), state)
                    state = (held[0] + push[0], held[1] + push[1])
                    found[j] = state
                states[batch * groups + q] = state
                more = visit(more, batch, q, first, start, found, (src_re, src_im))
            more = visit(more, batch, None, first, start, keeps, None)
        return tuple(states), more

    return lax.fori_loop(0, steps // 2, pair, (tuple(init), extra), unroll=4)


def zero_states(batches, groups):
    zero = jnp.zeros((CHUNKS, LANES), f32)
    return [(zero, zero)] * (batches * groups)


def local_ends(meta, source, inject, dec, batches, span, groups, reverse, prefix, total):
    ones = tuple(jnp.ones((CHUNKS, LANES), f32) for _ in range(batches))

    def visit(more, batch, q, first, start, found, src):
        if q is not None:
            return more
        return tuple(
            value * found[0] * found[1] if at == batch else value for at, value in enumerate(more)
        )

    dec_chunk = coef_tiles(power(dec, span // CHUNKS), groups)
    ends, kept = scan(
        meta, source, inject, coef_tiles(dec, groups), batches, span, groups, reverse, reverse,
        zero_states(batches, groups), ones, visit,
    )
    half = groups * LANES
    row = lax.broadcasted_iota(jnp.int32, (CHUNKS, LANES), 0)
    for batch in range(batches):
        for q in range(groups):
            end = ends[batch * groups + q]
            decay = (kept[batch] * dec_chunk[q][0], kept[batch] * dec_chunk[q][1])
            for shift in (1, 2, 4):
                turn = CHUNKS - shift if reverse else shift
                valid = row < CHUNKS - shift if reverse else row >= shift
                before = [pltpu.roll(value, turn, 0) for value in (*end, *decay)]
                from_before = times(decay, (before[0], before[1]))
                end = (
                    end[0] + jnp.where(valid, from_before[0], 0.0),
                    end[1] + jnp.where(valid, from_before[1], 0.0),
                )
                longer = times(decay, (before[2], before[3]))
                decay = (
                    jnp.where(valid, longer[0], decay[0]),
                    jnp.where(valid, longer[1], decay[1]),
                )
            rows = slice(batch * CHUNKS, (batch + 1) * CHUNKS)
            prefix[0, rows, lanes_of(q)] = end[0]
            prefix[0, rows, lanes_of(q, half)] = end[1]
            prefix[1, rows, lanes_of(q)] = decay[0]
            prefix[1, rows, lanes_of(q, half)] = decay[1]
            last = 0 if reverse else CHUNKS - 1
            total[batch : batch + 1, lanes_of(q)] = end[0][last : last + 1]
            total[batch : batch + 1, lanes_of(q, half)] = end[1][last : last + 1]


def chunk_carries(meta, gathered, dec, prefix, batches, span, groups, reverse):
    half = groups * LANES
    dec_span = power(dec, span)
    row = lax.broadcasted_iota(jnp.int32, (CHUNKS, LANES), 0)
    mine = meta[0][-1]
    core = lax.rem(mine, 2)
    out = []
    for batch in range(batches):
        enter = (jnp.zeros((1, half), f32), jnp.zeros((1, half), f32))
        for away in range(len(gathered) - 1, -1, -1):
            for kind in (1, 0) if reverse else (0, 1):
                if away == 0 and kind == (0 if reverse else 1):
                    continue
                if reverse:
                    other = mine - core + 2 * away + kind
                    reaches = meta[batch][-3] > other * span
                else:
                    other = mine - core - 2 * away + kind
                    reaches = meta[batch][-4] < (other + 1) * span
                same = gathered[away][batch : batch + 1, :]
                unlike = gathered[away][batches + batch : batches + batch + 1, :]
                value = jnp.where(reaches, jnp.where(core == kind, same, unlike), 0.0)
                moved = times(dec_span, enter)
                after = (moved[0] + value[:, :half], moved[1] + value[:, half:])
                if away == 0:
                    after = tuple(jnp.where(core == kind, old, new) for old, new in zip(enter, after))
                enter = after
        rows = slice(batch * CHUNKS, (batch + 1) * CHUNKS)
        for q in range(groups):
            own = tuple(jnp.broadcast_to(part[:, lanes_of(q)], (CHUNKS, LANES)) for part in enter)
            end = (prefix[0, rows, lanes_of(q)], prefix[0, rows, lanes_of(q, half)])
            decay = (prefix[1, rows, lanes_of(q)], prefix[1, rows, lanes_of(q, half)])
            moved = times(decay, own)
            turn, first = (CHUNKS - 1, CHUNKS - 1) if reverse else (1, 0)
            out.append(
                tuple(
                    jnp.where(row == first, own[i], pltpu.roll(end[i] + moved[i], turn, 0))
                    for i in (0, 1)
                )
            )
    return out


def add_sums(target, batches, sums):
    for kind, per_batch in enumerate(sums):
        for batch in range(batches):
            target[kind * batches + batch : kind * batches + batch + 1, :] = jnp.sum(
                per_batch[batch], axis=0, keepdims=True
            )


def fold(value):
    return sum(value[i : i + CHUNKS] for i in range(CHUNKS, value.shape[0], CHUNKS)) + value[:CHUNKS]


def order_rows(batches, span, inverse, x, out):
    turn = reorder(span, inverse)
    for batch in range(batches):
        rows = slice(batch * span, (batch + 1) * span)
        out[rows, :] = dot(turn, x[rows, :]).astype(bf16)


def first_sums(batches, span, x, stats):
    width = x.shape[1]
    sums, squares = [], []
    for batch in range(batches):

        def body(start, carry, batch=batch):
            value = x[pl.ds(batch * span + start, ROWS), :].astype(f32)
            return carry[0] + fold(value), carry[1] + fold(value * value)

        zero = jnp.zeros((CHUNKS, width), f32)
        one, two = row_loop(span, body, (zero, zero))
        sums.append(one)
        squares.append(two)
    add_sums(stats, batches, (sums, squares))


def enter_layer(
    cfg, place, stats, hidden, norms, disc, b_proj, u, drive, prefix, total, norm
):
    layer, reverse, batches, span, groups, tokens, count = cfg
    sums = sum(part[...] for part in stats)
    average = sums[:batches] / tokens
    spread = sums[batches:] / tokens - average * average
    scale = lax.rsqrt(spread + epsilon)
    norm[:batches, :] = average
    norm[batches:, :] = scale
    gain_now, shift_now = norms[layer : layer + 1, :], norms[layer + 2 : layer + 3, :]
    for batch in range(batches):

        def body(start, carry, batch=batch):
            rows = pl.ds(batch * span + start, ROWS)
            normed = (hidden[rows, :].astype(f32) - average[batch : batch + 1]) * scale[
                batch : batch + 1
            ]
            u[rows, :] = (normed * gain_now + shift_now).astype(bf16)
            return carry

        row_loop(span, body)
    drive[...] = dot(u[...], b_proj[layer])
    meta = place_documents(cfg, place)
    dec, inj = constants(disc, layer)
    local_ends(
        meta, drive, coef_tiles(inj, groups), dec, batches, span, groups, reverse, prefix, total
    )


def finish_states(cfg, meta, ends, prefix, disc, drive, states, states_low):
    layer, reverse, batches, span, groups, tokens, count = cfg
    half = groups * LANES
    padded = span + CHUNKS
    dec, inj = constants(disc, layer)
    init = chunk_carries(meta, ends, dec, prefix, batches, span, groups, reverse)
    for batch in range(batches):
        edge = batch * padded + (span if reverse else 0)
        for q in range(groups):
            states[edge : edge + CHUNKS, lanes_of(q)] = init[batch * groups + q][0]
            states[edge : edge + CHUNKS, lanes_of(q, half)] = init[batch * groups + q][1]

    def visit(more, batch, q, first, start, found, src):
        if q is not None:
            for part, off in ((0, 0), (1, half)):
                both = jnp.concatenate([found[0][part], found[1][part]], axis=0)
                at = batch * padded + (0 if reverse else CHUNKS)
                states[pl.ds(at + start, 2 * CHUNKS), lanes_of(q, off)] = both
                states_low[pl.ds(batch * span + start, 2 * CHUNKS), lanes_of(q, off)] = both.astype(
                    bf16
                )
        return more

    scan(
        meta, drive, coef_tiles(inj, groups), coef_tiles(dec, groups), batches, span, groups,
        reverse, reverse, init, 0, visit,
    )


def forward_finish(
    cfg, meta, ends, prefix, disc, drive, u, hidden, c_proj, norms, w_gate,
    states, states_low, act, sig, slope, result, wide, emit,
):
    layer, reverse, batches, span, groups, tokens, count = cfg
    finish_states(cfg, meta, ends, prefix, disc, drive, states, states_low)
    wide[...] = dot(states_low[...], c_proj[layer])
    skip = norms[layer + 4 : layer + 5, :]

    def body(start, carry):
        rows = pl.ds(start, ROWS)
        mixed = wide[rows, :] + skip * u[rows, :].astype(f32)
        square = mixed * mixed
        th = jnp.tanh(tanh_scale * (mixed + cubic_term * square * mixed))
        half_one = 0.5 * (1.0 + th)
        act[rows, :] = (mixed * half_one).astype(bf16)
        slope[rows, :] = half_one + 0.5 * mixed * (1.0 - th * th) * tanh_scale * (
            1.0 + 3.0 * cubic_term * square
        )
        return carry

    row_loop(batches * span, body)
    wide[...] = dot(act[...], w_gate[layer])
    sums, squares = [], []
    for batch in range(batches):

        def gate(start, carry, batch=batch):
            rows = pl.ds(batch * span + start, ROWS)
            sig_now = 0.5 + 0.5 * jnp.tanh(0.5 * wide[rows, :])
            sig[rows, :] = sig_now
            value = hidden[rows, :].astype(f32) + act[rows, :].astype(f32) * sig_now
            result[rows, :] = value.astype(result.dtype)
            if emit is None:
                return carry
            return carry[0] + fold(value), carry[1] + fold(value * value)

        zero = jnp.zeros((CHUNKS, wide.shape[1]), f32)
        one, two = row_loop(span, gate, (zero, zero))
        sums.append(one)
        squares.append(two)
    if emit is not None:
        add_sums(emit, batches, (sums, squares))


def backward_start(
    cfg, meta, grad_out, disc, u, c_proj, w_gate, states_low, act, sig, slope,
    grad_gate, grad_mixed, grad_low, source, prefix, total, grad_d, wide,
):
    layer, reverse, batches, span, groups, tokens, count = cfg

    def body(start, carry):
        rows = pl.ds(start, ROWS)
        sig_now = sig[rows, :]
        grad_gate[rows, :] = (
            grad_out[rows, :].astype(f32) * act[rows, :].astype(f32) * sig_now * (1.0 - sig_now)
        ).astype(bf16)
        return carry

    row_loop(batches * span, body)
    wide[...] = dot(grad_gate[...], w_gate[layer], (1, 1))

    def mixed(start, carry):
        rows = pl.ds(start, ROWS)
        value = (grad_out[rows, :].astype(f32) * sig[rows, :] + wide[rows, :]) * slope[rows, :]
        grad_mixed[rows, :] = value
        grad_low[rows, :] = value.astype(bf16)
        return carry + fold(value * u[rows, :].astype(f32))

    gd = row_loop(batches * span, mixed, jnp.zeros((CHUNKS, wide.shape[1]), f32))
    grad_d[...] = jnp.sum(gd, axis=0, keepdims=True)
    source[...] = dot(grad_low[...], c_proj[layer], (1, 1))
    local_ends(
        meta, source, None, conj(constants(disc, layer)[0]), batches, span, groups, not reverse,
        prefix, total,
    )


def middle_forward(
    cfg, place, ends, prefix, disc, drive, u, hidden, c_proj, norms, w_gate,
    states, states_low, act, sig, slope, result, stats, wide,
):
    meta = place_documents(cfg, place)
    forward_finish(
        cfg, meta, ends, prefix, disc, drive, u, hidden, c_proj, norms, w_gate,
        states, states_low, act, sig, slope, result, wide, stats,
    )


def turn_around(
    cfg, place, ends, prefix, disc, drive, u, hidden, c_proj, norms, w_gate, ordered_cot,
    result, states, states_low, act, grad_gate, grad_mixed, grad_low, source,
    back_prefix, total, grad_d, sig, slope, wide,
):
    layer, reverse, batches, span, groups, tokens, count = cfg
    meta = place_documents(cfg, place)
    forward_finish(
        cfg, meta, ends, prefix, disc, drive, u, hidden, c_proj, norms, w_gate,
        states, states_low, act, sig, slope, result, wide, None,
    )
    backward_start(
        cfg, meta, ordered_cot, disc, u, c_proj, w_gate, states_low, act, sig, slope,
        grad_gate, grad_mixed, grad_low, source, back_prefix, total, grad_d, wide,
    )


def backward_finish(
    cfg, place, ends, prefix, disc, source, drive, states, u, grad_mixed, grad_d, hidden, norm,
    norms, b_proj, grad_proj, grad_u, stats, small,
):
    layer, reverse, batches, span, groups, tokens, count = cfg
    half = groups * LANES
    padded = span + CHUNKS
    steps = span // CHUNKS
    meta = place_documents(cfg, place)
    dec, inj = constants(disc, layer)
    dec = conj(dec)
    init = chunk_carries(meta, ends, dec, prefix, batches, span, groups, not reverse)
    inj = coef_tiles(inj, groups)
    base = base_positions(meta, steps)
    zero = jnp.zeros((CHUNKS, LANES), f32)

    def visit(more, batch, q, first, start, found, src):
        if q is None:
            return more
        more = list(more)
        rows = pl.ds(batch * span + start, 2 * CHUNKS)
        drive_re, drive_im = drive[rows, lanes_of(q)], drive[rows, lanes_of(q, half)]
        before = pl.ds(batch * padded + start + (CHUNKS if reverse else 0), 2 * CHUNKS)
        prior_re, prior_im = states[before, lanes_of(q)], states[before, lanes_of(q, half)]
        dec_re, dec_im, inj_re, inj_im = more[q]
        out_re, out_im = [], []
        for j in (0, 1):
            part = slice(j * CHUNKS, (j + 1) * CHUNKS)
            adj_re, adj_im = found[j]
            keep = keep_of(meta, batch, base, first + j, reverse)
            kept_re, kept_im = keep * adj_re, keep * adj_im
            dec_re = dec_re + kept_re * prior_re[part] + kept_im * prior_im[part]
            dec_im = dec_im + kept_im * prior_re[part] - kept_re * prior_im[part]
            inj_re = inj_re + adj_re * drive_re[part] + adj_im * drive_im[part]
            inj_im = inj_im + adj_im * drive_re[part] - adj_re * drive_im[part]
            out_re.append(inj[q][0] * adj_re + inj[q][1] * adj_im)
            out_im.append(inj[q][0] * adj_im - inj[q][1] * adj_re)
        grad_proj[rows, lanes_of(q)] = jnp.concatenate(out_re, axis=0).astype(bf16)
        grad_proj[rows, lanes_of(q, half)] = jnp.concatenate(out_im, axis=0).astype(bf16)
        more[q] = (dec_re, dec_im, inj_re, inj_im)
        return tuple(more)

    _, sums = scan(
        meta, source, None, coef_tiles(dec, groups), batches, span, groups,
        not reverse, not reverse, init, ((zero,) * 4,) * groups, visit,
    )
    small[...] = jnp.zeros_like(small)
    for q in range(groups):
        for kind in range(4):
            small[kind : kind + 1, lanes_of(q)] = jnp.sum(sums[q][kind], axis=0, keepdims=True)
    small[4:5, :] = grad_d[...]
    grad_u[...] = dot(grad_proj[...], b_proj[layer], (1, 1))
    skip = norms[layer + 4 : layer + 5, :]
    plain, times_normed = [], []
    for batch in range(batches):
        average = norm[batch : batch + 1, :]
        scale = norm[batches + batch : batches + batch + 1, :]

        def body(start, carry, batch=batch, average=average, scale=scale):
            rows = pl.ds(batch * span + start, ROWS)
            value = grad_u[rows, :] + grad_mixed[rows, :] * skip
            grad_u[rows, :] = value
            normed = (hidden[rows, :].astype(f32) - average) * scale
            return carry[0] + fold(value), carry[1] + fold(value * normed)

        zero_sum = jnp.zeros((CHUNKS, grad_u.shape[1]), f32)
        one, two = row_loop(span, body, (zero_sum, zero_sum))
        plain.append(one)
        times_normed.append(two)
    add_sums(stats, batches, (plain, times_normed))


def backward_finish_last(cfg, *refs):
    ins, before, (grad_proj, grad_u, sums) = refs[:-4], refs[-4], refs[-3:]
    sums[...] = jnp.zeros_like(sums)
    sums[2 * CHUNKS :, :] = before[...]
    backward_finish(
        cfg, *ins, grad_proj, grad_u, sums.at[pl.ds(0, CHUNKS)], sums.at[pl.ds(CHUNKS, CHUNKS)]
    )


def norm_backward(cfg, stats, grad_out, grad_u, hidden, norm, norms, store, shared):
    layer, reverse, batches, span, groups, tokens, count = cfg
    sums = sum(part[...] for part in stats)
    shared[0:1, :] = jnp.sum(sums[batches:], axis=0, keepdims=True)
    shared[1:2, :] = jnp.sum(sums[:batches], axis=0, keepdims=True)
    gain_now = norms[layer : layer + 1, :]
    for batch in range(batches):
        average = norm[batch : batch + 1, :]
        scale = norm[batches + batch : batches + batch + 1, :]
        plain = gain_now * sums[batch : batch + 1] / tokens
        slanted = gain_now * sums[batches + batch : batches + batch + 1] / tokens

        def body(start, carry, batch=batch, average=average, scale=scale, plain=plain, slanted=slanted):
            rows = pl.ds(batch * span + start, ROWS)
            normed = (hidden[rows, :].astype(f32) - average) * scale
            value = grad_out[rows, :].astype(f32) + scale * (
                grad_u[rows, :] * gain_now - plain - normed * slanted
            )
            store(rows, value)
            return carry

        row_loop(span, body)


def between_layers(
    cfg, lower, place, stats, upper_out, upper_u, upper_hidden, upper_norm, norms,
    disc, u, c_proj, w_gate, states_low, act, sig, slope,
    grad_out, shared, grad_gate, grad_mixed, grad_low, source, prefix, total, grad_d, wide,
):
    def store(rows, value):
        grad_out[rows, :] = value

    norm_backward(cfg, stats, upper_out, upper_u, upper_hidden, upper_norm, norms, store, shared)
    meta = place_documents(lower, place)
    backward_start(
        lower, meta, grad_out, disc, u, c_proj, w_gate, states_low, act, sig, slope,
        grad_gate, grad_mixed, grad_low, source, prefix, total, grad_d, wide,
    )


def last_step(cfg, stats, grad_out, grad_u, hidden, norm, norms, target, shared, ordered):
    layer, reverse, batches, span, groups, tokens, count = cfg
    planes = target.shape[1] // LANES

    def store(rows, value):
        for plane in range(planes):
            ordered[plane, rows, :] = value[:, lanes_of(plane)]

    norm_backward(cfg, stats, grad_out, grad_u, hidden, norm, norms, store, shared)
    steps = span // CHUNKS
    for batch in range(batches):
        for chunk in range(CHUNKS):
            at = batch * span
            for plane in range(planes):
                target[at + chunk * steps : at + (chunk + 1) * steps, lanes_of(plane)] = ordered[
                    plane, pl.ds(at + chunk, steps, stride=CHUNKS), :
                ]


def half_weights(core, refs, own, sent):
    for target, half in ((own, core), (sent, 1 - core)):
        at = 0
        for left, right in refs:
            rows = left.shape[1] // 2
            cols = pl.ds(pl.multiple_of(half * rows, LANES), rows)
            target[at : at + rows, :] = dot(left[:, cols], right[...], (0, 0))
            at += rows


def all_weights(here, act, grad_gate, states_low, grad_low, grad_proj, u, own, sent):
    refs = ((act, grad_gate), (states_low, grad_low), (grad_proj, u))
    half_weights(lax.rem(here[0], 2), refs, own, sent)


def gate_weights(here, act, grad_gate, states_low, grad_low, own, sent):
    half_weights(lax.rem(here[0], 2), ((act, grad_gate), (states_low, grad_low)), own, sent)


def input_weights(here, grad_proj, u, own, sent):
    half_weights(lax.rem(here[0], 2), ((grad_proj, u),), own, sent)


def run(body, name, args, outs, scratch=(), scalars=1):
    vmem, smem = pl.BlockSpec(memory_space=pltpu.VMEM), pl.BlockSpec(memory_space=pltpu.SMEM)
    specs = tuple(
        jax.tree.map(lambda _, at=at: smem if at < scalars else vmem, arg)
        for at, arg in enumerate(args)
    )
    return pl.pallas_call(
        body,
        name=name,
        out_shape=tuple(jax.ShapeDtypeStruct(*out) for out in outs),
        in_specs=specs,
        out_specs=(vmem,) * len(outs),
        scratch_shapes=[pltpu.VMEM(*entry) for entry in scratch],
        compiler_params=pltpu.CompilerParams(vmem_limit_bytes=VMEM_LIMIT),
    )(*args)


def put_in_place(layer, here, halves, outs, before, pieces=1):
    width, states = outs[0][0][1], outs[1][0][1]
    rows_w, rows_c = width // 2, states // 2
    vmem, count = pl.BlockSpec(memory_space=pltpu.VMEM), len(halves)

    def half(step, here):
        core = lax.rem(here[0], 2)
        spots = [1 - core if other else core for other, _ in halves]
        return spots[0] if count == 1 else jnp.where(step == 0, *spots)

    blocks = (
        pl.BlockSpec((1, rows_w, width), lambda i, here: (layer, half(i, here), 0)),
        pl.BlockSpec((1, rows_c, width), lambda i, here: (layer, half(i, here), 0)),
        pl.BlockSpec((1, width, rows_c), lambda i, here: (layer, 0, half(i, here))),
    )

    def body(here, *refs):
        grad_w, grad_c, grad_b = refs[-3:]
        for now in range(count):

            @pl.when(pl.program_id(0) == now)
            def _(source=refs[now]):
                gates, inputs = (rows_w + rows_c) // pieces, rows_c // pieces
                columns = []
                for piece in range(pieces):
                    at, row = piece * (gates + inputs), piece * gates
                    turn = min(max(rows_w - row, 0), gates)
                    if turn:
                        grad_w[0, row : row + turn, :] = source[at : at + turn, :]
                    if turn < gates:
                        to = row + turn - rows_w
                        grad_c[0, to : to + gates - turn, :] = source[at + turn : at + gates, :]
                    columns.append(source[at + gates : at + gates + inputs, :])
                grad_b[0] = jnp.concatenate(columns, axis=0).T

    return pl.pallas_call(
        body,
        name="put_in_place",
        out_shape=tuple(jax.ShapeDtypeStruct(*out) for out in outs),
        grid_spec=pltpu.PrefetchScalarGridSpec(
            num_scalar_prefetch=1,
            grid=(count,),
            in_specs=[vmem] * count + [pl.BlockSpec(memory_space=pl.ANY)] * len(before),
            out_specs=blocks,
        ),
        input_output_aliases={1 + count + i: i for i in range(len(before))},
        compiler_params=pltpu.CompilerParams(vmem_limit_bytes=VMEM_LIMIT),
    )(here, *(rows for _, rows in halves), *before)


def axis_parts():
    count, depth = lax.axis_size("seq"), lax.axis_size("dp")
    return (("seq", 2, 1, count), ("seq", count // 2, 2, count), ("dp", depth, 1, depth))


def shifted(value, part, away):
    name, size, stride, count = part
    pairs = []
    for i in range(count):
        place = (i // stride) % size
        pairs.append((i, i + ((place + away) % size - place) * stride))
    return lax.ppermute(value, name, pairs)


def add_by_shifts(value, parts, *earlier):
    for number, part in enumerate(parts):
        if number:
            value = sum(terms[1:], terms[0])
        if number == len(parts) - 1:
            value, *earlier = lax.optimization_barrier((value, *earlier))
        terms = [value] + [shifted(value, part, away) for away in range(1, part[1])]
    return terms, *earlier


def bits_of(size, stride=1):
    bits = []
    while size > 1:
        bits.append(stride)
        size, stride = size // 2, stride * 2
    return bits


def plane_bits():
    chip_bits = bits_of(lax.axis_size("seq") // 2, 2)
    middle = (len(chip_bits) + 1) // 2
    inner, outer = chip_bits[:middle], chip_bits[middle:]
    return list(zip(inner + outer, outer + inner))


def swap(value, axis, bit):
    return lax.ppermute(value, axis, [(i, i ^ bit) for i in range(lax.axis_size(axis))])


def bit_at(here, axis, bit):
    return lax.rem(lax.div(here[0 if axis == "seq" else 1], bit), 2)


def rows_at(half, rows):
    return pl.ds(pl.multiple_of(half * rows, CHUNKS), rows)


def fold_cores(bits, here, *refs):
    terms, targets = refs[:-4], refs[-4:]
    rows, cols = targets[0].shape
    for side in (0, 1):
        kept, sent = targets[2 * side : 2 * side + 2]
        where = slice(side * cols, (side + 1) * cols)
        bit = bit_at(here, "seq", bits[side])
        for half in (0, 1):

            @pl.when(bit == half)
            def _(half=half, kept=kept, sent=sent, where=where):
                start = 0
                for own, found in zip(terms[0::2], terms[1::2]):
                    for part, target in ((half, kept), (1 - half, sent)):
                        low = max(start, part * rows)
                        high = min(start + own.shape[0], (part + 1) * rows)
                        if low < high:
                            source = slice(low - start, high - start)
                            target[low - part * rows : high - part * rows, :] = (
                                own[source, where] + found[source, where]
                            )
                    start += own.shape[0]


def fold_sides(bits, here, *refs):
    targets, blocks = refs[-4:], refs[:-4]
    for side in (0, 1):
        kept, sent = targets[2 * side : 2 * side + 2]
        half, start = bit_at(here, "seq", bits[side]), 0
        for at in range(0, len(blocks), 4):
            own, found = blocks[at + 2 * side : at + 2 * side + 2]
            rows = own.shape[0] // 2
            to = slice(start, start + rows)
            kept[to, :] = own[rows_at(half, rows), :] + found[rows_at(half, rows), :]
            sent[to, :] = own[rows_at(1 - half, rows), :] + found[rows_at(1 - half, rows), :]
            start += rows


def fold_join(bit, here, left, found_left, right, found_right, kept, sent):
    rows, cols = kept.shape[0], left.shape[1]
    half = bit_at(here, "dp", bit)
    for side, (own, found) in enumerate(((left, found_left), (right, found_right))):
        where = slice(side * cols, (side + 1) * cols)
        kept[:, where] = own[rows_at(half, rows), :] + found[rows_at(half, rows), :]
        sent[:, where] = own[rows_at(1 - half, rows), :] + found[rows_at(1 - half, rows), :]


def fold_depth(bit, here, own, found, kept, sent):
    half, rows = bit_at(here, "dp", bit), kept.shape[0]
    kept[...] = own[rows_at(half, rows), :] + found[rows_at(half, rows), :]
    sent[...] = own[rows_at(1 - half, rows), :] + found[rows_at(1 - half, rows), :]


def add_two(own, found, out):
    out[...] = own[...] + found[...]


def unfold(bit, here, own, found, out):
    half, rows = bit_at(here, "dp", bit), own.shape[0]
    out[rows_at(half, rows), :] = own[...]
    out[rows_at(1 - half, rows), :] = found[...]


def unfold_split(bit, here, own, found, left, right):
    half, rows, cols = bit_at(here, "dp", bit), own.shape[0], left.shape[1]
    for side, out in enumerate((left, right)):
        where = slice(side * cols, (side + 1) * cols)
        out[rows_at(half, rows), :] = own[:, where]
        out[rows_at(1 - half, rows), :] = found[:, where]


def unfold_sides(bits, joined, here, *refs):
    for side in (0, 1):
        own, found = refs[2 * side : 2 * side + 2]
        half, (rows, cols) = bit_at(here, "seq", bits[side]), own.shape
        out = refs[4] if joined else refs[4 + side]
        where = slice(side * cols, (side + 1) * cols) if joined else slice(0, cols)
        out[rows_at(half, rows), where] = own[...]
        out[rows_at(1 - half, rows), where] = found[...]


def link_call(body, here, args, shapes):
    name = body.func.__name__
    return run(body, name, (here, *args), tuple((shape, f32) for shape in shapes))


class LinkSum:
    def __init__(self, here, terms):
        self.here, self.plane = here, plane_bits()
        self.depth = bits_of(lax.axis_size("dp"))
        rows = sum(term.shape[0] for term in terms[::2])
        self.shape = (rows // 2, terms[0].shape[1] // 2)
        self.parts = link_call(
            functools.partial(fold_cores, self.plane[0]), here, terms, (self.shape,) * 4
        )

    def swap_plane(self, stage):
        (left, right), pieces = self.plane[stage], self.parts
        self.parts = (
            pieces[0], swap(pieces[1], "seq", left), pieces[2], swap(pieces[3], "seq", right)
        )

    def down_plane(self, stage, *others):
        parts, rows, cols = list(self.parts), *self.shape
        for other in others:
            parts += other.parts
            rows += other.shape[0]
        self.shape = (rows // 2, cols)
        body = functools.partial(fold_sides, self.plane[stage])
        self.parts = link_call(body, self.here, parts, (self.shape,) * 4)

    def down_join(self):
        rows, cols = self.shape
        self.shape = (rows // 2, 2 * cols)
        body = functools.partial(fold_join, self.depth[0])
        self.parts = link_call(body, self.here, self.parts, (self.shape,) * 2)

    def swap_depth(self, stage):
        self.parts = (self.parts[0], swap(self.parts[1], "dp", self.depth[stage]))

    def down_depth(self, stage):
        rows, cols = self.shape
        self.shape = (rows // 2, cols)
        body = functools.partial(fold_depth, self.depth[stage])
        self.parts = link_call(body, self.here, self.parts, (self.shape,) * 2)

    def middle(self):
        (value,) = run(add_two, "add_two", self.parts, ((self.shape, f32),), scalars=0)
        self.parts = (value, value)

    def up_depth(self, stage):
        rows, cols = self.shape
        self.shape = (rows * 2, cols)
        body = functools.partial(unfold, self.depth[stage])
        (value,) = link_call(body, self.here, self.parts, (self.shape,))
        self.parts = (value, value)

    def up_split(self):
        rows, cols = self.shape
        self.shape = (rows * 2, cols // 2)
        body = functools.partial(unfold_split, self.depth[0])
        left, right = link_call(body, self.here, self.parts, (self.shape,) * 2)
        self.parts = (left, left, right, right)

    def up_plane(self, stage):
        rows, cols = self.shape
        if stage:
            self.shape = (rows * 2, cols)
            body = functools.partial(unfold_sides, self.plane[stage], False)
            left, right = link_call(body, self.here, self.parts, (self.shape,) * 2)
            self.parts = (left, left, right, right)
        else:
            self.shape = (rows * 2, cols * 2)
            body = functools.partial(unfold_sides, self.plane[stage], True)
            self.parts = link_call(body, self.here, self.parts, (self.shape,))

    def after(self, *values):
        self.parts, values = lax.optimization_barrier((self.parts, values))
        return values

    def to_depth(self):
        for stage in range(2, len(self.plane)):
            self.swap_plane(stage - 1)
            self.down_plane(stage)
        self.swap_plane(len(self.plane) - 1)

    def scatter_depth(self):
        for stage in range(len(self.depth) - 1):
            if stage:
                self.down_depth(stage)
            self.swap_depth(stage)

    def swap_whole(self):
        self.parts = (self.parts[0], swap(self.parts[0], "dp", self.depth[-1]))

    def gather_depth(self):
        for stage in range(len(self.depth) - 2, 0, -1):
            self.swap_depth(stage)
            self.up_depth(stage)
        self.swap_depth(0)


def wait_for(*things):
    sums = [thing for thing in things if isinstance(thing, LinkSum)]
    values = [thing for thing in things if not isinstance(thing, LinkSum)]
    parts, values = lax.optimization_barrier(([entry.parts for entry in sums], values))
    for entry, part in zip(sums, parts):
        entry.parts = part
    return values


def discretize(lam_re, lam_im, log_step):
    step_size = jnp.exp(log_step)
    decay_abs = jnp.exp(lam_re * step_size)
    rotation = lam_im * step_size
    dec_re = decay_abs * jnp.cos(rotation)
    dec_im = decay_abs * jnp.sin(rotation)
    denom_sq = lam_re * lam_re + lam_im * lam_im
    inj_re = ((dec_re - 1.0) * lam_re + dec_im * lam_im) / denom_sq
    inj_im = (dec_im * lam_re - (dec_re - 1.0) * lam_im) / denom_sq
    return (dec_re, dec_im, inj_re, inj_im)


def per_device(
    block_in, cotangent, doc_lengths, norm_gain, norm_shift, log_step, lam_re, lam_im,
    b_proj, c_proj, d_skip, w_gate,
):
    batches, seqs, span, width = block_in.shape
    assert seqs == 1 and span % (4 * CHUNKS) == 0 and span & (span - 1) == 0
    half = lam_re.shape[1]
    groups = half // LANES
    rows = batches * span
    count = lax.axis_size("seq")
    tokens = float(seqs * lax.axis_size("dp") * span * count)
    here = jnp.stack([lax.axis_index("seq"), lax.axis_index("dp")]).astype(jnp.int32)
    place = jnp.concatenate([here] + [doc_lengths[batch, 0] for batch in range(batches)])
    place, block_in = lax.optimization_barrier((place, block_in))
    here = place
    disc = discretize(lam_re, lam_im, log_step)

    x = block_in.reshape(rows, width)
    cot = cotangent.reshape(rows, width)
    lower = (0, False, batches, span, groups, tokens, count)
    upper = (1, True, batches, span, groups, tokens, count)
    part = functools.partial

    flat, low = ((rows, width), f32), ((rows, width), bf16)
    wide, wide_low = ((rows, 2 * half), f32), ((rows, 2 * half), bf16)
    padded = ((batches * (span + CHUNKS), 2 * half), f32)
    sums = ((2 * batches, width), f32)
    prefix = ((2, batches * CHUNKS, 2 * half), f32)
    total = ((batches, 2 * half), f32)
    line, shared = ((1, width), f32), ((2, width), f32)
    small = ((8, width), f32)

    def gather_row(value, reverse):
        both = jnp.concatenate([value, swap(value, "seq", 1)], axis=0)
        chips = count // 2
        return [both] + [
            shifted(both, plane, chips - away if reverse else away) for away in range(1, chips)
        ]

    (stats,) = run(part(first_sums, batches, span), "first_sums", (x,), (sums,), scalars=0)

    def order(value, inverse):
        body = part(order_rows, batches, span, inverse)
        return run(body, "order_rows", (value,), (low,), scalars=0)[0]

    norms = jnp.concatenate([norm_gain, norm_shift, d_skip], axis=0)

    def forward(cfg, hidden, stats):
        return run(
            part(enter_layer, cfg),
            "enter_layer",
            (place, stats, hidden, norms, disc, b_proj),
            (low, wide, prefix, total, sums),
        )

    links, plane, depth = axis_parts()
    stats, ordered = lax.optimization_barrier(
        (add_by_shifts(stats, (links, plane, depth))[0], order(x, False))
    )
    u0, drive0, prefix0, total0, norm0 = forward(lower, ordered, stats)
    states0, states_low0, act0, sig0, slope0, hidden1, stats = run(
        part(middle_forward, lower),
        "middle_forward",
        (place, gather_row(total0, False), prefix0, disc, drive0, u0, ordered, c_proj, norms, w_gate),
        (padded, wide_low, low, flat, flat, flat, sums),
        (flat,),
    )
    cot, stats = lax.optimization_barrier((cot, stats))
    stats, ordered_cot = lax.optimization_barrier(
        (add_by_shifts(stats, (links, plane, depth))[0], order(cot, False))
    )
    u1, drive1, prefix1, total1, norm1 = forward(upper, hidden1, stats)
    (
        result1, states1, states_low1, act1, grad_gate1, grad_mixed1, grad_low1,
        source1, prefix1, total1, grad_d1,
    ) = run(
        part(turn_around, upper),
        "turn_around",
        (
            place, gather_row(total1, True), prefix1, disc, drive1, u1, hidden1, c_proj, norms, w_gate,
            ordered_cot,
        ),
        (low, padded, wide_low, low, low, flat, low, wide, prefix, total, line),
        (flat, flat, flat),
    )

    def halves(length):
        return (((length // 2, width), f32),) * 2

    grad_proj1, grad_u1, stats, small1 = run(
        part(backward_finish, upper),
        "backward_finish",
        (
            place, gather_row(total1, False), prefix1, disc, source1, drive1, states1, u1, grad_mixed1,
            grad_d1, hidden1, norm1, norms, b_proj,
        ),
        (wide_low, flat, sums, small),
    )
    sizes = (width + 2 * half, 2 * half)
    own1, sent1 = run(
        all_weights,
        "all_weights",
        (here, act1, grad_gate1, states_low1, grad_low1, grad_proj1, u1),
        halves(sum(sizes)),
    )
    stats = stats + swap(stats, "seq", 1)
    stats, sent1 = lax.optimization_barrier((stats, sent1))
    upper_sum = LinkSum(here, (own1, swap(sent1, "seq", 1)))
    stats, upper_sum.parts = add_by_shifts(stats, (plane, depth), upper_sum.parts)
    upper_sum.swap_plane(0)
    (
        grad_out0, shared1, grad_gate0, grad_mixed0, grad_low0, source0, prefix0, total0, grad_d0,
    ) = run(
        part(between_layers, upper, lower),
        "between_layers",
        (
            place, stats, ordered_cot, grad_u1, hidden1, norm1, norms,
            disc, u0, c_proj, w_gate, states_low0, act0, sig0, slope0,
        ),
        (flat, shared, low, flat, low, wide, prefix, total, line),
        (flat,),
    )
    (total0,) = upper_sum.after(total0)
    upper_sum.down_plane(1)
    (total0,) = upper_sum.after(total0)
    upper_sum.to_depth()
    ends, grad_gate0 = wait_for(upper_sum, gather_row(total0, True), grad_gate0)
    upper_sum.down_join()
    ends, grad_gate0 = wait_for(upper_sum, ends, grad_gate0)
    upper_sum.scatter_depth()
    own_gates, sent_gates = run(
        gate_weights, "gate_weights", (here, act0, grad_gate0, states_low0, grad_low0),
        halves(sizes[0]),
    )
    own_gates, ends = lax.optimization_barrier((own_gates, ends))
    grad_proj0, grad_u0, last_sums = run(
        part(backward_finish_last, lower),
        "backward_finish",
        (
            place, ends, prefix0, disc, source0, drive0, states0, u0, grad_mixed0, grad_d0,
            ordered, norm0, norms, b_proj, small1,
        ),
        (wide_low, flat, ((3 * CHUNKS, width), f32)),
    )
    lower_sum = LinkSum(here, (own_gates, swap(sent_gates, "seq", 1)))
    (grad_proj0,) = wait_for(upper_sum, lower_sum, grad_proj0)
    own_inputs, sent_inputs = run(
        input_weights, "input_weights", (here, grad_proj0, u0), halves(sizes[1])
    )
    inputs_sum = LinkSum(here, (own_inputs, swap(sent_inputs, "seq", 1)))
    upper_sum.middle()
    upper_sum.swap_whole()
    lower_sum.swap_plane(0)
    inputs_sum.swap_plane(0)
    wait_for(upper_sum, lower_sum, inputs_sum)

    lower_sum.down_plane(1, inputs_sum)
    upper_sum.middle()
    upper_sum.gather_depth()
    lower_sum.to_depth()
    wait_for(upper_sum, lower_sum)

    lower_sum.down_join()
    upper_sum.up_split()
    lower_sum.scatter_depth()
    upper_sum.swap_plane(len(upper_sum.plane) - 1)
    wait_for(upper_sum, lower_sum)

    lower_sum.middle()
    lower_sum.swap_whole()
    for stage in range(len(upper_sum.plane) - 1, 0, -1):
        upper_sum.up_plane(stage)
        upper_sum.swap_plane(stage - 1)
    (last_sums,) = wait_for(upper_sum, lower_sum, last_sums)

    lower_sum.middle()
    (last_sums,) = lower_sum.after(last_sums)
    lower_sum.gather_depth()
    last_sums = last_sums + swap(last_sums, "seq", 1)
    last_terms = [last_sums] + [shifted(last_sums, plane, away) for away in range(1, plane[1])]
    last_terms = wait_for(lower_sum, *last_terms)

    lower_sum.up_split()
    wait_for(upper_sum, lower_sum)
    lower_sum.swap_plane(len(lower_sum.plane) - 1)
    upper_sum.up_plane(0)
    own1, result1 = lax.optimization_barrier((upper_sum.parts[0], result1))
    other1 = swap(own1, "seq", 1)
    block_out = order(result1, True)
    final = (((2, width, width), f32), ((2, 2 * half, width), f32), ((2, width, 2 * half), f32))
    placed = put_in_place(1, here, ((False, own1), (True, other1)), final, ())
    summed = sum(last_terms)
    for bit in bits_of(lax.axis_size("dp")):
        summed = summed + swap(summed, "dp", bit)
    summed, block_out = wait_for(lower_sum, summed, block_out)

    for stage in range(len(lower_sum.plane) - 1, 0, -1):
        lower_sum.up_plane(stage)
        if stage == 1:
            (summed,) = lower_sum.after(summed)
        lower_sum.swap_plane(stage - 1)
    grad_input, shared0 = run(
        part(last_step, lower),
        "last_step",
        ((summed[: 2 * batches],), grad_out0, grad_u0, ordered, norm0, norms),
        (flat, shared),
        (((width // LANES, rows, LANES), f32),),
        scalars=0,
    )
    small_sum = summed[CHUNKS:].reshape(2, CHUNKS, width)
    _, pullback = jax.vjp(discretize, lam_re, lam_im, log_step)
    grad_lr, grad_li, grad_ls = pullback(tuple(small_sum[:, kind, :half] for kind in range(4)))
    both = jnp.stack([shared0, shared1])
    grad_gain, grad_shift = both[:, 0], both[:, 1]
    early = [swap(lower_sum.parts[at], "seq", 1) for at in (0, 2)]
    grad_skip = small_sum[:, 4]
    grad_input, grad_lr, grad_li, grad_ls, grad_gain, grad_shift, grad_skip, *rest = wait_for(
        lower_sum, grad_input, grad_lr, grad_li, grad_ls, grad_gain, grad_shift, grad_skip,
        *early, *placed,
    )
    early, placed = rest[:2], rest[2:]

    late = [swap(lower_sum.parts[at], "seq", 1) for at in (1, 3)]
    other_sum = copy.copy(lower_sum)
    other_sum.parts = (early[0], late[0], early[1], late[1])
    lower_sum.up_plane(0)
    placed = put_in_place(0, here, ((False, lower_sum.parts[0]),), final, placed, 4)
    other_sum.up_plane(0)
    grad_w, grad_c, grad_b = put_in_place(
        0, here, ((True, other_sum.parts[0]),), final, placed, 4
    )
    shape = block_in.shape
    return (
        block_out.reshape(shape), grad_input.reshape(shape), grad_gain, grad_shift,
        grad_ls, grad_lr, grad_li, grad_b, grad_c, grad_skip, grad_w,
    )


def solution(mesh):
    split = P(None, "dp", "seq", None)
    return jax.shard_map(
        per_device,
        mesh=mesh,
        in_specs=(split, split, P(None, "dp", None)) + (P(),) * 9,
        out_specs=(split, split) + (P(),) * 9,
        check_vma=False,
    )
```
